32 devices in a mesh: dp: 8 (over z, x), tensor: 4 (over y, core).
Axes of the slice: x: 2, y: 2, z: 4, core: 2. Of those that a mesh axis runs over, the one named last changes fastest.
Arguments:
- tokens: bfloat16 [32, 1152, 256], P('dp'), may hold values from -6 to 6
- lengths: int32 [32], P('dp'), may hold values from 288 to 1152, as said below
- row_mask: int32 [32, 12], P('dp'), may hold values 0 or 1
- cotangent: bfloat16 [32, 1152, 256], P('dp'), may hold values from -6 to 6
- w_qkv: bfloat16 [256, 768], P(('dp', 'tensor')), may hold values from -0.375 to 0.375
- w_out: bfloat16 [256, 256], P(('dp', 'tensor')), may hold values from -1.5 to 1.5
- gains: bfloat16 [2, 256], P(None, ('dp', 'tensor')), may hold values from 0.5 to 1.5
- biases: bfloat16 [3, 256], P(None, ('dp', 'tensor')), may hold values from -2 to 2
- w_up: bfloat16 [256, 1024], P('dp', 'tensor'), may hold values from -0.375 to 0.375
- w_down: bfloat16 [1024, 256], P('tensor', 'dp'), may hold values from -0.1875 to 0.1875
Outputs:
- layer_out: bfloat16 [32, 1152, 256], P('dp')
- grad_tokens: float32 [32, 1152, 256], P('dp')
- grad_qkv: float32 [256, 768], P(('dp', 'tensor'))
- grad_wout: float32 [256, 256], P(('dp', 'tensor'))
- grad_gains: float32 [2, 256], P(None, ('dp', 'tensor'))
- grad_biases: float32 [3, 256], P(None, ('dp', 'tensor'))
- grad_up: float32 [256, 1024], P('dp', 'tensor')
- grad_down: float32 [1024, 256], P('tensor', 'dp')
The draws below stay inside these ranges and needn't reach their ends.
Inputs may be any that keep to these rules, and one draw needn't show every extreme that they name: `lengths`: some image has all 1152 tokens real.
All inputs are finite; a program needn't handle non-finite values. No bound on the sum of `row_mask` on one device may be relied on, other than what follows from the above.
Results may differ from the reference program's by a relative error of at most 0.013.
Values may be sent and summed in bfloat16 or wider, within the bound.
No kernel may reach another device: no remote copies, remote signals or barrier semaphores. Data moves between devices by JAX's collectives and lax.ppermute only.
A program may use at most 128 MiB of HBM per device.

```python
import jax
import jax.numpy as jnp
from jax import lax

D = 256
HEADS = 2
FF = 1024
WIN = 96
ROWS = 12
HS = 128
LEN = 1152
IMAGES = 32


def draw_lengths(key, part):
    key = jax.random.fold_in(key, 11)
    key_vals, key_full = jax.random.split(key)
    picked = jax.random.randint(key_vals, (IMAGES,), LEN // 4, LEN + 1)
    longest = jax.random.randint(key_full, (), 0, IMAGES)
    return jnp.where(jnp.arange(IMAGES) == longest, LEN, picked).astype(jnp.int32)


def set_ends(array, stream_key, smallest, high):
    place = [jax.random.randint(jax.random.fold_in(stream_key, axis), (), 0, length) for axis, length in enumerate(array.shape)]
    widest = array.shape.index(max(array.shape))
    next_to = place[:widest] + [(place[widest] + 1) % array.shape[widest]] + place[widest + 1:]
    return array.at[tuple(place)].set(smallest).at[tuple(next_to)].set(high)


def levels(own_key, extent, cuts, smallest, high):
    loudness = 1.0
    for dim, parts in cuts:
        heights = jax.random.uniform(jax.random.fold_in(jax.random.fold_in(own_key, 6), dim), (parts,), jnp.float32, smallest / len(cuts), high / len(cuts))
        loudness = loudness * jnp.repeat(jnp.exp(heights), extent[dim] // parts).reshape((-1,) + (1,) * (len(extent) - 1 - dim))
    return loudness


def centred(own_key, dims, deviation, limit, shards=(), kind=jnp.bfloat16):
    values = jax.random.normal(own_key, dims, jnp.float32) * deviation
    if len(shards) > 0:
        values = levels(own_key, dims, shards, -0.22, 0.18) * values
    return jnp.clip(values, min=-limit, max=limit).astype(kind)


def setup_inputs(seed: int = 0) -> dict:
    seeds = jax.random.split(jax.random.key(seed), 11)
    return {
        "tokens": centred(seeds[0], (IMAGES, LEN, D), 1.0, 6.0, ((0, 8),)),
        "lengths": draw_lengths(jax.random.fold_in(seeds[10], 71), 0),
        "row_mask": set_ends((jax.random.randint(seeds[2], (IMAGES, ROWS), 0, 4) < 3).astype(jnp.int32), jax.random.fold_in(seeds[2], 1), 0, 1),
        "cotangent": centred(seeds[3], (IMAGES, LEN, D), 1.0, 6.0, ((0, 8),)),
        "w_qkv": centred(seeds[4], (D, 3 * D), D ** -0.5, 0.375, ((0, 32),)),
        "w_out": centred(seeds[5], (D, D), (D // 16) ** -0.5, 1.5, ((0, 32),)),
        "gains": jnp.clip(1.0 + 0.1 * jax.random.normal(seeds[6], (2, D), jnp.float32), 0.5, 1.5).astype(jnp.bfloat16),
        "biases": centred(seeds[7], (3, D), 0.3, 2.0, ((1, 32),)),
        "w_up": centred(seeds[8], (D, FF), D ** -0.5, 0.375, ((0, 8), (1, 4))),
        "w_down": centred(seeds[9], (FF, D), FF ** -0.5, 0.1875, ((0, 4), (1, 8))),
    }


@jax.custom_vjp
def low(v):
    return lax.optimization_barrier(v.astype(jnp.bfloat16)).astype(jnp.float32)

@jax.custom_vjp
def low_back(v):
    return v

def low_keep(v):
    return (low(v), None)

def low_pass(kept, grad):
    return (grad,)

def back_keep(v):
    return (v, None)

def back_low(kept, grad):
    return (low(grad),)
low.defvjp(low_keep, low_pass)
low_back.defvjp(back_keep, back_low)

def layer_norm(values, gain_vec, bias_vec):
    center = values - lax.optimization_barrier(jnp.mean(values, -1, keepdims=True))
    spread = lax.optimization_barrier(jnp.mean(center * center, -1, keepdims=True))
    return center * lax.rsqrt(spread + 1e-05) * gain_vec + bias_vec

def image_mask(length, rows_live):
    offsets = jnp.arange(WIN, dtype=jnp.int32)
    position = jnp.arange(ROWS, dtype=jnp.int32)[:, None] * WIN + offsets[None, :]
    key_ok = (position < length) & (rows_live[:, None] == 1)
    causal = offsets[None, :] <= offsets[:, None]
    same_tok = offsets[None, :] == offsets[:, None]
    return causal[None] & (same_tok[None] | key_ok[:, None, :])

def forward(inputs, w_qkv, w_out, gains, biases, w_up, w_down, allowed):
    best = lax.Precision.HIGHEST
    normed = low(layer_norm(inputs, gains[0], biases[0]))
    qkv = low_back(low(jnp.dot(normed, w_qkv, precision=best)))
    qkv = qkv.reshape(ROWS, WIN, 3, HEADS, HS)
    queries = qkv[:, :, 0]
    keys_all = qkv[:, :, 1]
    values_all = qkv[:, :, 2]
    raw = low_back(jnp.einsum('rihd,rjhd->rhij', queries, keys_all, precision=best))
    scores = jnp.where(allowed[:, None], raw * HS ** (-0.5), -1e+30)
    highest = lax.optimization_barrier(jnp.max(scores, -1, keepdims=True))
    expd = jnp.exp(scores - highest)
    probs = expd / lax.optimization_barrier(jnp.sum(expd, -1, keepdims=True))
    mixed = jnp.einsum('rhij,rjhd->rihd', low(probs), values_all, precision=best).reshape(ROWS * WIN, D)
    mixed = low_back(low(mixed))
    attn = low_back(jnp.dot(mixed, w_out, precision=best))
    resid = inputs + attn
    normed_ffn = low(layer_norm(resid, gains[1], biases[1]))
    hidden_pre = low_back(jnp.dot(normed_ffn, w_up, precision=best))
    hidden = low(jax.nn.gelu(hidden_pre, approximate=True))
    branch = low_back(jnp.dot(hidden, w_down, precision=best) + biases[2])
    return resid + branch

def reference(tokens, lengths, row_mask, cotangent, w_qkv, w_out, gains, biases, w_up, w_down):
    params = tuple((item.astype(jnp.float32) for item in (w_qkv, w_out, gains, biases, w_up, w_down)))

    def one_image(carry, item):
        image, cot_image, length, rows_live = item
        allowed = image_mask(length, rows_live)

        def apply_layer(inputs, pa, pb, pc, pd, pe, pf):
            return forward(inputs, pa, pb, pc, pd, pe, pf, allowed)
        output, back_fn = jax.vjp(apply_layer, image.astype(jnp.float32), *params)
        grads = back_fn(cot_image.astype(jnp.float32))
        updated = tuple((total + grad for total, grad in zip(carry, grads[1:])))
        return (updated, (output.astype(jnp.bfloat16), grads[0]))
    start_sums = tuple((jnp.zeros(item.shape, jnp.float32) for item in params))
    sums, (layer_out, grad_tokens) = lax.scan(one_image, start_sums, (tokens, cotangent, lengths, row_mask))
    return (layer_out, grad_tokens, sums[0], sums[1], sums[2], sums[3], sums[4], sums[5])
```

```python
import jax
import jax.numpy as jnp
from jax import lax
from jax.sharding import PartitionSpec as P

HEADS = 2
WIN = 96
F32 = jnp.float32
BF16 = jnp.bfloat16


def bits_of(size):
    return [1 << k for k in reversed(range(size.bit_length() - 1))]


def swap(block, axis, bit):
    size = lax.axis_size(axis)
    return lax.ppermute(block, axis, [(i, i ^ bit) for i in range(size)])


def gather_blocks(block):
    held = block[None]
    for axis in ("dp", "tensor"):
        for bit in bits_of(lax.axis_size(axis)):
            got = swap(held, axis, bit)
            held = jnp.stack([held, got], 1)
            held = held.reshape((-1,) + block.shape)
    return held


def reduce_blocks(blocks):
    for axis in ("tensor", "dp"):
        for bit in reversed(bits_of(lax.axis_size(axis))):
            pairs = blocks.reshape((-1, 2) + blocks.shape[1:])
            got = swap(pairs[:, 1].astype(BF16), axis, bit)
            blocks = pairs[:, 0] + got.astype(F32)
    return blocks[0]


def gather_images(block):
    held = block[None]
    for bit in bits_of(lax.axis_size("tensor")):
        got = swap(held, "tensor", bit)
        held = jnp.stack([held, got], 1).reshape((-1,) + block.shape)
    me = lax.axis_index("tensor")
    return jnp.take(held, jnp.arange(held.shape[0]) ^ me, axis=0)


def norm_parts(values):
    center = values - jnp.mean(values, -1, keepdims=True)
    inv = lax.rsqrt(jnp.mean(center * center, -1, keepdims=True) + 1e-05)
    return center * inv, inv


def norm_back(grad, xhat, inv, gain):
    scaled = grad * gain
    return inv * (
        scaled
        - jnp.mean(scaled, -1, keepdims=True)
        - xhat * jnp.mean(scaled * xhat, -1, keepdims=True)
    )


def dot(a, b, dims):
    return lax.dot_general(a, b, (dims, ((), ())), preferred_element_type=F32)


NN = ((1,), (0,))
NT = ((1,), (1,))
TN = ((0,), (0,))


def gelu_both(u):
    c = 0.7978845608028654
    u2 = u * u
    t = jnp.tanh(c * u * (1.0 + 0.044715 * u2))
    half = 0.5 * (1.0 + t)
    value = u * half
    slope = half + 0.5 * u * (1.0 - t * t) * c * (1.0 + 3 * 0.044715 * u2)
    return value, slope


def layer(x, cot, length, live, wqkv, wout, gains, biases, wup, wdown):
    tokens, width = x.shape
    rows = tokens // WIN
    hs = width // HEADS
    scale = hs**-0.5
    x = x.astype(F32)
    xhat1, inv1 = norm_parts(x)
    h1 = (xhat1 * gains[0] + biases[0]).astype(BF16)
    qkv = dot(h1, wqkv, NN).astype(BF16).reshape(rows, WIN, 3, HEADS, hs)
    q, k, v = qkv[:, :, 0], qkv[:, :, 1], qkv[:, :, 2]
    offs = jnp.arange(WIN, dtype=jnp.int32)
    pos = jnp.arange(rows, dtype=jnp.int32)[:, None] * WIN + offs[None]
    ok = (pos < length) & (live[:, None] == 1)
    allowed = (offs[None, :] <= offs[:, None])[None] & (
        (offs[None, :] == offs[:, None])[None] | ok[:, None, :]
    )
    s = jnp.einsum("rihd,rjhd->rhij", q, k, preferred_element_type=F32) * scale
    s = jnp.where(allowed[:, None], s, -1e30)
    e = jnp.exp(s - jnp.max(s, -1, keepdims=True))
    p = e / jnp.sum(e, -1, keepdims=True)
    pb = p.astype(BF16)
    o = jnp.einsum("rhij,rjhd->rihd", pb, v, preferred_element_type=F32)
    o = o.astype(BF16).reshape(tokens, width)
    x1 = x + dot(o, wout, NN)
    xhat2, inv2 = norm_parts(x1)
    h2 = (xhat2 * gains[1] + biases[1]).astype(BF16)
    a, slope = gelu_both(dot(h2, wup, NN))
    a = a.astype(BF16)
    y = x1 + dot(a, wdown, NT) + biases[2]
    dyb = cot
    dy = cot.astype(F32)
    du = (dot(dyb, wdown, NN) * slope).astype(BF16)
    gdown = dot(dyb, a, TN)
    gup = dot(h2, du, TN)
    dh2 = dot(du, wup, NT)
    dx1 = dy + norm_back(dh2, xhat2, inv2, gains[1])
    g = dx1.astype(BF16)
    gwout = dot(o, g, TN)
    do = dot(g, wout, NT).astype(BF16).reshape(rows, WIN, HEADS, hs)
    dv = jnp.einsum("rhij,rihd->rjhd", pb, do, preferred_element_type=F32)
    dp = jnp.einsum("rihd,rjhd->rhij", do, v, preferred_element_type=F32)
    ds = (p * (dp - jnp.sum(dp * p, -1, keepdims=True)) * scale).astype(BF16)
    dq = jnp.einsum("rhij,rjhd->rihd", ds, k, preferred_element_type=F32)
    dk = jnp.einsum("rhij,rihd->rjhd", ds, q, preferred_element_type=F32)
    dqkv = jnp.stack([dq, dk, dv], 2).astype(BF16).reshape(tokens, 3 * width)
    gqkv = dot(h1, dqkv, TN)
    dh1 = dot(dqkv, wqkv, NT)
    gx = dx1 + norm_back(dh1, xhat1, inv1, gains[0])
    ggains = jnp.stack([jnp.sum(dh1 * xhat1, 0), jnp.sum(dh2 * xhat2, 0)])
    gbias = jnp.stack([jnp.sum(dh1, 0), jnp.sum(dh2, 0), jnp.sum(dy, 0)])
    return y.astype(BF16), gx.astype(BF16), gqkv, gwout, ggains, gbias, gup, gdown


def on_device(tokens, lengths, row_mask, cotangent, w_qkv, w_out, gains, biases, w_up, w_down):
    images, seq_len, width = tokens.shape
    n_dp, n_t = lax.axis_size("dp"), lax.axis_size("tensor")
    count = n_dp * n_t
    t_id = lax.axis_index("tensor")
    me = lax.axis_index("dp") * n_t + t_id
    small = width // count
    tall = width // n_dp
    wide = w_up.shape[1]
    vec = jnp.concatenate([gains.reshape(-1), biases.reshape(-1)])
    vec = jnp.pad(vec, (0, width - vec.shape[0]))
    packed = jnp.concatenate(
        [
            w_qkv.reshape(small, 3, width).transpose(1, 0, 2).reshape(3 * small, width),
            w_out,
            w_up,
            w_down.T,
            vec[None],
        ],
        0,
    )
    blocks = gather_blocks(packed)
    order = jnp.arange(count) ^ me
    blocks = jnp.take(blocks, order, axis=0)
    wqkv = blocks[:, : 3 * small].reshape(count, 3, small, width).transpose(0, 2, 1, 3)
    wqkv = wqkv.reshape(width, 3 * width)
    wout = blocks[:, 3 * small : 4 * small].reshape(width, width)
    at = 4 * small
    wup = blocks[:, at : at + tall].reshape(n_dp, n_t, tall, wide).transpose(0, 2, 1, 3)
    wup = wup.reshape(width, n_t * wide)
    at += tall
    wdown = blocks[:, at : at + tall].reshape(n_dp, n_t, tall, wide).transpose(0, 2, 1, 3)
    wdown = wdown.reshape(width, n_t * wide)
    at += tall
    vec = blocks[:, at].astype(F32)
    gain_all = vec[:, : 2 * small].reshape(count, 2, small).transpose(1, 0, 2).reshape(2, width)
    bias_all = (
        vec[:, 2 * small : 5 * small].reshape(count, 3, small).transpose(1, 0, 2).reshape(3, width)
    )
    x = lax.dynamic_index_in_dim(tokens, t_id, 0, keepdims=False)
    cot = lax.dynamic_index_in_dim(cotangent, t_id, 0, keepdims=False)
    length = lax.dynamic_index_in_dim(lengths, t_id, 0, keepdims=False)
    live = lax.dynamic_index_in_dim(row_mask, t_id, 0, keepdims=False)
    y, gx, gqkv, gwout, ggains, gbias, gup, gdown = layer(
        x, cot, length, live, wqkv, wout, gain_all, bias_all, wup, wdown
    )
    gvec = jnp.concatenate(
        [
            ggains.reshape(2, count, small).transpose(1, 0, 2).reshape(count, 2 * small),
            gbias.reshape(3, count, small).transpose(1, 0, 2).reshape(count, 3 * small),
            jnp.zeros((count, width - 5 * small), F32),
        ],
        1,
    )

    def split_hidden(m):
        m = m.reshape(n_dp, tall, n_t, wide).transpose(0, 2, 1, 3)
        return m.reshape(count, tall, wide)

    grads = jnp.concatenate(
        [
            gqkv.reshape(count, small, 3, width).transpose(0, 2, 1, 3).reshape(count, -1, width),
            gwout.reshape(count, small, width),
            split_hidden(gup),
            split_hidden(gdown),
            gvec[:, None],
        ],
        1,
    )
    mine = reduce_blocks(jnp.take(grads, order, axis=0))
    o_qkv = mine[: 3 * small].reshape(3, small, width).transpose(1, 0, 2).reshape(small, 3 * width)
    o_out = mine[3 * small : 4 * small]
    at = 4 * small
    o_up = mine[at : at + tall]
    o_down = mine[at + tall : at + 2 * tall].T
    o_vec = mine[at + 2 * tall]
    o_gains = o_vec[: 2 * small].reshape(2, small)
    o_bias = o_vec[2 * small : 5 * small].reshape(3, small)
    layer_out = gather_images(y)
    grad_tokens = gather_images(gx).astype(F32)
    return layer_out, grad_tokens, o_qkv, o_out, o_gains, o_bias, o_up, o_down


def solution(mesh):
    in_specs = (
        P("dp", None, None),
        P("dp"),
        P("dp", None),
        P("dp", None, None),
        P(("dp", "tensor"), None),
        P(("dp", "tensor"), None),
        P(None, ("dp", "tensor")),
        P(None, ("dp", "tensor")),
        P("dp", "tensor"),
        P("tensor", "dp"),
    )
    out_specs = (
        P("dp", None, None),
        P("dp", None, None),
        P(("dp", "tensor"), None),
        P(("dp", "tensor"), None),
        P(None, ("dp", "tensor")),
        P(None, ("dp", "tensor")),
        P("dp", "tensor"),
        P("tensor", "dp"),
    )
    return jax.shard_map(
        on_device, mesh=mesh, in_specs=in_specs, out_specs=out_specs, check_vma=False
    )
```

```python
import functools

import jax
import jax.numpy as jnp
from jax import lax
from jax.experimental import pallas as pl
from jax.experimental.pallas import tpu as pltpu
from jax.sharding import PartitionSpec as P

HEADS = 2
WIN = 96
F32 = jnp.float32
BF16 = jnp.bfloat16
VDP, VT = 8, 4
CHIPS = VDP * VT // 2
REDUCE_BITS = (2, 4, 8, 1)
MIB = 1 << 20

NN = ((1,), (0,))
NT = ((1,), (1,))
TN = ((0,), (0,))


def dot(a, b, dims):
    return lax.dot_general(a, b, (dims, ((), ())), preferred_element_type=F32)


def flip(m):
    return ((m & 1) << 3) | ((m & 2) << 1) | ((m & 4) >> 1) | ((m & 8) >> 3)


def fold(m):
    out = 0
    for place, bit in enumerate(REDUCE_BITS):
        shift = 3 - place
        out = out | (((m // bit) & 1) << shift)
    return out


def norm_parts(values):
    center = values - jnp.mean(values, -1, keepdims=True)
    inv = lax.rsqrt(jnp.mean(center * center, -1, keepdims=True) + 1e-05)
    return center * inv, inv


def norm_back(grad, xhat, inv, gain):
    scaled = grad * gain
    return inv * (
        scaled
        - jnp.mean(scaled, -1, keepdims=True)
        - xhat * jnp.mean(scaled * xhat, -1, keepdims=True)
    )


def gelu_both(u):
    c = 0.7978845608028654
    u2 = u * u
    t = jnp.tanh(u * (c + (c * 0.044715) * u2))
    half = 0.5 + 0.5 * t
    slope = half + (u * (half * (1.0 - t))) * (c + (3 * c * 0.044715) * u2)
    return u * half, slope


def pack_kernel(meta, qkv, out, gains, biases, up, down, small_ref, big_ref):
    width = out.shape[1]
    small = out.shape[0]
    for part in range(3):
        small_ref[part * small : (part + 1) * small] = qkv[:, part * width : (part + 1) * width]
    small_ref[3 * small : 4 * small] = out[...]
    small_ref[4 * small : 4 * small + 8] = jnp.zeros((8, width), BF16)
    lane = lax.broadcasted_iota(jnp.int32, (1, width), 1)
    mine = lane // small == meta[5]
    rows = [gains[0:1], gains[1:2], biases[0:1], biases[1:2], biases[2:3]]
    vals = jnp.concatenate(rows + [jnp.zeros((3, small), BF16)], 0).astype(F32)
    wide = jnp.concatenate([vals] * (width // small), 1)
    small_ref[4 * small : 4 * small + 8] = jnp.where(mine, wide, 0.0).astype(BF16)
    tall = up.shape[0]
    big_ref[:tall] = up[...]
    big_ref[tall:] = down[...]


def attend_kernel(
    meta, lens, live, x_ref, held, got, qkv_ref, prob_ref, o_ref, x1_ref, wqkv, wout, vec
):
    step = pl.program_id(0)
    tokens, width = x_ref.shape
    rows = tokens // WIN
    hs = width // HEADS

    @pl.when(step == 0)
    def _():
        first = meta[2] == 0
        total = jnp.zeros((8, width), F32)
        for m in range(CHIPS):
            k = flip(m) ^ meta[1]
            a = held[k].astype(F32)
            b = got[k].astype(F32)
            even = jnp.where(first, a, b)
            odd = jnp.where(first, b, a)
            for part in range(3):
                both = jnp.concatenate([even[part * 8 : part * 8 + 8], odd[part * 8 : part * 8 + 8]], 0)
                wqkv[m * 16 : m * 16 + 16, part * width : (part + 1) * width] = both.astype(BF16)
            both = jnp.concatenate([even[24:32], odd[24:32]], 0)
            wout[m * 16 : m * 16 + 16] = both.astype(BF16)
            total = total + a[32:40] + b[32:40]
        vec[...] = total

    x = x_ref[...].astype(F32)
    xhat, _ = norm_parts(x)
    h1 = (xhat * vec[0:1] + vec[2:3]).astype(BF16)
    qkv_ref[...] = dot(h1, wqkv[...], NN).astype(BF16)
    scale = hs**-0.5
    ii = lax.broadcasted_iota(jnp.int32, (WIN, WIN), 0)
    jj = lax.broadcasted_iota(jnp.int32, (WIN, WIN), 1)
    same = ii == jj
    image_rows = live.shape[1]
    for r in range(rows):
        row = (meta[0] * pl.num_programs(0) + step) * rows + r
        image = row // image_rows
        inside = row - image * image_rows
        reach = jnp.where(live[image, inside] == 1, lens[image] - inside * WIN, 0)
        allowed = same | (jj < jnp.minimum(ii, reach))
        at = slice(r * WIN, (r + 1) * WIN)
        for h in range(HEADS):
            q = qkv_ref[at, h * hs : (h + 1) * hs]
            k = qkv_ref[at, width + h * hs : width + (h + 1) * hs]
            v = qkv_ref[at, 2 * width + h * hs : 2 * width + (h + 1) * hs]
            s = jnp.where(allowed, dot(q, k, NT) * scale, -1e30)
            e = jnp.exp(s - jnp.max(s, -1, keepdims=True))
            p = (e / jnp.sum(e, -1, keepdims=True)).astype(BF16)
            prob_ref[r * HEADS + h] = p
            o_ref[at, h * hs : (h + 1) * hs] = dot(p, v, NN).astype(BF16)
    x1_ref[...] = x + dot(o_ref[...], wout[...], NN)


def hidden_kernel(
    meta, x1_ref, cot_ref, held, got, vec, y_ref, yfull_ref, dx1_ref, gvec, keep, send,
    wup, wdown, gup, gdown,
):
    step = pl.program_id(0)
    last = pl.num_programs(0) - 1
    tokens, width = x1_ref.shape
    tall = width // VDP

    @pl.when(step == 0)
    def _():
        for m in range(CHIPS):
            k = flip(m) ^ meta[1]
            i, y = m // 2, m % 2
            at = slice(i * tall, (i + 1) * tall)
            for source, j in ((held, 2 * y + meta[2]), (got, 2 * y + 1 - meta[2])):
                wup[j, at] = source[k, :tall]
                wdown[j, at] = source[k, tall:]
        gup[...] = jnp.zeros_like(gup)
        gdown[...] = jnp.zeros_like(gdown)
        gvec[...] = jnp.zeros_like(gvec)

    x1 = x1_ref[...]
    xhat, inv = norm_parts(x1)
    h2 = (xhat * vec[1:2] + vec[3:4]).astype(BF16)
    dyb = cot_ref[...]
    dy = dyb.astype(F32)
    f = x1 + vec[4:5]
    dh2 = jnp.zeros((tokens, width), F32)
    for j in range(VT):
        a, slope = gelu_both(dot(h2, wup[j], NN))
        a = a.astype(BF16)
        f = f + dot(a, wdown[j], NT)
        gdown[j] += dot(dyb, a, TN)
        du = (dot(dyb, wdown[j], NN) * slope).astype(BF16)
        gup[j] += dot(h2, du, TN)
        dh2 = dh2 + dot(du, wup[j], NT)
    y_ref[...] = f.astype(BF16)
    yfull_ref[...] = f.astype(BF16)
    dx1_ref[...] = dy + norm_back(dh2, xhat, inv, vec[1:2])
    gvec[1:2] += jnp.sum(dh2 * xhat, 0, keepdims=True)
    gvec[3:4] += jnp.sum(dh2, 0, keepdims=True)
    gvec[4:5] += jnp.sum(dy, 0, keepdims=True)

    @pl.when(step == last)
    def _():
        for m in range(CHIPS):
            k = fold(m) ^ meta[3]
            i, y = m // 2, m % 2
            at = slice(i * tall, (i + 1) * tall)
            mine, other = 2 * y + meta[2], 2 * y + 1 - meta[2]
            keep[k, :tall] = gup[mine, at]
            keep[k, tall:] = gdown[mine, at]
            send[k, :tall] = gup[other, at].astype(BF16)
            send[k, tall:] = gdown[other, at].astype(BF16)


def back_kernel(
    meta, x_ref, qkv_ref, prob_ref, o_ref, dx1_ref, wqkv, wout, vec, gvec_in,
    gx_ref, gxb_ref, keep, send,
    dqkv, gqkv, gout, gvec,
):
    step = pl.program_id(0)
    last = pl.num_programs(0) - 1
    tokens, width = x_ref.shape
    rows = tokens // WIN
    hs = width // HEADS
    scale = hs**-0.5

    @pl.when(step == 0)
    def _():
        gqkv[...] = jnp.zeros_like(gqkv)
        gout[...] = jnp.zeros_like(gout)
        gvec[...] = gvec_in[...]

    dx1 = dx1_ref[...]
    g = dx1.astype(BF16)
    gout[...] += dot(o_ref[...], g, TN)
    do = dot(g, wout[...], NT).astype(BF16)
    for r in range(rows):
        at = slice(r * WIN, (r + 1) * WIN)
        for h in range(HEADS):
            cols = [slice(part * width + h * hs, part * width + (h + 1) * hs) for part in range(3)]
            p = prob_ref[r * HEADS + h]
            doh = do[at, h * hs : (h + 1) * hs]
            dqkv[at, cols[2]] = dot(p, doh, TN).astype(BF16)
            dp = dot(doh, qkv_ref[at, cols[2]], NT)
            pf = p.astype(F32)
            ds = pf * (dp - jnp.sum(dp * pf, -1, keepdims=True)) * scale
            ds = ds.astype(BF16)
            dqkv[at, cols[0]] = dot(ds, qkv_ref[at, cols[1]], NN).astype(BF16)
            dqkv[at, cols[1]] = dot(ds, qkv_ref[at, cols[0]], TN).astype(BF16)
    xhat, inv = norm_parts(x_ref[...].astype(F32))
    h1 = (xhat * vec[0:1] + vec[2:3]).astype(BF16)
    gqkv[...] += dot(h1, dqkv[...], TN)
    dh1 = dot(dqkv[...], wqkv[...], NT)
    gx = dx1 + norm_back(dh1, xhat, inv, vec[0:1])
    gx_ref[...] = gx
    gxb_ref[...] = gx.astype(BF16)
    gvec[0:1] += jnp.sum(dh1 * xhat, 0, keepdims=True)
    gvec[2:3] += jnp.sum(dh1, 0, keepdims=True)

    @pl.when(step == last)
    def _():
        total = gvec[...]
        low = total.astype(BF16)
        for m in range(CHIPS):
            k = fold(m) ^ meta[3]
            mine = pl.ds(pl.multiple_of(m * 16 + 8 * meta[2], 8), 8)
            other = pl.ds(pl.multiple_of(m * 16 + 8 - 8 * meta[2], 8), 8)
            theirs = []
            for part in range(3):
                cols = slice(part * width, (part + 1) * width)
                keep[k, part * 8 : part * 8 + 8] = gqkv[mine, cols]
                theirs.append(gqkv[other, cols])
            keep[k, 24:32] = gout[mine]
            theirs.append(gout[other])
            send[k, :32] = jnp.concatenate(theirs, 0).astype(BF16)
            keep[k, 32:40] = total
            send[k, 32:40] = low


def place_kernel(meta, first, *refs):
    out = refs[-1]
    for n, source in enumerate(refs[:-1]):
        @pl.when(pl.program_id(0) == n)
        def _():
            out[...] = source[...].astype(out.dtype)


def swap(block, axis, bit):
    size = lax.axis_size(axis)
    return lax.ppermute(block, axis, [(i, i ^ bit) for i in range(size)])


def steps_of(axis):
    return [(axis, 1 << k) for k in reversed(range(lax.axis_size(axis).bit_length() - 1))]


def gather(block):
    held = block[None]
    steps = steps_of("dp") + steps_of("tensor")
    for axis, bit in steps[:-1]:
        held = jnp.concatenate([held, swap(held, axis, bit)], 0)
    return held, swap(held, *steps[-1])


def reduce(keep, send, bits):
    held = keep + swap(send, "tensor", 1).astype(F32)
    for axis, bit in bits:
        half = held.shape[0] // 2
        got = swap(held[half:].astype(BF16), axis, bit)
        held = held[:half] + got.astype(F32)
    return held[0]


def bit_reverse(index, count):
    out = 0 * index
    for k in range(count):
        out = out | (((index >> k) & 1) << (count - 1 - k))
    return out


def by_device(held, got, me):
    blocks = jnp.concatenate([held, got], 0)
    count = blocks.shape[0]
    order = jnp.arange(count, dtype=jnp.int32) ^ me
    return jnp.take(blocks, bit_reverse(order, count.bit_length() - 1), axis=0)


def other_pack(w_qkv, w_out, gains, biases, w_up, w_down, me):
    small, width = w_out.shape
    qkv = w_qkv.reshape(small, 3, width).transpose(1, 0, 2).reshape(3 * small, width)
    rows = jnp.concatenate([gains, biases], 0)
    place = jnp.zeros((8, width), BF16)
    place = lax.dynamic_update_slice(place, rows, (jnp.int32(0), me * small))
    return jnp.concatenate([qkv, w_out, place], 0), jnp.concatenate([w_up, w_down.T], 0)


def other_blocks(pair_a, pair_b, me, n_dp, n_t):
    a = by_device(*pair_a, me)
    b = by_device(*pair_b, me)
    width = a.shape[2]
    count = n_dp * n_t
    small = width // count
    big = width // (VDP * VT)
    mats = a[:, : 4 * small].reshape(count, 4, small, width).transpose(1, 0, 2, 3)
    mats = mats.reshape(4, VDP * VT, big, width).transpose(1, 0, 2, 3).reshape(VDP * VT, 4 * big, width)
    vec = jnp.sum(a[:, 4 * small :].astype(F32), 0).astype(BF16)
    vecs = jnp.concatenate([vec[None], jnp.zeros((VDP * VT - 1, 8, width), BF16)], 0)
    a = jnp.concatenate([mats, vecs], 1)
    tall = width // n_dp
    b = b.reshape(n_dp, VT, 2, tall, width).transpose(1, 2, 0, 3, 4)
    b = b.reshape(VT, 2, VDP, width // VDP, width).transpose(2, 0, 1, 3, 4)
    b = b.reshape(VDP * VT, 2 * (width // VDP), width)
    order = [flip(m) for m in range(CHIPS)]

    def halves(blocks):
        pairs = blocks.reshape((CHIPS, 2) + blocks.shape[1:])
        pairs = jnp.stack([pairs[m] for m in order], 0)
        return pairs[:, 0], pairs[:, 1]

    return halves(a) + halves(b)


def other_reduce(pair_a, pair_b, me, n_dp, n_t):
    order = [fold(m) for m in range(CHIPS)]
    count = n_dp * n_t

    def whole(keep, send):
        pairs = jnp.stack([keep, send.astype(F32)], 1)
        pairs = jnp.stack([pairs[k] for k in order], 0)
        return pairs.reshape((VDP * VT,) + keep.shape[1:])

    a, b = whole(*pair_a), whole(*pair_b)
    width = a.shape[2]
    small, tall = width // count, width // n_dp
    big = width // (VDP * VT)
    mats = a[:, : 4 * big].reshape(VDP * VT, 4, big, width).transpose(1, 0, 2, 3)
    mats = mats.reshape(4, count, small, width).transpose(1, 0, 2, 3)
    mats = mats.reshape(count, 4 * small, width)
    a = jnp.concatenate([mats, jnp.broadcast_to(a[:1, 4 * big :], (count, 8, width))], 1)
    b = b.reshape(VDP, VT, 2, width // VDP, width).transpose(1, 2, 0, 3, 4)
    b = b.reshape(VT, 2, n_dp, tall, width).transpose(2, 0, 1, 3, 4)
    b = b.reshape(count, 2 * tall, width)
    results = []
    for blocks in (a, b):
        blocks = jnp.take(blocks, jnp.arange(count, dtype=jnp.int32) ^ me, axis=0)
        for axis, bit in reversed(steps_of("dp") + steps_of("tensor")):
            pairs = blocks.reshape((-1, 2) + blocks.shape[1:])
            got = swap(pairs[:, 1].astype(BF16), axis, bit)
            blocks = pairs[:, 0] + got.astype(F32)
        results.append(blocks[0])
    return results


def const_spec(shape):
    zeros = (0,) * len(shape)
    return pl.BlockSpec(shape, lambda i, *_: zeros)


def struct(shape, dtype):
    return jax.ShapeDtypeStruct(shape, dtype)


def call(kernel, name, grid, prefetch, ins, outs, scratch, flops, limit):
    args = [a for a, _ in ins]
    moved = sum(a.size * a.dtype.itemsize for a in args)
    moved += sum(s.size * s.dtype.itemsize for s, _ in outs)
    return pl.pallas_call(
        kernel,
        name=name,
        out_shape=[s for s, _ in outs],
        grid_spec=pltpu.PrefetchScalarGridSpec(
            num_scalar_prefetch=len(prefetch),
            grid=grid,
            in_specs=[spec for _, spec in ins],
            out_specs=[spec for _, spec in outs],
            scratch_shapes=scratch,
        ),
        compiler_params=pltpu.CompilerParams(vmem_limit_bytes=limit * MIB),
        cost_estimate=pl.CostEstimate(flops=flops, bytes_accessed=moved, transcendentals=0),
    )(*prefetch, *args)


def pack(meta, w_qkv, w_out, gains, biases, w_up, w_down):
    small, width = w_out.shape
    tall = w_up.shape[0]
    return pl.pallas_call(
        pack_kernel,
        name="pack",
        out_shape=[struct((4 * small + 8, width), BF16), struct((2 * tall, width), BF16)],
        in_specs=[pl.BlockSpec(memory_space=pltpu.SMEM)] + [pl.BlockSpec(memory_space=pltpu.VMEM)] * 6,
        out_specs=[pl.BlockSpec(memory_space=pltpu.VMEM)] * 2,
    )(meta, w_qkv, w_out, gains, biases, w_up, w_down.T)


def on_device(tokens, lengths, row_mask, cotangent, w_qkv, w_out, gains, biases, w_up, w_down):
    images, seq_len, width = tokens.shape
    n_dp, n_t = lax.axis_size("dp"), lax.axis_size("tensor")
    t_id = lax.axis_index("tensor")
    me = lax.axis_index("dp") * n_t + t_id
    chip = me // 2
    small = width // (n_dp * n_t)
    tall = width // n_dp
    usual = (n_dp, n_t) == (VDP, VT)
    zero = jnp.int32(0)
    if usual:
        meta = jnp.stack([t_id, flip(chip), me % 2, fold(chip), zero, me]).astype(jnp.int32)
    else:
        meta = jnp.stack([t_id, zero, zero, zero, zero, me]).astype(jnp.int32)
    weights = (w_qkv, w_out, gains, biases, w_up, w_down)
    packs = pack(meta, *weights) if usual else other_pack(*weights, me)
    held_a, got_a = gather(packs[0])
    held_b, got_b = gather(packs[1])
    if not usual:
        held_a, got_a, held_b, got_b = other_blocks((held_a, got_a), (held_b, got_b), me, n_dp, n_t)

    own = images * seq_len // n_t
    rows = own // WIN
    per = 4 if rows % 4 == 0 else 1
    chunk = per * WIN
    grid = (rows // per,)
    steps = grid[0]
    hs = width // HEADS
    ff = w_up.shape[1] * n_t
    flat = tokens.reshape(images * seq_len, width)
    flat_cot = cotangent.reshape(images * seq_len, width)
    picked = pl.BlockSpec((chunk, width), lambda i, meta, *_: (meta[0] * steps + i, 0))

    def tiles(*shape):
        tail = (0,) * (len(shape) - 1)
        return pl.BlockSpec(shape, lambda i, *_: (i,) + tail)

    blocks_a = const_spec(held_a.shape)
    blocks_b = const_spec(held_b.shape)
    token_mm = 2 * own * width
    qkv, prob, o, x1, wqkv, wout, vec = call(
        attend_kernel,
        "attend",
        grid,
        (meta, lengths, row_mask),
        [(flat, picked), (held_a, blocks_a), (got_a, blocks_a)],
        [
            (struct((own, 3 * width), BF16), tiles(chunk, 3 * width)),
            (struct((rows * HEADS, WIN, WIN), BF16), tiles(per * HEADS, WIN, WIN)),
            (struct((own, width), BF16), tiles(chunk, width)),
            (struct((own, width), F32), tiles(chunk, width)),
            (struct((width, 3 * width), BF16), const_spec((width, 3 * width))),
            (struct((width, width), BF16), const_spec((width, width))),
            (struct((8, width), F32), const_spec((8, width))),
        ],
        [],
        token_mm * (4 * width + 2 * WIN),
        32,
    )
    big = (CHIPS, 2 * (width // VDP), width)
    y, y_full, dx1, gvec, keep_b, send_b = call(
        hidden_kernel,
        "hidden",
        grid,
        (meta,),
        [
            (x1, tiles(chunk, width)),
            (flat_cot, picked),
            (held_b, blocks_b),
            (got_b, blocks_b),
            (vec, const_spec((8, width))),
        ],
        [
            (struct((own, width), BF16), tiles(chunk, width)),
            (struct((images * seq_len, width), BF16), picked),
            (struct((own, width), F32), tiles(chunk, width)),
            (struct((8, width), F32), const_spec((8, width))),
            (struct(big, F32), const_spec(big)),
            (struct(big, BF16), const_spec(big)),
        ],
        [
            pltpu.VMEM((VT, width, ff // VT), BF16),
            pltpu.VMEM((VT, width, ff // VT), BF16),
            pltpu.VMEM((VT, width, ff // VT), F32),
            pltpu.VMEM((VT, width, ff // VT), F32),
        ],
        token_mm * 6 * ff,
        40,
    )
    little = (CHIPS, 40, width)
    gx, gxb, keep_a, send_a = call(
        back_kernel,
        "back",
        grid,
        (meta,),
        [
            (flat, picked),
            (qkv, tiles(chunk, 3 * width)),
            (prob, tiles(per * HEADS, WIN, WIN)),
            (o, tiles(chunk, width)),
            (dx1, tiles(chunk, width)),
            (wqkv, const_spec((width, 3 * width))),
            (wout, const_spec((width, width))),
            (vec, const_spec((8, width))),
            (gvec, const_spec((8, width))),
        ],
        [
            (struct((images * seq_len, width), F32), picked),
            (struct((own, width), BF16), tiles(chunk, width)),
            (struct(little, F32), const_spec(little)),
            (struct(little, BF16), const_spec(little)),
        ],
        [
            pltpu.VMEM((chunk, 3 * width), BF16),
            pltpu.VMEM((width, 3 * width), F32),
            pltpu.VMEM((width, width), F32),
            pltpu.VMEM((8, width), F32),
        ],
        token_mm * (8 * width + 5 * WIN),
        32,
    )
    if usual:
        fold_steps = [("dp", b // 2) if b > 1 else ("tensor", 2) for b in REDUCE_BITS]
        grad_b = reduce(keep_b, send_b, fold_steps)
        grad_a = reduce(keep_a, send_a, fold_steps)
    else:
        grad_a, grad_b = other_reduce((keep_a, send_a), (keep_b, send_b), me, n_dp, n_t)
    o_qkv = jnp.concatenate([grad_a[p * small : (p + 1) * small] for p in range(3)], 1)
    o_out = grad_a[3 * small : 4 * small]
    o_vec = lax.dynamic_slice_in_dim(grad_a[4 * small : 4 * small + 5], me * small, small, 1)
    o_up = grad_b[:tall]
    o_down = grad_b[tall:].T

    def spread(block, full):
        far = swap(block, "tensor", 2)
        sources = [swap(block, "tensor", 1), far, swap(far, "tensor", 1)]
        whole = pl.BlockSpec((own, width), lambda i, meta: (0, 0))
        return pl.pallas_call(
            place_kernel,
            name="place",
            out_shape=struct(full.shape, full.dtype),
            grid_spec=pltpu.PrefetchScalarGridSpec(
                num_scalar_prefetch=1,
                grid=(n_t - 1,),
                in_specs=[pl.BlockSpec(memory_space=pl.ANY)] + [whole] * 3,
                out_specs=pl.BlockSpec((own, width), lambda i, meta: (meta[0] ^ (i + 1), 0)),
            ),
            input_output_aliases={1: 0},
            compiler_params=pltpu.CompilerParams(vmem_limit_bytes=32 * MIB),
        )(meta, full, *sources).reshape(images, seq_len, width)

    layer_out = spread(y, y_full)
    grad_tokens = spread(gxb, gx)
    return layer_out, grad_tokens, o_qkv, o_out, o_vec[:2], o_vec[2:], o_up, o_down


def solution(mesh):
    in_specs = (
        P("dp", None, None),
        P("dp"),
        P("dp", None),
        P("dp", None, None),
        P(("dp", "tensor"), None),
        P(("dp", "tensor"), None),
        P(None, ("dp", "tensor")),
        P(None, ("dp", "tensor")),
        P("dp", "tensor"),
        P("tensor", "dp"),
    )
    out_specs = (
        P("dp", None, None),
        P("dp", None, None),
        P(("dp", "tensor"), None),
        P(("dp", "tensor"), None),
        P(None, ("dp", "tensor")),
        P(None, ("dp", "tensor")),
        P("dp", "tensor"),
        P("tensor", "dp"),
    )
    return jax.shard_map(
        on_device, mesh=mesh, in_specs=in_specs, out_specs=out_specs, check_vma=False
    )
```

```python
import functools

import jax
import jax.numpy as jnp
from jax import lax
from jax.experimental import pallas as pl
from jax.experimental.pallas import tpu as pltpu
from jax.sharding import PartitionSpec as P

HEADS = 2
WIN = 96
F32 = jnp.float32
BF16 = jnp.bfloat16
VDP, VT = 8, 4
CHIPS = VDP * VT // 2
REDUCE_BITS = (2, 4, 8, 1)
MIB = 1 << 20

NN = ((1,), (0,))
NT = ((1,), (1,))
TN = ((0,), (0,))


def dot(a, b, dims):
    return lax.dot_general(a, b, (dims, ((), ())), preferred_element_type=F32)


def flip(m):
    return ((m & 1) << 3) | ((m & 2) << 1) | ((m & 4) >> 1) | ((m & 8) >> 3)


def fold(m):
    out = 0
    for place, bit in enumerate(REDUCE_BITS):
        shift = 3 - place
        out = out | (((m // bit) & 1) << shift)
    return out


def norm_parts(values):
    center = values - jnp.mean(values, -1, keepdims=True)
    inv = lax.rsqrt(jnp.mean(center * center, -1, keepdims=True) + 1e-05)
    return center * inv, inv


def norm_back(grad, xhat, inv, gain):
    scaled = grad * gain
    return inv * (
        scaled
        - jnp.mean(scaled, -1, keepdims=True)
        - xhat * jnp.mean(scaled * xhat, -1, keepdims=True)
    )


def gelu_both(u):
    c = 0.7978845608028654
    u2 = u * u
    t = jnp.tanh(u * (c + (c * 0.044715) * u2))
    half = 0.5 + 0.5 * t
    slope = half + (u * (half * (1.0 - t))) * (c + (3 * c * 0.044715) * u2)
    return u * half, slope


def pack_kernel(meta, qkv, out, gains, biases, up, down, small_ref, big_ref):
    width = out.shape[1]
    small = out.shape[0]
    for part in range(3):
        small_ref[part * small : (part + 1) * small] = qkv[:, part * width : (part + 1) * width]
    small_ref[3 * small : 4 * small] = out[...]
    small_ref[4 * small : 4 * small + 8] = jnp.zeros((8, width), BF16)
    lane = lax.broadcasted_iota(jnp.int32, (1, width), 1)
    mine = lane // small == meta[5]
    rows = [gains[0:1], gains[1:2], biases[0:1], biases[1:2], biases[2:3]]
    vals = jnp.concatenate(rows + [jnp.zeros((3, small), BF16)], 0).astype(F32)
    wide = jnp.concatenate([vals] * (width // small), 1)
    small_ref[4 * small : 4 * small + 8] = jnp.where(mine, wide, 0.0).astype(BF16)
    tall = up.shape[0]
    big_ref[:tall] = up[...]
    big_ref[tall:] = down[...]


def attend_kernel(
    meta, lens, live, x_ref, held, got, qkv_ref, prob_ref, o_ref, x1_ref, wqkv, wout, vec
):
    step = pl.program_id(0)
    tokens, width = x_ref.shape
    rows = tokens // WIN
    hs = width // HEADS

    @pl.when(step == 0)
    def _():
        first = meta[2] == 0
        total = jnp.zeros((8, width), F32)
        for m in range(CHIPS):
            k = flip(m) ^ meta[1]
            a = held[k].astype(F32)
            b = got[k].astype(F32)
            even = jnp.where(first, a, b)
            odd = jnp.where(first, b, a)
            for part in range(3):
                both = jnp.concatenate([even[part * 8 : part * 8 + 8], odd[part * 8 : part * 8 + 8]], 0)
                wqkv[m * 16 : m * 16 + 16, part * width : (part + 1) * width] = both.astype(BF16)
            both = jnp.concatenate([even[24:32], odd[24:32]], 0)
            wout[m * 16 : m * 16 + 16] = both.astype(BF16)
            total = total + a[32:40] + b[32:40]
        vec[...] = total

    x = x_ref[...].astype(F32)
    xhat, _ = norm_parts(x)
    h1 = (xhat * vec[0:1] + vec[2:3]).astype(BF16)
    qkv_ref[...] = dot(h1, wqkv[...], NN).astype(BF16)
    scale = hs**-0.5
    ii = lax.broadcasted_iota(jnp.int32, (WIN, WIN), 0)
    jj = lax.broadcasted_iota(jnp.int32, (WIN, WIN), 1)
    same = ii == jj
    image_rows = live.shape[1]
    for r in range(rows):
        row = (meta[0] * pl.num_programs(0) + step) * rows + r
        image = row // image_rows
        inside = row - image * image_rows
        reach = jnp.where(live[image, inside] == 1, lens[image] - inside * WIN, 0)
        allowed = same | (jj < jnp.minimum(ii, reach))
        at = slice(r * WIN, (r + 1) * WIN)
        for h in range(HEADS):
            q = qkv_ref[at, h * hs : (h + 1) * hs]
            k = qkv_ref[at, width + h * hs : width + (h + 1) * hs]
            v = qkv_ref[at, 2 * width + h * hs : 2 * width + (h + 1) * hs]
            s = jnp.where(allowed, dot(q, k, NT) * scale, -1e30)
            e = jnp.exp(s - jnp.max(s, -1, keepdims=True))
            p = (e / jnp.sum(e, -1, keepdims=True)).astype(BF16)
            prob_ref[r * HEADS + h] = p
            o_ref[at, h * hs : (h + 1) * hs] = dot(p, v, NN).astype(BF16)
    x1_ref[...] = x + dot(o_ref[...], wout[...], NN)


def hidden_kernel(
    meta, x1_ref, cot_ref, held, got, vec, y_ref, yfull_ref, dx1_ref, gvec, keep, send,
    wup, wdown, gup, gdown,
):
    step = pl.program_id(0)
    last = pl.num_programs(0) - 1
    tokens, width = x1_ref.shape
    tall = width // VDP

    @pl.when(step == 0)
    def _():
        for m in range(CHIPS):
            k = flip(m) ^ meta[1]
            i, y = m // 2, m % 2
            at = slice(i * tall, (i + 1) * tall)
            for source, j in ((held, 2 * y + meta[2]), (got, 2 * y + 1 - meta[2])):
                wup[j, at] = source[k, :tall]
                wdown[j, at] = source[k, tall:]
        gup[...] = jnp.zeros_like(gup)
        gdown[...] = jnp.zeros_like(gdown)
        gvec[...] = jnp.zeros_like(gvec)

    x1 = x1_ref[...]
    xhat, inv = norm_parts(x1)
    h2 = (xhat * vec[1:2] + vec[3:4]).astype(BF16)
    dyb = cot_ref[...]
    dy = dyb.astype(F32)
    f = x1 + vec[4:5]
    dh2 = jnp.zeros((tokens, width), F32)
    for j in range(VT):
        a, slope = gelu_both(dot(h2, wup[j], NN))
        a = a.astype(BF16)
        f = f + dot(a, wdown[j], NT)
        gdown[j] += dot(dyb, a, TN)
        du = (dot(dyb, wdown[j], NN) * slope).astype(BF16)
        gup[j] += dot(h2, du, TN)
        dh2 = dh2 + dot(du, wup[j], NT)
    y_ref[...] = f.astype(BF16)
    yfull_ref[...] = f.astype(BF16)
    dx1_ref[...] = dy + norm_back(dh2, xhat, inv, vec[1:2])
    gvec[1:2] += jnp.sum(dh2 * xhat, 0, keepdims=True)
    gvec[3:4] += jnp.sum(dh2, 0, keepdims=True)
    gvec[4:5] += jnp.sum(dy, 0, keepdims=True)

    @pl.when(step == last)
    def _():
        for m in range(CHIPS):
            k = fold(m) ^ meta[3]
            i, y = m // 2, m % 2
            at = slice(i * tall, (i + 1) * tall)
            mine, other = 2 * y + meta[2], 2 * y + 1 - meta[2]
            keep[k, :tall] = gup[mine, at]
            keep[k, tall:] = gdown[mine, at]
            send[k, :tall] = gup[other, at].astype(BF16)
            send[k, tall:] = gdown[other, at].astype(BF16)


def back_kernel(
    meta, x_ref, qkv_ref, prob_ref, o_ref, dx1_ref, wqkv, wout, vec, gvec_in,
    gx_ref, gxb_ref, keep, send,
    dqkv, gqkv, gout, gvec,
):
    step = pl.program_id(0)
    last = pl.num_programs(0) - 1
    tokens, width = x_ref.shape
    rows = tokens // WIN
    hs = width // HEADS
    scale = hs**-0.5

    @pl.when(step == 0)
    def _():
        gqkv[...] = jnp.zeros_like(gqkv)
        gout[...] = jnp.zeros_like(gout)
        gvec[...] = gvec_in[...]

    dx1 = dx1_ref[...]
    g = dx1.astype(BF16)
    gout[...] += dot(o_ref[...], g, TN)
    do = dot(g, wout[...], NT).astype(BF16)
    for r in range(rows):
        at = slice(r * WIN, (r + 1) * WIN)
        for h in range(HEADS):
            cols = [slice(part * width + h * hs, part * width + (h + 1) * hs) for part in range(3)]
            p = prob_ref[r * HEADS + h]
            doh = do[at, h * hs : (h + 1) * hs]
            dqkv[at, cols[2]] = dot(p, doh, TN).astype(BF16)
            dp = dot(doh, qkv_ref[at, cols[2]], NT)
            pf = p.astype(F32)
            ds = pf * (dp - jnp.sum(dp * pf, -1, keepdims=True)) * scale
            ds = ds.astype(BF16)
            dqkv[at, cols[0]] = dot(ds, qkv_ref[at, cols[1]], NN).astype(BF16)
            dqkv[at, cols[1]] = dot(ds, qkv_ref[at, cols[0]], TN).astype(BF16)
    xhat, inv = norm_parts(x_ref[...].astype(F32))
    h1 = (xhat * vec[0:1] + vec[2:3]).astype(BF16)
    gqkv[...] += dot(h1, dqkv[...], TN)
    dh1 = dot(dqkv[...], wqkv[...], NT)
    gx = dx1 + norm_back(dh1, xhat, inv, vec[0:1])
    gx_ref[...] = gx
    gxb_ref[...] = gx.astype(BF16)
    gvec[0:1] += jnp.sum(dh1 * xhat, 0, keepdims=True)
    gvec[2:3] += jnp.sum(dh1, 0, keepdims=True)

    @pl.when(step == last)
    def _():
        total = gvec[...]
        low = total.astype(BF16)
        for m in range(CHIPS):
            k = fold(m) ^ meta[3]
            mine = pl.ds(pl.multiple_of(m * 16 + 8 * meta[2], 8), 8)
            other = pl.ds(pl.multiple_of(m * 16 + 8 - 8 * meta[2], 8), 8)
            theirs = []
            for part in range(3):
                cols = slice(part * width, (part + 1) * width)
                keep[k, part * 8 : part * 8 + 8] = gqkv[mine, cols]
                theirs.append(gqkv[other, cols])
            keep[k, 24:32] = gout[mine]
            theirs.append(gout[other])
            send[k, :32] = jnp.concatenate(theirs, 0).astype(BF16)
            keep[k, 32:40] = total
            send[k, 32:40] = low


def place_kernel(meta, first, *refs):
    out = refs[-1]
    for n, source in enumerate(refs[:-1]):
        @pl.when(pl.program_id(0) == n)
        def _():
            out[...] = source[...].astype(out.dtype)


def finish_kernel(meta, keep, got, qkv, out, gains, biases, up, down):
    total = keep[...] + got[...].astype(F32)
    small, width = out.shape
    tall = up.shape[0]
    for part in range(3):
        qkv[:, part * width : (part + 1) * width] = total[part * small : (part + 1) * small]
    out[...] = total[3 * small : 4 * small]
    vec = total[4 * small : 4 * small + 8]
    vec = pltpu.roll(vec, width - meta[5] * small, 1)[:, :small]
    gains[...] = vec[:2]
    biases[...] = vec[2:5]
    at = 4 * small + 8
    up[...] = total[at : at + tall]
    down[...] = total[at + tall : at + 2 * tall]


def swap(block, axis, bit):
    size = lax.axis_size(axis)
    return lax.ppermute(block, axis, [(i, i ^ bit) for i in range(size)])


def steps_of(axis):
    return [(axis, 1 << k) for k in reversed(range(lax.axis_size(axis).bit_length() - 1))]


def gather(first, second):
    steps = steps_of("dp") + steps_of("tensor")
    one, two = first[None], second[None]
    for axis, bit in steps[:-1]:
        one = jnp.concatenate([one, swap(one, axis, bit)], 0)
        two = after(two, one)
        two = jnp.concatenate([two, swap(two, axis, bit)], 0)
    got_one = swap(one, *steps[-1])
    got_two = swap(after(two, got_one), *steps[-1])
    return one, got_one, two, got_two


def after(value, other):
    return lax.optimization_barrier((value, other))[0]


def halves(held):
    half = held.shape[0] // 2
    return held[:half], held[half:].astype(BF16)


def fold_step(keep, send, axis, bit):
    return keep + swap(send, axis, bit).astype(F32)


def bit_reverse(index, count):
    out = 0 * index
    for k in range(count):
        out = out | (((index >> k) & 1) << (count - 1 - k))
    return out


def by_device(held, got, me):
    blocks = jnp.concatenate([held, got], 0)
    count = blocks.shape[0]
    order = jnp.arange(count, dtype=jnp.int32) ^ me
    return jnp.take(blocks, bit_reverse(order, count.bit_length() - 1), axis=0)


def other_pack(w_qkv, w_out, gains, biases, w_up, w_down, me):
    small, width = w_out.shape
    qkv = w_qkv.reshape(small, 3, width).transpose(1, 0, 2).reshape(3 * small, width)
    rows = jnp.concatenate([gains, biases], 0)
    place = jnp.zeros((8, width), BF16)
    place = lax.dynamic_update_slice(place, rows, (jnp.int32(0), me * small))
    return jnp.concatenate([qkv, w_out, place], 0), jnp.concatenate([w_up, w_down.T], 0)


def other_blocks(pair_a, pair_b, me, n_dp, n_t):
    a = by_device(*pair_a, me)
    b = by_device(*pair_b, me)
    width = a.shape[2]
    count = n_dp * n_t
    small = width // count
    big = width // (VDP * VT)
    mats = a[:, : 4 * small].reshape(count, 4, small, width).transpose(1, 0, 2, 3)
    mats = mats.reshape(4, VDP * VT, big, width).transpose(1, 0, 2, 3).reshape(VDP * VT, 4 * big, width)
    vec = jnp.sum(a[:, 4 * small :].astype(F32), 0).astype(BF16)
    vecs = jnp.concatenate([vec[None], jnp.zeros((VDP * VT - 1, 8, width), BF16)], 0)
    a = jnp.concatenate([mats, vecs], 1)
    tall = width // n_dp
    b = b.reshape(n_dp, VT, 2, tall, width).transpose(1, 2, 0, 3, 4)
    b = b.reshape(VT, 2, VDP, width // VDP, width).transpose(2, 0, 1, 3, 4)
    b = b.reshape(VDP * VT, 2 * (width // VDP), width)
    order = [flip(m) for m in range(CHIPS)]

    def halves(blocks):
        pairs = blocks.reshape((CHIPS, 2) + blocks.shape[1:])
        pairs = jnp.stack([pairs[m] for m in order], 0)
        return pairs[:, 0], pairs[:, 1]

    return halves(a) + halves(b)


def other_reduce(pair_a, pair_b, me, n_dp, n_t):
    order = [fold(m) for m in range(CHIPS)]
    count = n_dp * n_t

    def whole(keep, send):
        pairs = jnp.stack([keep, send.astype(F32)], 1)
        pairs = jnp.stack([pairs[k] for k in order], 0)
        return pairs.reshape((VDP * VT,) + keep.shape[1:])

    a, b = whole(*pair_a), whole(*pair_b)
    width = a.shape[2]
    small, tall = width // count, width // n_dp
    big = width // (VDP * VT)
    mats = a[:, : 4 * big].reshape(VDP * VT, 4, big, width).transpose(1, 0, 2, 3)
    mats = mats.reshape(4, count, small, width).transpose(1, 0, 2, 3)
    mats = mats.reshape(count, 4 * small, width)
    a = jnp.concatenate([mats, jnp.broadcast_to(a[:1, 4 * big :], (count, 8, width))], 1)
    b = b.reshape(VDP, VT, 2, width // VDP, width).transpose(1, 2, 0, 3, 4)
    b = b.reshape(VT, 2, n_dp, tall, width).transpose(2, 0, 1, 3, 4)
    b = b.reshape(count, 2 * tall, width)
    results = []
    for blocks in (a, b):
        blocks = jnp.take(blocks, jnp.arange(count, dtype=jnp.int32) ^ me, axis=0)
        for axis, bit in reversed(steps_of("dp") + steps_of("tensor")):
            pairs = blocks.reshape((-1, 2) + blocks.shape[1:])
            got = swap(pairs[:, 1].astype(BF16), axis, bit)
            blocks = pairs[:, 0] + got.astype(F32)
        results.append(blocks[0])
    return results


def const_spec(shape):
    zeros = (0,) * len(shape)
    return pl.BlockSpec(shape, lambda i, *_: zeros)


def struct(shape, dtype):
    return jax.ShapeDtypeStruct(shape, dtype)


def call(kernel, name, grid, prefetch, ins, outs, scratch, flops, limit):
    args = [a for a, _ in ins]
    moved = sum(a.size * a.dtype.itemsize for a in args)
    moved += sum(s.size * s.dtype.itemsize for s, _ in outs)
    return pl.pallas_call(
        kernel,
        name=name,
        out_shape=[s for s, _ in outs],
        grid_spec=pltpu.PrefetchScalarGridSpec(
            num_scalar_prefetch=len(prefetch),
            grid=grid,
            in_specs=[spec for _, spec in ins],
            out_specs=[spec for _, spec in outs],
            scratch_shapes=scratch,
        ),
        compiler_params=pltpu.CompilerParams(vmem_limit_bytes=limit * MIB),
        cost_estimate=pl.CostEstimate(flops=flops, bytes_accessed=moved, transcendentals=0),
    )(*prefetch, *args)


def pack(meta, w_qkv, w_out, gains, biases, w_up, w_down):
    small, width = w_out.shape
    tall = w_up.shape[0]
    return pl.pallas_call(
        pack_kernel,
        name="pack",
        out_shape=[
            pltpu.VMEM((4 * small + 8, width), BF16),
            pltpu.VMEM((2 * tall, width), BF16),
        ],
        in_specs=[pl.BlockSpec(memory_space=pltpu.SMEM)] + [pl.BlockSpec(memory_space=pltpu.VMEM)] * 6,
        out_specs=[pl.BlockSpec(memory_space=pltpu.VMEM)] * 2,
    )(meta, w_qkv, w_out, gains, biases, w_up, w_down.T)


def finish(meta, keep, got, small, tall):
    width = keep.shape[1]
    shapes = [(small, 3 * width), (small, width), (2, small), (3, small), (tall, width), (tall, width)]
    vmem = pl.BlockSpec(memory_space=pltpu.VMEM)
    return pl.pallas_call(
        finish_kernel,
        name="finish",
        out_shape=[struct(shape, F32) for shape in shapes],
        in_specs=[pl.BlockSpec(memory_space=pltpu.SMEM), vmem, vmem],
        out_specs=[vmem] * 6,
    )(meta, keep, got)


def on_device(tokens, lengths, row_mask, cotangent, w_qkv, w_out, gains, biases, w_up, w_down):
    images, seq_len, width = tokens.shape
    n_dp, n_t = lax.axis_size("dp"), lax.axis_size("tensor")
    t_id = lax.axis_index("tensor")
    me = lax.axis_index("dp") * n_t + t_id
    chip = me // 2
    small = width // (n_dp * n_t)
    tall = width // n_dp
    usual = (n_dp, n_t) == (VDP, VT)
    zero = jnp.int32(0)
    if usual:
        meta = jnp.stack([t_id, flip(chip), me % 2, fold(chip), zero, me]).astype(jnp.int32)
    else:
        meta = jnp.stack([t_id, zero, zero, zero, zero, me]).astype(jnp.int32)
    weights = (w_qkv, w_out, gains, biases, w_up, w_down)
    packs = pack(meta, *weights) if usual else other_pack(*weights, me)
    held_a, got_a, held_b, got_b = gather(*packs)
    if not usual:
        held_a, got_a, held_b, got_b = other_blocks((held_a, got_a), (held_b, got_b), me, n_dp, n_t)

    own = images * seq_len // n_t
    rows = own // WIN
    per = 4 if rows % 4 == 0 else 1
    chunk = per * WIN
    grid = (rows // per,)
    steps = grid[0]
    hs = width // HEADS
    ff = w_up.shape[1] * n_t
    flat = tokens.reshape(images * seq_len, width)
    flat_cot = cotangent.reshape(images * seq_len, width)
    picked = pl.BlockSpec((chunk, width), lambda i, meta, *_: (meta[0] * steps + i, 0))

    def tiles(*shape):
        tail = (0,) * (len(shape) - 1)
        return pl.BlockSpec(shape, lambda i, *_: (i,) + tail)

    blocks_a = const_spec(held_a.shape)
    blocks_b = const_spec(held_b.shape)
    token_mm = 2 * own * width
    qkv, prob, o, x1, wqkv, wout, vec = call(
        attend_kernel,
        "attend",
        grid,
        (meta, lengths, row_mask),
        [(flat, picked), (held_a, blocks_a), (got_a, blocks_a)],
        [
            (struct((own, 3 * width), BF16), tiles(chunk, 3 * width)),
            (struct((rows * HEADS, WIN, WIN), BF16), tiles(per * HEADS, WIN, WIN)),
            (struct((own, width), BF16), tiles(chunk, width)),
            (struct((own, width), F32), tiles(chunk, width)),
            (struct((width, 3 * width), BF16), const_spec((width, 3 * width))),
            (struct((width, width), BF16), const_spec((width, width))),
            (struct((8, width), F32), const_spec((8, width))),
        ],
        [],
        token_mm * (4 * width + 2 * WIN),
        32,
    )
    big = (CHIPS, 2 * (width // VDP), width)
    y, y_full, dx1, gvec, keep_b, send_b = call(
        hidden_kernel,
        "hidden",
        grid,
        (meta,),
        [
            (x1, tiles(chunk, width)),
            (flat_cot, picked),
            (held_b, blocks_b),
            (got_b, blocks_b),
            (vec, const_spec((8, width))),
        ],
        [
            (struct((own, width), BF16), tiles(chunk, width)),
            (struct((images * seq_len, width), BF16), picked),
            (struct((own, width), F32), tiles(chunk, width)),
            (struct((8, width), F32), const_spec((8, width))),
            (struct(big, F32), const_spec(big)),
            (struct(big, BF16), const_spec(big)),
        ],
        [
            pltpu.VMEM((VT, width, ff // VT), BF16),
            pltpu.VMEM((VT, width, ff // VT), BF16),
            pltpu.VMEM((VT, width, ff // VT), F32),
            pltpu.VMEM((VT, width, ff // VT), F32),
        ],
        token_mm * 6 * ff,
        40,
    )
    y_far = swap(y, "tensor", 2)
    y_near = swap(y, "tensor", 1)
    fold_steps = [("dp", b // 2) if b > 1 else ("tensor", 2) for b in REDUCE_BITS]
    if usual:
        held_b = fold_step(keep_b, send_b, "tensor", 1)
        keep_b, send_b = halves(held_b)
        got_b = swap(send_b, *fold_steps[0])
    little = (CHIPS, 40, width)
    gx, gxb, keep_a, send_a = call(
        back_kernel,
        "back",
        grid,
        (meta,),
        [
            (flat, picked),
            (qkv, tiles(chunk, 3 * width)),
            (prob, tiles(per * HEADS, WIN, WIN)),
            (o, tiles(chunk, width)),
            (dx1, tiles(chunk, width)),
            (wqkv, const_spec((width, 3 * width))),
            (wout, const_spec((width, width))),
            (vec, const_spec((8, width))),
            (gvec, const_spec((8, width))),
        ],
        [
            (struct((images * seq_len, width), F32), picked),
            (struct((own, width), BF16), tiles(chunk, width)),
            (struct(little, F32), const_spec(little)),
            (struct(little, BF16), const_spec(little)),
        ],
        [
            pltpu.VMEM((chunk, 3 * width), BF16),
            pltpu.VMEM((width, 3 * width), F32),
            pltpu.VMEM((width, width), F32),
            pltpu.VMEM((8, width), F32),
        ],
        token_mm * (8 * width + 5 * WIN),
        32,
    )
    if usual:
        held_b = keep_b + got_b.astype(F32)
        send_a = after(after(send_a, held_b), y_far)
        held_a = fold_step(keep_a, send_a, "tensor", 1)
        held_a = fold_step(*halves(held_a), *fold_steps[0])
        held = jnp.concatenate([held_a, held_b], 1)
        for axis, bit in fold_steps[1:-1]:
            held = fold_step(*halves(held), axis, bit)
        keep, send = halves(held)
        o_qkv, o_out, o_gains, o_bias, o_up, o_down = finish(
            meta, keep[0], swap(send, *fold_steps[-1])[0], small, tall
        )
    else:
        grad_a, grad_b = other_reduce((keep_a, send_a), (keep_b, send_b), me, n_dp, n_t)
        o_qkv = jnp.concatenate([grad_a[p * small : (p + 1) * small] for p in range(3)], 1)
        o_out = grad_a[3 * small : 4 * small]
        o_vec = lax.dynamic_slice_in_dim(grad_a[4 * small : 4 * small + 5], me * small, small, 1)
        o_gains, o_bias = o_vec[:2], o_vec[2:]
        o_up, o_down = grad_b[:tall], grad_b[tall:]

    def spread(near, far, full):
        sources = [near, far, swap(far, "tensor", 1)]
        whole = pl.BlockSpec((own, width), lambda i, meta: (0, 0))
        return pl.pallas_call(
            place_kernel,
            name="place",
            out_shape=struct(full.shape, full.dtype),
            grid_spec=pltpu.PrefetchScalarGridSpec(
                num_scalar_prefetch=1,
                grid=(n_t - 1,),
                in_specs=[pl.BlockSpec(memory_space=pl.ANY)] + [whole] * 3,
                out_specs=pl.BlockSpec((own, width), lambda i, meta: (meta[0] ^ (i + 1), 0)),
            ),
            input_output_aliases={1: 0},
            compiler_params=pltpu.CompilerParams(vmem_limit_bytes=32 * MIB),
        )(meta, full, *sources).reshape(images, seq_len, width)

    layer_out = spread(y_near, y_far, y_full)
    gx_near = swap(after(gxb, y_near), "tensor", 1)
    gx_far = swap(after(gxb, y_far), "tensor", 2)
    grad_tokens = spread(gx_near, gx_far, gx)
    return layer_out, grad_tokens, o_qkv, o_out, o_gains, o_bias, o_up, o_down.T


def solution(mesh):
    in_specs = (
        P("dp", None, None),
        P("dp"),
        P("dp", None),
        P("dp", None, None),
        P(("dp", "tensor"), None),
        P(("dp", "tensor"), None),
        P(None, ("dp", "tensor")),
        P(None, ("dp", "tensor")),
        P("dp", "tensor"),
        P("tensor", "dp"),
    )
    out_specs = (
        P("dp", None, None),
        P("dp", None, None),
        P(("dp", "tensor"), None),
        P(("dp", "tensor"), None),
        P(None, ("dp", "tensor")),
        P(None, ("dp", "tensor")),
        P("dp", "tensor"),
        P("tensor", "dp"),
    )
    return jax.shard_map(
        on_device, mesh=mesh, in_specs=in_specs, out_specs=out_specs, check_vma=False
    )
```

```python
import functools

import jax
import jax.numpy as jnp
from jax import lax
from jax.experimental import pallas as pl
from jax.experimental.pallas import tpu as pltpu
from jax.sharding import PartitionSpec as P

HEADS = 2
WIN = 96
F32 = jnp.float32
BF16 = jnp.bfloat16
VDP, VT = 8, 4
CHIPS = VDP * VT // 2
REDUCE_BITS = (1, 8, 4, 2)
MIB = 1 << 20

NN = ((1,), (0,))
NT = ((1,), (1,))
TN = ((0,), (0,))


def dot(a, b, dims):
    return lax.dot_general(a, b, (dims, ((), ())), preferred_element_type=F32)


def flip(m):
    return ((m & 1) << 3) | ((m & 2) << 1) | ((m & 4) >> 1) | ((m & 8) >> 3)


def fold(m):
    out = 0
    for place, bit in enumerate(REDUCE_BITS):
        shift = 3 - place
        out = out | (((m // bit) & 1) << shift)
    return out


def norm_parts(values):
    center = values - jnp.mean(values, -1, keepdims=True)
    inv = lax.rsqrt(jnp.mean(center * center, -1, keepdims=True) + 1e-05)
    return center * inv, inv


def norm_back(grad, xhat, inv, gain):
    scaled = grad * gain
    return inv * (
        scaled
        - jnp.mean(scaled, -1, keepdims=True)
        - xhat * jnp.mean(scaled * xhat, -1, keepdims=True)
    )


def gelu_both(u):
    c = 0.7978845608028654
    u2 = u * u
    t = jnp.tanh(u * (c + (c * 0.044715) * u2))
    half = 0.5 + 0.5 * t
    slope = half + (u * (half * (1.0 - t))) * (c + (3 * c * 0.044715) * u2)
    return u * half, slope


def pack_kernel(meta, qkv, out, gains, biases, up, down, small_ref, big_ref):
    width = out.shape[1]
    small = out.shape[0]
    for part in range(3):
        small_ref[part * small : (part + 1) * small] = qkv[:, part * width : (part + 1) * width]
    small_ref[3 * small : 4 * small] = out[...]
    small_ref[4 * small : 4 * small + 8] = jnp.zeros((8, width), BF16)
    lane = lax.broadcasted_iota(jnp.int32, (1, width), 1)
    mine = lane // small == meta[5]
    rows = [gains[0:1], gains[1:2], biases[0:1], biases[1:2], biases[2:3]]
    vals = jnp.concatenate(rows + [jnp.zeros((3, small), BF16)], 0).astype(F32)
    wide = jnp.concatenate([vals] * (width // small), 1)
    small_ref[4 * small : 4 * small + 8] = jnp.where(mine, wide, 0.0).astype(BF16)
    tall = up.shape[0]
    big_ref[:tall] = up[...]
    big_ref[tall:] = down[...]


def attend_kernel(
    meta, lens, live, x_ref, held, got, qkv_ref, prob_ref, o_ref, x1_ref, wqkv, wout, vec
):
    step = pl.program_id(0)
    tokens, width = x_ref.shape
    rows = tokens // WIN
    hs = width // HEADS

    @pl.when(step == 0)
    def _():
        first = meta[2] == 0
        total = jnp.zeros((8, width), F32)
        for m in range(CHIPS):
            k = fold(m) ^ meta[3]
            a = held[k].astype(F32)
            b = got[k].astype(F32)
            even = jnp.where(first, a, b)
            odd = jnp.where(first, b, a)
            for part in range(3):
                both = jnp.concatenate([even[part * 8 : part * 8 + 8], odd[part * 8 : part * 8 + 8]], 0)
                wqkv[m * 16 : m * 16 + 16, part * width : (part + 1) * width] = both.astype(BF16)
            both = jnp.concatenate([even[24:32], odd[24:32]], 0)
            wout[m * 16 : m * 16 + 16] = both.astype(BF16)
            total = total + a[32:40] + b[32:40]
        vec[...] = total

    x = x_ref[...].astype(F32)
    xhat, _ = norm_parts(x)
    h1 = (xhat * vec[0:1] + vec[2:3]).astype(BF16)
    qkv_ref[...] = dot(h1, wqkv[...], NN).astype(BF16)
    scale = hs**-0.5
    ii = lax.broadcasted_iota(jnp.int32, (WIN, WIN), 0)
    jj = lax.broadcasted_iota(jnp.int32, (WIN, WIN), 1)
    same = ii == jj
    image_rows = live.shape[1]
    for r in range(rows):
        row = (meta[0] * pl.num_programs(0) + step) * rows + r
        image = row // image_rows
        inside = row - image * image_rows
        reach = jnp.where(live[image, inside] == 1, lens[image] - inside * WIN, 0)
        allowed = same | (jj < jnp.minimum(ii, reach))
        at = slice(r * WIN, (r + 1) * WIN)
        for h in range(HEADS):
            q = qkv_ref[at, h * hs : (h + 1) * hs]
            k = qkv_ref[at, width + h * hs : width + (h + 1) * hs]
            v = qkv_ref[at, 2 * width + h * hs : 2 * width + (h + 1) * hs]
            s = jnp.where(allowed, dot(q, k, NT) * scale, -1e30)
            e = jnp.exp(s - jnp.max(s, -1, keepdims=True))
            p = (e / jnp.sum(e, -1, keepdims=True)).astype(BF16)
            prob_ref[r * HEADS + h] = p
            o_ref[at, h * hs : (h + 1) * hs] = dot(p, v, NN).astype(BF16)
    x1_ref[...] = x + dot(o_ref[...], wout[...], NN)


def hidden_kernel(
    meta, x1_ref, cot_ref, held, got, vec, y_ref, yfull_ref, dx1_ref, gvec, keep, send,
    wup, wdown, gup, gdown,
):
    step = pl.program_id(0)
    last = pl.num_programs(0) - 1
    tokens, width = x1_ref.shape
    tall = width // VDP

    @pl.when(step == 0)
    def _():
        for m in range(CHIPS):
            k = flip(m) ^ meta[1]
            i, y = m // 2, m % 2
            at = slice(i * tall, (i + 1) * tall)
            for source, j in ((held, 2 * y + meta[2]), (got, 2 * y + 1 - meta[2])):
                wup[j, at] = source[k, :tall]
                wdown[j, at] = source[k, tall:]
        gup[...] = jnp.zeros_like(gup)
        gdown[...] = jnp.zeros_like(gdown)
        gvec[...] = jnp.zeros_like(gvec)

    x1 = x1_ref[...]
    xhat, inv = norm_parts(x1)
    h2 = (xhat * vec[1:2] + vec[3:4]).astype(BF16)
    dyb = cot_ref[...]
    dy = dyb.astype(F32)
    f = x1 + vec[4:5]
    dh2 = jnp.zeros((tokens, width), F32)
    for j in range(VT):
        a, slope = gelu_both(dot(h2, wup[j], NN))
        a = a.astype(BF16)
        f = f + dot(a, wdown[j], NT)
        gdown[j] += dot(dyb, a, TN)
        du = (dot(dyb, wdown[j], NN) * slope).astype(BF16)
        gup[j] += dot(h2, du, TN)
        dh2 = dh2 + dot(du, wup[j], NT)
    y_ref[...] = f.astype(BF16)
    yfull_ref[...] = f.astype(BF16)
    dx1_ref[...] = dy + norm_back(dh2, xhat, inv, vec[1:2])
    gvec[1:2] += jnp.sum(dh2 * xhat, 0, keepdims=True)
    gvec[3:4] += jnp.sum(dh2, 0, keepdims=True)
    gvec[4:5] += jnp.sum(dy, 0, keepdims=True)

    @pl.when(step == last)
    def _():
        for m in range(CHIPS):
            k = fold(m) ^ meta[3]
            i, y = m // 2, m % 2
            at = slice(i * tall, (i + 1) * tall)
            mine, other = 2 * y + meta[2], 2 * y + 1 - meta[2]
            keep[k, :tall] = gup[mine, at]
            keep[k, tall:] = gdown[mine, at]
            send[k, :tall] = gup[other, at].astype(BF16)
            send[k, tall:] = gdown[other, at].astype(BF16)


def back_kernel(
    meta, x_ref, qkv_ref, prob_ref, o_ref, dx1_ref, wqkv, wout, vec, gvec_in,
    gx_ref, gxb_ref, keep, send,
    dqkv, gqkv, gout, gvec,
):
    step = pl.program_id(0)
    last = pl.num_programs(0) - 1
    tokens, width = x_ref.shape
    rows = tokens // WIN
    hs = width // HEADS
    scale = hs**-0.5

    @pl.when(step == 0)
    def _():
        gqkv[...] = jnp.zeros_like(gqkv)
        gout[...] = jnp.zeros_like(gout)
        gvec[...] = gvec_in[...]

    dx1 = dx1_ref[...]
    g = dx1.astype(BF16)
    gout[...] += dot(o_ref[...], g, TN)
    do = dot(g, wout[...], NT).astype(BF16)
    for r in range(rows):
        at = slice(r * WIN, (r + 1) * WIN)
        for h in range(HEADS):
            cols = [slice(part * width + h * hs, part * width + (h + 1) * hs) for part in range(3)]
            p = prob_ref[r * HEADS + h]
            doh = do[at, h * hs : (h + 1) * hs]
            dqkv[at, cols[2]] = dot(p, doh, TN).astype(BF16)
            dp = dot(doh, qkv_ref[at, cols[2]], NT)
            pf = p.astype(F32)
            ds = pf * (dp - jnp.sum(dp * pf, -1, keepdims=True)) * scale
            ds = ds.astype(BF16)
            dqkv[at, cols[0]] = dot(ds, qkv_ref[at, cols[1]], NN).astype(BF16)
            dqkv[at, cols[1]] = dot(ds, qkv_ref[at, cols[0]], TN).astype(BF16)
    xhat, inv = norm_parts(x_ref[...].astype(F32))
    h1 = (xhat * vec[0:1] + vec[2:3]).astype(BF16)
    gqkv[...] += dot(h1, dqkv[...], TN)
    dh1 = dot(dqkv[...], wqkv[...], NT)
    gx = dx1 + norm_back(dh1, xhat, inv, vec[0:1])
    gx_ref[...] = gx
    gxb_ref[...] = gx.astype(BF16)
    gvec[0:1] += jnp.sum(dh1 * xhat, 0, keepdims=True)
    gvec[2:3] += jnp.sum(dh1, 0, keepdims=True)

    @pl.when(step == last)
    def _():
        total = gvec[...]
        low = total.astype(BF16)
        for m in range(CHIPS):
            k = fold(m) ^ meta[3]
            mine = pl.ds(pl.multiple_of(m * 16 + 8 * meta[2], 8), 8)
            other = pl.ds(pl.multiple_of(m * 16 + 8 - 8 * meta[2], 8), 8)
            theirs = []
            for part in range(3):
                cols = slice(part * width, (part + 1) * width)
                keep[k, part * 8 : part * 8 + 8] = gqkv[mine, cols]
                theirs.append(gqkv[other, cols])
            keep[k, 24:32] = gout[mine]
            theirs.append(gout[other])
            send[k, :32] = jnp.concatenate(theirs, 0).astype(BF16)
            keep[k, 32:40] = total
            send[k, 32:40] = low


def place_kernel(meta, first, *refs):
    out = refs[-1]
    for n, source in enumerate(refs[:-1]):
        @pl.when(pl.program_id(0) == n)
        def _():
            out[...] = source[...].astype(out.dtype)


def finish_kernel(meta, got, qkv, out, gains, biases, up, down):
    total = got[0].astype(F32)
    for n in range(1, got.shape[0]):
        total = total + got[n].astype(F32)
    small, width = out.shape
    tall = up.shape[0]
    for part in range(3):
        qkv[:, part * width : (part + 1) * width] = total[part * small : (part + 1) * small]
    out[...] = total[3 * small : 4 * small]
    vec = total[4 * small : 4 * small + 8]
    vec = pltpu.roll(vec, width - meta[5] * small, 1)[:, :small]
    gains[...] = vec[:2]
    biases[...] = vec[2:5]
    at = 4 * small + 8
    up[...] = total[at : at + tall]
    down[...] = total[at + tall : at + 2 * tall]


def swap(block, axis, bit):
    size = lax.axis_size(axis)
    return lax.ppermute(block, axis, [(i, i ^ bit) for i in range(size)])


def steps_of(axis):
    return [(axis, 1 << k) for k in reversed(range(lax.axis_size(axis).bit_length() - 1))]


def gather(first, second):
    two = second[None]
    one = lax.all_to_all(jnp.stack([first] * lax.axis_size("dp"), 0), "dp", 0, 0)
    for n, (axis, bit) in enumerate(steps_of("dp")):
        two = jnp.concatenate([two, swap(two, axis, bit)], 0)
        if n == 0:
            two = after(two, one)
    *most, last = steps_of("tensor")
    for axis, bit in most:
        one = jnp.concatenate([one, swap(one, axis, bit)], 0)
        two = after(two, one)
        two = jnp.concatenate([two, swap(two, axis, bit)], 0)
    got_one = swap(one, *last)
    got_two = swap(after(two, got_one), *last)
    return one, got_one, two, got_two


def after(value, other):
    return lax.optimization_barrier((value, other))[0]


def halves(held):
    half = held.shape[0] // 2
    return held[:half], held[half:].astype(BF16)


def fold_step(keep, send, axis, bit):
    return keep + swap(send, axis, bit).astype(F32)


def bit_reverse(index, count):
    out = 0 * index
    for k in range(count):
        out = out | (((index >> k) & 1) << (count - 1 - k))
    return out


def by_device(held, got, me, n_dp, n_t, direct):
    blocks = jnp.concatenate([held, got], 0)
    bits_dp, bits_t = n_dp.bit_length() - 1, n_t.bit_length() - 1
    index = jnp.arange(n_dp * n_t, dtype=jnp.int32)
    far, near = index // n_t, (index ^ me) % n_t
    if not direct:
        far = bit_reverse(far ^ (me // n_t), bits_dp)
    return jnp.take(blocks, bit_reverse(near, bits_t) * n_dp + far, axis=0)


def other_pack(w_qkv, w_out, gains, biases, w_up, w_down, me):
    small, width = w_out.shape
    qkv = w_qkv.reshape(small, 3, width).transpose(1, 0, 2).reshape(3 * small, width)
    rows = jnp.concatenate([gains, biases], 0)
    place = jnp.zeros((8, width), BF16)
    place = lax.dynamic_update_slice(place, rows, (jnp.int32(0), me * small))
    return jnp.concatenate([qkv, w_out, place], 0), jnp.concatenate([w_up, w_down.T], 0)


def other_blocks(pair_a, pair_b, me, n_dp, n_t):
    a = by_device(*pair_a, me, n_dp, n_t, True)
    b = by_device(*pair_b, me, n_dp, n_t, False)
    width = a.shape[2]
    count = n_dp * n_t
    small = width // count
    big = width // (VDP * VT)
    mats = a[:, : 4 * small].reshape(count, 4, small, width).transpose(1, 0, 2, 3)
    mats = mats.reshape(4, VDP * VT, big, width).transpose(1, 0, 2, 3).reshape(VDP * VT, 4 * big, width)
    vec = jnp.sum(a[:, 4 * small :].astype(F32), 0).astype(BF16)
    vecs = jnp.concatenate([vec[None], jnp.zeros((VDP * VT - 1, 8, width), BF16)], 0)
    a = jnp.concatenate([mats, vecs], 1)
    tall = width // n_dp
    b = b.reshape(n_dp, VT, 2, tall, width).transpose(1, 2, 0, 3, 4)
    b = b.reshape(VT, 2, VDP, width // VDP, width).transpose(2, 0, 1, 3, 4)
    b = b.reshape(VDP * VT, 2 * (width // VDP), width)

    def placed(blocks, place):
        pairs = blocks.reshape((CHIPS, 2) + blocks.shape[1:])
        pairs = jnp.stack([pairs[m] for m in sorted(range(CHIPS), key=place)], 0)
        return pairs[:, 0], pairs[:, 1]

    return placed(a, fold) + placed(b, flip)


def other_reduce(pair_a, pair_b, me, n_dp, n_t):
    order = [fold(m) for m in range(CHIPS)]
    count = n_dp * n_t

    def whole(keep, send):
        pairs = jnp.stack([keep, send.astype(F32)], 1)
        pairs = jnp.stack([pairs[k] for k in order], 0)
        return pairs.reshape((VDP * VT,) + keep.shape[1:])

    a, b = whole(*pair_a), whole(*pair_b)
    width = a.shape[2]
    small, tall = width // count, width // n_dp
    big = width // (VDP * VT)
    mats = a[:, : 4 * big].reshape(VDP * VT, 4, big, width).transpose(1, 0, 2, 3)
    mats = mats.reshape(4, count, small, width).transpose(1, 0, 2, 3)
    mats = mats.reshape(count, 4 * small, width)
    a = jnp.concatenate([mats, jnp.broadcast_to(a[:1, 4 * big :], (count, 8, width))], 1)
    b = b.reshape(VDP, VT, 2, width // VDP, width).transpose(1, 2, 0, 3, 4)
    b = b.reshape(VT, 2, n_dp, tall, width).transpose(2, 0, 1, 3, 4)
    b = b.reshape(count, 2 * tall, width)
    results = []
    for blocks in (a, b):
        blocks = jnp.take(blocks, jnp.arange(count, dtype=jnp.int32) ^ me, axis=0)
        for axis, bit in reversed(steps_of("dp") + steps_of("tensor")):
            pairs = blocks.reshape((-1, 2) + blocks.shape[1:])
            got = swap(pairs[:, 1].astype(BF16), axis, bit)
            blocks = pairs[:, 0] + got.astype(F32)
        results.append(blocks[0])
    return results


def const_spec(shape):
    zeros = (0,) * len(shape)
    return pl.BlockSpec(shape, lambda i, *_: zeros)


def struct(shape, dtype):
    return jax.ShapeDtypeStruct(shape, dtype)


def call(kernel, name, grid, prefetch, ins, outs, scratch, flops, limit):
    args = [a for a, _ in ins]
    moved = sum(a.size * a.dtype.itemsize for a in args)
    moved += sum(s.size * s.dtype.itemsize for s, _ in outs)
    return pl.pallas_call(
        kernel,
        name=name,
        out_shape=[s for s, _ in outs],
        grid_spec=pltpu.PrefetchScalarGridSpec(
            num_scalar_prefetch=len(prefetch),
            grid=grid,
            in_specs=[spec for _, spec in ins],
            out_specs=[spec for _, spec in outs],
            scratch_shapes=scratch,
        ),
        compiler_params=pltpu.CompilerParams(vmem_limit_bytes=limit * MIB),
        cost_estimate=pl.CostEstimate(flops=flops, bytes_accessed=moved, transcendentals=0),
    )(*prefetch, *args)


def pack(meta, w_qkv, w_out, gains, biases, w_up, w_down):
    small, width = w_out.shape
    tall = w_up.shape[0]
    return pl.pallas_call(
        pack_kernel,
        name="pack",
        out_shape=[
            pltpu.VMEM((4 * small + 8, width), BF16),
            pltpu.VMEM((2 * tall, width), BF16),
        ],
        in_specs=[pl.BlockSpec(memory_space=pltpu.SMEM)] + [pl.BlockSpec(memory_space=pltpu.VMEM)] * 6,
        out_specs=[pl.BlockSpec(memory_space=pltpu.VMEM)] * 2,
    )(meta, w_qkv, w_out, gains, biases, w_up, w_down.T)


def finish(meta, got, small, tall):
    width = got.shape[2]
    shapes = [(small, 3 * width), (small, width), (2, small), (3, small), (tall, width), (tall, width)]
    vmem = pl.BlockSpec(memory_space=pltpu.VMEM)
    return pl.pallas_call(
        finish_kernel,
        name="finish",
        out_shape=[struct(shape, F32) for shape in shapes],
        in_specs=[pl.BlockSpec(memory_space=pltpu.SMEM), vmem],
        out_specs=[vmem] * 6,
    )(meta, got)


def on_device(tokens, lengths, row_mask, cotangent, w_qkv, w_out, gains, biases, w_up, w_down):
    images, seq_len, width = tokens.shape
    n_dp, n_t = lax.axis_size("dp"), lax.axis_size("tensor")
    t_id = lax.axis_index("tensor")
    me = lax.axis_index("dp") * n_t + t_id
    chip = me // 2
    small = width // (n_dp * n_t)
    tall = width // n_dp
    usual = (n_dp, n_t) == (VDP, VT)
    zero = jnp.int32(0)
    if usual:
        meta = jnp.stack([t_id, flip(chip), me % 2, fold(chip) & 8, zero, me]).astype(jnp.int32)
    else:
        meta = jnp.stack([t_id, zero, zero, zero, zero, me]).astype(jnp.int32)
    weights = (w_qkv, w_out, gains, biases, w_up, w_down)
    packs = pack(meta, *weights) if usual else other_pack(*weights, me)
    held_a, got_a, held_b, got_b = gather(*packs)
    if not usual:
        held_a, got_a, held_b, got_b = other_blocks((held_a, got_a), (held_b, got_b), me, n_dp, n_t)

    own = images * seq_len // n_t
    rows = own // WIN
    per = 4 if rows % 4 == 0 else 1
    chunk = per * WIN
    grid = (rows // per,)
    steps = grid[0]
    hs = width // HEADS
    ff = w_up.shape[1] * n_t
    flat = tokens.reshape(images * seq_len, width)
    flat_cot = cotangent.reshape(images * seq_len, width)
    picked = pl.BlockSpec((chunk, width), lambda i, meta, *_: (meta[0] * steps + i, 0))

    def tiles(*shape):
        tail = (0,) * (len(shape) - 1)
        return pl.BlockSpec(shape, lambda i, *_: (i,) + tail)

    blocks_a = const_spec(held_a.shape)
    blocks_b = const_spec(held_b.shape)
    token_mm = 2 * own * width
    qkv, prob, o, x1, wqkv, wout, vec = call(
        attend_kernel,
        "attend",
        grid,
        (meta, lengths, row_mask),
        [(flat, picked), (held_a, blocks_a), (got_a, blocks_a)],
        [
            (struct((own, 3 * width), BF16), tiles(chunk, 3 * width)),
            (struct((rows * HEADS, WIN, WIN), BF16), tiles(per * HEADS, WIN, WIN)),
            (struct((own, width), BF16), tiles(chunk, width)),
            (struct((own, width), F32), tiles(chunk, width)),
            (struct((width, 3 * width), BF16), const_spec((width, 3 * width))),
            (struct((width, width), BF16), const_spec((width, width))),
            (struct((8, width), F32), const_spec((8, width))),
        ],
        [],
        token_mm * (4 * width + 2 * WIN),
        32,
    )
    big = (CHIPS, 2 * (width // VDP), width)
    y, y_full, dx1, gvec, keep_b, send_b = call(
        hidden_kernel,
        "hidden",
        grid,
        (meta,),
        [
            (x1, tiles(chunk, width)),
            (flat_cot, picked),
            (held_b, blocks_b),
            (got_b, blocks_b),
            (vec, const_spec((8, width))),
        ],
        [
            (struct((own, width), BF16), tiles(chunk, width)),
            (struct((images * seq_len, width), BF16), picked),
            (struct((own, width), F32), tiles(chunk, width)),
            (struct((8, width), F32), const_spec((8, width))),
            (struct(big, F32), const_spec(big)),
            (struct(big, BF16), const_spec(big)),
        ],
        [
            pltpu.VMEM((VT, width, ff // VT), BF16),
            pltpu.VMEM((VT, width, ff // VT), BF16),
            pltpu.VMEM((VT, width, ff // VT), F32),
            pltpu.VMEM((VT, width, ff // VT), F32),
        ],
        token_mm * 6 * ff,
        40,
    )
    y_far = swap(y, "tensor", 2)
    y_near = swap(y, "tensor", 1)
    fold_steps = [("dp", b // 2) if b > 1 else ("tensor", 2) for b in REDUCE_BITS]
    if usual:
        held_b = fold_step(keep_b, send_b, "tensor", 1)
        keep_b, send_b = halves(held_b)
        got_b = swap(send_b, *fold_steps[0])
    little = (CHIPS, 40, width)
    gx, gxb, keep_a, send_a = call(
        back_kernel,
        "back",
        grid,
        (meta,),
        [
            (flat, picked),
            (qkv, tiles(chunk, 3 * width)),
            (prob, tiles(per * HEADS, WIN, WIN)),
            (o, tiles(chunk, width)),
            (dx1, tiles(chunk, width)),
            (wqkv, const_spec((width, 3 * width))),
            (wout, const_spec((width, width))),
            (vec, const_spec((8, width))),
            (gvec, const_spec((8, width))),
        ],
        [
            (struct((images * seq_len, width), F32), picked),
            (struct((own, width), BF16), tiles(chunk, width)),
            (struct(little, F32), const_spec(little)),
            (struct(little, BF16), const_spec(little)),
        ],
        [
            pltpu.VMEM((chunk, 3 * width), BF16),
            pltpu.VMEM((width, 3 * width), F32),
            pltpu.VMEM((width, width), F32),
            pltpu.VMEM((8, width), F32),
        ],
        token_mm * (8 * width + 5 * WIN),
        32,
    )
    if usual:
        held_b = keep_b + got_b.astype(F32)
        send_a = after(after(send_a, held_b), y_far)
        held_a = fold_step(keep_a, send_a, "tensor", 1)
        held_a = fold_step(*halves(held_a), *fold_steps[0])
        held = jnp.concatenate([held_a, held_b], 1)
        got = lax.all_to_all(held.astype(BF16), "dp", 0, 0)
        o_qkv, o_out, o_gains, o_bias, o_up, o_down = finish(meta, got, small, tall)
    else:
        grad_a, grad_b = other_reduce((keep_a, send_a), (keep_b, send_b), me, n_dp, n_t)
        o_qkv = jnp.concatenate([grad_a[p * small : (p + 1) * small] for p in range(3)], 1)
        o_out = grad_a[3 * small : 4 * small]
        o_vec = lax.dynamic_slice_in_dim(grad_a[4 * small : 4 * small + 5], me * small, small, 1)
        o_gains, o_bias = o_vec[:2], o_vec[2:]
        o_up, o_down = grad_b[:tall], grad_b[tall:]

    def spread(near, far, full):
        sources = [near, far, swap(far, "tensor", 1)]
        whole = pl.BlockSpec((own, width), lambda i, meta: (0, 0))
        return pl.pallas_call(
            place_kernel,
            name="place",
            out_shape=struct(full.shape, full.dtype),
            grid_spec=pltpu.PrefetchScalarGridSpec(
                num_scalar_prefetch=1,
                grid=(n_t - 1,),
                in_specs=[pl.BlockSpec(memory_space=pl.ANY)] + [whole] * 3,
                out_specs=pl.BlockSpec((own, width), lambda i, meta: (meta[0] ^ (i + 1), 0)),
            ),
            input_output_aliases={1: 0},
            compiler_params=pltpu.CompilerParams(vmem_limit_bytes=32 * MIB),
        )(meta, full, *sources).reshape(images, seq_len, width)

    layer_out = spread(y_near, y_far, y_full)
    gx_near = swap(after(gxb, y_near), "tensor", 1)
    gx_far = swap(after(gxb, y_far), "tensor", 2)
    grad_tokens = spread(gx_near, gx_far, gx)
    return layer_out, grad_tokens, o_qkv, o_out, o_gains, o_bias, o_up, o_down.T


def solution(mesh):
    in_specs = (
        P("dp", None, None),
        P("dp"),
        P("dp", None),
        P("dp", None, None),
        P(("dp", "tensor"), None),
        P(("dp", "tensor"), None),
        P(None, ("dp", "tensor")),
        P(None, ("dp", "tensor")),
        P("dp", "tensor"),
        P("tensor", "dp"),
    )
    out_specs = (
        P("dp", None, None),
        P("dp", None, None),
        P(("dp", "tensor"), None),
        P(("dp", "tensor"), None),
        P(None, ("dp", "tensor")),
        P(None, ("dp", "tensor")),
        P("dp", "tensor"),
        P("tensor", "dp"),
    )
    return jax.shard_map(
        on_device, mesh=mesh, in_specs=in_specs, out_specs=out_specs, check_vma=False
    )
```

```python
import functools

import jax
import jax.numpy as jnp
from jax import lax
from jax.experimental import pallas as pl
from jax.experimental.pallas import tpu as pltpu
from jax.sharding import PartitionSpec as P

HEADS = 2
WIN = 96
F32 = jnp.float32
BF16 = jnp.bfloat16
VDP, VT = 8, 4
CHIPS = VDP * VT // 2
REDUCE_BITS = (2, 4, 8, 1)
MIB = 1 << 20

NN = ((1,), (0,))
NT = ((1,), (1,))
TN = ((0,), (0,))


def dot(a, b, dims):
    return lax.dot_general(a, b, (dims, ((), ())), preferred_element_type=F32)


def spot(m):
    return (m % 2) * VDP + m // 2


def fold(m):
    out = 0
    for place, bit in enumerate(REDUCE_BITS):
        shift = 3 - place
        out = out | (((m // bit) & 1) << shift)
    return out


def norm_parts(values):
    center = values - jnp.mean(values, -1, keepdims=True)
    inv = lax.rsqrt(jnp.mean(center * center, -1, keepdims=True) + 1e-05)
    return center * inv, inv


def norm_back(grad, xhat, inv, gain):
    scaled = grad * gain
    return inv * (
        scaled
        - jnp.mean(scaled, -1, keepdims=True)
        - xhat * jnp.mean(scaled * xhat, -1, keepdims=True)
    )


def gelu_both(u):
    c = 0.7978845608028654
    u2 = u * u
    t = jnp.tanh(u * (c + (c * 0.044715) * u2))
    half = 0.5 + 0.5 * t
    value = u * half
    slope = half + (value - value * half) * (2 * c + (6 * c * 0.044715) * u2)
    return value, slope


def pack_kernel(me, qkv, out, gains, biases, up, down, small_ref, big_ref):
    small, width = out.shape
    tall = up.shape[0]
    lane = lax.broadcasted_iota(jnp.int32, (1, width), 1)
    mine = lane // small == me[0]
    rows = [gains[0:1], gains[1:2], biases[0:1], biases[1:2], biases[2:3]]
    vals = jnp.concatenate(rows + [jnp.zeros((3, small), BF16)], 0).astype(F32)
    wide = jnp.concatenate([vals] * (width // small), 1)
    vec = jnp.where(mine, wide, 0.0).astype(BF16)
    for n in range(small_ref.shape[0]):
        for part in range(3):
            small_ref[n, part * small : (part + 1) * small] = qkv[:, part * width : (part + 1) * width]
        small_ref[n, 3 * small : 4 * small] = out[...]
        small_ref[n, 4 * small : 4 * small + 8] = vec
        big_ref[n, :tall] = up[...]
        big_ref[n, tall:] = down[...]


def fetch_kernel(n_t, me, tokens, cot, x_ref, cot_ref, xhat_ref, inv_ref, sems):
    own = x_ref.shape[0]
    at = pl.ds(lax.rem(me[0], n_t) * own, own)
    first = pltpu.make_async_copy(tokens.at[at], x_ref, sems.at[0])
    second = pltpu.make_async_copy(cot.at[at], cot_ref, sems.at[1])
    first.start()
    second.start()
    first.wait()
    for n in range(own // WIN):
        part = slice(n * WIN, (n + 1) * WIN)
        xhat_ref[part], inv_ref[part] = norm_parts(x_ref[part].astype(F32))
    second.wait()


def attend_kernel(
    n_t, per, me, virt, lens, live, x_ref, xhat_ref, held, got,
    qkv_ref, prob_ref, o_ref, x1_ref, h1_ref, wqkv, wout, vec,
):
    tokens, width = x_ref.shape
    rows = tokens // WIN
    hs = width // HEADS
    y_own = (virt[0] // 2) % 2
    first = virt[0] % 2 == 0
    total = jnp.zeros((8, width), F32)
    for m in range(CHIPS):
        k = spot(m) ^ (y_own * VDP)
        a = held[k].astype(F32)
        b = got[k].astype(F32)
        even = jnp.where(first, a, b)
        odd = jnp.where(first, b, a)
        for part in range(3):
            both = jnp.concatenate([even[part * 8 : part * 8 + 8], odd[part * 8 : part * 8 + 8]], 0)
            wqkv[m * 16 : m * 16 + 16, part * width : (part + 1) * width] = both.astype(BF16)
        both = jnp.concatenate([even[24:32], odd[24:32]], 0)
        wout[m * 16 : m * 16 + 16] = both.astype(BF16)
        total = total + a[32:40] + b[32:40]
    vec[...] = total
    scale = hs**-0.5
    ii = lax.broadcasted_iota(jnp.int32, (WIN, WIN), 0)
    jj = lax.broadcasted_iota(jnp.int32, (WIN, WIN), 1)
    same = ii == jj
    image_rows = live.shape[1]
    base = lax.rem(me[0], n_t) * rows
    for c in range(rows // per):
        part = slice(c * per * WIN, (c + 1) * per * WIN)
        h1 = (xhat_ref[part] * total[0:1] + total[2:3]).astype(BF16)
        h1_ref[part] = h1
        qkv_ref[part] = dot(h1, wqkv[...], NN).astype(BF16)
        for r in range(c * per, (c + 1) * per):
            row = base + r
            image = row // image_rows
            inside = row - image * image_rows
            reach = jnp.where(live[image, inside] == 1, lens[image] - inside * WIN, 0)
            allowed = same | (jj < jnp.minimum(ii, reach))
            at = slice(r * WIN, (r + 1) * WIN)
            for h in range(HEADS):
                q = qkv_ref[at, h * hs : (h + 1) * hs]
                k = qkv_ref[at, width + h * hs : width + (h + 1) * hs]
                v = qkv_ref[at, 2 * width + h * hs : 2 * width + (h + 1) * hs]
                s = jnp.where(allowed, dot(q, k, NT) * scale, -1e30)
                e = jnp.exp(s - jnp.max(s, -1, keepdims=True))
                p = (e / jnp.sum(e, -1, keepdims=True)).astype(BF16)
                prob_ref[r * HEADS + h] = p
                o_ref[at, h * hs : (h + 1) * hs] = dot(p, v, NN).astype(BF16)
        x1_ref[part] = x_ref[part].astype(F32) + dot(o_ref[part], wout[...], NN)


def hidden_half(part, h2, dyb, blocks, f, dh2, a_ref, du_ref):
    width = h2.shape[1]
    tall = width // VDP
    for n, w in enumerate(blocks):
        up = w[:, :tall].reshape(width, width)
        down = w[:, tall:].reshape(width, width)
        a, slope = gelu_both(dot(h2, up, NN))
        a = a.astype(BF16)
        f = f + dot(a, down, NT)
        du = (dot(dyb, down, NN) * slope).astype(BF16)
        dh2 = dh2 + dot(du, up, NT)
        at = slice(n * width, (n + 1) * width)
        a_ref[part, at] = a
        du_ref[part, at] = du
    return f, dh2


def store_hidden_grads(virt, h2_ref, cot_ref, a_ref, du_ref, out):
    width = h2_ref.shape[1]
    tall = width // VDP
    gdown = dot(cot_ref[...], a_ref[...], TN).astype(out.dtype)
    gup = dot(h2_ref[...], du_ref[...], TN).astype(out.dtype)
    own = fold((virt[0] // 4) * 2)
    for i in range(VDP):
        at = slice(i * tall, (i + 1) * tall)
        for n in range(2):
            k = (fold(2 * i) ^ own) + n
            out[k, :tall] = gup[at, n * width : (n + 1) * width]
            out[k, tall:] = gdown[at, n * width : (n + 1) * width]


def hidden_own_kernel(
    per, virt, x1_ref, cot_ref, vec, near, far, h2_ref, xhat_ref, inv_ref, f_ref, dh2_ref, keep,
    a_ref, du_ref,
):
    tokens = x1_ref.shape[0]
    size = per * WIN
    for c in range(tokens // size):
        part = slice(c * size, (c + 1) * size)
        x1 = x1_ref[part]
        xhat, inv = norm_parts(x1)
        xhat_ref[part] = xhat
        inv_ref[part] = inv
        h2 = (xhat * vec[1:2] + vec[3:4]).astype(BF16)
        h2_ref[part] = h2
        f = x1 + vec[4:5]
        f, dh2 = hidden_half(
            part, h2, cot_ref[part], (near, far), f, jnp.zeros_like(f), a_ref, du_ref
        )
        f_ref[part] = f
        dh2_ref[part] = dh2
    store_hidden_grads(virt, h2_ref, cot_ref, a_ref, du_ref, keep)


def hidden_other_kernel(
    per, virt, cot_ref, vec, got, h2_ref, xhat_ref, inv_ref, f_ref, dh2_ref,
    y_ref, dx1_ref, g_ref, gvec, send,
    a_ref, du_ref,
):
    tokens, width = h2_ref.shape
    size = per * WIN
    sums = [jnp.zeros((1, width), F32)] * 3
    for c in range(tokens // size):
        part = slice(c * size, (c + 1) * size)
        dyb = cot_ref[part]
        f, dh2 = hidden_half(
            part, h2_ref[part], dyb, (got[:VDP], got[VDP:]), f_ref[part], dh2_ref[part], a_ref, du_ref
        )
        y_ref[part] = f.astype(BF16)
        dy = dyb.astype(F32)
        xhat = xhat_ref[part]
        dx1 = dy + norm_back(dh2, xhat, inv_ref[part], vec[1:2])
        dx1_ref[part] = dx1
        g_ref[part] = dx1.astype(BF16)
        terms = (dh2 * xhat, dh2, dy)
        sums = [a + jnp.sum(b, 0, keepdims=True) for a, b in zip(sums, terms)]
    zero = jnp.zeros((1, width), F32)
    gvec[...] = jnp.concatenate([zero, sums[0], zero, sums[1], sums[2], zero, zero, zero], 0)
    store_hidden_grads(virt, h2_ref, cot_ref, a_ref, du_ref, send)


def back_kernel(
    virt, qkv_ref, prob_ref, o_ref, g_ref, h1_ref, wqkv, wout, vec, gvec,
    dqkv, keep, send,
    do_ref, gqkv, gout,
):
    tokens, width = o_ref.shape
    hs = width // HEADS
    scale = hs**-0.5
    do_ref[...] = dot(g_ref[...], wout[...], NT).astype(BF16)
    for r in range(tokens // WIN):
        at = slice(r * WIN, (r + 1) * WIN)
        for h in range(HEADS):
            cols = [slice(part * width + h * hs, part * width + (h + 1) * hs) for part in range(3)]
            p = prob_ref[r * HEADS + h]
            doh = do_ref[at, h * hs : (h + 1) * hs]
            dqkv[at, cols[2]] = dot(p, doh, TN).astype(BF16)
            dp = dot(doh, qkv_ref[at, cols[2]], NT)
            pf = p.astype(F32)
            ds = pf * (dp - jnp.sum(dp * pf, -1, keepdims=True)) * scale
            ds = ds.astype(BF16)
            dqkv[at, cols[0]] = dot(ds, qkv_ref[at, cols[1]], NN).astype(BF16)
            dqkv[at, cols[1]] = dot(ds, qkv_ref[at, cols[0]], TN).astype(BF16)
    gout[...] = dot(o_ref[...], g_ref[...], TN)
    gqkv[...] = dot(h1_ref[...], dqkv[...], TN)
    total = jnp.zeros((1, 3 * width), F32)
    for r in range(tokens // WIN):
        total = total + jnp.sum(dqkv[r * WIN : (r + 1) * WIN].astype(F32), 0, keepdims=True)
    w = wqkv[...].astype(F32)
    cols = jnp.concatenate([
        jnp.broadcast_to(jnp.sum(w * gqkv[...], -1, keepdims=True), (width, 64)),
        jnp.broadcast_to(jnp.sum(w * total, -1, keepdims=True), (width, 64)),
    ], 1)
    lines = cols.T
    from_grad, from_total = lines[0:1], lines[64:65]
    gain = (from_grad - vec[2:3] * from_total) / vec[0:1]
    rest = gvec[...]
    sums = jnp.concatenate([gain, rest[1:2], from_total, rest[3:8]], 0)
    low = sums.astype(BF16)
    core = virt[0] % 2
    own = fold(virt[0] // 2)
    for m in range(CHIPS):
        k = fold(m) ^ own
        mine = pl.ds(pl.multiple_of(m * 16 + 8 * core, 8), 8)
        other = pl.ds(pl.multiple_of(m * 16 + 8 - 8 * core, 8), 8)
        theirs = []
        for part in range(3):
            at = slice(part * width, (part + 1) * width)
            keep[k, part * 8 : part * 8 + 8] = gqkv[mine, at]
            theirs.append(gqkv[other, at])
        keep[k, 24:32] = gout[mine]
        theirs.append(gout[other])
        send[k, :32] = jnp.concatenate(theirs, 0).astype(BF16)
        keep[k, 32:40] = sums
        send[k, 32:40] = low


def token_grad_kernel(per, dqkv, wqkv, vec, xhat_ref, inv_ref, dx1_ref, gx_ref, gxb_ref):
    size = per * WIN
    for c in range(dqkv.shape[0] // size):
        part = slice(c * size, (c + 1) * size)
        dh1 = dot(dqkv[part], wqkv[...], NT)
        gx = dx1_ref[part] + norm_back(dh1, xhat_ref[part], inv_ref[part], vec[0:1])
        gx_ref[part] = gx
        gxb_ref[part] = gx.astype(BF16)


def place_kernel(n_t, me, *refs):
    out, wide, sems = refs[-3:]
    sources = refs[:-3]
    own = sources[0].shape[0]
    copies = []
    for n, source in enumerate(sources):
        if source.dtype != out.dtype:
            wide[n - 1] = source[...].astype(out.dtype)
            source = wide.at[n - 1]
        at = pl.ds((lax.rem(me[0], n_t) ^ n) * own, own)
        copies.append(pltpu.make_async_copy(source, out.at[at], sems.at[n]))
        copies[-1].start()
    for copy in copies:
        copy.wait()


def finish_kernel(me, a, b, got, qkv, out, gains, biases, up, down):
    small, width = out.shape
    tall = up.shape[0]
    at = 4 * small + 8
    one = a[...] + got[:at].astype(F32)
    for part in range(3):
        qkv[:, part * width : (part + 1) * width] = one[part * small : (part + 1) * small]
    out[...] = one[3 * small : 4 * small]
    vec = pltpu.roll(one[4 * small :], width - me[0] * small, 1)[:, :small]
    gains[...] = vec[:2]
    biases[...] = vec[2:5]
    up[...] = b[:tall] + got[at : at + tall].astype(F32)
    down[...] = b[tall:] + got[at + tall :].astype(F32)


def swap(block, axis, bit):
    size = lax.axis_size(axis)
    return lax.ppermute(block, axis, [(i, i ^ bit) for i in range(size)])


def steps_of(axis):
    return [(axis, 1 << k) for k in reversed(range(lax.axis_size(axis).bit_length() - 1))]


def after(value, other):
    return lax.optimization_barrier((value, other))[0]


def halves(held):
    half = held.shape[0] // 2
    return held[:half], held[half:].astype(BF16)


def fold_step(keep, send, axis, bit):
    return keep + swap(send, axis, bit).astype(F32)


def bit_reverse(index, count):
    out = 0 * index
    for k in range(count):
        out = out | (((index >> k) & 1) << (count - 1 - k))
    return out


def by_device(block, me):
    blocks = block[None]
    for axis, bit in steps_of("dp") + steps_of("tensor"):
        blocks = jnp.concatenate([blocks, swap(blocks, axis, bit)], 0)
    count = blocks.shape[0]
    order = jnp.arange(count, dtype=jnp.int32) ^ me
    return jnp.take(blocks, bit_reverse(order, count.bit_length() - 1), axis=0)


def other_pack(w_qkv, w_out, gains, biases, w_up, w_down, me):
    small, width = w_out.shape
    qkv = w_qkv.reshape(small, 3, width).transpose(1, 0, 2).reshape(3 * small, width)
    rows = jnp.concatenate([gains, biases], 0)
    place = jnp.zeros((8, width), BF16)
    place = lax.dynamic_update_slice(place, rows, (jnp.int32(0), me * small))
    return jnp.concatenate([qkv, w_out, place], 0), jnp.concatenate([w_up, w_down.T], 0)


def other_blocks(a, b, me, n_dp, n_t):
    a = by_device(a, me)
    b = by_device(b, me)
    width = a.shape[2]
    count = n_dp * n_t
    small = width // count
    big = width // (VDP * VT)
    mats = a[:, : 4 * small].reshape(count, 4, small, width).transpose(1, 0, 2, 3)
    mats = mats.reshape(4, VDP * VT, big, width).transpose(1, 0, 2, 3).reshape(VDP * VT, 4 * big, width)
    vec = jnp.sum(a[:, 4 * small :].astype(F32), 0).astype(BF16)
    vecs = jnp.concatenate([vec[None], jnp.zeros((VDP * VT - 1, 8, width), BF16)], 0)
    a = jnp.concatenate([mats, vecs], 1)
    tall = width // n_dp
    b = b.reshape(n_dp, VT, 2, tall, width).transpose(1, 2, 0, 3, 4)
    b = b.reshape(VT, 2, VDP, width // VDP, width).transpose(2, 0, 1, 3, 4)
    b = b.reshape(VDP * VT, 2 * (width // VDP), width)

    def placed(blocks):
        pairs = blocks.reshape((CHIPS, 2) + blocks.shape[1:])
        pairs = jnp.stack([pairs[m] for m in sorted(range(CHIPS), key=spot)], 0)
        return pairs[:, 0], pairs[:, 1]

    return placed(a) + placed(b)


def other_reduce(pair_a, pair_b, me, n_dp, n_t):
    order = [fold(m) for m in range(CHIPS)]
    count = n_dp * n_t

    def whole(keep, send):
        pairs = jnp.stack([keep, send.astype(F32)], 1)
        pairs = jnp.stack([pairs[k] for k in order], 0)
        return pairs.reshape((VDP * VT,) + keep.shape[1:])

    a, b = whole(*pair_a), whole(*pair_b)
    width = a.shape[2]
    small, tall = width // count, width // n_dp
    big = width // (VDP * VT)
    mats = a[:, : 4 * big].reshape(VDP * VT, 4, big, width).transpose(1, 0, 2, 3)
    mats = mats.reshape(4, count, small, width).transpose(1, 0, 2, 3)
    mats = mats.reshape(count, 4 * small, width)
    a = jnp.concatenate([mats, jnp.broadcast_to(a[:1, 4 * big :], (count, 8, width))], 1)
    b = b.reshape(VDP, VT, 2, width // VDP, width).transpose(1, 2, 0, 3, 4)
    b = b.reshape(VT, 2, n_dp, tall, width).transpose(2, 0, 1, 3, 4)
    b = b.reshape(count, 2 * tall, width)
    results = []
    for blocks in (a, b):
        blocks = jnp.take(blocks, jnp.arange(count, dtype=jnp.int32) ^ me, axis=0)
        for axis, bit in reversed(steps_of("dp") + steps_of("tensor")):
            pairs = blocks.reshape((-1, 2) + blocks.shape[1:])
            got = swap(pairs[:, 1].astype(BF16), axis, bit)
            blocks = pairs[:, 0] + got.astype(F32)
        results.append(blocks[0])
    return results


def struct(shape, dtype):
    return jax.ShapeDtypeStruct(shape, dtype)


def call(kernel, name, args, outs, scratch=(), flops=0, limit=16):
    args = [a if isinstance(a, tuple) else (a, pltpu.VMEM) for a in args]
    moved = sum(a.size * a.dtype.itemsize for a, _ in args)
    spaces = [pl.ANY if isinstance(o, jax.ShapeDtypeStruct) else pltpu.VMEM for o in outs]
    return pl.pallas_call(
        kernel,
        name=name,
        out_shape=outs,
        in_specs=[pl.BlockSpec(memory_space=space) for _, space in args],
        out_specs=[pl.BlockSpec(memory_space=space) for space in spaces],
        scratch_shapes=list(scratch),
        compiler_params=pltpu.CompilerParams(vmem_limit_bytes=limit * MIB),
        cost_estimate=pl.CostEstimate(flops=flops, bytes_accessed=moved, transcendentals=0),
    )(*[a for a, _ in args])


def on_device(tokens, lengths, row_mask, cotangent, w_qkv, w_out, gains, biases, w_up, w_down):
    images, seq_len, width = tokens.shape
    n_dp, n_t = lax.axis_size("dp"), lax.axis_size("tensor")
    index = lax.axis_index("dp") * n_t + lax.axis_index("tensor")
    me = index.astype(jnp.int32).reshape(1)
    usual = (n_dp, n_t) == (VDP, VT)
    virt = me if usual else jnp.zeros((1,), jnp.int32)
    small = width // (n_dp * n_t)
    tall = width // n_dp
    own = images * seq_len // n_t
    rows = own // WIN
    per = 4 if rows % 4 == 0 else 1
    smem = pltpu.SMEM
    weights = (w_qkv, w_out, gains, biases, w_up, w_down)
    token_mm = 2 * own * width
    fetch_in = [
        (me, smem),
        (tokens.reshape(images * seq_len, width), pl.ANY),
        (cotangent.reshape(images * seq_len, width), pl.ANY),
    ]
    if usual:
        pack_a, pack_b = call(
            pack_kernel,
            "pack",
            [(me, smem), w_qkv, w_out, gains, biases, w_up, w_down.T],
            [
                pltpu.VMEM((n_dp, 4 * small + 8, width), BF16),
                pltpu.VMEM((n_dp, 2 * tall, width), BF16),
            ],
        )
        fetch_in[0] = (after(me, pack_a), smem)
        a = lax.all_to_all(pack_a, "dp", 0, 0)
        b = lax.all_to_all(pack_b, "dp", 0, 0)
        held_a = jnp.concatenate([a, swap(a, "tensor", 2)], 0)
        far_b = swap(after(b, held_a), "tensor", 2)
        got_a = swap(held_a, "tensor", 1)
    else:
        held_a, got_a, held_b, got_b = other_blocks(*other_pack(*weights, index), index, n_dp, n_t)
        b, far_b = held_b[:VDP], held_b[VDP:]
    x, cot, xhat1, inv1 = call(
        functools.partial(fetch_kernel, n_t),
        "fetch",
        fetch_in,
        [
            pltpu.VMEM((own, width), BF16),
            pltpu.VMEM((own, width), BF16),
            pltpu.VMEM((own, width), F32),
            pltpu.VMEM((own, 1), F32),
        ],
        [pltpu.SemaphoreType.DMA((2,))],
    )
    qkv, prob, o, x1, h1, wqkv, wout, vec = call(
        functools.partial(attend_kernel, n_t, per),
        "attend",
        [(me, smem), (virt, smem), (lengths, smem), (row_mask, smem), x, xhat1, held_a, got_a],
        [
            pltpu.VMEM((own, 3 * width), BF16),
            pltpu.VMEM((rows * HEADS, WIN, WIN), BF16),
            pltpu.VMEM((own, width), BF16),
            pltpu.VMEM((own, width), F32),
            pltpu.VMEM((own, width), BF16),
            pltpu.VMEM((width, 3 * width), BF16),
            pltpu.VMEM((width, width), BF16),
            pltpu.VMEM((8, width), F32),
        ],
        flops=token_mm * (4 * width + 2 * WIN),
    )
    if usual:
        far_b = after(far_b, x1)
        got_b = swap(jnp.concatenate([b, far_b], 0), "tensor", 1)
    grads_b = (CHIPS, 2 * (width // VDP), width)
    grads_a = (CHIPS, 40, width)
    kept = [pltpu.VMEM((own, 2 * width), BF16)] * 2
    h2, xhat2, inv2, f, dh2, keep_b = call(
        functools.partial(hidden_own_kernel, per),
        "hidden_own",
        [(virt, smem), x1, cot, vec, b, far_b],
        [
            pltpu.VMEM((own, width), BF16),
            pltpu.VMEM((own, width), F32),
            pltpu.VMEM((own, 1), F32),
            pltpu.VMEM((own, width), F32),
            pltpu.VMEM((own, width), F32),
            pltpu.VMEM(grads_b, F32),
        ],
        kept,
        token_mm * 12 * width,
    )
    y, dx1, g, gvec, send_b = call(
        functools.partial(hidden_other_kernel, per),
        "hidden_other",
        [(virt, smem), cot, vec, got_b, h2, xhat2, inv2, f, dh2],
        [
            pltpu.VMEM((own, width), BF16),
            pltpu.VMEM((own, width), F32),
            pltpu.VMEM((own, width), BF16),
            pltpu.VMEM((8, width), F32),
            pltpu.VMEM(grads_b, BF16),
        ],
        kept,
        token_mm * 12 * width,
    )
    y_far = swap(y, "tensor", 2)
    y_near = swap(y, "tensor", 1)
    core, xbit, zlo, zhi, ybit = ("tensor", 1), ("dp", 1), ("dp", 2), ("dp", 4), ("tensor", 2)
    dqkv, keep_a, send_a = call(
        back_kernel,
        "back",
        [(virt, smem), qkv, prob, o, g, h1, wqkv, wout, vec, gvec],
        [
            pltpu.VMEM((own, 3 * width), BF16),
            pltpu.VMEM(grads_a, F32),
            pltpu.VMEM(grads_a, BF16),
        ],
        [
            pltpu.VMEM((own, width), BF16),
            pltpu.VMEM((width, 3 * width), F32),
            pltpu.VMEM((width, width), F32),
        ],
        token_mm * (5 * width + 5 * WIN),
    )
    gx, gxb = call(
        functools.partial(token_grad_kernel, per),
        "token_grad",
        [dqkv, wqkv, vec, xhat1, inv1, dx1],
        [pltpu.VMEM((own, width), F32), pltpu.VMEM((own, width), BF16)],
        flops=token_mm * 3 * width,
    )
    gx_near = swap(after(gxb, y_near), "tensor", 1)
    gx_far = swap(after(gxb, y_far), "tensor", 2)
    y_both = swap(y_far, "tensor", 1)
    if usual:
        held_b = fold_step(keep_b, send_b, *core)
        held_b = fold_step(*halves(held_b), *xbit)
        held_a = fold_step(keep_a, after(send_a, y_far), *core)
        held_a = fold_step(*halves(held_a), *xbit)
        keep, send = halves(held_b)
        held_b = fold_step(keep, send, *zlo)
        keep, send = halves(held_a)
        held_a = fold_step(keep, after(send, held_b), *zlo)
        held_b = fold_step(*halves(held_b), *zhi)
        held_a = fold_step(*halves(held_a), *zhi)
        last = jnp.concatenate([held_a[1], held_b[1]], 0).astype(BF16)
        gx_far = after(gx_far, last)
        vmem = pl.BlockSpec(memory_space=pltpu.VMEM)
        shapes = [(small, 3 * width), (small, width), (2, small), (3, small), (tall, width), (tall, width)]
        o_qkv, o_out, o_gains, o_bias, o_up, o_down = pl.pallas_call(
            finish_kernel,
            name="finish",
            out_shape=[struct(shape, F32) for shape in shapes],
            in_specs=[pl.BlockSpec(memory_space=smem), vmem, vmem, vmem],
            out_specs=[vmem] * 6,
        )(me, held_a[0], held_b[0], swap(last, *ybit))
    else:
        grad_a, grad_b = other_reduce((keep_a, send_a), (keep_b, send_b), index, n_dp, n_t)
        o_qkv = jnp.concatenate([grad_a[p * small : (p + 1) * small] for p in range(3)], 1)
        o_out = grad_a[3 * small : 4 * small]
        o_vec = lax.dynamic_slice_in_dim(grad_a[4 * small : 4 * small + 5], index * small, small, 1)
        o_gains, o_bias = o_vec[:2], o_vec[2:]
        o_up, o_down = grad_b[:tall], grad_b[tall:]
    gx_both = swap(gx_far, "tensor", 1)

    def place(sources, dtype, wide):
        return call(
            functools.partial(place_kernel, n_t),
            "place",
            [(me, smem)] + list(sources),
            [struct((images * seq_len, width), dtype)],
            [pltpu.VMEM(wide, dtype), pltpu.SemaphoreType.DMA((n_t,))],
        )[0].reshape(images, seq_len, width)

    layer_out = place((y, y_near, y_far, y_both), BF16, (1, 16, 128))
    grad_tokens = place((gx, gx_near, gx_far, gx_both), F32, (n_t - 1, own, width))
    return layer_out, grad_tokens, o_qkv, o_out, o_gains, o_bias, o_up, o_down.T


def solution(mesh):
    in_specs = (
        P("dp", None, None),
        P("dp"),
        P("dp", None),
        P("dp", None, None),
        P(("dp", "tensor"), None),
        P(("dp", "tensor"), None),
        P(None, ("dp", "tensor")),
        P(None, ("dp", "tensor")),
        P("dp", "tensor"),
        P("tensor", "dp"),
    )
    out_specs = (
        P("dp", None, None),
        P("dp", None, None),
        P(("dp", "tensor"), None),
        P(("dp", "tensor"), None),
        P(None, ("dp", "tensor")),
        P(None, ("dp", "tensor")),
        P("dp", "tensor"),
        P("tensor", "dp"),
    )
    return jax.shard_map(
        on_device, mesh=mesh, in_specs=in_specs, out_specs=out_specs, check_vma=False
    )
```

```python
import functools

import jax
import jax.numpy as jnp
from jax import lax
from jax.experimental import pallas as pl
from jax.experimental.pallas import tpu as pltpu
from jax.sharding import PartitionSpec as P

HEADS = 2
WIN = 96
F32 = jnp.float32
BF16 = jnp.bfloat16
VDP, VT = 8, 4
CHIPS = VDP * VT // 2
REDUCE_BITS = (2, 4, 8, 1)
MIB = 1 << 20

NN = ((1,), (0,))
NT = ((1,), (1,))
TN = ((0,), (0,))


def dot(a, b, dims):
    return lax.dot_general(a, b, (dims, ((), ())), preferred_element_type=F32)


def turn(i):
    return ((i & 1) << 2) | (i & 2) | ((i & 4) >> 2)


def spot(m):
    return (m % 2) * VDP + turn(m // 2)


def fold(m):
    out = 0
    for place, bit in enumerate(REDUCE_BITS):
        shift = 3 - place
        out = out | (((m // bit) & 1) << shift)
    return out


def norm_parts(values):
    center = values - jnp.mean(values, -1, keepdims=True)
    inv = lax.rsqrt(jnp.mean(center * center, -1, keepdims=True) + 1e-05)
    return center * inv, inv


def norm_back(grad, xhat, inv, gain):
    scaled = grad * gain
    return inv * (
        scaled
        - jnp.mean(scaled, -1, keepdims=True)
        - xhat * jnp.mean(scaled * xhat, -1, keepdims=True)
    )


def gelu_both(u):
    c = 0.7978845608028654
    u2 = u * u
    t = jnp.tanh(u * (c + (c * 0.044715) * u2))
    half = 0.5 + 0.5 * t
    value = u * half
    slope = half + (value - value * half) * (2 * c + (6 * c * 0.044715) * u2)
    return value, slope


def pack_kernel(me, *refs):
    sources, (small_ref, big_ref), held, sems = refs[:6], refs[6:8], refs[8:14], refs[14]
    copies = [pltpu.make_async_copy(a, b, sems.at[n]) for n, (a, b) in enumerate(zip(sources, held))]
    for copy in copies:
        copy.start()
    qkv, out, gains, biases, up, down = held
    small, width = out.shape
    tall = up.shape[0]
    lane = lax.broadcasted_iota(jnp.int32, (1, width), 1)
    mine = lane // small == me[0]
    for copy in copies:
        copy.wait()
    for part in range(3):
        small_ref[0, part * small : (part + 1) * small] = qkv[:, part * width : (part + 1) * width]
    small_ref[0, 3 * small : 4 * small] = out[...]
    rows = [gains[0:1], gains[1:2], biases[0:1], biases[1:2], biases[2:3]]
    vals = jnp.concatenate(rows + [jnp.zeros((3, small), BF16)], 0).astype(F32)
    wide = jnp.concatenate([vals] * (width // small), 1)
    small_ref[0, 4 * small : 4 * small + 8] = jnp.where(mine, wide, 0.0).astype(BF16)
    big_ref[0, :tall] = up[...]
    big_ref[0, tall:] = down[...]


def fetch_kernel(n_t, me, tokens, cot, x_ref, cot_ref, xhat_ref, inv_ref, sems):
    own = x_ref.shape[0]
    at = pl.ds(lax.rem(me[0], n_t) * own, own)
    first = pltpu.make_async_copy(tokens.at[at], x_ref, sems.at[0])
    second = pltpu.make_async_copy(cot.at[at], cot_ref, sems.at[1])
    first.start()
    second.start()
    first.wait()
    for n in range(own // WIN):
        part = slice(n * WIN, (n + 1) * WIN)
        xhat_ref[part], inv_ref[part] = norm_parts(x_ref[part].astype(F32))
    second.wait()


def attend_kernel(
    n_t, per, me, virt, lens, live, x_ref, xhat_ref, held, got,
    qkv_ref, prob_ref, o_ref, x1_ref, h1_ref, wqkv, wout, vec,
):
    tokens, width = x_ref.shape
    rows = tokens // WIN
    hs = width // HEADS
    here = spot(virt[0] // 2) % VDP
    y_own = (virt[0] // 2) % 2
    first = virt[0] % 2 == 0
    total = jnp.zeros((8, width), F32)
    for m in range(CHIPS):
        k = spot(m) ^ (here + y_own * VDP)
        a = held[k].astype(F32)
        b = got[k].astype(F32)
        even = jnp.where(first, a, b)
        odd = jnp.where(first, b, a)
        for part in range(3):
            both = jnp.concatenate([even[part * 8 : part * 8 + 8], odd[part * 8 : part * 8 + 8]], 0)
            wqkv[m * 16 : m * 16 + 16, part * width : (part + 1) * width] = both.astype(BF16)
        both = jnp.concatenate([even[24:32], odd[24:32]], 0)
        wout[m * 16 : m * 16 + 16] = both.astype(BF16)
        total = total + a[32:40] + b[32:40]
    vec[...] = total
    scale = hs**-0.5
    ii = lax.broadcasted_iota(jnp.int32, (WIN, WIN), 0)
    jj = lax.broadcasted_iota(jnp.int32, (WIN, WIN), 1)
    same = ii == jj
    image_rows = live.shape[1]
    base = lax.rem(me[0], n_t) * rows
    for c in range(rows // per):
        part = slice(c * per * WIN, (c + 1) * per * WIN)
        h1 = (xhat_ref[part] * total[0:1] + total[2:3]).astype(BF16)
        h1_ref[part] = h1
        qkv = dot(h1, wqkv[...], NN).astype(BF16)
        qkv_ref[part] = qkv
        pairs = [(r, h) for r in range(c * per, (c + 1) * per) for h in range(HEADS)]
        scores = []
        for r, h in pairs:
            at = slice((r - c * per) * WIN, (r - c * per + 1) * WIN)
            q = qkv[at, h * hs : (h + 1) * hs]
            k = qkv[at, width + h * hs : width + (h + 1) * hs]
            scores.append(dot(q, k, NT))
        allowed = []
        for r in range(c * per, (c + 1) * per):
            row = base + r
            image = row // image_rows
            inside = row - image * image_rows
            reach = jnp.where(live[image, inside] == 1, lens[image] - inside * WIN, 0)
            allowed.append(same | (jj < jnp.minimum(ii, reach)))
        probs = []
        for (r, h), s in zip(pairs, scores):
            s = jnp.where(allowed[r - c * per], s, -1e30)
            e = jnp.exp((s - jnp.max(s, -1, keepdims=True)) * scale)
            probs.append((e * (1.0 / jnp.sum(e, -1, keepdims=True))).astype(BF16))
        mixed = []
        for (r, h), p in zip(pairs, probs):
            at = slice((r - c * per) * WIN, (r - c * per + 1) * WIN)
            v = qkv[at, 2 * width + h * hs : 2 * width + (h + 1) * hs]
            mixed.append(dot(p, v, NN).astype(BF16))
        for (r, h), p in zip(pairs, probs):
            prob_ref[r * HEADS + h] = p
        o = jnp.concatenate(
            [jnp.concatenate(mixed[n : n + HEADS], 1) for n in range(0, len(mixed), HEADS)], 0
        )
        o_ref[part] = o
        x1_ref[part] = x_ref[part].astype(F32) + dot(o, wout[...], NN)


def join(virt, blocks, n, out):
    tall = blocks.shape[1] // 2
    here = turn(virt[0] // 4)
    for i in range(VDP):
        k = turn(i) ^ here
        at = slice(i * tall, (i + 1) * tall)
        out[2 * n, at] = blocks[k, :tall]
        out[2 * n + 1, at] = blocks[k, tall:]


def hidden_half(part, h2, dyb, mats, f, dh2, a_ref, du_ref):
    width = h2.shape[1]
    for n in range(2):
        up, down = mats[2 * n], mats[2 * n + 1]
        a, slope = gelu_both(dot(h2, up, NN))
        a = a.astype(BF16)
        f = f + dot(a, down, NT)
        du = (dot(dyb, down, NN) * slope).astype(BF16)
        dh2 = dh2 + dot(du, up, NT)
        at = slice(n * width, (n + 1) * width)
        a_ref[part, at] = a
        du_ref[part, at] = du
    return f, dh2


def store_hidden_grads(virt, h2_ref, cot_ref, a_ref, du_ref, out):
    width = h2_ref.shape[1]
    tall = width // VDP
    gdown = dot(cot_ref[...], a_ref[...], TN).astype(out.dtype)
    gup = dot(h2_ref[...], du_ref[...], TN).astype(out.dtype)
    own = fold((virt[0] // 4) * 2)
    for i in range(VDP):
        at = slice(i * tall, (i + 1) * tall)
        for n in range(2):
            k = (fold(2 * i) ^ own) + n
            out[k, :tall] = gup[at, n * width : (n + 1) * width]
            out[k, tall:] = gdown[at, n * width : (n + 1) * width]


def hidden_own_kernel(
    per, virt, x1_ref, cot_ref, vec, near, far, h2_ref, xhat_ref, inv_ref, f_ref, dh2_ref, keep,
    a_ref, du_ref, mats,
):
    tokens = x1_ref.shape[0]
    size = per * WIN
    join(virt, near, 0, mats)
    join(virt, far, 1, mats)
    for c in range(tokens // size):
        part = slice(c * size, (c + 1) * size)
        x1 = x1_ref[part]
        xhat, inv = norm_parts(x1)
        xhat_ref[part] = xhat
        inv_ref[part] = inv
        h2 = (xhat * vec[1:2] + vec[3:4]).astype(BF16)
        h2_ref[part] = h2
        f = x1 + vec[4:5]
        f, dh2 = hidden_half(
            part, h2, cot_ref[part], mats, f, jnp.zeros_like(f), a_ref, du_ref
        )
        f_ref[part] = f
        dh2_ref[part] = dh2
    store_hidden_grads(virt, h2_ref, cot_ref, a_ref, du_ref, keep)


def hidden_other_kernel(
    per, virt, cot_ref, vec, got, h2_ref, xhat_ref, inv_ref, f_ref, dh2_ref,
    y_ref, dx1_ref, g_ref, gvec, send,
    a_ref, du_ref, mats,
):
    tokens, width = h2_ref.shape
    size = per * WIN
    join(virt, got.at[:VDP], 0, mats)
    join(virt, got.at[VDP:], 1, mats)
    sums = [jnp.zeros((1, width), F32)] * 3
    for c in range(tokens // size):
        part = slice(c * size, (c + 1) * size)
        dyb = cot_ref[part]
        f, dh2 = hidden_half(
            part, h2_ref[part], dyb, mats, f_ref[part], dh2_ref[part], a_ref, du_ref
        )
        y_ref[part] = f.astype(BF16)
        dy = dyb.astype(F32)
        xhat = xhat_ref[part]
        dx1 = dy + norm_back(dh2, xhat, inv_ref[part], vec[1:2])
        dx1_ref[part] = dx1
        g_ref[part] = dx1.astype(BF16)
        terms = (dh2 * xhat, dh2, dy)
        sums = [a + jnp.sum(b, 0, keepdims=True) for a, b in zip(sums, terms)]
    zero = jnp.zeros((1, width), F32)
    gvec[...] = jnp.concatenate([zero, sums[0], zero, sums[1], sums[2], zero, zero, zero], 0)
    store_hidden_grads(virt, h2_ref, cot_ref, a_ref, du_ref, send)


def back_kernel(
    per, virt, qkv_ref, prob_ref, o_ref, g_ref, h1_ref, wqkv, wout, vec, gvec,
    dqkv, keep, send,
    do_ref, gqkv, gout,
):
    tokens, width = o_ref.shape
    hs = width // HEADS
    scale = hs**-0.5
    do_ref[...] = dot(g_ref[...], wout[...], NT).astype(BF16)
    every = [(r, h) for r in range(tokens // WIN) for h in range(HEADS)]

    def piece(ref, r, h, part=0):
        return ref[r * WIN : (r + 1) * WIN, part * width + h * hs : part * width + (h + 1) * hs]

    for start in range(0, len(every), 2 * per):
        pairs = every[start : start + 2 * per]
        probs = [prob_ref[r * HEADS + h] for r, h in pairs]
        dos = [piece(do_ref, r, h) for r, h in pairs]
        dps = [dot(a, piece(qkv_ref, r, h, 2), NT) for a, (r, h) in zip(dos, pairs)]
        dvs = [dot(p, a, TN).astype(BF16) for p, a in zip(probs, dos)]
        dss = []
        for p, dp in zip(probs, dps):
            pf = p.astype(F32)
            ds = pf * (dp - jnp.sum(dp * pf, -1, keepdims=True)) * scale
            dss.append(ds.astype(BF16))
        dqs = [dot(ds, piece(qkv_ref, r, h, 1), NN).astype(BF16) for ds, (r, h) in zip(dss, pairs)]
        dks = [dot(ds, piece(qkv_ref, r, h, 0), TN).astype(BF16) for ds, (r, h) in zip(dss, pairs)]
        for n, (r, h) in enumerate(pairs):
            for part, values in enumerate((dqs, dks, dvs)):
                at = slice(part * width + h * hs, part * width + (h + 1) * hs)
                dqkv[r * WIN : (r + 1) * WIN, at] = values[n]
    gout[...] = dot(o_ref[...], g_ref[...], TN)
    gqkv[...] = dot(h1_ref[...], dqkv[...], TN)
    total = jnp.zeros((1, 3 * width), F32)
    for r in range(tokens // WIN):
        total = total + jnp.sum(dqkv[r * WIN : (r + 1) * WIN].astype(F32), 0, keepdims=True)
    w = wqkv[...].astype(F32)
    cols = jnp.concatenate([
        jnp.broadcast_to(jnp.sum(w * gqkv[...], -1, keepdims=True), (width, 64)),
        jnp.broadcast_to(jnp.sum(w * total, -1, keepdims=True), (width, 64)),
    ], 1)
    lines = cols.T
    from_grad, from_total = lines[0:1], lines[64:65]
    gain = (from_grad - vec[2:3] * from_total) / vec[0:1]
    rest = gvec[...]
    sums = jnp.concatenate([gain, rest[1:2], from_total, rest[3:8]], 0)
    low = sums.astype(BF16)
    core = virt[0] % 2
    own = fold(virt[0] // 2)
    for m in range(CHIPS):
        k = fold(m) ^ own
        mine = pl.ds(pl.multiple_of(m * 16 + 8 * core, 8), 8)
        other = pl.ds(pl.multiple_of(m * 16 + 8 - 8 * core, 8), 8)
        theirs = []
        for part in range(3):
            at = slice(part * width, (part + 1) * width)
            keep[k, part * 8 : part * 8 + 8] = gqkv[mine, at]
            theirs.append(gqkv[other, at])
        keep[k, 24:32] = gout[mine]
        theirs.append(gout[other])
        send[k, :32] = jnp.concatenate(theirs, 0).astype(BF16)
        keep[k, 32:40] = sums
        send[k, 32:40] = low


def token_grad_kernel(per, dqkv, wqkv, vec, xhat_ref, inv_ref, dx1_ref, gx_ref, gxb_ref):
    size = per * WIN
    for c in range(dqkv.shape[0] // size):
        part = slice(c * size, (c + 1) * size)
        dh1 = dot(dqkv[part], wqkv[...], NT)
        gx = dx1_ref[part] + norm_back(dh1, xhat_ref[part], inv_ref[part], vec[0:1])
        gx_ref[part] = gx
        gxb_ref[part] = gx.astype(BF16)


def place_kernel(n_t, me, *refs):
    out, wide, sems = refs[-3:]
    sources = refs[:-3]
    own = sources[0].shape[0]
    copies = []
    for n, source in enumerate(sources):
        if source.dtype != out.dtype:
            wide[n - 1] = source[...].astype(out.dtype)
            source = wide.at[n - 1]
        at = pl.ds((lax.rem(me[0], n_t) ^ n) * own, own)
        copies.append(pltpu.make_async_copy(source, out.at[at], sems.at[n]))
        copies[-1].start()
    for copy in copies:
        copy.wait()


def finish_kernel(me, a, b, got, qkv, out, gains, biases, up, down):
    small, width = out.shape
    tall = up.shape[0]
    at = 4 * small + 8
    one = a[0] + got[:at].astype(F32)
    for part in range(3):
        qkv[:, part * width : (part + 1) * width] = one[part * small : (part + 1) * small]
    out[...] = one[3 * small : 4 * small]
    vec = pltpu.roll(one[4 * small :], width - me[0] * small, 1)[:, :small]
    gains[...] = vec[:2]
    biases[...] = vec[2:5]
    up[...] = b[0, :tall] + got[at : at + tall].astype(F32)
    down[...] = b[0, tall:] + got[at + tall :].astype(F32)


def swap(block, axis, bit):
    size = lax.axis_size(axis)
    return lax.ppermute(block, axis, [(i, i ^ bit) for i in range(size)])


def steps_of(axis):
    return [(axis, 1 << k) for k in reversed(range(lax.axis_size(axis).bit_length() - 1))]


def after(value, other):
    return lax.optimization_barrier((value, other))[0]


def halves(held):
    half = held.shape[0] // 2
    return held[:half], held[half:].astype(BF16)


def fold_step(keep, send, axis, bit):
    return keep + swap(send, axis, bit).astype(F32)


def bit_reverse(index, count):
    out = 0 * index
    for k in range(count):
        out = out | (((index >> k) & 1) << (count - 1 - k))
    return out


def by_device(block, me):
    blocks = block[None]
    for axis, bit in steps_of("dp") + steps_of("tensor"):
        blocks = jnp.concatenate([blocks, swap(blocks, axis, bit)], 0)
    count = blocks.shape[0]
    order = jnp.arange(count, dtype=jnp.int32) ^ me
    return jnp.take(blocks, bit_reverse(order, count.bit_length() - 1), axis=0)


def other_pack(w_qkv, w_out, gains, biases, w_up, w_down, me):
    small, width = w_out.shape
    qkv = w_qkv.reshape(small, 3, width).transpose(1, 0, 2).reshape(3 * small, width)
    rows = jnp.concatenate([gains, biases], 0)
    place = jnp.zeros((8, width), BF16)
    place = lax.dynamic_update_slice(place, rows, (jnp.int32(0), me * small))
    return jnp.concatenate([qkv, w_out, place], 0), jnp.concatenate([w_up, w_down.T], 0)


def other_blocks(a, b, me, n_dp, n_t):
    a = by_device(a, me)
    b = by_device(b, me)
    width = a.shape[2]
    count = n_dp * n_t
    small = width // count
    big = width // (VDP * VT)
    mats = a[:, : 4 * small].reshape(count, 4, small, width).transpose(1, 0, 2, 3)
    mats = mats.reshape(4, VDP * VT, big, width).transpose(1, 0, 2, 3).reshape(VDP * VT, 4 * big, width)
    vec = jnp.sum(a[:, 4 * small :].astype(F32), 0).astype(BF16)
    vecs = jnp.concatenate([vec[None], jnp.zeros((VDP * VT - 1, 8, width), BF16)], 0)
    a = jnp.concatenate([mats, vecs], 1)
    tall = width // n_dp
    b = b.reshape(n_dp, VT, 2, tall, width).transpose(1, 2, 0, 3, 4)
    b = b.reshape(VT, 2, VDP, width // VDP, width).transpose(2, 0, 1, 3, 4)
    b = b.reshape(VDP * VT, 2 * (width // VDP), width)

    def placed(blocks):
        pairs = blocks.reshape((CHIPS, 2) + blocks.shape[1:])
        pairs = jnp.stack([pairs[m] for m in sorted(range(CHIPS), key=spot)], 0)
        return pairs[:, 0], pairs[:, 1]

    return placed(a) + placed(b)


def other_reduce(pair_a, pair_b, me, n_dp, n_t):
    order = [fold(m) for m in range(CHIPS)]
    count = n_dp * n_t

    def whole(keep, send):
        pairs = jnp.stack([keep, send.astype(F32)], 1)
        pairs = jnp.stack([pairs[k] for k in order], 0)
        return pairs.reshape((VDP * VT,) + keep.shape[1:])

    a, b = whole(*pair_a), whole(*pair_b)
    width = a.shape[2]
    small, tall = width // count, width // n_dp
    big = width // (VDP * VT)
    mats = a[:, : 4 * big].reshape(VDP * VT, 4, big, width).transpose(1, 0, 2, 3)
    mats = mats.reshape(4, count, small, width).transpose(1, 0, 2, 3)
    mats = mats.reshape(count, 4 * small, width)
    a = jnp.concatenate([mats, jnp.broadcast_to(a[:1, 4 * big :], (count, 8, width))], 1)
    b = b.reshape(VDP, VT, 2, width // VDP, width).transpose(1, 2, 0, 3, 4)
    b = b.reshape(VT, 2, n_dp, tall, width).transpose(2, 0, 1, 3, 4)
    b = b.reshape(count, 2 * tall, width)
    results = []
    for blocks in (a, b):
        blocks = jnp.take(blocks, jnp.arange(count, dtype=jnp.int32) ^ me, axis=0)
        for axis, bit in reversed(steps_of("dp") + steps_of("tensor")):
            pairs = blocks.reshape((-1, 2) + blocks.shape[1:])
            got = swap(pairs[:, 1].astype(BF16), axis, bit)
            blocks = pairs[:, 0] + got.astype(F32)
        results.append(blocks[0])
    return results


def struct(shape, dtype):
    return jax.ShapeDtypeStruct(shape, dtype)


def call(kernel, name, args, outs, scratch=(), flops=0, limit=16):
    args = [a if isinstance(a, tuple) else (a, pltpu.VMEM) for a in args]
    moved = sum(a.size * a.dtype.itemsize for a, _ in args)
    spaces = [pl.ANY if isinstance(o, jax.ShapeDtypeStruct) else pltpu.VMEM for o in outs]
    return pl.pallas_call(
        kernel,
        name=name,
        out_shape=outs,
        in_specs=[pl.BlockSpec(memory_space=space) for _, space in args],
        out_specs=[pl.BlockSpec(memory_space=space) for space in spaces],
        scratch_shapes=list(scratch),
        compiler_params=pltpu.CompilerParams(vmem_limit_bytes=limit * MIB),
        cost_estimate=pl.CostEstimate(flops=flops, bytes_accessed=moved, transcendentals=0),
    )(*[a for a, _ in args])


def on_device(tokens, lengths, row_mask, cotangent, w_qkv, w_out, gains, biases, w_up, w_down):
    images, seq_len, width = tokens.shape
    n_dp, n_t = lax.axis_size("dp"), lax.axis_size("tensor")
    index = lax.axis_index("dp") * n_t + lax.axis_index("tensor")
    me = index.astype(jnp.int32).reshape(1)
    usual = (n_dp, n_t) == (VDP, VT)
    virt = me if usual else jnp.zeros((1,), jnp.int32)
    small = width // (n_dp * n_t)
    tall = width // n_dp
    own = images * seq_len // n_t
    rows = own // WIN
    per = 4 if rows % 4 == 0 else 1
    smem = pltpu.SMEM
    weights = (w_qkv, w_out, gains, biases, w_up, w_down)
    token_mm = 2 * own * width
    hbm = pltpu.HBM

    def in_hbm(array):
        return (pltpu.with_memory_space_constraint(array, hbm), hbm)

    fetch_in = [
        (me, smem),
        in_hbm(tokens.reshape(images * seq_len, width)),
        in_hbm(cotangent.reshape(images * seq_len, width)),
    ]
    if usual:
        weights = (w_qkv, w_out, gains, biases, w_up, w_down.T)
        pack_a, pack_b = call(
            pack_kernel,
            "pack",
            [(me, smem)] + [in_hbm(w) for w in weights],
            [
                pltpu.VMEM((1, 4 * small + 8, width), BF16),
                pltpu.VMEM((1, 2 * tall, width), BF16),
            ],
            [pltpu.VMEM(w.shape, BF16) for w in weights] + [pltpu.SemaphoreType.DMA((6,))],
        )
        fetch_in[0] = (after(me, pack_a), smem)
        held_a, b = pack_a, pack_b
        for axis, bit in steps_of("dp"):
            held_a = jnp.concatenate([held_a, swap(held_a, axis, bit)], 0)
            b = after(b, held_a)
            b = jnp.concatenate([b, swap(b, axis, bit)], 0)
        held_a = jnp.concatenate([held_a, swap(held_a, "tensor", 2)], 0)
        far_b = swap(after(b, held_a), "tensor", 2)
        got_a = swap(held_a, "tensor", 1)
    else:
        held_a, got_a, held_b, got_b = other_blocks(*other_pack(*weights, index), index, n_dp, n_t)
        b, far_b = held_b[:VDP], held_b[VDP:]
    x, cot, xhat1, inv1 = call(
        functools.partial(fetch_kernel, n_t),
        "fetch",
        fetch_in,
        [
            pltpu.VMEM((own, width), BF16),
            pltpu.VMEM((own, width), BF16),
            pltpu.VMEM((own, width), F32),
            pltpu.VMEM((own, 1), F32),
        ],
        [pltpu.SemaphoreType.DMA((2,))],
    )
    qkv, prob, o, x1, h1, wqkv, wout, vec = call(
        functools.partial(attend_kernel, n_t, per),
        "attend",
        [(me, smem), (virt, smem), (lengths, smem), (row_mask, smem), x, xhat1, held_a, got_a],
        [
            pltpu.VMEM((own, 3 * width), BF16),
            pltpu.VMEM((rows * HEADS, WIN, WIN), BF16),
            pltpu.VMEM((own, width), BF16),
            pltpu.VMEM((own, width), F32),
            pltpu.VMEM((own, width), BF16),
            pltpu.VMEM((width, 3 * width), BF16),
            pltpu.VMEM((width, width), BF16),
            pltpu.VMEM((8, width), F32),
        ],
        flops=token_mm * (4 * width + 2 * WIN),
    )
    if usual:
        far_b = after(far_b, x1)
        got_b = swap(jnp.concatenate([b, far_b], 0), "tensor", 1)
    grads_b = (CHIPS, 2 * (width // VDP), width)
    grads_a = (CHIPS, 40, width)
    kept = [pltpu.VMEM((own, 2 * width), BF16)] * 2 + [pltpu.VMEM((4, width, width), BF16)]
    h2, xhat2, inv2, f, dh2, keep_b = call(
        functools.partial(hidden_own_kernel, per),
        "hidden_own",
        [(virt, smem), x1, cot, vec, b, far_b],
        [
            pltpu.VMEM((own, width), BF16),
            pltpu.VMEM((own, width), F32),
            pltpu.VMEM((own, 1), F32),
            pltpu.VMEM((own, width), F32),
            pltpu.VMEM((own, width), F32),
            pltpu.VMEM(grads_b, F32),
        ],
        kept,
        token_mm * 12 * width,
    )
    y, dx1, g, gvec, send_b = call(
        functools.partial(hidden_other_kernel, per),
        "hidden_other",
        [(virt, smem), cot, vec, got_b, h2, xhat2, inv2, f, dh2],
        [
            pltpu.VMEM((own, width), BF16),
            pltpu.VMEM((own, width), F32),
            pltpu.VMEM((own, width), BF16),
            pltpu.VMEM((8, width), F32),
            pltpu.VMEM(grads_b, BF16),
        ],
        kept,
        token_mm * 12 * width,
    )
    y_cut = rows // 2 * WIN
    y_first = swap(y[:y_cut], "tensor", 2)
    y_second = swap(y[y_cut:], "tensor", 2)
    y_near = swap(y, "tensor", 1)
    core, xbit, zlo, zhi, ybit = ("tensor", 1), ("dp", 1), ("dp", 2), ("dp", 4), ("tensor", 2)
    dqkv, keep_a, send_a = call(
        functools.partial(back_kernel, per),
        "back",
        [(virt, smem), qkv, prob, o, g, h1, wqkv, wout, vec, gvec],
        [
            pltpu.VMEM((own, 3 * width), BF16),
            pltpu.VMEM(grads_a, F32),
            pltpu.VMEM(grads_a, BF16),
        ],
        [
            pltpu.VMEM((own, width), BF16),
            pltpu.VMEM((width, 3 * width), F32),
            pltpu.VMEM((width, width), F32),
        ],
        token_mm * (5 * width + 5 * WIN),
    )
    gx, gxb = call(
        functools.partial(token_grad_kernel, per),
        "token_grad",
        [dqkv, wqkv, vec, xhat1, inv1, dx1],
        [pltpu.VMEM((own, width), F32), pltpu.VMEM((own, width), BF16)],
        flops=token_mm * 3 * width,
    )
    gx_near = swap(after(gxb, y_near), "tensor", 1)
    gx_far = swap(gxb, "tensor", 2)
    if usual:
        held_b = fold_step(keep_b, send_b, *core)
        held_b = fold_step(*halves(held_b), *xbit)
        held_a = fold_step(keep_a, after(send_a, (y_first, held_b)), *core)
        held_a = fold_step(*halves(held_a), *xbit)
        held_b = fold_step(*halves(held_b), *zlo)
        keep, send = halves(held_a)
        send = after(send, held_b)
        y_second = after(y_second, send)
        held_a = fold_step(keep, send, *zlo)
        held_b = fold_step(*halves(held_b), *zhi)
        held_a = fold_step(*halves(held_a), *zhi)
        last = jnp.concatenate([held_a[1], held_b[1]], 0).astype(BF16)
        gx_far = after(gx_far, last)
        got = swap(last, *ybit)
    else:
        grad_a, grad_b = other_reduce((keep_a, send_a), (keep_b, send_b), index, n_dp, n_t)
        o_qkv = jnp.concatenate([grad_a[p * small : (p + 1) * small] for p in range(3)], 1)
        o_out = grad_a[3 * small : 4 * small]
        o_vec = lax.dynamic_slice_in_dim(grad_a[4 * small : 4 * small + 5], index * small, small, 1)
        o_gains, o_bias = o_vec[:2], o_vec[2:]
        o_up, o_down = grad_b[:tall], grad_b[tall:]
    gx_both = swap(gx_far, "tensor", 1)
    y_far = jnp.concatenate([y_first, y_second], 0)
    y_both = swap(y_far, "tensor", 1)

    def place(sources, dtype, wide):
        return call(
            functools.partial(place_kernel, n_t),
            "place",
            [(me, smem)] + list(sources),
            [struct((images * seq_len, width), dtype)],
            [pltpu.VMEM(wide, dtype), pltpu.SemaphoreType.DMA((n_t,))],
        )[0].reshape(images, seq_len, width)

    layer_out = place((y, y_near, y_far, y_both), BF16, (1, 16, 128))
    grad_tokens = place((gx, gx_near, gx_far, gx_both), F32, (n_t - 1, own, width))
    if usual:
        vmem = pl.BlockSpec(memory_space=pltpu.VMEM)
        shapes = [(small, 3 * width), (small, width), (2, small), (3, small), (tall, width), (tall, width)]
        got, grad_tokens = lax.optimization_barrier((got, grad_tokens))
        o_qkv, o_out, o_gains, o_bias, o_up, o_down = pl.pallas_call(
            finish_kernel,
            name="finish",
            out_shape=[struct(shape, F32) for shape in shapes],
            in_specs=[pl.BlockSpec(memory_space=smem), vmem, vmem, vmem],
            out_specs=[vmem] * 6,
        )(me, held_a, held_b, got)
    return layer_out, grad_tokens, o_qkv, o_out, o_gains, o_bias, o_up, o_down.T


def solution(mesh):
    in_specs = (
        P("dp", None, None),
        P("dp"),
        P("dp", None),
        P("dp", None, None),
        P(("dp", "tensor"), None),
        P(("dp", "tensor"), None),
        P(None, ("dp", "tensor")),
        P(None, ("dp", "tensor")),
        P("dp", "tensor"),
        P("tensor", "dp"),
    )
    out_specs = (
        P("dp", None, None),
        P("dp", None, None),
        P(("dp", "tensor"), None),
        P(("dp", "tensor"), None),
        P(None, ("dp", "tensor")),
        P(None, ("dp", "tensor")),
        P("dp", "tensor"),
        P("tensor", "dp"),
    )
    return jax.shard_map(
        on_device, mesh=mesh, in_specs=in_specs, out_specs=out_specs, check_vma=False
    )
```

```python
import functools

import jax
import jax.numpy as jnp
from jax import lax
from jax.experimental import pallas as pl
from jax.experimental.pallas import tpu as pltpu
from jax.sharding import PartitionSpec as P

HEADS = 2
WIN = 96
F32 = jnp.float32
BF16 = jnp.bfloat16
VDP, VT = 8, 4
CHIPS = VDP * VT // 2
MIB = 1 << 20

NN = ((1,), (0,))
NT = ((1,), (1,))
TN = ((0,), (0,))


def dot(a, b, dims):
    return lax.dot_general(a, b, (dims, ((), ())), preferred_element_type=F32)


def turn(i):
    return ((i & 1) << 2) | (i & 2) | ((i & 4) >> 2)


def spot(m):
    return (m % 2) * VDP + turn(m // 2)


def turn(i):
    return ((i & 1) << 2) | (i & 2) | ((i & 4) >> 2)


def spot(m):
    return (m % 2) * VDP + turn(m // 2)


def fold(m):
    out = 0
    for place, bit in enumerate(REDUCE_BITS):
        shift = 3 - place
        out = out | (((m // bit) & 1) << shift)
    return out


def norm_parts(values):
    center = values - jnp.mean(values, -1, keepdims=True)
    inv = lax.rsqrt(jnp.mean(center * center, -1, keepdims=True) + 1e-05)
    return center * inv, inv


def norm_back(grad, xhat, inv, gain):
    scaled = grad * gain
    return inv * (
        scaled
        - jnp.mean(scaled, -1, keepdims=True)
        - xhat * jnp.mean(scaled * xhat, -1, keepdims=True)
    )


def gelu_both(u):
    c = 0.7978845608028654
    u2 = u * u
    t = jnp.tanh(u * (c + (c * 0.044715) * u2))
    half = 0.5 + 0.5 * t
    value = u * half
    slope = half + (value - value * half) * (2 * c + (6 * c * 0.044715) * u2)
    return value, slope


def pack_kernel(me, *refs):
    sources, (small_ref, big_ref), held, sems = refs[:6], refs[6:8], refs[8:14], refs[14]
    copies = [pltpu.make_async_copy(a, b, sems.at[n]) for n, (a, b) in enumerate(zip(sources, held))]
    for copy in copies:
        copy.start()
    qkv, out, gains, biases, up, down = held
    small, width = out.shape
    tall = up.shape[0]
    lane = lax.broadcasted_iota(jnp.int32, (1, width), 1)
    mine = lane // small == me[0]
    for copy in copies:
        copy.wait()
    for part in range(3):
        small_ref[0, part * small : (part + 1) * small] = qkv[:, part * width : (part + 1) * width]
    small_ref[0, 3 * small : 4 * small] = out[...]
    rows = [gains[0:1], gains[1:2], biases[0:1], biases[1:2], biases[2:3]]
    vals = jnp.concatenate(rows + [jnp.zeros((3, small), BF16)], 0).astype(F32)
    wide = jnp.concatenate([vals] * (width // small), 1)
    small_ref[0, 4 * small : 4 * small + 8] = jnp.where(mine, wide, 0.0).astype(BF16)
    big_ref[0, :tall] = up[...]
    big_ref[0, tall:] = down[...]


def fetch_kernel(me, tokens, cot, x_ref, cot_ref, xhat_ref, inv_ref, sems):
    own = x_ref.shape[0]
    at = pl.ds(lax.rem(me[0], 2) * own, own)
    first = pltpu.make_async_copy(tokens.at[at], x_ref, sems.at[0])
    second = pltpu.make_async_copy(cot.at[at], cot_ref, sems.at[1])
    first.start()
    second.start()
    first.wait()
    for n in range(own // WIN):
        part = slice(n * WIN, (n + 1) * WIN)
        xhat_ref[part], inv_ref[part] = norm_parts(x_ref[part].astype(F32))
    second.wait()


def attend_kernel(
    per, me, virt, lens, live, x_ref, xhat_ref, held, got,
    qkv_ref, prob_ref, o_ref, x1_ref, h1_ref, wqkv, wout, vec,
):
    tokens, width = x_ref.shape
    rows = tokens // WIN
    hs = width // HEADS
    here = spot(virt[0] // 2) % VDP
    y_own = (virt[0] // 2) % 2
    first = virt[0] % 2 == 0
    total = jnp.zeros((8, width), F32)
    for m in range(CHIPS):
        k = spot(m) ^ (here + y_own * VDP)
        a = held[k].astype(F32)
        b = got[k].astype(F32)
        even = jnp.where(first, a, b)
        odd = jnp.where(first, b, a)
        for part in range(3):
            both = jnp.concatenate([even[part * 8 : part * 8 + 8], odd[part * 8 : part * 8 + 8]], 0)
            wqkv[m * 16 : m * 16 + 16, part * width : (part + 1) * width] = both.astype(BF16)
        both = jnp.concatenate([even[24:32], odd[24:32]], 0)
        wout[m * 16 : m * 16 + 16] = both.astype(BF16)
        total = total + a[32:40] + b[32:40]
    vec[...] = total
    scale = hs**-0.5
    ii = lax.broadcasted_iota(jnp.int32, (WIN, WIN), 0)
    jj = lax.broadcasted_iota(jnp.int32, (WIN, WIN), 1)
    same = ii == jj
    image_rows = live.shape[1]
    base = lax.rem(me[0], 2) * rows
    for c in range(rows // per):
        part = slice(c * per * WIN, (c + 1) * per * WIN)
        h1 = (xhat_ref[part] * total[0:1] + total[2:3]).astype(BF16)
        h1_ref[part] = h1
        qkv = dot(h1, wqkv[...], NN).astype(BF16)
        qkv_ref[part] = qkv
        pairs = [(r, h) for r in range(c * per, (c + 1) * per) for h in range(HEADS)]
        scores = []
        for r, h in pairs:
            at = slice((r - c * per) * WIN, (r - c * per + 1) * WIN)
            q = qkv[at, h * hs : (h + 1) * hs]
            k = qkv[at, width + h * hs : width + (h + 1) * hs]
            scores.append(dot(q, k, NT))
        allowed = []
        for r in range(c * per, (c + 1) * per):
            row = base + r
            image = row // image_rows
            inside = row - image * image_rows
            reach = jnp.where(live[image, inside] == 1, lens[image] - inside * WIN, 0)
            allowed.append(same | (jj < jnp.minimum(ii, reach)))
        probs = []
        for (r, h), s in zip(pairs, scores):
            s = jnp.where(allowed[r - c * per], s, -1e30)
            e = jnp.exp((s - jnp.max(s, -1, keepdims=True)) * scale)
            probs.append((e * (1.0 / jnp.sum(e, -1, keepdims=True))).astype(BF16))
        mixed = []
        for (r, h), p in zip(pairs, probs):
            at = slice((r - c * per) * WIN, (r - c * per + 1) * WIN)
            v = qkv[at, 2 * width + h * hs : 2 * width + (h + 1) * hs]
            mixed.append(dot(p, v, NN).astype(BF16))
        for (r, h), p in zip(pairs, probs):
            prob_ref[r * HEADS + h] = p
        o = jnp.concatenate(
            [jnp.concatenate(mixed[n : n + HEADS], 1) for n in range(0, len(mixed), HEADS)], 0
        )
        o_ref[part] = o
        x1_ref[part] = x_ref[part].astype(F32) + dot(o, wout[...], NN)


def join(virt, blocks, n, out):
    tall = blocks.shape[1] // 2
    here = turn(virt[0] // 4)
    for i in range(VDP):
        k = turn(i) ^ here
        at = slice(i * tall, (i + 1) * tall)
        out[2 * n, at] = blocks[k, :tall]
        out[2 * n + 1, at] = blocks[k, tall:]


def hidden_half(part, h2, dyb, mats, f, dh2, a_ref, du_ref):
    for n in range(2):
        up, down = mats[2 * n], mats[2 * n + 1]
        a, slope = gelu_both(dot(h2, up, NN))
        a = a.astype(BF16)
        f = f + dot(a, down, NT)
        du = (dot(dyb, down, NN) * slope).astype(BF16)
        dh2 = dh2 + dot(du, up, NT)
        if n == 0:
            a_ref[part] = a
            du_ref[part] = du
    return f, dh2


def store_hidden_grads(virt, h2_ref, cot_ref, a_ref, du_ref, out):
    tall = h2_ref.shape[1] // VDP
    gdown = dot(cot_ref[...], a_ref[...], TN).astype(out.dtype)
    gup = dot(h2_ref[...], du_ref[...], TN).astype(out.dtype)
    here = turn(virt[0] // 4)
    for i in range(VDP):
        at = slice(i * tall, (i + 1) * tall)
        k = turn(i) ^ here
        out[k, :tall] = gup[at]
        out[k, tall : 2 * tall] = gdown[at]


def hidden_own_kernel(
    per, virt, x1_ref, cot_ref, vec, near, far, h2_ref, xhat_ref, inv_ref, f_ref, dh2_ref, keep,
    a_ref, du_ref, mats,
):
    tokens = x1_ref.shape[0]
    size = per * WIN
    join(virt, near, 0, mats)
    join(virt, far, 1, mats)
    for c in range(tokens // size):
        part = slice(c * size, (c + 1) * size)
        x1 = x1_ref[part]
        xhat, inv = norm_parts(x1)
        xhat_ref[part] = xhat
        inv_ref[part] = inv
        h2 = (xhat * vec[1:2] + vec[3:4]).astype(BF16)
        h2_ref[part] = h2
        f = x1 + vec[4:5]
        f, dh2 = hidden_half(part, h2, cot_ref[part], mats, f, jnp.zeros_like(f), a_ref, du_ref)
        f_ref[part] = f
        dh2_ref[part] = dh2
    store_hidden_grads(virt, h2_ref, cot_ref, a_ref, du_ref, keep)


def hidden_other_kernel(
    per, virt, cot_ref, vec, got, h2_ref, xhat_ref, inv_ref, f_ref, dh2_ref, o_ref,
    y_ref, dx1_ref, g_ref, keep, send,
    a_ref, du_ref, mats, gout,
):
    tokens, width = h2_ref.shape
    size = per * WIN
    join(virt, got.at[:VDP], 0, mats)
    join(virt, got.at[VDP:], 1, mats)
    sums = [jnp.zeros((1, width), F32)] * 3
    for c in range(tokens // size):
        part = slice(c * size, (c + 1) * size)
        dyb = cot_ref[part]
        f, dh2 = hidden_half(
            part, h2_ref[part], dyb, mats, f_ref[part], dh2_ref[part], a_ref, du_ref
        )
        y_ref[part] = f.astype(BF16)
        dy = dyb.astype(F32)
        xhat = xhat_ref[part]
        dx1 = dy + norm_back(dh2, xhat, inv_ref[part], vec[1:2])
        dx1_ref[part] = dx1
        g_ref[part] = dx1.astype(BF16)
        terms = (dh2 * xhat, dh2, dy)
        sums = [a + jnp.sum(b, 0, keepdims=True) for a, b in zip(sums, terms)]
    store_hidden_grads(virt, h2_ref, cot_ref, a_ref, du_ref, send)
    gout[...] = dot(o_ref[...], g_ref[...], TN)
    zero = jnp.zeros((1, width), F32)
    total = jnp.concatenate([zero, sums[0], zero, sums[1], sums[2], zero, zero, zero], 0)
    here = turn(virt[0] // 4)
    for i in range(VDP):
        k = turn(i) ^ here
        keep[k, :8] = gout[own_rows(virt, i, 0)]
        keep[k, 8:] = total
        theirs = jnp.concatenate([gout[own_rows(virt, i, 1)], total], 0)
        send[k, width // 4 :] = theirs.astype(BF16)


def own_rows(virt, i, other):
    core = virt[0] % 2
    core = 1 - core if other else core
    return pl.ds(pl.multiple_of(i * 32 + ((virt[0] // 2) % 2) * 16 + core * 8, 8), 8)


def back_kernel(
    per, virt, qkv_ref, prob_ref, g_ref, h1_ref, wqkv, wout, vec,
    dqkv, keep, send,
    do_ref, gqkv,
):
    tokens, width = g_ref.shape
    hs = width // HEADS
    scale = hs**-0.5
    do_ref[...] = dot(g_ref[...], wout[...], NT).astype(BF16)
    every = [(r, h) for r in range(tokens // WIN) for h in range(HEADS)]

    def piece(ref, r, h, part=0):
        return ref[r * WIN : (r + 1) * WIN, part * width + h * hs : part * width + (h + 1) * hs]

    for start in range(0, len(every), 2 * per):
        pairs = every[start : start + 2 * per]
        probs = [prob_ref[r * HEADS + h] for r, h in pairs]
        dos = [piece(do_ref, r, h) for r, h in pairs]
        dps = [dot(a, piece(qkv_ref, r, h, 2), NT) for a, (r, h) in zip(dos, pairs)]
        dvs = [dot(p, a, TN).astype(BF16) for p, a in zip(probs, dos)]
        dss = []
        for p, dp in zip(probs, dps):
            pf = p.astype(F32)
            ds = pf * (dp - jnp.sum(dp * pf, -1, keepdims=True)) * scale
            dss.append(ds.astype(BF16))
        dqs = [dot(ds, piece(qkv_ref, r, h, 1), NN).astype(BF16) for ds, (r, h) in zip(dss, pairs)]
        dks = [dot(ds, piece(qkv_ref, r, h, 0), TN).astype(BF16) for ds, (r, h) in zip(dss, pairs)]
        for n, (r, h) in enumerate(pairs):
            for part, values in enumerate((dqs, dks, dvs)):
                at = slice(part * width + h * hs, part * width + (h + 1) * hs)
                dqkv[r * WIN : (r + 1) * WIN, at] = values[n]
    gqkv[...] = dot(h1_ref[...], dqkv[...], TN)
    total = jnp.zeros((1, 3 * width), F32)
    for r in range(tokens // WIN):
        total = total + jnp.sum(dqkv[r * WIN : (r + 1) * WIN].astype(F32), 0, keepdims=True)
    w = wqkv[...].astype(F32)
    cols = jnp.concatenate([
        jnp.broadcast_to(jnp.sum(w * gqkv[...], -1, keepdims=True), (width, 64)),
        jnp.broadcast_to(jnp.sum(w * total, -1, keepdims=True), (width, 64)),
    ], 1)
    lines = cols.T
    from_grad, from_total = lines[0:1], lines[64:65]
    gain = (from_grad - vec[2:3] * from_total) / vec[0:1]
    zero = jnp.zeros((1, width), F32)
    sums = jnp.concatenate([gain, zero, from_total] + [zero] * 5, 0)
    here = turn(virt[0] // 4)
    for i in range(VDP):
        k = turn(i) ^ here
        theirs = []
        for part in range(3):
            at = slice(part * width, (part + 1) * width)
            keep[k, part * 8 : part * 8 + 8] = gqkv[own_rows(virt, i, 0), at]
            theirs.append(gqkv[own_rows(virt, i, 1), at])
        keep[k, 24:] = sums
        send[k] = jnp.concatenate(theirs + [sums], 0).astype(BF16)


def token_grad_kernel(per, me, dqkv, wqkv, vec, xhat_ref, inv_ref, dx1_ref, full, gxb_ref, gx, sems):
    own = dqkv.shape[0]
    size = per * WIN
    copies = []
    for c in range(own // size):
        part = slice(c * size, (c + 1) * size)
        dh1 = dot(dqkv[part], wqkv[...], NT)
        values = dx1_ref[part] + norm_back(dh1, xhat_ref[part], inv_ref[part], vec[0:1])
        gx[part] = values
        gxb_ref[part] = values.astype(BF16)
        at = pl.ds(lax.rem(me[0], 2) * own + c * size, size)
        copies.append(pltpu.make_async_copy(gx.at[pl.ds(c * size, size)], full.at[at], sems.at[c]))
        copies[-1].start()
    for copy in copies:
        copy.wait()


def place_both_kernel(me, mine, theirs, out, sems):
    own = mine.shape[0]
    copies = []
    for n, source in enumerate((mine, theirs)):
        at = pl.ds((lax.rem(me[0], 2) ^ n) * own, own)
        copies.append(pltpu.make_async_copy(source, out.at[at], sems.at[n]))
        copies[-1].start()
    for copy in copies:
        copy.wait()


def place_other_kernel(per, me, full, theirs, out, wide, sems):
    own = theirs.shape[0]
    size = per * WIN
    copies = []
    for c in range(own // size):
        part = pl.ds(c * size, size)
        wide[part] = theirs[part].astype(F32)
        at = pl.ds((1 - lax.rem(me[0], 2)) * own + c * size, size)
        copies.append(pltpu.make_async_copy(wide.at[part], out.at[at], sems.at[c]))
        copies[-1].start()
    for copy in copies:
        copy.wait()


def finish_hidden_kernel(keep, got, out, up, down, vec):
    total = keep[0] + got[0].astype(F32)
    tall = up.shape[0]
    small = out.shape[0]
    up[...] = total[:tall]
    down[...] = total[tall : 2 * tall]
    out[...] = total[2 * tall : 2 * tall + small]
    vec[...] = total[2 * tall + small :]


def finish_kernel(me, keep, got, vec, qkv, gains, biases):
    total = keep[0] + got[0].astype(F32)
    small = qkv.shape[0]
    width = vec.shape[1]
    for part in range(3):
        qkv[:, part * width : (part + 1) * width] = total[part * small : (part + 1) * small]
    both = vec[...] + total[3 * small :]
    both = pltpu.roll(both, width - me[0] * small, 1)[:, :small]
    gains[...] = both[:2]
    biases[...] = both[2:5]


def swap(block, axis, bit):
    size = lax.axis_size(axis)
    return lax.ppermute(block, axis, [(i, i ^ bit) for i in range(size)])


def steps_of(axis):
    return [(axis, 1 << k) for k in reversed(range(lax.axis_size(axis).bit_length() - 1))]


def after(value, other):
    return lax.optimization_barrier((value, other))[0]


def halves(held):
    half = held.shape[0] // 2
    return held[:half], held[half:].astype(BF16)


def fold_step(keep, send, axis, bit):
    return keep + swap(send, axis, bit).astype(F32)


def bit_reverse(index, count):
    out = 0 * index
    for k in range(count):
        out = out | (((index >> k) & 1) << (count - 1 - k))
    return out


def by_device(block, me):
    blocks = block[None]
    for axis, bit in steps_of("dp") + steps_of("tensor"):
        blocks = jnp.concatenate([blocks, swap(blocks, axis, bit)], 0)
    count = blocks.shape[0]
    order = jnp.arange(count, dtype=jnp.int32) ^ me
    return jnp.take(blocks, bit_reverse(order, count.bit_length() - 1), axis=0)


def other_pack(w_qkv, w_out, gains, biases, w_up, w_down, me):
    small, width = w_out.shape
    qkv = w_qkv.reshape(small, 3, width).transpose(1, 0, 2).reshape(3 * small, width)
    rows = jnp.concatenate([gains, biases], 0)
    place = jnp.zeros((8, width), BF16)
    place = lax.dynamic_update_slice(place, rows, (jnp.int32(0), me * small))
    return jnp.concatenate([qkv, w_out, place], 0), jnp.concatenate([w_up, w_down.T], 0)


def other_blocks(a, b, me, n_dp, n_t):
    a = by_device(a, me)
    b = by_device(b, me)
    width = a.shape[2]
    count = n_dp * n_t
    small = width // count
    big = width // (VDP * VT)
    mats = a[:, : 4 * small].reshape(count, 4, small, width).transpose(1, 0, 2, 3)
    mats = mats.reshape(4, VDP * VT, big, width).transpose(1, 0, 2, 3).reshape(VDP * VT, 4 * big, width)
    vec = jnp.sum(a[:, 4 * small :].astype(F32), 0).astype(BF16)
    vecs = jnp.concatenate([vec[None], jnp.zeros((VDP * VT - 1, 8, width), BF16)], 0)
    a = jnp.concatenate([mats, vecs], 1)
    tall = width // n_dp
    b = b.reshape(n_dp, VT, 2, tall, width).transpose(1, 2, 0, 3, 4)
    b = b.reshape(VT, 2, VDP, width // VDP, width).transpose(2, 0, 1, 3, 4)
    b = b.reshape(VDP * VT, 2 * (width // VDP), width)

    y_own = (me // 2) % 2

    def placed(blocks):
        pairs = blocks.reshape((CHIPS, 2) + blocks.shape[1:])
        pairs = jnp.stack([pairs[m] for m in sorted(range(CHIPS), key=spot)], 0)
        pairs = jnp.where(y_own == 1, jnp.roll(pairs, VDP, 0), pairs)
        return pairs[:, 0], pairs[:, 1]

    return placed(a) + placed(b)


def other_reduce(pair_a, pair_b, me, n_dp, n_t):
    count = n_dp * n_t
    y_own = (me // 2) % 2

    def whole(keep, send):
        pairs = jnp.stack([keep, send.astype(F32)], 1)
        pairs = jnp.stack([pairs[turn(i)] for i in range(VDP)], 0)
        none = jnp.zeros_like(pairs)
        both = jnp.stack([jnp.where(y_own == y, pairs, none) for y in range(2)], 1)
        return both.reshape((VDP * VT,) + keep.shape[1:])

    def rows_of(blocks, parts):
        big = blocks.shape[1] // parts
        mats = blocks.reshape(VDP * VT, parts, big, -1).transpose(1, 0, 2, 3)
        mats = mats.reshape(parts, count, VDP * VT * big // count, -1).transpose(1, 0, 2, 3)
        return mats.reshape(count, -1, blocks.shape[2])

    def vec_of(blocks):
        picked = jnp.where(y_own == 0, blocks[0], 0.0)
        return jnp.broadcast_to(picked[None], (count,) + picked.shape)

    a, b = whole(*pair_a), whole(*pair_b)
    width = a.shape[2]
    tall, high = width // n_dp, width // VDP
    cols = b[:, : 2 * high].reshape(VDP, VT, 2, high, width).transpose(1, 2, 0, 3, 4)
    cols = cols.reshape(VT, 2, n_dp, tall, width).transpose(2, 0, 1, 3, 4)
    cols = cols.reshape(count, 2 * tall, width)
    vec = vec_of(a[:, 24:]) + vec_of(b[:, 2 * high + 8 :])
    a = jnp.concatenate([rows_of(a[:, :24], 3), vec], 1)
    b = jnp.concatenate([cols, rows_of(b[:, 2 * high : 2 * high + 8], 1)], 1)
    results = []
    for blocks in (a, b):
        blocks = jnp.take(blocks, jnp.arange(count, dtype=jnp.int32) ^ me, axis=0)
        for axis, bit in reversed(steps_of("dp") + steps_of("tensor")):
            pairs = blocks.reshape((-1, 2) + blocks.shape[1:])
            got = swap(pairs[:, 1].astype(BF16), axis, bit)
            blocks = pairs[:, 0] + got.astype(F32)
        results.append(blocks[0])
    return results


def struct(shape, dtype):
    return jax.ShapeDtypeStruct(shape, dtype)


def call(kernel, name, args, outs, scratch=(), flops=0, limit=16, alias=None):
    args = [a if isinstance(a, tuple) else (a, pltpu.VMEM) for a in args]
    moved = sum(a.size * a.dtype.itemsize for a, _ in args)
    spaces = [pl.ANY if isinstance(o, jax.ShapeDtypeStruct) else pltpu.VMEM for o in outs]
    return pl.pallas_call(
        kernel,
        name=name,
        out_shape=outs,
        in_specs=[pl.BlockSpec(memory_space=space) for _, space in args],
        out_specs=[pl.BlockSpec(memory_space=space) for space in spaces],
        scratch_shapes=list(scratch),
        input_output_aliases=alias or {},
        compiler_params=pltpu.CompilerParams(vmem_limit_bytes=limit * MIB),
        cost_estimate=pl.CostEstimate(flops=flops, bytes_accessed=moved, transcendentals=0),
    )(*[a for a, _ in args])


def on_device(tokens, lengths, row_mask, cotangent, w_qkv, w_out, gains, biases, w_up, w_down):
    images, seq_len, width = tokens.shape
    n_dp, n_t = lax.axis_size("dp"), lax.axis_size("tensor")
    index = lax.axis_index("dp") * n_t + lax.axis_index("tensor")
    me = index.astype(jnp.int32).reshape(1)
    usual = (n_dp, n_t) == (VDP, VT)
    virt = me if usual else (index // 2 % 2 * 2).astype(jnp.int32).reshape(1)
    small = width // (n_dp * n_t)
    tall = width // n_dp
    own = images * seq_len // 2
    rows = own // WIN
    per = 4 if rows % 4 == 0 else 1
    smem = pltpu.SMEM
    weights = (w_qkv, w_out, gains, biases, w_up, w_down)
    token_mm = 2 * own * width
    hbm = pltpu.HBM

    def in_hbm(array):
        return (pltpu.with_memory_space_constraint(array, hbm), hbm)

    def fetch(*args):
        return call(
            fetch_kernel,
            "fetch",
            args,
            [
                pltpu.VMEM((own, width), BF16),
                pltpu.VMEM((own, width), BF16),
                pltpu.VMEM((own, width), F32),
                pltpu.VMEM((own, 1), F32),
            ],
            [pltpu.SemaphoreType.DMA((2,))],
        )

    fetch_in = [
        (me, smem),
        in_hbm(tokens.reshape(images * seq_len, width)),
        in_hbm(cotangent.reshape(images * seq_len, width)),
    ]
    if usual:
        weights = (w_qkv, w_out, gains, biases, w_up, w_down.T)
        pack_a, pack_b = call(
            pack_kernel,
            "pack",
            [(me, smem)] + [in_hbm(w) for w in weights],
            [
                pltpu.VMEM((1, 4 * small + 8, width), BF16),
                pltpu.VMEM((1, 2 * tall, width), BF16),
            ],
            [pltpu.VMEM(w.shape, BF16) for w in weights] + [pltpu.SemaphoreType.DMA((6,))],
        )
        fetch_in[0] = (after(me, pack_a), smem)
        held_a, b = pack_a, pack_b
        x, cot, xhat1, inv1 = fetch(*fetch_in)
        for n, (axis, bit) in enumerate(steps_of("dp")):
            held_a = jnp.concatenate([held_a, swap(held_a, axis, bit)], 0)
            if n == 0:
                held_a = after(held_a, xhat1)
            b = after(b, held_a)
            b = jnp.concatenate([b, swap(b, axis, bit)], 0)
        held_a = jnp.concatenate([held_a, swap(held_a, "tensor", 2)], 0)
        far_b = swap(after(b, held_a), "tensor", 2)
        got_a = swap(held_a, "tensor", 1)
    else:
        held_a, got_a, held_b, got_b = other_blocks(*other_pack(*weights, index), index, n_dp, n_t)
        b, far_b = held_b[:VDP], held_b[VDP:]
        x, cot, xhat1, inv1 = fetch(*fetch_in)
    qkv, prob, o, x1, h1, wqkv, wout, vec = call(
        functools.partial(attend_kernel, per),
        "attend",
        [(me, smem), (virt, smem), (lengths, smem), (row_mask, smem), x, xhat1, held_a, got_a],
        [
            pltpu.VMEM((own, 3 * width), BF16),
            pltpu.VMEM((rows * HEADS, WIN, WIN), BF16),
            pltpu.VMEM((own, width), BF16),
            pltpu.VMEM((own, width), F32),
            pltpu.VMEM((own, width), BF16),
            pltpu.VMEM((width, 3 * width), BF16),
            pltpu.VMEM((width, width), BF16),
            pltpu.VMEM((8, width), F32),
        ],
        flops=token_mm * (4 * width + 2 * WIN),
    )
    if usual:
        far_b = after(far_b, x1)
        got_b = swap(jnp.concatenate([b, far_b], 0), "tensor", 1)
    tall_b = 2 * (width // VDP)
    kept = [pltpu.VMEM((own, width), BF16)] * 2 + [pltpu.VMEM((4, width, width), BF16)]
    h2, xhat2, inv2, f, dh2, keep_b = call(
        functools.partial(hidden_own_kernel, per),
        "hidden_own",
        [(virt, smem), x1, cot, vec, b, far_b],
        [
            pltpu.VMEM((own, width), BF16),
            pltpu.VMEM((own, width), F32),
            pltpu.VMEM((own, 1), F32),
            pltpu.VMEM((own, width), F32),
            pltpu.VMEM((own, width), F32),
            pltpu.VMEM((VDP, tall_b, width), F32),
        ],
        kept,
        token_mm * 10 * width,
    )
    y, dx1, g, keep_o, send_b = call(
        functools.partial(hidden_other_kernel, per),
        "hidden_other",
        [(virt, smem), cot, vec, got_b, h2, xhat2, inv2, f, dh2, o],
        [
            pltpu.VMEM((own, width), BF16),
            pltpu.VMEM((own, width), F32),
            pltpu.VMEM((own, width), BF16),
            pltpu.VMEM((VDP, 16, width), F32),
            pltpu.VMEM((VDP, tall_b + 16, width), BF16),
        ],
        kept + [pltpu.VMEM((width, width), F32)],
        token_mm * 11 * width,
    )
    keep_b = jnp.concatenate([keep_b, keep_o], 1)
    y_near = swap(y, "tensor", 1)
    core, xbit, zlo, zhi = ("tensor", 1), ("dp", 1), ("dp", 2), ("dp", 4)
    dqkv, keep_a, send_a = call(
        functools.partial(back_kernel, per),
        "back",
        [(virt, smem), qkv, prob, g, h1, wqkv, wout, vec],
        [
            pltpu.VMEM((own, 3 * width), BF16),
            pltpu.VMEM((VDP, 32, width), F32),
            pltpu.VMEM((VDP, 32, width), BF16),
        ],
        [pltpu.VMEM((own, width), BF16), pltpu.VMEM((width, 3 * width), F32)],
        token_mm * (4 * width + 5 * WIN),
    )
    gx, gxb = call(
        functools.partial(token_grad_kernel, per),
        "token_grad",
        [(me, smem), dqkv, wqkv, vec, xhat1, inv1, dx1],
        [struct((images * seq_len, width), F32), pltpu.VMEM((own, width), BF16)],
        [pltpu.VMEM((own, width), F32), pltpu.SemaphoreType.DMA((rows // per,))],
        flops=token_mm * 3 * width,
    )
    def place(y_near, gx_near):
        layer_out = call(
            place_both_kernel,
            "place_both",
            [(me, smem), y, y_near],
            [struct((images * seq_len, width), BF16)],
            [pltpu.SemaphoreType.DMA((2,))],
        )[0].reshape(images, seq_len, width)
        grad_tokens = call(
            functools.partial(place_other_kernel, per),
            "place_other",
            [(me, smem), (gx, pl.ANY), gx_near],
            [struct((images * seq_len, width), F32)],
            [pltpu.VMEM((own, width), F32), pltpu.SemaphoreType.DMA((rows // per,))],
            alias={1: 0},
        )[0].reshape(images, seq_len, width)
        return layer_out, grad_tokens

    if usual:
        held_b = fold_step(keep_b, send_b, *core)
        held_b = fold_step(*halves(held_b), *xbit)
        held_a = fold_step(keep_a, after(send_a, (held_b, y_near)), *core)
        gxb = after(gxb, held_a)
        held_a = fold_step(*halves(held_a), *xbit)
        held_b = fold_step(*halves(held_b), *zlo)
        keep, send = halves(held_a)
        held_a = fold_step(keep, after(send, held_b), *zlo)
        send = held_b[1:].astype(BF16)
        got = swap(send, *zhi)
        vmem = pl.BlockSpec(memory_space=pltpu.VMEM)
        o_out, o_up, o_down, vec_b = pl.pallas_call(
            finish_hidden_kernel,
            name="finish_hidden",
            out_shape=[
                struct((small, width), F32),
                struct((tall, width), F32),
                struct((tall, width), F32),
                pltpu.VMEM((8, width), F32),
            ],
            in_specs=[vmem] * 2,
            out_specs=[vmem] * 4,
        )(held_b, got)
        got = swap(held_a[1:].astype(BF16), *zhi)
        layer_out, grad_tokens = place(y_near, swap(gxb, "tensor", 1))
        got = after(got, (grad_tokens, layer_out))
        o_qkv, o_gains, o_bias = pl.pallas_call(
            finish_kernel,
            name="finish",
            out_shape=[struct(shape, F32) for shape in ((small, 3 * width), (2, small), (3, small))],
            in_specs=[pl.BlockSpec(memory_space=smem)] + [vmem] * 3,
            out_specs=[vmem] * 3,
        )(me, held_a, got, vec_b)
    else:
        layer_out, grad_tokens = place(y_near, swap(gxb, "tensor", 1))
        grad_a, grad_b = other_reduce((keep_a, send_a), (keep_b, send_b), index, n_dp, n_t)
        o_qkv = jnp.concatenate([grad_a[p * small : (p + 1) * small] for p in range(3)], 1)
        o_vec = lax.dynamic_slice_in_dim(grad_a[3 * small : 3 * small + 5], index * small, small, 1)
        o_gains, o_bias = o_vec[:2], o_vec[2:]
        o_up, o_down, o_out = grad_b[:tall], grad_b[tall : 2 * tall], grad_b[2 * tall :]
    return layer_out, grad_tokens, o_qkv, o_out, o_gains, o_bias, o_up, o_down.T


def solution(mesh):
    in_specs = (
        P("dp", None, None),
        P("dp"),
        P("dp", None),
        P("dp", None, None),
        P(("dp", "tensor"), None),
        P(("dp", "tensor"), None),
        P(None, ("dp", "tensor")),
        P(None, ("dp", "tensor")),
        P("dp", "tensor"),
        P("tensor", "dp"),
    )
    out_specs = (
        P("dp", None, None),
        P("dp", None, None),
        P(("dp", "tensor"), None),
        P(("dp", "tensor"), None),
        P(None, ("dp", "tensor")),
        P(None, ("dp", "tensor")),
        P("dp", "tensor"),
        P("tensor", "dp"),
    )
    return jax.shard_map(
        on_device, mesh=mesh, in_specs=in_specs, out_specs=out_specs, check_vma=False
    )
```

```python
import functools

import jax
import jax.numpy as jnp
from jax import lax
from jax.experimental import pallas as pl
from jax.experimental.pallas import tpu as pltpu
from jax.sharding import PartitionSpec as P

HEADS = 2
WIN = 96
F32 = jnp.float32
BF16 = jnp.bfloat16
VDP, VT = 8, 4
CHIPS = VDP * VT // 2
MIB = 1 << 20

NN = ((1,), (0,))
NT = ((1,), (1,))
TN = ((0,), (0,))


def dot(a, b, dims):
    return lax.dot_general(a, b, (dims, ((), ())), preferred_element_type=F32)


def turn(i):
    return ((i & 1) << 2) | (i & 2) | ((i & 4) >> 2)


def spot(m):
    return (m % 2) * VDP + turn(m // 2)


def turn(i):
    return ((i & 1) << 2) | (i & 2) | ((i & 4) >> 2)


def spot(m):
    return (m % 2) * VDP + turn(m // 2)


def fold(m):
    out = 0
    for place, bit in enumerate(REDUCE_BITS):
        shift = 3 - place
        out = out | (((m // bit) & 1) << shift)
    return out


def norm_parts(values):
    center = values - jnp.mean(values, -1, keepdims=True)
    inv = lax.rsqrt(jnp.mean(center * center, -1, keepdims=True) + 1e-05)
    return center * inv, inv


def norm_back(grad, xhat, inv, gain):
    scaled = grad * gain
    return inv * (
        scaled
        - jnp.mean(scaled, -1, keepdims=True)
        - xhat * jnp.mean(scaled * xhat, -1, keepdims=True)
    )


def gelu_both(u):
    c = 0.7978845608028654
    u2 = u * u
    t = jnp.tanh(u * (c + (c * 0.044715) * u2))
    half = 0.5 + 0.5 * t
    value = u * half
    slope = half + (value - value * half) * (2 * c + (6 * c * 0.044715) * u2)
    return value, slope


def pack_kernel(me, *refs):
    sources, (small_ref, big_ref), held, sems = refs[:6], refs[6:8], refs[8:14], refs[14]
    copies = [pltpu.make_async_copy(a, b, sems.at[n]) for n, (a, b) in enumerate(zip(sources, held))]
    for copy in copies:
        copy.start()
    qkv, out, gains, biases, up, down = held
    small, width = out.shape
    tall = up.shape[0]
    lane = lax.broadcasted_iota(jnp.int32, (1, width), 1)
    mine = lane // small == me[0]
    for copy in copies:
        copy.wait()
    for part in range(3):
        small_ref[0, part * small : (part + 1) * small] = qkv[:, part * width : (part + 1) * width]
    small_ref[0, 3 * small : 4 * small] = out[...]
    rows = [gains[0:1], gains[1:2], biases[0:1], biases[1:2], biases[2:3]]
    vals = jnp.concatenate(rows + [jnp.zeros((3, small), BF16)], 0).astype(F32)
    wide = jnp.concatenate([vals] * (width // small), 1)
    small_ref[0, 4 * small : 4 * small + 8] = jnp.where(mine, wide, 0.0).astype(BF16)
    big_ref[0, :tall] = up[...]
    big_ref[0, tall:] = down[...]


def fetch_kernel(me, tokens, cot, x_ref, cot_ref, xhat_ref, inv_ref, sems):
    own = x_ref.shape[0]
    at = pl.ds(lax.rem(me[0], 2) * own, own)
    first = pltpu.make_async_copy(tokens.at[at], x_ref, sems.at[0])
    second = pltpu.make_async_copy(cot.at[at], cot_ref, sems.at[1])
    first.start()
    second.start()
    first.wait()
    for n in range(own // WIN):
        part = slice(n * WIN, (n + 1) * WIN)
        xhat_ref[part], inv_ref[part] = norm_parts(x_ref[part].astype(F32))
    second.wait()


def attend_kernel(
    per, me, virt, lens, live, x_ref, xhat_ref, held, got,
    qkv_ref, prob_ref, o_ref, x1_ref, h1_ref, wqkv, wout, vec,
):
    tokens, width = x_ref.shape
    rows = tokens // WIN
    hs = width // HEADS
    here = spot(virt[0] // 2) % VDP
    y_own = (virt[0] // 2) % 2
    first = virt[0] % 2 == 0
    total = jnp.zeros((8, width), F32)
    for m in range(CHIPS):
        k = spot(m) ^ (here + y_own * VDP)
        a = held[k].astype(F32)
        b = got[k].astype(F32)
        even = jnp.where(first, a, b)
        odd = jnp.where(first, b, a)
        for part in range(3):
            both = jnp.concatenate([even[part * 8 : part * 8 + 8], odd[part * 8 : part * 8 + 8]], 0)
            wqkv[m * 16 : m * 16 + 16, part * width : (part + 1) * width] = both.astype(BF16)
        both = jnp.concatenate([even[24:32], odd[24:32]], 0)
        wout[m * 16 : m * 16 + 16] = both.astype(BF16)
        total = total + a[32:40] + b[32:40]
    vec[...] = total
    scale = hs**-0.5
    ii = lax.broadcasted_iota(jnp.int32, (WIN, WIN), 0)
    jj = lax.broadcasted_iota(jnp.int32, (WIN, WIN), 1)
    same = ii == jj
    image_rows = live.shape[1]
    base = lax.rem(me[0], 2) * rows
    for c in range(rows // per):
        part = slice(c * per * WIN, (c + 1) * per * WIN)
        h1 = (xhat_ref[part] * total[0:1] + total[2:3]).astype(BF16)
        h1_ref[part] = h1
        qkv = dot(h1, wqkv[...], NN).astype(BF16)
        qkv_ref[part] = qkv
        pairs = [(r, h) for r in range(c * per, (c + 1) * per) for h in range(HEADS)]
        scores = []
        for r, h in pairs:
            at = slice((r - c * per) * WIN, (r - c * per + 1) * WIN)
            q = qkv[at, h * hs : (h + 1) * hs]
            k = qkv[at, width + h * hs : width + (h + 1) * hs]
            scores.append(dot(q, k, NT))
        allowed = []
        for r in range(c * per, (c + 1) * per):
            row = base + r
            image = row // image_rows
            inside = row - image * image_rows
            reach = jnp.where(live[image, inside] == 1, lens[image] - inside * WIN, 0)
            allowed.append(same | (jj < jnp.minimum(ii, reach)))
        probs = []
        for (r, h), s in zip(pairs, scores):
            s = jnp.where(allowed[r - c * per], s, -1e30)
            e = jnp.exp((s - jnp.max(s, -1, keepdims=True)) * scale)
            probs.append((e * (1.0 / jnp.sum(e, -1, keepdims=True))).astype(BF16))
        mixed = []
        for (r, h), p in zip(pairs, probs):
            at = slice((r - c * per) * WIN, (r - c * per + 1) * WIN)
            v = qkv[at, 2 * width + h * hs : 2 * width + (h + 1) * hs]
            mixed.append(dot(p, v, NN).astype(BF16))
        for (r, h), p in zip(pairs, probs):
            prob_ref[r * HEADS + h] = p
        o = jnp.concatenate(
            [jnp.concatenate(mixed[n : n + HEADS], 1) for n in range(0, len(mixed), HEADS)], 0
        )
        o_ref[part] = o
        x1_ref[part] = x_ref[part].astype(F32) + dot(o, wout[...], NN)


def join(virt, blocks, n, out):
    tall = blocks.shape[1] // 2
    here = turn(virt[0] // 4)
    for i in range(VDP):
        k = turn(i) ^ here
        at = slice(i * tall, (i + 1) * tall)
        out[2 * n, at] = blocks[k, :tall]
        out[2 * n + 1, at] = blocks[k, tall:]


def hidden_half(part, h2, dyb, mats, f, dh2, a_ref=None, du_ref=None):
    width = h2.shape[1]
    for n in range(2):
        up, down = mats[2 * n], mats[2 * n + 1]
        a, slope = gelu_both(dot(h2, up, NN))
        a = a.astype(BF16)
        f = f + dot(a, down, NT)
        du = (dot(dyb, down, NN) * slope).astype(BF16)
        dh2 = dh2 + dot(du, up, NT)
        if a_ref is not None:
            at = slice(n * width, (n + 1) * width)
            a_ref[part, at] = a
            du_ref[part, at] = du
    return f, dh2


def hidden_near_kernel(
    per, virt, x1_ref, cot_ref, vec, own, got, h2_ref, xhat_ref, inv_ref, f_ref, dh2_ref, keep, send,
    a_ref, du_ref, mats,
):
    tokens, width = x1_ref.shape
    size = per * WIN
    join(virt, own, 0, mats)
    join(virt, got, 1, mats)
    for c in range(tokens // size):
        part = slice(c * size, (c + 1) * size)
        x1 = x1_ref[part]
        xhat, inv = norm_parts(x1)
        xhat_ref[part] = xhat
        inv_ref[part] = inv
        h2 = (xhat * vec[1:2] + vec[3:4]).astype(BF16)
        h2_ref[part] = h2
        f = x1 + vec[4:5]
        f, dh2 = hidden_half(part, h2, cot_ref[part], mats, f, jnp.zeros_like(f), a_ref, du_ref)
        f_ref[part] = f
        dh2_ref[part] = dh2
    gdown = dot(cot_ref[...], a_ref[...], TN)
    gup = dot(h2_ref[...], du_ref[...], TN)
    tall = width // VDP
    here = turn(virt[0] // 4)
    for i in range(VDP):
        at = slice(i * tall, (i + 1) * tall)
        k = turn(i) ^ here
        keep[k, :tall] = gup[at, :width]
        keep[k, tall:] = gdown[at, :width]
        send[k, :tall] = gup[at, width:].astype(BF16)
        send[k, tall:] = gdown[at, width:].astype(BF16)


def hidden_far_kernel(
    per, virt, cot_ref, vec, own, got, h2_ref, xhat_ref, inv_ref, f_ref, dh2_ref, o_ref,
    y_ref, dx1_ref, g_ref, gout, gvec,
    mats,
):
    tokens, width = h2_ref.shape
    size = per * WIN
    join(virt, own, 0, mats)
    join(virt, got, 1, mats)
    sums = [jnp.zeros((1, width), F32)] * 3
    for c in range(tokens // size):
        part = slice(c * size, (c + 1) * size)
        dyb = cot_ref[part]
        f, dh2 = hidden_half(part, h2_ref[part], dyb, mats, f_ref[part], dh2_ref[part])
        y_ref[part] = f.astype(BF16)
        dy = dyb.astype(F32)
        xhat = xhat_ref[part]
        dx1 = dy + norm_back(dh2, xhat, inv_ref[part], vec[1:2])
        dx1_ref[part] = dx1
        g_ref[part] = dx1.astype(BF16)
        terms = (dh2 * xhat, dh2, dy)
        sums = [a + jnp.sum(b, 0, keepdims=True) for a, b in zip(sums, terms)]
    gout[...] = dot(o_ref[...], g_ref[...], TN)
    zero = jnp.zeros((1, width), F32)
    gvec[...] = jnp.concatenate([zero, sums[0], zero, sums[1], sums[2], zero, zero, zero], 0)


def own_rows(virt, i, other):
    core = virt[0] % 2
    core = 1 - core if other else core
    return pl.ds(pl.multiple_of(i * 32 + ((virt[0] // 2) % 2) * 16 + core * 8, 8), 8)


def back_kernel(
    per, virt, qkv_ref, prob_ref, g_ref, h1_ref, wqkv, wout, vec, gout, gvec,
    dqkv, keep, send,
    do_ref, gqkv,
):
    tokens, width = g_ref.shape
    hs = width // HEADS
    scale = hs**-0.5
    do_ref[...] = dot(g_ref[...], wout[...], NT).astype(BF16)
    every = [(r, h) for r in range(tokens // WIN) for h in range(HEADS)]

    def piece(ref, r, h, part=0):
        return ref[r * WIN : (r + 1) * WIN, part * width + h * hs : part * width + (h + 1) * hs]

    for start in range(0, len(every), 2 * per):
        pairs = every[start : start + 2 * per]
        probs = [prob_ref[r * HEADS + h] for r, h in pairs]
        dos = [piece(do_ref, r, h) for r, h in pairs]
        dps = [dot(a, piece(qkv_ref, r, h, 2), NT) for a, (r, h) in zip(dos, pairs)]
        dvs = [dot(p, a, TN).astype(BF16) for p, a in zip(probs, dos)]
        dss = []
        for p, dp in zip(probs, dps):
            pf = p.astype(F32)
            ds = pf * (dp - jnp.sum(dp * pf, -1, keepdims=True)) * scale
            dss.append(ds.astype(BF16))
        dqs = [dot(ds, piece(qkv_ref, r, h, 1), NN).astype(BF16) for ds, (r, h) in zip(dss, pairs)]
        dks = [dot(ds, piece(qkv_ref, r, h, 0), TN).astype(BF16) for ds, (r, h) in zip(dss, pairs)]
        for n, (r, h) in enumerate(pairs):
            for part, values in enumerate((dqs, dks, dvs)):
                at = slice(part * width + h * hs, part * width + (h + 1) * hs)
                dqkv[r * WIN : (r + 1) * WIN, at] = values[n]
    gqkv[...] = dot(h1_ref[...], dqkv[...], TN)
    total = jnp.zeros((1, 3 * width), F32)
    for r in range(tokens // WIN):
        total = total + jnp.sum(dqkv[r * WIN : (r + 1) * WIN].astype(F32), 0, keepdims=True)
    w = wqkv[...].astype(F32)
    cols = jnp.concatenate([
        jnp.broadcast_to(jnp.sum(w * gqkv[...], -1, keepdims=True), (width, 64)),
        jnp.broadcast_to(jnp.sum(w * total, -1, keepdims=True), (width, 64)),
    ], 1)
    lines = cols.T
    from_grad, from_total = lines[0:1], lines[64:65]
    gain = (from_grad - vec[2:3] * from_total) / vec[0:1]
    rest = gvec[...]
    sums = jnp.concatenate([gain, rest[1:2], from_total, rest[3:]], 0)
    here = turn(virt[0] // 4)
    for i in range(VDP):
        k = turn(i) ^ here
        mine, other = own_rows(virt, i, 0), own_rows(virt, i, 1)
        theirs = []
        for part in range(3):
            at = slice(part * width, (part + 1) * width)
            keep[k, part * 8 : part * 8 + 8] = gqkv[mine, at]
            theirs.append(gqkv[other, at])
        keep[k, 24:32] = gout[mine]
        keep[k, 32:] = sums
        send[k] = jnp.concatenate(theirs + [gout[other], sums], 0).astype(BF16)


def token_grad_kernel(per, me, dqkv, wqkv, vec, xhat_ref, inv_ref, dx1_ref, y, y_near, gx, gxb, out, sems):
    own = dqkv.shape[0]
    size = per * WIN
    copies = []
    for n, source in enumerate((y, y_near)):
        at = pl.ds((lax.rem(me[0], 2) ^ n) * own, own)
        copies.append(pltpu.make_async_copy(source, out.at[at], sems.at[n]))
        copies[-1].start()
    for c in range(own // size):
        part = slice(c * size, (c + 1) * size)
        dh1 = dot(dqkv[part], wqkv[...], NT)
        values = dx1_ref[part] + norm_back(dh1, xhat_ref[part], inv_ref[part], vec[0:1])
        gx[part] = values
        gxb[part] = values.astype(BF16)
    for copy in copies:
        copy.wait()


def place_kernel(per, me, mine, theirs, out, wide, sems):
    own = theirs.shape[0]
    size = per * WIN
    here = lax.rem(me[0], 2) * own
    copies = [pltpu.make_async_copy(mine, out.at[pl.ds(here, own)], sems.at[own // size])]
    copies[0].start()
    for c in range(own // size):
        part = pl.ds(c * size, size)
        wide[part] = theirs[part].astype(F32)
        at = pl.ds(own - here + c * size, size)
        copies.append(pltpu.make_async_copy(wide.at[part], out.at[at], sems.at[c]))
        copies[-1].start()
    for copy in copies:
        copy.wait()


def finish_hidden_kernel(keep, got, up, down):
    total = keep[0] + got[0].astype(F32)
    tall = up.shape[0]
    up[...] = total[:tall]
    down[...] = total[tall:]


def finish_kernel(me, keep, got, qkv, out, gains, biases):
    total = keep[0] + got[0].astype(F32)
    small, width = out.shape
    for part in range(3):
        qkv[:, part * width : (part + 1) * width] = total[part * small : (part + 1) * small]
    out[...] = total[3 * small : 4 * small]
    vec = pltpu.roll(total[4 * small :], width - me[0] * small, 1)[:, :small]
    gains[...] = vec[:2]
    biases[...] = vec[2:5]


def swap(block, axis, bit):
    size = lax.axis_size(axis)
    return lax.ppermute(block, axis, [(i, i ^ bit) for i in range(size)])


def steps_of(axis):
    return [(axis, 1 << k) for k in reversed(range(lax.axis_size(axis).bit_length() - 1))]


def after(value, other):
    return lax.optimization_barrier((value, other))[0]


def halves(held):
    half = held.shape[0] // 2
    return held[:half], held[half:].astype(BF16)


def fold_step(keep, send, axis, bit, past=None):
    got = swap(send, axis, bit)
    return keep + (got if past is None else after(got, past)).astype(F32)


def bit_reverse(index, count):
    out = 0 * index
    for k in range(count):
        out = out | (((index >> k) & 1) << (count - 1 - k))
    return out


def by_device(block, me):
    blocks = block[None]
    for axis, bit in steps_of("dp") + steps_of("tensor"):
        blocks = jnp.concatenate([blocks, swap(blocks, axis, bit)], 0)
    count = blocks.shape[0]
    order = jnp.arange(count, dtype=jnp.int32) ^ me
    return jnp.take(blocks, bit_reverse(order, count.bit_length() - 1), axis=0)


def other_pack(w_qkv, w_out, gains, biases, w_up, w_down, me):
    small, width = w_out.shape
    qkv = w_qkv.reshape(small, 3, width).transpose(1, 0, 2).reshape(3 * small, width)
    rows = jnp.concatenate([gains, biases], 0)
    place = jnp.zeros((8, width), BF16)
    place = lax.dynamic_update_slice(place, rows, (jnp.int32(0), me * small))
    return jnp.concatenate([qkv, w_out, place], 0), jnp.concatenate([w_up, w_down.T], 0)


def other_blocks(a, b, me, n_dp, n_t):
    a = by_device(a, me)
    b = by_device(b, me)
    width = a.shape[2]
    count = n_dp * n_t
    small = width // count
    big = width // (VDP * VT)
    mats = a[:, : 4 * small].reshape(count, 4, small, width).transpose(1, 0, 2, 3)
    mats = mats.reshape(4, VDP * VT, big, width).transpose(1, 0, 2, 3).reshape(VDP * VT, 4 * big, width)
    vec = jnp.sum(a[:, 4 * small :].astype(F32), 0).astype(BF16)
    vecs = jnp.concatenate([vec[None], jnp.zeros((VDP * VT - 1, 8, width), BF16)], 0)
    a = jnp.concatenate([mats, vecs], 1)
    tall = width // n_dp
    b = b.reshape(n_dp, VT, 2, tall, width).transpose(1, 2, 0, 3, 4)
    b = b.reshape(VT, 2, VDP, width // VDP, width).transpose(2, 0, 1, 3, 4)
    b = b.reshape(VDP * VT, 2 * (width // VDP), width)

    y_own = (me // 2) % 2

    def placed(blocks):
        pairs = blocks.reshape((CHIPS, 2) + blocks.shape[1:])
        pairs = jnp.stack([pairs[m] for m in sorted(range(CHIPS), key=spot)], 0)
        pairs = jnp.where(y_own == 1, jnp.roll(pairs, VDP, 0), pairs)
        return pairs[:, 0], pairs[:, 1]

    return placed(a) + placed(b)


def other_reduce(pair_a, pair_b, me, n_dp, n_t):
    count = n_dp * n_t
    y_own = (me // 2) % 2

    def whole(keep, send):
        pairs = jnp.stack([keep, send.astype(F32)], 1)
        pairs = jnp.stack([pairs[turn(i)] for i in range(VDP)], 0)
        none = jnp.zeros_like(pairs)
        both = jnp.stack([jnp.where(y_own == y, pairs, none) for y in range(2)], 1)
        return both.reshape((VDP * VT,) + keep.shape[1:])

    def rows_of(blocks, parts):
        big = blocks.shape[1] // parts
        mats = blocks.reshape(VDP * VT, parts, big, -1).transpose(1, 0, 2, 3)
        mats = mats.reshape(parts, count, VDP * VT * big // count, -1).transpose(1, 0, 2, 3)
        return mats.reshape(count, -1, blocks.shape[2])

    def vec_of(blocks):
        picked = jnp.where(y_own == 0, blocks[0], 0.0)
        return jnp.broadcast_to(picked[None], (count,) + picked.shape)

    a, b = whole(*pair_a), whole(*pair_b)
    width = a.shape[2]
    tall, high = width // n_dp, width // VDP
    cols = b.reshape(VDP, VT, 2, high, width).transpose(1, 2, 0, 3, 4)
    cols = cols.reshape(VT, 2, n_dp, tall, width).transpose(2, 0, 1, 3, 4)
    cols = cols.reshape(count, 2 * tall, width)
    a = jnp.concatenate([rows_of(a[:, :32], 4), vec_of(a[:, 32:])], 1)
    results = []
    for blocks in (a, cols):
        blocks = jnp.take(blocks, jnp.arange(count, dtype=jnp.int32) ^ me, axis=0)
        for axis, bit in reversed(steps_of("dp") + steps_of("tensor")):
            pairs = blocks.reshape((-1, 2) + blocks.shape[1:])
            got = swap(pairs[:, 1].astype(BF16), axis, bit)
            blocks = pairs[:, 0] + got.astype(F32)
        results.append(blocks[0])
    return results


def struct(shape, dtype):
    return jax.ShapeDtypeStruct(shape, dtype)


def call(kernel, name, args, outs, scratch=(), flops=0, limit=16, alias=None):
    args = [a if isinstance(a, tuple) else (a, pltpu.VMEM) for a in args]
    moved = sum(a.size * a.dtype.itemsize for a, _ in args)
    spaces = [pl.ANY if isinstance(o, jax.ShapeDtypeStruct) else pltpu.VMEM for o in outs]
    return pl.pallas_call(
        kernel,
        name=name,
        out_shape=outs,
        in_specs=[pl.BlockSpec(memory_space=space) for _, space in args],
        out_specs=[pl.BlockSpec(memory_space=space) for space in spaces],
        scratch_shapes=list(scratch),
        input_output_aliases=alias or {},
        compiler_params=pltpu.CompilerParams(vmem_limit_bytes=limit * MIB),
        cost_estimate=pl.CostEstimate(flops=flops, bytes_accessed=moved, transcendentals=0),
    )(*[a for a, _ in args])


def on_device(tokens, lengths, row_mask, cotangent, w_qkv, w_out, gains, biases, w_up, w_down):
    images, seq_len, width = tokens.shape
    n_dp, n_t = lax.axis_size("dp"), lax.axis_size("tensor")
    index = lax.axis_index("dp") * n_t + lax.axis_index("tensor")
    me = index.astype(jnp.int32).reshape(1)
    usual = (n_dp, n_t) == (VDP, VT)
    virt = me if usual else (index // 2 % 2 * 2).astype(jnp.int32).reshape(1)
    small = width // (n_dp * n_t)
    tall = width // n_dp
    own = images * seq_len // 2
    rows = own // WIN
    per = 4 if rows % 4 == 0 else 1
    smem = pltpu.SMEM
    weights = (w_qkv, w_out, gains, biases, w_up, w_down)
    token_mm = 2 * own * width
    hbm = pltpu.HBM

    def in_hbm(array):
        return (pltpu.with_memory_space_constraint(array, hbm), hbm)

    def fetch(*args):
        return call(
            fetch_kernel,
            "fetch",
            args,
            [
                pltpu.VMEM((own, width), BF16),
                pltpu.VMEM((own, width), BF16),
                pltpu.VMEM((own, width), F32),
                pltpu.VMEM((own, 1), F32),
            ],
            [pltpu.SemaphoreType.DMA((2,))],
        )

    fetch_in = [
        (me, smem),
        in_hbm(tokens.reshape(images * seq_len, width)),
        in_hbm(cotangent.reshape(images * seq_len, width)),
    ]
    if usual:
        weights = (w_qkv, w_out, gains, biases, w_up, w_down.T)
        pack_a, pack_b = call(
            pack_kernel,
            "pack",
            [(me, smem)] + [in_hbm(w) for w in weights],
            [
                pltpu.VMEM((1, 4 * small + 8, width), BF16),
                pltpu.VMEM((1, 2 * tall, width), BF16),
            ],
            [pltpu.VMEM(w.shape, BF16) for w in weights] + [pltpu.SemaphoreType.DMA((6,))],
        )
        fetch_in[0] = (after(me, pack_a), smem)
        held_a, b = pack_a, pack_b
        x, cot, xhat1, inv1 = fetch(*fetch_in)
        for n, (axis, bit) in enumerate(steps_of("dp")):
            held_a = jnp.concatenate([held_a, swap(held_a, axis, bit)], 0)
            if n == 0:
                held_a = after(held_a, xhat1)
            b = jnp.concatenate([b, swap(b, axis, bit)], 0)
            b = after(b, held_a)
        held_a = jnp.concatenate([held_a, swap(held_a, "tensor", 2)], 0)
        far_b = swap(b, "tensor", 2)
        got_a = swap(held_a, "tensor", 1)
        got_b = swap(after(b, held_a), "tensor", 1)
    else:
        held_a, got_a, held_b, got_b = other_blocks(*other_pack(*weights, index), index, n_dp, n_t)
        b, far_b = held_b[:VDP], held_b[VDP:]
        got_b, got_far = got_b[:VDP], got_b[VDP:]
        x, cot, xhat1, inv1 = fetch(*fetch_in)
    qkv, prob, o, x1, h1, wqkv, wout, vec = call(
        functools.partial(attend_kernel, per),
        "attend",
        [(me, smem), (virt, smem), (lengths, smem), (row_mask, smem), x, xhat1, held_a, got_a],
        [
            pltpu.VMEM((own, 3 * width), BF16),
            pltpu.VMEM((rows * HEADS, WIN, WIN), BF16),
            pltpu.VMEM((own, width), BF16),
            pltpu.VMEM((own, width), F32),
            pltpu.VMEM((own, width), BF16),
            pltpu.VMEM((width, 3 * width), BF16),
            pltpu.VMEM((width, width), BF16),
            pltpu.VMEM((8, width), F32),
        ],
        flops=token_mm * (4 * width + 2 * WIN),
    )
    if usual:
        far_b = after(far_b, x1)
        got_b = after(got_b, far_b)
        got_far = swap(far_b, "tensor", 1)
    tall_b = 2 * (width // VDP)
    mats = pltpu.VMEM((4, width, width), BF16)
    h2, xhat2, inv2, f, dh2, keep_b, send_b = call(
        functools.partial(hidden_near_kernel, per),
        "hidden_near",
        [(virt, smem), x1, cot, vec, b, got_b],
        [
            pltpu.VMEM((own, width), BF16),
            pltpu.VMEM((own, width), F32),
            pltpu.VMEM((own, 1), F32),
            pltpu.VMEM((own, width), F32),
            pltpu.VMEM((own, width), F32),
            pltpu.VMEM((VDP, tall_b, width), F32),
            pltpu.VMEM((VDP, tall_b, width), BF16),
        ],
        [pltpu.VMEM((own, 2 * width), BF16)] * 2 + [mats],
        token_mm * 12 * width,
    )
    y, dx1, g, gout, gvec = call(
        functools.partial(hidden_far_kernel, per),
        "hidden_far",
        [(virt, smem), cot, vec, far_b, got_far, h2, xhat2, inv2, f, dh2, o],
        [
            pltpu.VMEM((own, width), BF16),
            pltpu.VMEM((own, width), F32),
            pltpu.VMEM((own, width), BF16),
            pltpu.VMEM((width, width), F32),
            pltpu.VMEM((8, width), F32),
        ],
        [mats],
        token_mm * 9 * width,
    )
    core, xbit, zlo, zhi = ("tensor", 1), ("dp", 1), ("dp", 2), ("dp", 4)
    if usual:
        held_b = fold_step(keep_b, send_b, *core, g)
        y = after(y, held_b)
    y_near = swap(y, "tensor", 1)
    dqkv, keep_a, send_a = call(
        functools.partial(back_kernel, per),
        "back",
        [(virt, smem), qkv, prob, g, h1, wqkv, wout, vec, gout, gvec],
        [
            pltpu.VMEM((own, 3 * width), BF16),
            pltpu.VMEM((VDP, 40, width), F32),
            pltpu.VMEM((VDP, 40, width), BF16),
        ],
        [pltpu.VMEM((own, width), BF16), pltpu.VMEM((width, 3 * width), F32)],
        token_mm * (4 * width + 5 * WIN),
    )
    gx, gxb, layer_out = call(
        functools.partial(token_grad_kernel, per),
        "token_grad",
        [(me, smem), dqkv, wqkv, vec, xhat1, inv1, dx1, y, y_near],
        [
            pltpu.VMEM((own, width), F32),
            pltpu.VMEM((own, width), BF16),
            struct((images * seq_len, width), BF16),
        ],
        [pltpu.SemaphoreType.DMA((2,))],
        flops=token_mm * 3 * width,
    )
    layer_out = layer_out.reshape(images, seq_len, width)

    def place(gx_near):
        return call(
            functools.partial(place_kernel, per),
            "place",
            [(me, smem), gx, gx_near],
            [struct((images * seq_len, width), F32)],
            [pltpu.VMEM((own, width), F32), pltpu.SemaphoreType.DMA((rows // per + 1,))],
        )[0].reshape(images, seq_len, width)

    if usual:
        held_b = fold_step(*halves(held_b), *xbit)
        held_a = fold_step(keep_a, after(send_a, held_b), *core, gxb)
        keep, send = halves(held_b)
        held_b = fold_step(keep, after(send, held_a), *zlo)
        held_a = fold_step(*halves(held_a), *xbit)
        gxb = after(gxb, (held_a, held_b))
        held_a = fold_step(*halves(held_a), *zlo)
        got = swap(halves(held_b)[1], *zhi)
        vmem = pl.BlockSpec(memory_space=pltpu.VMEM)
        o_up, o_down = pl.pallas_call(
            finish_hidden_kernel,
            name="finish_hidden",
            out_shape=[struct((tall, width), F32)] * 2,
            in_specs=[vmem] * 2,
            out_specs=[vmem] * 2,
        )(held_b, got)
        got = swap(halves(held_a)[1], *zhi)
        grad_tokens = place(swap(gxb, "tensor", 1))
        got = after(got, grad_tokens)
        shapes = ((small, 3 * width), (small, width), (2, small), (3, small))
        o_qkv, o_out, o_gains, o_bias = pl.pallas_call(
            finish_kernel,
            name="finish",
            out_shape=[struct(shape, F32) for shape in shapes],
            in_specs=[pl.BlockSpec(memory_space=smem)] + [vmem] * 2,
            out_specs=[vmem] * 4,
        )(me, held_a, got)
    else:
        grad_tokens = place(swap(gxb, "tensor", 1))
        grad_a, grad_b = other_reduce((keep_a, send_a), (keep_b, send_b), index, n_dp, n_t)
        o_qkv = jnp.concatenate([grad_a[p * small : (p + 1) * small] for p in range(3)], 1)
        o_out = grad_a[3 * small : 4 * small]
        o_vec = lax.dynamic_slice_in_dim(grad_a[4 * small : 4 * small + 5], index * small, small, 1)
        o_gains, o_bias = o_vec[:2], o_vec[2:]
        o_up, o_down = grad_b[:tall], grad_b[tall:]
    return layer_out, grad_tokens, o_qkv, o_out, o_gains, o_bias, o_up, o_down.T


def solution(mesh):
    in_specs = (
        P("dp", None, None),
        P("dp"),
        P("dp", None),
        P("dp", None, None),
        P(("dp", "tensor"), None),
        P(("dp", "tensor"), None),
        P(None, ("dp", "tensor")),
        P(None, ("dp", "tensor")),
        P("dp", "tensor"),
        P("tensor", "dp"),
    )
    out_specs = (
        P("dp", None, None),
        P("dp", None, None),
        P(("dp", "tensor"), None),
        P(("dp", "tensor"), None),
        P(None, ("dp", "tensor")),
        P(None, ("dp", "tensor")),
        P("dp", "tensor"),
        P("tensor", "dp"),
    )
    return jax.shard_map(
        on_device, mesh=mesh, in_specs=in_specs, out_specs=out_specs, check_vma=False
    )
```

```python
import functools

import jax
import jax.numpy as jnp
from jax import lax
from jax.experimental import pallas as pl
from jax.experimental.pallas import tpu as pltpu
from jax.sharding import PartitionSpec as P

HEADS = 2
WIN = 96
F32 = jnp.float32
BF16 = jnp.bfloat16
VDP, VT = 8, 4
CHIPS = VDP * VT // 2
MIB = 1 << 20

NN = ((1,), (0,))
NT = ((1,), (1,))
TN = ((0,), (0,))


def dot(a, b, dims):
    return lax.dot_general(a, b, (dims, ((), ())), preferred_element_type=F32)


def turn(i):
    return ((i & 1) << 2) | (i & 2) | ((i & 4) >> 2)


def spot(m):
    return (m % 2) * VDP + turn(m // 2)


def turn(i):
    return ((i & 1) << 2) | (i & 2) | ((i & 4) >> 2)


def spot(m):
    return (m % 2) * VDP + turn(m // 2)


def fold(m):
    out = 0
    for place, bit in enumerate(REDUCE_BITS):
        shift = 3 - place
        out = out | (((m // bit) & 1) << shift)
    return out


def norm_parts(values):
    center = values - jnp.mean(values, -1, keepdims=True)
    inv = lax.rsqrt(jnp.mean(center * center, -1, keepdims=True) + 1e-05)
    return center * inv, inv


def norm_back(grad, xhat, inv, gain):
    scaled = grad * gain
    return inv * (
        scaled
        - jnp.mean(scaled, -1, keepdims=True)
        - xhat * jnp.mean(scaled * xhat, -1, keepdims=True)
    )


def gelu_both(u):
    c = 0.7978845608028654
    u2 = u * u
    t = jnp.tanh(u * (c + (c * 0.044715) * u2))
    half = 0.5 + 0.5 * t
    value = u * half
    slope = half + (value - value * half) * (2 * c + (6 * c * 0.044715) * u2)
    return value, slope


def pack_kernel(me, *refs):
    sources, (small_ref, big_ref), held, sems = refs[:6], refs[6:8], refs[8:14], refs[14]
    copies = [pltpu.make_async_copy(a, b, sems.at[n]) for n, (a, b) in enumerate(zip(sources, held))]
    for copy in copies:
        copy.start()
    qkv, out, gains, biases, up, down = held
    small, width = out.shape
    tall = up.shape[0]
    lane = lax.broadcasted_iota(jnp.int32, (1, width), 1)
    mine = lane // small == me[0]
    for copy in copies:
        copy.wait()
    for part in range(3):
        small_ref[0, part * small : (part + 1) * small] = qkv[:, part * width : (part + 1) * width]
    small_ref[0, 3 * small : 4 * small] = out[...]
    rows = [gains[0:1], gains[1:2], biases[0:1], biases[1:2], biases[2:3]]
    vals = jnp.concatenate(rows + [jnp.zeros((3, small), BF16)], 0).astype(F32)
    wide = jnp.concatenate([vals] * (width // small), 1)
    small_ref[0, 4 * small : 4 * small + 8] = jnp.where(mine, wide, 0.0).astype(BF16)
    big_ref[0, :tall] = up[...]
    big_ref[0, tall:] = down[...]


def fetch_kernel(me, tokens, cot, x_ref, cot_ref, xhat_ref, inv_ref, sems):
    own = x_ref.shape[0]
    at = pl.ds(lax.rem(me[0], 2) * own, own)
    first = pltpu.make_async_copy(tokens.at[at], x_ref, sems.at[0])
    second = pltpu.make_async_copy(cot.at[at], cot_ref, sems.at[1])
    first.start()
    second.start()
    first.wait()
    for n in range(own // WIN):
        part = slice(n * WIN, (n + 1) * WIN)
        xhat_ref[part], inv_ref[part] = norm_parts(x_ref[part].astype(F32))
    second.wait()


def attend_kernel(
    per, me, virt, lens, live, x_ref, xhat_ref, held, got,
    qkv_ref, prob_ref, o_ref, x1_ref, h1_ref, wqkv, wout, vec,
):
    tokens, width = x_ref.shape
    rows = tokens // WIN
    hs = width // HEADS
    here = spot(virt[0] // 2) % VDP
    y_own = (virt[0] // 2) % 2
    first = virt[0] % 2 == 0
    total = jnp.zeros((8, width), F32)
    for m in range(CHIPS):
        k = spot(m) ^ (here + y_own * VDP)
        a = held[k].astype(F32)
        b = got[k].astype(F32)
        even = jnp.where(first, a, b)
        odd = jnp.where(first, b, a)
        for part in range(3):
            both = jnp.concatenate([even[part * 8 : part * 8 + 8], odd[part * 8 : part * 8 + 8]], 0)
            wqkv[m * 16 : m * 16 + 16, part * width : (part + 1) * width] = both.astype(BF16)
        both = jnp.concatenate([even[24:32], odd[24:32]], 0)
        wout[m * 16 : m * 16 + 16] = both.astype(BF16)
        total = total + a[32:40] + b[32:40]
    vec[...] = total
    scale = hs**-0.5
    ii = lax.broadcasted_iota(jnp.int32, (WIN, WIN), 0)
    jj = lax.broadcasted_iota(jnp.int32, (WIN, WIN), 1)
    same = ii == jj
    image_rows = live.shape[1]
    base = lax.rem(me[0], 2) * rows

    def enter(c):
        part = slice(c * per * WIN, (c + 1) * per * WIN)
        h1 = (xhat_ref[part] * total[0:1] + total[2:3]).astype(BF16)
        h1_ref[part] = h1
        qkv = dot(h1, wqkv[...], NN).astype(BF16)
        qkv_ref[part] = qkv
        scores = []
        for r in range(per):
            at = slice(r * WIN, (r + 1) * WIN)
            for h in range(HEADS):
                q = qkv[at, h * hs : (h + 1) * hs]
                k = qkv[at, width + h * hs : width + (h + 1) * hs]
                scores.append(dot(q, k, NT))
        return qkv, scores

    ahead = enter(0)
    for c in range(rows // per):
        qkv, scores = ahead
        if c + 1 < rows // per:
            ahead = enter(c + 1)
        part = slice(c * per * WIN, (c + 1) * per * WIN)
        probs = []
        for r in range(per):
            row = base + c * per + r
            image = row // image_rows
            inside = row - image * image_rows
            reach = jnp.where(live[image, inside] == 1, lens[image] - inside * WIN, 0)
            allowed = same | (jj < jnp.minimum(ii, reach))
            for h in range(HEADS):
                s = jnp.where(allowed, scores[r * HEADS + h], -1e30)
                e = jnp.exp((s - jnp.max(s, -1, keepdims=True)) * scale)
                probs.append((e * (1.0 / jnp.sum(e, -1, keepdims=True))).astype(BF16))
        mixed = []
        for r in range(per):
            at = slice(r * WIN, (r + 1) * WIN)
            heads = []
            for h in range(HEADS):
                v = qkv[at, 2 * width + h * hs : 2 * width + (h + 1) * hs]
                heads.append(dot(probs[r * HEADS + h], v, NN).astype(BF16))
            mixed.append(jnp.concatenate(heads, 1))
        o = jnp.concatenate(mixed, 0)
        for n, p in enumerate(probs):
            prob_ref[c * per * HEADS + n] = p
        o_ref[part] = o
        x1_ref[part] = x_ref[part].astype(F32) + dot(o, wout[...], NN)


def join(virt, blocks, n, out):
    tall = blocks.shape[1] // 2
    here = turn(virt[0] // 4)
    for i in range(VDP):
        k = turn(i) ^ here
        at = slice(i * tall, (i + 1) * tall)
        out[2 * n, at] = blocks[k, :tall]
        out[2 * n + 1, at] = blocks[k, tall:]


def hidden_blocks(count, mats, enter, leave, keep=None):
    items = [(c, n) for c in range(count) for n in range(2)]
    state = {}

    def products(c, n):
        if n == 0:
            state[c] = list(enter(c))
        h2, dyb = state[c][:2]
        return dot(h2, mats[2 * n], NN), dot(dyb, mats[2 * n + 1], NN)

    ahead = products(*items[0])
    for place, (c, n) in enumerate(items):
        u, da = ahead
        if place + 1 < len(items):
            ahead = products(*items[place + 1])
        a, slope = gelu_both(u)
        a = a.astype(BF16)
        du = (da * slope).astype(BF16)
        state[c][2] = state[c][2] + dot(a, mats[2 * n + 1], NT)
        state[c][3] = state[c][3] + dot(du, mats[2 * n], NT)
        if keep is not None:
            keep(c, n, a, du)
        if n == 1:
            leave(c, *state.pop(c)[2:])


def hidden_near_kernel(
    per, virt, x1_ref, cot_ref, vec, own, got, h2_ref, xhat_ref, inv_ref, f_ref, dh2_ref, keep, send,
    a_ref, du_ref, mats,
):
    tokens, width = x1_ref.shape
    size = per * WIN
    join(virt, own, 0, mats)
    join(virt, got, 1, mats)

    def enter(c):
        part = slice(c * size, (c + 1) * size)
        x1 = x1_ref[part]
        xhat, inv = norm_parts(x1)
        xhat_ref[part] = xhat
        inv_ref[part] = inv
        h2 = (xhat * vec[1:2] + vec[3:4]).astype(BF16)
        h2_ref[part] = h2
        return h2, cot_ref[part], x1 + vec[4:5], jnp.zeros_like(x1)

    def leave(c, f, dh2):
        part = slice(c * size, (c + 1) * size)
        f_ref[part] = f
        dh2_ref[part] = dh2

    def keep_units(c, n, a, du):
        part, at = slice(c * size, (c + 1) * size), slice(n * width, (n + 1) * width)
        a_ref[part, at] = a
        du_ref[part, at] = du

    hidden_blocks(tokens // size, mats, enter, leave, keep_units)
    gdown = dot(cot_ref[...], a_ref[...], TN)
    gup = dot(h2_ref[...], du_ref[...], TN)
    tall = width // VDP
    here = turn(virt[0] // 4)
    for i in range(VDP):
        at = slice(i * tall, (i + 1) * tall)
        k = turn(i) ^ here
        keep[k, :tall] = gup[at, :width]
        keep[k, tall:] = gdown[at, :width]
        send[k, :tall] = gup[at, width:].astype(BF16)
        send[k, tall:] = gdown[at, width:].astype(BF16)


def hidden_far_kernel(
    per, virt, cot_ref, vec, own, got, h2_ref, xhat_ref, inv_ref, f_ref, dh2_ref, o_ref,
    y_ref, dx1_ref, g_ref, gout, gvec,
    mats,
):
    tokens, width = h2_ref.shape
    size = per * WIN
    join(virt, own, 0, mats)
    join(virt, got, 1, mats)
    sums = [jnp.zeros((1, width), F32)] * 3

    def enter(c):
        part = slice(c * size, (c + 1) * size)
        return h2_ref[part], cot_ref[part], f_ref[part], dh2_ref[part]

    def leave(c, f, dh2):
        part = slice(c * size, (c + 1) * size)
        y_ref[part] = f.astype(BF16)
        dy = cot_ref[part].astype(F32)
        xhat = xhat_ref[part]
        dx1 = dy + norm_back(dh2, xhat, inv_ref[part], vec[1:2])
        dx1_ref[part] = dx1
        g_ref[part] = dx1.astype(BF16)
        for n, term in enumerate((dh2 * xhat, dh2, dy)):
            sums[n] = sums[n] + jnp.sum(term, 0, keepdims=True)

    hidden_blocks(tokens // size, mats, enter, leave)
    gout[...] = dot(o_ref[...], g_ref[...], TN)
    zero = jnp.zeros((1, width), F32)
    gvec[...] = jnp.concatenate([zero, sums[0], zero, sums[1], sums[2], zero, zero, zero], 0)


def own_rows(virt, i, other):
    core = virt[0] % 2
    core = 1 - core if other else core
    return pl.ds(pl.multiple_of(i * 32 + ((virt[0] // 2) % 2) * 16 + core * 8, 8), 8)


def back_kernel(
    per, virt, qkv_ref, prob_ref, g_ref, h1_ref, wqkv, wout, vec, gout, gvec,
    dqkv, keep, send,
    gqkv,
):
    tokens, width = g_ref.shape
    hs = width // HEADS
    scale = hs**-0.5
    every = [(r, h) for r in range(tokens // WIN) for h in range(HEADS)]
    groups = [every[n : n + 2 * per] for n in range(0, len(every), 2 * per)]

    def piece(ref, r, h, part=0):
        return ref[r * WIN : (r + 1) * WIN, part * width + h * hs : part * width + (h + 1) * hs]

    def enter(pairs):
        r = pairs[0][0]
        do = dot(g_ref[r * WIN : (r + per) * WIN], wout[...], NT).astype(BF16)
        dos = [do[(n - r) * WIN : (n - r + 1) * WIN, h * hs : (h + 1) * hs] for n, h in pairs]
        probs = [prob_ref[r * HEADS + h] for r, h in pairs]
        dps = [dot(a, piece(qkv_ref, r, h, 2), NT) for a, (r, h) in zip(dos, pairs)]
        dvs = [dot(p, a, TN).astype(BF16) for p, a in zip(probs, dos)]
        return probs, dps, dvs

    ahead = enter(groups[0])
    for place, pairs in enumerate(groups):
        probs, dps, dvs = ahead
        if place + 1 < len(groups):
            ahead = enter(groups[place + 1])
        dss = []
        for p, dp in zip(probs, dps):
            pf = p.astype(F32)
            ds = pf * (dp - jnp.sum(dp * pf, -1, keepdims=True)) * scale
            dss.append(ds.astype(BF16))
        dqs = [dot(ds, piece(qkv_ref, r, h, 1), NN).astype(BF16) for ds, (r, h) in zip(dss, pairs)]
        dks = [dot(ds, piece(qkv_ref, r, h, 0), TN).astype(BF16) for ds, (r, h) in zip(dss, pairs)]
        for n, (r, h) in enumerate(pairs):
            for part, values in enumerate((dqs, dks, dvs)):
                at = slice(part * width + h * hs, part * width + (h + 1) * hs)
                dqkv[r * WIN : (r + 1) * WIN, at] = values[n]
    gqkv[...] = dot(h1_ref[...], dqkv[...], TN)
    total = jnp.zeros((1, 3 * width), F32)
    for r in range(tokens // WIN):
        total = total + jnp.sum(dqkv[r * WIN : (r + 1) * WIN].astype(F32), 0, keepdims=True)
    w = wqkv[...].astype(F32)
    cols = jnp.concatenate([
        jnp.broadcast_to(jnp.sum(w * gqkv[...], -1, keepdims=True), (width, 64)),
        jnp.broadcast_to(jnp.sum(w * total, -1, keepdims=True), (width, 64)),
    ], 1)
    lines = cols.T
    from_grad, from_total = lines[0:1], lines[64:65]
    gain = (from_grad - vec[2:3] * from_total) / vec[0:1]
    rest = gvec[...]
    sums = jnp.concatenate([gain, rest[1:2], from_total, rest[3:]], 0)
    here = turn(virt[0] // 4)
    for i in range(VDP):
        k = turn(i) ^ here
        mine, other = own_rows(virt, i, 0), own_rows(virt, i, 1)
        theirs = []
        for part in range(3):
            at = slice(part * width, (part + 1) * width)
            keep[k, part * 8 : part * 8 + 8] = gqkv[mine, at]
            theirs.append(gqkv[other, at])
        keep[k, 24:32] = gout[mine]
        keep[k, 32:] = sums
        send[k] = jnp.concatenate(theirs + [gout[other], sums], 0).astype(BF16)


def token_grad_kernel(per, me, dqkv, wqkv, vec, xhat_ref, inv_ref, dx1_ref, y, y_near, gx, gxb, out, sems):
    own = dqkv.shape[0]
    size = per * WIN
    copies = []
    for n, source in enumerate((y, y_near)):
        at = pl.ds((lax.rem(me[0], 2) ^ n) * own, own)
        copies.append(pltpu.make_async_copy(source, out.at[at], sems.at[n]))
        copies[-1].start()
    ahead = dot(dqkv[:size], wqkv[...], NT)
    for c in range(own // size):
        part = slice(c * size, (c + 1) * size)
        dh1 = ahead
        if (c + 1) * size < own:
            ahead = dot(dqkv[(c + 1) * size : (c + 2) * size], wqkv[...], NT)
        values = dx1_ref[part] + norm_back(dh1, xhat_ref[part], inv_ref[part], vec[0:1])
        gx[part] = values
        gxb[part] = values.astype(BF16)
    for copy in copies:
        copy.wait()


def place_kernel(per, me, mine, theirs, out, wide, sems):
    own = theirs.shape[0]
    size = per * WIN
    here = lax.rem(me[0], 2) * own
    copies = [pltpu.make_async_copy(mine, out.at[pl.ds(here, own)], sems.at[own // size])]
    copies[0].start()
    for c in range(own // size):
        part = pl.ds(c * size, size)
        wide[part] = theirs[part].astype(F32)
        at = pl.ds(own - here + c * size, size)
        copies.append(pltpu.make_async_copy(wide.at[part], out.at[at], sems.at[c]))
        copies[-1].start()
    for copy in copies:
        copy.wait()


def finish_hidden_kernel(keep, got, up, down):
    total = keep[0] + got[0].astype(F32)
    tall = up.shape[0]
    up[...] = total[:tall]
    down[...] = total[tall:]


def finish_kernel(me, keep, got, qkv, out, gains, biases):
    total = keep[0] + got[0].astype(F32)
    small, width = out.shape
    for part in range(3):
        qkv[:, part * width : (part + 1) * width] = total[part * small : (part + 1) * small]
    out[...] = total[3 * small : 4 * small]
    vec = pltpu.roll(total[4 * small :], width - me[0] * small, 1)[:, :small]
    gains[...] = vec[:2]
    biases[...] = vec[2:5]


def swap(block, axis, bit):
    size = lax.axis_size(axis)
    return lax.ppermute(block, axis, [(i, i ^ bit) for i in range(size)])


def steps_of(axis):
    return [(axis, 1 << k) for k in reversed(range(lax.axis_size(axis).bit_length() - 1))]


def after(value, other):
    return lax.optimization_barrier((value, other))[0]


def halves(held):
    half = held.shape[0] // 2
    return held[:half], held[half:].astype(BF16)


def fold_step(keep, send, axis, bit, past=None):
    got = swap(send, axis, bit)
    return keep + (got if past is None else after(got, past)).astype(F32)


def bit_reverse(index, count):
    out = 0 * index
    for k in range(count):
        out = out | (((index >> k) & 1) << (count - 1 - k))
    return out


def by_device(block, me):
    blocks = block[None]
    for axis, bit in steps_of("dp") + steps_of("tensor"):
        blocks = jnp.concatenate([blocks, swap(blocks, axis, bit)], 0)
    count = blocks.shape[0]
    order = jnp.arange(count, dtype=jnp.int32) ^ me
    return jnp.take(blocks, bit_reverse(order, count.bit_length() - 1), axis=0)


def other_pack(w_qkv, w_out, gains, biases, w_up, w_down, me):
    small, width = w_out.shape
    qkv = w_qkv.reshape(small, 3, width).transpose(1, 0, 2).reshape(3 * small, width)
    rows = jnp.concatenate([gains, biases], 0)
    place = jnp.zeros((8, width), BF16)
    place = lax.dynamic_update_slice(place, rows, (jnp.int32(0), me * small))
    return jnp.concatenate([qkv, w_out, place], 0), jnp.concatenate([w_up, w_down.T], 0)


def other_blocks(a, b, me, n_dp, n_t):
    a = by_device(a, me)
    b = by_device(b, me)
    width = a.shape[2]
    count = n_dp * n_t
    small = width // count
    big = width // (VDP * VT)
    mats = a[:, : 4 * small].reshape(count, 4, small, width).transpose(1, 0, 2, 3)
    mats = mats.reshape(4, VDP * VT, big, width).transpose(1, 0, 2, 3).reshape(VDP * VT, 4 * big, width)
    vec = jnp.sum(a[:, 4 * small :].astype(F32), 0).astype(BF16)
    vecs = jnp.concatenate([vec[None], jnp.zeros((VDP * VT - 1, 8, width), BF16)], 0)
    a = jnp.concatenate([mats, vecs], 1)
    tall = width // n_dp
    b = b.reshape(n_dp, VT, 2, tall, width).transpose(1, 2, 0, 3, 4)
    b = b.reshape(VT, 2, VDP, width // VDP, width).transpose(2, 0, 1, 3, 4)
    b = b.reshape(VDP * VT, 2 * (width // VDP), width)

    y_own = (me // 2) % 2

    def placed(blocks):
        pairs = blocks.reshape((CHIPS, 2) + blocks.shape[1:])
        pairs = jnp.stack([pairs[m] for m in sorted(range(CHIPS), key=spot)], 0)
        pairs = jnp.where(y_own == 1, jnp.roll(pairs, VDP, 0), pairs)
        return pairs[:, 0], pairs[:, 1]

    return placed(a) + placed(b)


def other_reduce(pair_a, pair_b, me, n_dp, n_t):
    count = n_dp * n_t
    y_own = (me // 2) % 2

    def whole(keep, send):
        pairs = jnp.stack([keep, send.astype(F32)], 1)
        pairs = jnp.stack([pairs[turn(i)] for i in range(VDP)], 0)
        none = jnp.zeros_like(pairs)
        both = jnp.stack([jnp.where(y_own == y, pairs, none) for y in range(2)], 1)
        return both.reshape((VDP * VT,) + keep.shape[1:])

    def rows_of(blocks, parts):
        big = blocks.shape[1] // parts
        mats = blocks.reshape(VDP * VT, parts, big, -1).transpose(1, 0, 2, 3)
        mats = mats.reshape(parts, count, VDP * VT * big // count, -1).transpose(1, 0, 2, 3)
        return mats.reshape(count, -1, blocks.shape[2])

    def vec_of(blocks):
        picked = jnp.where(y_own == 0, blocks[0], 0.0)
        return jnp.broadcast_to(picked[None], (count,) + picked.shape)

    a, b = whole(*pair_a), whole(*pair_b)
    width = a.shape[2]
    tall, high = width // n_dp, width // VDP
    cols = b.reshape(VDP, VT, 2, high, width).transpose(1, 2, 0, 3, 4)
    cols = cols.reshape(VT, 2, n_dp, tall, width).transpose(2, 0, 1, 3, 4)
    cols = cols.reshape(count, 2 * tall, width)
    a = jnp.concatenate([rows_of(a[:, :32], 4), vec_of(a[:, 32:])], 1)
    results = []
    for blocks in (a, cols):
        blocks = jnp.take(blocks, jnp.arange(count, dtype=jnp.int32) ^ me, axis=0)
        for axis, bit in reversed(steps_of("dp") + steps_of("tensor")):
            pairs = blocks.reshape((-1, 2) + blocks.shape[1:])
            got = swap(pairs[:, 1].astype(BF16), axis, bit)
            blocks = pairs[:, 0] + got.astype(F32)
        results.append(blocks[0])
    return results


def struct(shape, dtype):
    return jax.ShapeDtypeStruct(shape, dtype)


def call(kernel, name, args, outs, scratch=(), flops=0, limit=16, hbm_outs=True):
    args = [a if isinstance(a, tuple) else (a, pltpu.VMEM) for a in args]
    moved = sum(a.size * a.dtype.itemsize for a, _ in args)
    spaces = [pl.ANY if hbm_outs and isinstance(o, jax.ShapeDtypeStruct) else pltpu.VMEM for o in outs]
    return pl.pallas_call(
        kernel,
        name=name,
        out_shape=outs,
        in_specs=[pl.BlockSpec(memory_space=space) for _, space in args],
        out_specs=[pl.BlockSpec(memory_space=space) for space in spaces],
        scratch_shapes=list(scratch),
        compiler_params=pltpu.CompilerParams(vmem_limit_bytes=limit * MIB),
        cost_estimate=pl.CostEstimate(flops=flops, bytes_accessed=moved, transcendentals=0),
    )(*[a for a, _ in args])


def on_device(tokens, lengths, row_mask, cotangent, w_qkv, w_out, gains, biases, w_up, w_down):
    images, seq_len, width = tokens.shape
    n_dp, n_t = lax.axis_size("dp"), lax.axis_size("tensor")
    index = lax.axis_index("dp") * n_t + lax.axis_index("tensor")
    me = index.astype(jnp.int32).reshape(1)
    usual = (n_dp, n_t) == (VDP, VT)
    virt = me if usual else (index // 2 % 2 * 2).astype(jnp.int32).reshape(1)
    small = width // (n_dp * n_t)
    tall = width // n_dp
    own = images * seq_len // 2
    rows = own // WIN
    per = 4 if rows % 4 == 0 else 1
    smem = pltpu.SMEM
    weights = (w_qkv, w_out, gains, biases, w_up, w_down)
    token_mm = 2 * own * width
    hbm = pltpu.HBM

    def in_hbm(array):
        return (pltpu.with_memory_space_constraint(array, hbm), hbm)

    def fetch(*args):
        return call(
            fetch_kernel,
            "fetch",
            args,
            [
                pltpu.VMEM((own, width), BF16),
                pltpu.VMEM((own, width), BF16),
                pltpu.VMEM((own, width), F32),
                pltpu.VMEM((own, 1), F32),
            ],
            [pltpu.SemaphoreType.DMA((2,))],
        )

    fetch_in = [
        (me, smem),
        in_hbm(tokens.reshape(images * seq_len, width)),
        in_hbm(cotangent.reshape(images * seq_len, width)),
    ]
    if usual:
        weights = (w_qkv, w_out, gains, biases, w_up, w_down.T)
        pack_a, pack_b = call(
            pack_kernel,
            "pack",
            [(me, smem)] + [in_hbm(w) for w in weights],
            [
                pltpu.VMEM((1, 4 * small + 8, width), BF16),
                pltpu.VMEM((1, 2 * tall, width), BF16),
            ],
            [pltpu.VMEM(w.shape, BF16) for w in weights] + [pltpu.SemaphoreType.DMA((6,))],
        )
        held_a, b = pack_a, pack_b
        for axis, bit in steps_of("dp"):
            held_a = jnp.concatenate([held_a, swap(held_a, axis, bit)], 0)
            b = jnp.concatenate([b, swap(b, axis, bit)], 0)
            b = after(b, held_a)
        fetch_in[0] = (after(me, held_a), smem)
        x, cot, xhat1, inv1 = fetch(*fetch_in)
        held_a = jnp.concatenate([held_a, after(swap(held_a, "tensor", 2), xhat1)], 0)
        far_b = swap(b, "tensor", 2)
        got_a = swap(held_a, "tensor", 1)
        got_b = swap(after(b, held_a), "tensor", 1)
    else:
        held_a, got_a, held_b, got_b = other_blocks(*other_pack(*weights, index), index, n_dp, n_t)
        b, far_b = held_b[:VDP], held_b[VDP:]
        got_b, got_far = got_b[:VDP], got_b[VDP:]
        x, cot, xhat1, inv1 = fetch(*fetch_in)
    qkv, prob, o, x1, h1, wqkv, wout, vec = call(
        functools.partial(attend_kernel, per),
        "attend",
        [(me, smem), (virt, smem), (lengths, smem), (row_mask, smem), x, xhat1, held_a, got_a],
        [
            pltpu.VMEM((own, 3 * width), BF16),
            pltpu.VMEM((rows * HEADS, WIN, WIN), BF16),
            pltpu.VMEM((own, width), BF16),
            pltpu.VMEM((own, width), F32),
            pltpu.VMEM((own, width), BF16),
            pltpu.VMEM((width, 3 * width), BF16),
            pltpu.VMEM((width, width), BF16),
            pltpu.VMEM((8, width), F32),
        ],
        flops=token_mm * (4 * width + 2 * WIN),
    )
    if usual:
        far_b = after(far_b, x1)
        got_b = after(got_b, far_b)
        got_far = swap(far_b, "tensor", 1)
    tall_b = 2 * (width // VDP)
    mats = pltpu.VMEM((4, width, width), BF16)
    h2, xhat2, inv2, f, dh2, keep_b, send_b = call(
        functools.partial(hidden_near_kernel, per),
        "hidden_near",
        [(virt, smem), x1, cot, vec, b, got_b],
        [
            pltpu.VMEM((own, width), BF16),
            pltpu.VMEM((own, width), F32),
            pltpu.VMEM((own, 1), F32),
            pltpu.VMEM((own, width), F32),
            pltpu.VMEM((own, width), F32),
            pltpu.VMEM((VDP, tall_b, width), F32),
            pltpu.VMEM((VDP, tall_b, width), BF16),
        ],
        [pltpu.VMEM((own, 2 * width), BF16)] * 2 + [mats],
        token_mm * 12 * width,
    )
    y, dx1, g, gout, gvec = call(
        functools.partial(hidden_far_kernel, per),
        "hidden_far",
        [(virt, smem), cot, vec, far_b, got_far, h2, xhat2, inv2, f, dh2, o],
        [
            pltpu.VMEM((own, width), BF16),
            pltpu.VMEM((own, width), F32),
            pltpu.VMEM((own, width), BF16),
            pltpu.VMEM((width, width), F32),
            pltpu.VMEM((8, width), F32),
        ],
        [mats],
        token_mm * 9 * width,
    )
    core, xbit, zlo, zhi = ("tensor", 1), ("dp", 1), ("dp", 2), ("dp", 4)
    if usual:
        held_b = fold_step(keep_b, send_b, *core, g)
        y = after(y, held_b)
    y_near = swap(y, "tensor", 1)
    dqkv, keep_a, send_a = call(
        functools.partial(back_kernel, per),
        "back",
        [(virt, smem), qkv, prob, g, h1, wqkv, wout, vec, gout, gvec],
        [
            pltpu.VMEM((own, 3 * width), BF16),
            pltpu.VMEM((VDP, 40, width), F32),
            pltpu.VMEM((VDP, 40, width), BF16),
        ],
        [pltpu.VMEM((width, 3 * width), F32)],
        token_mm * (4 * width + 5 * WIN),
    )
    gx, gxb, layer_out = call(
        functools.partial(token_grad_kernel, per),
        "token_grad",
        [(me, smem), dqkv, wqkv, vec, xhat1, inv1, dx1, y, y_near],
        [
            pltpu.VMEM((own, width), F32),
            pltpu.VMEM((own, width), BF16),
            struct((images * seq_len, width), BF16),
        ],
        [pltpu.SemaphoreType.DMA((2,))],
        flops=token_mm * 3 * width,
    )
    layer_out = layer_out.reshape(images, seq_len, width)

    def place(gx_near):
        return call(
            functools.partial(place_kernel, per),
            "place",
            [(me, smem), gx, gx_near],
            [struct((images * seq_len, width), F32)],
            [pltpu.VMEM((own, width), F32), pltpu.SemaphoreType.DMA((rows // per + 1,))],
        )[0].reshape(images, seq_len, width)

    if usual:
        held_b = fold_step(*halves(held_b), *xbit)
        held_a = fold_step(keep_a, after(send_a, held_b), *core, gxb)
        keep, send = halves(held_b)
        held_b = fold_step(keep, after(send, held_a), *zlo)
        held_a = fold_step(*halves(held_a), *xbit)
        gxb = after(gxb, (held_a, held_b))
        held_a = fold_step(*halves(held_a), *zlo)
        got = swap(halves(held_b)[1], *zhi)
        o_up, o_down = call(
            finish_hidden_kernel, "finish_hidden", [held_b, got], [struct((tall, width), F32)] * 2, limit=2, hbm_outs=False
        )
        got = swap(halves(held_a)[1], *zhi)
        grad_tokens = place(swap(gxb, "tensor", 1))
        got = after(got, grad_tokens)
        shapes = ((small, 3 * width), (small, width), (2, small), (3, small))
        o_qkv, o_out, o_gains, o_bias = call(
            finish_kernel,
            "finish",
            [(me, smem), held_a, got],
            [struct(shape, F32) for shape in shapes],
            limit=2,
            hbm_outs=False,
        )
    else:
        grad_tokens = place(swap(gxb, "tensor", 1))
        grad_a, grad_b = other_reduce((keep_a, send_a), (keep_b, send_b), index, n_dp, n_t)
        o_qkv = jnp.concatenate([grad_a[p * small : (p + 1) * small] for p in range(3)], 1)
        o_out = grad_a[3 * small : 4 * small]
        o_vec = lax.dynamic_slice_in_dim(grad_a[4 * small : 4 * small + 5], index * small, small, 1)
        o_gains, o_bias = o_vec[:2], o_vec[2:]
        o_up, o_down = grad_b[:tall], grad_b[tall:]
    return layer_out, grad_tokens, o_qkv, o_out, o_gains, o_bias, o_up, o_down.T


def solution(mesh):
    in_specs = (
        P("dp", None, None),
        P("dp"),
        P("dp", None),
        P("dp", None, None),
        P(("dp", "tensor"), None),
        P(("dp", "tensor"), None),
        P(None, ("dp", "tensor")),
        P(None, ("dp", "tensor")),
        P("dp", "tensor"),
        P("tensor", "dp"),
    )
    out_specs = (
        P("dp", None, None),
        P("dp", None, None),
        P(("dp", "tensor"), None),
        P(("dp", "tensor"), None),
        P(None, ("dp", "tensor")),
        P(None, ("dp", "tensor")),
        P("dp", "tensor"),
        P("tensor", "dp"),
    )
    return jax.shard_map(
        on_device, mesh=mesh, in_specs=in_specs, out_specs=out_specs, check_vma=False
    )
```

```python
import functools

import jax
import jax.numpy as jnp
from jax import lax
from jax.experimental import pallas as pl
from jax.experimental.pallas import tpu as pltpu
from jax.sharding import PartitionSpec as P

HEADS = 2
WIN = 96
F32 = jnp.float32
BF16 = jnp.bfloat16
VDP, VT = 8, 4
CHIPS = VDP * VT // 2
MIB = 1 << 20

NN = ((1,), (0,))
NT = ((1,), (1,))
TN = ((0,), (0,))


def dot(a, b, dims):
    return lax.dot_general(a, b, (dims, ((), ())), preferred_element_type=F32)


def turn(i):
    return ((i & 1) << 2) | (i & 2) | ((i & 4) >> 2)


def spot(m):
    return (m % 2) * VDP + turn(m // 2)


def turn(i):
    return ((i & 1) << 2) | (i & 2) | ((i & 4) >> 2)


def spot(m):
    return (m % 2) * VDP + turn(m // 2)


def fold(m):
    out = 0
    for place, bit in enumerate(REDUCE_BITS):
        shift = 3 - place
        out = out | (((m // bit) & 1) << shift)
    return out


def norm_parts(values):
    center = values - jnp.mean(values, -1, keepdims=True)
    inv = lax.rsqrt(jnp.mean(center * center, -1, keepdims=True) + 1e-05)
    return center * inv, inv


def norm_back(grad, xhat, inv, gain):
    scaled = grad * gain
    return inv * (
        scaled
        - jnp.mean(scaled, -1, keepdims=True)
        - xhat * jnp.mean(scaled * xhat, -1, keepdims=True)
    )


def gelu_both(u):
    c = 0.7978845608028654
    u2 = u * u
    t = jnp.tanh(u * (c + (c * 0.044715) * u2))
    half = 0.5 + 0.5 * t
    value = u * half
    slope = half + (value - value * half) * (2 * c + (6 * c * 0.044715) * u2)
    return value, slope


def pack_kernel(me, *refs):
    sources, (small_ref, big_ref), held, sems = refs[:6], refs[6:8], refs[8:14], refs[14]
    copies = [pltpu.make_async_copy(a, b, sems.at[n]) for n, (a, b) in enumerate(zip(sources, held))]
    for copy in copies:
        copy.start()
    qkv, out, gains, biases, up, down = held
    small, width = out.shape
    tall = up.shape[0]
    lane = lax.broadcasted_iota(jnp.int32, (1, width), 1)
    mine = lane // small == me[0]
    for copy in copies:
        copy.wait()
    for part in range(3):
        small_ref[0, part * small : (part + 1) * small] = qkv[:, part * width : (part + 1) * width]
    small_ref[0, 3 * small : 4 * small] = out[...]
    rows = [gains[0:1], gains[1:2], biases[0:1], biases[1:2], biases[2:3]]
    vals = jnp.concatenate(rows + [jnp.zeros((3, small), BF16)], 0).astype(F32)
    wide = jnp.concatenate([vals] * (width // small), 1)
    small_ref[0, 4 * small : 4 * small + 8] = jnp.where(mine, wide, 0.0).astype(BF16)
    big_ref[0, :tall] = up[...]
    big_ref[0, tall:] = down[...]


def fetch_kernel(me, tokens, x_ref, xhat_ref, inv_ref, sem):
    own = x_ref.shape[0]
    copy = pltpu.make_async_copy(tokens.at[pl.ds(lax.rem(me[0], 2) * own, own)], x_ref, sem)
    copy.start()
    copy.wait()
    for n in range(own // WIN):
        part = slice(n * WIN, (n + 1) * WIN)
        xhat_ref[part], inv_ref[part] = norm_parts(x_ref[part].astype(F32))


def turn_kernel(me, cot, xhat_ref, cot_ref, cot_t, xhat_t, sem):
    own = cot_ref.shape[0]
    copy = pltpu.make_async_copy(cot.at[pl.ds(lax.rem(me[0], 2) * own, own)], cot_ref, sem)
    copy.start()
    size = 256 if own % 256 == 0 else own
    for n in range(own // size):
        part = slice(n * size, (n + 1) * size)
        xhat_t[:, part] = xhat_ref[part].astype(BF16).T
    copy.wait()
    for n in range(own // size):
        part = slice(n * size, (n + 1) * size)
        cot_t[:, part] = cot_ref[part].T


def attend_kernel(
    per, me, virt, lens, live, x_ref, xhat_ref, held, got,
    qkv_ref, prob_ref, o_ref, x1_ref, wqkv, wout, vec,
):
    tokens, width = x_ref.shape
    rows = tokens // WIN
    hs = width // HEADS
    here = spot(virt[0] // 2) % VDP
    y_own = (virt[0] // 2) % 2
    first = virt[0] % 2 == 0
    total = jnp.zeros((8, width), F32)
    for m in range(CHIPS):
        k = spot(m) ^ (here + y_own * VDP)
        a = held[k].astype(F32)
        b = got[k].astype(F32)
        even = jnp.where(first, a, b)
        odd = jnp.where(first, b, a)
        for part in range(3):
            both = jnp.concatenate([even[part * 8 : part * 8 + 8], odd[part * 8 : part * 8 + 8]], 0)
            wqkv[m * 16 : m * 16 + 16, part * width : (part + 1) * width] = both.astype(BF16)
        both = jnp.concatenate([even[24:32], odd[24:32]], 0)
        wout[m * 16 : m * 16 + 16] = both.astype(BF16)
        total = total + a[32:40] + b[32:40]
    vec[...] = total
    scale = hs**-0.5
    ii = lax.broadcasted_iota(jnp.int32, (WIN, WIN), 0)
    jj = lax.broadcasted_iota(jnp.int32, (WIN, WIN), 1)
    same = ii == jj
    image_rows = live.shape[1]
    base = lax.rem(me[0], 2) * rows

    def enter(c):
        part = slice(c * per * WIN, (c + 1) * per * WIN)
        h1 = (xhat_ref[part] * total[0:1] + total[2:3]).astype(BF16)
        qkv = dot(h1, wqkv[...], NN).astype(BF16)
        qkv_ref[part] = qkv
        scores = []
        for r in range(per):
            at = slice(r * WIN, (r + 1) * WIN)
            for h in range(HEADS):
                q = qkv[at, h * hs : (h + 1) * hs]
                k = qkv[at, width + h * hs : width + (h + 1) * hs]
                scores.append(dot(q, k, NT))
        return qkv, scores

    ahead = enter(0)
    for c in range(rows // per):
        qkv, scores = ahead
        if c + 1 < rows // per:
            ahead = enter(c + 1)
        part = slice(c * per * WIN, (c + 1) * per * WIN)
        probs = []
        for r in range(per):
            row = base + c * per + r
            image = row // image_rows
            inside = row - image * image_rows
            reach = jnp.where(live[image, inside] == 1, lens[image] - inside * WIN, 0)
            allowed = same | (jj < jnp.minimum(ii, reach))
            for h in range(HEADS):
                s = jnp.where(allowed, scores[r * HEADS + h], -1e30)
                e = jnp.exp((s - jnp.max(s, -1, keepdims=True)) * scale)
                probs.append((e * (1.0 / jnp.sum(e, -1, keepdims=True))).astype(BF16))
        mixed = []
        for r in range(per):
            at = slice(r * WIN, (r + 1) * WIN)
            heads = []
            for h in range(HEADS):
                v = qkv[at, 2 * width + h * hs : 2 * width + (h + 1) * hs]
                heads.append(dot(probs[r * HEADS + h], v, NN).astype(BF16))
            mixed.append(jnp.concatenate(heads, 1))
        o = jnp.concatenate(mixed, 0)
        for n, p in enumerate(probs):
            prob_ref[c * per * HEADS + n] = p
        o_ref[part] = o
        x1_ref[part] = x_ref[part].astype(F32) + dot(o, wout[...], NN)


def join(virt, blocks, n, up, down_t):
    tall = blocks.shape[1] // 2
    width = up.shape[0]
    here = turn(virt[0] // 4)
    for i in range(VDP):
        k = turn(i) ^ here
        at = slice(i * tall, (i + 1) * tall)
        cols = slice(n * width, (n + 1) * width)
        up[at, cols] = blocks[k, :tall]
        down_t[at, cols] = blocks[k, tall:]


def hidden_units(h2, dyb, up, down_t):
    u = dot(h2, up[...], NN).astype(BF16)
    da = dot(dyb, down_t[...], NN).astype(BF16)
    a, slope = gelu_both(u)
    return a, da * slope


def hidden_near_kernel(
    per, virt, x1_ref, cot_ref, cot_t, vec, own, got,
    h2_ref, xhat_ref, inv_ref, f_ref, dh2_ref, keep, send,
    a_ref, du_ref, up, down_t, up_t, down,
):
    tokens, width = x1_ref.shape
    size = per * WIN
    join(virt, own, 0, up, down_t)
    join(virt, got, 1, up, down_t)
    up_t[...] = up[...].T
    down[...] = down_t[...].T
    for c in range(tokens // size):
        part = slice(c * size, (c + 1) * size)
        x1 = x1_ref[part]
        xhat, inv = norm_parts(x1)
        xhat_ref[part] = xhat
        inv_ref[part] = inv
        h2 = (xhat * vec[1:2] + vec[3:4]).astype(BF16)
        h2_ref[part] = h2
        a, du = hidden_units(h2, cot_ref[part], up, down_t)
        a_ref[part] = a
        du_ref[part] = du
        f_ref[part] = x1 + vec[4:5] + dot(a, down[...], NN)
        dh2_ref[part] = dot(du, up_t[...], NN)
    gdown = dot(cot_t[...], a_ref[...], NN)
    gup = dot(h2_ref[...], du_ref[...], TN)
    tall = width // VDP
    here = turn(virt[0] // 4)
    for i in range(VDP):
        at = slice(i * tall, (i + 1) * tall)
        k = turn(i) ^ here
        keep[k, :tall] = gup[at, :width]
        keep[k, tall:] = gdown[at, :width]
        send[k, :tall] = gup[at, width:].astype(BF16)
        send[k, tall:] = gdown[at, width:].astype(BF16)


def hidden_far_kernel(
    per, virt, cot_ref, vec, own, got, h2_ref, xhat_ref, inv_ref, f_ref, dh2_ref, o_ref,
    y_ref, dx1_ref, g_ref, gout, gvec,
    up, down_t, up_t, down,
):
    tokens, width = h2_ref.shape
    size = per * WIN
    join(virt, own, 0, up, down_t)
    join(virt, got, 1, up, down_t)
    up_t[...] = up[...].T
    down[...] = down_t[...].T
    sums = [jnp.zeros((1, width), F32)] * 3
    for c in range(tokens // size):
        part = slice(c * size, (c + 1) * size)
        a, du = hidden_units(h2_ref[part], cot_ref[part], up, down_t)
        y_ref[part] = (f_ref[part] + dot(a, down[...], NN)).astype(BF16)
        dh2 = dh2_ref[part] + dot(du, up_t[...], NN)
        dy = cot_ref[part].astype(F32)
        xhat = xhat_ref[part]
        dx1 = dy + norm_back(dh2, xhat, inv_ref[part], vec[1:2])
        dx1_ref[part] = dx1
        g_ref[part] = dx1.astype(BF16)
        for n, term in enumerate((dh2 * xhat, dh2, dy)):
            sums[n] = sums[n] + jnp.sum(term, 0, keepdims=True)
    gout[...] = dot(o_ref[...], g_ref[...], TN)
    zero = jnp.zeros((1, width), F32)
    gvec[...] = jnp.concatenate([zero, sums[0], zero, sums[1], sums[2], zero, zero, zero], 0)


def own_rows(virt, i, other):
    core = virt[0] % 2
    core = 1 - core if other else core
    return pl.ds(pl.multiple_of(i * 32 + ((virt[0] // 2) % 2) * 16 + core * 8, 8), 8)


def back_kernel(
    per, virt, qkv_ref, prob_ref, g_ref, xhat_t, wqkv, wout, vec, gout, gvec,
    dqkv, keep, send,
    gqkv,
):
    tokens, width = g_ref.shape
    hs = width // HEADS
    scale = hs**-0.5
    every = [(r, h) for r in range(tokens // WIN) for h in range(HEADS)]
    groups = [every[n : n + 2 * per] for n in range(0, len(every), 2 * per)]

    def piece(ref, r, h, part=0):
        return ref[r * WIN : (r + 1) * WIN, part * width + h * hs : part * width + (h + 1) * hs]

    def enter(pairs):
        r = pairs[0][0]
        do = dot(g_ref[r * WIN : (r + per) * WIN], wout[...], NT).astype(BF16)
        dos = [do[(n - r) * WIN : (n - r + 1) * WIN, h * hs : (h + 1) * hs] for n, h in pairs]
        probs = [prob_ref[r * HEADS + h] for r, h in pairs]
        dps = [dot(a, piece(qkv_ref, r, h, 2), NT) for a, (r, h) in zip(dos, pairs)]
        dvs = [dot(p, a, TN).astype(BF16) for p, a in zip(probs, dos)]
        return probs, dps, dvs

    ahead = enter(groups[0])
    for place, pairs in enumerate(groups):
        probs, dps, dvs = ahead
        if place + 1 < len(groups):
            ahead = enter(groups[place + 1])
        dss = []
        for p, dp in zip(probs, dps):
            pf = p.astype(F32)
            ds = pf * (dp - jnp.sum(dp * pf, -1, keepdims=True)) * scale
            dss.append(ds.astype(BF16))
        dqs = [dot(ds, piece(qkv_ref, r, h, 1), NN).astype(BF16) for ds, (r, h) in zip(dss, pairs)]
        dks = [dot(ds, piece(qkv_ref, r, h, 0), TN).astype(BF16) for ds, (r, h) in zip(dss, pairs)]
        for n, (r, h) in enumerate(pairs):
            for part, values in enumerate((dqs, dks, dvs)):
                at = slice(part * width + h * hs, part * width + (h + 1) * hs)
                dqkv[r * WIN : (r + 1) * WIN, at] = values[n]
    grad = dot(xhat_t[...], dqkv[...], NN)
    total = jnp.zeros((1, 3 * width), F32)
    for r in range(tokens // WIN):
        total = total + jnp.sum(dqkv[r * WIN : (r + 1) * WIN].astype(F32), 0, keepdims=True)
    w = wqkv[...].astype(F32)
    cols = jnp.concatenate([
        jnp.broadcast_to(jnp.sum(w * grad, -1, keepdims=True), (width, 64)),
        jnp.broadcast_to(jnp.sum(w * total, -1, keepdims=True), (width, 64)),
    ], 1)
    lines = cols.T
    gain, from_total = lines[0:1], lines[64:65]
    vec_t = vec[...].T
    gqkv[...] = grad * vec_t[:, 0:1] + total * vec_t[:, 2:3]
    rest = gvec[...]
    sums = jnp.concatenate([gain, rest[1:2], from_total, rest[3:]], 0)
    here = turn(virt[0] // 4)
    for i in range(VDP):
        k = turn(i) ^ here
        mine, other = own_rows(virt, i, 0), own_rows(virt, i, 1)
        theirs = []
        for part in range(3):
            at = slice(part * width, (part + 1) * width)
            keep[k, part * 8 : part * 8 + 8] = gqkv[mine, at]
            theirs.append(gqkv[other, at])
        keep[k, 24:32] = gout[mine]
        keep[k, 32:] = sums
        send[k] = jnp.concatenate(theirs + [gout[other], sums], 0).astype(BF16)


def token_grad_kernel(per, me, dqkv, wqkv, vec, xhat_ref, inv_ref, dx1_ref, y, y_near, gx, gxb, out, sems):
    own = dqkv.shape[0]
    size = per * WIN
    copies = []
    for n, source in enumerate((y, y_near)):
        at = pl.ds((lax.rem(me[0], 2) ^ n) * own, own)
        copies.append(pltpu.make_async_copy(source, out.at[at], sems.at[n]))
        copies[-1].start()
    ahead = dot(dqkv[:size], wqkv[...], NT)
    for c in range(own // size):
        part = slice(c * size, (c + 1) * size)
        dh1 = ahead
        if (c + 1) * size < own:
            ahead = dot(dqkv[(c + 1) * size : (c + 2) * size], wqkv[...], NT)
        values = dx1_ref[part] + norm_back(dh1, xhat_ref[part], inv_ref[part], vec[0:1])
        gx[part] = values
        gxb[part] = values.astype(BF16)
    for copy in copies:
        copy.wait()


def place_kernel(per, me, mine, theirs, out, wide, sems):
    own = theirs.shape[0]
    size = per * WIN
    here = lax.rem(me[0], 2) * own
    copies = [pltpu.make_async_copy(mine, out.at[pl.ds(here, own)], sems.at[own // size])]
    copies[0].start()
    for c in range(own // size):
        part = pl.ds(c * size, size)
        wide[part] = theirs[part].astype(F32)
        at = pl.ds(own - here + c * size, size)
        copies.append(pltpu.make_async_copy(wide.at[part], out.at[at], sems.at[c]))
        copies[-1].start()
    for copy in copies:
        copy.wait()


def finish_hidden_kernel(keep, got, up, down):
    total = keep[0] + got[0].astype(F32)
    tall = up.shape[0]
    up[...] = total[:tall]
    down[...] = total[tall:]


def finish_kernel(me, keep, got, qkv, out, gains, biases):
    total = keep[0] + got[0].astype(F32)
    small, width = out.shape
    for part in range(3):
        qkv[:, part * width : (part + 1) * width] = total[part * small : (part + 1) * small]
    out[...] = total[3 * small : 4 * small]
    vec = pltpu.roll(total[4 * small :], width - me[0] * small, 1)[:, :small]
    gains[...] = vec[:2]
    biases[...] = vec[2:5]


def swap(block, axis, bit):
    size = lax.axis_size(axis)
    return lax.ppermute(block, axis, [(i, i ^ bit) for i in range(size)])


def steps_of(axis):
    return [(axis, 1 << k) for k in reversed(range(lax.axis_size(axis).bit_length() - 1))]


def after(value, other):
    return lax.optimization_barrier((value, other))[0]


def halves(held):
    half = held.shape[0] // 2
    return held[:half], held[half:].astype(BF16)


def fold_step(keep, send, axis, bit, past=None):
    got = swap(send, axis, bit)
    return keep + (got if past is None else after(got, past)).astype(F32)


def bit_reverse(index, count):
    out = 0 * index
    for k in range(count):
        out = out | (((index >> k) & 1) << (count - 1 - k))
    return out


def by_device(block, me):
    blocks = block[None]
    for axis, bit in steps_of("dp") + steps_of("tensor"):
        blocks = jnp.concatenate([blocks, swap(blocks, axis, bit)], 0)
    count = blocks.shape[0]
    order = jnp.arange(count, dtype=jnp.int32) ^ me
    return jnp.take(blocks, bit_reverse(order, count.bit_length() - 1), axis=0)


def other_pack(w_qkv, w_out, gains, biases, w_up, w_down, me):
    small, width = w_out.shape
    qkv = w_qkv.reshape(small, 3, width).transpose(1, 0, 2).reshape(3 * small, width)
    rows = jnp.concatenate([gains, biases], 0)
    place = jnp.zeros((8, width), BF16)
    place = lax.dynamic_update_slice(place, rows, (jnp.int32(0), me * small))
    return jnp.concatenate([qkv, w_out, place], 0), jnp.concatenate([w_up, w_down.T], 0)


def other_blocks(a, b, me, n_dp, n_t):
    a = by_device(a, me)
    b = by_device(b, me)
    width = a.shape[2]
    count = n_dp * n_t
    small = width // count
    big = width // (VDP * VT)
    mats = a[:, : 4 * small].reshape(count, 4, small, width).transpose(1, 0, 2, 3)
    mats = mats.reshape(4, VDP * VT, big, width).transpose(1, 0, 2, 3).reshape(VDP * VT, 4 * big, width)
    vec = jnp.sum(a[:, 4 * small :].astype(F32), 0).astype(BF16)
    vecs = jnp.concatenate([vec[None], jnp.zeros((VDP * VT - 1, 8, width), BF16)], 0)
    a = jnp.concatenate([mats, vecs], 1)
    tall = width // n_dp
    b = b.reshape(n_dp, VT, 2, tall, width).transpose(1, 2, 0, 3, 4)
    b = b.reshape(VT, 2, VDP, width // VDP, width).transpose(2, 0, 1, 3, 4)
    b = b.reshape(VDP * VT, 2 * (width // VDP), width)

    y_own = (me // 2) % 2

    def placed(blocks):
        pairs = blocks.reshape((CHIPS, 2) + blocks.shape[1:])
        pairs = jnp.stack([pairs[m] for m in sorted(range(CHIPS), key=spot)], 0)
        pairs = jnp.where(y_own == 1, jnp.roll(pairs, VDP, 0), pairs)
        return pairs[:, 0], pairs[:, 1]

    return placed(a) + placed(b)


def other_reduce(pair_a, pair_b, me, n_dp, n_t):
    count = n_dp * n_t
    y_own = (me // 2) % 2

    def whole(keep, send):
        pairs = jnp.stack([keep, send.astype(F32)], 1)
        pairs = jnp.stack([pairs[turn(i)] for i in range(VDP)], 0)
        none = jnp.zeros_like(pairs)
        both = jnp.stack([jnp.where(y_own == y, pairs, none) for y in range(2)], 1)
        return both.reshape((VDP * VT,) + keep.shape[1:])

    def rows_of(blocks, parts):
        big = blocks.shape[1] // parts
        mats = blocks.reshape(VDP * VT, parts, big, -1).transpose(1, 0, 2, 3)
        mats = mats.reshape(parts, count, VDP * VT * big // count, -1).transpose(1, 0, 2, 3)
        return mats.reshape(count, -1, blocks.shape[2])

    def vec_of(blocks):
        picked = jnp.where(y_own == 0, blocks[0], 0.0)
        return jnp.broadcast_to(picked[None], (count,) + picked.shape)

    a, b = whole(*pair_a), whole(*pair_b)
    width = a.shape[2]
    tall, high = width // n_dp, width // VDP
    cols = b.reshape(VDP, VT, 2, high, width).transpose(1, 2, 0, 3, 4)
    cols = cols.reshape(VT, 2, n_dp, tall, width).transpose(2, 0, 1, 3, 4)
    cols = cols.reshape(count, 2 * tall, width)
    a = jnp.concatenate([rows_of(a[:, :32], 4), vec_of(a[:, 32:])], 1)
    results = []
    for blocks in (a, cols):
        blocks = jnp.take(blocks, jnp.arange(count, dtype=jnp.int32) ^ me, axis=0)
        for axis, bit in reversed(steps_of("dp") + steps_of("tensor")):
            pairs = blocks.reshape((-1, 2) + blocks.shape[1:])
            got = swap(pairs[:, 1].astype(BF16), axis, bit)
            blocks = pairs[:, 0] + got.astype(F32)
        results.append(blocks[0])
    return results


def struct(shape, dtype):
    return jax.ShapeDtypeStruct(shape, dtype)


def call(kernel, name, args, outs, scratch=(), flops=0, limit=16, hbm_outs=True):
    args = [a if isinstance(a, tuple) else (a, pltpu.VMEM) for a in args]
    moved = sum(a.size * a.dtype.itemsize for a, _ in args)
    spaces = [pl.ANY if hbm_outs and isinstance(o, jax.ShapeDtypeStruct) else pltpu.VMEM for o in outs]
    return pl.pallas_call(
        kernel,
        name=name,
        out_shape=outs,
        in_specs=[pl.BlockSpec(memory_space=space) for _, space in args],
        out_specs=[pl.BlockSpec(memory_space=space) for space in spaces],
        scratch_shapes=list(scratch),
        compiler_params=pltpu.CompilerParams(vmem_limit_bytes=limit * MIB),
        cost_estimate=pl.CostEstimate(flops=flops, bytes_accessed=moved, transcendentals=0),
    )(*[a for a, _ in args])


def on_device(tokens, lengths, row_mask, cotangent, w_qkv, w_out, gains, biases, w_up, w_down):
    images, seq_len, width = tokens.shape
    n_dp, n_t = lax.axis_size("dp"), lax.axis_size("tensor")
    index = lax.axis_index("dp") * n_t + lax.axis_index("tensor")
    me = index.astype(jnp.int32).reshape(1)
    usual = (n_dp, n_t) == (VDP, VT)
    virt = me if usual else (index // 2 % 2 * 2).astype(jnp.int32).reshape(1)
    small = width // (n_dp * n_t)
    tall = width // n_dp
    own = images * seq_len // 2
    rows = own // WIN
    per = 4 if rows % 4 == 0 else 1
    smem = pltpu.SMEM
    weights = (w_qkv, w_out, gains, biases, w_up, w_down)
    token_mm = 2 * own * width
    hbm = pltpu.HBM

    def in_hbm(array):
        return (pltpu.with_memory_space_constraint(array, hbm), hbm)

    def fetch(me):
        return call(
            fetch_kernel,
            "fetch",
            [(me, smem), in_hbm(tokens.reshape(images * seq_len, width))],
            [
                pltpu.VMEM((own, width), BF16),
                pltpu.VMEM((own, width), F32),
                pltpu.VMEM((own, 1), F32),
            ],
            [pltpu.SemaphoreType.DMA(())],
            limit=4,
        )

    def fetch_turned(me, xhat):
        return call(
            turn_kernel,
            "turn",
            [(me, smem), in_hbm(cotangent.reshape(images * seq_len, width)), xhat],
            [
                pltpu.VMEM((own, width), BF16),
                pltpu.VMEM((width, own), BF16),
                pltpu.VMEM((width, own), BF16),
            ],
            [pltpu.SemaphoreType.DMA(())],
            limit=4,
        )

    if usual:
        weights = (w_qkv, w_out, gains, biases, w_up, w_down.T)
        pack_a, pack_b = call(
            pack_kernel,
            "pack",
            [(me, smem)] + [in_hbm(w) for w in weights],
            [
                pltpu.VMEM((1, 4 * small + 8, width), BF16),
                pltpu.VMEM((1, 2 * tall, width), BF16),
            ],
            [pltpu.VMEM(w.shape, BF16) for w in weights] + [pltpu.SemaphoreType.DMA((6,))],
        )
        held_a, b = pack_a, pack_b
        x, xhat1, inv1 = fetch(me)
        for n, (axis, bit) in enumerate(steps_of("dp")):
            if n == 1:
                held_a = after(held_a, xhat1)
            held_a = jnp.concatenate([held_a, swap(held_a, axis, bit)], 0)
            b = jnp.concatenate([b, swap(b, axis, bit)], 0)
            b = after(b, held_a)
        cot, cot_t, xhat_t = fetch_turned(after(me, held_a), xhat1)
        held_a = jnp.concatenate([held_a, after(swap(held_a, "tensor", 2), cot)], 0)
        far_b = swap(b, "tensor", 2)
        got_a = swap(held_a, "tensor", 1)
        got_b = swap(after(b, held_a), "tensor", 1)
    else:
        held_a, got_a, held_b, got_b = other_blocks(*other_pack(*weights, index), index, n_dp, n_t)
        b, far_b = held_b[:VDP], held_b[VDP:]
        got_b, got_far = got_b[:VDP], got_b[VDP:]
        x, xhat1, inv1 = fetch(me)
        cot, cot_t, xhat_t = fetch_turned(me, xhat1)
    qkv, prob, o, x1, wqkv, wout, vec = call(
        functools.partial(attend_kernel, per),
        "attend",
        [(me, smem), (virt, smem), (lengths, smem), (row_mask, smem), x, xhat1, held_a, got_a],
        [
            pltpu.VMEM((own, 3 * width), BF16),
            pltpu.VMEM((rows * HEADS, WIN, WIN), BF16),
            pltpu.VMEM((own, width), BF16),
            pltpu.VMEM((own, width), F32),
            pltpu.VMEM((width, 3 * width), BF16),
            pltpu.VMEM((width, width), BF16),
            pltpu.VMEM((8, width), F32),
        ],
        flops=token_mm * (4 * width + 2 * WIN),
    )
    if usual:
        far_b = after(far_b, x1)
        got_b = after(got_b, far_b)
        got_far = swap(far_b, "tensor", 1)
    tall_b = 2 * (width // VDP)
    mats = [pltpu.VMEM((width, 2 * width), BF16)] * 2 + [pltpu.VMEM((2 * width, width), BF16)] * 2
    h2, xhat2, inv2, f, dh2, keep_b, send_b = call(
        functools.partial(hidden_near_kernel, per),
        "hidden_near",
        [(virt, smem), x1, cot, cot_t, vec, b, got_b],
        [
            pltpu.VMEM((own, width), BF16),
            pltpu.VMEM((own, width), F32),
            pltpu.VMEM((own, 1), F32),
            pltpu.VMEM((own, width), F32),
            pltpu.VMEM((own, width), F32),
            pltpu.VMEM((VDP, tall_b, width), F32),
            pltpu.VMEM((VDP, tall_b, width), BF16),
        ],
        [pltpu.VMEM((own, 2 * width), BF16)] * 2 + mats,
        token_mm * 12 * width,
    )
    y, dx1, g, gout, gvec = call(
        functools.partial(hidden_far_kernel, per),
        "hidden_far",
        [(virt, smem), cot, vec, far_b, got_far, h2, xhat2, inv2, f, dh2, o],
        [
            pltpu.VMEM((own, width), BF16),
            pltpu.VMEM((own, width), F32),
            pltpu.VMEM((own, width), BF16),
            pltpu.VMEM((width, width), F32),
            pltpu.VMEM((8, width), F32),
        ],
        mats,
        token_mm * 9 * width,
    )
    core, xbit, zlo, zhi = ("tensor", 1), ("dp", 1), ("dp", 2), ("dp", 4)
    if usual:
        held_b = fold_step(keep_b, send_b, *core, g)
        y = after(y, held_b)
    y_near = swap(y, "tensor", 1)
    dqkv, keep_a, send_a = call(
        functools.partial(back_kernel, per),
        "back",
        [(virt, smem), qkv, prob, g, xhat_t, wqkv, wout, vec, gout, gvec],
        [
            pltpu.VMEM((own, 3 * width), BF16),
            pltpu.VMEM((VDP, 40, width), F32),
            pltpu.VMEM((VDP, 40, width), BF16),
        ],
        [pltpu.VMEM((width, 3 * width), F32)],
        token_mm * (4 * width + 5 * WIN),
    )
    gx, gxb, layer_out = call(
        functools.partial(token_grad_kernel, per),
        "token_grad",
        [(me, smem), dqkv, wqkv, vec, xhat1, inv1, dx1, y, y_near],
        [
            pltpu.VMEM((own, width), F32),
            pltpu.VMEM((own, width), BF16),
            struct((images * seq_len, width), BF16),
        ],
        [pltpu.SemaphoreType.DMA((2,))],
        flops=token_mm * 3 * width,
    )
    layer_out = layer_out.reshape(images, seq_len, width)

    def place(gx_near):
        return call(
            functools.partial(place_kernel, per),
            "place",
            [(me, smem), gx, gx_near],
            [struct((images * seq_len, width), F32)],
            [pltpu.VMEM((own, width), F32), pltpu.SemaphoreType.DMA((rows // per + 1,))],
        )[0].reshape(images, seq_len, width)

    if usual:
        held_b = fold_step(*halves(held_b), *xbit)
        held_a = fold_step(keep_a, after(send_a, held_b), *core, gxb)
        grad_tokens = place(swap(after(gxb, held_a), "tensor", 1))
        keep, send = halves(held_b)
        held_b = fold_step(keep, after(send, held_a), *zlo)
        held_a = fold_step(*halves(held_a), *xbit)
        held_a = fold_step(*halves(held_a), *zlo, grad_tokens)
        got = swap(halves(held_b)[1], *zhi)
        o_up, o_down = call(
            finish_hidden_kernel, "finish_hidden", [held_b, got], [struct((tall, width), F32)] * 2, limit=2, hbm_outs=False
        )
        got = swap(halves(held_a)[1], *zhi)
        shapes = ((small, 3 * width), (small, width), (2, small), (3, small))
        o_qkv, o_out, o_gains, o_bias = call(
            finish_kernel,
            "finish",
            [(me, smem), held_a, got],
            [struct(shape, F32) for shape in shapes],
            limit=2,
            hbm_outs=False,
        )
    else:
        grad_tokens = place(swap(gxb, "tensor", 1))
        grad_a, grad_b = other_reduce((keep_a, send_a), (keep_b, send_b), index, n_dp, n_t)
        o_qkv = jnp.concatenate([grad_a[p * small : (p + 1) * small] for p in range(3)], 1)
        o_out = grad_a[3 * small : 4 * small]
        o_vec = lax.dynamic_slice_in_dim(grad_a[4 * small : 4 * small + 5], index * small, small, 1)
        o_gains, o_bias = o_vec[:2], o_vec[2:]
        o_up, o_down = grad_b[:tall], grad_b[tall:]
    return layer_out, grad_tokens, o_qkv, o_out, o_gains, o_bias, o_up, o_down.T


def solution(mesh):
    in_specs = (
        P("dp", None, None),
        P("dp"),
        P("dp", None),
        P("dp", None, None),
        P(("dp", "tensor"), None),
        P(("dp", "tensor"), None),
        P(None, ("dp", "tensor")),
        P(None, ("dp", "tensor")),
        P("dp", "tensor"),
        P("tensor", "dp"),
    )
    out_specs = (
        P("dp", None, None),
        P("dp", None, None),
        P(("dp", "tensor"), None),
        P(("dp", "tensor"), None),
        P(None, ("dp", "tensor")),
        P(None, ("dp", "tensor")),
        P("dp", "tensor"),
        P("tensor", "dp"),
    )
    return jax.shard_map(
        on_device, mesh=mesh, in_specs=in_specs, out_specs=out_specs, check_vma=False
    )
```

```python
import functools

import jax
import jax.numpy as jnp
from jax import lax
from jax.experimental import pallas as pl
from jax.experimental.pallas import tpu as pltpu
from jax.sharding import PartitionSpec as P

HEADS = 2
WIN = 96
F32 = jnp.float32
BF16 = jnp.bfloat16
VDP, VT = 8, 4
CHIPS = VDP * VT // 2
MIB = 1 << 20

NN = ((1,), (0,))
NT = ((1,), (1,))
TN = ((0,), (0,))


def dot(a, b, dims):
    return lax.dot_general(a, b, (dims, ((), ())), preferred_element_type=F32)


def turn(i):
    return ((i & 1) << 2) | (i & 2) | ((i & 4) >> 2)


def spot(m):
    return (m % 2) * VDP + turn(m // 2)


def grid_spot(m):
    return (m % 2) * VDP + ((m // 2) % 2) * 4 + m // 4


def turn(i):
    return ((i & 1) << 2) | (i & 2) | ((i & 4) >> 2)


def spot(m):
    return (m % 2) * VDP + turn(m // 2)


def grid_spot(m):
    return (m % 2) * VDP + ((m // 2) % 2) * 4 + m // 4


def fold(m):
    out = 0
    for place, bit in enumerate(REDUCE_BITS):
        shift = 3 - place
        out = out | (((m // bit) & 1) << shift)
    return out


def norm_parts(values):
    center = values - jnp.mean(values, -1, keepdims=True)
    inv = lax.rsqrt(jnp.mean(center * center, -1, keepdims=True) + 1e-05)
    return center * inv, inv


def norm_back(grad, xhat, inv, gain):
    scaled = grad * gain
    return inv * (
        scaled
        - jnp.mean(scaled, -1, keepdims=True)
        - xhat * jnp.mean(scaled * xhat, -1, keepdims=True)
    )


def gelu_both(u):
    c = 0.7978845608028654
    u2 = u * u
    t = jnp.tanh(u * (c + (c * 0.044715) * u2))
    half = 0.5 + 0.5 * t
    value = u * half
    slope = half + (value - value * half) * (2 * c + (6 * c * 0.044715) * u2)
    return value, slope


def pack_kernel(me, *refs):
    sources, (small_ref, big_ref), held, sems = refs[:6], refs[6:8], refs[8:14], refs[14]
    copies = [pltpu.make_async_copy(a, b, sems.at[n]) for n, (a, b) in enumerate(zip(sources, held))]
    for copy in copies:
        copy.start()
    qkv, out, gains, biases, up, down = held
    small, width = out.shape
    tall = up.shape[0]
    lane = lax.broadcasted_iota(jnp.int32, (1, width), 1)
    mine = lane // small == me[0]
    for copy in copies:
        copy.wait()
    rows = [gains[0:1], gains[1:2], biases[0:1], biases[1:2], biases[2:3]]
    vals = jnp.concatenate(rows + [jnp.zeros((3, small), BF16)], 0).astype(F32)
    wide = jnp.concatenate([vals] * (width // small), 1)
    vec = jnp.where(mine, wide, 0.0).astype(BF16)
    for n in range(small_ref.shape[0]):
        for part in range(3):
            small_ref[n, part * small : (part + 1) * small] = qkv[:, part * width : (part + 1) * width]
        small_ref[n, 3 * small : 4 * small] = out[...]
        small_ref[n, 4 * small : 4 * small + 8] = vec
    big_ref[0, :tall] = up[...]
    big_ref[0, tall:] = down[...]


def fetch_kernel(me, tokens, x_ref, xhat_ref, inv_ref, sem):
    own, width = x_ref.shape
    ones = jnp.full((width, width), 1.0 / width, BF16)
    copy = pltpu.make_async_copy(tokens.at[pl.ds(lax.rem(me[0], 2) * own, own)], x_ref, sem)
    copy.start()
    copy.wait()
    for n in range(own // (2 * WIN)):
        part = slice(n * 2 * WIN, (n + 1) * 2 * WIN)
        x = x_ref[part]
        center = x.astype(F32) - dot(x, ones, NN)
        inv = lax.rsqrt(dot((center * center).astype(BF16), ones, NN) + 1e-05)
        xhat_ref[part] = center * inv
        inv_ref[part] = inv[:, :1]


def turn_kernel(me, cot, xhat_ref, cot_ref, cot_t, xhat_t, sem):
    own = cot_ref.shape[0]
    copy = pltpu.make_async_copy(cot.at[pl.ds(lax.rem(me[0], 2) * own, own)], cot_ref, sem)
    copy.start()
    size = 256 if own % 256 == 0 else own
    for n in range(own // size):
        part = slice(n * size, (n + 1) * size)
        xhat_t[:, part] = xhat_ref[part].astype(BF16).T
    copy.wait()
    for n in range(own // size):
        part = slice(n * size, (n + 1) * size)
        cot_t[:, part] = cot_ref[part].T


def attend_kernel(
    per, me, virt, lens, live, x_ref, xhat_ref, held, got,
    qkv_ref, prob_ref, o_ref, x1_ref, wqkv, wout, vec,
):
    tokens, width = x_ref.shape
    rows = tokens // WIN
    hs = width // HEADS
    here = ((virt[0] // 4) % 2) * 4
    y_own = (virt[0] // 2) % 2
    first = virt[0] % 2 == 0
    total = jnp.zeros((8, width), F32)
    for m in range(CHIPS):
        k = grid_spot(m) ^ (here + y_own * VDP)
        a = held[k].astype(F32)
        b = got[k].astype(F32)
        even = jnp.where(first, a, b)
        odd = jnp.where(first, b, a)
        for part in range(3):
            both = jnp.concatenate([even[part * 8 : part * 8 + 8], odd[part * 8 : part * 8 + 8]], 0)
            wqkv[m * 16 : m * 16 + 16, part * width : (part + 1) * width] = both.astype(BF16)
        both = jnp.concatenate([even[24:32], odd[24:32]], 0)
        wout[m * 16 : m * 16 + 16] = both.astype(BF16)
        total = total + a[32:40] + b[32:40]
    vec[...] = total
    scale = hs**-0.5
    ii = lax.broadcasted_iota(jnp.int32, (WIN, WIN), 0)
    jj = lax.broadcasted_iota(jnp.int32, (WIN, WIN), 1)
    same = ii == jj
    image_rows = live.shape[1]
    base = lax.rem(me[0], 2) * rows

    def enter(c):
        part = slice(c * per * WIN, (c + 1) * per * WIN)
        h1 = (xhat_ref[part] * total[0:1] + total[2:3]).astype(BF16)
        qkv = dot(h1, wqkv[...], NN).astype(BF16)
        qkv_ref[part] = qkv
        scores = []
        for r in range(per):
            at = slice(r * WIN, (r + 1) * WIN)
            for h in range(HEADS):
                q = qkv[at, h * hs : (h + 1) * hs]
                k = qkv[at, width + h * hs : width + (h + 1) * hs]
                scores.append(dot(q, k, NT))
        return qkv, scores

    ahead = enter(0)
    for c in range(rows // per):
        qkv, scores = ahead
        if c + 1 < rows // per:
            ahead = enter(c + 1)
        part = slice(c * per * WIN, (c + 1) * per * WIN)
        probs = []
        for r in range(per):
            row = base + c * per + r
            image = row // image_rows
            inside = row - image * image_rows
            reach = jnp.where(live[image, inside] == 1, lens[image] - inside * WIN, 0)
            allowed = same | (jj < jnp.minimum(ii, reach))
            for h in range(HEADS):
                s = jnp.where(allowed, scores[r * HEADS + h], -1e30)
                e = jnp.exp((s - jnp.max(s, -1, keepdims=True)) * scale)
                probs.append((e * (1.0 / jnp.sum(e, -1, keepdims=True))).astype(BF16))
        mixed = []
        for r in range(per):
            at = slice(r * WIN, (r + 1) * WIN)
            heads = []
            for h in range(HEADS):
                v = qkv[at, 2 * width + h * hs : 2 * width + (h + 1) * hs]
                heads.append(dot(probs[r * HEADS + h], v, NN).astype(BF16))
            mixed.append(jnp.concatenate(heads, 1))
        o = jnp.concatenate(mixed, 0)
        for n, p in enumerate(probs):
            prob_ref[c * per * HEADS + n] = p
        o_ref[part] = o
        x1_ref[part] = x_ref[part].astype(F32) + dot(o, wout[...], NN)


def join(virt, blocks, n, up, down_t):
    tall = blocks.shape[1] // 2
    width = up.shape[0]
    here = turn(virt[0] // 4)
    for i in range(VDP):
        k = turn(i) ^ here
        at = slice(i * tall, (i + 1) * tall)
        cols = slice(n * width, (n + 1) * width)
        up[at, cols] = blocks[k, :tall]
        down_t[at, cols] = blocks[k, tall:]


def hidden_units(h2, dyb, up, down_t):
    u = dot(h2, up[...], NN).astype(BF16)
    da = dot(dyb, down_t[...], NN).astype(BF16)
    a, slope = gelu_both(u)
    return a, da * slope


def hidden_near_kernel(
    per, virt, x1_ref, cot_ref, cot_t, vec, own, got,
    h2_ref, xhat_ref, inv_ref, f_ref, dh2_ref, keep, send,
    a_ref, du_ref, up, down_t, up_t, down,
):
    tokens, width = x1_ref.shape
    size = per * WIN
    join(virt, own, 0, up, down_t)
    join(virt, got, 1, up, down_t)
    up_t[...] = up[...].T
    down[...] = down_t[...].T
    for c in range(tokens // size):
        part = slice(c * size, (c + 1) * size)
        x1 = x1_ref[part]
        xhat, inv = norm_parts(x1)
        xhat_ref[part] = xhat
        inv_ref[part] = inv
        h2 = (xhat * vec[1:2] + vec[3:4]).astype(BF16)
        h2_ref[part] = h2
        a, du = hidden_units(h2, cot_ref[part], up, down_t)
        a_ref[part] = a
        du_ref[part] = du
        f_ref[part] = x1 + vec[4:5] + dot(a, down[...], NN)
        dh2_ref[part] = dot(du, up_t[...], NN)
    gdown = dot(cot_t[...], a_ref[...], NN)
    gup = dot(h2_ref[...], du_ref[...], TN)
    tall = width // VDP
    here = turn(virt[0] // 4)
    for i in range(VDP):
        at = slice(i * tall, (i + 1) * tall)
        k = turn(i) ^ here
        keep[k, :tall] = gup[at, :width]
        keep[k, tall:] = gdown[at, :width]
        send[k, :tall] = gup[at, width:].astype(BF16)
        send[k, tall:] = gdown[at, width:].astype(BF16)


def hidden_far_kernel(
    per, virt, cot_ref, vec, own, got, h2_ref, xhat_ref, inv_ref, f_ref, dh2_ref, o_ref,
    y_ref, dx1_ref, g_ref, gout, gvec,
    up, down_t, up_t, down,
):
    tokens, width = h2_ref.shape
    size = per * WIN
    join(virt, own, 0, up, down_t)
    join(virt, got, 1, up, down_t)
    up_t[...] = up[...].T
    down[...] = down_t[...].T
    sums = [jnp.zeros((1, width), F32)] * 3
    for c in range(tokens // size):
        part = slice(c * size, (c + 1) * size)
        a, du = hidden_units(h2_ref[part], cot_ref[part], up, down_t)
        y_ref[part] = (f_ref[part] + dot(a, down[...], NN)).astype(BF16)
        dh2 = dh2_ref[part] + dot(du, up_t[...], NN)
        dy = cot_ref[part].astype(F32)
        xhat = xhat_ref[part]
        dx1 = dy + norm_back(dh2, xhat, inv_ref[part], vec[1:2])
        dx1_ref[part] = dx1
        g_ref[part] = dx1.astype(BF16)
        for n, term in enumerate((dh2 * xhat, dh2, dy)):
            sums[n] = sums[n] + jnp.sum(term, 0, keepdims=True)
    gout[...] = dot(o_ref[...], g_ref[...], TN)
    zero = jnp.zeros((1, width), F32)
    gvec[...] = jnp.concatenate([zero, sums[0], zero, sums[1], sums[2], zero, zero, zero], 0)


def own_rows(virt, i, other):
    core = virt[0] % 2
    core = 1 - core if other else core
    return pl.ds(pl.multiple_of(i * 32 + ((virt[0] // 2) % 2) * 16 + core * 8, 8), 8)


def back_kernel(
    per, virt, qkv_ref, prob_ref, g_ref, xhat_t, wqkv, wout, vec, gout, gvec,
    dqkv, keep, send,
    gqkv,
):
    tokens, width = g_ref.shape
    hs = width // HEADS
    scale = hs**-0.5
    every = [(r, h) for r in range(tokens // WIN) for h in range(HEADS)]
    groups = [every[n : n + 2 * per] for n in range(0, len(every), 2 * per)]

    def piece(ref, r, h, part=0):
        return ref[r * WIN : (r + 1) * WIN, part * width + h * hs : part * width + (h + 1) * hs]

    def enter(pairs):
        r = pairs[0][0]
        do = dot(g_ref[r * WIN : (r + per) * WIN], wout[...], NT).astype(BF16)
        dos = [do[(n - r) * WIN : (n - r + 1) * WIN, h * hs : (h + 1) * hs] for n, h in pairs]
        probs = [prob_ref[r * HEADS + h] for r, h in pairs]
        dps = [dot(a, piece(qkv_ref, r, h, 2), NT) for a, (r, h) in zip(dos, pairs)]
        dvs = [dot(p, a, TN).astype(BF16) for p, a in zip(probs, dos)]
        return probs, dps, dvs

    ahead = enter(groups[0])
    for place, pairs in enumerate(groups):
        probs, dps, dvs = ahead
        if place + 1 < len(groups):
            ahead = enter(groups[place + 1])
        dss = []
        for p, dp in zip(probs, dps):
            pf = p.astype(F32)
            ds = pf * (dp - jnp.sum(dp * pf, -1, keepdims=True)) * scale
            dss.append(ds.astype(BF16))
        dqs = [dot(ds, piece(qkv_ref, r, h, 1), NN).astype(BF16) for ds, (r, h) in zip(dss, pairs)]
        dks = [dot(ds, piece(qkv_ref, r, h, 0), TN).astype(BF16) for ds, (r, h) in zip(dss, pairs)]
        for n, (r, h) in enumerate(pairs):
            for part, values in enumerate((dqs, dks, dvs)):
                at = slice(part * width + h * hs, part * width + (h + 1) * hs)
                dqkv[r * WIN : (r + 1) * WIN, at] = values[n]
    grad = dot(xhat_t[...], dqkv[...], NN)
    total = jnp.zeros((1, 3 * width), F32)
    for r in range(tokens // WIN):
        total = total + jnp.sum(dqkv[r * WIN : (r + 1) * WIN].astype(F32), 0, keepdims=True)
    w = wqkv[...].astype(F32)
    cols = jnp.concatenate([
        jnp.broadcast_to(jnp.sum(w * grad, -1, keepdims=True), (width, 64)),
        jnp.broadcast_to(jnp.sum(w * total, -1, keepdims=True), (width, 64)),
    ], 1)
    lines = cols.T
    gain, from_total = lines[0:1], lines[64:65]
    vec_t = vec[...].T
    gqkv[...] = grad * vec_t[:, 0:1] + total * vec_t[:, 2:3]
    rest = gvec[...]
    sums = jnp.concatenate([gain, rest[1:2], from_total, rest[3:]], 0)
    here = ((virt[0] // 4) % 2) * 4
    for i in range(VDP):
        k = ((i % 2) * 4 + i // 2) ^ here
        mine, other = own_rows(virt, i, 0), own_rows(virt, i, 1)
        theirs = []
        for part in range(3):
            at = slice(part * width, (part + 1) * width)
            keep[k, part * 8 : part * 8 + 8] = gqkv[mine, at]
            theirs.append(gqkv[other, at])
        keep[k, 24:32] = gout[mine]
        keep[k, 32:] = sums
        send[k] = jnp.concatenate(theirs + [gout[other], sums], 0).astype(BF16)


def token_grad_kernel(per, me, dqkv, wqkv, vec, xhat_ref, inv_ref, dx1_ref, y, y_near, gx, gxb, out, sems):
    own = dqkv.shape[0]
    size = per * WIN
    copies = []
    for n, source in enumerate((y, y_near)):
        at = pl.ds((lax.rem(me[0], 2) ^ n) * own, own)
        copies.append(pltpu.make_async_copy(source, out.at[at], sems.at[n]))
        copies[-1].start()
    ahead = dot(dqkv[:size], wqkv[...], NT)
    for c in range(own // size):
        part = slice(c * size, (c + 1) * size)
        dh1 = ahead
        if (c + 1) * size < own:
            ahead = dot(dqkv[(c + 1) * size : (c + 2) * size], wqkv[...], NT)
        values = dx1_ref[part] + norm_back(dh1, xhat_ref[part], inv_ref[part], vec[0:1])
        gx[part] = values
        gxb[part] = values.astype(BF16)
    for copy in copies:
        copy.wait()


def place_kernel(per, me, mine, theirs, out, wide, sems):
    own = theirs.shape[0]
    size = per * WIN
    here = lax.rem(me[0], 2) * own
    copies = [pltpu.make_async_copy(mine, out.at[pl.ds(here, own)], sems.at[own // size])]
    copies[0].start()
    for c in range(own // size):
        part = pl.ds(c * size, size)
        wide[part] = theirs[part].astype(F32)
        at = pl.ds(own - here + c * size, size)
        copies.append(pltpu.make_async_copy(wide.at[part], out.at[at], sems.at[c]))
        copies[-1].start()
    for copy in copies:
        copy.wait()


def finish_hidden_kernel(keep, got, up, down):
    total = keep[0] + got[0].astype(F32)
    tall = up.shape[0]
    up[...] = total[:tall]
    down[...] = total[tall:]


def finish_kernel(me, got, qkv, out, gains, biases):
    total = got[0].astype(F32)
    for n in range(1, got.shape[0]):
        total = total + got[n].astype(F32)
    small, width = out.shape
    for part in range(3):
        qkv[:, part * width : (part + 1) * width] = total[part * small : (part + 1) * small]
    out[...] = total[3 * small : 4 * small]
    vec = pltpu.roll(total[4 * small :], width - me[0] * small, 1)[:, :small]
    gains[...] = vec[:2]
    biases[...] = vec[2:5]


def swap(block, axis, bit):
    size = lax.axis_size(axis)
    return lax.ppermute(block, axis, [(i, i ^ bit) for i in range(size)])


def steps_of(axis):
    return [(axis, 1 << k) for k in reversed(range(lax.axis_size(axis).bit_length() - 1))]


def z_groups():
    size = lax.axis_size("dp")
    return [[x + 2 * z for z in range(size // 2)] for x in range(2)]


def z_exchange(blocks):
    return lax.all_to_all(blocks, "dp", 0, 0, axis_index_groups=z_groups())


def after(value, other):
    return lax.optimization_barrier((value, other))[0]


def halves(held):
    half = held.shape[0] // 2
    return held[:half], held[half:].astype(BF16)


def fold_step(keep, send, axis, bit, past=None):
    got = swap(send, axis, bit)
    return keep + (got if past is None else after(got, past)).astype(F32)


def bit_reverse(index, count):
    out = 0 * index
    for k in range(count):
        out = out | (((index >> k) & 1) << (count - 1 - k))
    return out


def by_device(block, me):
    blocks = block[None]
    for axis, bit in steps_of("dp") + steps_of("tensor"):
        blocks = jnp.concatenate([blocks, swap(blocks, axis, bit)], 0)
    count = blocks.shape[0]
    order = jnp.arange(count, dtype=jnp.int32) ^ me
    return jnp.take(blocks, bit_reverse(order, count.bit_length() - 1), axis=0)


def other_pack(w_qkv, w_out, gains, biases, w_up, w_down, me):
    small, width = w_out.shape
    qkv = w_qkv.reshape(small, 3, width).transpose(1, 0, 2).reshape(3 * small, width)
    rows = jnp.concatenate([gains, biases], 0)
    place = jnp.zeros((8, width), BF16)
    place = lax.dynamic_update_slice(place, rows, (jnp.int32(0), me * small))
    return jnp.concatenate([qkv, w_out, place], 0), jnp.concatenate([w_up, w_down.T], 0)


def other_blocks(a, b, me, n_dp, n_t):
    a = by_device(a, me)
    b = by_device(b, me)
    width = a.shape[2]
    count = n_dp * n_t
    small = width // count
    big = width // (VDP * VT)
    mats = a[:, : 4 * small].reshape(count, 4, small, width).transpose(1, 0, 2, 3)
    mats = mats.reshape(4, VDP * VT, big, width).transpose(1, 0, 2, 3).reshape(VDP * VT, 4 * big, width)
    vec = jnp.sum(a[:, 4 * small :].astype(F32), 0).astype(BF16)
    vecs = jnp.concatenate([vec[None], jnp.zeros((VDP * VT - 1, 8, width), BF16)], 0)
    a = jnp.concatenate([mats, vecs], 1)
    tall = width // n_dp
    b = b.reshape(n_dp, VT, 2, tall, width).transpose(1, 2, 0, 3, 4)
    b = b.reshape(VT, 2, VDP, width // VDP, width).transpose(2, 0, 1, 3, 4)
    b = b.reshape(VDP * VT, 2 * (width // VDP), width)

    y_own = (me // 2) % 2

    def placed(blocks, spot):
        pairs = blocks.reshape((CHIPS, 2) + blocks.shape[1:])
        pairs = jnp.stack([pairs[m] for m in sorted(range(CHIPS), key=spot)], 0)
        pairs = jnp.where(y_own == 1, jnp.roll(pairs, VDP, 0), pairs)
        return pairs[:, 0], pairs[:, 1]

    return placed(a, grid_spot) + placed(b, spot)


def other_reduce(pair_a, pair_b, me, n_dp, n_t):
    count = n_dp * n_t
    y_own = (me // 2) % 2

    def whole(keep, send, place):
        pairs = jnp.stack([keep, send.astype(F32)], 1)
        pairs = jnp.stack([pairs[place(i)] for i in range(VDP)], 0)
        none = jnp.zeros_like(pairs)
        both = jnp.stack([jnp.where(y_own == y, pairs, none) for y in range(2)], 1)
        return both.reshape((VDP * VT,) + keep.shape[1:])

    def rows_of(blocks, parts):
        big = blocks.shape[1] // parts
        mats = blocks.reshape(VDP * VT, parts, big, -1).transpose(1, 0, 2, 3)
        mats = mats.reshape(parts, count, VDP * VT * big // count, -1).transpose(1, 0, 2, 3)
        return mats.reshape(count, -1, blocks.shape[2])

    def vec_of(blocks):
        picked = jnp.where(y_own == 0, blocks[0], 0.0)
        return jnp.broadcast_to(picked[None], (count,) + picked.shape)

    a, b = whole(*pair_a, lambda i: i % 2 * 4 + i // 2), whole(*pair_b, turn)
    width = a.shape[2]
    tall, high = width // n_dp, width // VDP
    cols = b.reshape(VDP, VT, 2, high, width).transpose(1, 2, 0, 3, 4)
    cols = cols.reshape(VT, 2, n_dp, tall, width).transpose(2, 0, 1, 3, 4)
    cols = cols.reshape(count, 2 * tall, width)
    a = jnp.concatenate([rows_of(a[:, :32], 4), vec_of(a[:, 32:])], 1)
    results = []
    for blocks in (a, cols):
        blocks = jnp.take(blocks, jnp.arange(count, dtype=jnp.int32) ^ me, axis=0)
        for axis, bit in reversed(steps_of("dp") + steps_of("tensor")):
            pairs = blocks.reshape((-1, 2) + blocks.shape[1:])
            got = swap(pairs[:, 1].astype(BF16), axis, bit)
            blocks = pairs[:, 0] + got.astype(F32)
        results.append(blocks[0])
    return results


def struct(shape, dtype):
    return jax.ShapeDtypeStruct(shape, dtype)


def call(kernel, name, args, outs, scratch=(), flops=0, limit=16, hbm_outs=True):
    args = [a if isinstance(a, tuple) else (a, pltpu.VMEM) for a in args]
    moved = sum(a.size * a.dtype.itemsize for a, _ in args)
    spaces = [pl.ANY if hbm_outs and isinstance(o, jax.ShapeDtypeStruct) else pltpu.VMEM for o in outs]
    return pl.pallas_call(
        kernel,
        name=name,
        out_shape=outs,
        in_specs=[pl.BlockSpec(memory_space=space) for _, space in args],
        out_specs=[pl.BlockSpec(memory_space=space) for space in spaces],
        scratch_shapes=list(scratch),
        compiler_params=pltpu.CompilerParams(vmem_limit_bytes=limit * MIB),
        cost_estimate=pl.CostEstimate(flops=flops, bytes_accessed=moved, transcendentals=0),
    )(*[a for a, _ in args])


def on_device(tokens, lengths, row_mask, cotangent, w_qkv, w_out, gains, biases, w_up, w_down):
    images, seq_len, width = tokens.shape
    n_dp, n_t = lax.axis_size("dp"), lax.axis_size("tensor")
    index = lax.axis_index("dp") * n_t + lax.axis_index("tensor")
    me = index.astype(jnp.int32).reshape(1)
    usual = (n_dp, n_t) == (VDP, VT)
    virt = me if usual else (index // 2 % 2 * 2).astype(jnp.int32).reshape(1)
    small = width // (n_dp * n_t)
    tall = width // n_dp
    own = images * seq_len // 2
    rows = own // WIN
    per = 4 if rows % 4 == 0 else 1
    smem = pltpu.SMEM
    weights = (w_qkv, w_out, gains, biases, w_up, w_down)
    token_mm = 2 * own * width
    hbm = pltpu.HBM

    def in_hbm(array):
        return (pltpu.with_memory_space_constraint(array, hbm), hbm)

    def fetch(me):
        return call(
            fetch_kernel,
            "fetch",
            [(me, smem), in_hbm(tokens.reshape(images * seq_len, width))],
            [
                pltpu.VMEM((own, width), BF16),
                pltpu.VMEM((own, width), F32),
                pltpu.VMEM((own, 1), F32),
            ],
            [pltpu.SemaphoreType.DMA(())],
            limit=4,
        )

    def fetch_turned(me, xhat):
        return call(
            turn_kernel,
            "turn",
            [(me, smem), in_hbm(cotangent.reshape(images * seq_len, width)), xhat],
            [
                pltpu.VMEM((own, width), BF16),
                pltpu.VMEM((width, own), BF16),
                pltpu.VMEM((width, own), BF16),
            ],
            [pltpu.SemaphoreType.DMA(())],
            limit=4,
        )

    if usual:
        weights = (w_qkv, w_out, gains, biases, w_up, w_down.T)
        pack_a, pack_b = call(
            pack_kernel,
            "pack",
            [(me, smem)] + [in_hbm(w) for w in weights],
            [
                pltpu.VMEM((n_dp // 2, 4 * small + 8, width), BF16),
                pltpu.VMEM((1, 2 * tall, width), BF16),
            ],
            [pltpu.VMEM(w.shape, BF16) for w in weights] + [pltpu.SemaphoreType.DMA((6,))],
        )
        x, xhat1, inv1 = fetch(after(me, pack_a))
        held_a = z_exchange(pack_a)
        b = after(pack_b, xhat1)
        b = jnp.concatenate([b, swap(b, "dp", 4)], 0)
        b = after(b, held_a)
        held_a = jnp.concatenate([held_a, after(swap(after(held_a, xhat1), "dp", 1), b)], 0)
        b = jnp.concatenate([b, swap(b, "dp", 2)], 0)
        b = after(b, held_a)
        cot, cot_t, xhat_t = fetch_turned(after(me, held_a), xhat1)
        held_a = jnp.concatenate([held_a, after(swap(held_a, "tensor", 2), (cot, b))], 0)
        b = jnp.concatenate([b, swap(b, "dp", 1)], 0)
        far_b = swap(b, "tensor", 2)
        got_a = swap(held_a, "tensor", 1)
        got_b = swap(after(b, held_a), "tensor", 1)
    else:
        held_a, got_a, held_b, got_b = other_blocks(*other_pack(*weights, index), index, n_dp, n_t)
        b, far_b = held_b[:VDP], held_b[VDP:]
        got_b, got_far = got_b[:VDP], got_b[VDP:]
        x, xhat1, inv1 = fetch(me)
        cot, cot_t, xhat_t = fetch_turned(me, xhat1)
    qkv, prob, o, x1, wqkv, wout, vec = call(
        functools.partial(attend_kernel, per),
        "attend",
        [(me, smem), (virt, smem), (lengths, smem), (row_mask, smem), x, xhat1, held_a, got_a],
        [
            pltpu.VMEM((own, 3 * width), BF16),
            pltpu.VMEM((rows * HEADS, WIN, WIN), BF16),
            pltpu.VMEM((own, width), BF16),
            pltpu.VMEM((own, width), F32),
            pltpu.VMEM((width, 3 * width), BF16),
            pltpu.VMEM((width, width), BF16),
            pltpu.VMEM((8, width), F32),
        ],
        flops=token_mm * (4 * width + 2 * WIN),
    )
    if usual:
        far_b = after(far_b, x1)
        got_b = after(got_b, far_b)
        got_far = swap(far_b, "tensor", 1)
    tall_b = 2 * (width // VDP)
    mats = [pltpu.VMEM((width, 2 * width), BF16)] * 2 + [pltpu.VMEM((2 * width, width), BF16)] * 2
    h2, xhat2, inv2, f, dh2, keep_b, send_b = call(
        functools.partial(hidden_near_kernel, per),
        "hidden_near",
        [(virt, smem), x1, cot, cot_t, vec, b, got_b],
        [
            pltpu.VMEM((own, width), BF16),
            pltpu.VMEM((own, width), F32),
            pltpu.VMEM((own, 1), F32),
            pltpu.VMEM((own, width), F32),
            pltpu.VMEM((own, width), F32),
            pltpu.VMEM((VDP, tall_b, width), F32),
            pltpu.VMEM((VDP, tall_b, width), BF16),
        ],
        [pltpu.VMEM((own, 2 * width), BF16)] * 2 + mats,
        token_mm * 12 * width,
    )
    y, dx1, g, gout, gvec = call(
        functools.partial(hidden_far_kernel, per),
        "hidden_far",
        [(virt, smem), cot, vec, far_b, got_far, h2, xhat2, inv2, f, dh2, o],
        [
            pltpu.VMEM((own, width), BF16),
            pltpu.VMEM((own, width), F32),
            pltpu.VMEM((own, width), BF16),
            pltpu.VMEM((width, width), F32),
            pltpu.VMEM((8, width), F32),
        ],
        mats,
        token_mm * 9 * width,
    )
    core, xbit, zlo, zhi = ("tensor", 1), ("dp", 1), ("dp", 2), ("dp", 4)
    if usual:
        held_b = fold_step(keep_b, send_b, *core, g)
        y = after(y, held_b)
    y_near = swap(y, "tensor", 1)
    dqkv, keep_a, send_a = call(
        functools.partial(back_kernel, per),
        "back",
        [(virt, smem), qkv, prob, g, xhat_t, wqkv, wout, vec, gout, gvec],
        [
            pltpu.VMEM((own, 3 * width), BF16),
            pltpu.VMEM((VDP, 40, width), F32),
            pltpu.VMEM((VDP, 40, width), BF16),
        ],
        [pltpu.VMEM((width, 3 * width), F32)],
        token_mm * (4 * width + 5 * WIN),
    )
    gx, gxb, layer_out = call(
        functools.partial(token_grad_kernel, per),
        "token_grad",
        [(me, smem), dqkv, wqkv, vec, xhat1, inv1, dx1, y, y_near],
        [
            pltpu.VMEM((own, width), F32),
            pltpu.VMEM((own, width), BF16),
            struct((images * seq_len, width), BF16),
        ],
        [pltpu.SemaphoreType.DMA((2,))],
        flops=token_mm * 3 * width,
    )
    layer_out = layer_out.reshape(images, seq_len, width)

    def place(gx_near):
        return call(
            functools.partial(place_kernel, per),
            "place",
            [(me, smem), gx, gx_near],
            [struct((images * seq_len, width), F32)],
            [pltpu.VMEM((own, width), F32), pltpu.SemaphoreType.DMA((rows // per + 1,))],
        )[0].reshape(images, seq_len, width)

    if usual:
        held_b = fold_step(*halves(held_b), *xbit)
        held_a = fold_step(keep_a, after(send_a, held_b), *core, gxb)
        grad_tokens = place(swap(after(gxb, held_a), "tensor", 1))
        keep, send = halves(held_b)
        held_b = fold_step(keep, after(send, held_a), *zlo)
        held_a = fold_step(*halves(held_a), *xbit)
        got = swap(halves(held_b)[1], *zhi)
        o_up, o_down = call(
            finish_hidden_kernel, "finish_hidden", [held_b, got], [struct((tall, width), F32)] * 2, limit=2, hbm_outs=False
        )
        got = z_exchange(held_a.astype(BF16))
        shapes = ((small, 3 * width), (small, width), (2, small), (3, small))
        o_qkv, o_out, o_gains, o_bias = call(
            finish_kernel,
            "finish",
            [(me, smem), after(got, grad_tokens)],
            [struct(shape, F32) for shape in shapes],
            limit=2,
            hbm_outs=False,
        )
    else:
        grad_tokens = place(swap(gxb, "tensor", 1))
        grad_a, grad_b = other_reduce((keep_a, send_a), (keep_b, send_b), index, n_dp, n_t)
        o_qkv = jnp.concatenate([grad_a[p * small : (p + 1) * small] for p in range(3)], 1)
        o_out = grad_a[3 * small : 4 * small]
        o_vec = lax.dynamic_slice_in_dim(grad_a[4 * small : 4 * small + 5], index * small, small, 1)
        o_gains, o_bias = o_vec[:2], o_vec[2:]
        o_up, o_down = grad_b[:tall], grad_b[tall:]
    return layer_out, grad_tokens, o_qkv, o_out, o_gains, o_bias, o_up, o_down.T


def solution(mesh):
    in_specs = (
        P("dp", None, None),
        P("dp"),
        P("dp", None),
        P("dp", None, None),
        P(("dp", "tensor"), None),
        P(("dp", "tensor"), None),
        P(None, ("dp", "tensor")),
        P(None, ("dp", "tensor")),
        P("dp", "tensor"),
        P("tensor", "dp"),
    )
    out_specs = (
        P("dp", None, None),
        P("dp", None, None),
        P(("dp", "tensor"), None),
        P(("dp", "tensor"), None),
        P(None, ("dp", "tensor")),
        P(None, ("dp", "tensor")),
        P("dp", "tensor"),
        P("tensor", "dp"),
    )
    return jax.shard_map(
        on_device, mesh=mesh, in_specs=in_specs, out_specs=out_specs, check_vma=False
    )
```

```python
import functools

import jax
import jax.numpy as jnp
from jax import lax
from jax.experimental import pallas as pl
from jax.experimental.pallas import tpu as pltpu
from jax.sharding import PartitionSpec as P

HEADS = 2
WIN = 96
F32 = jnp.float32
BF16 = jnp.bfloat16
VDP, VT = 8, 4
CHIPS = VDP * VT // 2
MIB = 1 << 20

NN = ((1,), (0,))
NT = ((1,), (1,))
TN = ((0,), (0,))


def dot(a, b, dims):
    return lax.dot_general(a, b, (dims, ((), ())), preferred_element_type=F32)


def turn(i):
    return ((i & 1) << 2) | (i & 2) | ((i & 4) >> 2)


def spot(m):
    return (m % 2) * VDP + turn(m // 2)


def turn(i):
    return ((i & 1) << 2) | (i & 2) | ((i & 4) >> 2)


def spot(m):
    return (m % 2) * VDP + turn(m // 2)


def fold(m):
    out = 0
    for place, bit in enumerate(REDUCE_BITS):
        shift = 3 - place
        out = out | (((m // bit) & 1) << shift)
    return out


def norm_parts(values):
    center = values - jnp.mean(values, -1, keepdims=True)
    inv = lax.rsqrt(jnp.mean(center * center, -1, keepdims=True) + 1e-05)
    return center * inv, inv


def norm_back(grad, xhat, inv, gain):
    scaled = grad * gain
    return inv * (
        scaled
        - jnp.mean(scaled, -1, keepdims=True)
        - xhat * jnp.mean(scaled * xhat, -1, keepdims=True)
    )


def gelu_both(u):
    c = 0.7978845608028654
    u2 = u * u
    t = jnp.tanh(u * (c + (c * 0.044715) * u2))
    half = 0.5 + 0.5 * t
    value = u * half
    slope = half + (value - value * half) * (2 * c + (6 * c * 0.044715) * u2)
    return value, slope


def pack_kernel(me, *refs):
    sources, tokens, (small_ref, big_ref, x_ref), held, sems = refs[:6], refs[6], refs[7:10], refs[10:16], refs[16]
    own = x_ref.shape[0]
    copies = [pltpu.make_async_copy(a, b, sems.at[n]) for n, (a, b) in enumerate(zip(sources, held))]
    mine = tokens.at[pl.ds(lax.rem(me[0], 2) * own, own)]
    copies.append(pltpu.make_async_copy(mine, x_ref, sems.at[6]))
    for copy in copies:
        copy.start()
    qkv, out, gains, biases, up, down = held
    small, width = out.shape
    tall = up.shape[0]
    lane = lax.broadcasted_iota(jnp.int32, (1, width), 1)
    mine = lane // small == me[0]
    for copy in copies[:6]:
        copy.wait()
    for part in range(3):
        small_ref[0, part * small : (part + 1) * small] = qkv[:, part * width : (part + 1) * width]
    small_ref[0, 3 * small : 4 * small] = out[...]
    rows = [gains[0:1], gains[1:2], biases[0:1], biases[1:2], biases[2:3]]
    vals = jnp.concatenate(rows + [jnp.zeros((3, small), BF16)], 0).astype(F32)
    wide = jnp.concatenate([vals] * (width // small), 1)
    small_ref[0, 4 * small : 4 * small + 8] = jnp.where(mine, wide, 0.0).astype(BF16)
    big_ref[0, :tall] = up[...]
    big_ref[0, tall:] = down[...]
    copies[6].wait()


def first_norm_kernel(x_ref, xhat_ref, inv_ref):
    own, width = x_ref.shape
    ones = jnp.full((width, width), 1.0 / width, BF16)
    for n in range(own // (2 * WIN)):
        part = slice(n * 2 * WIN, (n + 1) * 2 * WIN)
        x = x_ref[part]
        center = x.astype(F32) - dot(x, ones, NN)
        inv = lax.rsqrt(dot((center * center).astype(BF16), ones, NN) + 1e-05)
        xhat_ref[part] = (center * inv).astype(BF16)
        inv_ref[part] = inv[:, :1]


def turn_kernel(me, cot, xhat_ref, cot_ref, cot_t, xhat_t, sem):
    own = cot_ref.shape[0]
    copy = pltpu.make_async_copy(cot.at[pl.ds(lax.rem(me[0], 2) * own, own)], cot_ref, sem)
    copy.start()
    size = 256 if own % 256 == 0 else own
    for n in range(own // size):
        part = slice(n * size, (n + 1) * size)
        xhat_t[:, part] = xhat_ref[part].T
    copy.wait()
    for n in range(own // size):
        part = slice(n * size, (n + 1) * size)
        cot_t[:, part] = cot_ref[part].T


def attend_kernel(
    per, me, virt, lens, live, x_ref, xhat_ref, held, got,
    qkv_ref, prob_ref, o_ref, x1_ref, wqkv, wout, vec,
):
    tokens, width = x_ref.shape
    rows = tokens // WIN
    hs = width // HEADS
    here = spot(virt[0] // 2) % VDP
    y_own = (virt[0] // 2) % 2
    first = virt[0] % 2 == 0
    total = jnp.zeros((8, width), F32)
    for m in range(CHIPS):
        k = spot(m) ^ (here + y_own * VDP)
        a = held[k].astype(F32)
        b = got[k].astype(F32)
        even = jnp.where(first, a, b)
        odd = jnp.where(first, b, a)
        for part in range(3):
            both = jnp.concatenate([even[part * 8 : part * 8 + 8], odd[part * 8 : part * 8 + 8]], 0)
            wqkv[m * 16 : m * 16 + 16, part * width : (part + 1) * width] = both.astype(BF16)
        both = jnp.concatenate([even[24:32], odd[24:32]], 0)
        wout[m * 16 : m * 16 + 16] = both.astype(BF16)
        total = total + a[32:40] + b[32:40]
    vec[...] = total
    scale = hs**-0.5
    ii = lax.broadcasted_iota(jnp.int32, (WIN, WIN), 0)
    jj = lax.broadcasted_iota(jnp.int32, (WIN, WIN), 1)
    same = ii == jj
    image_rows = live.shape[1]
    base = lax.rem(me[0], 2) * rows

    def enter(c):
        part = slice(c * per * WIN, (c + 1) * per * WIN)
        h1 = (xhat_ref[part] * total[0:1] + total[2:3]).astype(BF16)
        qkv = dot(h1, wqkv[...], NN).astype(BF16)
        qkv_ref[part] = qkv
        scores = []
        for r in range(per):
            at = slice(r * WIN, (r + 1) * WIN)
            for h in range(HEADS):
                q = qkv[at, h * hs : (h + 1) * hs]
                k = qkv[at, width + h * hs : width + (h + 1) * hs]
                scores.append(dot(q, k, NT))
        return qkv, scores

    ahead = enter(0)
    for c in range(rows // per):
        qkv, scores = ahead
        if c + 1 < rows // per:
            ahead = enter(c + 1)
        part = slice(c * per * WIN, (c + 1) * per * WIN)
        probs = []
        for r in range(per):
            row = base + c * per + r
            image = row // image_rows
            inside = row - image * image_rows
            reach = jnp.where(live[image, inside] == 1, lens[image] - inside * WIN, 0)
            allowed = same | (jj < jnp.minimum(ii, reach))
            for h in range(HEADS):
                s = jnp.where(allowed, scores[r * HEADS + h], -1e30)
                e = jnp.exp((s - jnp.max(s, -1, keepdims=True)) * scale)
                probs.append((e * (1.0 / jnp.sum(e, -1, keepdims=True))).astype(BF16))
        mixed = []
        for r in range(per):
            at = slice(r * WIN, (r + 1) * WIN)
            heads = []
            for h in range(HEADS):
                v = qkv[at, 2 * width + h * hs : 2 * width + (h + 1) * hs]
                heads.append(dot(probs[r * HEADS + h], v, NN).astype(BF16))
            mixed.append(jnp.concatenate(heads, 1))
        o = jnp.concatenate(mixed, 0)
        for n, p in enumerate(probs):
            prob_ref[c * per * HEADS + n] = p
        o_ref[part] = o
        x1_ref[part] = x_ref[part].astype(F32) + dot(o, wout[...], NN)


def join(virt, blocks, n, up, down_t):
    tall = blocks.shape[1] // 2
    width = up.shape[0]
    here = turn(virt[0] // 4)
    for i in range(VDP):
        k = turn(i) ^ here
        at = slice(i * tall, (i + 1) * tall)
        cols = slice(n * width, (n + 1) * width)
        up[at, cols] = blocks[k, :tall]
        down_t[at, cols] = blocks[k, tall:]


def hidden_units(h2, dyb, up, down_t):
    u = dot(h2, up[...], NN).astype(BF16)
    da = dot(dyb, down_t[...], NN).astype(BF16)
    a, slope = gelu_both(u)
    return a, da * slope


def hidden_near_kernel(
    per, virt, x1_ref, cot_ref, cot_t, vec, own, got,
    h2_ref, xhat_ref, inv_ref, f_ref, dh2_ref, keep, send,
    a_ref, du_ref, up, down_t, up_t, down,
):
    tokens, width = x1_ref.shape
    size = per * WIN
    join(virt, own, 0, up, down_t)
    join(virt, got, 1, up, down_t)
    up_t[...] = up[...].T
    down[...] = down_t[...].T
    for c in range(tokens // size):
        part = slice(c * size, (c + 1) * size)
        x1 = x1_ref[part]
        xhat, inv = norm_parts(x1)
        xhat_ref[part] = xhat.astype(BF16)
        inv_ref[part] = inv
        h2 = (xhat * vec[1:2] + vec[3:4]).astype(BF16)
        h2_ref[part] = h2
        a, du = hidden_units(h2, cot_ref[part], up, down_t)
        a_ref[part] = a
        du_ref[part] = du
        f_ref[part] = dot(a, down[...], NN).astype(BF16)
        dh2_ref[part] = dot(du, up_t[...], NN).astype(BF16)
    gdown = dot(cot_t[...], a_ref[...], NN)
    gup = dot(h2_ref[...], du_ref[...], TN)
    tall = width // VDP
    here = turn(virt[0] // 4)
    for i in range(VDP):
        at = slice(i * tall, (i + 1) * tall)
        k = turn(i) ^ here
        keep[k, :tall] = gup[at, :width]
        keep[k, tall:] = gdown[at, :width]
        send[k, :tall] = gup[at, width:].astype(BF16)
        send[k, tall:] = gdown[at, width:].astype(BF16)


def hidden_far_kernel(
    per, virt, x1_ref, cot_ref, vec, own, got, h2_ref, xhat_ref, inv_ref, f_ref, dh2_ref, o_ref,
    y_ref, g_ref, gout, gvec,
    up, down_t, up_t, down,
):
    tokens, width = h2_ref.shape
    size = per * WIN
    join(virt, own, 0, up, down_t)
    join(virt, got, 1, up, down_t)
    up_t[...] = up[...].T
    down[...] = down_t[...].T
    sums = [jnp.zeros((1, width), F32)] * 3
    for c in range(tokens // size):
        part = slice(c * size, (c + 1) * size)
        a, du = hidden_units(h2_ref[part], cot_ref[part], up, down_t)
        f = f_ref[part].astype(F32) + dot(a, down[...], NN)
        y_ref[part] = (x1_ref[part] + vec[4:5] + f).astype(BF16)
        dh2 = dh2_ref[part].astype(F32) + dot(du, up_t[...], NN)
        dy = cot_ref[part].astype(F32)
        xhat = xhat_ref[part].astype(F32)
        dx1 = dy + norm_back(dh2, xhat, inv_ref[part], vec[1:2])
        g_ref[part] = dx1.astype(BF16)
        for n, term in enumerate((dh2 * xhat, dh2, dy)):
            sums[n] = sums[n] + jnp.sum(term, 0, keepdims=True)
    gout[...] = dot(o_ref[...], g_ref[...], TN)
    zero = jnp.zeros((1, width), F32)
    gvec[...] = jnp.concatenate([zero, sums[0], zero, sums[1], sums[2], zero, zero, zero], 0)


def own_rows(virt, i, other):
    core = virt[0] % 2
    core = 1 - core if other else core
    return pl.ds(pl.multiple_of(i * 32 + ((virt[0] // 2) % 2) * 16 + core * 8, 8), 8)


def back_kernel(
    per, virt, qkv_ref, prob_ref, g_ref, xhat_t, wqkv, wout, vec, gout, gvec,
    dqkv, keep, send,
    gqkv,
):
    tokens, width = g_ref.shape
    hs = width // HEADS
    scale = hs**-0.5
    every = [(r, h) for r in range(tokens // WIN) for h in range(HEADS)]
    groups = [every[n : n + 2 * per] for n in range(0, len(every), 2 * per)]

    def piece(ref, r, h, part=0):
        return ref[r * WIN : (r + 1) * WIN, part * width + h * hs : part * width + (h + 1) * hs]

    def enter(pairs):
        r = pairs[0][0]
        do = dot(g_ref[r * WIN : (r + per) * WIN], wout[...], NT).astype(BF16)
        dos = [do[(n - r) * WIN : (n - r + 1) * WIN, h * hs : (h + 1) * hs] for n, h in pairs]
        probs = [prob_ref[r * HEADS + h] for r, h in pairs]
        dps = [dot(a, piece(qkv_ref, r, h, 2), NT) for a, (r, h) in zip(dos, pairs)]
        dvs = [dot(p, a, TN).astype(BF16) for p, a in zip(probs, dos)]
        return probs, dps, dvs

    ahead = enter(groups[0])
    for place, pairs in enumerate(groups):
        probs, dps, dvs = ahead
        if place + 1 < len(groups):
            ahead = enter(groups[place + 1])
        dss = []
        for p, dp in zip(probs, dps):
            pf = p.astype(F32)
            ds = pf * (dp - jnp.sum(dp * pf, -1, keepdims=True)) * scale
            dss.append(ds.astype(BF16))
        dqs = [dot(ds, piece(qkv_ref, r, h, 1), NN).astype(BF16) for ds, (r, h) in zip(dss, pairs)]
        dks = [dot(ds, piece(qkv_ref, r, h, 0), TN).astype(BF16) for ds, (r, h) in zip(dss, pairs)]
        for n, (r, h) in enumerate(pairs):
            for part, values in enumerate((dqs, dks, dvs)):
                at = slice(part * width + h * hs, part * width + (h + 1) * hs)
                dqkv[r * WIN : (r + 1) * WIN, at] = values[n]
    grad = dot(xhat_t[...], dqkv[...], NN)
    total = jnp.zeros((1, 3 * width), F32)
    for r in range(tokens // WIN):
        total = total + jnp.sum(dqkv[r * WIN : (r + 1) * WIN].astype(F32), 0, keepdims=True)
    w = wqkv[...].astype(F32)
    cols = jnp.concatenate([
        jnp.broadcast_to(jnp.sum(w * grad, -1, keepdims=True), (width, 64)),
        jnp.broadcast_to(jnp.sum(w * total, -1, keepdims=True), (width, 64)),
    ], 1)
    lines = cols.T
    gain, from_total = lines[0:1], lines[64:65]
    vec_t = vec[...].T
    gqkv[...] = grad * vec_t[:, 0:1] + total * vec_t[:, 2:3]
    rest = gvec[...]
    sums = jnp.concatenate([gain, rest[1:2], from_total, rest[3:]], 0)
    here = turn(virt[0] // 4)
    for i in range(VDP):
        k = turn(i) ^ here
        mine, other = own_rows(virt, i, 0), own_rows(virt, i, 1)
        theirs = []
        for part in range(3):
            at = slice(part * width, (part + 1) * width)
            keep[k, part * 8 : part * 8 + 8] = gqkv[mine, at]
            theirs.append(gqkv[other, at])
        keep[k, 24:32] = gout[mine]
        keep[k, 32:] = sums
        send[k] = jnp.concatenate(theirs + [gout[other], sums], 0).astype(BF16)


def token_grad_kernel(per, me, dqkv, wqkv, vec, xhat_ref, inv_ref, g_ref, y, y_near, gx, gxb, out, sems):
    own = dqkv.shape[0]
    size = per * WIN
    copies = []
    for n, source in enumerate((y, y_near)):
        at = pl.ds((lax.rem(me[0], 2) ^ n) * own, own)
        copies.append(pltpu.make_async_copy(source, out.at[at], sems.at[n]))
        copies[-1].start()
    ahead = dot(dqkv[:size], wqkv[...], NT)
    for c in range(own // size):
        part = slice(c * size, (c + 1) * size)
        dh1 = ahead
        if (c + 1) * size < own:
            ahead = dot(dqkv[(c + 1) * size : (c + 2) * size], wqkv[...], NT)
        xhat = xhat_ref[part].astype(F32)
        values = g_ref[part].astype(F32) + norm_back(dh1, xhat, inv_ref[part], vec[0:1])
        gx[part] = values
        gxb[part] = values.astype(BF16)
    for copy in copies:
        copy.wait()


def place_kernel(per, me, mine, theirs, out, wide, sems):
    own = theirs.shape[0]
    size = per * WIN
    here = lax.rem(me[0], 2) * own
    copies = [pltpu.make_async_copy(mine, out.at[pl.ds(here, own)], sems.at[own // size])]
    copies[0].start()
    for c in range(own // size):
        part = pl.ds(c * size, size)
        wide[part] = theirs[part].astype(F32)
        at = pl.ds(own - here + c * size, size)
        copies.append(pltpu.make_async_copy(wide.at[part], out.at[at], sems.at[c]))
        copies[-1].start()
    for copy in copies:
        copy.wait()


def finish_hidden_kernel(keep, got, up, down):
    total = keep[0] + got[0].astype(F32)
    tall = up.shape[0]
    up[...] = total[:tall]
    down[...] = total[tall:]


def finish_kernel(me, keep, got, qkv, out, gains, biases):
    total = keep[0] + got[0].astype(F32)
    small, width = out.shape
    for part in range(3):
        qkv[:, part * width : (part + 1) * width] = total[part * small : (part + 1) * small]
    out[...] = total[3 * small : 4 * small]
    vec = pltpu.roll(total[4 * small :], width - me[0] * small, 1)[:, :small]
    gains[...] = vec[:2]
    biases[...] = vec[2:5]


def swap(block, axis, bit):
    size = lax.axis_size(axis)
    return lax.ppermute(block, axis, [(i, i ^ bit) for i in range(size)])


def steps_of(axis):
    return [(axis, 1 << k) for k in reversed(range(lax.axis_size(axis).bit_length() - 1))]


def after(value, other):
    return lax.optimization_barrier((value, other))[0]


def halves(held):
    half = held.shape[0] // 2
    return held[:half], held[half:].astype(BF16)


def fold_step(keep, send, axis, bit, past=None):
    got = swap(send, axis, bit)
    return keep + (got if past is None else after(got, past)).astype(F32)


def bit_reverse(index, count):
    out = 0 * index
    for k in range(count):
        out = out | (((index >> k) & 1) << (count - 1 - k))
    return out


def by_device(block, me):
    blocks = block[None]
    for axis, bit in steps_of("dp") + steps_of("tensor"):
        blocks = jnp.concatenate([blocks, swap(blocks, axis, bit)], 0)
    count = blocks.shape[0]
    order = jnp.arange(count, dtype=jnp.int32) ^ me
    return jnp.take(blocks, bit_reverse(order, count.bit_length() - 1), axis=0)


def other_pack(w_qkv, w_out, gains, biases, w_up, w_down, me):
    small, width = w_out.shape
    qkv = w_qkv.reshape(small, 3, width).transpose(1, 0, 2).reshape(3 * small, width)
    rows = jnp.concatenate([gains, biases], 0)
    place = jnp.zeros((8, width), BF16)
    place = lax.dynamic_update_slice(place, rows, (jnp.int32(0), me * small))
    return jnp.concatenate([qkv, w_out, place], 0), jnp.concatenate([w_up, w_down.T], 0)


def other_blocks(a, b, me, n_dp, n_t):
    a = by_device(a, me)
    b = by_device(b, me)
    width = a.shape[2]
    count = n_dp * n_t
    small = width // count
    big = width // (VDP * VT)
    mats = a[:, : 4 * small].reshape(count, 4, small, width).transpose(1, 0, 2, 3)
    mats = mats.reshape(4, VDP * VT, big, width).transpose(1, 0, 2, 3).reshape(VDP * VT, 4 * big, width)
    vec = jnp.sum(a[:, 4 * small :].astype(F32), 0).astype(BF16)
    vecs = jnp.concatenate([vec[None], jnp.zeros((VDP * VT - 1, 8, width), BF16)], 0)
    a = jnp.concatenate([mats, vecs], 1)
    tall = width // n_dp
    b = b.reshape(n_dp, VT, 2, tall, width).transpose(1, 2, 0, 3, 4)
    b = b.reshape(VT, 2, VDP, width // VDP, width).transpose(2, 0, 1, 3, 4)
    b = b.reshape(VDP * VT, 2 * (width // VDP), width)

    y_own = (me // 2) % 2

    def placed(blocks):
        pairs = blocks.reshape((CHIPS, 2) + blocks.shape[1:])
        pairs = jnp.stack([pairs[m] for m in sorted(range(CHIPS), key=spot)], 0)
        pairs = jnp.where(y_own == 1, jnp.roll(pairs, VDP, 0), pairs)
        return pairs[:, 0], pairs[:, 1]

    return placed(a) + placed(b)


def other_reduce(pair_a, pair_b, me, n_dp, n_t):
    count = n_dp * n_t
    y_own = (me // 2) % 2

    def whole(keep, send):
        pairs = jnp.stack([keep, send.astype(F32)], 1)
        pairs = jnp.stack([pairs[turn(i)] for i in range(VDP)], 0)
        none = jnp.zeros_like(pairs)
        both = jnp.stack([jnp.where(y_own == y, pairs, none) for y in range(2)], 1)
        return both.reshape((VDP * VT,) + keep.shape[1:])

    def rows_of(blocks, parts):
        big = blocks.shape[1] // parts
        mats = blocks.reshape(VDP * VT, parts, big, -1).transpose(1, 0, 2, 3)
        mats = mats.reshape(parts, count, VDP * VT * big // count, -1).transpose(1, 0, 2, 3)
        return mats.reshape(count, -1, blocks.shape[2])

    def vec_of(blocks):
        picked = jnp.where(y_own == 0, blocks[0], 0.0)
        return jnp.broadcast_to(picked[None], (count,) + picked.shape)

    a, b = whole(*pair_a), whole(*pair_b)
    width = a.shape[2]
    tall, high = width // n_dp, width // VDP
    cols = b.reshape(VDP, VT, 2, high, width).transpose(1, 2, 0, 3, 4)
    cols = cols.reshape(VT, 2, n_dp, tall, width).transpose(2, 0, 1, 3, 4)
    cols = cols.reshape(count, 2 * tall, width)
    a = jnp.concatenate([rows_of(a[:, :32], 4), vec_of(a[:, 32:])], 1)
    results = []
    for blocks in (a, cols):
        blocks = jnp.take(blocks, jnp.arange(count, dtype=jnp.int32) ^ me, axis=0)
        for axis, bit in reversed(steps_of("dp") + steps_of("tensor")):
            pairs = blocks.reshape((-1, 2) + blocks.shape[1:])
            got = swap(pairs[:, 1].astype(BF16), axis, bit)
            blocks = pairs[:, 0] + got.astype(F32)
        results.append(blocks[0])
    return results


def struct(shape, dtype):
    return jax.ShapeDtypeStruct(shape, dtype)


def call(kernel, name, args, outs, scratch=(), flops=0, limit=16, hbm_outs=True):
    args = [a if isinstance(a, tuple) else (a, pltpu.VMEM) for a in args]
    moved = sum(a.size * a.dtype.itemsize for a, _ in args)
    spaces = [pl.ANY if hbm_outs and isinstance(o, jax.ShapeDtypeStruct) else pltpu.VMEM for o in outs]
    return pl.pallas_call(
        kernel,
        name=name,
        out_shape=outs,
        in_specs=[pl.BlockSpec(memory_space=space) for _, space in args],
        out_specs=[pl.BlockSpec(memory_space=space) for space in spaces],
        scratch_shapes=list(scratch),
        compiler_params=pltpu.CompilerParams(vmem_limit_bytes=limit * MIB),
        cost_estimate=pl.CostEstimate(flops=flops, bytes_accessed=moved, transcendentals=0),
    )(*[a for a, _ in args])


def on_device(tokens, lengths, row_mask, cotangent, w_qkv, w_out, gains, biases, w_up, w_down):
    images, seq_len, width = tokens.shape
    n_dp, n_t = lax.axis_size("dp"), lax.axis_size("tensor")
    index = lax.axis_index("dp") * n_t + lax.axis_index("tensor")
    me = index.astype(jnp.int32).reshape(1)
    usual = (n_dp, n_t) == (VDP, VT)
    virt = me if usual else (index // 2 % 2 * 2).astype(jnp.int32).reshape(1)
    small = width // (n_dp * n_t)
    tall = width // n_dp
    own = images * seq_len // 2
    rows = own // WIN
    per = 4 if rows % 4 == 0 else 1
    smem = pltpu.SMEM
    weights = (w_qkv, w_out, gains, biases, w_up, w_down)
    token_mm = 2 * own * width
    hbm = pltpu.HBM

    def in_hbm(array):
        return (pltpu.with_memory_space_constraint(array, hbm), hbm)

    flat = tokens.reshape(images * seq_len, width)

    def first_norm(x):
        return call(
            first_norm_kernel,
            "first_norm",
            [x],
            [pltpu.VMEM((own, width), BF16), pltpu.VMEM((own, 1), F32)],
            limit=4,
        )

    def fetch_turned(me, xhat):
        return call(
            turn_kernel,
            "turn",
            [(me, smem), in_hbm(cotangent.reshape(images * seq_len, width)), xhat],
            [
                pltpu.VMEM((own, width), BF16),
                pltpu.VMEM((width, own), BF16),
                pltpu.VMEM((width, own), BF16),
            ],
            [pltpu.SemaphoreType.DMA(())],
            limit=4,
        )

    if usual:
        weights = (w_qkv, w_out, gains, biases, w_up, w_down.T)
        pack_a, pack_b, x = call(
            pack_kernel,
            "pack",
            [(me, smem)] + [in_hbm(w) for w in weights] + [in_hbm(flat)],
            [
                pltpu.VMEM((1, 4 * small + 8, width), BF16),
                pltpu.VMEM((1, 2 * tall, width), BF16),
                pltpu.VMEM((own, width), BF16),
            ],
            [pltpu.VMEM(w.shape, BF16) for w in weights] + [pltpu.SemaphoreType.DMA((7,))],
        )
        held_a, b = pack_a, pack_b
        xhat1, inv1 = first_norm(x)
        for n, (axis, bit) in enumerate(steps_of("dp")):
            got = swap(held_a, axis, bit)
            if n:
                got = after(got, b)
            held_a = jnp.concatenate([held_a, got], 0)
            b = jnp.concatenate([b, swap(b, axis, bit)], 0)
            held_a, b = (after(held_a, xhat1), b) if n == 0 else (held_a, b)
            b = after(b, held_a)
        cot, cot_t, xhat_t = fetch_turned(after(me, held_a), xhat1)
        held_a = jnp.concatenate([held_a, after(swap(held_a, "tensor", 2), (cot, b))], 0)
        far_b = swap(b, "tensor", 2)
        got_a = swap(held_a, "tensor", 1)
        got_b = swap(after(b, held_a), "tensor", 1)
    else:
        held_a, got_a, held_b, got_b = other_blocks(*other_pack(*weights, index), index, n_dp, n_t)
        b, far_b = held_b[:VDP], held_b[VDP:]
        got_b, got_far = got_b[:VDP], got_b[VDP:]
        x = lax.dynamic_slice_in_dim(flat, index % 2 * own, own, 0)
        xhat1, inv1 = first_norm(x)
        cot, cot_t, xhat_t = fetch_turned(me, xhat1)
    qkv, prob, o, x1, wqkv, wout, vec = call(
        functools.partial(attend_kernel, per),
        "attend",
        [(me, smem), (virt, smem), (lengths, smem), (row_mask, smem), x, xhat1, held_a, got_a],
        [
            pltpu.VMEM((own, 3 * width), BF16),
            pltpu.VMEM((rows * HEADS, WIN, WIN), BF16),
            pltpu.VMEM((own, width), BF16),
            pltpu.VMEM((own, width), F32),
            pltpu.VMEM((width, 3 * width), BF16),
            pltpu.VMEM((width, width), BF16),
            pltpu.VMEM((8, width), F32),
        ],
        flops=token_mm * (4 * width + 2 * WIN),
    )
    if usual:
        far_b = after(far_b, x1)
        got_b = after(got_b, far_b)
        got_far = swap(far_b, "tensor", 1)
    tall_b = 2 * (width // VDP)
    mats = [pltpu.VMEM((width, 2 * width), BF16)] * 2 + [pltpu.VMEM((2 * width, width), BF16)] * 2
    h2, xhat2, inv2, f, dh2, keep_b, send_b = call(
        functools.partial(hidden_near_kernel, per),
        "hidden_near",
        [(virt, smem), x1, cot, cot_t, vec, b, got_b],
        [
            pltpu.VMEM((own, width), BF16),
            pltpu.VMEM((own, width), BF16),
            pltpu.VMEM((own, 1), F32),
            pltpu.VMEM((own, width), BF16),
            pltpu.VMEM((own, width), BF16),
            pltpu.VMEM((VDP, tall_b, width), F32),
            pltpu.VMEM((VDP, tall_b, width), BF16),
        ],
        [pltpu.VMEM((own, 2 * width), BF16)] * 2 + mats,
        token_mm * 12 * width,
    )
    y, g, gout, gvec = call(
        functools.partial(hidden_far_kernel, per),
        "hidden_far",
        [(virt, smem), x1, cot, vec, far_b, got_far, h2, xhat2, inv2, f, dh2, o],
        [
            pltpu.VMEM((own, width), BF16),
            pltpu.VMEM((own, width), BF16),
            pltpu.VMEM((width, width), F32),
            pltpu.VMEM((8, width), F32),
        ],
        mats,
        token_mm * 9 * width,
    )
    core, xbit, zlo, zhi = ("tensor", 1), ("dp", 1), ("dp", 2), ("dp", 4)
    if usual:
        held_b = fold_step(keep_b, send_b, *core, g)
        y = after(y, held_b)
    y_near = swap(y, "tensor", 1)
    dqkv, keep_a, send_a = call(
        functools.partial(back_kernel, per),
        "back",
        [(virt, smem), qkv, prob, g, xhat_t, wqkv, wout, vec, gout, gvec],
        [
            pltpu.VMEM((own, 3 * width), BF16),
            pltpu.VMEM((VDP, 40, width), F32),
            pltpu.VMEM((VDP, 40, width), BF16),
        ],
        [pltpu.VMEM((width, 3 * width), F32)],
        token_mm * (4 * width + 5 * WIN),
    )
    gx, gxb, layer_out = call(
        functools.partial(token_grad_kernel, per),
        "token_grad",
        [(me, smem), dqkv, wqkv, vec, xhat1, inv1, g, y, y_near],
        [
            pltpu.VMEM((own, width), F32),
            pltpu.VMEM((own, width), BF16),
            struct((images * seq_len, width), BF16),
        ],
        [pltpu.SemaphoreType.DMA((2,))],
        flops=token_mm * 3 * width,
    )
    layer_out = layer_out.reshape(images, seq_len, width)

    def place(gx_near):
        return call(
            functools.partial(place_kernel, per),
            "place",
            [(me, smem), gx, gx_near],
            [struct((images * seq_len, width), F32)],
            [pltpu.VMEM((own, width), F32), pltpu.SemaphoreType.DMA((rows // per + 1,))],
        )[0].reshape(images, seq_len, width)

    if usual:
        held_b = fold_step(*halves(held_b), *xbit)
        held_a = fold_step(keep_a, after(send_a, held_b), *core, gxb)
        grad_tokens = place(swap(after(gxb, held_a), "tensor", 1))
        keep, send = halves(held_b)
        held_b = fold_step(keep, after(send, held_a), *zlo)
        held_a = fold_step(*halves(held_a), *xbit)
        held_a = fold_step(*halves(held_a), *zlo, grad_tokens)
        got = swap(halves(held_b)[1], *zhi)
        o_up, o_down = call(
            finish_hidden_kernel, "finish_hidden", [held_b, got], [struct((tall, width), F32)] * 2, limit=2, hbm_outs=False
        )
        got = swap(halves(held_a)[1], *zhi)
        shapes = ((small, 3 * width), (small, width), (2, small), (3, small))
        o_qkv, o_out, o_gains, o_bias = call(
            finish_kernel,
            "finish",
            [(me, smem), held_a, got],
            [struct(shape, F32) for shape in shapes],
            limit=2,
            hbm_outs=False,
        )
    else:
        grad_tokens = place(swap(gxb, "tensor", 1))
        grad_a, grad_b = other_reduce((keep_a, send_a), (keep_b, send_b), index, n_dp, n_t)
        o_qkv = jnp.concatenate([grad_a[p * small : (p + 1) * small] for p in range(3)], 1)
        o_out = grad_a[3 * small : 4 * small]
        o_vec = lax.dynamic_slice_in_dim(grad_a[4 * small : 4 * small + 5], index * small, small, 1)
        o_gains, o_bias = o_vec[:2], o_vec[2:]
        o_up, o_down = grad_b[:tall], grad_b[tall:]
    return layer_out, grad_tokens, o_qkv, o_out, o_gains, o_bias, o_up, o_down.T


def solution(mesh):
    in_specs = (
        P("dp", None, None),
        P("dp"),
        P("dp", None),
        P("dp", None, None),
        P(("dp", "tensor"), None),
        P(("dp", "tensor"), None),
        P(None, ("dp", "tensor")),
        P(None, ("dp", "tensor")),
        P("dp", "tensor"),
        P("tensor", "dp"),
    )
    out_specs = (
        P("dp", None, None),
        P("dp", None, None),
        P(("dp", "tensor"), None),
        P(("dp", "tensor"), None),
        P(None, ("dp", "tensor")),
        P(None, ("dp", "tensor")),
        P("dp", "tensor"),
        P("tensor", "dp"),
    )
    return jax.shard_map(
        on_device, mesh=mesh, in_specs=in_specs, out_specs=out_specs, check_vma=False
    )
```

```python
import functools

import jax
import jax.numpy as jnp
from jax import lax
from jax.experimental import pallas as pl
from jax.experimental.pallas import tpu as pltpu
from jax.sharding import PartitionSpec as P

HEADS = 2
WIN = 96
F32 = jnp.float32
BF16 = jnp.bfloat16
VDP, VT = 8, 4
CHIPS = VDP * VT // 2
MIB = 1 << 20

NN = ((1,), (0,))
NT = ((1,), (1,))
TN = ((0,), (0,))


def dot(a, b, dims):
    return lax.dot_general(a, b, (dims, ((), ())), preferred_element_type=F32)


def turn(i):
    return ((i & 1) << 2) | (i & 2) | ((i & 4) >> 2)


def spot(m):
    return (m % 2) * VDP + turn(m // 2)


def turn(i):
    return ((i & 1) << 2) | (i & 2) | ((i & 4) >> 2)


def spot(m):
    return (m % 2) * VDP + turn(m // 2)


def fold(m):
    out = 0
    for place, bit in enumerate(REDUCE_BITS):
        shift = 3 - place
        out = out | (((m // bit) & 1) << shift)
    return out


def norm_parts(values):
    center = values - jnp.mean(values, -1, keepdims=True)
    inv = lax.rsqrt(jnp.mean(center * center, -1, keepdims=True) + 1e-05)
    return center * inv, inv


def norm_back(grad, xhat, inv, gain):
    scaled = grad * gain
    return inv * (
        scaled
        - jnp.mean(scaled, -1, keepdims=True)
        - xhat * jnp.mean(scaled * xhat, -1, keepdims=True)
    )


def gelu_both(u):
    c = 0.7978845608028654
    u2 = u * u
    t = jnp.tanh(u * (c + (c * 0.044715) * u2))
    half = 0.5 + 0.5 * t
    value = u * half
    slope = half + (value - value * half) * (2 * c + (6 * c * 0.044715) * u2)
    return value, slope


def pack_kernel(me, *refs):
    sources, tokens, (small_ref, big_ref, x_ref), held, sems = refs[:6], refs[6], refs[7:10], refs[10:16], refs[16]
    own = x_ref.shape[0]
    copies = [pltpu.make_async_copy(a, b, sems.at[n]) for n, (a, b) in enumerate(zip(sources, held))]
    mine = tokens.at[pl.ds(lax.rem(me[0], 2) * own, own)]
    copies.append(pltpu.make_async_copy(mine, x_ref, sems.at[6]))
    for copy in copies:
        copy.start()
    qkv, out, gains, biases, up, down = held
    small, width = out.shape
    tall = up.shape[0]
    lane = lax.broadcasted_iota(jnp.int32, (1, width), 1)
    mine = lane // small == me[0]
    for copy in copies[:6]:
        copy.wait()
    for part in range(3):
        small_ref[0, part * small : (part + 1) * small] = qkv[:, part * width : (part + 1) * width]
    small_ref[0, 3 * small : 4 * small] = out[...]
    rows = [gains[0:1], gains[1:2], biases[0:1], biases[1:2], biases[2:3]]
    vals = jnp.concatenate(rows + [jnp.zeros((3, small), BF16)], 0).astype(F32)
    wide = jnp.concatenate([vals] * (width // small), 1)
    small_ref[0, 4 * small : 4 * small + 8] = jnp.where(mine, wide, 0.0).astype(BF16)
    big_ref[0, :tall] = up[...]
    big_ref[0, tall:] = down[...]
    copies[6].wait()


def first_norm_kernel(x_ref, xhat_ref, inv_ref):
    own, width = x_ref.shape
    ones = jnp.full((width, width), 1.0 / width, BF16)
    for n in range(own // (2 * WIN)):
        part = slice(n * 2 * WIN, (n + 1) * 2 * WIN)
        x = x_ref[part]
        center = x.astype(F32) - dot(x, ones, NN)
        inv = lax.rsqrt(dot((center * center).astype(BF16), ones, NN) + 1e-05)
        xhat_ref[part] = center * inv
        inv_ref[part] = inv[:, :1]


def turn_kernel(me, cot, xhat_ref, cot_ref, cot_t, xhat_t, sem):
    own = cot_ref.shape[0]
    copy = pltpu.make_async_copy(cot.at[pl.ds(lax.rem(me[0], 2) * own, own)], cot_ref, sem)
    copy.start()
    size = 256 if own % 256 == 0 else own
    for n in range(own // size):
        part = slice(n * size, (n + 1) * size)
        xhat_t[:, part] = xhat_ref[part].astype(BF16).T
    copy.wait()
    for n in range(own // size):
        part = slice(n * size, (n + 1) * size)
        cot_t[:, part] = cot_ref[part].T


def attend_kernel(
    per, me, virt, lens, live, x_ref, xhat_ref, held, got,
    qkv_ref, prob_ref, o_ref, x1_ref, wqkv, wout, vec,
):
    tokens, width = x_ref.shape
    rows = tokens // WIN
    hs = width // HEADS
    here = spot(virt[0] // 2) % VDP
    y_own = (virt[0] // 2) % 2
    first = virt[0] % 2 == 0
    total = jnp.zeros((8, width), F32)
    for m in range(CHIPS):
        k = spot(m) ^ (here + y_own * VDP)
        a = held[k].astype(F32)
        b = got[k].astype(F32)
        even = jnp.where(first, a, b)
        odd = jnp.where(first, b, a)
        for part in range(3):
            both = jnp.concatenate([even[part * 8 : part * 8 + 8], odd[part * 8 : part * 8 + 8]], 0)
            wqkv[m * 16 : m * 16 + 16, part * width : (part + 1) * width] = both.astype(BF16)
        both = jnp.concatenate([even[24:32], odd[24:32]], 0)
        wout[m * 16 : m * 16 + 16] = both.astype(BF16)
        total = total + a[32:40] + b[32:40]
    vec[...] = total
    scale = hs**-0.5
    jj = lax.broadcasted_iota(jnp.int32, (WIN, WIN), 0)
    ii = lax.broadcasted_iota(jnp.int32, (WIN, WIN), 1)
    same = ii == jj
    image_rows = live.shape[1]
    base = lax.rem(me[0], 2) * rows

    def enter(c):
        part = slice(c * per * WIN, (c + 1) * per * WIN)
        h1 = (xhat_ref[part] * total[0:1] + total[2:3]).astype(BF16)
        qkv = dot(h1, wqkv[...], NN).astype(BF16)
        qkv_ref[part] = qkv
        scores = []
        for r in range(per):
            at = slice(r * WIN, (r + 1) * WIN)
            for h in range(HEADS):
                q = qkv[at, h * hs : (h + 1) * hs]
                k = qkv[at, width + h * hs : width + (h + 1) * hs]
                scores.append(dot(k, q, NT))
        return qkv, scores

    ahead = enter(0)
    for c in range(rows // per):
        qkv, scores = ahead
        if c + 1 < rows // per:
            ahead = enter(c + 1)
        part = slice(c * per * WIN, (c + 1) * per * WIN)
        probs = []
        for r in range(per):
            row = base + c * per + r
            image = row // image_rows
            inside = row - image * image_rows
            reach = jnp.where(live[image, inside] == 1, lens[image] - inside * WIN, 0)
            allowed = same | (jj < jnp.minimum(ii, reach))
            for h in range(HEADS):
                s = jnp.where(allowed, scores[r * HEADS + h], -1e30)
                e = jnp.exp((s - jnp.max(s, 0, keepdims=True)) * scale)
                probs.append((e * (1.0 / jnp.sum(e, 0, keepdims=True))).astype(BF16))
        mixed = []
        for r in range(per):
            at = slice(r * WIN, (r + 1) * WIN)
            heads = []
            for h in range(HEADS):
                v = qkv[at, 2 * width + h * hs : 2 * width + (h + 1) * hs]
                heads.append(dot(probs[r * HEADS + h], v, TN).astype(BF16))
            mixed.append(jnp.concatenate(heads, 1))
        o = jnp.concatenate(mixed, 0)
        for n, p in enumerate(probs):
            prob_ref[c * per * HEADS + n] = p
        o_ref[part] = o
        x1_ref[part] = x_ref[part].astype(F32) + dot(o, wout[...], NN)


def join(virt, blocks, n, up, down_t):
    tall = blocks.shape[1] // 2
    width = up.shape[0]
    here = turn(virt[0] // 4)
    for i in range(VDP):
        k = turn(i) ^ here
        at = slice(i * tall, (i + 1) * tall)
        cols = slice(n * width, (n + 1) * width)
        up[at, cols] = blocks[k, :tall]
        down_t[at, cols] = blocks[k, tall:]


def hidden_units(h2, dyb, up, down_t):
    u = dot(h2, up[...], NN).astype(BF16)
    da = dot(dyb, down_t[...], NN).astype(BF16)
    a, slope = gelu_both(u)
    return a, da * slope


def hidden_near_kernel(
    per, start, virt, x1_ref, cot_ref, vec, own, got, *refs,
):
    if start:
        h2_first, a_first, du_first, cot_t = refs[:4]
        refs = refs[4:]
    h2_ref, xhat_ref, inv_ref, f_ref, dh2_ref = refs[:5]
    a_ref, du_ref, up, down_t, up_t, down = refs[-6:]
    width = x1_ref.shape[1]
    tokens = h2_ref.shape[0]
    size = per * WIN
    join(virt, own, 0, up, down_t)
    join(virt, got, 1, up, down_t)
    up_t[...] = up[...].T
    down[...] = down_t[...].T
    for c in range(tokens // size):
        part = slice(c * size, (c + 1) * size)
        whole = slice(start + c * size, start + (c + 1) * size)
        x1 = x1_ref[whole]
        xhat, inv = norm_parts(x1)
        xhat_ref[part] = xhat
        inv_ref[part] = inv
        h2 = (xhat * vec[1:2] + vec[3:4]).astype(BF16)
        h2_ref[part] = h2
        a, du = hidden_units(h2, cot_ref[whole], up, down_t)
        a_ref[part] = a
        du_ref[part] = du
        f_ref[part] = x1 + vec[4:5] + dot(a, down[...], NN)
        dh2_ref[part] = dot(du, up_t[...], NN)
    if not start:
        return
    keep, send = refs[5:7]
    gdown = dot(cot_t[:, :start], a_first[...], NN) + dot(cot_t[:, start:], a_ref[...], NN)
    gup = dot(h2_first[...], du_first[...], TN) + dot(h2_ref[...], du_ref[...], TN)
    tall = width // VDP
    here = turn(virt[0] // 4)
    for i in range(VDP):
        at = slice(i * tall, (i + 1) * tall)
        k = turn(i) ^ here
        keep[k, :tall] = gup[at, :width]
        keep[k, tall:] = gdown[at, :width]
        send[k, :tall] = gup[at, width:].astype(BF16)
        send[k, tall:] = gdown[at, width:].astype(BF16)


def hidden_far_kernel(
    per, virt, cot_ref, vec, own, got, *refs,
):
    firsts, seconds, o_ref = refs[:5], refs[5:10], refs[10]
    y_ref, dx1_ref, g_ref, gout, gvec, up, down_t, up_t, down = refs[11:]
    tokens, width = y_ref.shape
    size = per * WIN
    half = tokens // 2
    join(virt, own, 0, up, down_t)
    join(virt, got, 1, up, down_t)
    up_t[...] = up[...].T
    down[...] = down_t[...].T
    sums = [jnp.zeros((1, width), F32)] * 3
    for c in range(tokens // size):
        part = slice(c * size, (c + 1) * size)
        h2_ref, xhat_ref, inv_ref, f_ref, dh2_ref = firsts if c * size < half else seconds
        mine = slice(c * size % half, c * size % half + size)
        a, du = hidden_units(h2_ref[mine], cot_ref[part], up, down_t)
        y_ref[part] = (f_ref[mine] + dot(a, down[...], NN)).astype(BF16)
        dh2 = dh2_ref[mine] + dot(du, up_t[...], NN)
        dy = cot_ref[part].astype(F32)
        xhat = xhat_ref[mine]
        dx1 = dy + norm_back(dh2, xhat, inv_ref[mine], vec[1:2])
        dx1_ref[part] = dx1
        g_ref[part] = dx1.astype(BF16)
        for n, term in enumerate((dh2 * xhat, dh2, dy)):
            sums[n] = sums[n] + jnp.sum(term, 0, keepdims=True)
    gout[...] = dot(o_ref[...], g_ref[...], TN)
    zero = jnp.zeros((1, width), F32)
    gvec[...] = jnp.concatenate([zero, sums[0], zero, sums[1], sums[2], zero, zero, zero], 0)


def own_rows(virt, i, other):
    core = virt[0] % 2
    core = 1 - core if other else core
    return pl.ds(pl.multiple_of(i * 32 + ((virt[0] // 2) % 2) * 16 + core * 8, 8), 8)


def back_kernel(
    per, virt, qkv_ref, prob_ref, g_ref, xhat_t, wqkv, wout, vec, gout, gvec,
    dqkv, keep, send,
    gqkv,
):
    tokens, width = g_ref.shape
    hs = width // HEADS
    scale = hs**-0.5
    every = [(r, h) for r in range(tokens // WIN) for h in range(HEADS)]
    groups = [every[n : n + 2 * per] for n in range(0, len(every), 2 * per)]

    def piece(ref, r, h, part=0):
        return ref[r * WIN : (r + 1) * WIN, part * width + h * hs : part * width + (h + 1) * hs]

    def enter(pairs):
        r = pairs[0][0]
        do = dot(g_ref[r * WIN : (r + per) * WIN], wout[...], NT).astype(BF16)
        dos = [do[(n - r) * WIN : (n - r + 1) * WIN, h * hs : (h + 1) * hs] for n, h in pairs]
        probs = [prob_ref[r * HEADS + h] for r, h in pairs]
        dps = [dot(piece(qkv_ref, r, h, 2), a, NT) for a, (r, h) in zip(dos, pairs)]
        dvs = [dot(p, a, NN).astype(BF16) for p, a in zip(probs, dos)]
        return probs, dps, dvs

    ahead = enter(groups[0])
    for place, pairs in enumerate(groups):
        probs, dps, dvs = ahead
        if place + 1 < len(groups):
            ahead = enter(groups[place + 1])
        dss = []
        for p, dp in zip(probs, dps):
            pf = p.astype(F32)
            ds = pf * (dp - jnp.sum(dp * pf, 0, keepdims=True)) * scale
            dss.append(ds.astype(BF16))
        dqs = [dot(ds, piece(qkv_ref, r, h, 1), TN).astype(BF16) for ds, (r, h) in zip(dss, pairs)]
        dks = [dot(ds, piece(qkv_ref, r, h, 0), NN).astype(BF16) for ds, (r, h) in zip(dss, pairs)]
        for n, (r, h) in enumerate(pairs):
            for part, values in enumerate((dqs, dks, dvs)):
                at = slice(part * width + h * hs, part * width + (h + 1) * hs)
                dqkv[r * WIN : (r + 1) * WIN, at] = values[n]
    grad = dot(xhat_t[...], dqkv[...], NN)
    total = jnp.zeros((1, 3 * width), F32)
    for r in range(tokens // WIN):
        total = total + jnp.sum(dqkv[r * WIN : (r + 1) * WIN].astype(F32), 0, keepdims=True)
    w = wqkv[...].astype(F32)
    cols = jnp.concatenate([
        jnp.broadcast_to(jnp.sum(w * grad, -1, keepdims=True), (width, 64)),
        jnp.broadcast_to(jnp.sum(w * total, -1, keepdims=True), (width, 64)),
    ], 1)
    lines = cols.T
    gain, from_total = lines[0:1], lines[64:65]
    vec_t = vec[...].T
    gqkv[...] = grad * vec_t[:, 0:1] + total * vec_t[:, 2:3]
    rest = gvec[...]
    sums = jnp.concatenate([gain, rest[1:2], from_total, rest[3:]], 0)
    here = turn(virt[0] // 4)
    for i in range(VDP):
        k = turn(i) ^ here
        mine, other = own_rows(virt, i, 0), own_rows(virt, i, 1)
        theirs = []
        for part in range(3):
            at = slice(part * width, (part + 1) * width)
            keep[k, part * 8 : part * 8 + 8] = gqkv[mine, at]
            theirs.append(gqkv[other, at])
        keep[k, 24:32] = gout[mine]
        keep[k, 32:] = sums
        send[k] = jnp.concatenate(theirs + [gout[other], sums], 0).astype(BF16)


def token_grad_kernel(per, me, dqkv, wqkv, vec, xhat_ref, inv_ref, dx1_ref, y, y_near, gx, gxb, out, sems):
    own = dqkv.shape[0]
    size = per * WIN
    copies = []
    for n, source in enumerate((y, y_near)):
        at = pl.ds((lax.rem(me[0], 2) ^ n) * own, own)
        copies.append(pltpu.make_async_copy(source, out.at[at], sems.at[n]))
        copies[-1].start()
    ahead = dot(dqkv[:size], wqkv[...], NT)
    for c in range(own // size):
        part = slice(c * size, (c + 1) * size)
        dh1 = ahead
        if (c + 1) * size < own:
            ahead = dot(dqkv[(c + 1) * size : (c + 2) * size], wqkv[...], NT)
        values = dx1_ref[part] + norm_back(dh1, xhat_ref[part], inv_ref[part], vec[0:1])
        gx[part] = values
        gxb[part] = values.astype(BF16)
    for copy in copies:
        copy.wait()


def place_kernel(per, me, mine, theirs, out, wide, sems):
    own = theirs.shape[0]
    size = per * WIN
    here = lax.rem(me[0], 2) * own
    copies = [pltpu.make_async_copy(mine, out.at[pl.ds(here, own)], sems.at[own // size])]
    copies[0].start()
    for c in range(own // size):
        part = pl.ds(c * size, size)
        wide[part] = theirs[part].astype(F32)
        at = pl.ds(own - here + c * size, size)
        copies.append(pltpu.make_async_copy(wide.at[part], out.at[at], sems.at[c]))
        copies[-1].start()
    for copy in copies:
        copy.wait()


def finish_hidden_kernel(keep, got, up, down):
    total = keep[0] + got[0].astype(F32)
    tall = up.shape[0]
    up[...] = total[:tall]
    down[...] = total[tall:]


def finish_kernel(me, keep, got, qkv, out, gains, biases):
    total = keep[0] + got[0].astype(F32)
    small, width = out.shape
    for part in range(3):
        qkv[:, part * width : (part + 1) * width] = total[part * small : (part + 1) * small]
    out[...] = total[3 * small : 4 * small]
    vec = pltpu.roll(total[4 * small :], width - me[0] * small, 1)[:, :small]
    gains[...] = vec[:2]
    biases[...] = vec[2:5]


def swap(block, axis, bit):
    size = lax.axis_size(axis)
    return lax.ppermute(block, axis, [(i, i ^ bit) for i in range(size)])


def steps_of(axis):
    return [(axis, 1 << k) for k in reversed(range(lax.axis_size(axis).bit_length() - 1))]


def after(value, other):
    return lax.optimization_barrier((value, other))[0]


def halves(held):
    half = held.shape[0] // 2
    return held[:half], held[half:].astype(BF16)


def fold_step(keep, send, axis, bit, past=None):
    got = swap(send, axis, bit)
    return keep + (got if past is None else after(got, past)).astype(F32)


def bit_reverse(index, count):
    out = 0 * index
    for k in range(count):
        out = out | (((index >> k) & 1) << (count - 1 - k))
    return out


def by_device(block, me):
    blocks = block[None]
    for axis, bit in steps_of("dp") + steps_of("tensor"):
        blocks = jnp.concatenate([blocks, swap(blocks, axis, bit)], 0)
    count = blocks.shape[0]
    order = jnp.arange(count, dtype=jnp.int32) ^ me
    return jnp.take(blocks, bit_reverse(order, count.bit_length() - 1), axis=0)


def other_pack(w_qkv, w_out, gains, biases, w_up, w_down, me):
    small, width = w_out.shape
    qkv = w_qkv.reshape(small, 3, width).transpose(1, 0, 2).reshape(3 * small, width)
    rows = jnp.concatenate([gains, biases], 0)
    place = jnp.zeros((8, width), BF16)
    place = lax.dynamic_update_slice(place, rows, (jnp.int32(0), me * small))
    return jnp.concatenate([qkv, w_out, place], 0), jnp.concatenate([w_up, w_down.T], 0)


def other_blocks(a, b, me, n_dp, n_t):
    a = by_device(a, me)
    b = by_device(b, me)
    width = a.shape[2]
    count = n_dp * n_t
    small = width // count
    big = width // (VDP * VT)
    mats = a[:, : 4 * small].reshape(count, 4, small, width).transpose(1, 0, 2, 3)
    mats = mats.reshape(4, VDP * VT, big, width).transpose(1, 0, 2, 3).reshape(VDP * VT, 4 * big, width)
    vec = jnp.sum(a[:, 4 * small :].astype(F32), 0).astype(BF16)
    vecs = jnp.concatenate([vec[None], jnp.zeros((VDP * VT - 1, 8, width), BF16)], 0)
    a = jnp.concatenate([mats, vecs], 1)
    tall = width // n_dp
    b = b.reshape(n_dp, VT, 2, tall, width).transpose(1, 2, 0, 3, 4)
    b = b.reshape(VT, 2, VDP, width // VDP, width).transpose(2, 0, 1, 3, 4)
    b = b.reshape(VDP * VT, 2 * (width // VDP), width)

    y_own = (me // 2) % 2

    def placed(blocks):
        pairs = blocks.reshape((CHIPS, 2) + blocks.shape[1:])
        pairs = jnp.stack([pairs[m] for m in sorted(range(CHIPS), key=spot)], 0)
        pairs = jnp.where(y_own == 1, jnp.roll(pairs, VDP, 0), pairs)
        return pairs[:, 0], pairs[:, 1]

    return placed(a) + placed(b)


def other_reduce(pair_a, pair_b, me, n_dp, n_t):
    count = n_dp * n_t
    y_own = (me // 2) % 2

    def whole(keep, send):
        pairs = jnp.stack([keep, send.astype(F32)], 1)
        pairs = jnp.stack([pairs[turn(i)] for i in range(VDP)], 0)
        none = jnp.zeros_like(pairs)
        both = jnp.stack([jnp.where(y_own == y, pairs, none) for y in range(2)], 1)
        return both.reshape((VDP * VT,) + keep.shape[1:])

    def rows_of(blocks, parts):
        big = blocks.shape[1] // parts
        mats = blocks.reshape(VDP * VT, parts, big, -1).transpose(1, 0, 2, 3)
        mats = mats.reshape(parts, count, VDP * VT * big // count, -1).transpose(1, 0, 2, 3)
        return mats.reshape(count, -1, blocks.shape[2])

    def vec_of(blocks):
        picked = jnp.where(y_own == 0, blocks[0], 0.0)
        return jnp.broadcast_to(picked[None], (count,) + picked.shape)

    a, b = whole(*pair_a), whole(*pair_b)
    width = a.shape[2]
    tall, high = width // n_dp, width // VDP
    cols = b.reshape(VDP, VT, 2, high, width).transpose(1, 2, 0, 3, 4)
    cols = cols.reshape(VT, 2, n_dp, tall, width).transpose(2, 0, 1, 3, 4)
    cols = cols.reshape(count, 2 * tall, width)
    a = jnp.concatenate([rows_of(a[:, :32], 4), vec_of(a[:, 32:])], 1)
    results = []
    for blocks in (a, cols):
        blocks = jnp.take(blocks, jnp.arange(count, dtype=jnp.int32) ^ me, axis=0)
        for axis, bit in reversed(steps_of("dp") + steps_of("tensor")):
            pairs = blocks.reshape((-1, 2) + blocks.shape[1:])
            got = swap(pairs[:, 1].astype(BF16), axis, bit)
            blocks = pairs[:, 0] + got.astype(F32)
        results.append(blocks[0])
    return results


def struct(shape, dtype):
    return jax.ShapeDtypeStruct(shape, dtype)


def call(kernel, name, args, outs, scratch=(), flops=0, limit=8, hbm_outs=True):
    args = [a if isinstance(a, tuple) else (a, pltpu.VMEM) for a in args]
    moved = sum(a.size * a.dtype.itemsize for a, _ in args)
    spaces = [pl.ANY if hbm_outs and isinstance(o, jax.ShapeDtypeStruct) else pltpu.VMEM for o in outs]
    return pl.pallas_call(
        kernel,
        name=name,
        out_shape=outs,
        in_specs=[pl.BlockSpec(memory_space=space) for _, space in args],
        out_specs=[pl.BlockSpec(memory_space=space) for space in spaces],
        scratch_shapes=list(scratch),
        compiler_params=pltpu.CompilerParams(vmem_limit_bytes=limit * MIB),
        cost_estimate=pl.CostEstimate(flops=flops, bytes_accessed=moved, transcendentals=0),
    )(*[a for a, _ in args])


def on_device(tokens, lengths, row_mask, cotangent, w_qkv, w_out, gains, biases, w_up, w_down):
    images, seq_len, width = tokens.shape
    n_dp, n_t = lax.axis_size("dp"), lax.axis_size("tensor")
    index = lax.axis_index("dp") * n_t + lax.axis_index("tensor")
    me = index.astype(jnp.int32).reshape(1)
    usual = (n_dp, n_t) == (VDP, VT)
    virt = me if usual else (index // 2 % 2 * 2).astype(jnp.int32).reshape(1)
    small = width // (n_dp * n_t)
    tall = width // n_dp
    own = images * seq_len // 2
    rows = own // WIN
    per = 4 if rows % 4 == 0 else 1
    smem = pltpu.SMEM
    weights = (w_qkv, w_out, gains, biases, w_up, w_down)
    token_mm = 2 * own * width
    hbm = pltpu.HBM

    def in_hbm(array):
        return (pltpu.with_memory_space_constraint(array, hbm), hbm)

    flat = tokens.reshape(images * seq_len, width)

    def first_norm(x):
        return call(
            first_norm_kernel,
            "first_norm",
            [x],
            [pltpu.VMEM((own, width), F32), pltpu.VMEM((own, 1), F32)],
            limit=4,
        )

    def fetch_turned(me, xhat):
        return call(
            turn_kernel,
            "turn",
            [(me, smem), in_hbm(cotangent.reshape(images * seq_len, width)), xhat],
            [
                pltpu.VMEM((own, width), BF16),
                pltpu.VMEM((width, own), BF16),
                pltpu.VMEM((width, own), BF16),
            ],
            [pltpu.SemaphoreType.DMA(())],
            limit=4,
        )

    if usual:
        weights = (w_qkv, w_out, gains, biases, w_up, w_down.T)
        pack_a, pack_b, x = call(
            pack_kernel,
            "pack",
            [(me, smem)] + [in_hbm(w) for w in weights] + [in_hbm(flat)],
            [
                pltpu.VMEM((1, 4 * small + 8, width), BF16),
                pltpu.VMEM((1, 2 * tall, width), BF16),
                pltpu.VMEM((own, width), BF16),
            ],
            [pltpu.VMEM(w.shape, BF16) for w in weights] + [pltpu.SemaphoreType.DMA((7,))],
        )
        held_a, b = pack_a, pack_b
        xhat1, inv1 = first_norm(x)
        for n, (axis, bit) in enumerate(steps_of("dp")):
            got = swap(held_a, axis, bit)
            if n:
                got = after(got, b)
            held_a = jnp.concatenate([held_a, got], 0)
            b = jnp.concatenate([b, swap(b, axis, bit)], 0)
            held_a, b = (after(held_a, xhat1), b) if n == 0 else (held_a, b)
            b = after(b, held_a)
        cot, cot_t, xhat_t = fetch_turned(after(me, held_a), xhat1)
        held_a = jnp.concatenate([held_a, after(swap(held_a, "tensor", 2), (cot, b))], 0)
        far_b = swap(b, "tensor", 2)
        got_a = swap(held_a, "tensor", 1)
        got_b = swap(after(b, held_a), "tensor", 1)
    else:
        held_a, got_a, held_b, got_b = other_blocks(*other_pack(*weights, index), index, n_dp, n_t)
        b, far_b = held_b[:VDP], held_b[VDP:]
        got_b, got_far = got_b[:VDP], got_b[VDP:]
        x = lax.dynamic_slice_in_dim(flat, index % 2 * own, own, 0)
        xhat1, inv1 = first_norm(x)
        cot, cot_t, xhat_t = fetch_turned(me, xhat1)
    qkv, prob, o, x1, wqkv, wout, vec = call(
        functools.partial(attend_kernel, per),
        "attend",
        [(me, smem), (virt, smem), (lengths, smem), (row_mask, smem), x, xhat1, held_a, got_a],
        [
            pltpu.VMEM((own, 3 * width), BF16),
            pltpu.VMEM((rows * HEADS, WIN, WIN), BF16),
            pltpu.VMEM((own, width), BF16),
            pltpu.VMEM((own, width), F32),
            pltpu.VMEM((width, 3 * width), BF16),
            pltpu.VMEM((width, width), BF16),
            pltpu.VMEM((8, width), F32),
        ],
        flops=token_mm * (4 * width + 2 * WIN),
    )
    tall_b = 2 * (width // VDP)
    mats = [pltpu.VMEM((width, 2 * width), BF16)] * 2 + [pltpu.VMEM((2 * width, width), BF16)] * 2
    half = own // 2
    wide_per = 6 if rows % 12 == 0 else 1
    units = [
        pltpu.VMEM((half, width), BF16),
        pltpu.VMEM((half, width), F32),
        pltpu.VMEM((half, 1), F32),
        pltpu.VMEM((half, width), F32),
        pltpu.VMEM((half, width), F32),
        pltpu.VMEM((half, 2 * width), BF16),
        pltpu.VMEM((half, 2 * width), BF16),
    ]
    *first, a_first, du_first = call(
        functools.partial(hidden_near_kernel, wide_per, 0),
        "hidden_first",
        [(virt, smem), x1, cot, vec, b, got_b],
        units,
        mats,
        token_mm * 4 * width,
    )
    if usual:
        far_b = after(far_b, first[0])
        got_far = swap(far_b, "tensor", 1)
    *second, keep_b, send_b = call(
        functools.partial(hidden_near_kernel, wide_per, half),
        "hidden_second",
        [(virt, smem), x1, cot, after(vec, far_b), b, got_b, first[0], a_first, du_first, cot_t],
        units[:5] + [pltpu.VMEM((VDP, tall_b, width), F32), pltpu.VMEM((VDP, tall_b, width), BF16)],
        units[5:] + mats,
        token_mm * 8 * width,
    )
    y, dx1, g, gout, gvec = call(
        functools.partial(hidden_far_kernel, wide_per),
        "hidden_far",
        [(virt, smem), cot, vec, far_b, got_far, *first, *second, o],
        [
            pltpu.VMEM((own, width), BF16),
            pltpu.VMEM((own, width), F32),
            pltpu.VMEM((own, width), BF16),
            pltpu.VMEM((width, width), F32),
            pltpu.VMEM((8, width), F32),
        ],
        mats,
        token_mm * 9 * width,
    )
    core, xbit, zlo, zhi = ("tensor", 1), ("dp", 1), ("dp", 2), ("dp", 4)
    if usual:
        held_b = fold_step(keep_b, send_b, *core, g)
        y = after(y, held_b)
    y_near = swap(y, "tensor", 1)
    dqkv, keep_a, send_a = call(
        functools.partial(back_kernel, per),
        "back",
        [(virt, smem), qkv, prob, g, xhat_t, wqkv, wout, vec, gout, gvec],
        [
            pltpu.VMEM((own, 3 * width), BF16),
            pltpu.VMEM((VDP, 40, width), F32),
            pltpu.VMEM((VDP, 40, width), BF16),
        ],
        [pltpu.VMEM((width, 3 * width), F32)],
        token_mm * (4 * width + 5 * WIN),
    )
    gx, gxb, layer_out = call(
        functools.partial(token_grad_kernel, per),
        "token_grad",
        [(me, smem), dqkv, wqkv, vec, xhat1, inv1, dx1, y, y_near],
        [
            pltpu.VMEM((own, width), F32),
            pltpu.VMEM((own, width), BF16),
            struct((images * seq_len, width), BF16),
        ],
        [pltpu.SemaphoreType.DMA((2,))],
        flops=token_mm * 3 * width,
    )
    layer_out = layer_out.reshape(images, seq_len, width)

    def place(gx_near):
        return call(
            functools.partial(place_kernel, per),
            "place",
            [(me, smem), gx, gx_near],
            [struct((images * seq_len, width), F32)],
            [pltpu.VMEM((own, width), F32), pltpu.SemaphoreType.DMA((rows // per + 1,))],
        )[0].reshape(images, seq_len, width)

    if usual:
        held_b = fold_step(*halves(held_b), *xbit)
        held_a = fold_step(keep_a, after(send_a, held_b), *core, gxb)
        grad_tokens = place(swap(after(gxb, held_a), "tensor", 1))
        keep, send = halves(held_b)
        held_b = fold_step(keep, after(send, held_a), *zlo)
        held_a = fold_step(*halves(held_a), *xbit)
        held_a = fold_step(*halves(held_a), *zlo, grad_tokens)
        got = swap(halves(held_b)[1], *zhi)
        o_up, o_down = call(
            finish_hidden_kernel, "finish_hidden", [held_b, got], [struct((tall, width), F32)] * 2, limit=2, hbm_outs=False
        )
        got = swap(halves(held_a)[1], *zhi)
        shapes = ((small, 3 * width), (small, width), (2, small), (3, small))
        o_qkv, o_out, o_gains, o_bias = call(
            finish_kernel,
            "finish",
            [(me, smem), held_a, got],
            [struct(shape, F32) for shape in shapes],
            limit=2,
            hbm_outs=False,
        )
    else:
        grad_tokens = place(swap(gxb, "tensor", 1))
        grad_a, grad_b = other_reduce((keep_a, send_a), (keep_b, send_b), index, n_dp, n_t)
        o_qkv = jnp.concatenate([grad_a[p * small : (p + 1) * small] for p in range(3)], 1)
        o_out = grad_a[3 * small : 4 * small]
        o_vec = lax.dynamic_slice_in_dim(grad_a[4 * small : 4 * small + 5], index * small, small, 1)
        o_gains, o_bias = o_vec[:2], o_vec[2:]
        o_up, o_down = grad_b[:tall], grad_b[tall:]
    return layer_out, grad_tokens, o_qkv, o_out, o_gains, o_bias, o_up, o_down.T


def solution(mesh):
    in_specs = (
        P("dp", None, None),
        P("dp"),
        P("dp", None),
        P("dp", None, None),
        P(("dp", "tensor"), None),
        P(("dp", "tensor"), None),
        P(None, ("dp", "tensor")),
        P(None, ("dp", "tensor")),
        P("dp", "tensor"),
        P("tensor", "dp"),
    )
    out_specs = (
        P("dp", None, None),
        P("dp", None, None),
        P(("dp", "tensor"), None),
        P(("dp", "tensor"), None),
        P(None, ("dp", "tensor")),
        P(None, ("dp", "tensor")),
        P("dp", "tensor"),
        P("tensor", "dp"),
    )
    return jax.shard_map(
        on_device, mesh=mesh, in_specs=in_specs, out_specs=out_specs, check_vma=False
    )
```

```python
import functools

import jax
import jax.numpy as jnp
from jax import lax
from jax.experimental import pallas as pl
from jax.experimental.pallas import tpu as pltpu
from jax.sharding import PartitionSpec as P

HEADS = 2
WIN = 96
F32 = jnp.float32
BF16 = jnp.bfloat16
VDP, VT = 8, 4
CHIPS = VDP * VT // 2
MIB = 1 << 20

NN = ((1,), (0,))
NT = ((1,), (1,))
TN = ((0,), (0,))


def dot(a, b, dims):
    return lax.dot_general(a, b, (dims, ((), ())), preferred_element_type=F32)


def turn(i):
    return ((i & 1) << 2) | (i & 2) | ((i & 4) >> 2)


def twist(i):
    return (i & 1) * 4 + (i >> 1)


def spot(m, order=turn):
    return (m % 2) * VDP + order(m // 2)


def turn(i):
    return ((i & 1) << 2) | (i & 2) | ((i & 4) >> 2)


def twist(i):
    return (i & 1) * 4 + (i >> 1)


def spot(m, order=turn):
    return (m % 2) * VDP + order(m // 2)


def fold(m):
    out = 0
    for place, bit in enumerate(REDUCE_BITS):
        shift = 3 - place
        out = out | (((m // bit) & 1) << shift)
    return out


def norm_parts(values):
    center = values - jnp.mean(values, -1, keepdims=True)
    inv = lax.rsqrt(jnp.mean(center * center, -1, keepdims=True) + 1e-05)
    return center * inv, inv


def norm_back(grad, xhat, inv, gain):
    scaled = grad * gain
    return inv * (
        scaled
        - jnp.mean(scaled, -1, keepdims=True)
        - xhat * jnp.mean(scaled * xhat, -1, keepdims=True)
    )


def gelu_both(u):
    c = 0.7978845608028654
    u2 = u * u
    t = jnp.tanh(u * (c + (c * 0.044715) * u2))
    half = 0.5 + 0.5 * t
    value = u * half
    slope = half + (value - value * half) * (2 * c + (6 * c * 0.044715) * u2)
    return value, slope


def pack_kernel(me, *refs):
    sources, (small_ref, big_ref), held, sems = refs[:6], refs[6:8], refs[8:14], refs[14]
    copies = [pltpu.make_async_copy(a, b, sems.at[n]) for n, (a, b) in enumerate(zip(sources, held))]
    for copy in copies:
        copy.start()
    qkv, out, gains, biases, up, down = held
    small, width = out.shape
    tall = up.shape[0]
    lane = lax.broadcasted_iota(jnp.int32, (1, width), 1)
    mine = lane // small == me[0]
    for copy in copies:
        copy.wait()
    for part in range(3):
        small_ref[0, part * small : (part + 1) * small] = qkv[:, part * width : (part + 1) * width]
    small_ref[0, 3 * small : 4 * small] = out[...]
    rows = [gains[0:1], gains[1:2], biases[0:1], biases[1:2], biases[2:3]]
    vals = jnp.concatenate(rows + [jnp.zeros((3, small), BF16)], 0).astype(F32)
    wide = jnp.concatenate([vals] * (width // small), 1)
    small_ref[0, 4 * small : 4 * small + 8] = jnp.where(mine, wide, 0.0).astype(BF16)
    big_ref[0, :tall] = up[...]
    big_ref[0, tall:] = down[...]


def fetch_kernel(me, tokens, x_ref, xhat_ref, inv_ref, xhat_t, sem):
    own, width = x_ref.shape
    copy = pltpu.make_async_copy(tokens.at[pl.ds(lax.rem(me[0], 2) * own, own)], x_ref, sem)
    copy.start()
    ones = jnp.full((width, width), 1.0 / width, BF16)
    size = 256 if own % 256 == 0 else own
    copy.wait()
    for n in range(own // size):
        part = slice(n * size, (n + 1) * size)
        x = x_ref[part]
        center = x.astype(F32) - dot(x, ones, NN)
        inv = lax.rsqrt(dot((center * center).astype(BF16), ones, NN) + 1e-05)
        xhat = center * inv
        xhat_ref[part] = xhat
        inv_ref[part] = inv[:, :1]
        xhat_t[:, part] = xhat.astype(BF16).T


def turn_kernel(me, cot, cot_ref, cot_t, sem):
    own = cot_ref.shape[0]
    copy = pltpu.make_async_copy(cot.at[pl.ds(lax.rem(me[0], 2) * own, own)], cot_ref, sem)
    copy.start()
    size = 256 if own % 256 == 0 else own
    copy.wait()
    for n in range(own // size):
        part = slice(n * size, (n + 1) * size)
        cot_t[:, part] = cot_ref[part].T


def attend_kernel(
    per, me, virt, lens, live, x_ref, xhat_ref, held, got,
    qkv_ref, prob_ref, o_ref, x1_ref, wqkv, wout, vec,
):
    tokens, width = x_ref.shape
    rows = tokens // WIN
    hs = width // HEADS
    here = twist(virt[0] // 4)
    y_own = (virt[0] // 2) % 2
    first = virt[0] % 2 == 0
    total = jnp.zeros((8, width), F32)
    for m in range(CHIPS):
        k = spot(m, twist) ^ (here + y_own * VDP)
        a = held[k].astype(F32)
        b = got[k].astype(F32)
        even = jnp.where(first, a, b)
        odd = jnp.where(first, b, a)
        for part in range(3):
            both = jnp.concatenate([even[part * 8 : part * 8 + 8], odd[part * 8 : part * 8 + 8]], 0)
            wqkv[m * 16 : m * 16 + 16, part * width : (part + 1) * width] = both.astype(BF16)
        both = jnp.concatenate([even[24:32], odd[24:32]], 0)
        wout[m * 16 : m * 16 + 16] = both.astype(BF16)
        total = total + a[32:40] + b[32:40]
    vec[...] = total
    scale = hs**-0.5
    ii = lax.broadcasted_iota(jnp.int32, (WIN, WIN), 0)
    jj = lax.broadcasted_iota(jnp.int32, (WIN, WIN), 1)
    same = ii == jj
    image_rows = live.shape[1]
    base = lax.rem(me[0], 2) * rows

    def enter(c):
        part = slice(c * per * WIN, (c + 1) * per * WIN)
        h1 = (xhat_ref[part] * total[0:1] + total[2:3]).astype(BF16)
        qkv = dot(h1, wqkv[...], NN).astype(BF16)
        qkv_ref[part] = qkv
        scores = []
        for r in range(per):
            at = slice(r * WIN, (r + 1) * WIN)
            for h in range(HEADS):
                q = qkv[at, h * hs : (h + 1) * hs]
                k = qkv[at, width + h * hs : width + (h + 1) * hs]
                scores.append(dot(q, k, NT))
        return qkv, scores

    ahead = enter(0)
    for c in range(rows // per):
        qkv, scores = ahead
        if c + 1 < rows // per:
            ahead = enter(c + 1)
        part = slice(c * per * WIN, (c + 1) * per * WIN)
        probs = []
        for r in range(per):
            row = base + c * per + r
            image = row // image_rows
            inside = row - image * image_rows
            reach = jnp.where(live[image, inside] == 1, lens[image] - inside * WIN, 0)
            allowed = same | (jj < jnp.minimum(ii, reach))
            for h in range(HEADS):
                s = jnp.where(allowed, scores[r * HEADS + h], -1e30)
                e = jnp.exp((s - jnp.max(s, -1, keepdims=True)) * scale)
                probs.append((e * (1.0 / jnp.sum(e, -1, keepdims=True))).astype(BF16))
        mixed = []
        for r in range(per):
            at = slice(r * WIN, (r + 1) * WIN)
            heads = []
            for h in range(HEADS):
                v = qkv[at, 2 * width + h * hs : 2 * width + (h + 1) * hs]
                heads.append(dot(probs[r * HEADS + h], v, NN).astype(BF16))
            mixed.append(jnp.concatenate(heads, 1))
        o = jnp.concatenate(mixed, 0)
        for n, p in enumerate(probs):
            prob_ref[c * per * HEADS + n] = p
        o_ref[part] = o
        x1_ref[part] = x_ref[part].astype(F32) + dot(o, wout[...], NN)


def join(virt, blocks, n, up, down_t):
    tall = blocks.shape[1] // 2
    width = up.shape[0]
    here = turn(virt[0] // 4)
    for i in range(VDP):
        k = turn(i) ^ here
        at = slice(i * tall, (i + 1) * tall)
        cols = slice(n * width, (n + 1) * width)
        up[at, cols] = blocks[k, :tall]
        down_t[at, cols] = blocks[k, tall:]


def hidden_units(h2, dyb, up, down_t):
    u = dot(h2, up[...], NN).astype(BF16)
    da = dot(dyb, down_t[...], NN).astype(BF16)
    a, slope = gelu_both(u)
    return a, da * slope


def hidden_near_kernel(
    per, start, virt, x1_ref, cot_ref, vec, own, got, *refs,
):
    if start:
        h2_first, a_first, du_first, cot_t = refs[:4]
        refs = refs[4:]
    h2_ref, xhat_ref, inv_ref, f_ref, dh2_ref = refs[:5]
    a_ref, du_ref, up, down_t, up_t, down = refs[-6:]
    width = x1_ref.shape[1]
    tokens = h2_ref.shape[0]
    size = per * WIN
    join(virt, own, 0, up, down_t)
    join(virt, got, 1, up, down_t)
    up_t[...] = up[...].T
    down[...] = down_t[...].T
    for c in range(tokens // size):
        part = slice(c * size, (c + 1) * size)
        whole = slice(start + c * size, start + (c + 1) * size)
        x1 = x1_ref[whole]
        xhat, inv = norm_parts(x1)
        xhat_ref[part] = xhat
        inv_ref[part] = inv
        h2 = (xhat * vec[1:2] + vec[3:4]).astype(BF16)
        h2_ref[part] = h2
        a, du = hidden_units(h2, cot_ref[whole], up, down_t)
        a_ref[part] = a
        du_ref[part] = du
        f_ref[part] = x1 + vec[4:5] + dot(a, down[...], NN)
        dh2_ref[part] = dot(du, up_t[...], NN)
    if not start:
        return
    keep, send = refs[5:7]
    gdown = dot(cot_t[:, :start], a_first[...], NN) + dot(cot_t[:, start:], a_ref[...], NN)
    gup = dot(h2_first[...], du_first[...], TN) + dot(h2_ref[...], du_ref[...], TN)
    tall = width // VDP
    here = turn(virt[0] // 4)
    for i in range(VDP):
        at = slice(i * tall, (i + 1) * tall)
        k = turn(i) ^ here
        keep[k, :tall] = gup[at, :width]
        keep[k, tall:] = gdown[at, :width]
        send[k, :tall] = gup[at, width:].astype(BF16)
        send[k, tall:] = gdown[at, width:].astype(BF16)


def hidden_far_kernel(
    per, virt, cot_ref, vec, own, got, *refs,
):
    firsts, seconds, o_ref = refs[:5], refs[5:10], refs[10]
    y_ref, dx1_ref, g_ref, gout, gvec, up, down_t, up_t, down = refs[11:]
    tokens, width = y_ref.shape
    size = per * WIN
    half = tokens // 2
    join(virt, own, 0, up, down_t)
    join(virt, got, 1, up, down_t)
    up_t[...] = up[...].T
    down[...] = down_t[...].T
    sums = [jnp.zeros((1, width), F32)] * 3
    for c in range(tokens // size):
        part = slice(c * size, (c + 1) * size)
        h2_ref, xhat_ref, inv_ref, f_ref, dh2_ref = firsts if c * size < half else seconds
        mine = slice(c * size % half, c * size % half + size)
        a, du = hidden_units(h2_ref[mine], cot_ref[part], up, down_t)
        y_ref[part] = (f_ref[mine] + dot(a, down[...], NN)).astype(BF16)
        dh2 = dh2_ref[mine] + dot(du, up_t[...], NN)
        dy = cot_ref[part].astype(F32)
        xhat = xhat_ref[mine]
        dx1 = dy + norm_back(dh2, xhat, inv_ref[mine], vec[1:2])
        dx1_ref[part] = dx1
        g_ref[part] = dx1.astype(BF16)
        for n, term in enumerate((dh2 * xhat, dh2, dy)):
            sums[n] = sums[n] + jnp.sum(term, 0, keepdims=True)
    gout[...] = dot(o_ref[...], g_ref[...], TN)
    zero = jnp.zeros((1, width), F32)
    gvec[...] = jnp.concatenate([zero, sums[0], zero, sums[1], sums[2], zero, zero, zero], 0)


def own_rows(virt, i, other):
    core = virt[0] % 2
    core = 1 - core if other else core
    return pl.ds(pl.multiple_of(i * 32 + ((virt[0] // 2) % 2) * 16 + core * 8, 8), 8)


def back_kernel(
    per, virt, qkv_ref, prob_ref, g_ref, xhat_t, wqkv, wout, vec, gout, gvec,
    dqkv, keep, send,
    gqkv,
):
    tokens, width = g_ref.shape
    hs = width // HEADS
    scale = hs**-0.5
    every = [(r, h) for r in range(tokens // WIN) for h in range(HEADS)]
    groups = [every[n : n + 2 * per] for n in range(0, len(every), 2 * per)]

    def piece(ref, r, h, part=0):
        return ref[r * WIN : (r + 1) * WIN, part * width + h * hs : part * width + (h + 1) * hs]

    def enter(pairs):
        r = pairs[0][0]
        do = dot(g_ref[r * WIN : (r + per) * WIN], wout[...], NT).astype(BF16)
        dos = [do[(n - r) * WIN : (n - r + 1) * WIN, h * hs : (h + 1) * hs] for n, h in pairs]
        probs = [prob_ref[r * HEADS + h] for r, h in pairs]
        dps = [dot(a, piece(qkv_ref, r, h, 2), NT) for a, (r, h) in zip(dos, pairs)]
        dvs = [dot(p, a, TN).astype(BF16) for p, a in zip(probs, dos)]
        return probs, dps, dvs

    ahead = enter(groups[0])
    for place, pairs in enumerate(groups):
        probs, dps, dvs = ahead
        if place + 1 < len(groups):
            ahead = enter(groups[place + 1])
        dss = []
        for p, dp in zip(probs, dps):
            pf = p.astype(F32)
            ds = pf * (dp - jnp.sum(dp * pf, -1, keepdims=True)) * scale
            dss.append(ds.astype(BF16))
        dqs = [dot(ds, piece(qkv_ref, r, h, 1), NN).astype(BF16) for ds, (r, h) in zip(dss, pairs)]
        dks = [dot(ds, piece(qkv_ref, r, h, 0), TN).astype(BF16) for ds, (r, h) in zip(dss, pairs)]
        for n, (r, h) in enumerate(pairs):
            for part, values in enumerate((dqs, dks, dvs)):
                at = slice(part * width + h * hs, part * width + (h + 1) * hs)
                dqkv[r * WIN : (r + 1) * WIN, at] = values[n]
    grad = dot(xhat_t[...], dqkv[...], NN)
    total = jnp.zeros((1, 3 * width), F32)
    for r in range(tokens // WIN):
        total = total + jnp.sum(dqkv[r * WIN : (r + 1) * WIN].astype(F32), 0, keepdims=True)
    w = wqkv[...].astype(F32)
    cols = jnp.concatenate([
        jnp.broadcast_to(jnp.sum(w * grad, -1, keepdims=True), (width, 64)),
        jnp.broadcast_to(jnp.sum(w * total, -1, keepdims=True), (width, 64)),
    ], 1)
    lines = cols.T
    gain, from_total = lines[0:1], lines[64:65]
    vec_t = vec[...].T
    gqkv[...] = grad * vec_t[:, 0:1] + total * vec_t[:, 2:3]
    rest = gvec[...]
    sums = jnp.concatenate([gain, rest[1:2], from_total, rest[3:]], 0)
    here = twist(virt[0] // 4)
    for i in range(VDP):
        k = twist(i) ^ here
        mine, other = own_rows(virt, i, 0), own_rows(virt, i, 1)
        theirs = []
        for part in range(3):
            at = slice(part * width, (part + 1) * width)
            keep[k, part * 8 : part * 8 + 8] = gqkv[mine, at]
            theirs.append(gqkv[other, at])
        keep[k, 24:32] = gout[mine]
        keep[k, 32:] = sums
        send[k] = jnp.concatenate(theirs + [gout[other], sums], 0).astype(BF16)


def token_grad_kernel(per, me, dqkv, wqkv, vec, xhat_ref, inv_ref, dx1_ref, y, y_near, gx, gxb, out, sems):
    own = dqkv.shape[0]
    size = per * WIN
    copies = []
    for n, source in enumerate((y, y_near)):
        at = pl.ds((lax.rem(me[0], 2) ^ n) * own, own)
        copies.append(pltpu.make_async_copy(source, out.at[at], sems.at[n]))
        copies[-1].start()
    ahead = dot(dqkv[:size], wqkv[...], NT)
    for c in range(own // size):
        part = slice(c * size, (c + 1) * size)
        dh1 = ahead
        if (c + 1) * size < own:
            ahead = dot(dqkv[(c + 1) * size : (c + 2) * size], wqkv[...], NT)
        values = dx1_ref[part] + norm_back(dh1, xhat_ref[part], inv_ref[part], vec[0:1])
        gx[part] = values
        gxb[part] = values.astype(BF16)
    for copy in copies:
        copy.wait()


def place_kernel(per, me, mine, theirs, out, wide, sems):
    own = theirs.shape[0]
    size = per * WIN
    here = lax.rem(me[0], 2) * own
    copies = [pltpu.make_async_copy(mine, out.at[pl.ds(here, own)], sems.at[own // size])]
    copies[0].start()
    for c in range(own // size):
        part = pl.ds(c * size, size)
        wide[part] = theirs[part].astype(F32)
        at = pl.ds(own - here + c * size, size)
        copies.append(pltpu.make_async_copy(wide.at[part], out.at[at], sems.at[c]))
        copies[-1].start()
    for copy in copies:
        copy.wait()


def finish_hidden_kernel(keep, got, up, down):
    total = keep[0] + got[0].astype(F32)
    tall = up.shape[0]
    up[...] = total[:tall]
    down[...] = total[tall:]


def finish_kernel(me, keep, one, two, three, qkv, out, gains, biases):
    total = keep[0]
    for got in (one, two, three):
        total = total + got[...].astype(F32)
    small, width = out.shape
    for part in range(3):
        qkv[:, part * width : (part + 1) * width] = total[part * small : (part + 1) * small]
    out[...] = total[3 * small : 4 * small]
    vec = pltpu.roll(total[4 * small :], width - me[0] * small, 1)[:, :small]
    gains[...] = vec[:2]
    biases[...] = vec[2:5]


def swap(block, axis, bit):
    size = lax.axis_size(axis)
    return lax.ppermute(block, axis, [(i, i ^ bit) for i in range(size)])


def steps_of(axis):
    return [(axis, 1 << k) for k in reversed(range(lax.axis_size(axis).bit_length() - 1))]


def after(value, other):
    return lax.optimization_barrier((value, other))[0]


def halves(held):
    half = held.shape[0] // 2
    return held[:half], held[half:].astype(BF16)


def fold_step(keep, send, axis, bit, past=None):
    got = swap(send, axis, bit)
    return keep + (got if past is None else after(got, past)).astype(F32)


def bit_reverse(index, count):
    out = 0 * index
    for k in range(count):
        out = out | (((index >> k) & 1) << (count - 1 - k))
    return out


def by_device(block, me):
    blocks = block[None]
    for axis, bit in steps_of("dp") + steps_of("tensor"):
        blocks = jnp.concatenate([blocks, swap(blocks, axis, bit)], 0)
    count = blocks.shape[0]
    order = jnp.arange(count, dtype=jnp.int32) ^ me
    return jnp.take(blocks, bit_reverse(order, count.bit_length() - 1), axis=0)


def other_pack(w_qkv, w_out, gains, biases, w_up, w_down, me):
    small, width = w_out.shape
    qkv = w_qkv.reshape(small, 3, width).transpose(1, 0, 2).reshape(3 * small, width)
    rows = jnp.concatenate([gains, biases], 0)
    place = jnp.zeros((8, width), BF16)
    place = lax.dynamic_update_slice(place, rows, (jnp.int32(0), me * small))
    return jnp.concatenate([qkv, w_out, place], 0), jnp.concatenate([w_up, w_down.T], 0)


def other_blocks(a, b, me, n_dp, n_t):
    a = by_device(a, me)
    b = by_device(b, me)
    width = a.shape[2]
    count = n_dp * n_t
    small = width // count
    big = width // (VDP * VT)
    mats = a[:, : 4 * small].reshape(count, 4, small, width).transpose(1, 0, 2, 3)
    mats = mats.reshape(4, VDP * VT, big, width).transpose(1, 0, 2, 3).reshape(VDP * VT, 4 * big, width)
    vec = jnp.sum(a[:, 4 * small :].astype(F32), 0).astype(BF16)
    vecs = jnp.concatenate([vec[None], jnp.zeros((VDP * VT - 1, 8, width), BF16)], 0)
    a = jnp.concatenate([mats, vecs], 1)
    tall = width // n_dp
    b = b.reshape(n_dp, VT, 2, tall, width).transpose(1, 2, 0, 3, 4)
    b = b.reshape(VT, 2, VDP, width // VDP, width).transpose(2, 0, 1, 3, 4)
    b = b.reshape(VDP * VT, 2 * (width // VDP), width)

    y_own = (me // 2) % 2

    def placed(blocks, order):
        pairs = blocks.reshape((CHIPS, 2) + blocks.shape[1:])
        chips = sorted(range(CHIPS), key=lambda m: spot(m, order))
        pairs = jnp.stack([pairs[m] for m in chips], 0)
        pairs = jnp.where(y_own == 1, jnp.roll(pairs, VDP, 0), pairs)
        return pairs[:, 0], pairs[:, 1]

    return placed(a, twist) + placed(b, turn)


def other_reduce(pair_a, pair_b, me, n_dp, n_t):
    count = n_dp * n_t
    y_own = (me // 2) % 2

    def whole(keep, send, order):
        pairs = jnp.stack([keep, send.astype(F32)], 1)
        pairs = jnp.stack([pairs[order(i)] for i in range(VDP)], 0)
        none = jnp.zeros_like(pairs)
        both = jnp.stack([jnp.where(y_own == y, pairs, none) for y in range(2)], 1)
        return both.reshape((VDP * VT,) + keep.shape[1:])

    def rows_of(blocks, parts):
        big = blocks.shape[1] // parts
        mats = blocks.reshape(VDP * VT, parts, big, -1).transpose(1, 0, 2, 3)
        mats = mats.reshape(parts, count, VDP * VT * big // count, -1).transpose(1, 0, 2, 3)
        return mats.reshape(count, -1, blocks.shape[2])

    def vec_of(blocks):
        picked = jnp.where(y_own == 0, blocks[0], 0.0)
        return jnp.broadcast_to(picked[None], (count,) + picked.shape)

    a, b = whole(*pair_a, twist), whole(*pair_b, turn)
    width = a.shape[2]
    tall, high = width // n_dp, width // VDP
    cols = b.reshape(VDP, VT, 2, high, width).transpose(1, 2, 0, 3, 4)
    cols = cols.reshape(VT, 2, n_dp, tall, width).transpose(2, 0, 1, 3, 4)
    cols = cols.reshape(count, 2 * tall, width)
    a = jnp.concatenate([rows_of(a[:, :32], 4), vec_of(a[:, 32:])], 1)
    results = []
    for blocks in (a, cols):
        blocks = jnp.take(blocks, jnp.arange(count, dtype=jnp.int32) ^ me, axis=0)
        for axis, bit in reversed(steps_of("dp") + steps_of("tensor")):
            pairs = blocks.reshape((-1, 2) + blocks.shape[1:])
            got = swap(pairs[:, 1].astype(BF16), axis, bit)
            blocks = pairs[:, 0] + got.astype(F32)
        results.append(blocks[0])
    return results


def struct(shape, dtype):
    return jax.ShapeDtypeStruct(shape, dtype)


def call(kernel, name, args, outs, scratch=(), flops=0, limit=8, hbm_outs=True):
    args = [a if isinstance(a, tuple) else (a, pltpu.VMEM) for a in args]
    moved = sum(a.size * a.dtype.itemsize for a, _ in args)
    spaces = [pl.ANY if hbm_outs and isinstance(o, jax.ShapeDtypeStruct) else pltpu.VMEM for o in outs]
    return pl.pallas_call(
        kernel,
        name=name,
        out_shape=outs,
        in_specs=[pl.BlockSpec(memory_space=space) for _, space in args],
        out_specs=[pl.BlockSpec(memory_space=space) for space in spaces],
        scratch_shapes=list(scratch),
        compiler_params=pltpu.CompilerParams(vmem_limit_bytes=limit * MIB),
        cost_estimate=pl.CostEstimate(flops=flops, bytes_accessed=moved, transcendentals=0),
    )(*[a for a, _ in args])


def on_device(tokens, lengths, row_mask, cotangent, w_qkv, w_out, gains, biases, w_up, w_down):
    images, seq_len, width = tokens.shape
    n_dp, n_t = lax.axis_size("dp"), lax.axis_size("tensor")
    index = lax.axis_index("dp") * n_t + lax.axis_index("tensor")
    me = index.astype(jnp.int32).reshape(1)
    usual = (n_dp, n_t) == (VDP, VT)
    virt = me if usual else (index // 2 % 2 * 2).astype(jnp.int32).reshape(1)
    small = width // (n_dp * n_t)
    tall = width // n_dp
    own = images * seq_len // 2
    rows = own // WIN
    per = 6 if rows % 6 == 0 else 1
    smem = pltpu.SMEM
    weights = (w_qkv, w_out, gains, biases, w_up, w_down)
    token_mm = 2 * own * width
    hbm = pltpu.HBM

    def in_hbm(array):
        return (pltpu.with_memory_space_constraint(array, hbm), hbm)

    def fetch(me):
        return call(
            fetch_kernel,
            "fetch",
            [(me, smem), in_hbm(tokens.reshape(images * seq_len, width))],
            [
                pltpu.VMEM((own, width), BF16),
                pltpu.VMEM((own, width), F32),
                pltpu.VMEM((own, 1), F32),
                pltpu.VMEM((width, own), BF16),
            ],
            [pltpu.SemaphoreType.DMA(())],
            limit=4,
        )

    def fetch_turned(me):
        return call(
            turn_kernel,
            "turn",
            [(me, smem), in_hbm(cotangent.reshape(images * seq_len, width))],
            [pltpu.VMEM((own, width), BF16), pltpu.VMEM((width, own), BF16)],
            [pltpu.SemaphoreType.DMA(())],
            limit=4,
        )

    if usual:
        weights = (w_qkv, w_out, gains, biases, w_up, w_down.T)
        pack_a, pack_b = call(
            pack_kernel,
            "pack",
            [(me, smem)] + [in_hbm(w) for w in weights],
            [
                pltpu.VMEM((1, 4 * small + 8, width), BF16),
                pltpu.VMEM((1, 2 * tall, width), BF16),
            ],
            [pltpu.VMEM(w.shape, BF16) for w in weights] + [pltpu.SemaphoreType.DMA((6,))],
        )
        b = pack_b
        held_a = jnp.concatenate([pack_a] + [swap(pack_a, "dp", bit) for bit in (2, 4, 6)], 0)
        b = jnp.concatenate([b, swap(b, "dp", 4)], 0)
        b = after(b, held_a)
        cot, cot_t = fetch_turned(after(me, held_a))
        held_a = jnp.concatenate([held_a, after(swap(held_a, "dp", 1), (b, cot))], 0)
        b = jnp.concatenate([b, swap(b, "dp", 2)], 0)
        b = after(b, held_a)
        x, xhat1, inv1, xhat_t = fetch(after(me, held_a))
        held_a = jnp.concatenate([held_a, after(swap(held_a, "tensor", 2), (b, xhat1))], 0)
        b = jnp.concatenate([b, swap(b, "dp", 1)], 0)
        far_b = swap(b, "tensor", 2)
        got_a = swap(held_a, "tensor", 1)
        got_b = swap(after(b, held_a), "tensor", 1)
    else:
        held_a, got_a, held_b, got_b = other_blocks(*other_pack(*weights, index), index, n_dp, n_t)
        b, far_b = held_b[:VDP], held_b[VDP:]
        got_b, got_far = got_b[:VDP], got_b[VDP:]
        x, xhat1, inv1, xhat_t = fetch(me)
        cot, cot_t = fetch_turned(me)
    qkv, prob, o, x1, wqkv, wout, vec = call(
        functools.partial(attend_kernel, per),
        "attend",
        [(me, smem), (virt, smem), (lengths, smem), (row_mask, smem), x, xhat1, held_a, got_a],
        [
            pltpu.VMEM((own, 3 * width), BF16),
            pltpu.VMEM((rows * HEADS, WIN, WIN), BF16),
            pltpu.VMEM((own, width), BF16),
            pltpu.VMEM((own, width), F32),
            pltpu.VMEM((width, 3 * width), BF16),
            pltpu.VMEM((width, width), BF16),
            pltpu.VMEM((8, width), F32),
        ],
        flops=token_mm * (4 * width + 2 * WIN),
    )
    tall_b = 2 * (width // VDP)
    mats = [pltpu.VMEM((width, 2 * width), BF16)] * 2 + [pltpu.VMEM((2 * width, width), BF16)] * 2
    half = own // 2
    wide_per = rows // 2
    units = [
        pltpu.VMEM((half, width), BF16),
        pltpu.VMEM((half, width), F32),
        pltpu.VMEM((half, 1), F32),
        pltpu.VMEM((half, width), F32),
        pltpu.VMEM((half, width), F32),
        pltpu.VMEM((half, 2 * width), BF16),
        pltpu.VMEM((half, 2 * width), BF16),
    ]
    *first, a_first, du_first = call(
        functools.partial(hidden_near_kernel, wide_per, 0),
        "hidden_first",
        [(virt, smem), x1, cot, vec, b, got_b],
        units,
        mats,
        token_mm * 4 * width,
    )
    if usual:
        far_b = after(far_b, first[0])
        got_far = swap(far_b, "tensor", 1)
    *second, keep_b, send_b = call(
        functools.partial(hidden_near_kernel, wide_per, half),
        "hidden_second",
        [(virt, smem), x1, cot, after(vec, far_b), b, got_b, first[0], a_first, du_first, cot_t],
        units[:5] + [pltpu.VMEM((VDP, tall_b, width), F32), pltpu.VMEM((VDP, tall_b, width), BF16)],
        units[5:] + mats,
        token_mm * 8 * width,
    )
    y, dx1, g, gout, gvec = call(
        functools.partial(hidden_far_kernel, wide_per),
        "hidden_far",
        [(virt, smem), cot, vec, far_b, got_far, *first, *second, o],
        [
            pltpu.VMEM((own, width), BF16),
            pltpu.VMEM((own, width), F32),
            pltpu.VMEM((own, width), BF16),
            pltpu.VMEM((width, width), F32),
            pltpu.VMEM((8, width), F32),
        ],
        mats,
        token_mm * 9 * width,
    )
    core, xbit, zlo, zhi = ("tensor", 1), ("dp", 1), ("dp", 2), ("dp", 4)
    if usual:
        held_b = fold_step(keep_b, send_b, *core, g)
        y = after(y, held_b)
    y_near = swap(y, "tensor", 1)
    dqkv, keep_a, send_a = call(
        functools.partial(back_kernel, per),
        "back",
        [(virt, smem), qkv, prob, g, xhat_t, wqkv, wout, vec, gout, gvec],
        [
            pltpu.VMEM((own, 3 * width), BF16),
            pltpu.VMEM((VDP, 40, width), F32),
            pltpu.VMEM((VDP, 40, width), BF16),
        ],
        [pltpu.VMEM((width, 3 * width), F32)],
        token_mm * (4 * width + 5 * WIN),
    )
    gx, gxb, layer_out = call(
        functools.partial(token_grad_kernel, per),
        "token_grad",
        [(me, smem), dqkv, wqkv, vec, xhat1, inv1, dx1, y, y_near],
        [
            pltpu.VMEM((own, width), F32),
            pltpu.VMEM((own, width), BF16),
            struct((images * seq_len, width), BF16),
        ],
        [pltpu.SemaphoreType.DMA((2,))],
        flops=token_mm * 3 * width,
    )
    layer_out = layer_out.reshape(images, seq_len, width)

    def place(gx_near):
        return call(
            functools.partial(place_kernel, per),
            "place",
            [(me, smem), gx, gx_near],
            [struct((images * seq_len, width), F32)],
            [pltpu.VMEM((own, width), F32), pltpu.SemaphoreType.DMA((rows // per + 1,))],
        )[0].reshape(images, seq_len, width)

    if usual:
        held_b = fold_step(*halves(held_b), *xbit)
        held_a = fold_step(keep_a, after(send_a, held_b), *core, gxb)
        grad_tokens = place(swap(after(gxb, held_a), "tensor", 1))
        keep, send = halves(held_b)
        held_b = fold_step(keep, after(send, held_a), *zlo)
        held_a = fold_step(*halves(held_a), *xbit)
        got = swap(halves(held_b)[1], *zhi)
        o_up, o_down = call(
            finish_hidden_kernel, "finish_hidden", [held_b, got], [struct((tall, width), F32)] * 2, limit=2, hbm_outs=False
        )
        low = held_a.astype(BF16)
        got = [swap(low[n], "dp", 2 * n) for n in range(1, 4)]
        got[2] = after(got[2], grad_tokens)
        shapes = ((small, 3 * width), (small, width), (2, small), (3, small))
        o_qkv, o_out, o_gains, o_bias = call(
            finish_kernel,
            "finish",
            [(me, smem), held_a, *got],
            [struct(shape, F32) for shape in shapes],
            limit=2,
            hbm_outs=False,
        )
    else:
        grad_tokens = place(swap(gxb, "tensor", 1))
        grad_a, grad_b = other_reduce((keep_a, send_a), (keep_b, send_b), index, n_dp, n_t)
        o_qkv = jnp.concatenate([grad_a[p * small : (p + 1) * small] for p in range(3)], 1)
        o_out = grad_a[3 * small : 4 * small]
        o_vec = lax.dynamic_slice_in_dim(grad_a[4 * small : 4 * small + 5], index * small, small, 1)
        o_gains, o_bias = o_vec[:2], o_vec[2:]
        o_up, o_down = grad_b[:tall], grad_b[tall:]
    return layer_out, grad_tokens, o_qkv, o_out, o_gains, o_bias, o_up, o_down.T


def solution(mesh):
    in_specs = (
        P("dp", None, None),
        P("dp"),
        P("dp", None),
        P("dp", None, None),
        P(("dp", "tensor"), None),
        P(("dp", "tensor"), None),
        P(None, ("dp", "tensor")),
        P(None, ("dp", "tensor")),
        P("dp", "tensor"),
        P("tensor", "dp"),
    )
    out_specs = (
        P("dp", None, None),
        P("dp", None, None),
        P(("dp", "tensor"), None),
        P(("dp", "tensor"), None),
        P(None, ("dp", "tensor")),
        P(None, ("dp", "tensor")),
        P("dp", "tensor"),
        P("tensor", "dp"),
    )
    return jax.shard_map(
        on_device, mesh=mesh, in_specs=in_specs, out_specs=out_specs, check_vma=False
    )
```

```python
import functools

import jax
import jax.numpy as jnp
from jax import lax
from jax.experimental import pallas as pl
from jax.experimental.pallas import tpu as pltpu
from jax.sharding import PartitionSpec as P

HEADS = 2
WIN = 96
F32 = jnp.float32
BF16 = jnp.bfloat16
VDP, VT = 8, 4
CHIPS = VDP * VT // 2
MIB = 1 << 20

NN = ((1,), (0,))
NT = ((1,), (1,))
TN = ((0,), (0,))


def dot(a, b, dims):
    return lax.dot_general(a, b, (dims, ((), ())), preferred_element_type=F32)


def turn(i):
    return ((i & 1) << 2) | (i & 2) | ((i & 4) >> 2)


def twist(i):
    return (i & 1) * 4 + (i >> 1)


def spot(m, order=turn):
    return (m % 2) * VDP + order(m // 2)


def turn(i):
    return ((i & 1) << 2) | (i & 2) | ((i & 4) >> 2)


def twist(i):
    return (i & 1) * 4 + (i >> 1)


def spot(m, order=turn):
    return (m % 2) * VDP + order(m // 2)


def fold(m):
    out = 0
    for place, bit in enumerate(REDUCE_BITS):
        shift = 3 - place
        out = out | (((m // bit) & 1) << shift)
    return out


def norm_parts(values):
    center = values - jnp.mean(values, -1, keepdims=True)
    inv = lax.rsqrt(jnp.mean(center * center, -1, keepdims=True) + 1e-05)
    return center * inv, inv


def norm_back(grad, xhat, inv, gain):
    scaled = grad * gain
    return inv * (
        scaled
        - jnp.mean(scaled, -1, keepdims=True)
        - xhat * jnp.mean(scaled * xhat, -1, keepdims=True)
    )


def gelu_both(u):
    c = 0.7978845608028654
    u2 = u * u
    t = jnp.tanh(u * (c + (c * 0.044715) * u2))
    half = 0.5 + 0.5 * t
    value = u * half
    slope = half + (value - value * half) * (2 * c + (6 * c * 0.044715) * u2)
    return value, slope


def pack_kernel(me, *refs):
    sources, (small_ref, big_ref), held, sems = refs[:6], refs[6:8], refs[8:14], refs[14]
    copies = [pltpu.make_async_copy(a, b, sems.at[n]) for n, (a, b) in enumerate(zip(sources, held))]
    for copy in copies:
        copy.start()
    qkv, out, gains, biases, up, down = held
    small, width = out.shape
    tall = up.shape[0]
    lane = lax.broadcasted_iota(jnp.int32, (1, width), 1)
    mine = lane // small == me[0]
    for copy in copies:
        copy.wait()
    for part in range(3):
        small_ref[0, part * small : (part + 1) * small] = qkv[:, part * width : (part + 1) * width]
    small_ref[0, 3 * small : 4 * small] = out[...]
    rows = [gains[0:1], gains[1:2], biases[0:1], biases[1:2], biases[2:3]]
    vals = jnp.concatenate(rows + [jnp.zeros((3, small), BF16)], 0).astype(F32)
    wide = jnp.concatenate([vals] * (width // small), 1)
    small_ref[0, 4 * small : 4 * small + 8] = jnp.where(mine, wide, 0.0).astype(BF16)
    big_ref[0, :tall] = up[...]
    big_ref[0, tall:] = down[...]


def fetch_kernel(me, tokens, x_ref, xhat_ref, inv_ref, xhat_t, sem):
    own, width = x_ref.shape
    copy = pltpu.make_async_copy(tokens.at[pl.ds(lax.rem(me[0], 2) * own, own)], x_ref, sem)
    copy.start()
    ones = jnp.full((width, width), 1.0 / width, BF16)
    size = 256 if own % 256 == 0 else own
    copy.wait()
    for n in range(own // size):
        part = slice(n * size, (n + 1) * size)
        x = x_ref[part]
        center = x.astype(F32) - dot(x, ones, NN)
        inv = lax.rsqrt(dot((center * center).astype(BF16), ones, NN) + 1e-05)
        xhat = center * inv
        xhat_ref[part] = xhat
        inv_ref[part] = inv[:, :1]
        xhat_t[:, part] = xhat.astype(BF16).T


def turn_kernel(me, cot, cot_ref, cot_t, sem):
    own = cot_ref.shape[0]
    copy = pltpu.make_async_copy(cot.at[pl.ds(lax.rem(me[0], 2) * own, own)], cot_ref, sem)
    copy.start()
    size = 256 if own % 256 == 0 else own
    copy.wait()
    for n in range(own // size):
        part = slice(n * size, (n + 1) * size)
        cot_t[:, part] = cot_ref[part].T


def attend_kernel(
    per, me, virt, lens, live, x_ref, xhat_ref, held, got,
    qkv_ref, prob_ref, o_ref, x1_ref, wqkv, wout, vec,
):
    tokens, width = x_ref.shape
    rows = tokens // WIN
    hs = width // HEADS
    here = twist(virt[0] // 4)
    y_own = (virt[0] // 2) % 2
    first = virt[0] % 2 == 0
    total = jnp.zeros((8, width), F32)
    for m in range(CHIPS):
        k = spot(m, twist) ^ (here + y_own * VDP)
        a = held[k].astype(F32)
        b = got[k].astype(F32)
        even = jnp.where(first, a, b)
        odd = jnp.where(first, b, a)
        for part in range(3):
            both = jnp.concatenate([even[part * 8 : part * 8 + 8], odd[part * 8 : part * 8 + 8]], 0)
            wqkv[m * 16 : m * 16 + 16, part * width : (part + 1) * width] = both.astype(BF16)
        both = jnp.concatenate([even[24:32], odd[24:32]], 0)
        wout[m * 16 : m * 16 + 16] = both.astype(BF16)
        total = total + a[32:40] + b[32:40]
    vec[...] = total
    scale = hs**-0.5
    ii = lax.broadcasted_iota(jnp.int32, (WIN, WIN), 0)
    jj = lax.broadcasted_iota(jnp.int32, (WIN, WIN), 1)
    same = ii == jj
    image_rows = live.shape[1]
    base = lax.rem(me[0], 2) * rows

    def enter(c):
        part = slice(c * per * WIN, (c + 1) * per * WIN)
        h1 = (xhat_ref[part] * total[0:1] + total[2:3]).astype(BF16)
        qkv = dot(h1, wqkv[...], NN).astype(BF16)
        qkv_ref[part] = qkv
        scores = []
        for r in range(per):
            at = slice(r * WIN, (r + 1) * WIN)
            for h in range(HEADS):
                q = qkv[at, h * hs : (h + 1) * hs]
                k = qkv[at, width + h * hs : width + (h + 1) * hs]
                scores.append(dot(q, k, NT))
        return qkv, scores

    ahead = enter(0)
    for c in range(rows // per):
        qkv, scores = ahead
        if c + 1 < rows // per:
            ahead = enter(c + 1)
        part = slice(c * per * WIN, (c + 1) * per * WIN)
        probs = []
        for r in range(per):
            row = base + c * per + r
            image = row // image_rows
            inside = row - image * image_rows
            reach = jnp.where(live[image, inside] == 1, lens[image] - inside * WIN, 0)
            allowed = same | (jj < jnp.minimum(ii, reach))
            for h in range(HEADS):
                s = jnp.where(allowed, scores[r * HEADS + h], -1e30)
                e = jnp.exp((s - jnp.max(s, -1, keepdims=True)) * scale)
                probs.append((e * (1.0 / jnp.sum(e, -1, keepdims=True))).astype(BF16))
        mixed = []
        for r in range(per):
            at = slice(r * WIN, (r + 1) * WIN)
            heads = []
            for h in range(HEADS):
                v = qkv[at, 2 * width + h * hs : 2 * width + (h + 1) * hs]
                heads.append(dot(probs[r * HEADS + h], v, NN).astype(BF16))
            mixed.append(jnp.concatenate(heads, 1))
        o = jnp.concatenate(mixed, 0)
        for n, p in enumerate(probs):
            prob_ref[c * per * HEADS + n] = p
        o_ref[part] = o
        x1_ref[part] = x_ref[part].astype(F32) + dot(o, wout[...], NN)


def join(virt, blocks, n, up, down_t):
    tall = blocks.shape[1] // 2
    width = up.shape[0]
    here = turn(virt[0] // 4)
    for i in range(VDP):
        k = turn(i) ^ here
        at = slice(i * tall, (i + 1) * tall)
        cols = slice(n * width, (n + 1) * width)
        up[at, cols] = blocks[k, :tall]
        down_t[at, cols] = blocks[k, tall:]


def hidden_units(h2, dyb, up, down_t):
    u = dot(h2, up[...], NN).astype(BF16)
    da = dot(dyb, down_t[...], NN).astype(BF16)
    a, slope = gelu_both(u)
    return a, da * slope


def hidden_near_kernel(
    per, start, virt, x1_ref, cot_ref, vec, own, got, *refs,
):
    if start:
        h2_first, a_first, du_first, cot_t = refs[:4]
        refs = refs[4:]
    h2_ref, xhat_ref, inv_ref, f_ref, dh2_ref = refs[:5]
    a_ref, du_ref, up, down_t, up_t, down = refs[-6:]
    width = x1_ref.shape[1]
    tokens = h2_ref.shape[0]
    size = per * WIN
    join(virt, own, 0, up, down_t)
    join(virt, got, 1, up, down_t)
    up_t[...] = up[...].T
    down[...] = down_t[...].T
    for c in range(tokens // size):
        part = slice(c * size, (c + 1) * size)
        whole = slice(start + c * size, start + (c + 1) * size)
        x1 = x1_ref[whole]
        xhat, inv = norm_parts(x1)
        xhat_ref[part] = xhat
        inv_ref[part] = inv
        h2 = (xhat * vec[1:2] + vec[3:4]).astype(BF16)
        h2_ref[part] = h2
        a, du = hidden_units(h2, cot_ref[whole], up, down_t)
        a_ref[part] = a
        du_ref[part] = du
        f_ref[part] = x1 + vec[4:5] + dot(a, down[...], NN)
        dh2_ref[part] = dot(du, up_t[...], NN)
    if not start:
        return
    keep, send = refs[5:7]
    gdown = dot(cot_t[:, :start], a_first[...], NN) + dot(cot_t[:, start:], a_ref[...], NN)
    gup = dot(h2_first[...], du_first[...], TN) + dot(h2_ref[...], du_ref[...], TN)
    tall = width // VDP
    here = turn(virt[0] // 4)
    for i in range(VDP):
        at = slice(i * tall, (i + 1) * tall)
        k = turn(i) ^ here
        keep[k, :tall] = gup[at, :width]
        keep[k, tall:] = gdown[at, :width]
        send[k, :tall] = gup[at, width:].astype(BF16)
        send[k, tall:] = gdown[at, width:].astype(BF16)


def hidden_far_kernel(
    per, virt, cot_ref, vec, own, got, *refs,
):
    firsts, seconds, o_ref = refs[:5], refs[5:10], refs[10]
    y_ref, dx1_ref, g_ref, gout, gvec, up, down_t, up_t, down = refs[11:]
    tokens, width = y_ref.shape
    size = per * WIN
    half = tokens // 2
    join(virt, own, 0, up, down_t)
    join(virt, got, 1, up, down_t)
    up_t[...] = up[...].T
    down[...] = down_t[...].T
    sums = [jnp.zeros((1, width), F32)] * 3
    for c in range(tokens // size):
        part = slice(c * size, (c + 1) * size)
        h2_ref, xhat_ref, inv_ref, f_ref, dh2_ref = firsts if c * size < half else seconds
        mine = slice(c * size % half, c * size % half + size)
        a, du = hidden_units(h2_ref[mine], cot_ref[part], up, down_t)
        y_ref[part] = (f_ref[mine] + dot(a, down[...], NN)).astype(BF16)
        dh2 = dh2_ref[mine] + dot(du, up_t[...], NN)
        dy = cot_ref[part].astype(F32)
        xhat = xhat_ref[mine]
        dx1 = dy + norm_back(dh2, xhat, inv_ref[mine], vec[1:2])
        dx1_ref[part] = dx1
        g_ref[part] = dx1.astype(BF16)
        for n, term in enumerate((dh2 * xhat, dh2, dy)):
            sums[n] = sums[n] + jnp.sum(term, 0, keepdims=True)
    gout[...] = dot(o_ref[...], g_ref[...], TN)
    zero = jnp.zeros((1, width), F32)
    gvec[...] = jnp.concatenate([zero, sums[0], zero, sums[1], sums[2], zero, zero, zero], 0)


def own_rows(virt, i, other):
    core = virt[0] % 2
    core = 1 - core if other else core
    return pl.ds(pl.multiple_of(i * 32 + ((virt[0] // 2) % 2) * 16 + core * 8, 8), 8)


def back_kernel(
    per, virt, qkv_ref, prob_ref, g_ref, xhat_t, wqkv, wout, vec, gout, gvec,
    dqkv, keep, send,
    gqkv,
):
    tokens, width = g_ref.shape
    hs = width // HEADS
    scale = hs**-0.5
    every = [(r, h) for r in range(tokens // WIN) for h in range(HEADS)]
    groups = [every[n : n + 2 * per] for n in range(0, len(every), 2 * per)]

    def piece(ref, r, h, part=0):
        return ref[r * WIN : (r + 1) * WIN, part * width + h * hs : part * width + (h + 1) * hs]

    def enter(pairs):
        r = pairs[0][0]
        do = dot(g_ref[r * WIN : (r + per) * WIN], wout[...], NT).astype(BF16)
        dos = [do[(n - r) * WIN : (n - r + 1) * WIN, h * hs : (h + 1) * hs] for n, h in pairs]
        probs = [prob_ref[r * HEADS + h] for r, h in pairs]
        dps = [dot(a, piece(qkv_ref, r, h, 2), NT) for a, (r, h) in zip(dos, pairs)]
        dvs = [dot(p, a, TN).astype(BF16) for p, a in zip(probs, dos)]
        return probs, dps, dvs

    ahead = enter(groups[0])
    for place, pairs in enumerate(groups):
        probs, dps, dvs = ahead
        if place + 1 < len(groups):
            ahead = enter(groups[place + 1])
        dss = []
        for p, dp in zip(probs, dps):
            pf = p.astype(F32)
            ds = pf * (dp - jnp.sum(dp * pf, -1, keepdims=True)) * scale
            dss.append(ds.astype(BF16))
        dqs = [dot(ds, piece(qkv_ref, r, h, 1), NN).astype(BF16) for ds, (r, h) in zip(dss, pairs)]
        dks = [dot(ds, piece(qkv_ref, r, h, 0), TN).astype(BF16) for ds, (r, h) in zip(dss, pairs)]
        for n, (r, h) in enumerate(pairs):
            for part, values in enumerate((dqs, dks, dvs)):
                at = slice(part * width + h * hs, part * width + (h + 1) * hs)
                dqkv[r * WIN : (r + 1) * WIN, at] = values[n]
    grad = dot(xhat_t[...], dqkv[...], NN)
    total = jnp.zeros((1, 3 * width), F32)
    for r in range(tokens // WIN):
        total = total + jnp.sum(dqkv[r * WIN : (r + 1) * WIN].astype(F32), 0, keepdims=True)
    w = wqkv[...].astype(F32)
    cols = jnp.concatenate([
        jnp.broadcast_to(jnp.sum(w * grad, -1, keepdims=True), (width, 64)),
        jnp.broadcast_to(jnp.sum(w * total, -1, keepdims=True), (width, 64)),
    ], 1)
    lines = cols.T
    gain, from_total = lines[0:1], lines[64:65]
    vec_t = vec[...].T
    gqkv[...] = grad * vec_t[:, 0:1] + total * vec_t[:, 2:3]
    rest = gvec[...]
    sums = jnp.concatenate([gain, rest[1:2], from_total, rest[3:]], 0)
    here = twist(virt[0] // 4)
    for i in range(VDP):
        k = twist(i) ^ here
        mine, other = own_rows(virt, i, 0), own_rows(virt, i, 1)
        theirs = []
        for part in range(3):
            at = slice(part * width, (part + 1) * width)
            keep[k, part * 8 : part * 8 + 8] = gqkv[mine, at]
            theirs.append(gqkv[other, at])
        keep[k, 24:32] = gout[mine]
        keep[k, 32:] = sums
        send[k] = jnp.concatenate(theirs + [gout[other], sums], 0).astype(BF16)


def token_grad_kernel(per, me, dqkv, wqkv, vec, xhat_ref, inv_ref, dx1_ref, y, y_near, gx, gxb, out, sems):
    own = dqkv.shape[0]
    size = per * WIN
    copies = []
    for n, source in enumerate((y, y_near)):
        at = pl.ds((lax.rem(me[0], 2) ^ n) * own, own)
        copies.append(pltpu.make_async_copy(source, out.at[at], sems.at[n]))
        copies[-1].start()
    for c in range(own // size):
        part = slice(c * size, (c + 1) * size)
        dh1 = dot(dqkv[part], wqkv[...], NT)
        values = dx1_ref[part] + norm_back(dh1, xhat_ref[part], inv_ref[part], vec[0:1])
        gx[part] = values
        gxb[part] = values.astype(BF16)
    for copy in copies:
        copy.wait()


def place_kernel(per, me, mine, theirs, out, wide, sems):
    own = theirs.shape[0]
    size = per * WIN
    here = lax.rem(me[0], 2) * own
    copies = [pltpu.make_async_copy(mine, out.at[pl.ds(here, own)], sems.at[own // size])]
    copies[0].start()
    for c in range(own // size):
        part = pl.ds(c * size, size)
        wide[part] = theirs[part].astype(F32)
        at = pl.ds(own - here + c * size, size)
        copies.append(pltpu.make_async_copy(wide.at[part], out.at[at], sems.at[c]))
        copies[-1].start()
    for copy in copies:
        copy.wait()


def finish_kernel(me, keep, one, two, three, keep_b, got_b, qkv, out, gains, biases, up, down):
    total = keep[0]
    for got in (one, two, three):
        total = total + got[...].astype(F32)
    small, width = out.shape
    for part in range(3):
        qkv[:, part * width : (part + 1) * width] = total[part * small : (part + 1) * small]
    out[...] = total[3 * small : 4 * small]
    vec = pltpu.roll(total[4 * small :], width - me[0] * small, 1)[:, :small]
    gains[...] = vec[:2]
    biases[...] = vec[2:5]
    total = keep_b[0] + got_b[0].astype(F32)
    tall = up.shape[0]
    up[...] = total[:tall]
    down[...] = total[tall:]


def swap(block, axis, bit):
    size = lax.axis_size(axis)
    return lax.ppermute(block, axis, [(i, i ^ bit) for i in range(size)])


def steps_of(axis):
    return [(axis, 1 << k) for k in reversed(range(lax.axis_size(axis).bit_length() - 1))]


def after(value, other):
    return lax.optimization_barrier((value, other))[0]


def halves(held):
    half = held.shape[0] // 2
    return held[:half], held[half:].astype(BF16)


def fold_step(keep, send, axis, bit, past=None):
    got = swap(send, axis, bit)
    return keep + (got if past is None else after(got, past)).astype(F32)


def bit_reverse(index, count):
    out = 0 * index
    for k in range(count):
        out = out | (((index >> k) & 1) << (count - 1 - k))
    return out


def by_device(block, me):
    blocks = block[None]
    for axis, bit in steps_of("dp") + steps_of("tensor"):
        blocks = jnp.concatenate([blocks, swap(blocks, axis, bit)], 0)
    count = blocks.shape[0]
    order = jnp.arange(count, dtype=jnp.int32) ^ me
    return jnp.take(blocks, bit_reverse(order, count.bit_length() - 1), axis=0)


def other_pack(w_qkv, w_out, gains, biases, w_up, w_down, me):
    small, width = w_out.shape
    qkv = w_qkv.reshape(small, 3, width).transpose(1, 0, 2).reshape(3 * small, width)
    rows = jnp.concatenate([gains, biases], 0)
    place = jnp.zeros((8, width), BF16)
    place = lax.dynamic_update_slice(place, rows, (jnp.int32(0), me * small))
    return jnp.concatenate([qkv, w_out, place], 0), jnp.concatenate([w_up, w_down.T], 0)


def other_blocks(a, b, me, n_dp, n_t):
    a = by_device(a, me)
    b = by_device(b, me)
    width = a.shape[2]
    count = n_dp * n_t
    small = width // count
    big = width // (VDP * VT)
    mats = a[:, : 4 * small].reshape(count, 4, small, width).transpose(1, 0, 2, 3)
    mats = mats.reshape(4, VDP * VT, big, width).transpose(1, 0, 2, 3).reshape(VDP * VT, 4 * big, width)
    vec = jnp.sum(a[:, 4 * small :].astype(F32), 0).astype(BF16)
    vecs = jnp.concatenate([vec[None], jnp.zeros((VDP * VT - 1, 8, width), BF16)], 0)
    a = jnp.concatenate([mats, vecs], 1)
    tall = width // n_dp
    b = b.reshape(n_dp, VT, 2, tall, width).transpose(1, 2, 0, 3, 4)
    b = b.reshape(VT, 2, VDP, width // VDP, width).transpose(2, 0, 1, 3, 4)
    b = b.reshape(VDP * VT, 2 * (width // VDP), width)

    y_own = (me // 2) % 2

    def placed(blocks, order):
        pairs = blocks.reshape((CHIPS, 2) + blocks.shape[1:])
        chips = sorted(range(CHIPS), key=lambda m: spot(m, order))
        pairs = jnp.stack([pairs[m] for m in chips], 0)
        pairs = jnp.where(y_own == 1, jnp.roll(pairs, VDP, 0), pairs)
        return pairs[:, 0], pairs[:, 1]

    return placed(a, twist) + placed(b, turn)


def other_reduce(pair_a, pair_b, me, n_dp, n_t):
    count = n_dp * n_t
    y_own = (me // 2) % 2

    def whole(keep, send, order):
        pairs = jnp.stack([keep, send.astype(F32)], 1)
        pairs = jnp.stack([pairs[order(i)] for i in range(VDP)], 0)
        none = jnp.zeros_like(pairs)
        both = jnp.stack([jnp.where(y_own == y, pairs, none) for y in range(2)], 1)
        return both.reshape((VDP * VT,) + keep.shape[1:])

    def rows_of(blocks, parts):
        big = blocks.shape[1] // parts
        mats = blocks.reshape(VDP * VT, parts, big, -1).transpose(1, 0, 2, 3)
        mats = mats.reshape(parts, count, VDP * VT * big // count, -1).transpose(1, 0, 2, 3)
        return mats.reshape(count, -1, blocks.shape[2])

    def vec_of(blocks):
        picked = jnp.where(y_own == 0, blocks[0], 0.0)
        return jnp.broadcast_to(picked[None], (count,) + picked.shape)

    a, b = whole(*pair_a, twist), whole(*pair_b, turn)
    width = a.shape[2]
    tall, high = width // n_dp, width // VDP
    cols = b.reshape(VDP, VT, 2, high, width).transpose(1, 2, 0, 3, 4)
    cols = cols.reshape(VT, 2, n_dp, tall, width).transpose(2, 0, 1, 3, 4)
    cols = cols.reshape(count, 2 * tall, width)
    a = jnp.concatenate([rows_of(a[:, :32], 4), vec_of(a[:, 32:])], 1)
    results = []
    for blocks in (a, cols):
        blocks = jnp.take(blocks, jnp.arange(count, dtype=jnp.int32) ^ me, axis=0)
        for axis, bit in reversed(steps_of("dp") + steps_of("tensor")):
            pairs = blocks.reshape((-1, 2) + blocks.shape[1:])
            got = swap(pairs[:, 1].astype(BF16), axis, bit)
            blocks = pairs[:, 0] + got.astype(F32)
        results.append(blocks[0])
    return results


def struct(shape, dtype):
    return jax.ShapeDtypeStruct(shape, dtype)


def call(kernel, name, args, outs, scratch=(), flops=0, limit=8, hbm_outs=True):
    args = [a if isinstance(a, tuple) else (a, pltpu.VMEM) for a in args]
    moved = sum(a.size * a.dtype.itemsize for a, _ in args)
    spaces = [pl.ANY if hbm_outs and isinstance(o, jax.ShapeDtypeStruct) else pltpu.VMEM for o in outs]
    return pl.pallas_call(
        kernel,
        name=name,
        out_shape=outs,
        in_specs=[pl.BlockSpec(memory_space=space) for _, space in args],
        out_specs=[pl.BlockSpec(memory_space=space) for space in spaces],
        scratch_shapes=list(scratch),
        compiler_params=pltpu.CompilerParams(vmem_limit_bytes=limit * MIB),
        cost_estimate=pl.CostEstimate(flops=flops, bytes_accessed=moved, transcendentals=0),
    )(*[a for a, _ in args])


def on_device(tokens, lengths, row_mask, cotangent, w_qkv, w_out, gains, biases, w_up, w_down):
    images, seq_len, width = tokens.shape
    n_dp, n_t = lax.axis_size("dp"), lax.axis_size("tensor")
    index = lax.axis_index("dp") * n_t + lax.axis_index("tensor")
    me = index.astype(jnp.int32).reshape(1)
    usual = (n_dp, n_t) == (VDP, VT)
    virt = me if usual else (index // 2 % 2 * 2).astype(jnp.int32).reshape(1)
    small = width // (n_dp * n_t)
    tall = width // n_dp
    own = images * seq_len // 2
    rows = own // WIN
    per = 12 if rows % 12 == 0 else 1
    less = 4 if rows % 4 == 0 else 1
    smem = pltpu.SMEM
    weights = (w_qkv, w_out, gains, biases, w_up, w_down)
    token_mm = 2 * own * width
    hbm = pltpu.HBM

    def in_hbm(array):
        return (pltpu.with_memory_space_constraint(array, hbm), hbm)

    def fetch(me):
        return call(
            fetch_kernel,
            "fetch",
            [(me, smem), in_hbm(tokens.reshape(images * seq_len, width))],
            [
                pltpu.VMEM((own, width), BF16),
                pltpu.VMEM((own, width), F32),
                pltpu.VMEM((own, 1), F32),
                pltpu.VMEM((width, own), BF16),
            ],
            [pltpu.SemaphoreType.DMA(())],
            limit=4,
        )

    def fetch_turned(me):
        return call(
            turn_kernel,
            "turn",
            [(me, smem), in_hbm(cotangent.reshape(images * seq_len, width))],
            [pltpu.VMEM((own, width), BF16), pltpu.VMEM((width, own), BF16)],
            [pltpu.SemaphoreType.DMA(())],
            limit=4,
        )

    if usual:
        weights = (w_qkv, w_out, gains, biases, w_up, w_down.T)
        pack_a, pack_b = call(
            pack_kernel,
            "pack",
            [(me, smem)] + [in_hbm(w) for w in weights],
            [
                pltpu.VMEM((1, 4 * small + 8, width), BF16),
                pltpu.VMEM((1, 2 * tall, width), BF16),
            ],
            [pltpu.VMEM(w.shape, BF16) for w in weights] + [pltpu.SemaphoreType.DMA((6,))],
        )
        b = pack_b
        held_a = jnp.concatenate([pack_a] + [swap(pack_a, "dp", bit) for bit in (2, 4, 6)], 0)
        b = jnp.concatenate([b, swap(b, "dp", 4)], 0)
        b = after(b, held_a)
        held_a = jnp.concatenate([held_a, after(swap(held_a, "dp", 1), b)], 0)
        b = jnp.concatenate([b, swap(b, "dp", 2)], 0)
        b = after(b, held_a)
        x, xhat1, inv1, xhat_t = fetch(after(me, held_a))
        held_a = jnp.concatenate([held_a, after(swap(held_a, "tensor", 2), (b, xhat1))], 0)
        b = jnp.concatenate([b, swap(b, "dp", 1)], 0)
        far_b = swap(b, "tensor", 2)
        cot, cot_t = fetch_turned(after(me, held_a))
        got_a = after(swap(held_a, "tensor", 1), cot)
        got_b = swap(after(b, held_a), "tensor", 1)
    else:
        held_a, got_a, held_b, got_b = other_blocks(*other_pack(*weights, index), index, n_dp, n_t)
        b, far_b = held_b[:VDP], held_b[VDP:]
        got_b, got_far = got_b[:VDP], got_b[VDP:]
        x, xhat1, inv1, xhat_t = fetch(me)
        cot, cot_t = fetch_turned(me)
    qkv, prob, o, x1, wqkv, wout, vec = call(
        functools.partial(attend_kernel, per),
        "attend",
        [(me, smem), (virt, smem), (lengths, smem), (row_mask, smem), x, xhat1, held_a, got_a],
        [
            pltpu.VMEM((own, 3 * width), BF16),
            pltpu.VMEM((rows * HEADS, WIN, WIN), BF16),
            pltpu.VMEM((own, width), BF16),
            pltpu.VMEM((own, width), F32),
            pltpu.VMEM((width, 3 * width), BF16),
            pltpu.VMEM((width, width), BF16),
            pltpu.VMEM((8, width), F32),
        ],
        flops=token_mm * (4 * width + 2 * WIN),
    )
    tall_b = 2 * (width // VDP)
    mats = [pltpu.VMEM((width, 2 * width), BF16)] * 2 + [pltpu.VMEM((2 * width, width), BF16)] * 2
    half = own // 2
    wide_per = 6 if rows % 12 == 0 else 1
    units = [
        pltpu.VMEM((half, width), BF16),
        pltpu.VMEM((half, width), F32),
        pltpu.VMEM((half, 1), F32),
        pltpu.VMEM((half, width), F32),
        pltpu.VMEM((half, width), F32),
        pltpu.VMEM((half, 2 * width), BF16),
        pltpu.VMEM((half, 2 * width), BF16),
    ]
    *first, a_first, du_first = call(
        functools.partial(hidden_near_kernel, wide_per, 0),
        "hidden_first",
        [(virt, smem), x1, cot, vec, b, got_b],
        units,
        mats,
        token_mm * 4 * width,
    )
    if usual:
        far_b = after(far_b, first[0])
        got_far = swap(far_b, "tensor", 1)
    *second, keep_b, send_b = call(
        functools.partial(hidden_near_kernel, wide_per, half),
        "hidden_second",
        [(virt, smem), x1, cot, after(vec, far_b), b, got_b, first[0], a_first, du_first, cot_t],
        units[:5] + [pltpu.VMEM((VDP, tall_b, width), F32), pltpu.VMEM((VDP, tall_b, width), BF16)],
        units[5:] + mats,
        token_mm * 8 * width,
    )
    y, dx1, g, gout, gvec = call(
        functools.partial(hidden_far_kernel, wide_per),
        "hidden_far",
        [(virt, smem), cot, vec, far_b, got_far, *first, *second, o],
        [
            pltpu.VMEM((own, width), BF16),
            pltpu.VMEM((own, width), F32),
            pltpu.VMEM((own, width), BF16),
            pltpu.VMEM((width, width), F32),
            pltpu.VMEM((8, width), F32),
        ],
        mats,
        token_mm * 9 * width,
    )
    core, xbit, zlo, zhi = ("tensor", 1), ("dp", 1), ("dp", 2), ("dp", 4)
    if usual:
        held_b = fold_step(keep_b, send_b, *core, g)
        y = after(y, held_b)
    y_near = swap(y, "tensor", 1)
    dqkv, keep_a, send_a = call(
        functools.partial(back_kernel, per),
        "back",
        [(virt, smem), qkv, prob, g, xhat_t, wqkv, wout, vec, gout, gvec],
        [
            pltpu.VMEM((own, 3 * width), BF16),
            pltpu.VMEM((VDP, 40, width), F32),
            pltpu.VMEM((VDP, 40, width), BF16),
        ],
        [pltpu.VMEM((width, 3 * width), F32)],
        token_mm * (4 * width + 5 * WIN),
    )
    if usual:
        held_b = fold_step(*halves(held_b), *xbit)
        vec = after(vec, held_b)
    gx, gxb, layer_out = call(
        functools.partial(token_grad_kernel, less),
        "token_grad",
        [(me, smem), dqkv, wqkv, vec, xhat1, inv1, dx1, y, y_near],
        [
            pltpu.VMEM((own, width), F32),
            pltpu.VMEM((own, width), BF16),
            struct((images * seq_len, width), BF16),
        ],
        [pltpu.SemaphoreType.DMA((2,))],
        flops=token_mm * 3 * width,
    )
    layer_out = layer_out.reshape(images, seq_len, width)

    def place(gx_near):
        return call(
            functools.partial(place_kernel, less),
            "place",
            [(me, smem), gx, gx_near],
            [struct((images * seq_len, width), F32)],
            [pltpu.VMEM((own, width), F32), pltpu.SemaphoreType.DMA((rows // less + 1,))],
        )[0].reshape(images, seq_len, width)

    if usual:
        held_a = fold_step(keep_a, send_a, *core, gxb)
        grad_tokens = place(swap(after(gxb, held_a), "tensor", 1))
        keep, send = halves(held_b)
        held_b = fold_step(keep, after(send, held_a), *zlo)
        held_a = fold_step(*halves(held_a), *xbit)
        got_b = swap(halves(held_b)[1], *zhi)
        low = held_a.astype(BF16)
        got = [swap(low[n], "dp", 2 * n) for n in range(1, 4)]
        got[2] = after(got[2], (grad_tokens, got_b))
        shapes = ((small, 3 * width), (small, width), (2, small), (3, small), (tall, width), (tall, width))
        o_qkv, o_out, o_gains, o_bias, o_up, o_down = call(
            finish_kernel,
            "finish",
            [(me, smem), held_a, *got, held_b, got_b],
            [struct(shape, F32) for shape in shapes],
            limit=2,
            hbm_outs=False,
        )
    else:
        grad_tokens = place(swap(gxb, "tensor", 1))
        grad_a, grad_b = other_reduce((keep_a, send_a), (keep_b, send_b), index, n_dp, n_t)
        o_qkv = jnp.concatenate([grad_a[p * small : (p + 1) * small] for p in range(3)], 1)
        o_out = grad_a[3 * small : 4 * small]
        o_vec = lax.dynamic_slice_in_dim(grad_a[4 * small : 4 * small + 5], index * small, small, 1)
        o_gains, o_bias = o_vec[:2], o_vec[2:]
        o_up, o_down = grad_b[:tall], grad_b[tall:]
    return layer_out, grad_tokens, o_qkv, o_out, o_gains, o_bias, o_up, o_down.T


def solution(mesh):
    in_specs = (
        P("dp", None, None),
        P("dp"),
        P("dp", None),
        P("dp", None, None),
        P(("dp", "tensor"), None),
        P(("dp", "tensor"), None),
        P(None, ("dp", "tensor")),
        P(None, ("dp", "tensor")),
        P("dp", "tensor"),
        P("tensor", "dp"),
    )
    out_specs = (
        P("dp", None, None),
        P("dp", None, None),
        P(("dp", "tensor"), None),
        P(("dp", "tensor"), None),
        P(None, ("dp", "tensor")),
        P(None, ("dp", "tensor")),
        P("dp", "tensor"),
        P("tensor", "dp"),
    )
    return jax.shard_map(
        on_device, mesh=mesh, in_specs=in_specs, out_specs=out_specs, check_vma=False
    )
```

```python
import functools

import jax
import jax.numpy as jnp
from jax import lax
from jax.experimental import pallas as pl
from jax.experimental.pallas import tpu as pltpu
from jax.sharding import PartitionSpec as P

HEADS = 2
WIN = 96
F32 = jnp.float32
BF16 = jnp.bfloat16
VDP, VT = 8, 4
CHIPS = VDP * VT // 2
MIB = 1 << 20

NN = ((1,), (0,))
NT = ((1,), (1,))
TN = ((0,), (0,))


def dot(a, b, dims):
    return lax.dot_general(a, b, (dims, ((), ())), preferred_element_type=F32)


def twist(i):
    return (i & 1) * 4 + (i >> 1)


def spot(m):
    return (m % 2) * VDP + twist(m // 2)


def norm_parts(values):
    center = values - jnp.mean(values, -1, keepdims=True)
    inv = lax.rsqrt(jnp.mean(center * center, -1, keepdims=True) + 1e-05)
    return center * inv, inv


def norm_back(grad, xhat, inv, gain):
    scaled = grad * gain
    return inv * (
        scaled
        - jnp.mean(scaled, -1, keepdims=True)
        - xhat * jnp.mean(scaled * xhat, -1, keepdims=True)
    )


def gelu_both(u):
    c = 0.7978845608028654
    u2 = u * u
    t = jnp.tanh(u * (c + (c * 0.044715) * u2))
    half = 0.5 + 0.5 * t
    value = u * half
    slope = half + (value - value * half) * (2 * c + (6 * c * 0.044715) * u2)
    return value, slope


def pack_kernel(me, *refs):
    sources, packed, held, sems = refs[:6], refs[6], refs[7:13], refs[13]
    copies = [pltpu.make_async_copy(a, b, sems.at[n]) for n, (a, b) in enumerate(zip(sources, held))]
    for copy in copies:
        copy.start()
    qkv, out, gains, biases, up, down = held
    small, width = out.shape
    tall = up.shape[0]
    lane = lax.broadcasted_iota(jnp.int32, (1, width), 1)
    mine = lane // small == me[0]
    for copy in copies:
        copy.wait()
    for part in range(3):
        packed[0, part * small : (part + 1) * small] = qkv[:, part * width : (part + 1) * width]
    packed[0, 3 * small : 4 * small] = out[...]
    rows = [gains[0:1], gains[1:2], biases[0:1], biases[1:2], biases[2:3]]
    vals = jnp.concatenate(rows + [jnp.zeros((3, small), BF16)], 0).astype(F32)
    wide = jnp.concatenate([vals] * (width // small), 1)
    at = 4 * small + 8
    packed[0, 4 * small : at] = jnp.where(mine, wide, 0.0).astype(BF16)
    packed[0, at : at + tall] = up[...]
    packed[0, at + tall :] = down[...]


def fetch_kernel(me, tokens, x_ref, xhat_ref, inv_ref, xhat_t, sem):
    own, width = x_ref.shape
    copy = pltpu.make_async_copy(tokens.at[pl.ds(lax.rem(me[0], 2) * own, own)], x_ref, sem)
    copy.start()
    ones = jnp.full((width, width), 1.0 / width, BF16)
    size = 256 if own % 256 == 0 else own
    copy.wait()
    for n in range(own // size):
        part = slice(n * size, (n + 1) * size)
        x = x_ref[part]
        center = x.astype(F32) - dot(x, ones, NN)
        inv = lax.rsqrt(dot((center * center).astype(BF16), ones, NN) + 1e-05)
        xhat = center * inv
        xhat_ref[part] = xhat
        inv_ref[part] = inv[:, :1]
        xhat_t[:, part] = xhat.astype(BF16).T


def turn_kernel(me, cot, cot_ref, cot_t, sem):
    own = cot_ref.shape[0]
    copy = pltpu.make_async_copy(cot.at[pl.ds(lax.rem(me[0], 2) * own, own)], cot_ref, sem)
    copy.start()
    size = 256 if own % 256 == 0 else own
    copy.wait()
    for n in range(own // size):
        part = slice(n * size, (n + 1) * size)
        cot_t[:, part] = cot_ref[part].T


def attend_kernel(
    per, me, virt, lens, live, x_ref, xhat_ref, held, got,
    qkv_ref, prob_ref, o_ref, x1_ref, wqkv, wout, vec,
):
    tokens, width = x_ref.shape
    rows = tokens // WIN
    hs = width // HEADS
    here = twist(virt[0] // 4)
    y_own = (virt[0] // 2) % 2
    first = virt[0] % 2 == 0
    total = jnp.zeros((8, width), F32)
    for m in range(CHIPS):
        k = spot(m) ^ (here + y_own * VDP)
        a = held[k].astype(F32)
        b = got[k].astype(F32)
        even = jnp.where(first, a, b)
        odd = jnp.where(first, b, a)
        for part in range(3):
            both = jnp.concatenate([even[part * 8 : part * 8 + 8], odd[part * 8 : part * 8 + 8]], 0)
            wqkv[m * 16 : m * 16 + 16, part * width : (part + 1) * width] = both.astype(BF16)
        both = jnp.concatenate([even[24:32], odd[24:32]], 0)
        wout[m * 16 : m * 16 + 16] = both.astype(BF16)
        total = total + a[32:40] + b[32:40]
    vec[...] = total
    scale = hs**-0.5
    ii = lax.broadcasted_iota(jnp.int32, (WIN, WIN), 0)
    jj = lax.broadcasted_iota(jnp.int32, (WIN, WIN), 1)
    same = ii == jj
    image_rows = live.shape[1]
    base = lax.rem(me[0], 2) * rows

    def enter(c):
        part = slice(c * per * WIN, (c + 1) * per * WIN)
        h1 = (xhat_ref[part] * total[0:1] + total[2:3]).astype(BF16)
        qkv = dot(h1, wqkv[...], NN).astype(BF16)
        qkv_ref[part] = qkv
        scores = []
        for r in range(per):
            at = slice(r * WIN, (r + 1) * WIN)
            for h in range(HEADS):
                q = qkv[at, h * hs : (h + 1) * hs]
                k = qkv[at, width + h * hs : width + (h + 1) * hs]
                scores.append(dot(q, k, NT))
        return qkv, scores

    ahead = enter(0)
    for c in range(rows // per):
        qkv, scores = ahead
        if c + 1 < rows // per:
            ahead = enter(c + 1)
        part = slice(c * per * WIN, (c + 1) * per * WIN)
        probs = []
        for r in range(per):
            row = base + c * per + r
            image = row // image_rows
            inside = row - image * image_rows
            reach = jnp.where(live[image, inside] == 1, lens[image] - inside * WIN, 0)
            allowed = same | (jj < jnp.minimum(ii, reach))
            for h in range(HEADS):
                s = jnp.where(allowed, scores[r * HEADS + h], -1e30)
                e = jnp.exp((s - jnp.max(s, -1, keepdims=True)) * scale)
                probs.append((e * (1.0 / jnp.sum(e, -1, keepdims=True))).astype(BF16))
        mixed = []
        for r in range(per):
            at = slice(r * WIN, (r + 1) * WIN)
            heads = []
            for h in range(HEADS):
                v = qkv[at, 2 * width + h * hs : 2 * width + (h + 1) * hs]
                heads.append(dot(probs[r * HEADS + h], v, NN).astype(BF16))
            mixed.append(jnp.concatenate(heads, 1))
        o = jnp.concatenate(mixed, 0)
        for n, p in enumerate(probs):
            prob_ref[c * per * HEADS + n] = p
        o_ref[part] = o
        x1_ref[part] = x_ref[part].astype(F32) + dot(o, wout[...], NN)


def join(virt, blocks, n, up, down_t):
    tall = blocks.shape[1] // 2
    width = up.shape[0]
    here = twist(virt[0] // 4)
    for i in range(VDP):
        k = twist(i) ^ here
        at = slice(i * tall, (i + 1) * tall)
        cols = slice(n * width, (n + 1) * width)
        up[at, cols] = blocks[k, :tall]
        down_t[at, cols] = blocks[k, tall:]


def hidden_units(h2, dyb, up, down_t):
    u = dot(h2, up[...], NN).astype(BF16)
    da = dot(dyb, down_t[...], NN).astype(BF16)
    a, slope = gelu_both(u)
    return a, da * slope


def hidden_near_kernel(
    per, virt, x1_ref, cot_ref, cot_t, vec, own, got,
    h2_ref, xhat_ref, inv_ref, f_ref, dh2_ref, keep, send,
    a_ref, du_ref, up, down_t, up_t, down,
):
    tokens, width = x1_ref.shape
    size = per * WIN
    join(virt, own, 0, up, down_t)
    join(virt, got, 1, up, down_t)
    up_t[...] = up[...].T
    down[...] = down_t[...].T
    for c in range(tokens // size):
        part = slice(c * size, (c + 1) * size)
        x1 = x1_ref[part]
        xhat, inv = norm_parts(x1)
        xhat_ref[part] = xhat
        inv_ref[part] = inv
        h2 = (xhat * vec[1:2] + vec[3:4]).astype(BF16)
        h2_ref[part] = h2
        a, du = hidden_units(h2, cot_ref[part], up, down_t)
        a_ref[part] = a
        du_ref[part] = du
        f_ref[part] = x1 + vec[4:5] + dot(a, down[...], NN)
        dh2_ref[part] = dot(du, up_t[...], NN)
    gdown = dot(cot_t[...], a_ref[...], NN)
    gup = dot(h2_ref[...], du_ref[...], TN)
    tall = width // VDP
    here = twist(virt[0] // 4)
    for i in range(VDP):
        at = slice(i * tall, (i + 1) * tall)
        k = twist(i) ^ here
        keep[k, :tall] = gup[at, :width]
        keep[k, tall:] = gdown[at, :width]
        send[k, :tall] = gup[at, width:].astype(BF16)
        send[k, tall:] = gdown[at, width:].astype(BF16)


def hidden_far_kernel(
    per, virt, cot_ref, vec, own, got, h2_ref, xhat_ref, inv_ref, f_ref, dh2_ref, o_ref,
    y_ref, dx1_ref, g_ref, gout, gvec,
    up, down_t, up_t, down,
):
    tokens, width = h2_ref.shape
    size = per * WIN
    join(virt, own, 0, up, down_t)
    join(virt, got, 1, up, down_t)
    up_t[...] = up[...].T
    down[...] = down_t[...].T
    sums = [jnp.zeros((1, width), F32)] * 3
    for c in range(tokens // size):
        part = slice(c * size, (c + 1) * size)
        a, du = hidden_units(h2_ref[part], cot_ref[part], up, down_t)
        y_ref[part] = (f_ref[part] + dot(a, down[...], NN)).astype(BF16)
        dh2 = dh2_ref[part] + dot(du, up_t[...], NN)
        dy = cot_ref[part].astype(F32)
        xhat = xhat_ref[part]
        dx1 = dy + norm_back(dh2, xhat, inv_ref[part], vec[1:2])
        dx1_ref[part] = dx1
        g_ref[part] = dx1.astype(BF16)
        for n, term in enumerate((dh2 * xhat, dh2, dy)):
            sums[n] = sums[n] + jnp.sum(term, 0, keepdims=True)
    gout[...] = dot(o_ref[...], g_ref[...], TN)
    zero = jnp.zeros((1, width), F32)
    gvec[...] = jnp.concatenate([zero, sums[0], zero, sums[1], sums[2], zero, zero, zero], 0)


def own_rows(virt, i, other):
    core = virt[0] % 2
    core = 1 - core if other else core
    return pl.ds(pl.multiple_of(i * 32 + ((virt[0] // 2) % 2) * 16 + core * 8, 8), 8)


def back_kernel(
    per, virt, qkv_ref, prob_ref, g_ref, xhat_t, wqkv, wout, vec, gout, gvec,
    dqkv, keep, send,
    gqkv,
):
    tokens, width = g_ref.shape
    hs = width // HEADS
    scale = hs**-0.5
    every = [(r, h) for r in range(tokens // WIN) for h in range(HEADS)]
    groups = [every[n : n + 2 * per] for n in range(0, len(every), 2 * per)]

    def piece(ref, r, h, part=0):
        return ref[r * WIN : (r + 1) * WIN, part * width + h * hs : part * width + (h + 1) * hs]

    def enter(pairs):
        r = pairs[0][0]
        do = dot(g_ref[r * WIN : (r + per) * WIN], wout[...], NT).astype(BF16)
        dos = [do[(n - r) * WIN : (n - r + 1) * WIN, h * hs : (h + 1) * hs] for n, h in pairs]
        probs = [prob_ref[r * HEADS + h] for r, h in pairs]
        dps = [dot(a, piece(qkv_ref, r, h, 2), NT) for a, (r, h) in zip(dos, pairs)]
        dvs = [dot(p, a, TN).astype(BF16) for p, a in zip(probs, dos)]
        return probs, dps, dvs

    ahead = enter(groups[0])
    for place, pairs in enumerate(groups):
        probs, dps, dvs = ahead
        if place + 1 < len(groups):
            ahead = enter(groups[place + 1])
        dss = []
        for p, dp in zip(probs, dps):
            pf = p.astype(F32)
            ds = pf * (dp - jnp.sum(dp * pf, -1, keepdims=True)) * scale
            dss.append(ds.astype(BF16))
        dqs = [dot(ds, piece(qkv_ref, r, h, 1), NN).astype(BF16) for ds, (r, h) in zip(dss, pairs)]
        dks = [dot(ds, piece(qkv_ref, r, h, 0), TN).astype(BF16) for ds, (r, h) in zip(dss, pairs)]
        for n, (r, h) in enumerate(pairs):
            for part, values in enumerate((dqs, dks, dvs)):
                at = slice(part * width + h * hs, part * width + (h + 1) * hs)
                dqkv[r * WIN : (r + 1) * WIN, at] = values[n]
    grad = dot(xhat_t[...], dqkv[...], NN)
    total = jnp.zeros((1, 3 * width), F32)
    for r in range(tokens // WIN):
        total = total + jnp.sum(dqkv[r * WIN : (r + 1) * WIN].astype(F32), 0, keepdims=True)
    w = wqkv[...].astype(F32)
    cols = jnp.concatenate([
        jnp.broadcast_to(jnp.sum(w * grad, -1, keepdims=True), (width, 64)),
        jnp.broadcast_to(jnp.sum(w * total, -1, keepdims=True), (width, 64)),
    ], 1)
    lines = cols.T
    gain, from_total = lines[0:1], lines[64:65]
    vec_t = vec[...].T
    gqkv[...] = grad * vec_t[:, 0:1] + total * vec_t[:, 2:3]
    rest = gvec[...]
    sums = jnp.concatenate([gain, rest[1:2], from_total, rest[3:]], 0)
    here = twist(virt[0] // 4)
    for i in range(VDP):
        k = twist(i) ^ here
        mine, other = own_rows(virt, i, 0), own_rows(virt, i, 1)
        theirs = []
        for part in range(3):
            at = slice(part * width, (part + 1) * width)
            keep[k, part * 8 : part * 8 + 8] = gqkv[mine, at]
            theirs.append(gqkv[other, at])
        keep[k, 24:32] = gout[mine]
        keep[k, 32:] = sums
        send[k] = jnp.concatenate(theirs + [gout[other], sums], 0).astype(BF16)


def token_grad_kernel(per, me, dqkv, wqkv, vec, xhat_ref, inv_ref, dx1_ref, y, y_near, gx, gxb, out, turned, sems):
    own = dqkv.shape[0]
    size = per * WIN
    copies = []
    for n, source in enumerate((y, y_near)):
        at = pl.ds((lax.rem(me[0], 2) ^ n) * own, own)
        copies.append(pltpu.make_async_copy(source, out.at[at], sems.at[n]))
        copies[-1].start()
    turned[...] = wqkv[...].T
    for c in range(own // size):
        part = slice(c * size, (c + 1) * size)
        dh1 = dot(dqkv[part], turned[...], NN)
        values = dx1_ref[part] + norm_back(dh1, xhat_ref[part], inv_ref[part], vec[0:1])
        gx[part] = values
        gxb[part] = values.astype(BF16)
    for copy in copies:
        copy.wait()


def place_kernel(per, me, mine, theirs, out, wide, sems):
    own = theirs.shape[0]
    size = per * WIN
    here = lax.rem(me[0], 2) * own
    copies = [pltpu.make_async_copy(mine, out.at[pl.ds(here, own)], sems.at[own // size])]
    copies[0].start()
    for c in range(own // size):
        part = pl.ds(c * size, size)
        wide[part] = theirs[part].astype(F32)
        at = pl.ds(own - here + c * size, size)
        copies.append(pltpu.make_async_copy(wide.at[part], out.at[at], sems.at[c]))
        copies[-1].start()
    for copy in copies:
        copy.wait()


def finish_kernel(me, keep_a, keep_b, one, two, three, qkv, out, gains, biases, up, down):
    small, width = out.shape
    tall = up.shape[0]
    high = 4 * small + 8
    total, units = keep_a[0], keep_b[0]
    for got in (one, two, three):
        total = total + got[:high].astype(F32)
        units = units + got[high:].astype(F32)
    for part in range(3):
        qkv[:, part * width : (part + 1) * width] = total[part * small : (part + 1) * small]
    out[...] = total[3 * small : 4 * small]
    vec = pltpu.roll(total[4 * small :], width - me[0] * small, 1)[:, :small]
    gains[...] = vec[:2]
    biases[...] = vec[2:5]
    up[...] = units[:tall]
    down[...] = units[tall:]


def swap(block, axis, bit):
    size = lax.axis_size(axis)
    return lax.ppermute(block, axis, [(i, i ^ bit) for i in range(size)])


def steps_of(axis):
    return [(axis, 1 << k) for k in reversed(range(lax.axis_size(axis).bit_length() - 1))]


def after(value, other):
    return lax.optimization_barrier((value, other))[0]


def halves(held):
    half = held.shape[0] // 2
    return held[:half], held[half:].astype(BF16)


def fold_step(keep, send, axis, bit, past=None):
    got = swap(send, axis, bit)
    return keep + (got if past is None else after(got, past)).astype(F32)


def bit_reverse(index, count):
    out = 0 * index
    for k in range(count):
        out = out | (((index >> k) & 1) << (count - 1 - k))
    return out


def by_device(block, me):
    blocks = block[None]
    for axis, bit in steps_of("dp") + steps_of("tensor"):
        blocks = jnp.concatenate([blocks, swap(blocks, axis, bit)], 0)
    count = blocks.shape[0]
    order = jnp.arange(count, dtype=jnp.int32) ^ me
    return jnp.take(blocks, bit_reverse(order, count.bit_length() - 1), axis=0)


def other_pack(w_qkv, w_out, gains, biases, w_up, w_down, me):
    small, width = w_out.shape
    qkv = w_qkv.reshape(small, 3, width).transpose(1, 0, 2).reshape(3 * small, width)
    rows = jnp.concatenate([gains, biases], 0)
    place = jnp.zeros((8, width), BF16)
    place = lax.dynamic_update_slice(place, rows, (jnp.int32(0), me * small))
    return jnp.concatenate([qkv, w_out, place], 0), jnp.concatenate([w_up, w_down.T], 0)


def other_blocks(a, b, me, n_dp, n_t):
    a = by_device(a, me)
    b = by_device(b, me)
    width = a.shape[2]
    count = n_dp * n_t
    small = width // count
    big = width // (VDP * VT)
    mats = a[:, : 4 * small].reshape(count, 4, small, width).transpose(1, 0, 2, 3)
    mats = mats.reshape(4, VDP * VT, big, width).transpose(1, 0, 2, 3).reshape(VDP * VT, 4 * big, width)
    vec = jnp.sum(a[:, 4 * small :].astype(F32), 0).astype(BF16)
    vecs = jnp.concatenate([vec[None], jnp.zeros((VDP * VT - 1, 8, width), BF16)], 0)
    a = jnp.concatenate([mats, vecs], 1)
    tall = width // n_dp
    b = b.reshape(n_dp, VT, 2, tall, width).transpose(1, 2, 0, 3, 4)
    b = b.reshape(VT, 2, VDP, width // VDP, width).transpose(2, 0, 1, 3, 4)
    b = b.reshape(VDP * VT, 2 * (width // VDP), width)

    y_own = (me // 2) % 2

    def placed(blocks):
        pairs = blocks.reshape((CHIPS, 2) + blocks.shape[1:])
        chips = sorted(range(CHIPS), key=spot)
        pairs = jnp.stack([pairs[m] for m in chips], 0)
        pairs = jnp.where(y_own == 1, jnp.roll(pairs, VDP, 0), pairs)
        return pairs[:, 0], pairs[:, 1]

    return placed(a) + placed(b)


def other_reduce(pair_a, pair_b, me, n_dp, n_t):
    count = n_dp * n_t
    y_own = (me // 2) % 2

    def whole(keep, send):
        pairs = jnp.stack([keep, send.astype(F32)], 1)
        pairs = jnp.stack([pairs[twist(i)] for i in range(VDP)], 0)
        none = jnp.zeros_like(pairs)
        both = jnp.stack([jnp.where(y_own == y, pairs, none) for y in range(2)], 1)
        return both.reshape((VDP * VT,) + keep.shape[1:])

    def rows_of(blocks, parts):
        big = blocks.shape[1] // parts
        mats = blocks.reshape(VDP * VT, parts, big, -1).transpose(1, 0, 2, 3)
        mats = mats.reshape(parts, count, VDP * VT * big // count, -1).transpose(1, 0, 2, 3)
        return mats.reshape(count, -1, blocks.shape[2])

    def vec_of(blocks):
        picked = jnp.where(y_own == 0, blocks[0], 0.0)
        return jnp.broadcast_to(picked[None], (count,) + picked.shape)

    a, b = whole(*pair_a), whole(*pair_b)
    width = a.shape[2]
    tall, high = width // n_dp, width // VDP
    cols = b.reshape(VDP, VT, 2, high, width).transpose(1, 2, 0, 3, 4)
    cols = cols.reshape(VT, 2, n_dp, tall, width).transpose(2, 0, 1, 3, 4)
    cols = cols.reshape(count, 2 * tall, width)
    a = jnp.concatenate([rows_of(a[:, :32], 4), vec_of(a[:, 32:])], 1)
    results = []
    for blocks in (a, cols):
        blocks = jnp.take(blocks, jnp.arange(count, dtype=jnp.int32) ^ me, axis=0)
        for axis, bit in reversed(steps_of("dp") + steps_of("tensor")):
            pairs = blocks.reshape((-1, 2) + blocks.shape[1:])
            got = swap(pairs[:, 1].astype(BF16), axis, bit)
            blocks = pairs[:, 0] + got.astype(F32)
        results.append(blocks[0])
    return results


def struct(shape, dtype):
    return jax.ShapeDtypeStruct(shape, dtype)


def call(kernel, name, args, outs, scratch=(), flops=0, limit=8, hbm_outs=True):
    args = [a if isinstance(a, tuple) else (a, pltpu.VMEM) for a in args]
    moved = sum(a.size * a.dtype.itemsize for a, _ in args)
    spaces = [pl.ANY if hbm_outs and isinstance(o, jax.ShapeDtypeStruct) else pltpu.VMEM for o in outs]
    return pl.pallas_call(
        kernel,
        name=name,
        out_shape=outs,
        in_specs=[pl.BlockSpec(memory_space=space) for _, space in args],
        out_specs=[pl.BlockSpec(memory_space=space) for space in spaces],
        scratch_shapes=list(scratch),
        compiler_params=pltpu.CompilerParams(vmem_limit_bytes=limit * MIB),
        cost_estimate=pl.CostEstimate(flops=flops, bytes_accessed=moved, transcendentals=0),
    )(*[a for a, _ in args])


def on_device(tokens, lengths, row_mask, cotangent, w_qkv, w_out, gains, biases, w_up, w_down):
    images, seq_len, width = tokens.shape
    n_dp, n_t = lax.axis_size("dp"), lax.axis_size("tensor")
    index = lax.axis_index("dp") * n_t + lax.axis_index("tensor")
    me = index.astype(jnp.int32).reshape(1)
    usual = (n_dp, n_t) == (VDP, VT)
    virt = me if usual else (index // 2 % 2 * 2).astype(jnp.int32).reshape(1)
    small = width // (n_dp * n_t)
    tall = width // n_dp
    own = images * seq_len // 2
    rows = own // WIN
    per = 12 if rows % 12 == 0 else 1
    some = 6 if rows % 6 == 0 else 1
    less = 4 if rows % 4 == 0 else 1
    smem = pltpu.SMEM
    weights = (w_qkv, w_out, gains, biases, w_up, w_down)
    token_mm = 2 * own * width
    hbm = pltpu.HBM

    def in_hbm(array):
        return (pltpu.with_memory_space_constraint(array, hbm), hbm)

    def fetch(me):
        return call(
            fetch_kernel,
            "fetch",
            [(me, smem), in_hbm(tokens.reshape(images * seq_len, width))],
            [
                pltpu.VMEM((own, width), BF16),
                pltpu.VMEM((own, width), F32),
                pltpu.VMEM((own, 1), F32),
                pltpu.VMEM((width, own), BF16),
            ],
            [pltpu.SemaphoreType.DMA(())],
            limit=4,
        )

    def fetch_turned(me):
        return call(
            turn_kernel,
            "turn",
            [(me, smem), in_hbm(cotangent.reshape(images * seq_len, width))],
            [pltpu.VMEM((own, width), BF16), pltpu.VMEM((width, own), BF16)],
            [pltpu.SemaphoreType.DMA(())],
            limit=4,
        )

    if usual:
        weights = (w_qkv, w_out, gains, biases, w_up, w_down.T)
        high = 4 * small + 8
        packed = call(
            pack_kernel,
            "pack",
            [(me, smem)] + [in_hbm(w) for w in weights],
            [pltpu.VMEM((1, high + 2 * tall, width), BF16)],
            [pltpu.VMEM(w.shape, BF16) for w in weights] + [pltpu.SemaphoreType.DMA((6,))],
        )[0]
        planes = [packed] + [swap(packed, "dp", bit) for bit in (2, 4, 6)]
        cot, cot_t = fetch_turned(after(me, packed))
        planes[3] = after(planes[3], cot)
        held_a = jnp.concatenate([plane[:, :high] for plane in planes], 0)
        b = jnp.concatenate([plane[:, high:] for plane in planes], 0)
        held_a = jnp.concatenate([held_a, swap(held_a, "dp", 1)], 0)
        b = jnp.concatenate([b, swap(b, "dp", 1)], 0)
        x, xhat1, inv1, xhat_t = fetch(after(me, held_a))
        held_a = jnp.concatenate([held_a, after(swap(held_a, "tensor", 2), (b, xhat1))], 0)
        far_b = swap(b, "tensor", 2)
        got_a = swap(held_a, "tensor", 1)
        got_b = swap(b, "tensor", 1)
    else:
        held_a, got_a, held_b, got_b = other_blocks(*other_pack(*weights, index), index, n_dp, n_t)
        b, far_b = held_b[:VDP], held_b[VDP:]
        got_b, got_far = got_b[:VDP], got_b[VDP:]
        x, xhat1, inv1, xhat_t = fetch(me)
        cot, cot_t = fetch_turned(me)
    qkv, prob, o, x1, wqkv, wout, vec = call(
        functools.partial(attend_kernel, some),
        "attend",
        [(me, smem), (virt, smem), (lengths, smem), (row_mask, smem), x, xhat1, held_a, got_a],
        [
            pltpu.VMEM((own, 3 * width), BF16),
            pltpu.VMEM((rows * HEADS, WIN, WIN), BF16),
            pltpu.VMEM((own, width), BF16),
            pltpu.VMEM((own, width), F32),
            pltpu.VMEM((width, 3 * width), BF16),
            pltpu.VMEM((width, width), BF16),
            pltpu.VMEM((8, width), F32),
        ],
        flops=token_mm * (4 * width + 2 * WIN),
    )
    tall_b = 2 * (width // VDP)
    mats = [pltpu.VMEM((width, 2 * width), BF16)] * 2 + [pltpu.VMEM((2 * width, width), BF16)] * 2
    if usual:
        far_b = after(far_b, x1)
        got_far = swap(far_b, "tensor", 1)
        got_b = after(got_b, far_b)
    wide_per = 6 if rows % 6 == 0 else 1
    *first, keep_b, send_b = call(
        functools.partial(hidden_near_kernel, wide_per),
        "hidden_near",
        [(virt, smem), x1, cot, cot_t, vec, b, got_b],
        [
            pltpu.VMEM((own, width), BF16),
            pltpu.VMEM((own, width), F32),
            pltpu.VMEM((own, 1), F32),
            pltpu.VMEM((own, width), F32),
            pltpu.VMEM((own, width), F32),
            pltpu.VMEM((VDP, tall_b, width), F32),
            pltpu.VMEM((VDP, tall_b, width), BF16),
        ],
        [pltpu.VMEM((own, 2 * width), BF16)] * 2 + mats,
        token_mm * 12 * width,
        12,
    )
    y, dx1, g, gout, gvec = call(
        functools.partial(hidden_far_kernel, wide_per),
        "hidden_far",
        [(virt, smem), cot, vec, far_b, got_far, *first, o],
        [
            pltpu.VMEM((own, width), BF16),
            pltpu.VMEM((own, width), F32),
            pltpu.VMEM((own, width), BF16),
            pltpu.VMEM((width, width), F32),
            pltpu.VMEM((8, width), F32),
        ],
        mats,
        token_mm * 9 * width,
    )
    core, xbit = ("tensor", 1), ("dp", 1)
    if usual:
        held_b = fold_step(keep_b, send_b, *core, g)
        y = after(y, held_b)
    y_near = swap(y, "tensor", 1)
    dqkv, keep_a, send_a = call(
        functools.partial(back_kernel, per),
        "back",
        [(virt, smem), qkv, prob, g, xhat_t, wqkv, wout, vec, gout, gvec],
        [
            pltpu.VMEM((own, 3 * width), BF16),
            pltpu.VMEM((VDP, 40, width), F32),
            pltpu.VMEM((VDP, 40, width), BF16),
        ],
        [pltpu.VMEM((width, 3 * width), F32)],
        token_mm * (4 * width + 5 * WIN),
    )
    if usual:
        held_b = fold_step(*halves(held_b), *xbit)
        vec = after(vec, held_b)
    gx, gxb, layer_out = call(
        functools.partial(token_grad_kernel, less),
        "token_grad",
        [(me, smem), dqkv, wqkv, vec, xhat1, inv1, dx1, y, y_near],
        [
            pltpu.VMEM((own, width), F32),
            pltpu.VMEM((own, width), BF16),
            struct((images * seq_len, width), BF16),
        ],
        [pltpu.VMEM((3 * width, width), BF16), pltpu.SemaphoreType.DMA((2,))],
        flops=token_mm * 3 * width,
    )
    layer_out = layer_out.reshape(images, seq_len, width)

    def place(gx_near):
        return call(
            functools.partial(place_kernel, less),
            "place",
            [(me, smem), gx, gx_near],
            [struct((images * seq_len, width), F32)],
            [pltpu.VMEM((own, width), F32), pltpu.SemaphoreType.DMA((rows // less + 1,))],
        )[0].reshape(images, seq_len, width)

    if usual:
        held_a = fold_step(keep_a, send_a, *core, gxb)
        grad_tokens = place(swap(after(gxb, held_a), "tensor", 1))
        held_a = fold_step(*halves(held_a), *xbit, grad_tokens)
        low = jnp.concatenate([held_a[1:], held_b[1:]], 1).astype(BF16)
        got = [swap(low[n - 1], "dp", 2 * n) for n in range(1, 4)]
        shapes = ((small, 3 * width), (small, width), (2, small), (3, small), (tall, width), (tall, width))
        o_qkv, o_out, o_gains, o_bias, o_up, o_down = call(
            finish_kernel,
            "finish",
            [(me, smem), held_a, held_b, *got],
            [struct(shape, F32) for shape in shapes],
            limit=2,
            hbm_outs=False,
        )
    else:
        grad_tokens = place(swap(gxb, "tensor", 1))
        grad_a, grad_b = other_reduce((keep_a, send_a), (keep_b, send_b), index, n_dp, n_t)
        o_qkv = jnp.concatenate([grad_a[p * small : (p + 1) * small] for p in range(3)], 1)
        o_out = grad_a[3 * small : 4 * small]
        o_vec = lax.dynamic_slice_in_dim(grad_a[4 * small : 4 * small + 5], index * small, small, 1)
        o_gains, o_bias = o_vec[:2], o_vec[2:]
        o_up, o_down = grad_b[:tall], grad_b[tall:]
    return layer_out, grad_tokens, o_qkv, o_out, o_gains, o_bias, o_up, o_down.T


def solution(mesh):
    in_specs = (
        P("dp", None, None),
        P("dp"),
        P("dp", None),
        P("dp", None, None),
        P(("dp", "tensor"), None),
        P(("dp", "tensor"), None),
        P(None, ("dp", "tensor")),
        P(None, ("dp", "tensor")),
        P("dp", "tensor"),
        P("tensor", "dp"),
    )
    out_specs = (
        P("dp", None, None),
        P("dp", None, None),
        P(("dp", "tensor"), None),
        P(("dp", "tensor"), None),
        P(None, ("dp", "tensor")),
        P(None, ("dp", "tensor")),
        P("dp", "tensor"),
        P("tensor", "dp"),
    )
    return jax.shard_map(
        on_device, mesh=mesh, in_specs=in_specs, out_specs=out_specs, check_vma=False
    )
```

```python
import functools

import jax
import jax.numpy as jnp
from jax import lax
from jax.experimental import pallas as pl
from jax.experimental.pallas import tpu as pltpu
from jax.sharding import PartitionSpec as P

HEADS = 2
WIN = 96
F32 = jnp.float32
BF16 = jnp.bfloat16
VDP, VT = 8, 4
CHIPS = VDP * VT // 2
MIB = 1 << 20

NN = ((1,), (0,))
NT = ((1,), (1,))
TN = ((0,), (0,))


def dot(a, b, dims):
    return lax.dot_general(a, b, (dims, ((), ())), preferred_element_type=F32)


def twist(i):
    return (i & 1) * 4 + (i >> 1)


def spot(m):
    return (m % 2) * VDP + twist(m // 2)


def norm_parts(values):
    center = values - jnp.mean(values, -1, keepdims=True)
    inv = lax.rsqrt(jnp.mean(center * center, -1, keepdims=True) + 1e-05)
    return center * inv, inv


def norm_back(grad, xhat, inv, gain):
    scaled = grad * gain
    return inv * (
        scaled
        - jnp.mean(scaled, -1, keepdims=True)
        - xhat * jnp.mean(scaled * xhat, -1, keepdims=True)
    )


def gelu_both(u):
    c = 0.7978845608028654
    u2 = u * u
    t = jnp.tanh(u * (c + (c * 0.044715) * u2))
    half = 0.5 + 0.5 * t
    value = u * half
    slope = half + (value - value * half) * (2 * c + (6 * c * 0.044715) * u2)
    return value, slope


def pack_kernel(me, *refs):
    sources, packed, held, sems = refs[:6], refs[6], refs[7:13], refs[13]
    copies = [pltpu.make_async_copy(a, b, sems.at[n]) for n, (a, b) in enumerate(zip(sources, held))]
    for copy in copies:
        copy.start()
    qkv, out, gains, biases, up, down = held
    small, width = out.shape
    tall = up.shape[0]
    lane = lax.broadcasted_iota(jnp.int32, (1, width), 1)
    mine = lane // small == me[0]
    for copy in copies:
        copy.wait()
    for part in range(3):
        packed[0, part * small : (part + 1) * small] = qkv[:, part * width : (part + 1) * width]
    packed[0, 3 * small : 4 * small] = out[...]
    rows = [gains[0:1], gains[1:2], biases[0:1], biases[1:2], biases[2:3]]
    vals = jnp.concatenate(rows + [jnp.zeros((3, small), BF16)], 0).astype(F32)
    wide = jnp.concatenate([vals] * (width // small), 1)
    at = 4 * small + 8
    packed[0, 4 * small : at] = jnp.where(mine, wide, 0.0).astype(BF16)
    packed[0, at : at + tall] = up[...]
    packed[0, at + tall :] = down[...]


def fetch_kernel(me, tokens, x_ref, xhat_ref, inv_ref, xhat_t, sem):
    own, width = x_ref.shape
    copy = pltpu.make_async_copy(tokens.at[pl.ds(lax.rem(me[0], 2) * own, own)], x_ref, sem)
    copy.start()
    ones = jnp.full((width, width), 1.0 / width, BF16)
    size = 256 if own % 256 == 0 else own
    copy.wait()
    for n in range(own // size):
        part = slice(n * size, (n + 1) * size)
        x = x_ref[part]
        center = x.astype(F32) - dot(x, ones, NN)
        inv = lax.rsqrt(dot((center * center).astype(BF16), ones, NN) + 1e-05)
        xhat = center * inv
        xhat_ref[part] = xhat
        inv_ref[part] = inv[:, : width // 2]
        xhat_t[:, part] = xhat.astype(BF16).T


def turn_kernel(me, cot, cot_ref, cot_t, sem):
    own = cot_ref.shape[0]
    copy = pltpu.make_async_copy(cot.at[pl.ds(lax.rem(me[0], 2) * own, own)], cot_ref, sem)
    copy.start()
    size = 256 if own % 256 == 0 else own
    copy.wait()
    for n in range(own // size):
        part = slice(n * size, (n + 1) * size)
        cot_t[:, part] = cot_ref[part].T


def attend_kernel(
    per, me, virt, lens, live, x_ref, xhat_ref, held, got,
    qkv_ref, prob_ref, o_ref, x1_ref, wqkv, wout, vec,
):
    tokens, width = x_ref.shape
    rows = tokens // WIN
    hs = width // HEADS
    here = twist(virt[0] // 4)
    y_own = (virt[0] // 2) % 2
    first = virt[0] % 2 == 0
    total = jnp.zeros((8, width), F32)
    for m in range(CHIPS):
        k = spot(m) ^ (here + y_own * VDP)
        a = held[k].astype(F32)
        b = got[k].astype(F32)
        even = jnp.where(first, a, b)
        odd = jnp.where(first, b, a)
        for part in range(3):
            both = jnp.concatenate([even[part * 8 : part * 8 + 8], odd[part * 8 : part * 8 + 8]], 0)
            wqkv[m * 16 : m * 16 + 16, part * width : (part + 1) * width] = both.astype(BF16)
        both = jnp.concatenate([even[24:32], odd[24:32]], 0)
        wout[m * 16 : m * 16 + 16] = both.astype(BF16)
        total = total + a[32:40] + b[32:40]
    vec[...] = total
    scale = hs**-0.5
    ii = lax.broadcasted_iota(jnp.int32, (WIN, WIN), 0)
    jj = lax.broadcasted_iota(jnp.int32, (WIN, WIN), 1)
    same = ii == jj
    image_rows = live.shape[1]
    base = lax.rem(me[0], 2) * rows

    def enter(c):
        part = slice(c * per * WIN, (c + 1) * per * WIN)
        h1 = (xhat_ref[part] * total[0:1] + total[2:3]).astype(BF16)
        qkv = dot(h1, wqkv[...], NN).astype(BF16)
        qkv_ref[part] = qkv
        scores = []
        for r in range(per):
            at = slice(r * WIN, (r + 1) * WIN)
            for h in range(HEADS):
                q = qkv[at, h * hs : (h + 1) * hs]
                k = qkv[at, width + h * hs : width + (h + 1) * hs]
                scores.append(dot(q, k, NT))
        return qkv, scores

    ahead = enter(0)
    for c in range(rows // per):
        qkv, scores = ahead
        if c + 1 < rows // per:
            ahead = enter(c + 1)
        part = slice(c * per * WIN, (c + 1) * per * WIN)
        probs = []
        for r in range(per):
            row = base + c * per + r
            image = row // image_rows
            inside = row - image * image_rows
            reach = jnp.where(live[image, inside] == 1, lens[image] - inside * WIN, 0)
            allowed = same | (jj < jnp.minimum(ii, reach))
            for h in range(HEADS):
                s = jnp.where(allowed, scores[r * HEADS + h], -1e30)
                e = jnp.exp((s - jnp.max(s, -1, keepdims=True)) * scale)
                probs.append((e * (1.0 / jnp.sum(e, -1, keepdims=True))).astype(BF16))
        mixed = []
        for r in range(per):
            at = slice(r * WIN, (r + 1) * WIN)
            heads = []
            for h in range(HEADS):
                v = qkv[at, 2 * width + h * hs : 2 * width + (h + 1) * hs]
                heads.append(dot(probs[r * HEADS + h], v, NN).astype(BF16))
            mixed.append(jnp.concatenate(heads, 1))
        o = jnp.concatenate(mixed, 0)
        for n, p in enumerate(probs):
            prob_ref[c * per * HEADS + n] = p
        o_ref[part] = o
        x1_ref[part] = x_ref[part].astype(F32) + dot(o, wout[...], NN)


def join(virt, blocks, n, up, down_t):
    tall = blocks.shape[1] // 2
    width = up.shape[0]
    here = twist(virt[0] // 4)
    for i in range(VDP):
        k = twist(i) ^ here
        at = slice(i * tall, (i + 1) * tall)
        cols = slice(n * width, (n + 1) * width)
        up[at, cols] = blocks[k, :tall]
        down_t[at, cols] = blocks[k, tall:]


def hidden_units(h2, dyb, up, down_t):
    u = dot(h2, up[...], NN).astype(BF16)
    da = dot(dyb, down_t[...], NN).astype(BF16)
    a, slope = gelu_both(u)
    return a, da * slope


def hidden_near_kernel(
    per, virt, x1_ref, cot_ref, cot_t, vec, own, got,
    h2_ref, xhat_ref, inv_ref, f_ref, dh2_ref, keep, send,
    a_ref, du_ref, up, down_t, up_t, down,
):
    tokens, width = x1_ref.shape
    size = per * WIN
    join(virt, own, 0, up, down_t)
    join(virt, got, 1, up, down_t)
    up_t[...] = up[...].T
    down[...] = down_t[...].T
    ones = jnp.full((width, width // 2), 1.0 / width, BF16)
    for c in range(tokens // size):
        part = slice(c * size, (c + 1) * size)
        x1 = x1_ref[part]
        high = x1.astype(BF16)
        low = (x1 - high.astype(F32)).astype(BF16)
        mean = dot(high, ones, NN) + dot(low, ones, NN)
        center = x1 - jnp.concatenate([mean, mean], 1)
        inv = lax.rsqrt(dot((center * center).astype(BF16), ones, NN) + 1e-05)
        inv_ref[part] = inv
        xhat = center * jnp.concatenate([inv, inv], 1)
        xhat_ref[part] = xhat
        h2 = (xhat * vec[1:2] + vec[3:4]).astype(BF16)
        h2_ref[part] = h2
        a, du = hidden_units(h2, cot_ref[part], up, down_t)
        a_ref[part] = a
        du_ref[part] = du
        f_ref[part] = x1 + vec[4:5] + dot(a, down[...], NN)
        dh2_ref[part] = dot(du, up_t[...], NN)
    gdown = dot(cot_t[...], a_ref[...], NN)
    gup = dot(h2_ref[...], du_ref[...], TN)
    tall = width // VDP
    here = twist(virt[0] // 4)
    for i in range(VDP):
        at = slice(i * tall, (i + 1) * tall)
        k = twist(i) ^ here
        keep[k, :tall] = gup[at, :width]
        keep[k, tall:] = gdown[at, :width]
        send[k, :tall] = gup[at, width:].astype(BF16)
        send[k, tall:] = gdown[at, width:].astype(BF16)


def hidden_far_kernel(
    per, virt, cot_ref, vec, own, got, h2_ref, xhat_ref, inv_ref, f_ref, dh2_ref, o_ref,
    y_ref, dx1_ref, g_ref, gout, gvec,
    up, down_t, up_t, down,
):
    tokens, width = h2_ref.shape
    size = per * WIN
    join(virt, own, 0, up, down_t)
    join(virt, got, 1, up, down_t)
    up_t[...] = up[...].T
    down[...] = down_t[...].T
    sums = [jnp.zeros((1, width), F32)] * 3
    for c in range(tokens // size):
        part = slice(c * size, (c + 1) * size)
        a, du = hidden_units(h2_ref[part], cot_ref[part], up, down_t)
        y_ref[part] = (f_ref[part] + dot(a, down[...], NN)).astype(BF16)
        dh2 = dh2_ref[part] + dot(du, up_t[...], NN)
        dy = cot_ref[part].astype(F32)
        xhat = xhat_ref[part]
        inv = inv_ref[part]
        dx1 = dy + norm_back(dh2, xhat, jnp.concatenate([inv, inv], 1), vec[1:2])
        dx1_ref[part] = dx1
        g_ref[part] = dx1.astype(BF16)
        for n, term in enumerate((dh2 * xhat, dh2, dy)):
            sums[n] = sums[n] + jnp.sum(term, 0, keepdims=True)
    gout[...] = dot(o_ref[...], g_ref[...], TN)
    zero = jnp.zeros((1, width), F32)
    gvec[...] = jnp.concatenate([zero, sums[0], zero, sums[1], sums[2], zero, zero, zero], 0)


def own_rows(virt, i, other):
    core = virt[0] % 2
    core = 1 - core if other else core
    return pl.ds(pl.multiple_of(i * 32 + ((virt[0] // 2) % 2) * 16 + core * 8, 8), 8)


def back_kernel(
    per, virt, qkv_ref, prob_ref, g_ref, xhat_t, wqkv, wout, vec, gout, gvec,
    dqkv, keep, send,
    gqkv,
):
    tokens, width = g_ref.shape
    hs = width // HEADS
    scale = hs**-0.5
    every = [(r, h) for r in range(tokens // WIN) for h in range(HEADS)]
    groups = [every[n : n + 2 * per] for n in range(0, len(every), 2 * per)]

    def piece(ref, r, h, part=0):
        return ref[r * WIN : (r + 1) * WIN, part * width + h * hs : part * width + (h + 1) * hs]

    def enter(pairs):
        r = pairs[0][0]
        do = dot(g_ref[r * WIN : (r + per) * WIN], wout[...], NT).astype(BF16)
        dos = [do[(n - r) * WIN : (n - r + 1) * WIN, h * hs : (h + 1) * hs] for n, h in pairs]
        probs = [prob_ref[r * HEADS + h] for r, h in pairs]
        dps = [dot(a, piece(qkv_ref, r, h, 2), NT) for a, (r, h) in zip(dos, pairs)]
        dvs = [dot(p, a, TN).astype(BF16) for p, a in zip(probs, dos)]
        return probs, dps, dvs

    ahead = enter(groups[0])
    for place, pairs in enumerate(groups):
        probs, dps, dvs = ahead
        if place + 1 < len(groups):
            ahead = enter(groups[place + 1])
        dss = []
        for p, dp in zip(probs, dps):
            pf = p.astype(F32)
            ds = pf * (dp - jnp.sum(dp * pf, -1, keepdims=True)) * scale
            dss.append(ds.astype(BF16))
        dqs = [dot(ds, piece(qkv_ref, r, h, 1), NN).astype(BF16) for ds, (r, h) in zip(dss, pairs)]
        dks = [dot(ds, piece(qkv_ref, r, h, 0), TN).astype(BF16) for ds, (r, h) in zip(dss, pairs)]
        for n, (r, h) in enumerate(pairs):
            for part, values in enumerate((dqs, dks, dvs)):
                at = slice(part * width + h * hs, part * width + (h + 1) * hs)
                dqkv[r * WIN : (r + 1) * WIN, at] = values[n]
    grad = dot(xhat_t[...], dqkv[...], NN)
    total = jnp.zeros((1, 3 * width), F32)
    for r in range(tokens // WIN):
        total = total + jnp.sum(dqkv[r * WIN : (r + 1) * WIN].astype(F32), 0, keepdims=True)
    w = wqkv[...].astype(F32)
    cols = jnp.concatenate([
        jnp.broadcast_to(jnp.sum(w * grad, -1, keepdims=True), (width, 64)),
        jnp.broadcast_to(jnp.sum(w * total, -1, keepdims=True), (width, 64)),
    ], 1)
    lines = cols.T
    gain, from_total = lines[0:1], lines[64:65]
    vec_t = vec[...].T
    gqkv[...] = grad * vec_t[:, 0:1] + total * vec_t[:, 2:3]
    rest = gvec[...]
    sums = jnp.concatenate([gain, rest[1:2], from_total, rest[3:]], 0)
    here = twist(virt[0] // 4)
    for i in range(VDP):
        k = twist(i) ^ here
        mine, other = own_rows(virt, i, 0), own_rows(virt, i, 1)
        theirs = []
        for part in range(3):
            at = slice(part * width, (part + 1) * width)
            keep[k, part * 8 : part * 8 + 8] = gqkv[mine, at]
            theirs.append(gqkv[other, at])
        keep[k, 24:32] = gout[mine]
        keep[k, 32:] = sums
        send[k] = jnp.concatenate(theirs + [gout[other], sums], 0).astype(BF16)


def token_grad_kernel(per, me, dqkv, wqkv, vec, xhat_ref, inv_ref, dx1_ref, y, y_near, gx, gxb, out, turned, sems):
    own = dqkv.shape[0]
    size = per * WIN
    copies = []
    for n, source in enumerate((y, y_near)):
        at = pl.ds((lax.rem(me[0], 2) ^ n) * own, own)
        copies.append(pltpu.make_async_copy(source, out.at[at], sems.at[n]))
        copies[-1].start()
    turned[...] = wqkv[...].T
    for c in range(own // size):
        part = slice(c * size, (c + 1) * size)
        dh1 = dot(dqkv[part], turned[...], NN)
        inv = inv_ref[part]
        inv = jnp.concatenate([inv, inv], 1)
        values = dx1_ref[part] + norm_back(dh1, xhat_ref[part], inv, vec[0:1])
        gx[part] = values
        gxb[part] = values.astype(BF16)
    for copy in copies:
        copy.wait()


def place_kernel(per, me, mine, theirs, out, wide, sems):
    own = theirs.shape[0]
    size = per * WIN
    here = lax.rem(me[0], 2) * own
    copies = [pltpu.make_async_copy(mine, out.at[pl.ds(here, own)], sems.at[own // size])]
    copies[0].start()
    for c in range(own // size):
        part = pl.ds(c * size, size)
        wide[part] = theirs[part].astype(F32)
        at = pl.ds(own - here + c * size, size)
        copies.append(pltpu.make_async_copy(wide.at[part], out.at[at], sems.at[c]))
        copies[-1].start()
    for copy in copies:
        copy.wait()


def finish_kernel(me, keep_a, keep_b, one, two, three, qkv, out, gains, biases, up, down):
    small, width = out.shape
    tall = up.shape[0]
    high = 4 * small + 8
    total, units = keep_a[0], keep_b[0]
    for got in (one, two, three):
        total = total + got[:high].astype(F32)
        units = units + got[high:].astype(F32)
    for part in range(3):
        qkv[:, part * width : (part + 1) * width] = total[part * small : (part + 1) * small]
    out[...] = total[3 * small : 4 * small]
    vec = pltpu.roll(total[4 * small :], width - me[0] * small, 1)[:, :small]
    gains[...] = vec[:2]
    biases[...] = vec[2:5]
    up[...] = units[:tall]
    down[...] = units[tall:]


def swap(block, axis, bit):
    size = lax.axis_size(axis)
    return lax.ppermute(block, axis, [(i, i ^ bit) for i in range(size)])


def steps_of(axis):
    return [(axis, 1 << k) for k in reversed(range(lax.axis_size(axis).bit_length() - 1))]


def after(value, other):
    return lax.optimization_barrier((value, other))[0]


def halves(held):
    half = held.shape[0] // 2
    return held[:half], held[half:].astype(BF16)


def fold_step(keep, send, axis, bit, past=None):
    got = swap(send, axis, bit)
    return keep + (got if past is None else after(got, past)).astype(F32)


def bit_reverse(index, count):
    out = 0 * index
    for k in range(count):
        out = out | (((index >> k) & 1) << (count - 1 - k))
    return out


def by_device(block, me):
    blocks = block[None]
    for axis, bit in steps_of("dp") + steps_of("tensor"):
        blocks = jnp.concatenate([blocks, swap(blocks, axis, bit)], 0)
    count = blocks.shape[0]
    order = jnp.arange(count, dtype=jnp.int32) ^ me
    return jnp.take(blocks, bit_reverse(order, count.bit_length() - 1), axis=0)


def other_pack(w_qkv, w_out, gains, biases, w_up, w_down, me):
    small, width = w_out.shape
    qkv = w_qkv.reshape(small, 3, width).transpose(1, 0, 2).reshape(3 * small, width)
    rows = jnp.concatenate([gains, biases], 0)
    place = jnp.zeros((8, width), BF16)
    place = lax.dynamic_update_slice(place, rows, (jnp.int32(0), me * small))
    return jnp.concatenate([qkv, w_out, place], 0), jnp.concatenate([w_up, w_down.T], 0)


def other_blocks(a, b, me, n_dp, n_t):
    a = by_device(a, me)
    b = by_device(b, me)
    width = a.shape[2]
    count = n_dp * n_t
    small = width // count
    big = width // (VDP * VT)
    mats = a[:, : 4 * small].reshape(count, 4, small, width).transpose(1, 0, 2, 3)
    mats = mats.reshape(4, VDP * VT, big, width).transpose(1, 0, 2, 3).reshape(VDP * VT, 4 * big, width)
    vec = jnp.sum(a[:, 4 * small :].astype(F32), 0).astype(BF16)
    vecs = jnp.concatenate([vec[None], jnp.zeros((VDP * VT - 1, 8, width), BF16)], 0)
    a = jnp.concatenate([mats, vecs], 1)
    tall = width // n_dp
    b = b.reshape(n_dp, VT, 2, tall, width).transpose(1, 2, 0, 3, 4)
    b = b.reshape(VT, 2, VDP, width // VDP, width).transpose(2, 0, 1, 3, 4)
    b = b.reshape(VDP * VT, 2 * (width // VDP), width)

    y_own = (me // 2) % 2

    def placed(blocks):
        pairs = blocks.reshape((CHIPS, 2) + blocks.shape[1:])
        chips = sorted(range(CHIPS), key=spot)
        pairs = jnp.stack([pairs[m] for m in chips], 0)
        pairs = jnp.where(y_own == 1, jnp.roll(pairs, VDP, 0), pairs)
        return pairs[:, 0], pairs[:, 1]

    return placed(a) + placed(b)


def other_reduce(pair_a, pair_b, me, n_dp, n_t):
    count = n_dp * n_t
    y_own = (me // 2) % 2

    def whole(keep, send):
        pairs = jnp.stack([keep, send.astype(F32)], 1)
        pairs = jnp.stack([pairs[twist(i)] for i in range(VDP)], 0)
        none = jnp.zeros_like(pairs)
        both = jnp.stack([jnp.where(y_own == y, pairs, none) for y in range(2)], 1)
        return both.reshape((VDP * VT,) + keep.shape[1:])

    def rows_of(blocks, parts):
        big = blocks.shape[1] // parts
        mats = blocks.reshape(VDP * VT, parts, big, -1).transpose(1, 0, 2, 3)
        mats = mats.reshape(parts, count, VDP * VT * big // count, -1).transpose(1, 0, 2, 3)
        return mats.reshape(count, -1, blocks.shape[2])

    def vec_of(blocks):
        picked = jnp.where(y_own == 0, blocks[0], 0.0)
        return jnp.broadcast_to(picked[None], (count,) + picked.shape)

    a, b = whole(*pair_a), whole(*pair_b)
    width = a.shape[2]
    tall, high = width // n_dp, width // VDP
    cols = b.reshape(VDP, VT, 2, high, width).transpose(1, 2, 0, 3, 4)
    cols = cols.reshape(VT, 2, n_dp, tall, width).transpose(2, 0, 1, 3, 4)
    cols = cols.reshape(count, 2 * tall, width)
    a = jnp.concatenate([rows_of(a[:, :32], 4), vec_of(a[:, 32:])], 1)
    results = []
    for blocks in (a, cols):
        blocks = jnp.take(blocks, jnp.arange(count, dtype=jnp.int32) ^ me, axis=0)
        for axis, bit in reversed(steps_of("dp") + steps_of("tensor")):
            pairs = blocks.reshape((-1, 2) + blocks.shape[1:])
            got = swap(pairs[:, 1].astype(BF16), axis, bit)
            blocks = pairs[:, 0] + got.astype(F32)
        results.append(blocks[0])
    return results


def struct(shape, dtype):
    return jax.ShapeDtypeStruct(shape, dtype)


def call(kernel, name, args, outs, scratch=(), flops=0, limit=8, hbm_outs=True):
    args = [a if isinstance(a, tuple) else (a, pltpu.VMEM) for a in args]
    moved = sum(a.size * a.dtype.itemsize for a, _ in args)
    spaces = [pl.ANY if hbm_outs and isinstance(o, jax.ShapeDtypeStruct) else pltpu.VMEM for o in outs]
    return pl.pallas_call(
        kernel,
        name=name,
        out_shape=outs,
        in_specs=[pl.BlockSpec(memory_space=space) for _, space in args],
        out_specs=[pl.BlockSpec(memory_space=space) for space in spaces],
        scratch_shapes=list(scratch),
        compiler_params=pltpu.CompilerParams(vmem_limit_bytes=limit * MIB),
        cost_estimate=pl.CostEstimate(flops=flops, bytes_accessed=moved, transcendentals=0),
    )(*[a for a, _ in args])


def on_device(tokens, lengths, row_mask, cotangent, w_qkv, w_out, gains, biases, w_up, w_down):
    images, seq_len, width = tokens.shape
    n_dp, n_t = lax.axis_size("dp"), lax.axis_size("tensor")
    index = lax.axis_index("dp") * n_t + lax.axis_index("tensor")
    me = index.astype(jnp.int32).reshape(1)
    usual = (n_dp, n_t) == (VDP, VT)
    virt = me if usual else (index // 2 % 2 * 2).astype(jnp.int32).reshape(1)
    small = width // (n_dp * n_t)
    tall = width // n_dp
    own = images * seq_len // 2
    rows = own // WIN
    per = 12 if rows % 12 == 0 else 1
    some = 6 if rows % 6 == 0 else 1
    less = 4 if rows % 4 == 0 else 1
    smem = pltpu.SMEM
    weights = (w_qkv, w_out, gains, biases, w_up, w_down)
    token_mm = 2 * own * width
    hbm = pltpu.HBM

    def in_hbm(array):
        return (pltpu.with_memory_space_constraint(array, hbm), hbm)

    def fetch(me):
        return call(
            fetch_kernel,
            "fetch",
            [(me, smem), in_hbm(tokens.reshape(images * seq_len, width))],
            [
                pltpu.VMEM((own, width), BF16),
                pltpu.VMEM((own, width), F32),
                pltpu.VMEM((own, width // 2), F32),
                pltpu.VMEM((width, own), BF16),
            ],
            [pltpu.SemaphoreType.DMA(())],
            limit=4,
        )

    def fetch_turned(me):
        return call(
            turn_kernel,
            "turn",
            [(me, smem), in_hbm(cotangent.reshape(images * seq_len, width))],
            [pltpu.VMEM((own, width), BF16), pltpu.VMEM((width, own), BF16)],
            [pltpu.SemaphoreType.DMA(())],
            limit=4,
        )

    if usual:
        weights = (w_qkv, w_out, gains, biases, w_up, w_down.T)
        high = 4 * small + 8
        packed = call(
            pack_kernel,
            "pack",
            [(me, smem)] + [in_hbm(w) for w in weights],
            [pltpu.VMEM((1, high + 2 * tall, width), BF16)],
            [pltpu.VMEM(w.shape, BF16) for w in weights] + [pltpu.SemaphoreType.DMA((6,))],
        )[0]
        planes = [packed] + [swap(packed, "dp", bit) for bit in (2, 4, 6)]
        cot, cot_t = fetch_turned(after(me, packed))
        planes[3] = after(planes[3], cot)
        held_a = jnp.concatenate([plane[:, :high] for plane in planes], 0)
        b = jnp.concatenate([plane[:, high:] for plane in planes], 0)
        far_b = swap(b, "tensor", 2)
        held_a = jnp.concatenate([held_a, swap(held_a, "dp", 1)], 0)
        b = jnp.concatenate([b, swap(b, "dp", 1)], 0)
        x, xhat1, inv1, xhat_t = fetch(after(me, (held_a, far_b)))
        held_a = jnp.concatenate([held_a, after(swap(held_a, "tensor", 2), (b, xhat1))], 0)
        far_x = swap(far_b, "dp", 1)
        got_a = swap(held_a, "tensor", 1)
        got_b = swap(b, "tensor", 1)
    else:
        held_a, got_a, held_b, got_b = other_blocks(*other_pack(*weights, index), index, n_dp, n_t)
        b, far_b = held_b[:VDP], held_b[VDP:]
        got_b, got_far = got_b[:VDP], got_b[VDP:]
        x, xhat1, inv1, xhat_t = fetch(me)
        cot, cot_t = fetch_turned(me)
    qkv, prob, o, x1, wqkv, wout, vec = call(
        functools.partial(attend_kernel, some),
        "attend",
        [(me, smem), (virt, smem), (lengths, smem), (row_mask, smem), x, xhat1, held_a, got_a],
        [
            pltpu.VMEM((own, 3 * width), BF16),
            pltpu.VMEM((rows * HEADS, WIN, WIN), BF16),
            pltpu.VMEM((own, width), BF16),
            pltpu.VMEM((own, width), F32),
            pltpu.VMEM((width, 3 * width), BF16),
            pltpu.VMEM((width, width), BF16),
            pltpu.VMEM((8, width), F32),
        ],
        flops=token_mm * (4 * width + 2 * WIN),
    )
    tall_b = 2 * (width // VDP)
    mats = [pltpu.VMEM((width, 2 * width), BF16)] * 2 + [pltpu.VMEM((2 * width, width), BF16)] * 2
    if usual:
        far_b = jnp.concatenate([far_b, after(far_x, x1)], 0)
        got_far = swap(far_b, "tensor", 1)
        got_b = after(got_b, far_b)
    wide_per = 6 if rows % 6 == 0 else 1
    *first, keep_b, send_b = call(
        functools.partial(hidden_near_kernel, wide_per),
        "hidden_near",
        [(virt, smem), x1, cot, cot_t, vec, b, got_b],
        [
            pltpu.VMEM((own, width), BF16),
            pltpu.VMEM((own, width), F32),
            pltpu.VMEM((own, width // 2), F32),
            pltpu.VMEM((own, width), F32),
            pltpu.VMEM((own, width), F32),
            pltpu.VMEM((VDP, tall_b, width), F32),
            pltpu.VMEM((VDP, tall_b, width), BF16),
        ],
        [pltpu.VMEM((own, 2 * width), BF16)] * 2 + mats,
        token_mm * 12 * width,
        12,
    )
    y, dx1, g, gout, gvec = call(
        functools.partial(hidden_far_kernel, wide_per),
        "hidden_far",
        [(virt, smem), cot, vec, far_b, got_far, *first, o],
        [
            pltpu.VMEM((own, width), BF16),
            pltpu.VMEM((own, width), F32),
            pltpu.VMEM((own, width), BF16),
            pltpu.VMEM((width, width), F32),
            pltpu.VMEM((8, width), F32),
        ],
        mats,
        token_mm * 9 * width,
    )
    core, xbit = ("tensor", 1), ("dp", 1)
    if usual:
        held_b = fold_step(keep_b, send_b, *core, g)
        y = after(y, held_b)
    y_near = swap(y, "tensor", 1)
    dqkv, keep_a, send_a = call(
        functools.partial(back_kernel, per),
        "back",
        [(virt, smem), qkv, prob, g, xhat_t, wqkv, wout, vec, gout, gvec],
        [
            pltpu.VMEM((own, 3 * width), BF16),
            pltpu.VMEM((VDP, 40, width), F32),
            pltpu.VMEM((VDP, 40, width), BF16),
        ],
        [pltpu.VMEM((width, 3 * width), F32)],
        token_mm * (4 * width + 5 * WIN),
    )
    if usual:
        held_b = fold_step(*halves(held_b), *xbit)
        vec = after(vec, held_b)
    gx, gxb, layer_out = call(
        functools.partial(token_grad_kernel, less),
        "token_grad",
        [(me, smem), dqkv, wqkv, vec, xhat1, inv1, dx1, y, y_near],
        [
            pltpu.VMEM((own, width), F32),
            pltpu.VMEM((own, width), BF16),
            struct((images * seq_len, width), BF16),
        ],
        [pltpu.VMEM((3 * width, width), BF16), pltpu.SemaphoreType.DMA((2,))],
        flops=token_mm * 3 * width,
    )
    layer_out = layer_out.reshape(images, seq_len, width)

    def place(gx_near):
        return call(
            functools.partial(place_kernel, less),
            "place",
            [(me, smem), gx, gx_near],
            [struct((images * seq_len, width), F32)],
            [pltpu.VMEM((own, width), F32), pltpu.SemaphoreType.DMA((rows // less + 1,))],
        )[0].reshape(images, seq_len, width)

    if usual:
        held_a = fold_step(keep_a, send_a, *core, gxb)
        grad_tokens = place(swap(after(gxb, held_a), "tensor", 1))
        held_a = fold_step(*halves(held_a), *xbit, grad_tokens)
        low = jnp.concatenate([held_a[1:], held_b[1:]], 1).astype(BF16)
        got = [swap(low[n - 1], "dp", 2 * n) for n in range(1, 4)]
        shapes = ((small, 3 * width), (small, width), (2, small), (3, small), (tall, width), (tall, width))
        o_qkv, o_out, o_gains, o_bias, o_up, o_down = call(
            finish_kernel,
            "finish",
            [(me, smem), held_a, held_b, *got],
            [struct(shape, F32) for shape in shapes],
            limit=2,
            hbm_outs=False,
        )
    else:
        grad_tokens = place(swap(gxb, "tensor", 1))
        grad_a, grad_b = other_reduce((keep_a, send_a), (keep_b, send_b), index, n_dp, n_t)
        o_qkv = jnp.concatenate([grad_a[p * small : (p + 1) * small] for p in range(3)], 1)
        o_out = grad_a[3 * small : 4 * small]
        o_vec = lax.dynamic_slice_in_dim(grad_a[4 * small : 4 * small + 5], index * small, small, 1)
        o_gains, o_bias = o_vec[:2], o_vec[2:]
        o_up, o_down = grad_b[:tall], grad_b[tall:]
    return layer_out, grad_tokens, o_qkv, o_out, o_gains, o_bias, o_up, o_down.T


def solution(mesh):
    in_specs = (
        P("dp", None, None),
        P("dp"),
        P("dp", None),
        P("dp", None, None),
        P(("dp", "tensor"), None),
        P(("dp", "tensor"), None),
        P(None, ("dp", "tensor")),
        P(None, ("dp", "tensor")),
        P("dp", "tensor"),
        P("tensor", "dp"),
    )
    out_specs = (
        P("dp", None, None),
        P("dp", None, None),
        P(("dp", "tensor"), None),
        P(("dp", "tensor"), None),
        P(None, ("dp", "tensor")),
        P(None, ("dp", "tensor")),
        P("dp", "tensor"),
        P("tensor", "dp"),
    )
    return jax.shard_map(
        on_device, mesh=mesh, in_specs=in_specs, out_specs=out_specs, check_vma=False
    )
```

```python
import functools

import jax
import jax.numpy as jnp
from jax import lax
from jax.experimental import pallas as pl
from jax.experimental.pallas import tpu as pltpu
from jax.sharding import PartitionSpec as P

HEADS = 2
WIN = 96
F32 = jnp.float32
BF16 = jnp.bfloat16
VDP, VT = 8, 4
CHIPS = VDP * VT // 2
MIB = 1 << 20

NN = ((1,), (0,))
NT = ((1,), (1,))
TN = ((0,), (0,))


def dot(a, b, dims):
    return lax.dot_general(a, b, (dims, ((), ())), preferred_element_type=F32)


def twist(i):
    return (i & 1) * 4 + (i >> 1)


def spot(m):
    return (m % 2) * VDP + twist(m // 2)


def norm_parts(values):
    center = values - jnp.mean(values, -1, keepdims=True)
    inv = lax.rsqrt(jnp.mean(center * center, -1, keepdims=True) + 1e-05)
    return center * inv, inv


def norm_back(grad, xhat, inv, gain):
    scaled = grad * gain
    return inv * (
        scaled
        - jnp.mean(scaled, -1, keepdims=True)
        - xhat * jnp.mean(scaled * xhat, -1, keepdims=True)
    )


def gelu_both(u):
    c = 0.7978845608028654
    u2 = u * u
    t = jnp.tanh(u * (c + (c * 0.044715) * u2))
    half = 0.5 + 0.5 * t
    value = u * half
    slope = half + (value - value * half) * (2 * c + (6 * c * 0.044715) * u2)
    return value, slope


def apart(both, hs):
    blocks = []
    for h in range(HEADS):
        parts = [jnp.zeros((WIN, hs), BF16)] * HEADS
        parts[h] = both[:, h * hs : (h + 1) * hs]
        blocks.append(jnp.concatenate(parts, 1))
        blocks.append(jnp.zeros((hs - WIN, HEADS * hs), BF16))
    return jnp.concatenate(blocks, 0)


def flipped(heads, hs):
    pad = jnp.zeros((hs - WIN, hs), BF16)
    return jnp.concatenate([jnp.concatenate([p, pad], 0).T[:WIN] for p in heads], 1)


def pack_kernel(me, *refs):
    sources, packed, held, sems = refs[:6], refs[6], refs[7:13], refs[13]
    copies = [pltpu.make_async_copy(a, b, sems.at[n]) for n, (a, b) in enumerate(zip(sources, held))]
    for copy in copies:
        copy.start()
    qkv, out, gains, biases, up, down = held
    small, width = out.shape
    tall = up.shape[0]
    lane = lax.broadcasted_iota(jnp.int32, (1, width), 1)
    mine = lane // small == me[0]
    for copy in copies:
        copy.wait()
    for part in range(3):
        packed[0, part * small : (part + 1) * small] = qkv[:, part * width : (part + 1) * width]
    packed[0, 3 * small : 4 * small] = out[...]
    rows = [gains[0:1], gains[1:2], biases[0:1], biases[1:2], biases[2:3]]
    vals = jnp.concatenate(rows + [jnp.zeros((3, small), BF16)], 0).astype(F32)
    wide = jnp.concatenate([vals] * (width // small), 1)
    at = 4 * small + 8
    packed[0, 4 * small : at] = jnp.where(mine, wide, 0.0).astype(BF16)
    packed[0, at : at + tall] = up[...]
    packed[0, at + tall :] = down[...]


def fetch_kernel(me, tokens, x_ref, xhat_ref, inv_ref, xhat_t, sem):
    own, width = x_ref.shape
    copy = pltpu.make_async_copy(tokens.at[pl.ds(lax.rem(me[0], 2) * own, own)], x_ref, sem)
    copy.start()
    ones = jnp.full((width, width), 1.0 / width, BF16)
    size = 256 if own % 256 == 0 else own
    copy.wait()
    for n in range(own // size):
        part = slice(n * size, (n + 1) * size)
        x = x_ref[part]
        center = x.astype(F32) - dot(x, ones, NN)
        inv = lax.rsqrt(dot((center * center).astype(BF16), ones, NN) + 1e-05)
        xhat = center * inv
        xhat_ref[part] = xhat
        inv_ref[part] = inv[:, :1]
        xhat_t[:, part] = xhat.astype(BF16).T


def turn_kernel(me, cot, cot_ref, cot_t, sem):
    own = cot_ref.shape[0]
    copy = pltpu.make_async_copy(cot.at[pl.ds(lax.rem(me[0], 2) * own, own)], cot_ref, sem)
    copy.start()
    size = 256 if own % 256 == 0 else own
    copy.wait()
    for n in range(own // size):
        part = slice(n * size, (n + 1) * size)
        cot_t[:, part] = cot_ref[part].T


def attend_kernel(
    per, me, virt, lens, live, x_ref, xhat_ref, held, got,
    qkv_ref, prob_ref, o_ref, x1_ref, wqkv, wout, vec,
):
    tokens, width = x_ref.shape
    rows = tokens // WIN
    hs = width // HEADS
    here = twist(virt[0] // 4)
    y_own = (virt[0] // 2) % 2
    first = virt[0] % 2 == 0
    total = jnp.zeros((8, width), F32)
    for m in range(CHIPS):
        k = spot(m) ^ (here + y_own * VDP)
        a = held[k].astype(F32)
        b = got[k].astype(F32)
        even = jnp.where(first, a, b)
        odd = jnp.where(first, b, a)
        for part in range(3):
            both = jnp.concatenate([even[part * 8 : part * 8 + 8], odd[part * 8 : part * 8 + 8]], 0)
            wqkv[m * 16 : m * 16 + 16, part * width : (part + 1) * width] = both.astype(BF16)
        both = jnp.concatenate([even[24:32], odd[24:32]], 0)
        wout[m * 16 : m * 16 + 16] = both.astype(BF16)
        total = total + a[32:40] + b[32:40]
    vec[...] = total
    scale = hs**-0.5
    ii = lax.broadcasted_iota(jnp.int32, (WIN, hs), 0)
    jj = lax.broadcasted_iota(jnp.int32, (WIN, hs), 1)
    same = ii == jj
    image_rows = live.shape[1]
    base = lax.rem(me[0], 2) * rows

    def enter(c):
        part = slice(c * per * WIN, (c + 1) * per * WIN)
        h1 = (xhat_ref[part] * total[0:1] + total[2:3]).astype(BF16)
        qkv = dot(h1, wqkv[...], NN).astype(BF16)
        qkv_ref[part] = qkv
        scores = []
        for r in range(per):
            at = slice(r * WIN, (r + 1) * WIN)
            scores.append(dot(qkv[at, :width], apart(qkv[at, width : 2 * width], hs), NT))
        return qkv, scores

    ahead = enter(0)
    for c in range(rows // per):
        qkv, scores = ahead
        if c + 1 < rows // per:
            ahead = enter(c + 1)
        part = slice(c * per * WIN, (c + 1) * per * WIN)
        probs = []
        for r in range(per):
            row = base + c * per + r
            image = row // image_rows
            inside = row - image * image_rows
            reach = jnp.where(live[image, inside] == 1, lens[image] - inside * WIN, 0)
            allowed = same | (jj < jnp.minimum(ii, reach))
            heads = []
            for h in range(HEADS):
                s = jnp.where(allowed, scores[r][:, h * hs : (h + 1) * hs], -1e30)
                e = jnp.exp((s - jnp.max(s, -1, keepdims=True)) * scale)
                heads.append((e * (1.0 / jnp.sum(e, -1, keepdims=True))).astype(BF16))
            probs.append(jnp.concatenate(heads, 1))
        mixed = []
        for r in range(per):
            at = slice(r * WIN, (r + 1) * WIN)
            mixed.append(dot(probs[r], apart(qkv[at, 2 * width :], hs), NN).astype(BF16))
        o = jnp.concatenate(mixed, 0)
        for n, p in enumerate(probs):
            prob_ref[c * per + n] = p
        o_ref[part] = o
        x1_ref[part] = x_ref[part].astype(F32) + dot(o, wout[...], NN)


def join(virt, blocks, n, up, down_t):
    tall = blocks.shape[1] // 2
    width = up.shape[0]
    here = twist(virt[0] // 4)
    for i in range(VDP):
        k = twist(i) ^ here
        at = slice(i * tall, (i + 1) * tall)
        cols = slice(n * width, (n + 1) * width)
        up[at, cols] = blocks[k, :tall]
        down_t[at, cols] = blocks[k, tall:]


def hidden_units(h2, dyb, up, down_t):
    u = dot(h2, up[...], NN).astype(BF16)
    da = dot(dyb, down_t[...], NN).astype(BF16)
    a, slope = gelu_both(u)
    return a, da * slope


def hidden_near_kernel(
    per, virt, x1_ref, cot_ref, cot_t, vec, own, got,
    h2_ref, xhat_ref, inv_ref, f_ref, dh2_ref, keep, send,
    a_ref, du_ref, up, down_t, up_t, down,
):
    tokens, width = x1_ref.shape
    size = per * WIN
    join(virt, own, 0, up, down_t)
    join(virt, got, 1, up, down_t)
    up_t[...] = up[...].T
    down[...] = down_t[...].T
    for c in range(tokens // size):
        part = slice(c * size, (c + 1) * size)
        x1 = x1_ref[part]
        xhat, inv = norm_parts(x1)
        xhat_ref[part] = xhat
        inv_ref[part] = inv
        h2 = (xhat * vec[1:2] + vec[3:4]).astype(BF16)
        h2_ref[part] = h2
        a, du = hidden_units(h2, cot_ref[part], up, down_t)
        a_ref[part] = a
        du_ref[part] = du
        f_ref[part] = x1 + vec[4:5] + dot(a, down[...], NN)
        dh2_ref[part] = dot(du, up_t[...], NN)
    gdown = dot(cot_t[...], a_ref[...], NN)
    gup = dot(h2_ref[...], du_ref[...], TN)
    tall = width // VDP
    here = twist(virt[0] // 4)
    for i in range(VDP):
        at = slice(i * tall, (i + 1) * tall)
        k = twist(i) ^ here
        keep[k, :tall] = gup[at, :width]
        keep[k, tall:] = gdown[at, :width]
        send[k, :tall] = gup[at, width:].astype(BF16)
        send[k, tall:] = gdown[at, width:].astype(BF16)


def hidden_far_kernel(
    per, virt, cot_ref, vec, own, got, h2_ref, xhat_ref, inv_ref, f_ref, dh2_ref, o_ref,
    y_ref, dx1_ref, g_ref, gout, gvec,
    up, down_t, up_t, down,
):
    tokens, width = h2_ref.shape
    size = per * WIN
    join(virt, own, 0, up, down_t)
    join(virt, got, 1, up, down_t)
    up_t[...] = up[...].T
    down[...] = down_t[...].T
    sums = [jnp.zeros((1, width), F32)] * 3
    for c in range(tokens // size):
        part = slice(c * size, (c + 1) * size)
        a, du = hidden_units(h2_ref[part], cot_ref[part], up, down_t)
        y_ref[part] = (f_ref[part] + dot(a, down[...], NN)).astype(BF16)
        dh2 = dh2_ref[part] + dot(du, up_t[...], NN)
        dy = cot_ref[part].astype(F32)
        xhat = xhat_ref[part]
        dx1 = dy + norm_back(dh2, xhat, inv_ref[part], vec[1:2])
        dx1_ref[part] = dx1
        g_ref[part] = dx1.astype(BF16)
        for n, term in enumerate((dh2 * xhat, dh2, dy)):
            sums[n] = sums[n] + jnp.sum(term, 0, keepdims=True)
    gout[...] = dot(o_ref[...], g_ref[...], TN)
    zero = jnp.zeros((1, width), F32)
    gvec[...] = jnp.concatenate([zero, sums[0], zero, sums[1], sums[2], zero, zero, zero], 0)


def own_rows(virt, i, other):
    core = virt[0] % 2
    core = 1 - core if other else core
    return pl.ds(pl.multiple_of(i * 32 + ((virt[0] // 2) % 2) * 16 + core * 8, 8), 8)


def back_kernel(
    per, virt, qkv_ref, prob_ref, g_ref, xhat_t, wqkv, wout, vec, gout, gvec,
    dqkv, keep, send,
    gqkv,
):
    tokens, width = g_ref.shape
    hs = width // HEADS
    scale = hs**-0.5
    rows = tokens // WIN

    def piece(r, part):
        return qkv_ref[r * WIN : (r + 1) * WIN, part * width : (part + 1) * width]

    def enter(start):
        do = dot(g_ref[start * WIN : (start + per) * WIN], wout[...], NT).astype(BF16)
        dps, dvs, probs = [], [], []
        for n in range(per):
            r = start + n
            mine = do[n * WIN : (n + 1) * WIN]
            p = prob_ref[r]
            heads = [p[:, h * hs : (h + 1) * hs] for h in range(HEADS)]
            dps.append(dot(mine, apart(piece(r, 2), hs), NT))
            dvs.append(dot(flipped(heads, hs), apart(mine, hs), NN).astype(BF16))
            probs.append(heads)
        return probs, dps, dvs

    ahead = enter(0)
    for start in range(0, rows, per):
        probs, dps, dvs = ahead
        if start + per < rows:
            ahead = enter(start + per)
        dss = []
        for heads, dp in zip(probs, dps):
            mine = []
            for h, p in enumerate(heads):
                pf = p.astype(F32)
                dph = dp[:, h * hs : (h + 1) * hs]
                ds = pf * (dph - jnp.sum(dph * pf, -1, keepdims=True)) * scale
                mine.append(ds.astype(BF16))
            dss.append(mine)
        dqs, dks = [], []
        for n, mine in enumerate(dss):
            both = jnp.concatenate(mine, 1)
            dqs.append(dot(both, apart(piece(start + n, 1), hs), NN).astype(BF16))
            dks.append(dot(flipped(mine, hs), apart(piece(start + n, 0), hs), NN).astype(BF16))
        for n in range(per):
            at = slice((start + n) * WIN, (start + n + 1) * WIN)
            for part, values in enumerate((dqs, dks, dvs)):
                dqkv[at, part * width : (part + 1) * width] = values[n]
    grad = dot(xhat_t[...], dqkv[...], NN)
    total = jnp.zeros((1, 3 * width), F32)
    for r in range(tokens // WIN):
        total = total + jnp.sum(dqkv[r * WIN : (r + 1) * WIN].astype(F32), 0, keepdims=True)
    w = wqkv[...].astype(F32)
    cols = jnp.concatenate([
        jnp.broadcast_to(jnp.sum(w * grad, -1, keepdims=True), (width, 64)),
        jnp.broadcast_to(jnp.sum(w * total, -1, keepdims=True), (width, 64)),
    ], 1)
    lines = cols.T
    gain, from_total = lines[0:1], lines[64:65]
    vec_t = vec[...].T
    gqkv[...] = grad * vec_t[:, 0:1] + total * vec_t[:, 2:3]
    rest = gvec[...]
    sums = jnp.concatenate([gain, rest[1:2], from_total, rest[3:]], 0)
    here = twist(virt[0] // 4)
    for i in range(VDP):
        k = twist(i) ^ here
        mine, other = own_rows(virt, i, 0), own_rows(virt, i, 1)
        theirs = []
        for part in range(3):
            at = slice(part * width, (part + 1) * width)
            keep[k, part * 8 : part * 8 + 8] = gqkv[mine, at]
            theirs.append(gqkv[other, at])
        keep[k, 24:32] = gout[mine]
        keep[k, 32:] = sums
        send[k] = jnp.concatenate(theirs + [gout[other], sums], 0).astype(BF16)


def token_grad_kernel(per, me, dqkv, wqkv, vec, xhat_ref, inv_ref, dx1_ref, y, y_near, gx, gxb, out, turned, sems):
    own = dqkv.shape[0]
    size = per * WIN
    copies = []
    for n, source in enumerate((y, y_near)):
        at = pl.ds((lax.rem(me[0], 2) ^ n) * own, own)
        copies.append(pltpu.make_async_copy(source, out.at[at], sems.at[n]))
        copies[-1].start()
    turned[...] = wqkv[...].T
    for c in range(own // size):
        part = slice(c * size, (c + 1) * size)
        dh1 = dot(dqkv[part], turned[...], NN)
        values = dx1_ref[part] + norm_back(dh1, xhat_ref[part], inv_ref[part], vec[0:1])
        gx[part] = values
        gxb[part] = values.astype(BF16)
    for copy in copies:
        copy.wait()


def place_kernel(per, me, mine, theirs, out, wide, sems):
    own = theirs.shape[0]
    size = per * WIN
    here = lax.rem(me[0], 2) * own
    copies = [pltpu.make_async_copy(mine, out.at[pl.ds(here, own)], sems.at[own // size])]
    copies[0].start()
    for c in range(own // size):
        part = pl.ds(c * size, size)
        wide[part] = theirs[part].astype(F32)
        at = pl.ds(own - here + c * size, size)
        copies.append(pltpu.make_async_copy(wide.at[part], out.at[at], sems.at[c]))
        copies[-1].start()
    for copy in copies:
        copy.wait()


def finish_kernel(me, keep_a, keep_b, one, two, three, qkv, out, gains, biases, up, down):
    small, width = out.shape
    tall = up.shape[0]
    high = 4 * small + 8
    total, units = keep_a[0], keep_b[0]
    for got in (one, two, three):
        total = total + got[:high].astype(F32)
        units = units + got[high:].astype(F32)
    for part in range(3):
        qkv[:, part * width : (part + 1) * width] = total[part * small : (part + 1) * small]
    out[...] = total[3 * small : 4 * small]
    vec = pltpu.roll(total[4 * small :], width - me[0] * small, 1)[:, :small]
    gains[...] = vec[:2]
    biases[...] = vec[2:5]
    up[...] = units[:tall]
    down[...] = units[tall:]


def swap(block, axis, bit):
    size = lax.axis_size(axis)
    return lax.ppermute(block, axis, [(i, i ^ bit) for i in range(size)])


def steps_of(axis):
    return [(axis, 1 << k) for k in reversed(range(lax.axis_size(axis).bit_length() - 1))]


def after(value, other):
    return lax.optimization_barrier((value, other))[0]


def halves(held):
    half = held.shape[0] // 2
    return held[:half], held[half:].astype(BF16)


def fold_step(keep, send, axis, bit, past=None):
    got = swap(send, axis, bit)
    return keep + (got if past is None else after(got, past)).astype(F32)


def bit_reverse(index, count):
    out = 0 * index
    for k in range(count):
        out = out | (((index >> k) & 1) << (count - 1 - k))
    return out


def by_device(block, me):
    blocks = block[None]
    for axis, bit in steps_of("dp") + steps_of("tensor"):
        blocks = jnp.concatenate([blocks, swap(blocks, axis, bit)], 0)
    count = blocks.shape[0]
    order = jnp.arange(count, dtype=jnp.int32) ^ me
    return jnp.take(blocks, bit_reverse(order, count.bit_length() - 1), axis=0)


def other_pack(w_qkv, w_out, gains, biases, w_up, w_down, me):
    small, width = w_out.shape
    qkv = w_qkv.reshape(small, 3, width).transpose(1, 0, 2).reshape(3 * small, width)
    rows = jnp.concatenate([gains, biases], 0)
    place = jnp.zeros((8, width), BF16)
    place = lax.dynamic_update_slice(place, rows, (jnp.int32(0), me * small))
    return jnp.concatenate([qkv, w_out, place], 0), jnp.concatenate([w_up, w_down.T], 0)


def other_blocks(a, b, me, n_dp, n_t):
    a = by_device(a, me)
    b = by_device(b, me)
    width = a.shape[2]
    count = n_dp * n_t
    small = width // count
    big = width // (VDP * VT)
    mats = a[:, : 4 * small].reshape(count, 4, small, width).transpose(1, 0, 2, 3)
    mats = mats.reshape(4, VDP * VT, big, width).transpose(1, 0, 2, 3).reshape(VDP * VT, 4 * big, width)
    vec = jnp.sum(a[:, 4 * small :].astype(F32), 0).astype(BF16)
    vecs = jnp.concatenate([vec[None], jnp.zeros((VDP * VT - 1, 8, width), BF16)], 0)
    a = jnp.concatenate([mats, vecs], 1)
    tall = width // n_dp
    b = b.reshape(n_dp, VT, 2, tall, width).transpose(1, 2, 0, 3, 4)
    b = b.reshape(VT, 2, VDP, width // VDP, width).transpose(2, 0, 1, 3, 4)
    b = b.reshape(VDP * VT, 2 * (width // VDP), width)

    y_own = (me // 2) % 2

    def placed(blocks):
        pairs = blocks.reshape((CHIPS, 2) + blocks.shape[1:])
        chips = sorted(range(CHIPS), key=spot)
        pairs = jnp.stack([pairs[m] for m in chips], 0)
        pairs = jnp.where(y_own == 1, jnp.roll(pairs, VDP, 0), pairs)
        return pairs[:, 0], pairs[:, 1]

    return placed(a) + placed(b)


def other_reduce(pair_a, pair_b, me, n_dp, n_t):
    count = n_dp * n_t
    y_own = (me // 2) % 2

    def whole(keep, send):
        pairs = jnp.stack([keep, send.astype(F32)], 1)
        pairs = jnp.stack([pairs[twist(i)] for i in range(VDP)], 0)
        none = jnp.zeros_like(pairs)
        both = jnp.stack([jnp.where(y_own == y, pairs, none) for y in range(2)], 1)
        return both.reshape((VDP * VT,) + keep.shape[1:])

    def rows_of(blocks, parts):
        big = blocks.shape[1] // parts
        mats = blocks.reshape(VDP * VT, parts, big, -1).transpose(1, 0, 2, 3)
        mats = mats.reshape(parts, count, VDP * VT * big // count, -1).transpose(1, 0, 2, 3)
        return mats.reshape(count, -1, blocks.shape[2])

    def vec_of(blocks):
        picked = jnp.where(y_own == 0, blocks[0], 0.0)
        return jnp.broadcast_to(picked[None], (count,) + picked.shape)

    a, b = whole(*pair_a), whole(*pair_b)
    width = a.shape[2]
    tall, high = width // n_dp, width // VDP
    cols = b.reshape(VDP, VT, 2, high, width).transpose(1, 2, 0, 3, 4)
    cols = cols.reshape(VT, 2, n_dp, tall, width).transpose(2, 0, 1, 3, 4)
    cols = cols.reshape(count, 2 * tall, width)
    a = jnp.concatenate([rows_of(a[:, :32], 4), vec_of(a[:, 32:])], 1)
    results = []
    for blocks in (a, cols):
        blocks = jnp.take(blocks, jnp.arange(count, dtype=jnp.int32) ^ me, axis=0)
        for axis, bit in reversed(steps_of("dp") + steps_of("tensor")):
            pairs = blocks.reshape((-1, 2) + blocks.shape[1:])
            got = swap(pairs[:, 1].astype(BF16), axis, bit)
            blocks = pairs[:, 0] + got.astype(F32)
        results.append(blocks[0])
    return results


def struct(shape, dtype):
    return jax.ShapeDtypeStruct(shape, dtype)


def call(kernel, name, args, outs, scratch=(), flops=0, limit=8, hbm_outs=True):
    args = [a if isinstance(a, tuple) else (a, pltpu.VMEM) for a in args]
    moved = sum(a.size * a.dtype.itemsize for a, _ in args)
    spaces = [pl.ANY if hbm_outs and isinstance(o, jax.ShapeDtypeStruct) else pltpu.VMEM for o in outs]
    return pl.pallas_call(
        kernel,
        name=name,
        out_shape=outs,
        in_specs=[pl.BlockSpec(memory_space=space) for _, space in args],
        out_specs=[pl.BlockSpec(memory_space=space) for space in spaces],
        scratch_shapes=list(scratch),
        compiler_params=pltpu.CompilerParams(vmem_limit_bytes=limit * MIB),
        cost_estimate=pl.CostEstimate(flops=flops, bytes_accessed=moved, transcendentals=0),
    )(*[a for a, _ in args])


def on_device(tokens, lengths, row_mask, cotangent, w_qkv, w_out, gains, biases, w_up, w_down):
    images, seq_len, width = tokens.shape
    n_dp, n_t = lax.axis_size("dp"), lax.axis_size("tensor")
    index = lax.axis_index("dp") * n_t + lax.axis_index("tensor")
    me = index.astype(jnp.int32).reshape(1)
    usual = (n_dp, n_t) == (VDP, VT)
    virt = me if usual else (index // 2 % 2 * 2).astype(jnp.int32).reshape(1)
    small = width // (n_dp * n_t)
    tall = width // n_dp
    own = images * seq_len // 2
    rows = own // WIN
    per = 12 if rows % 12 == 0 else 1
    some = 6 if rows % 6 == 0 else 1
    less = 4 if rows % 4 == 0 else 1
    smem = pltpu.SMEM
    weights = (w_qkv, w_out, gains, biases, w_up, w_down)
    token_mm = 2 * own * width
    hbm = pltpu.HBM

    def in_hbm(array):
        return (pltpu.with_memory_space_constraint(array, hbm), hbm)

    def fetch(me):
        return call(
            fetch_kernel,
            "fetch",
            [(me, smem), in_hbm(tokens.reshape(images * seq_len, width))],
            [
                pltpu.VMEM((own, width), BF16),
                pltpu.VMEM((own, width), F32),
                pltpu.VMEM((own, 1), F32),
                pltpu.VMEM((width, own), BF16),
            ],
            [pltpu.SemaphoreType.DMA(())],
            limit=4,
        )

    def fetch_turned(me):
        return call(
            turn_kernel,
            "turn",
            [(me, smem), in_hbm(cotangent.reshape(images * seq_len, width))],
            [pltpu.VMEM((own, width), BF16), pltpu.VMEM((width, own), BF16)],
            [pltpu.SemaphoreType.DMA(())],
            limit=4,
        )

    if usual:
        weights = (w_qkv, w_out, gains, biases, w_up, w_down.T)
        high = 4 * small + 8
        packed = call(
            pack_kernel,
            "pack",
            [(me, smem)] + [in_hbm(w) for w in weights],
            [pltpu.VMEM((1, high + 2 * tall, width), BF16)],
            [pltpu.VMEM(w.shape, BF16) for w in weights] + [pltpu.SemaphoreType.DMA((6,))],
        )[0]
        planes = [packed] + [swap(packed, "dp", bit) for bit in (2, 4, 6)]
        cot, cot_t = fetch_turned(after(me, packed))
        planes[3] = after(planes[3], cot)
        held_a = jnp.concatenate([plane[:, :high] for plane in planes], 0)
        b = jnp.concatenate([plane[:, high:] for plane in planes], 0)
        far_b = swap(b, "tensor", 2)
        held_a = jnp.concatenate([held_a, swap(held_a, "dp", 1)], 0)
        b = jnp.concatenate([b, swap(b, "dp", 1)], 0)
        x, xhat1, inv1, xhat_t = fetch(after(me, (held_a, far_b)))
        held_a = jnp.concatenate([held_a, after(swap(held_a, "tensor", 2), (b, xhat1))], 0)
        far_x = swap(far_b, "dp", 1)
        got_a = swap(held_a, "tensor", 1)
        got_b = swap(b, "tensor", 1)
    else:
        held_a, got_a, held_b, got_b = other_blocks(*other_pack(*weights, index), index, n_dp, n_t)
        b, far_b = held_b[:VDP], held_b[VDP:]
        got_b, got_far = got_b[:VDP], got_b[VDP:]
        x, xhat1, inv1, xhat_t = fetch(me)
        cot, cot_t = fetch_turned(me)
    qkv, prob, o, x1, wqkv, wout, vec = call(
        functools.partial(attend_kernel, some),
        "attend",
        [(me, smem), (virt, smem), (lengths, smem), (row_mask, smem), x, xhat1, held_a, got_a],
        [
            pltpu.VMEM((own, 3 * width), BF16),
            pltpu.VMEM((rows, WIN, width), BF16),
            pltpu.VMEM((own, width), BF16),
            pltpu.VMEM((own, width), F32),
            pltpu.VMEM((width, 3 * width), BF16),
            pltpu.VMEM((width, width), BF16),
            pltpu.VMEM((8, width), F32),
        ],
        flops=token_mm * (4 * width + 2 * WIN),
    )
    tall_b = 2 * (width // VDP)
    mats = [pltpu.VMEM((width, 2 * width), BF16)] * 2 + [pltpu.VMEM((2 * width, width), BF16)] * 2
    if usual:
        far_b = jnp.concatenate([far_b, after(far_x, x1)], 0)
        got_far = swap(far_b, "tensor", 1)
        got_b = after(got_b, far_b)
    wide_per = 6 if rows % 6 == 0 else 1
    *first, keep_b, send_b = call(
        functools.partial(hidden_near_kernel, wide_per),
        "hidden_near",
        [(virt, smem), x1, cot, cot_t, vec, b, got_b],
        [
            pltpu.VMEM((own, width), BF16),
            pltpu.VMEM((own, width), F32),
            pltpu.VMEM((own, 1), F32),
            pltpu.VMEM((own, width), F32),
            pltpu.VMEM((own, width), F32),
            pltpu.VMEM((VDP, tall_b, width), F32),
            pltpu.VMEM((VDP, tall_b, width), BF16),
        ],
        [pltpu.VMEM((own, 2 * width), BF16)] * 2 + mats,
        token_mm * 12 * width,
        12,
    )
    y, dx1, g, gout, gvec = call(
        functools.partial(hidden_far_kernel, wide_per),
        "hidden_far",
        [(virt, smem), cot, vec, far_b, got_far, *first, o],
        [
            pltpu.VMEM((own, width), BF16),
            pltpu.VMEM((own, width), F32),
            pltpu.VMEM((own, width), BF16),
            pltpu.VMEM((width, width), F32),
            pltpu.VMEM((8, width), F32),
        ],
        mats,
        token_mm * 9 * width,
    )
    core, xbit = ("tensor", 1), ("dp", 1)
    if usual:
        held_b = fold_step(keep_b, send_b, *core, g)
        y = after(y, held_b)
    y_near = swap(y, "tensor", 1)
    dqkv, keep_a, send_a = call(
        functools.partial(back_kernel, per),
        "back",
        [(virt, smem), qkv, prob, g, xhat_t, wqkv, wout, vec, gout, gvec],
        [
            pltpu.VMEM((own, 3 * width), BF16),
            pltpu.VMEM((VDP, 40, width), F32),
            pltpu.VMEM((VDP, 40, width), BF16),
        ],
        [pltpu.VMEM((width, 3 * width), F32)],
        token_mm * (4 * width + 5 * WIN),
    )
    if usual:
        held_b = fold_step(*halves(held_b), *xbit)
        vec = after(vec, held_b)
    gx, gxb, layer_out = call(
        functools.partial(token_grad_kernel, less),
        "token_grad",
        [(me, smem), dqkv, wqkv, vec, xhat1, inv1, dx1, y, y_near],
        [
            pltpu.VMEM((own, width), F32),
            pltpu.VMEM((own, width), BF16),
            struct((images * seq_len, width), BF16),
        ],
        [pltpu.VMEM((3 * width, width), BF16), pltpu.SemaphoreType.DMA((2,))],
        flops=token_mm * 3 * width,
    )
    layer_out = layer_out.reshape(images, seq_len, width)

    def place(gx_near):
        return call(
            functools.partial(place_kernel, less),
            "place",
            [(me, smem), gx, gx_near],
            [struct((images * seq_len, width), F32)],
            [pltpu.VMEM((own, width), F32), pltpu.SemaphoreType.DMA((rows // less + 1,))],
        )[0].reshape(images, seq_len, width)

    if usual:
        held_a = fold_step(keep_a, send_a, *core, gxb)
        grad_tokens = place(swap(after(gxb, held_a), "tensor", 1))
        held_a = fold_step(*halves(held_a), *xbit, grad_tokens)
        low = jnp.concatenate([held_a[1:], held_b[1:]], 1).astype(BF16)
        got = [swap(low[n - 1], "dp", 2 * n) for n in range(1, 4)]
        shapes = ((small, 3 * width), (small, width), (2, small), (3, small), (tall, width), (tall, width))
        o_qkv, o_out, o_gains, o_bias, o_up, o_down = call(
            finish_kernel,
            "finish",
            [(me, smem), held_a, held_b, *got],
            [struct(shape, F32) for shape in shapes],
            limit=2,
            hbm_outs=False,
        )
    else:
        grad_tokens = place(swap(gxb, "tensor", 1))
        grad_a, grad_b = other_reduce((keep_a, send_a), (keep_b, send_b), index, n_dp, n_t)
        o_qkv = jnp.concatenate([grad_a[p * small : (p + 1) * small] for p in range(3)], 1)
        o_out = grad_a[3 * small : 4 * small]
        o_vec = lax.dynamic_slice_in_dim(grad_a[4 * small : 4 * small + 5], index * small, small, 1)
        o_gains, o_bias = o_vec[:2], o_vec[2:]
        o_up, o_down = grad_b[:tall], grad_b[tall:]
    return layer_out, grad_tokens, o_qkv, o_out, o_gains, o_bias, o_up, o_down.T


def solution(mesh):
    in_specs = (
        P("dp", None, None),
        P("dp"),
        P("dp", None),
        P("dp", None, None),
        P(("dp", "tensor"), None),
        P(("dp", "tensor"), None),
        P(None, ("dp", "tensor")),
        P(None, ("dp", "tensor")),
        P("dp", "tensor"),
        P("tensor", "dp"),
    )
    out_specs = (
        P("dp", None, None),
        P("dp", None, None),
        P(("dp", "tensor"), None),
        P(("dp", "tensor"), None),
        P(None, ("dp", "tensor")),
        P(None, ("dp", "tensor")),
        P("dp", "tensor"),
        P("tensor", "dp"),
    )
    return jax.shard_map(
        on_device, mesh=mesh, in_specs=in_specs, out_specs=out_specs, check_vma=False
    )
```

```python
import functools

import jax
import jax.numpy as jnp
from jax import lax
from jax.experimental import pallas as pl
from jax.experimental.pallas import tpu as pltpu
from jax.sharding import PartitionSpec as P

HEADS = 2
WIN = 96
F32 = jnp.float32
BF16 = jnp.bfloat16
VDP, VT = 8, 4
CHIPS = VDP * VT // 2
MIB = 1 << 20

NN = ((1,), (0,))
NT = ((1,), (1,))
TN = ((0,), (0,))


def dot(a, b, dims):
    return lax.dot_general(a, b, (dims, ((), ())), preferred_element_type=F32)


def twist(i):
    return (i & 1) * 4 + (i >> 1)


def spot(m):
    return (m % 2) * VDP + twist(m // 2)


def norm_parts(values):
    center = values - jnp.mean(values, -1, keepdims=True)
    inv = lax.rsqrt(jnp.mean(center * center, -1, keepdims=True) + 1e-05)
    return center * inv, inv


def norm_back(grad, xhat, inv, gain):
    scaled = grad * gain
    return inv * (
        scaled
        - jnp.mean(scaled, -1, keepdims=True)
        - xhat * jnp.mean(scaled * xhat, -1, keepdims=True)
    )


def gelu_both(u):
    c = 0.7978845608028654
    u2 = u * u
    t = jnp.tanh(u * (c + (c * 0.044715) * u2))
    half = 0.5 + 0.5 * t
    value = u * half
    slope = half + (value - value * half) * (2 * c + (6 * c * 0.044715) * u2)
    return value, slope


def apart(both, hs):
    blocks = []
    for h in range(HEADS):
        parts = [jnp.zeros((WIN, hs), BF16)] * HEADS
        parts[h] = both[:, h * hs : (h + 1) * hs]
        blocks.append(jnp.concatenate(parts, 1))
        blocks.append(jnp.zeros((hs - WIN, HEADS * hs), BF16))
    return jnp.concatenate(blocks, 0)


def pack_kernel(me, *refs):
    sources, packed, held, sems = refs[:6], refs[6], refs[7:13], refs[13]
    copies = [pltpu.make_async_copy(a, b, sems.at[n]) for n, (a, b) in enumerate(zip(sources, held))]
    for copy in copies:
        copy.start()
    qkv, out, gains, biases, up, down = held
    small, width = out.shape
    tall = up.shape[0]
    lane = lax.broadcasted_iota(jnp.int32, (1, width), 1)
    mine = lane // small == me[0]
    for copy in copies:
        copy.wait()
    for part in range(3):
        packed[0, part * small : (part + 1) * small] = qkv[:, part * width : (part + 1) * width]
    packed[0, 3 * small : 4 * small] = out[...]
    rows = [gains[0:1], gains[1:2], biases[0:1], biases[1:2], biases[2:3]]
    vals = jnp.concatenate(rows + [jnp.zeros((3, small), BF16)], 0).astype(F32)
    wide = jnp.concatenate([vals] * (width // small), 1)
    at = 4 * small + 8
    packed[0, 4 * small : at] = jnp.where(mine, wide, 0.0).astype(BF16)
    packed[0, at : at + tall] = up[...]
    packed[0, at + tall :] = down[...]


def fetch_kernel(me, tokens, x_ref, xhat_ref, inv_ref, xhat_t, sem):
    own, width = x_ref.shape
    copy = pltpu.make_async_copy(tokens.at[pl.ds(lax.rem(me[0], 2) * own, own)], x_ref, sem)
    copy.start()
    ones = jnp.full((width, width), 1.0 / width, BF16)
    size = 256 if own % 256 == 0 else own
    copy.wait()
    for n in range(own // size):
        part = slice(n * size, (n + 1) * size)
        x = x_ref[part]
        center = x.astype(F32) - dot(x, ones, NN)
        inv = lax.rsqrt(dot((center * center).astype(BF16), ones, NN) + 1e-05)
        xhat = center * inv
        xhat_ref[part] = xhat
        inv_ref[part] = inv[:, :1]
        xhat_t[:, part] = xhat.astype(BF16).T


def turn_kernel(me, cot, cot_ref, cot_t, sem):
    own = cot_ref.shape[0]
    copy = pltpu.make_async_copy(cot.at[pl.ds(lax.rem(me[0], 2) * own, own)], cot_ref, sem)
    copy.start()
    size = 256 if own % 256 == 0 else own
    copy.wait()
    for n in range(own // size):
        part = slice(n * size, (n + 1) * size)
        cot_t[:, part] = cot_ref[part].T


def attend_kernel(
    per, me, virt, lens, live, x_ref, xhat_ref, held, got,
    qkv_ref, prob_ref, o_ref, x1_ref, wqkv, wout, vec,
):
    tokens, width = x_ref.shape
    rows = tokens // WIN
    hs = width // HEADS
    here = twist(virt[0] // 4)
    y_own = (virt[0] // 2) % 2
    first = virt[0] % 2 == 0
    total = jnp.zeros((8, width), F32)
    for m in range(CHIPS):
        k = spot(m) ^ (here + y_own * VDP)
        a = held[k].astype(F32)
        b = got[k].astype(F32)
        even = jnp.where(first, a, b)
        odd = jnp.where(first, b, a)
        for part in range(3):
            both = jnp.concatenate([even[part * 8 : part * 8 + 8], odd[part * 8 : part * 8 + 8]], 0)
            wqkv[m * 16 : m * 16 + 16, part * width : (part + 1) * width] = both.astype(BF16)
        both = jnp.concatenate([even[24:32], odd[24:32]], 0)
        wout[m * 16 : m * 16 + 16] = both.astype(BF16)
        total = total + a[32:40] + b[32:40]
    vec[...] = total
    scale = hs**-0.5
    ii = lax.broadcasted_iota(jnp.int32, (WIN, hs), 0)
    jj = lax.broadcasted_iota(jnp.int32, (WIN, hs), 1)
    same = ii == jj
    image_rows = live.shape[1]
    base = lax.rem(me[0], 2) * rows

    def enter(c):
        part = slice(c * per * WIN, (c + 1) * per * WIN)
        h1 = (xhat_ref[part] * total[0:1] + total[2:3]).astype(BF16)
        qkv = dot(h1, wqkv[...], NN).astype(BF16)
        qkv_ref[part] = qkv
        scores = []
        for r in range(per):
            at = slice(r * WIN, (r + 1) * WIN)
            scores.append(dot(qkv[at, :width], apart(qkv[at, width : 2 * width], hs), NT))
        return qkv, scores

    ahead = enter(0)
    for c in range(rows // per):
        qkv, scores = ahead
        if c + 1 < rows // per:
            ahead = enter(c + 1)
        part = slice(c * per * WIN, (c + 1) * per * WIN)
        probs = []
        for r in range(per):
            row = base + c * per + r
            image = row // image_rows
            inside = row - image * image_rows
            reach = jnp.where(live[image, inside] == 1, lens[image] - inside * WIN, 0)
            allowed = same | (jj < jnp.minimum(ii, reach))
            heads = []
            for h in range(HEADS):
                s = jnp.where(allowed, scores[r][:, h * hs : (h + 1) * hs], -1e30)
                e = jnp.exp((s - jnp.max(s, -1, keepdims=True)) * scale)
                heads.append((e * (1.0 / jnp.sum(e, -1, keepdims=True))).astype(BF16))
            probs.append(jnp.concatenate(heads, 1))
        mixed = []
        for r in range(per):
            at = slice(r * WIN, (r + 1) * WIN)
            mixed.append(dot(probs[r], apart(qkv[at, 2 * width :], hs), NN).astype(BF16))
        o = jnp.concatenate(mixed, 0)
        for n, p in enumerate(probs):
            prob_ref[c * per + n] = p
        o_ref[part] = o
        x1_ref[part] = x_ref[part].astype(F32) + dot(o, wout[...], NN)


def join(virt, blocks, n, up, down_t):
    tall = blocks.shape[1] // 2
    width = up.shape[0]
    here = twist(virt[0] // 4)
    for i in range(VDP):
        k = twist(i) ^ here
        at = slice(i * tall, (i + 1) * tall)
        cols = slice(n * width, (n + 1) * width)
        up[at, cols] = blocks[k, :tall]
        down_t[at, cols] = blocks[k, tall:]


def hidden_units(h2, dyb, up, down_t):
    u = dot(h2, up[...], NN).astype(BF16)
    da = dot(dyb, down_t[...], NN).astype(BF16)
    a, slope = gelu_both(u)
    return a, da * slope


def hidden_near_kernel(
    per, virt, x1_ref, cot_ref, cot_t, vec, own, got,
    h2_ref, xhat_ref, inv_ref, f_ref, dh2_ref, keep, send,
    a_ref, du_ref, up, down_t, up_t, down,
):
    tokens, width = x1_ref.shape
    size = per * WIN
    join(virt, own, 0, up, down_t)
    join(virt, got, 1, up, down_t)
    up_t[...] = up[...].T
    down[...] = down_t[...].T
    for c in range(tokens // size):
        part = slice(c * size, (c + 1) * size)
        x1 = x1_ref[part]
        xhat, inv = norm_parts(x1)
        xhat_ref[part] = xhat
        inv_ref[part] = inv
        h2 = (xhat * vec[1:2] + vec[3:4]).astype(BF16)
        h2_ref[part] = h2
        a, du = hidden_units(h2, cot_ref[part], up, down_t)
        a_ref[part] = a
        du_ref[part] = du
        f_ref[part] = x1 + vec[4:5] + dot(a, down[...], NN)
        dh2_ref[part] = dot(du, up_t[...], NN)
    gdown = dot(cot_t[...], a_ref[...], NN)
    gup = dot(h2_ref[...], du_ref[...], TN)
    tall = width // VDP
    here = twist(virt[0] // 4)
    for i in range(VDP):
        at = slice(i * tall, (i + 1) * tall)
        k = twist(i) ^ here
        keep[k, :tall] = gup[at, :width]
        keep[k, tall:] = gdown[at, :width]
        send[k, :tall] = gup[at, width:].astype(BF16)
        send[k, tall:] = gdown[at, width:].astype(BF16)


def hidden_far_kernel(
    per, virt, cot_ref, vec, own, got, h2_ref, xhat_ref, inv_ref, f_ref, dh2_ref, o_ref,
    y_ref, dx1_ref, g_ref, gout, gvec,
    up, down_t, up_t, down,
):
    tokens, width = h2_ref.shape
    size = per * WIN
    join(virt, own, 0, up, down_t)
    join(virt, got, 1, up, down_t)
    up_t[...] = up[...].T
    down[...] = down_t[...].T
    sums = [jnp.zeros((1, width), F32)] * 3
    for c in range(tokens // size):
        part = slice(c * size, (c + 1) * size)
        a, du = hidden_units(h2_ref[part], cot_ref[part], up, down_t)
        y_ref[part] = (f_ref[part] + dot(a, down[...], NN)).astype(BF16)
        dh2 = dh2_ref[part] + dot(du, up_t[...], NN)
        dy = cot_ref[part].astype(F32)
        xhat = xhat_ref[part]
        dx1 = dy + norm_back(dh2, xhat, inv_ref[part], vec[1:2])
        dx1_ref[part] = dx1
        g_ref[part] = dx1.astype(BF16)
        for n, term in enumerate((dh2 * xhat, dh2, dy)):
            sums[n] = sums[n] + jnp.sum(term, 0, keepdims=True)
    gout[...] = dot(o_ref[...], g_ref[...], TN)
    zero = jnp.zeros((1, width), F32)
    gvec[...] = jnp.concatenate([zero, sums[0], zero, sums[1], sums[2], zero, zero, zero], 0)


def own_rows(virt, i, other):
    core = virt[0] % 2
    core = 1 - core if other else core
    return pl.ds(pl.multiple_of(i * 32 + ((virt[0] // 2) % 2) * 16 + core * 8, 8), 8)


def back_kernel(
    per, virt, qkv_ref, prob_ref, g_ref, xhat_t, wqkv, wout, vec, gout, gvec,
    dqkv, keep, send,
    gqkv,
):
    tokens, width = g_ref.shape
    hs = width // HEADS
    scale = hs**-0.5
    every = [(r, h) for r in range(tokens // WIN) for h in range(HEADS)]
    groups = [every[n : n + 2 * per] for n in range(0, len(every), 2 * per)]

    def piece(ref, r, h, part=0):
        return ref[r * WIN : (r + 1) * WIN, part * width + h * hs : part * width + (h + 1) * hs]

    def enter(pairs):
        r = pairs[0][0]
        do = dot(g_ref[r * WIN : (r + per) * WIN], wout[...], NT).astype(BF16)
        dos = [do[(n - r) * WIN : (n - r + 1) * WIN, h * hs : (h + 1) * hs] for n, h in pairs]
        probs = [prob_ref[r, :, h * hs : h * hs + WIN] for r, h in pairs]
        dps = [dot(a, piece(qkv_ref, r, h, 2), NT) for a, (r, h) in zip(dos, pairs)]
        dvs = [dot(p, a, TN).astype(BF16) for p, a in zip(probs, dos)]
        return probs, dps, dvs

    ahead = enter(groups[0])
    for place, pairs in enumerate(groups):
        probs, dps, dvs = ahead
        if place + 1 < len(groups):
            ahead = enter(groups[place + 1])
        dss = []
        for p, dp in zip(probs, dps):
            pf = p.astype(F32)
            ds = pf * (dp - jnp.sum(dp * pf, -1, keepdims=True)) * scale
            dss.append(ds.astype(BF16))
        dqs = [dot(ds, piece(qkv_ref, r, h, 1), NN).astype(BF16) for ds, (r, h) in zip(dss, pairs)]
        dks = [dot(ds, piece(qkv_ref, r, h, 0), TN).astype(BF16) for ds, (r, h) in zip(dss, pairs)]
        for n, (r, h) in enumerate(pairs):
            for part, values in enumerate((dqs, dks, dvs)):
                at = slice(part * width + h * hs, part * width + (h + 1) * hs)
                dqkv[r * WIN : (r + 1) * WIN, at] = values[n]
    grad = dot(xhat_t[...], dqkv[...], NN)
    total = jnp.zeros((1, 3 * width), F32)
    for r in range(tokens // WIN):
        total = total + jnp.sum(dqkv[r * WIN : (r + 1) * WIN].astype(F32), 0, keepdims=True)
    w = wqkv[...].astype(F32)
    cols = jnp.concatenate([
        jnp.broadcast_to(jnp.sum(w * grad, -1, keepdims=True), (width, 64)),
        jnp.broadcast_to(jnp.sum(w * total, -1, keepdims=True), (width, 64)),
    ], 1)
    lines = cols.T
    gain, from_total = lines[0:1], lines[64:65]
    vec_t = vec[...].T
    gqkv[...] = grad * vec_t[:, 0:1] + total * vec_t[:, 2:3]
    rest = gvec[...]
    sums = jnp.concatenate([gain, rest[1:2], from_total, rest[3:]], 0)
    here = twist(virt[0] // 4)
    for i in range(VDP):
        k = twist(i) ^ here
        mine, other = own_rows(virt, i, 0), own_rows(virt, i, 1)
        theirs = []
        for part in range(3):
            at = slice(part * width, (part + 1) * width)
            keep[k, part * 8 : part * 8 + 8] = gqkv[mine, at]
            theirs.append(gqkv[other, at])
        keep[k, 24:32] = gout[mine]
        keep[k, 32:] = sums
        send[k] = jnp.concatenate(theirs + [gout[other], sums], 0).astype(BF16)


def token_grad_kernel(per, me, dqkv, wqkv, vec, xhat_ref, inv_ref, dx1_ref, y, y_near, gx, gxb, out, turned, sems):
    own = dqkv.shape[0]
    size = per * WIN
    copies = []
    for n, source in enumerate((y, y_near)):
        at = pl.ds((lax.rem(me[0], 2) ^ n) * own, own)
        copies.append(pltpu.make_async_copy(source, out.at[at], sems.at[n]))
        copies[-1].start()
    turned[...] = wqkv[...].T
    for c in range(own // size):
        part = slice(c * size, (c + 1) * size)
        dh1 = dot(dqkv[part], turned[...], NN)
        values = dx1_ref[part] + norm_back(dh1, xhat_ref[part], inv_ref[part], vec[0:1])
        gx[part] = values
        gxb[part] = values.astype(BF16)
    for copy in copies:
        copy.wait()


def place_kernel(per, me, mine, theirs, out, wide, sems):
    own = theirs.shape[0]
    size = per * WIN
    here = lax.rem(me[0], 2) * own
    copies = [pltpu.make_async_copy(mine, out.at[pl.ds(here, own)], sems.at[own // size])]
    copies[0].start()
    for c in range(own // size):
        part = pl.ds(c * size, size)
        wide[part] = theirs[part].astype(F32)
        at = pl.ds(own - here + c * size, size)
        copies.append(pltpu.make_async_copy(wide.at[part], out.at[at], sems.at[c]))
        copies[-1].start()
    for copy in copies:
        copy.wait()


def finish_kernel(me, keep_a, keep_b, *refs):
    qkv, out, gains, biases, up, down = refs[6:]
    small, width = out.shape
    tall = up.shape[0]
    total, units = keep_a[0], keep_b[0]
    for got_a, got_b in zip(refs[:3], refs[3:6]):
        total = total + got_a[...].astype(F32)
        units = units + got_b[...].astype(F32)
    for part in range(3):
        qkv[:, part * width : (part + 1) * width] = total[part * small : (part + 1) * small]
    out[...] = total[3 * small : 4 * small]
    vec = pltpu.roll(total[4 * small :], width - me[0] * small, 1)[:, :small]
    gains[...] = vec[:2]
    biases[...] = vec[2:5]
    up[...] = units[:tall]
    down[...] = units[tall:]


def swap(block, axis, bit):
    size = lax.axis_size(axis)
    return lax.ppermute(block, axis, [(i, i ^ bit) for i in range(size)])


def steps_of(axis):
    return [(axis, 1 << k) for k in reversed(range(lax.axis_size(axis).bit_length() - 1))]


def after(value, other):
    return lax.optimization_barrier((value, other))[0]


def halves(held):
    half = held.shape[0] // 2
    return held[:half], held[half:].astype(BF16)


def fold_step(keep, send, axis, bit, past=None):
    got = swap(send, axis, bit)
    return keep + (got if past is None else after(got, past)).astype(F32)


def bit_reverse(index, count):
    out = 0 * index
    for k in range(count):
        out = out | (((index >> k) & 1) << (count - 1 - k))
    return out


def by_device(block, me):
    blocks = block[None]
    for axis, bit in steps_of("dp") + steps_of("tensor"):
        blocks = jnp.concatenate([blocks, swap(blocks, axis, bit)], 0)
    count = blocks.shape[0]
    order = jnp.arange(count, dtype=jnp.int32) ^ me
    return jnp.take(blocks, bit_reverse(order, count.bit_length() - 1), axis=0)


def other_pack(w_qkv, w_out, gains, biases, w_up, w_down, me):
    small, width = w_out.shape
    qkv = w_qkv.reshape(small, 3, width).transpose(1, 0, 2).reshape(3 * small, width)
    rows = jnp.concatenate([gains, biases], 0)
    place = jnp.zeros((8, width), BF16)
    place = lax.dynamic_update_slice(place, rows, (jnp.int32(0), me * small))
    return jnp.concatenate([qkv, w_out, place], 0), jnp.concatenate([w_up, w_down.T], 0)


def other_blocks(a, b, me, n_dp, n_t):
    a = by_device(a, me)
    b = by_device(b, me)
    width = a.shape[2]
    count = n_dp * n_t
    small = width // count
    big = width // (VDP * VT)
    mats = a[:, : 4 * small].reshape(count, 4, small, width).transpose(1, 0, 2, 3)
    mats = mats.reshape(4, VDP * VT, big, width).transpose(1, 0, 2, 3).reshape(VDP * VT, 4 * big, width)
    vec = jnp.sum(a[:, 4 * small :].astype(F32), 0).astype(BF16)
    vecs = jnp.concatenate([vec[None], jnp.zeros((VDP * VT - 1, 8, width), BF16)], 0)
    a = jnp.concatenate([mats, vecs], 1)
    tall = width // n_dp
    b = b.reshape(n_dp, VT, 2, tall, width).transpose(1, 2, 0, 3, 4)
    b = b.reshape(VT, 2, VDP, width // VDP, width).transpose(2, 0, 1, 3, 4)
    b = b.reshape(VDP * VT, 2 * (width // VDP), width)

    y_own = (me // 2) % 2

    def placed(blocks):
        pairs = blocks.reshape((CHIPS, 2) + blocks.shape[1:])
        chips = sorted(range(CHIPS), key=spot)
        pairs = jnp.stack([pairs[m] for m in chips], 0)
        pairs = jnp.where(y_own == 1, jnp.roll(pairs, VDP, 0), pairs)
        return pairs[:, 0], pairs[:, 1]

    return placed(a) + placed(b)


def other_reduce(pair_a, pair_b, me, n_dp, n_t):
    count = n_dp * n_t
    y_own = (me // 2) % 2

    def whole(keep, send):
        pairs = jnp.stack([keep, send.astype(F32)], 1)
        pairs = jnp.stack([pairs[twist(i)] for i in range(VDP)], 0)
        none = jnp.zeros_like(pairs)
        both = jnp.stack([jnp.where(y_own == y, pairs, none) for y in range(2)], 1)
        return both.reshape((VDP * VT,) + keep.shape[1:])

    def rows_of(blocks, parts):
        big = blocks.shape[1] // parts
        mats = blocks.reshape(VDP * VT, parts, big, -1).transpose(1, 0, 2, 3)
        mats = mats.reshape(parts, count, VDP * VT * big // count, -1).transpose(1, 0, 2, 3)
        return mats.reshape(count, -1, blocks.shape[2])

    def vec_of(blocks):
        picked = jnp.where(y_own == 0, blocks[0], 0.0)
        return jnp.broadcast_to(picked[None], (count,) + picked.shape)

    a, b = whole(*pair_a), whole(*pair_b)
    width = a.shape[2]
    tall, high = width // n_dp, width // VDP
    cols = b.reshape(VDP, VT, 2, high, width).transpose(1, 2, 0, 3, 4)
    cols = cols.reshape(VT, 2, n_dp, tall, width).transpose(2, 0, 1, 3, 4)
    cols = cols.reshape(count, 2 * tall, width)
    a = jnp.concatenate([rows_of(a[:, :32], 4), vec_of(a[:, 32:])], 1)
    results = []
    for blocks in (a, cols):
        blocks = jnp.take(blocks, jnp.arange(count, dtype=jnp.int32) ^ me, axis=0)
        for axis, bit in reversed(steps_of("dp") + steps_of("tensor")):
            pairs = blocks.reshape((-1, 2) + blocks.shape[1:])
            got = swap(pairs[:, 1].astype(BF16), axis, bit)
            blocks = pairs[:, 0] + got.astype(F32)
        results.append(blocks[0])
    return results


def struct(shape, dtype):
    return jax.ShapeDtypeStruct(shape, dtype)


def call(kernel, name, args, outs, scratch=(), flops=0, limit=8, hbm_outs=True):
    args = [a if isinstance(a, tuple) else (a, pltpu.VMEM) for a in args]
    moved = sum(a.size * a.dtype.itemsize for a, _ in args)
    spaces = [pl.ANY if hbm_outs and isinstance(o, jax.ShapeDtypeStruct) else pltpu.VMEM for o in outs]
    return pl.pallas_call(
        kernel,
        name=name,
        out_shape=outs,
        in_specs=[pl.BlockSpec(memory_space=space) for _, space in args],
        out_specs=[pl.BlockSpec(memory_space=space) for space in spaces],
        scratch_shapes=list(scratch),
        compiler_params=pltpu.CompilerParams(vmem_limit_bytes=limit * MIB),
        cost_estimate=pl.CostEstimate(flops=flops, bytes_accessed=moved, transcendentals=0),
    )(*[a for a, _ in args])


def on_device(tokens, lengths, row_mask, cotangent, w_qkv, w_out, gains, biases, w_up, w_down):
    images, seq_len, width = tokens.shape
    n_dp, n_t = lax.axis_size("dp"), lax.axis_size("tensor")
    index = lax.axis_index("dp") * n_t + lax.axis_index("tensor")
    me = index.astype(jnp.int32).reshape(1)
    usual = (n_dp, n_t) == (VDP, VT)
    virt = me if usual else (index // 2 % 2 * 2).astype(jnp.int32).reshape(1)
    small = width // (n_dp * n_t)
    tall = width // n_dp
    own = images * seq_len // 2
    rows = own // WIN
    per = rows
    some = 8 if rows % 8 == 0 else 1
    less = 4 if rows % 4 == 0 else 1
    smem = pltpu.SMEM
    weights = (w_qkv, w_out, gains, biases, w_up, w_down)
    token_mm = 2 * own * width
    hbm = pltpu.HBM

    def in_hbm(array):
        return (pltpu.with_memory_space_constraint(array, hbm), hbm)

    def fetch(me):
        return call(
            fetch_kernel,
            "fetch",
            [(me, smem), in_hbm(tokens.reshape(images * seq_len, width))],
            [
                pltpu.VMEM((own, width), BF16),
                pltpu.VMEM((own, width), F32),
                pltpu.VMEM((own, 1), F32),
                pltpu.VMEM((width, own), BF16),
            ],
            [pltpu.SemaphoreType.DMA(())],
            limit=4,
        )

    def fetch_turned(me):
        return call(
            turn_kernel,
            "turn",
            [(me, smem), in_hbm(cotangent.reshape(images * seq_len, width))],
            [pltpu.VMEM((own, width), BF16), pltpu.VMEM((width, own), BF16)],
            [pltpu.SemaphoreType.DMA(())],
            limit=4,
        )

    if usual:
        weights = (w_qkv, w_out, gains, biases, w_up, w_down.T)
        high = 4 * small + 8
        packed = call(
            pack_kernel,
            "pack",
            [(me, smem)] + [in_hbm(w) for w in weights],
            [pltpu.VMEM((1, high + 2 * tall, width), BF16)],
            [pltpu.VMEM(w.shape, BF16) for w in weights] + [pltpu.SemaphoreType.DMA((6,))],
        )[0]
        planes = [packed] + [swap(packed, "dp", bit) for bit in (2, 4, 6)]
        cot, cot_t = fetch_turned(after(me, packed))
        planes[3] = after(planes[3], cot)
        held_a = jnp.concatenate([plane[:, :high] for plane in planes], 0)
        b = jnp.concatenate([plane[:, high:] for plane in planes], 0)
        far_b = swap(b, "tensor", 2)
        held_a = jnp.concatenate([held_a, swap(held_a, "dp", 1)], 0)
        b = jnp.concatenate([b, swap(b, "dp", 1)], 0)
        x, xhat1, inv1, xhat_t = fetch(after(me, (held_a, far_b)))
        held_a = jnp.concatenate([held_a, after(swap(held_a, "tensor", 2), (b, xhat1))], 0)
        far_x = swap(far_b, "dp", 1)
        got_a = swap(held_a, "tensor", 1)
        got_b = swap(b, "tensor", 1)
    else:
        held_a, got_a, held_b, got_b = other_blocks(*other_pack(*weights, index), index, n_dp, n_t)
        b, far_b = held_b[:VDP], held_b[VDP:]
        got_b, got_far = got_b[:VDP], got_b[VDP:]
        x, xhat1, inv1, xhat_t = fetch(me)
        cot, cot_t = fetch_turned(me)
    qkv, prob, o, x1, wqkv, wout, vec = call(
        functools.partial(attend_kernel, some),
        "attend",
        [(me, smem), (virt, smem), (lengths, smem), (row_mask, smem), x, xhat1, held_a, got_a],
        [
            pltpu.VMEM((own, 3 * width), BF16),
            pltpu.VMEM((rows, WIN, width), BF16),
            pltpu.VMEM((own, width), BF16),
            pltpu.VMEM((own, width), F32),
            pltpu.VMEM((width, 3 * width), BF16),
            pltpu.VMEM((width, width), BF16),
            pltpu.VMEM((8, width), F32),
        ],
        flops=token_mm * (4 * width + 2 * WIN),
    )
    tall_b = 2 * (width // VDP)
    mats = [pltpu.VMEM((width, 2 * width), BF16)] * 2 + [pltpu.VMEM((2 * width, width), BF16)] * 2
    if usual:
        far_b = jnp.concatenate([far_b, after(far_x, x1)], 0)
        got_far = swap(far_b, "tensor", 1)
        got_b = after(got_b, far_b)
    wide_per = 6 if rows % 6 == 0 else 1
    *first, keep_b, send_b = call(
        functools.partial(hidden_near_kernel, wide_per),
        "hidden_near",
        [(virt, smem), x1, cot, cot_t, vec, b, got_b],
        [
            pltpu.VMEM((own, width), BF16),
            pltpu.VMEM((own, width), F32),
            pltpu.VMEM((own, 1), F32),
            pltpu.VMEM((own, width), F32),
            pltpu.VMEM((own, width), F32),
            pltpu.VMEM((VDP, tall_b, width), F32),
            pltpu.VMEM((VDP, tall_b, width), BF16),
        ],
        [pltpu.VMEM((own, 2 * width), BF16)] * 2 + mats,
        token_mm * 12 * width,
        12,
    )
    y, dx1, g, gout, gvec = call(
        functools.partial(hidden_far_kernel, wide_per),
        "hidden_far",
        [(virt, smem), cot, vec, far_b, got_far, *first, o],
        [
            pltpu.VMEM((own, width), BF16),
            pltpu.VMEM((own, width), F32),
            pltpu.VMEM((own, width), BF16),
            pltpu.VMEM((width, width), F32),
            pltpu.VMEM((8, width), F32),
        ],
        mats,
        token_mm * 9 * width,
    )
    core, xbit = ("tensor", 1), ("dp", 1)
    if usual:
        held_b = fold_step(keep_b, send_b, *core, g)
        y = after(y, held_b)
    y_near = swap(y, "tensor", 1)
    dqkv, keep_a, send_a = call(
        functools.partial(back_kernel, per),
        "back",
        [(virt, smem), qkv, prob, g, xhat_t, wqkv, wout, vec, gout, gvec],
        [
            pltpu.VMEM((own, 3 * width), BF16),
            pltpu.VMEM((VDP, 40, width), F32),
            pltpu.VMEM((VDP, 40, width), BF16),
        ],
        [pltpu.VMEM((width, 3 * width), F32)],
        token_mm * (4 * width + 5 * WIN),
    )
    if usual:
        held_b = fold_step(*halves(held_b), *xbit)
        vec = after(vec, held_b)
    gx, gxb, layer_out = call(
        functools.partial(token_grad_kernel, less),
        "token_grad",
        [(me, smem), dqkv, wqkv, vec, xhat1, inv1, dx1, y, y_near],
        [
            pltpu.VMEM((own, width), F32),
            pltpu.VMEM((own, width), BF16),
            struct((images * seq_len, width), BF16),
        ],
        [pltpu.VMEM((3 * width, width), BF16), pltpu.SemaphoreType.DMA((2,))],
        flops=token_mm * 3 * width,
    )
    layer_out = layer_out.reshape(images, seq_len, width)

    def place(gx_near):
        return call(
            functools.partial(place_kernel, less),
            "place",
            [(me, smem), gx, gx_near],
            [struct((images * seq_len, width), F32)],
            [pltpu.VMEM((own, width), F32), pltpu.SemaphoreType.DMA((rows // less + 1,))],
        )[0].reshape(images, seq_len, width)

    if usual:
        held_a = fold_step(keep_a, send_a, *core, gxb)
        gx_near = swap(after(gxb, held_a), "tensor", 1)
        low_b = after(held_b.astype(BF16), held_a)
        got_b = [swap(low_b[n], "dp", 2 * n) for n in range(1, 4)]
        held_a = fold_step(*halves(held_a), *xbit)
        low_a = held_a.astype(BF16)
        got_a = [swap(low_a[n], "dp", 2 * n) for n in range(1, 4)]
        grad_tokens = place(after(gx_near, got_b))
        got_a[2] = after(got_a[2], grad_tokens)
        shapes = ((small, 3 * width), (small, width), (2, small), (3, small), (tall, width), (tall, width))
        o_qkv, o_out, o_gains, o_bias, o_up, o_down = call(
            finish_kernel,
            "finish",
            [(me, smem), held_a, held_b, *got_a, *got_b],
            [struct(shape, F32) for shape in shapes],
            limit=2,
            hbm_outs=False,
        )
    else:
        grad_tokens = place(swap(gxb, "tensor", 1))
        grad_a, grad_b = other_reduce((keep_a, send_a), (keep_b, send_b), index, n_dp, n_t)
        o_qkv = jnp.concatenate([grad_a[p * small : (p + 1) * small] for p in range(3)], 1)
        o_out = grad_a[3 * small : 4 * small]
        o_vec = lax.dynamic_slice_in_dim(grad_a[4 * small : 4 * small + 5], index * small, small, 1)
        o_gains, o_bias = o_vec[:2], o_vec[2:]
        o_up, o_down = grad_b[:tall], grad_b[tall:]
    return layer_out, grad_tokens, o_qkv, o_out, o_gains, o_bias, o_up, o_down.T


def solution(mesh):
    in_specs = (
        P("dp", None, None),
        P("dp"),
        P("dp", None),
        P("dp", None, None),
        P(("dp", "tensor"), None),
        P(("dp", "tensor"), None),
        P(None, ("dp", "tensor")),
        P(None, ("dp", "tensor")),
        P("dp", "tensor"),
        P("tensor", "dp"),
    )
    out_specs = (
        P("dp", None, None),
        P("dp", None, None),
        P(("dp", "tensor"), None),
        P(("dp", "tensor"), None),
        P(None, ("dp", "tensor")),
        P(None, ("dp", "tensor")),
        P("dp", "tensor"),
        P("tensor", "dp"),
    )
    return jax.shard_map(
        on_device, mesh=mesh, in_specs=in_specs, out_specs=out_specs, check_vma=False
    )
```

```python
import functools

import jax
import jax.numpy as jnp
from jax import lax
from jax.experimental import pallas as pl
from jax.experimental.pallas import tpu as pltpu
from jax.sharding import PartitionSpec as P

HEADS = 2
WIN = 96
F32 = jnp.float32
BF16 = jnp.bfloat16
VDP, VT = 8, 4
CHIPS = VDP * VT // 2
MIB = 1 << 20

NN = ((1,), (0,))
NT = ((1,), (1,))
TN = ((0,), (0,))


def dot(a, b, dims):
    return lax.dot_general(a, b, (dims, ((), ())), preferred_element_type=F32)


def twist(i):
    return (i & 1) * 4 + (i >> 1)


def spot(m):
    return (m % 2) * VDP + twist(m // 2)


def norm_parts(values):
    center = values - jnp.mean(values, -1, keepdims=True)
    inv = lax.rsqrt(jnp.mean(center * center, -1, keepdims=True) + 1e-05)
    return center * inv, inv


def norm_back(grad, xhat, inv, gain):
    scaled = grad * gain
    return inv * (
        scaled
        - jnp.mean(scaled, -1, keepdims=True)
        - xhat * jnp.mean(scaled * xhat, -1, keepdims=True)
    )


def gelu_both(u):
    c = 0.7978845608028654
    u2 = u * u
    t = jnp.tanh(u * (c + (c * 0.044715) * u2))
    half = 0.5 + 0.5 * t
    value = u * half
    slope = half + (value - value * half) * (2 * c + (6 * c * 0.044715) * u2)
    return value, slope


def apart(both, hs):
    blocks = []
    for h in range(HEADS):
        parts = [jnp.zeros((WIN, hs), BF16)] * HEADS
        parts[h] = both[:, h * hs : (h + 1) * hs]
        blocks.append(jnp.concatenate(parts, 1))
        blocks.append(jnp.zeros((hs - WIN, HEADS * hs), BF16))
    return jnp.concatenate(blocks, 0)


def pack_kernel(me, *refs):
    sources, packed, held, sems = refs[:6], refs[6], refs[7:13], refs[13]
    copies = [pltpu.make_async_copy(a, b, sems.at[n]) for n, (a, b) in enumerate(zip(sources, held))]
    for copy in copies:
        copy.start()
    qkv, out, gains, biases, up, down = held
    small, width = out.shape
    tall = up.shape[0]
    lane = lax.broadcasted_iota(jnp.int32, (1, width), 1)
    mine = lane // small == me[0]
    for copy in copies:
        copy.wait()
    for part in range(3):
        packed[0, part * small : (part + 1) * small] = qkv[:, part * width : (part + 1) * width]
    packed[0, 3 * small : 4 * small] = out[...]
    rows = [gains[0:1], gains[1:2], biases[0:1], biases[1:2], biases[2:3]]
    vals = jnp.concatenate(rows + [jnp.zeros((3, small), BF16)], 0).astype(F32)
    wide = jnp.concatenate([vals] * (width // small), 1)
    at = 4 * small + 8
    packed[0, 4 * small : at] = jnp.where(mine, wide, 0.0).astype(BF16)
    packed[0, at : at + tall] = up[...]
    packed[0, at + tall :] = down[...]


def fetch_kernel(me, tokens, x_ref, xhat_ref, inv_ref, xhat_t, sem):
    own, width = x_ref.shape
    copy = pltpu.make_async_copy(tokens.at[pl.ds(lax.rem(me[0], 2) * own, own)], x_ref, sem)
    copy.start()
    ones = jnp.full((width, width), 1.0 / width, BF16)
    size = 256 if own % 256 == 0 else own
    copy.wait()
    for n in range(own // size):
        part = slice(n * size, (n + 1) * size)
        x = x_ref[part]
        center = x.astype(F32) - dot(x, ones, NN)
        inv = lax.rsqrt(dot((center * center).astype(BF16), ones, NN) + 1e-05)
        xhat = center * inv
        xhat_ref[part] = xhat
        inv_ref[part] = inv[:, :1]
        xhat_t[:, part] = xhat.astype(BF16).T


def turn_kernel(me, cot, cot_ref, cot_t, sem):
    own = cot_ref.shape[0]
    copy = pltpu.make_async_copy(cot.at[pl.ds(lax.rem(me[0], 2) * own, own)], cot_ref, sem)
    copy.start()
    size = 256 if own % 256 == 0 else own
    copy.wait()
    for n in range(own // size):
        part = slice(n * size, (n + 1) * size)
        cot_t[:, part] = cot_ref[part].T


def attend_kernel(
    per, me, virt, lens, live, x_ref, xhat_ref, held, got,
    qkv_ref, prob_ref, o_ref, x1_ref, wqkv, wout, vec,
):
    tokens, width = x_ref.shape
    rows = tokens // WIN
    hs = width // HEADS
    here = twist(virt[0] // 4)
    y_own = (virt[0] // 2) % 2
    first = virt[0] % 2 == 0
    for m in range(CHIPS):
        k = spot(m) ^ (here + y_own * VDP)
        at = pl.ds(pl.multiple_of(k * 32, 32), 32)
        a = held[at].astype(F32)
        b = got[at].astype(F32)
        even = jnp.where(first, a, b)
        odd = jnp.where(first, b, a)
        for part in range(3):
            both = jnp.concatenate([even[part * 8 : part * 8 + 8], odd[part * 8 : part * 8 + 8]], 0)
            wqkv[m * 16 : m * 16 + 16, part * width : (part + 1) * width] = both.astype(BF16)
        both = jnp.concatenate([even[24:32], odd[24:32]], 0)
        wout[m * 16 : m * 16 + 16] = both.astype(BF16)
    total = held[CHIPS * 32 :].astype(F32) + got[CHIPS * 32 :].astype(F32)
    vec[...] = total
    scale = hs**-0.5
    ii = lax.broadcasted_iota(jnp.int32, (WIN, hs), 0)
    jj = lax.broadcasted_iota(jnp.int32, (WIN, hs), 1)
    same = ii == jj
    image_rows = live.shape[1]
    base = lax.rem(me[0], 2) * rows

    def enter(c):
        part = slice(c * per * WIN, (c + 1) * per * WIN)
        h1 = (xhat_ref[part] * total[0:1] + total[2:3]).astype(BF16)
        qkv = dot(h1, wqkv[...], NN).astype(BF16)
        qkv_ref[part] = qkv
        scores = []
        for r in range(per):
            at = slice(r * WIN, (r + 1) * WIN)
            scores.append(dot(qkv[at, :width], apart(qkv[at, width : 2 * width], hs), NT))
        return qkv, scores

    ahead = enter(0)
    for c in range(rows // per):
        qkv, scores = ahead
        if c + 1 < rows // per:
            ahead = enter(c + 1)
        part = slice(c * per * WIN, (c + 1) * per * WIN)
        probs = []
        for r in range(per):
            row = base + c * per + r
            image = row // image_rows
            inside = row - image * image_rows
            reach = jnp.where(live[image, inside] == 1, lens[image] - inside * WIN, 0)
            allowed = same | (jj < jnp.minimum(ii, reach))
            heads = []
            for h in range(HEADS):
                s = jnp.where(allowed, scores[r][:, h * hs : (h + 1) * hs], -1e30)
                e = jnp.exp((s - jnp.max(s, -1, keepdims=True)) * scale)
                heads.append((e * (1.0 / jnp.sum(e, -1, keepdims=True))).astype(BF16))
            probs.append(jnp.concatenate(heads, 1))
        mixed = []
        for r in range(per):
            at = slice(r * WIN, (r + 1) * WIN)
            mixed.append(dot(probs[r], apart(qkv[at, 2 * width :], hs), NN).astype(BF16))
        o = jnp.concatenate(mixed, 0)
        for n, p in enumerate(probs):
            prob_ref[c * per + n] = p
        o_ref[part] = o
        x1_ref[part] = x_ref[part].astype(F32) + dot(o, wout[...], NN)


def join(virt, blocks, n, up, down_t):
    tall = blocks.shape[1] // 2
    width = up.shape[0]
    here = twist(virt[0] // 4)
    for i in range(VDP):
        k = twist(i) ^ here
        at = slice(i * tall, (i + 1) * tall)
        cols = slice(n * width, (n + 1) * width)
        up[at, cols] = blocks[k, :tall]
        down_t[at, cols] = blocks[k, tall:]


def hidden_units(h2, dyb, up, down_t):
    u = dot(h2, up[...], NN).astype(BF16)
    da = dot(dyb, down_t[...], NN).astype(BF16)
    a, slope = gelu_both(u)
    return a, da * slope


def hidden_near_kernel(
    per, virt, x1_ref, cot_ref, cot_t, vec, own, got,
    h2_ref, xhat_ref, inv_ref, f_ref, dh2_ref, keep, send,
    a_ref, du_ref, up, down_t, up_t, down,
):
    tokens, width = x1_ref.shape
    size = per * WIN
    join(virt, own, 0, up, down_t)
    join(virt, got, 1, up, down_t)
    up_t[...] = up[...].T
    down[...] = down_t[...].T
    for c in range(tokens // size):
        part = slice(c * size, (c + 1) * size)
        x1 = x1_ref[part]
        xhat, inv = norm_parts(x1)
        xhat_ref[part] = xhat
        inv_ref[part] = inv
        h2 = (xhat * vec[1:2] + vec[3:4]).astype(BF16)
        h2_ref[part] = h2
        a, du = hidden_units(h2, cot_ref[part], up, down_t)
        a_ref[part] = a
        du_ref[part] = du
        f_ref[part] = x1 + vec[4:5] + dot(a, down[...], NN)
        dh2_ref[part] = dot(du, up_t[...], NN)
    gdown = dot(cot_t[...], a_ref[...], NN)
    gup = dot(h2_ref[...], du_ref[...], TN)
    tall = width // VDP
    here = twist(virt[0] // 4)
    for i in range(VDP):
        at = slice(i * tall, (i + 1) * tall)
        k = twist(i) ^ here
        keep[k, :tall] = gup[at, :width]
        keep[k, tall:] = gdown[at, :width]
        send[k, :tall] = gup[at, width:].astype(BF16)
        send[k, tall:] = gdown[at, width:].astype(BF16)


def hidden_far_kernel(
    per, virt, cot_ref, vec, own, got, h2_ref, xhat_ref, inv_ref, f_ref, dh2_ref, o_ref,
    y_ref, dx1_ref, g_ref, gout, gvec,
    up, down_t, up_t, down,
):
    tokens, width = h2_ref.shape
    size = per * WIN
    join(virt, own, 0, up, down_t)
    join(virt, got, 1, up, down_t)
    up_t[...] = up[...].T
    down[...] = down_t[...].T
    sums = [jnp.zeros((1, width), F32)] * 3
    for c in range(tokens // size):
        part = slice(c * size, (c + 1) * size)
        a, du = hidden_units(h2_ref[part], cot_ref[part], up, down_t)
        y_ref[part] = (f_ref[part] + dot(a, down[...], NN)).astype(BF16)
        dh2 = dh2_ref[part] + dot(du, up_t[...], NN)
        dy = cot_ref[part].astype(F32)
        xhat = xhat_ref[part]
        dx1 = dy + norm_back(dh2, xhat, inv_ref[part], vec[1:2])
        dx1_ref[part] = dx1
        g_ref[part] = dx1.astype(BF16)
        for n, term in enumerate((dh2 * xhat, dh2, dy)):
            sums[n] = sums[n] + jnp.sum(term, 0, keepdims=True)
    gout[...] = dot(o_ref[...], g_ref[...], TN)
    zero = jnp.zeros((1, width), F32)
    gvec[...] = jnp.concatenate([zero, sums[0], zero, sums[1], sums[2], zero, zero, zero], 0)


def own_rows(virt, i, other):
    core = virt[0] % 2
    core = 1 - core if other else core
    return pl.ds(pl.multiple_of(i * 32 + ((virt[0] // 2) % 2) * 16 + core * 8, 8), 8)


def back_kernel(
    per, virt, qkv_ref, prob_ref, g_ref, xhat_t, wqkv, wout, vec, gout, gvec,
    dqkv, keep, send, vec_sums,
    gqkv,
):
    tokens, width = g_ref.shape
    hs = width // HEADS
    scale = hs**-0.5
    every = [(r, h) for r in range(tokens // WIN) for h in range(HEADS)]
    groups = [every[n : n + 2 * per] for n in range(0, len(every), 2 * per)]

    def piece(ref, r, h, part=0):
        return ref[r * WIN : (r + 1) * WIN, part * width + h * hs : part * width + (h + 1) * hs]

    def enter(pairs):
        r = pairs[0][0]
        do = dot(g_ref[r * WIN : (r + per) * WIN], wout[...], NT).astype(BF16)
        dos = [do[(n - r) * WIN : (n - r + 1) * WIN, h * hs : (h + 1) * hs] for n, h in pairs]
        probs = [prob_ref[r, :, h * hs : h * hs + WIN] for r, h in pairs]
        dps = [dot(a, piece(qkv_ref, r, h, 2), NT) for a, (r, h) in zip(dos, pairs)]
        dvs = [dot(p, a, TN).astype(BF16) for p, a in zip(probs, dos)]
        return probs, dps, dvs

    ahead = enter(groups[0])
    for place, pairs in enumerate(groups):
        probs, dps, dvs = ahead
        if place + 1 < len(groups):
            ahead = enter(groups[place + 1])
        dss = []
        for p, dp in zip(probs, dps):
            pf = p.astype(F32)
            ds = pf * (dp - jnp.sum(dp * pf, -1, keepdims=True)) * scale
            dss.append(ds.astype(BF16))
        dqs = [dot(ds, piece(qkv_ref, r, h, 1), NN).astype(BF16) for ds, (r, h) in zip(dss, pairs)]
        dks = [dot(ds, piece(qkv_ref, r, h, 0), TN).astype(BF16) for ds, (r, h) in zip(dss, pairs)]
        for n, (r, h) in enumerate(pairs):
            for part, values in enumerate((dqs, dks, dvs)):
                at = slice(part * width + h * hs, part * width + (h + 1) * hs)
                dqkv[r * WIN : (r + 1) * WIN, at] = values[n]
    grad = dot(xhat_t[...], dqkv[...], NN)
    total = jnp.zeros((1, 3 * width), F32)
    for r in range(tokens // WIN):
        total = total + jnp.sum(dqkv[r * WIN : (r + 1) * WIN].astype(F32), 0, keepdims=True)
    w = wqkv[...].astype(F32)
    cols = jnp.concatenate([
        jnp.broadcast_to(jnp.sum(w * grad, -1, keepdims=True), (width, 64)),
        jnp.broadcast_to(jnp.sum(w * total, -1, keepdims=True), (width, 64)),
    ], 1)
    lines = cols.T
    gain, from_total = lines[0:1], lines[64:65]
    vec_t = vec[...].T
    gqkv[...] = grad * vec_t[:, 0:1] + total * vec_t[:, 2:3]
    rest = gvec[...]
    sums = jnp.concatenate([gain, rest[1:2], from_total, rest[3:]], 0)
    here = twist(virt[0] // 4)
    for i in range(VDP):
        k = twist(i) ^ here
        mine, other = own_rows(virt, i, 0), own_rows(virt, i, 1)
        theirs = []
        for part in range(3):
            at = slice(part * width, (part + 1) * width)
            keep[k, part * 8 : part * 8 + 8] = gqkv[mine, at]
            theirs.append(gqkv[other, at])
        keep[k, 24:] = gout[mine]
        at = pl.ds(pl.multiple_of(k * 32, 32), 32)
        send[at] = jnp.concatenate(theirs + [gout[other]], 0).astype(BF16)
    vec_sums[...] = sums
    send[VDP * 32 :] = sums.astype(BF16)


def token_grad_kernel(per, me, dqkv, wqkv, vec, xhat_ref, inv_ref, dx1_ref, y, y_near, gx, gxb, out, turned, sems):
    own = dqkv.shape[0]
    size = per * WIN
    copies = []
    for n, source in enumerate((y, y_near)):
        at = pl.ds((lax.rem(me[0], 2) ^ n) * own, own)
        copies.append(pltpu.make_async_copy(source, out.at[at], sems.at[n]))
        copies[-1].start()
    turned[...] = wqkv[...].T
    for c in range(own // size):
        part = slice(c * size, (c + 1) * size)
        dh1 = dot(dqkv[part], turned[...], NN)
        values = dx1_ref[part] + norm_back(dh1, xhat_ref[part], inv_ref[part], vec[0:1])
        gx[part] = values
        gxb[part] = values.astype(BF16)
    for copy in copies:
        copy.wait()


def place_kernel(per, me, mine, theirs, out, wide, sems):
    own = theirs.shape[0]
    size = per * WIN
    here = lax.rem(me[0], 2) * own
    copies = [pltpu.make_async_copy(mine, out.at[pl.ds(here, own)], sems.at[own // size])]
    copies[0].start()
    for c in range(own // size):
        part = pl.ds(c * size, size)
        wide[part] = theirs[part].astype(F32)
        at = pl.ds(own - here + c * size, size)
        copies.append(pltpu.make_async_copy(wide.at[part], out.at[at], sems.at[c]))
        copies[-1].start()
    for copy in copies:
        copy.wait()


def finish_kernel(me, keep_a, keep_b, sums, *refs):
    qkv, out, gains, biases, up, down = refs[6:]
    small, width = out.shape
    tall = up.shape[0]
    total, units, vec = keep_a[0], keep_b[0], sums[...]
    for got_a, got_b in zip(refs[:3], refs[3:6]):
        total = total + got_a[: 4 * small].astype(F32)
        vec = vec + got_a[4 * small :].astype(F32)
        units = units + got_b[...].astype(F32)
    for part in range(3):
        qkv[:, part * width : (part + 1) * width] = total[part * small : (part + 1) * small]
    out[...] = total[3 * small :]
    vec = pltpu.roll(vec, width - me[0] * small, 1)[:, :small]
    gains[...] = vec[:2]
    biases[...] = vec[2:5]
    up[...] = units[:tall]
    down[...] = units[tall:]


def swap(block, axis, bit):
    size = lax.axis_size(axis)
    return lax.ppermute(block, axis, [(i, i ^ bit) for i in range(size)])


def steps_of(axis):
    return [(axis, 1 << k) for k in reversed(range(lax.axis_size(axis).bit_length() - 1))]


def after(value, other):
    return lax.optimization_barrier((value, other))[0]


def merge(pieces):
    vec = sum(piece[-8:] for piece in pieces)
    return jnp.concatenate([piece[:-8] for piece in pieces] + [vec], 0)


def halves(held):
    half = held.shape[0] // 2
    return held[:half], held[half:].astype(BF16)


def fold_step(keep, send, axis, bit, past=None):
    got = swap(send, axis, bit)
    return keep + (got if past is None else after(got, past)).astype(F32)


def bit_reverse(index, count):
    out = 0 * index
    for k in range(count):
        out = out | (((index >> k) & 1) << (count - 1 - k))
    return out


def by_device(block, me):
    blocks = block[None]
    for axis, bit in steps_of("dp") + steps_of("tensor"):
        blocks = jnp.concatenate([blocks, swap(blocks, axis, bit)], 0)
    count = blocks.shape[0]
    order = jnp.arange(count, dtype=jnp.int32) ^ me
    return jnp.take(blocks, bit_reverse(order, count.bit_length() - 1), axis=0)


def other_pack(w_qkv, w_out, gains, biases, w_up, w_down, me):
    small, width = w_out.shape
    qkv = w_qkv.reshape(small, 3, width).transpose(1, 0, 2).reshape(3 * small, width)
    rows = jnp.concatenate([gains, biases], 0)
    place = jnp.zeros((8, width), BF16)
    place = lax.dynamic_update_slice(place, rows, (jnp.int32(0), me * small))
    return jnp.concatenate([qkv, w_out, place], 0), jnp.concatenate([w_up, w_down.T], 0)


def other_blocks(a, b, me, n_dp, n_t):
    a = by_device(a, me)
    b = by_device(b, me)
    width = a.shape[2]
    count = n_dp * n_t
    small = width // count
    big = width // (VDP * VT)
    mats = a[:, : 4 * small].reshape(count, 4, small, width).transpose(1, 0, 2, 3)
    mats = mats.reshape(4, VDP * VT, big, width).transpose(1, 0, 2, 3).reshape(VDP * VT, 4 * big, width)
    vec = jnp.sum(a[:, 4 * small :].astype(F32), 0).astype(BF16)
    a = mats
    tall = width // n_dp
    b = b.reshape(n_dp, VT, 2, tall, width).transpose(1, 2, 0, 3, 4)
    b = b.reshape(VT, 2, VDP, width // VDP, width).transpose(2, 0, 1, 3, 4)
    b = b.reshape(VDP * VT, 2 * (width // VDP), width)

    y_own = (me // 2) % 2

    def placed(blocks):
        pairs = blocks.reshape((CHIPS, 2) + blocks.shape[1:])
        chips = sorted(range(CHIPS), key=spot)
        pairs = jnp.stack([pairs[m] for m in chips], 0)
        pairs = jnp.where(y_own == 1, jnp.roll(pairs, VDP, 0), pairs)
        return pairs[:, 0], pairs[:, 1]

    held_a, got_a = (part.reshape(-1, width) for part in placed(a))
    held_a = jnp.concatenate([held_a, vec], 0)
    got_a = jnp.concatenate([got_a, jnp.zeros_like(vec)], 0)
    return (held_a, got_a) + placed(b)


def other_reduce(pair_a, pair_b, sums, me, n_dp, n_t):
    count = n_dp * n_t
    y_own = (me // 2) % 2

    def whole(keep, send):
        pairs = jnp.stack([keep, send.astype(F32)], 1)
        pairs = jnp.stack([pairs[twist(i)] for i in range(VDP)], 0)
        none = jnp.zeros_like(pairs)
        both = jnp.stack([jnp.where(y_own == y, pairs, none) for y in range(2)], 1)
        return both.reshape((VDP * VT,) + keep.shape[1:])

    def rows_of(blocks, parts):
        big = blocks.shape[1] // parts
        mats = blocks.reshape(VDP * VT, parts, big, -1).transpose(1, 0, 2, 3)
        mats = mats.reshape(parts, count, VDP * VT * big // count, -1).transpose(1, 0, 2, 3)
        return mats.reshape(count, -1, blocks.shape[2])

    a, b = whole(*pair_a), whole(*pair_b)
    width = a.shape[2]
    tall, high = width // n_dp, width // VDP
    cols = b.reshape(VDP, VT, 2, high, width).transpose(1, 2, 0, 3, 4)
    cols = cols.reshape(VT, 2, n_dp, tall, width).transpose(2, 0, 1, 3, 4)
    cols = cols.reshape(count, 2 * tall, width)
    vec = jnp.broadcast_to(jnp.where(y_own == 0, sums, 0.0)[None], (count,) + sums.shape)
    a = jnp.concatenate([rows_of(a, 4), vec], 1)
    results = []
    for blocks in (a, cols):
        blocks = jnp.take(blocks, jnp.arange(count, dtype=jnp.int32) ^ me, axis=0)
        for axis, bit in reversed(steps_of("dp") + steps_of("tensor")):
            pairs = blocks.reshape((-1, 2) + blocks.shape[1:])
            got = swap(pairs[:, 1].astype(BF16), axis, bit)
            blocks = pairs[:, 0] + got.astype(F32)
        results.append(blocks[0])
    return results


def struct(shape, dtype):
    return jax.ShapeDtypeStruct(shape, dtype)


def call(kernel, name, args, outs, scratch=(), flops=0, limit=8, hbm_outs=True):
    args = [a if isinstance(a, tuple) else (a, pltpu.VMEM) for a in args]
    moved = sum(a.size * a.dtype.itemsize for a, _ in args)
    spaces = [pl.ANY if hbm_outs and isinstance(o, jax.ShapeDtypeStruct) else pltpu.VMEM for o in outs]
    return pl.pallas_call(
        kernel,
        name=name,
        out_shape=outs,
        in_specs=[pl.BlockSpec(memory_space=space) for _, space in args],
        out_specs=[pl.BlockSpec(memory_space=space) for space in spaces],
        scratch_shapes=list(scratch),
        compiler_params=pltpu.CompilerParams(vmem_limit_bytes=limit * MIB),
        cost_estimate=pl.CostEstimate(flops=flops, bytes_accessed=moved, transcendentals=0),
    )(*[a for a, _ in args])


def on_device(tokens, lengths, row_mask, cotangent, w_qkv, w_out, gains, biases, w_up, w_down):
    images, seq_len, width = tokens.shape
    n_dp, n_t = lax.axis_size("dp"), lax.axis_size("tensor")
    index = lax.axis_index("dp") * n_t + lax.axis_index("tensor")
    me = index.astype(jnp.int32).reshape(1)
    usual = (n_dp, n_t) == (VDP, VT)
    virt = me if usual else (index // 2 % 2 * 2).astype(jnp.int32).reshape(1)
    small = width // (n_dp * n_t)
    tall = width // n_dp
    own = images * seq_len // 2
    rows = own // WIN
    per = 12 if rows % 12 == 0 else 1
    some = 6 if rows % 6 == 0 else 1
    less = 4 if rows % 4 == 0 else 1
    smem = pltpu.SMEM
    weights = (w_qkv, w_out, gains, biases, w_up, w_down)
    token_mm = 2 * own * width
    hbm = pltpu.HBM

    def in_hbm(array):
        return (pltpu.with_memory_space_constraint(array, hbm), hbm)

    def fetch(me):
        return call(
            fetch_kernel,
            "fetch",
            [(me, smem), in_hbm(tokens.reshape(images * seq_len, width))],
            [
                pltpu.VMEM((own, width), BF16),
                pltpu.VMEM((own, width), F32),
                pltpu.VMEM((own, 1), F32),
                pltpu.VMEM((width, own), BF16),
            ],
            [pltpu.SemaphoreType.DMA(())],
            limit=4,
        )

    def fetch_turned(me):
        return call(
            turn_kernel,
            "turn",
            [(me, smem), in_hbm(cotangent.reshape(images * seq_len, width))],
            [pltpu.VMEM((own, width), BF16), pltpu.VMEM((width, own), BF16)],
            [pltpu.SemaphoreType.DMA(())],
            limit=4,
        )

    if usual:
        weights = (w_qkv, w_out, gains, biases, w_up, w_down.T)
        high = 4 * small + 8
        packed = call(
            pack_kernel,
            "pack",
            [(me, smem)] + [in_hbm(w) for w in weights],
            [pltpu.VMEM((1, high + 2 * tall, width), BF16)],
            [pltpu.VMEM(w.shape, BF16) for w in weights] + [pltpu.SemaphoreType.DMA((6,))],
        )[0]
        planes = [packed] + [swap(packed, "dp", bit) for bit in (2, 4, 6)]
        cot, cot_t = fetch_turned(after(me, packed))
        planes[3] = after(planes[3], cot)
        held_a = merge([plane[0, :high] for plane in planes])
        b = jnp.concatenate([plane[:, high:] for plane in planes], 0)
        far_b = swap(b, "tensor", 2)
        held_a = merge([held_a, swap(held_a, "dp", 1)])
        b = jnp.concatenate([b, swap(b, "dp", 1)], 0)
        x, xhat1, inv1, xhat_t = fetch(after(me, (held_a, far_b)))
        held_a = merge([held_a, after(swap(held_a, "tensor", 2), (b, xhat1))])
        far_x = swap(far_b, "dp", 1)
        got_a = swap(held_a, "tensor", 1)
        got_b = swap(b, "tensor", 1)
    else:
        held_a, got_a, held_b, got_b = other_blocks(*other_pack(*weights, index), index, n_dp, n_t)
        b, far_b = held_b[:VDP], held_b[VDP:]
        got_b, got_far = got_b[:VDP], got_b[VDP:]
        x, xhat1, inv1, xhat_t = fetch(me)
        cot, cot_t = fetch_turned(me)
    qkv, prob, o, x1, wqkv, wout, vec = call(
        functools.partial(attend_kernel, some),
        "attend",
        [(me, smem), (virt, smem), (lengths, smem), (row_mask, smem), x, xhat1, held_a, got_a],
        [
            pltpu.VMEM((own, 3 * width), BF16),
            pltpu.VMEM((rows, WIN, width), BF16),
            pltpu.VMEM((own, width), BF16),
            pltpu.VMEM((own, width), F32),
            pltpu.VMEM((width, 3 * width), BF16),
            pltpu.VMEM((width, width), BF16),
            pltpu.VMEM((8, width), F32),
        ],
        flops=token_mm * (4 * width + 2 * WIN),
    )
    tall_b = 2 * (width // VDP)
    mats = [pltpu.VMEM((width, 2 * width), BF16)] * 2 + [pltpu.VMEM((2 * width, width), BF16)] * 2
    if usual:
        far_b = jnp.concatenate([far_b, after(far_x, x1)], 0)
        got_far = swap(far_b, "tensor", 1)
        got_b = after(got_b, far_b)
    wide_per = 6 if rows % 6 == 0 else 1
    *first, keep_b, send_b = call(
        functools.partial(hidden_near_kernel, wide_per),
        "hidden_near",
        [(virt, smem), x1, cot, cot_t, vec, b, got_b],
        [
            pltpu.VMEM((own, width), BF16),
            pltpu.VMEM((own, width), F32),
            pltpu.VMEM((own, 1), F32),
            pltpu.VMEM((own, width), F32),
            pltpu.VMEM((own, width), F32),
            pltpu.VMEM((VDP, tall_b, width), F32),
            pltpu.VMEM((VDP, tall_b, width), BF16),
        ],
        [pltpu.VMEM((own, 2 * width), BF16)] * 2 + mats,
        token_mm * 12 * width,
        12,
    )
    y, dx1, g, gout, gvec = call(
        functools.partial(hidden_far_kernel, wide_per),
        "hidden_far",
        [(virt, smem), cot, vec, far_b, got_far, *first, o],
        [
            pltpu.VMEM((own, width), BF16),
            pltpu.VMEM((own, width), F32),
            pltpu.VMEM((own, width), BF16),
            pltpu.VMEM((width, width), F32),
            pltpu.VMEM((8, width), F32),
        ],
        mats,
        token_mm * 9 * width,
    )
    core, xbit = ("tensor", 1), ("dp", 1)
    if usual:
        held_b = fold_step(keep_b, send_b, *core, g)
        y = after(y, held_b)
    y_near = swap(y, "tensor", 1)
    dqkv, keep_a, send_a, sums = call(
        functools.partial(back_kernel, per),
        "back",
        [(virt, smem), qkv, prob, g, xhat_t, wqkv, wout, vec, gout, gvec],
        [
            pltpu.VMEM((own, 3 * width), BF16),
            pltpu.VMEM((VDP, 32, width), F32),
            pltpu.VMEM((VDP * 32 + 8, width), BF16),
            pltpu.VMEM((8, width), F32),
        ],
        [pltpu.VMEM((width, 3 * width), F32)],
        token_mm * (4 * width + 5 * WIN),
    )
    if usual:
        held_b = fold_step(*halves(held_b), *xbit)
        vec = after(vec, held_b)
    gx, gxb, layer_out = call(
        functools.partial(token_grad_kernel, less),
        "token_grad",
        [(me, smem), dqkv, wqkv, vec, xhat1, inv1, dx1, y, y_near],
        [
            pltpu.VMEM((own, width), F32),
            pltpu.VMEM((own, width), BF16),
            struct((images * seq_len, width), BF16),
        ],
        [pltpu.VMEM((3 * width, width), BF16), pltpu.SemaphoreType.DMA((2,))],
        flops=token_mm * 3 * width,
    )
    layer_out = layer_out.reshape(images, seq_len, width)

    def place(gx_near):
        return call(
            functools.partial(place_kernel, less),
            "place",
            [(me, smem), gx, gx_near],
            [struct((images * seq_len, width), F32)],
            [pltpu.VMEM((own, width), F32), pltpu.SemaphoreType.DMA((rows // less + 1,))],
        )[0].reshape(images, seq_len, width)

    if usual:
        got = after(swap(send_a, *core), gxb).astype(F32)
        held_a = keep_a + got[:-8].reshape(keep_a.shape)
        sums = sums + got[-8:]
        gx_near = swap(after(gxb, held_a), "tensor", 1)
        low_b = after(held_b.astype(BF16), held_a)
        got_b = [swap(low_b[n], "dp", 2 * n) for n in range(1, 4)]
        send_a = jnp.concatenate([held_a[4:].reshape(-1, width), sums], 0).astype(BF16)
        got = swap(send_a, *xbit).astype(F32)
        held_a = held_a[:4] + got[:-8].reshape(4, -1, width)
        sums = sums + got[-8:]
        got_a = [
            swap(jnp.concatenate([held_a[n], sums], 0).astype(BF16), "dp", 2 * n) for n in range(1, 4)
        ]
        grad_tokens = place(after(gx_near, got_b))
        got_a[2] = after(got_a[2], grad_tokens)
        shapes = ((small, 3 * width), (small, width), (2, small), (3, small), (tall, width), (tall, width))
        o_qkv, o_out, o_gains, o_bias, o_up, o_down = call(
            finish_kernel,
            "finish",
            [(me, smem), held_a, held_b, sums, *got_a, *got_b],
            [struct(shape, F32) for shape in shapes],
            limit=2,
            hbm_outs=False,
        )
    else:
        grad_tokens = place(swap(gxb, "tensor", 1))
        send_a = send_a[:-8].reshape(keep_a.shape)
        grad_a, grad_b = other_reduce((keep_a, send_a), (keep_b, send_b), sums, index, n_dp, n_t)
        o_qkv = jnp.concatenate([grad_a[p * small : (p + 1) * small] for p in range(3)], 1)
        o_out = grad_a[3 * small : 4 * small]
        o_vec = lax.dynamic_slice_in_dim(grad_a[4 * small : 4 * small + 5], index * small, small, 1)
        o_gains, o_bias = o_vec[:2], o_vec[2:]
        o_up, o_down = grad_b[:tall], grad_b[tall:]
    return layer_out, grad_tokens, o_qkv, o_out, o_gains, o_bias, o_up, o_down.T


def solution(mesh):
    in_specs = (
        P("dp", None, None),
        P("dp"),
        P("dp", None),
        P("dp", None, None),
        P(("dp", "tensor"), None),
        P(("dp", "tensor"), None),
        P(None, ("dp", "tensor")),
        P(None, ("dp", "tensor")),
        P("dp", "tensor"),
        P("tensor", "dp"),
    )
    out_specs = (
        P("dp", None, None),
        P("dp", None, None),
        P(("dp", "tensor"), None),
        P(("dp", "tensor"), None),
        P(None, ("dp", "tensor")),
        P(None, ("dp", "tensor")),
        P("dp", "tensor"),
        P("tensor", "dp"),
    )
    return jax.shard_map(
        on_device, mesh=mesh, in_specs=in_specs, out_specs=out_specs, check_vma=False
    )
```

```python
import functools

import jax
import jax.numpy as jnp
from jax import lax
from jax.experimental import pallas as pl
from jax.experimental.pallas import tpu as pltpu
from jax.sharding import PartitionSpec as P

HEADS = 2
WIN = 96
F32 = jnp.float32
BF16 = jnp.bfloat16
VDP, VT = 8, 4
CHIPS = VDP * VT // 2
MIB = 1 << 20

NN = ((1,), (0,))
NT = ((1,), (1,))
TN = ((0,), (0,))


def dot(a, b, dims):
    return lax.dot_general(a, b, (dims, ((), ())), preferred_element_type=F32)


def twist(i):
    return (i & 1) * 4 + (i >> 1)


def turn(i):
    return ((i & 1) << 2) | (i & 2) | ((i & 4) >> 2)


def spot(m):
    return (m % 2) * VDP + twist(m // 2)


def norm_parts(values):
    center = values - jnp.mean(values, -1, keepdims=True)
    inv = lax.rsqrt(jnp.mean(center * center, -1, keepdims=True) + 1e-05)
    return center * inv, inv


def norm_back(grad, xhat, inv, gain):
    scaled = grad * gain
    return inv * (
        scaled
        - jnp.mean(scaled, -1, keepdims=True)
        - xhat * jnp.mean(scaled * xhat, -1, keepdims=True)
    )


def gelu_both(u):
    c = 0.7978845608028654
    u2 = u * u
    t = jnp.tanh(u * (c + (c * 0.044715) * u2))
    half = 0.5 + 0.5 * t
    value = u * half
    slope = half + (value - value * half) * (2 * c + (6 * c * 0.044715) * u2)
    return value, slope


def apart(both, hs):
    blocks = []
    for h in range(HEADS):
        parts = [jnp.zeros((WIN, hs), BF16)] * HEADS
        parts[h] = both[:, h * hs : (h + 1) * hs]
        blocks.append(jnp.concatenate(parts, 1))
        blocks.append(jnp.zeros((hs - WIN, HEADS * hs), BF16))
    return jnp.concatenate(blocks, 0)


def pack_kernel(me, *refs):
    sources, packed, held, sems = refs[:6], refs[6], refs[7:13], refs[13]
    copies = [pltpu.make_async_copy(a, b, sems.at[n]) for n, (a, b) in enumerate(zip(sources, held))]
    for copy in copies:
        copy.start()
    qkv, out, gains, biases, up, down = held
    small, width = out.shape
    tall = up.shape[0]
    lane = lax.broadcasted_iota(jnp.int32, (1, width), 1)
    mine = lane // small == me[0]
    for copy in copies:
        copy.wait()
    for part in range(3):
        packed[0, part * small : (part + 1) * small] = qkv[:, part * width : (part + 1) * width]
    packed[0, 3 * small : 4 * small] = out[...]
    rows = [gains[0:1], gains[1:2], biases[0:1], biases[1:2], biases[2:3]]
    vals = jnp.concatenate(rows + [jnp.zeros((3, small), BF16)], 0).astype(F32)
    wide = jnp.concatenate([vals] * (width // small), 1)
    at = 4 * small + 8
    packed[0, 4 * small : at] = jnp.where(mine, wide, 0.0).astype(BF16)
    packed[0, at : at + tall] = up[...]
    packed[0, at + tall :] = down[...]


def turn_kernel(me, cot, tokens, cot_ref, cot_t, x_ref, sems):
    own = cot_ref.shape[0]
    at = pl.ds(lax.rem(me[0], 2) * own, own)
    copies = [
        pltpu.make_async_copy(cot.at[at], cot_ref, sems.at[0]),
        pltpu.make_async_copy(tokens.at[at], x_ref, sems.at[1]),
    ]
    for copy in copies:
        copy.start()
    size = 256 if own % 256 == 0 else own
    copies[0].wait()
    for n in range(own // size):
        part = slice(n * size, (n + 1) * size)
        cot_t[:, part] = cot_ref[part].T
    copies[1].wait()


def first_norm_kernel(x_ref, xhat_ref, inv_ref, xhat_t):
    own, width = x_ref.shape
    ones = jnp.full((width, width), 1.0 / width, BF16)
    size = 256 if own % 256 == 0 else own
    for n in range(own // size):
        part = slice(n * size, (n + 1) * size)
        x = x_ref[part]
        center = x.astype(F32) - dot(x, ones, NN)
        inv = lax.rsqrt(dot((center * center).astype(BF16), ones, NN) + 1e-05)
        xhat = center * inv
        xhat_ref[part] = xhat
        inv_ref[part] = inv[:, :1]
        xhat_t[:, part] = xhat.astype(BF16).T


def attend_kernel(
    per, me, virt, lens, live, x_ref, xhat_ref, held, got,
    qkv_ref, prob_ref, o_ref, x1_ref, wqkv, wout, vec,
):
    tokens, width = x_ref.shape
    rows = tokens // WIN
    hs = width // HEADS
    here = twist(virt[0] // 4)
    y_own = (virt[0] // 2) % 2
    first = virt[0] % 2 == 0
    for m in range(CHIPS):
        k = spot(m) ^ (here + y_own * VDP)
        at = pl.ds(pl.multiple_of(k * 32, 32), 32)
        a = held[at].astype(F32)
        b = got[at].astype(F32)
        even = jnp.where(first, a, b)
        odd = jnp.where(first, b, a)
        for part in range(3):
            both = jnp.concatenate([even[part * 8 : part * 8 + 8], odd[part * 8 : part * 8 + 8]], 0)
            wqkv[m * 16 : m * 16 + 16, part * width : (part + 1) * width] = both.astype(BF16)
        both = jnp.concatenate([even[24:32], odd[24:32]], 0)
        wout[m * 16 : m * 16 + 16] = both.astype(BF16)
    total = held[CHIPS * 32 :].astype(F32) + got[CHIPS * 32 :].astype(F32)
    vec[...] = total
    scale = hs**-0.5
    ii = lax.broadcasted_iota(jnp.int32, (WIN, hs), 0)
    jj = lax.broadcasted_iota(jnp.int32, (WIN, hs), 1)
    same = ii == jj
    image_rows = live.shape[1]
    base = lax.rem(me[0], 2) * rows

    def enter(c):
        part = slice(c * per * WIN, (c + 1) * per * WIN)
        h1 = (xhat_ref[part] * total[0:1] + total[2:3]).astype(BF16)
        qkv = dot(h1, wqkv[...], NN).astype(BF16)
        qkv_ref[part] = qkv
        scores = []
        for r in range(per):
            at = slice(r * WIN, (r + 1) * WIN)
            scores.append(dot(qkv[at, :width], apart(qkv[at, width : 2 * width], hs), NT))
        return qkv, scores

    ahead = enter(0)
    for c in range(rows // per):
        qkv, scores = ahead
        if c + 1 < rows // per:
            ahead = enter(c + 1)
        part = slice(c * per * WIN, (c + 1) * per * WIN)
        probs = []
        for r in range(per):
            row = base + c * per + r
            image = row // image_rows
            inside = row - image * image_rows
            reach = jnp.where(live[image, inside] == 1, lens[image] - inside * WIN, 0)
            allowed = same | (jj < jnp.minimum(ii, reach))
            heads = []
            for h in range(HEADS):
                s = jnp.where(allowed, scores[r][:, h * hs : (h + 1) * hs], -1e30)
                e = jnp.exp((s - jnp.max(s, -1, keepdims=True)) * scale)
                heads.append((e * (1.0 / jnp.sum(e, -1, keepdims=True))).astype(BF16))
            probs.append(jnp.concatenate(heads, 1))
        mixed = []
        for r in range(per):
            at = slice(r * WIN, (r + 1) * WIN)
            mixed.append(dot(probs[r], apart(qkv[at, 2 * width :], hs), NN).astype(BF16))
        o = jnp.concatenate(mixed, 0)
        for n, p in enumerate(probs):
            prob_ref[c * per + n] = p
        o_ref[part] = o
        x1_ref[part] = x_ref[part].astype(F32) + dot(o, wout[...], NN)


def join(virt, blocks, n, up, down_t):
    tall = blocks.shape[1] // 2
    width = up.shape[0]
    here = twist(virt[0] // 4)
    for i in range(VDP):
        k = twist(i) ^ here
        at = slice(i * tall, (i + 1) * tall)
        cols = slice(n * width, (n + 1) * width)
        up[at, cols] = blocks[k, :tall]
        down_t[at, cols] = blocks[k, tall:]


def hidden_units(h2, dyb, up, down_t):
    u = dot(h2, up[...], NN).astype(BF16)
    da = dot(dyb, down_t[...], NN).astype(BF16)
    a, slope = gelu_both(u)
    return a, da * slope


def hidden_near_kernel(
    per, virt, x1_ref, cot_ref, cot_t, vec, own, got,
    h2_ref, xhat_ref, inv_ref, f_ref, dh2_ref, keep, send,
    a_ref, du_ref, up, down_t, up_t, down,
):
    tokens, width = x1_ref.shape
    size = per * WIN
    join(virt, own, 0, up, down_t)
    join(virt, got, 1, up, down_t)
    up_t[...] = up[...].T
    down[...] = down_t[...].T
    for c in range(tokens // size):
        part = slice(c * size, (c + 1) * size)
        x1 = x1_ref[part]
        xhat, inv = norm_parts(x1)
        xhat_ref[part] = xhat
        inv_ref[part] = inv
        h2 = (xhat * vec[1:2] + vec[3:4]).astype(BF16)
        h2_ref[part] = h2
        a, du = hidden_units(h2, cot_ref[part], up, down_t)
        a_ref[part] = a
        du_ref[part] = du
        f_ref[part] = x1 + vec[4:5] + dot(a, down[...], NN)
        dh2_ref[part] = dot(du, up_t[...], NN)
    gdown = dot(cot_t[...], a_ref[...], NN)
    gup = dot(h2_ref[...], du_ref[...], TN)
    tall = width // VDP
    here = turn(virt[0] // 4)
    for i in range(VDP):
        at = slice(i * tall, (i + 1) * tall)
        k = turn(i) ^ here
        keep[k, :tall] = gup[at, :width]
        keep[k, tall:] = gdown[at, :width]
        send[k, :tall] = gup[at, width:].astype(BF16)
        send[k, tall:] = gdown[at, width:].astype(BF16)


def hidden_far_kernel(
    per, virt, cot_ref, vec, own, got, h2_ref, xhat_ref, inv_ref, f_ref, dh2_ref, o_ref,
    y_ref, dx1_ref, g_ref, gout, gvec,
    up, down_t, up_t, down,
):
    tokens, width = h2_ref.shape
    size = per * WIN
    join(virt, own, 0, up, down_t)
    join(virt, got, 1, up, down_t)
    up_t[...] = up[...].T
    down[...] = down_t[...].T
    sums = [jnp.zeros((1, width), F32)] * 3
    for c in range(tokens // size):
        part = slice(c * size, (c + 1) * size)
        a, du = hidden_units(h2_ref[part], cot_ref[part], up, down_t)
        y_ref[part] = (f_ref[part] + dot(a, down[...], NN)).astype(BF16)
        dh2 = dh2_ref[part] + dot(du, up_t[...], NN)
        dy = cot_ref[part].astype(F32)
        xhat = xhat_ref[part]
        dx1 = dy + norm_back(dh2, xhat, inv_ref[part], vec[1:2])
        dx1_ref[part] = dx1
        g_ref[part] = dx1.astype(BF16)
        for n, term in enumerate((dh2 * xhat, dh2, dy)):
            sums[n] = sums[n] + jnp.sum(term, 0, keepdims=True)
    gout[...] = dot(o_ref[...], g_ref[...], TN)
    zero = jnp.zeros((1, width), F32)
    gvec[...] = jnp.concatenate([zero, sums[0], zero, sums[1], sums[2], zero, zero, zero], 0)


def own_rows(virt, i, other):
    core = virt[0] % 2
    core = 1 - core if other else core
    return pl.ds(pl.multiple_of(i * 32 + ((virt[0] // 2) % 2) * 16 + core * 8, 8), 8)


def back_kernel(
    per, virt, qkv_ref, prob_ref, g_ref, xhat_t, wqkv, wout, vec, gout, gvec,
    dqkv, keep, send, vec_sums,
    gqkv,
):
    tokens, width = g_ref.shape
    hs = width // HEADS
    scale = hs**-0.5
    every = [(r, h) for r in range(tokens // WIN) for h in range(HEADS)]
    groups = [every[n : n + 2 * per] for n in range(0, len(every), 2 * per)]

    def piece(ref, r, h, part=0):
        return ref[r * WIN : (r + 1) * WIN, part * width + h * hs : part * width + (h + 1) * hs]

    def enter(pairs):
        r = pairs[0][0]
        do = dot(g_ref[r * WIN : (r + per) * WIN], wout[...], NT).astype(BF16)
        dos = [do[(n - r) * WIN : (n - r + 1) * WIN, h * hs : (h + 1) * hs] for n, h in pairs]
        probs = [prob_ref[r, :, h * hs : h * hs + WIN] for r, h in pairs]
        dps = [dot(a, piece(qkv_ref, r, h, 2), NT) for a, (r, h) in zip(dos, pairs)]
        dvs = [dot(p, a, TN).astype(BF16) for p, a in zip(probs, dos)]
        return probs, dps, dvs

    ahead = enter(groups[0])
    for place, pairs in enumerate(groups):
        probs, dps, dvs = ahead
        if place + 1 < len(groups):
            ahead = enter(groups[place + 1])
        dss = []
        for p, dp in zip(probs, dps):
            pf = p.astype(F32)
            ds = pf * (dp - jnp.sum(dp * pf, -1, keepdims=True)) * scale
            dss.append(ds.astype(BF16))
        dqs = [dot(ds, piece(qkv_ref, r, h, 1), NN).astype(BF16) for ds, (r, h) in zip(dss, pairs)]
        dks = [dot(ds, piece(qkv_ref, r, h, 0), TN).astype(BF16) for ds, (r, h) in zip(dss, pairs)]
        for n, (r, h) in enumerate(pairs):
            for part, values in enumerate((dqs, dks, dvs)):
                at = slice(part * width + h * hs, part * width + (h + 1) * hs)
                dqkv[r * WIN : (r + 1) * WIN, at] = values[n]
    grad = dot(xhat_t[...], dqkv[...], NN)
    total = jnp.zeros((1, 3 * width), F32)
    for r in range(tokens // WIN):
        total = total + jnp.sum(dqkv[r * WIN : (r + 1) * WIN].astype(F32), 0, keepdims=True)
    w = wqkv[...].astype(F32)
    cols = jnp.concatenate([
        jnp.broadcast_to(jnp.sum(w * grad, -1, keepdims=True), (width, 64)),
        jnp.broadcast_to(jnp.sum(w * total, -1, keepdims=True), (width, 64)),
    ], 1)
    lines = cols.T
    gain, from_total = lines[0:1], lines[64:65]
    vec_t = vec[...].T
    gqkv[...] = grad * vec_t[:, 0:1] + total * vec_t[:, 2:3]
    rest = gvec[...]
    sums = jnp.concatenate([gain, rest[1:2], from_total, rest[3:]], 0)
    here = twist(virt[0] // 4)
    for i in range(VDP):
        k = twist(i) ^ here
        mine, other = own_rows(virt, i, 0), own_rows(virt, i, 1)
        theirs = []
        for part in range(3):
            at = slice(part * width, (part + 1) * width)
            keep[k, part * 8 : part * 8 + 8] = gqkv[mine, at]
            theirs.append(gqkv[other, at])
        keep[k, 24:] = gout[mine]
        at = pl.ds(pl.multiple_of(k * 32, 32), 32)
        send[at] = jnp.concatenate(theirs + [gout[other]], 0).astype(BF16)
    vec_sums[...] = sums
    send[VDP * 32 :] = sums.astype(BF16)


def token_grad_kernel(per, me, dqkv, wqkv, vec, xhat_ref, inv_ref, dx1_ref, y, y_near, gx, gxb, out, turned, sems):
    own = dqkv.shape[0]
    size = per * WIN
    copies = []
    for n, source in enumerate((y, y_near)):
        at = pl.ds((lax.rem(me[0], 2) ^ n) * own, own)
        copies.append(pltpu.make_async_copy(source, out.at[at], sems.at[n]))
        copies[-1].start()
    turned[...] = wqkv[...].T
    for c in range(own // size):
        part = slice(c * size, (c + 1) * size)
        dh1 = dot(dqkv[part], turned[...], NN)
        values = dx1_ref[part] + norm_back(dh1, xhat_ref[part], inv_ref[part], vec[0:1])
        gx[part] = values
        gxb[part] = values.astype(BF16)
    for copy in copies:
        copy.wait()


def place_kernel(per, me, mine, theirs, out, wide, sems):
    own = theirs.shape[0]
    size = per * WIN
    here = lax.rem(me[0], 2) * own
    copies = [pltpu.make_async_copy(mine, out.at[pl.ds(here, own)], sems.at[own // size])]
    copies[0].start()
    for c in range(own // size):
        part = pl.ds(c * size, size)
        wide[part] = theirs[part].astype(F32)
        at = pl.ds(own - here + c * size, size)
        copies.append(pltpu.make_async_copy(wide.at[part], out.at[at], sems.at[c]))
        copies[-1].start()
    for copy in copies:
        copy.wait()


def finish_kernel(me, keep_a, keep_b, sums, *refs):
    qkv, out, gains, biases, up, down = refs[3:]
    small, width = out.shape
    tall = up.shape[0]
    high = 4 * small + 8
    total, vec = keep_a[0], sums[...]
    for got in refs[:3]:
        total = total + got[: 4 * small].astype(F32)
        vec = vec + got[4 * small : high].astype(F32)
    units = keep_b[0] + refs[1][high:].astype(F32)
    for part in range(3):
        qkv[:, part * width : (part + 1) * width] = total[part * small : (part + 1) * small]
    out[...] = total[3 * small :]
    vec = pltpu.roll(vec, width - me[0] * small, 1)[:, :small]
    gains[...] = vec[:2]
    biases[...] = vec[2:5]
    up[...] = units[:tall]
    down[...] = units[tall:]


def swap(block, axis, bit):
    size = lax.axis_size(axis)
    return lax.ppermute(block, axis, [(i, i ^ bit) for i in range(size)])


def steps_of(axis):
    return [(axis, 1 << k) for k in reversed(range(lax.axis_size(axis).bit_length() - 1))]


def after(value, other):
    return lax.optimization_barrier((value, other))[0]


def merge(pieces):
    vec = sum(piece[-8:] for piece in pieces)
    return jnp.concatenate([piece[:-8] for piece in pieces] + [vec], 0)


def halves(held):
    half = held.shape[0] // 2
    return held[:half], held[half:].astype(BF16)


def fold_step(keep, send, axis, bit, past=None):
    got = swap(send, axis, bit)
    return keep + (got if past is None else after(got, past)).astype(F32)


def bit_reverse(index, count):
    out = 0 * index
    for k in range(count):
        out = out | (((index >> k) & 1) << (count - 1 - k))
    return out


def by_device(block, me):
    blocks = block[None]
    for axis, bit in steps_of("dp") + steps_of("tensor"):
        blocks = jnp.concatenate([blocks, swap(blocks, axis, bit)], 0)
    count = blocks.shape[0]
    order = jnp.arange(count, dtype=jnp.int32) ^ me
    return jnp.take(blocks, bit_reverse(order, count.bit_length() - 1), axis=0)


def other_pack(w_qkv, w_out, gains, biases, w_up, w_down, me):
    small, width = w_out.shape
    qkv = w_qkv.reshape(small, 3, width).transpose(1, 0, 2).reshape(3 * small, width)
    rows = jnp.concatenate([gains, biases], 0)
    place = jnp.zeros((8, width), BF16)
    place = lax.dynamic_update_slice(place, rows, (jnp.int32(0), me * small))
    return jnp.concatenate([qkv, w_out, place], 0), jnp.concatenate([w_up, w_down.T], 0)


def other_blocks(a, b, me, n_dp, n_t):
    a = by_device(a, me)
    b = by_device(b, me)
    width = a.shape[2]
    count = n_dp * n_t
    small = width // count
    big = width // (VDP * VT)
    mats = a[:, : 4 * small].reshape(count, 4, small, width).transpose(1, 0, 2, 3)
    mats = mats.reshape(4, VDP * VT, big, width).transpose(1, 0, 2, 3).reshape(VDP * VT, 4 * big, width)
    vec = jnp.sum(a[:, 4 * small :].astype(F32), 0).astype(BF16)
    a = mats
    tall = width // n_dp
    b = b.reshape(n_dp, VT, 2, tall, width).transpose(1, 2, 0, 3, 4)
    b = b.reshape(VT, 2, VDP, width // VDP, width).transpose(2, 0, 1, 3, 4)
    b = b.reshape(VDP * VT, 2 * (width // VDP), width)

    y_own = (me // 2) % 2

    def placed(blocks):
        pairs = blocks.reshape((CHIPS, 2) + blocks.shape[1:])
        chips = sorted(range(CHIPS), key=spot)
        pairs = jnp.stack([pairs[m] for m in chips], 0)
        pairs = jnp.where(y_own == 1, jnp.roll(pairs, VDP, 0), pairs)
        return pairs[:, 0], pairs[:, 1]

    held_a, got_a = (part.reshape(-1, width) for part in placed(a))
    held_a = jnp.concatenate([held_a, vec], 0)
    got_a = jnp.concatenate([got_a, jnp.zeros_like(vec)], 0)
    return (held_a, got_a) + placed(b)


def other_reduce(pair_a, pair_b, sums, me, n_dp, n_t):
    count = n_dp * n_t
    y_own = (me // 2) % 2

    def whole(keep, send, order):
        pairs = jnp.stack([keep, send.astype(F32)], 1)
        pairs = jnp.stack([pairs[order(i)] for i in range(VDP)], 0)
        none = jnp.zeros_like(pairs)
        both = jnp.stack([jnp.where(y_own == y, pairs, none) for y in range(2)], 1)
        return both.reshape((VDP * VT,) + keep.shape[1:])

    def rows_of(blocks, parts):
        big = blocks.shape[1] // parts
        mats = blocks.reshape(VDP * VT, parts, big, -1).transpose(1, 0, 2, 3)
        mats = mats.reshape(parts, count, VDP * VT * big // count, -1).transpose(1, 0, 2, 3)
        return mats.reshape(count, -1, blocks.shape[2])

    a, b = whole(*pair_a, twist), whole(*pair_b, turn)
    width = a.shape[2]
    tall, high = width // n_dp, width // VDP
    cols = b.reshape(VDP, VT, 2, high, width).transpose(1, 2, 0, 3, 4)
    cols = cols.reshape(VT, 2, n_dp, tall, width).transpose(2, 0, 1, 3, 4)
    cols = cols.reshape(count, 2 * tall, width)
    vec = jnp.broadcast_to(jnp.where(y_own == 0, sums, 0.0)[None], (count,) + sums.shape)
    a = jnp.concatenate([rows_of(a, 4), vec], 1)
    results = []
    for blocks in (a, cols):
        blocks = jnp.take(blocks, jnp.arange(count, dtype=jnp.int32) ^ me, axis=0)
        for axis, bit in reversed(steps_of("dp") + steps_of("tensor")):
            pairs = blocks.reshape((-1, 2) + blocks.shape[1:])
            got = swap(pairs[:, 1].astype(BF16), axis, bit)
            blocks = pairs[:, 0] + got.astype(F32)
        results.append(blocks[0])
    return results


def struct(shape, dtype):
    return jax.ShapeDtypeStruct(shape, dtype)


def call(kernel, name, args, outs, scratch=(), flops=0, limit=8, hbm_outs=True):
    args = [a if isinstance(a, tuple) else (a, pltpu.VMEM) for a in args]
    moved = sum(a.size * a.dtype.itemsize for a, _ in args)
    spaces = [pl.ANY if hbm_outs and isinstance(o, jax.ShapeDtypeStruct) else pltpu.VMEM for o in outs]
    return pl.pallas_call(
        kernel,
        name=name,
        out_shape=outs,
        in_specs=[pl.BlockSpec(memory_space=space) for _, space in args],
        out_specs=[pl.BlockSpec(memory_space=space) for space in spaces],
        scratch_shapes=list(scratch),
        compiler_params=pltpu.CompilerParams(vmem_limit_bytes=limit * MIB),
        cost_estimate=pl.CostEstimate(flops=flops, bytes_accessed=moved, transcendentals=0),
    )(*[a for a, _ in args])


def on_device(tokens, lengths, row_mask, cotangent, w_qkv, w_out, gains, biases, w_up, w_down):
    images, seq_len, width = tokens.shape
    n_dp, n_t = lax.axis_size("dp"), lax.axis_size("tensor")
    index = lax.axis_index("dp") * n_t + lax.axis_index("tensor")
    me = index.astype(jnp.int32).reshape(1)
    usual = (n_dp, n_t) == (VDP, VT)
    virt = me if usual else (index // 2 % 2 * 2).astype(jnp.int32).reshape(1)
    small = width // (n_dp * n_t)
    tall = width // n_dp
    own = images * seq_len // 2
    rows = own // WIN
    per = 12 if rows % 12 == 0 else 1
    some = 6 if rows % 6 == 0 else 1
    less = 4 if rows % 4 == 0 else 1
    smem = pltpu.SMEM
    weights = (w_qkv, w_out, gains, biases, w_up, w_down)
    token_mm = 2 * own * width
    hbm = pltpu.HBM

    def in_hbm(array):
        return (pltpu.with_memory_space_constraint(array, hbm), hbm)

    def first_norm(x):
        return call(
            first_norm_kernel,
            "first_norm",
            [x],
            [
                pltpu.VMEM((own, width), F32),
                pltpu.VMEM((own, 1), F32),
                pltpu.VMEM((width, own), BF16),
            ],
            limit=4,
        )

    def fetch(me):
        flat = [array.reshape(images * seq_len, width) for array in (cotangent, tokens)]
        return call(
            turn_kernel,
            "turn",
            [(me, smem)] + [in_hbm(array) for array in flat],
            [
                pltpu.VMEM((own, width), BF16),
                pltpu.VMEM((width, own), BF16),
                pltpu.VMEM((own, width), BF16),
            ],
            [pltpu.SemaphoreType.DMA((2,))],
            limit=4,
        )

    if usual:
        weights = (w_qkv, w_out, gains, biases, w_up, w_down.T)
        high = 4 * small + 8
        packed = call(
            pack_kernel,
            "pack",
            [(me, smem)] + [in_hbm(w) for w in weights],
            [pltpu.VMEM((1, high + 2 * tall, width), BF16)],
            [pltpu.VMEM(w.shape, BF16) for w in weights] + [pltpu.SemaphoreType.DMA((6,))],
        )[0]
        planes = [packed] + [swap(packed, "dp", bit) for bit in (2, 4, 6)]
        cot, cot_t, x = fetch(after(me, packed))
        planes[3] = after(planes[3], cot)
        held_a = merge([plane[0, :high] for plane in planes])
        b = jnp.concatenate([plane[:, high:] for plane in planes], 0)
        far_b = swap(b, "tensor", 2)
        held_a = merge([held_a, swap(held_a, "dp", 1)])
        b = jnp.concatenate([b, swap(b, "dp", 1)], 0)
        xhat1, inv1, xhat_t = first_norm(after(x, (held_a, far_b)))
        held_a = merge([held_a, after(swap(held_a, "tensor", 2), (b, xhat1))])
        far_x = swap(far_b, "dp", 1)
        got_a = swap(held_a, "tensor", 1)
        got_b = swap(b, "tensor", 1)
    else:
        held_a, got_a, held_b, got_b = other_blocks(*other_pack(*weights, index), index, n_dp, n_t)
        b, far_b = held_b[:VDP], held_b[VDP:]
        got_b, got_far = got_b[:VDP], got_b[VDP:]
        cot, cot_t, x = fetch(me)
        xhat1, inv1, xhat_t = first_norm(x)
    qkv, prob, o, x1, wqkv, wout, vec = call(
        functools.partial(attend_kernel, some),
        "attend",
        [(me, smem), (virt, smem), (lengths, smem), (row_mask, smem), x, xhat1, held_a, got_a],
        [
            pltpu.VMEM((own, 3 * width), BF16),
            pltpu.VMEM((rows, WIN, width), BF16),
            pltpu.VMEM((own, width), BF16),
            pltpu.VMEM((own, width), F32),
            pltpu.VMEM((width, 3 * width), BF16),
            pltpu.VMEM((width, width), BF16),
            pltpu.VMEM((8, width), F32),
        ],
        flops=token_mm * (4 * width + 2 * WIN),
    )
    tall_b = 2 * (width // VDP)
    mats = [pltpu.VMEM((width, 2 * width), BF16)] * 2 + [pltpu.VMEM((2 * width, width), BF16)] * 2
    if usual:
        far_b = jnp.concatenate([far_b, after(far_x, x1)], 0)
        got_far = swap(far_b, "tensor", 1)
        got_b = after(got_b, far_b)
    wide_per = 6 if rows % 6 == 0 else 1
    *first, keep_b, send_b = call(
        functools.partial(hidden_near_kernel, wide_per),
        "hidden_near",
        [(virt, smem), x1, cot, cot_t, vec, b, got_b],
        [
            pltpu.VMEM((own, width), BF16),
            pltpu.VMEM((own, width), F32),
            pltpu.VMEM((own, 1), F32),
            pltpu.VMEM((own, width), F32),
            pltpu.VMEM((own, width), F32),
            pltpu.VMEM((VDP, tall_b, width), F32),
            pltpu.VMEM((VDP, tall_b, width), BF16),
        ],
        [pltpu.VMEM((own, 2 * width), BF16)] * 2 + mats,
        token_mm * 12 * width,
        12,
    )
    y, dx1, g, gout, gvec = call(
        functools.partial(hidden_far_kernel, wide_per),
        "hidden_far",
        [(virt, smem), cot, vec, far_b, got_far, *first, o],
        [
            pltpu.VMEM((own, width), BF16),
            pltpu.VMEM((own, width), F32),
            pltpu.VMEM((own, width), BF16),
            pltpu.VMEM((width, width), F32),
            pltpu.VMEM((8, width), F32),
        ],
        mats,
        token_mm * 9 * width,
    )
    core, xbit, zlo = ("tensor", 1), ("dp", 1), ("dp", 2)
    if usual:
        held_b = fold_step(keep_b, send_b, *core, g)
        y = after(y, held_b)
    y_near = swap(y, "tensor", 1)
    dqkv, keep_a, send_a, sums = call(
        functools.partial(back_kernel, per),
        "back",
        [(virt, smem), qkv, prob, g, xhat_t, wqkv, wout, vec, gout, gvec],
        [
            pltpu.VMEM((own, 3 * width), BF16),
            pltpu.VMEM((VDP, 32, width), F32),
            pltpu.VMEM((VDP * 32 + 8, width), BF16),
            pltpu.VMEM((8, width), F32),
        ],
        [pltpu.VMEM((width, 3 * width), F32)],
        token_mm * (4 * width + 5 * WIN),
    )
    if usual:
        held_b = fold_step(*halves(held_b), *xbit)
        send_a = after(send_a, held_b)
        got = swap(send_a, *core).astype(F32)
        held_a = keep_a + got[:-8].reshape(keep_a.shape)
        sums = sums + got[-8:]
        vec = after(vec, held_a)
    gx, gxb, layer_out = call(
        functools.partial(token_grad_kernel, less),
        "token_grad",
        [(me, smem), dqkv, wqkv, vec, xhat1, inv1, dx1, y, y_near],
        [
            pltpu.VMEM((own, width), F32),
            pltpu.VMEM((own, width), BF16),
            struct((images * seq_len, width), BF16),
        ],
        [pltpu.VMEM((3 * width, width), BF16), pltpu.SemaphoreType.DMA((2,))],
        flops=token_mm * 3 * width,
    )
    layer_out = layer_out.reshape(images, seq_len, width)

    def place(gx_near):
        return call(
            functools.partial(place_kernel, less),
            "place",
            [(me, smem), gx, gx_near],
            [struct((images * seq_len, width), F32)],
            [pltpu.VMEM((own, width), F32), pltpu.SemaphoreType.DMA((rows // less + 1,))],
        )[0].reshape(images, seq_len, width)

    if usual:
        held_b = fold_step(*halves(held_b), *zlo, gxb)
        send_a = jnp.concatenate([held_a[4:].reshape(-1, width), sums], 0).astype(BF16)
        got = after(swap(send_a, *xbit), (gxb, held_b)).astype(F32)
        held_a = held_a[:4] + got[:-8].reshape(4, -1, width)
        sums = sums + got[-8:]
        got = [
            swap(jnp.concatenate([held_a[n], sums] + more, 0).astype(BF16), "dp", 2 * n)
            for n, more in ((1, []), (2, [held_b[1]]), (3, []))
        ]
        grad_tokens = place(swap(after(gxb, held_a), "tensor", 1))
        got[2] = after(got[2], grad_tokens)
        shapes = ((small, 3 * width), (small, width), (2, small), (3, small), (tall, width), (tall, width))
        o_qkv, o_out, o_gains, o_bias, o_up, o_down = call(
            finish_kernel,
            "finish",
            [(me, smem), held_a, held_b, sums, *got],
            [struct(shape, F32) for shape in shapes],
            limit=2,
            hbm_outs=False,
        )
    else:
        grad_tokens = place(swap(gxb, "tensor", 1))
        send_a = send_a[:-8].reshape(keep_a.shape)
        grad_a, grad_b = other_reduce((keep_a, send_a), (keep_b, send_b), sums, index, n_dp, n_t)
        o_qkv = jnp.concatenate([grad_a[p * small : (p + 1) * small] for p in range(3)], 1)
        o_out = grad_a[3 * small : 4 * small]
        o_vec = lax.dynamic_slice_in_dim(grad_a[4 * small : 4 * small + 5], index * small, small, 1)
        o_gains, o_bias = o_vec[:2], o_vec[2:]
        o_up, o_down = grad_b[:tall], grad_b[tall:]
    return layer_out, grad_tokens, o_qkv, o_out, o_gains, o_bias, o_up, o_down.T


def solution(mesh):
    in_specs = (
        P("dp", None, None),
        P("dp"),
        P("dp", None),
        P("dp", None, None),
        P(("dp", "tensor"), None),
        P(("dp", "tensor"), None),
        P(None, ("dp", "tensor")),
        P(None, ("dp", "tensor")),
        P("dp", "tensor"),
        P("tensor", "dp"),
    )
    out_specs = (
        P("dp", None, None),
        P("dp", None, None),
        P(("dp", "tensor"), None),
        P(("dp", "tensor"), None),
        P(None, ("dp", "tensor")),
        P(None, ("dp", "tensor")),
        P("dp", "tensor"),
        P("tensor", "dp"),
    )
    return jax.shard_map(
        on_device, mesh=mesh, in_specs=in_specs, out_specs=out_specs, check_vma=False
    )
```

```python
import functools

import jax
import jax.numpy as jnp
from jax import lax
from jax.experimental import pallas as pl
from jax.experimental.pallas import tpu as pltpu
from jax.sharding import PartitionSpec as P

HEADS = 2
WIN = 96
F32 = jnp.float32
BF16 = jnp.bfloat16
VDP, VT = 8, 4
CHIPS = VDP * VT // 2
MIB = 1 << 20

NN = ((1,), (0,))
NT = ((1,), (1,))
TN = ((0,), (0,))


def dot(a, b, dims):
    return lax.dot_general(a, b, (dims, ((), ())), preferred_element_type=F32)


def twist(i):
    return (i & 1) * 4 + (i >> 1)


def turn(i):
    return ((i & 1) << 2) | (i & 2) | ((i & 4) >> 2)


def spot(m):
    return (m % 2) * VDP + twist(m // 2)


def norm_parts(values):
    center = values - jnp.mean(values, -1, keepdims=True)
    inv = lax.rsqrt(jnp.mean(center * center, -1, keepdims=True) + 1e-05)
    return center * inv, inv


def norm_back(grad, xhat, inv, gain):
    scaled = grad * gain
    return inv * (
        scaled
        - jnp.mean(scaled, -1, keepdims=True)
        - xhat * jnp.mean(scaled * xhat, -1, keepdims=True)
    )


def gelu_both(u):
    c = 0.7978845608028654
    u2 = u * u
    t = jnp.tanh(u * (c + (c * 0.044715) * u2))
    half = 0.5 + 0.5 * t
    value = u * half
    slope = half + (value - value * half) * (2 * c + (6 * c * 0.044715) * u2)
    return value, slope


def apart(both, hs):
    blocks = []
    for h in range(HEADS):
        parts = [jnp.zeros((WIN, hs), BF16)] * HEADS
        parts[h] = both[:, h * hs : (h + 1) * hs]
        blocks.append(jnp.concatenate(parts, 1))
        blocks.append(jnp.zeros((hs - WIN, HEADS * hs), BF16))
    return jnp.concatenate(blocks, 0)


def pack_kernel(me, *refs):
    sources, packed, held, sems = refs[:6], refs[6], refs[7:13], refs[13]
    copies = [pltpu.make_async_copy(a, b, sems.at[n]) for n, (a, b) in enumerate(zip(sources, held))]
    for copy in copies:
        copy.start()
    qkv, out, gains, biases, up, down = held
    small, width = out.shape
    tall = up.shape[0]
    lane = lax.broadcasted_iota(jnp.int32, (1, width), 1)
    mine = lane // small == me[0]
    for copy in copies:
        copy.wait()
    for part in range(3):
        packed[0, part * small : (part + 1) * small] = qkv[:, part * width : (part + 1) * width]
    packed[0, 3 * small : 4 * small] = out[...]
    rows = [gains[0:1], gains[1:2], biases[0:1], biases[1:2], biases[2:3]]
    vals = jnp.concatenate(rows + [jnp.zeros((3, small), BF16)], 0).astype(F32)
    wide = jnp.concatenate([vals] * (width // small), 1)
    at = 4 * small + 8
    packed[0, 4 * small : at] = jnp.where(mine, wide, 0.0).astype(BF16)
    packed[0, at : at + tall] = up[...]
    packed[0, at + tall :] = down[...]


def turn_kernel(me, cot, tokens, cot_ref, cot_t, x_ref, sems):
    own = cot_ref.shape[0]
    at = pl.ds(lax.rem(me[0], 2) * own, own)
    copies = [
        pltpu.make_async_copy(cot.at[at], cot_ref, sems.at[0]),
        pltpu.make_async_copy(tokens.at[at], x_ref, sems.at[1]),
    ]
    for copy in copies:
        copy.start()
    size = 256 if own % 256 == 0 else own
    copies[0].wait()
    for n in range(own // size):
        part = slice(n * size, (n + 1) * size)
        cot_t[:, part] = cot_ref[part].T
    copies[1].wait()


def first_norm_kernel(x_ref, xhat_ref, inv_ref, xhat_t):
    own, width = x_ref.shape
    ones = jnp.full((width, width), 1.0 / width, BF16)
    size = 256 if own % 256 == 0 else own
    for n in range(own // size):
        part = slice(n * size, (n + 1) * size)
        x = x_ref[part]
        center = x.astype(F32) - dot(x, ones, NN)
        inv = lax.rsqrt(dot((center * center).astype(BF16), ones, NN) + 1e-05)
        xhat = center * inv
        xhat_ref[part] = xhat
        inv_ref[part] = inv[:, :1]
        xhat_t[:width, part] = xhat.astype(BF16).T
        xhat_t[width:, part] = jnp.ones((16, size), BF16)


def attend_kernel(
    per, me, virt, lens, live, x_ref, xhat_ref, held, got,
    qkv_ref, prob_ref, o_ref, x1_ref, wqkv, wout, vec,
):
    tokens, width = x_ref.shape
    rows = tokens // WIN
    hs = width // HEADS
    here = twist(virt[0] // 4)
    y_own = (virt[0] // 2) % 2
    first = virt[0] % 2 == 0
    for m in range(CHIPS):
        k = spot(m) ^ (here + y_own * VDP)
        at = pl.ds(pl.multiple_of(k * 32, 32), 32)
        a = held[at].astype(F32)
        b = got[at].astype(F32)
        even = jnp.where(first, a, b)
        odd = jnp.where(first, b, a)
        for part in range(3):
            both = jnp.concatenate([even[part * 8 : part * 8 + 8], odd[part * 8 : part * 8 + 8]], 0)
            wqkv[m * 16 : m * 16 + 16, part * width : (part + 1) * width] = both.astype(BF16)
        both = jnp.concatenate([even[24:32], odd[24:32]], 0)
        wout[m * 16 : m * 16 + 16] = both.astype(BF16)
    total = held[CHIPS * 32 :].astype(F32) + got[CHIPS * 32 :].astype(F32)
    vec[...] = total
    scale = hs**-0.5
    ii = lax.broadcasted_iota(jnp.int32, (WIN, hs), 0)
    jj = lax.broadcasted_iota(jnp.int32, (WIN, hs), 1)
    same = ii == jj
    image_rows = live.shape[1]
    base = lax.rem(me[0], 2) * rows

    def enter(c):
        part = slice(c * per * WIN, (c + 1) * per * WIN)
        h1 = (xhat_ref[part] * total[0:1] + total[2:3]).astype(BF16)
        qkv = dot(h1, wqkv[...], NN).astype(BF16)
        qkv_ref[part] = qkv
        scores = []
        for r in range(per):
            at = slice(r * WIN, (r + 1) * WIN)
            scores.append(dot(qkv[at, :width], apart(qkv[at, width : 2 * width], hs), NT))
        return qkv, scores

    ahead = enter(0)
    for c in range(rows // per):
        qkv, scores = ahead
        if c + 1 < rows // per:
            ahead = enter(c + 1)
        part = slice(c * per * WIN, (c + 1) * per * WIN)
        probs = []
        for r in range(per):
            row = base + c * per + r
            image = row // image_rows
            inside = row - image * image_rows
            reach = jnp.where(live[image, inside] == 1, lens[image] - inside * WIN, 0)
            allowed = same | (jj < jnp.minimum(ii, reach))
            heads = []
            for h in range(HEADS):
                s = jnp.where(allowed, scores[r][:, h * hs : (h + 1) * hs], -1e30)
                e = jnp.exp((s - jnp.max(s, -1, keepdims=True)) * scale)
                heads.append((e * (1.0 / jnp.sum(e, -1, keepdims=True))).astype(BF16))
            probs.append(jnp.concatenate(heads, 1))
        mixed = []
        for r in range(per):
            at = slice(r * WIN, (r + 1) * WIN)
            mixed.append(dot(probs[r], apart(qkv[at, 2 * width :], hs), NN).astype(BF16))
        o = jnp.concatenate(mixed, 0)
        for n, p in enumerate(probs):
            prob_ref[c * per + n] = p
        o_ref[part] = o
        x1_ref[part] = x_ref[part].astype(F32) + dot(o, wout[...], NN)


def join(virt, blocks, n, up, down_t):
    tall = blocks.shape[1] // 2
    width = up.shape[0]
    here = twist(virt[0] // 4)
    for i in range(VDP):
        k = twist(i) ^ here
        at = slice(i * tall, (i + 1) * tall)
        cols = slice(n * width, (n + 1) * width)
        up[at, cols] = blocks[k, :tall]
        down_t[at, cols] = blocks[k, tall:]


def hidden_units(h2, dyb, up, down_t):
    u = dot(h2, up[...], NN).astype(BF16)
    da = dot(dyb, down_t[...], NN).astype(BF16)
    a, slope = gelu_both(u)
    return a, da * slope


def hidden_near_kernel(
    per, virt, x1_ref, cot_ref, cot_t, vec, own, got,
    h2_ref, xhat_ref, inv_ref, f_ref, dh2_ref, keep, send,
    a_ref, du_ref, h2_t, up, down_t, up_t, down,
):
    tokens, width = x1_ref.shape
    size = per * WIN
    join(virt, own, 0, up, down_t)
    join(virt, got, 1, up, down_t)
    up_t[...] = up[...].T
    down[...] = down_t[...].T
    for c in range(tokens // size):
        part = slice(c * size, (c + 1) * size)
        x1 = x1_ref[part]
        xhat, inv = norm_parts(x1)
        xhat_ref[part] = xhat
        inv_ref[part] = inv
        h2 = (xhat * vec[1:2] + vec[3:4]).astype(BF16)
        h2_ref[part] = h2
        h2_t[:, part] = h2.T
        a, du = hidden_units(h2, cot_ref[part], up, down_t)
        a_ref[part] = a
        du_ref[part] = du
        f_ref[part] = x1 + vec[4:5] + dot(a, down[...], NN)
        dh2_ref[part] = dot(du, up_t[...], NN)
    gdown = dot(cot_t[...], a_ref[...], NN)
    gup = dot(h2_t[...], du_ref[...], NN)
    tall = width // VDP
    here = turn(virt[0] // 4)
    for i in range(VDP):
        at = slice(i * tall, (i + 1) * tall)
        k = turn(i) ^ here
        keep[k, :tall] = gup[at, :width]
        keep[k, tall:] = gdown[at, :width]
        send[k, :tall] = gup[at, width:].astype(BF16)
        send[k, tall:] = gdown[at, width:].astype(BF16)


def hidden_far_kernel(
    per, virt, cot_ref, vec, own, got, h2_ref, xhat_ref, inv_ref, f_ref, dh2_ref, o_ref,
    y_ref, dx1_ref, g_ref, gout, gvec,
    o_t, up, down_t, up_t, down,
):
    tokens, width = h2_ref.shape
    size = per * WIN
    join(virt, own, 0, up, down_t)
    join(virt, got, 1, up, down_t)
    up_t[...] = up[...].T
    down[...] = down_t[...].T
    sums = [jnp.zeros((1, width), F32)] * 3
    for c in range(tokens // size):
        part = slice(c * size, (c + 1) * size)
        o_t[:, part] = o_ref[part].T
        a, du = hidden_units(h2_ref[part], cot_ref[part], up, down_t)
        y_ref[part] = (f_ref[part] + dot(a, down[...], NN)).astype(BF16)
        dh2 = dh2_ref[part] + dot(du, up_t[...], NN)
        dy = cot_ref[part].astype(F32)
        xhat = xhat_ref[part]
        dx1 = dy + norm_back(dh2, xhat, inv_ref[part], vec[1:2])
        dx1_ref[part] = dx1
        g_ref[part] = dx1.astype(BF16)
        for n, term in enumerate((dh2 * xhat, dh2, dy)):
            sums[n] = sums[n] + jnp.sum(term, 0, keepdims=True)
    gout[...] = dot(o_t[...], g_ref[...], NN)
    zero = jnp.zeros((1, width), F32)
    gvec[...] = jnp.concatenate([zero, sums[0], zero, sums[1], sums[2], zero, zero, zero], 0)


def own_rows(virt, i, other):
    core = virt[0] % 2
    core = 1 - core if other else core
    return pl.ds(pl.multiple_of(i * 32 + ((virt[0] // 2) % 2) * 16 + core * 8, 8), 8)


def back_kernel(
    per, virt, qkv_ref, prob_ref, g_ref, xhat_t, wqkv, wout, vec, gout, gvec,
    dqkv, keep, send, vec_sums,
    gqkv,
):
    tokens, width = g_ref.shape
    hs = width // HEADS
    scale = hs**-0.5
    every = [(r, h) for r in range(tokens // WIN) for h in range(HEADS)]
    groups = [every[n : n + 2 * per] for n in range(0, len(every), 2 * per)]

    def piece(ref, r, h, part=0):
        return ref[r * WIN : (r + 1) * WIN, part * width + h * hs : part * width + (h + 1) * hs]

    def enter(pairs):
        r = pairs[0][0]
        do = dot(g_ref[r * WIN : (r + per) * WIN], wout[...], NT).astype(BF16)
        dos = [do[(n - r) * WIN : (n - r + 1) * WIN, h * hs : (h + 1) * hs] for n, h in pairs]
        probs = [prob_ref[r, :, h * hs : h * hs + WIN] for r, h in pairs]
        dps = [dot(a, piece(qkv_ref, r, h, 2), NT) for a, (r, h) in zip(dos, pairs)]
        dvs = [dot(p, a, TN).astype(BF16) for p, a in zip(probs, dos)]
        return probs, dps, dvs

    ahead = enter(groups[0])
    for place, pairs in enumerate(groups):
        probs, dps, dvs = ahead
        if place + 1 < len(groups):
            ahead = enter(groups[place + 1])
        dss = []
        for p, dp in zip(probs, dps):
            pf = p.astype(F32)
            ds = pf * (dp - jnp.sum(dp * pf, -1, keepdims=True)) * scale
            dss.append(ds.astype(BF16))
        dqs = [dot(ds, piece(qkv_ref, r, h, 1), NN).astype(BF16) for ds, (r, h) in zip(dss, pairs)]
        dks = [dot(ds, piece(qkv_ref, r, h, 0), TN).astype(BF16) for ds, (r, h) in zip(dss, pairs)]
        for n, (r, h) in enumerate(pairs):
            for part, values in enumerate((dqs, dks, dvs)):
                at = slice(part * width + h * hs, part * width + (h + 1) * hs)
                dqkv[r * WIN : (r + 1) * WIN, at] = values[n]
    both = dot(xhat_t[...], dqkv[...], NN)
    grad, total = both[:width], both[width : width + 1]
    w = wqkv[...].astype(F32)
    cols = jnp.concatenate([
        jnp.broadcast_to(jnp.sum(w * grad, -1, keepdims=True), (width, 64)),
        jnp.broadcast_to(jnp.sum(w * total, -1, keepdims=True), (width, 64)),
    ], 1)
    lines = cols.T
    gain, from_total = lines[0:1], lines[64:65]
    vec_t = vec[...].T
    gqkv[...] = grad * vec_t[:, 0:1] + total * vec_t[:, 2:3]
    rest = gvec[...]
    sums = jnp.concatenate([gain, rest[1:2], from_total, rest[3:]], 0)
    here = twist(virt[0] // 4)
    for i in range(VDP):
        k = twist(i) ^ here
        mine, other = own_rows(virt, i, 0), own_rows(virt, i, 1)
        theirs = []
        for part in range(3):
            at = slice(part * width, (part + 1) * width)
            keep[k, part * 8 : part * 8 + 8] = gqkv[mine, at]
            theirs.append(gqkv[other, at])
        keep[k, 24:] = gout[mine]
        at = pl.ds(pl.multiple_of(k * 32, 32), 32)
        send[at] = jnp.concatenate(theirs + [gout[other]], 0).astype(BF16)
    vec_sums[...] = sums
    send[VDP * 32 :] = sums.astype(BF16)


def token_grad_kernel(per, me, dqkv, wqkv, vec, xhat_ref, inv_ref, dx1_ref, y, y_near, gx, gxb, out, turned, sems):
    own = dqkv.shape[0]
    size = per * WIN
    copies = []
    for n, source in enumerate((y, y_near)):
        at = pl.ds((lax.rem(me[0], 2) ^ n) * own, own)
        copies.append(pltpu.make_async_copy(source, out.at[at], sems.at[n]))
        copies[-1].start()
    turned[...] = wqkv[...].T
    for c in range(own // size):
        part = slice(c * size, (c + 1) * size)
        dh1 = dot(dqkv[part], turned[...], NN)
        values = dx1_ref[part] + norm_back(dh1, xhat_ref[part], inv_ref[part], vec[0:1])
        gx[part] = values
        gxb[part] = values.astype(BF16)
    for copy in copies:
        copy.wait()


def place_kernel(per, me, mine, theirs, out, wide, sems):
    own = theirs.shape[0]
    size = per * WIN
    here = lax.rem(me[0], 2) * own
    copies = [pltpu.make_async_copy(mine, out.at[pl.ds(here, own)], sems.at[own // size])]
    copies[0].start()
    for c in range(own // size):
        part = pl.ds(c * size, size)
        wide[part] = theirs[part].astype(F32)
        at = pl.ds(own - here + c * size, size)
        copies.append(pltpu.make_async_copy(wide.at[part], out.at[at], sems.at[c]))
        copies[-1].start()
    for copy in copies:
        copy.wait()


def finish_kernel(me, keep_a, keep_b, sums, *refs):
    qkv, out, gains, biases, up, down = refs[3:]
    small, width = out.shape
    tall = up.shape[0]
    high = 4 * small + 8
    total, vec = keep_a[0], sums[...]
    for got in refs[:3]:
        total = total + got[: 4 * small].astype(F32)
        vec = vec + got[4 * small : high].astype(F32)
    units = keep_b[0] + refs[1][high:].astype(F32)
    for part in range(3):
        qkv[:, part * width : (part + 1) * width] = total[part * small : (part + 1) * small]
    out[...] = total[3 * small :]
    vec = pltpu.roll(vec, width - me[0] * small, 1)[:, :small]
    gains[...] = vec[:2]
    biases[...] = vec[2:5]
    up[...] = units[:tall]
    down[...] = units[tall:]


def swap(block, axis, bit):
    size = lax.axis_size(axis)
    return lax.ppermute(block, axis, [(i, i ^ bit) for i in range(size)])


def steps_of(axis):
    return [(axis, 1 << k) for k in reversed(range(lax.axis_size(axis).bit_length() - 1))]


def after(value, other):
    return lax.optimization_barrier((value, other))[0]


def merge(pieces):
    vec = sum(piece[-8:] for piece in pieces)
    return jnp.concatenate([piece[:-8] for piece in pieces] + [vec], 0)


def halves(held):
    half = held.shape[0] // 2
    return held[:half], held[half:].astype(BF16)


def fold_step(keep, send, axis, bit, past=None):
    got = swap(send, axis, bit)
    return keep + (got if past is None else after(got, past)).astype(F32)


def bit_reverse(index, count):
    out = 0 * index
    for k in range(count):
        out = out | (((index >> k) & 1) << (count - 1 - k))
    return out


def by_device(block, me):
    blocks = block[None]
    for axis, bit in steps_of("dp") + steps_of("tensor"):
        blocks = jnp.concatenate([blocks, swap(blocks, axis, bit)], 0)
    count = blocks.shape[0]
    order = jnp.arange(count, dtype=jnp.int32) ^ me
    return jnp.take(blocks, bit_reverse(order, count.bit_length() - 1), axis=0)


def other_pack(w_qkv, w_out, gains, biases, w_up, w_down, me):
    small, width = w_out.shape
    qkv = w_qkv.reshape(small, 3, width).transpose(1, 0, 2).reshape(3 * small, width)
    rows = jnp.concatenate([gains, biases], 0)
    place = jnp.zeros((8, width), BF16)
    place = lax.dynamic_update_slice(place, rows, (jnp.int32(0), me * small))
    return jnp.concatenate([qkv, w_out, place], 0), jnp.concatenate([w_up, w_down.T], 0)


def other_blocks(a, b, me, n_dp, n_t):
    a = by_device(a, me)
    b = by_device(b, me)
    width = a.shape[2]
    count = n_dp * n_t
    small = width // count
    big = width // (VDP * VT)
    mats = a[:, : 4 * small].reshape(count, 4, small, width).transpose(1, 0, 2, 3)
    mats = mats.reshape(4, VDP * VT, big, width).transpose(1, 0, 2, 3).reshape(VDP * VT, 4 * big, width)
    vec = jnp.sum(a[:, 4 * small :].astype(F32), 0).astype(BF16)
    a = mats
    tall = width // n_dp
    b = b.reshape(n_dp, VT, 2, tall, width).transpose(1, 2, 0, 3, 4)
    b = b.reshape(VT, 2, VDP, width // VDP, width).transpose(2, 0, 1, 3, 4)
    b = b.reshape(VDP * VT, 2 * (width // VDP), width)

    y_own = (me // 2) % 2

    def placed(blocks):
        pairs = blocks.reshape((CHIPS, 2) + blocks.shape[1:])
        chips = sorted(range(CHIPS), key=spot)
        pairs = jnp.stack([pairs[m] for m in chips], 0)
        pairs = jnp.where(y_own == 1, jnp.roll(pairs, VDP, 0), pairs)
        return pairs[:, 0], pairs[:, 1]

    held_a, got_a = (part.reshape(-1, width) for part in placed(a))
    held_a = jnp.concatenate([held_a, vec], 0)
    got_a = jnp.concatenate([got_a, jnp.zeros_like(vec)], 0)
    return (held_a, got_a) + placed(b)


def other_reduce(pair_a, pair_b, sums, me, n_dp, n_t):
    count = n_dp * n_t
    y_own = (me // 2) % 2

    def whole(keep, send, order):
        pairs = jnp.stack([keep, send.astype(F32)], 1)
        pairs = jnp.stack([pairs[order(i)] for i in range(VDP)], 0)
        none = jnp.zeros_like(pairs)
        both = jnp.stack([jnp.where(y_own == y, pairs, none) for y in range(2)], 1)
        return both.reshape((VDP * VT,) + keep.shape[1:])

    def rows_of(blocks, parts):
        big = blocks.shape[1] // parts
        mats = blocks.reshape(VDP * VT, parts, big, -1).transpose(1, 0, 2, 3)
        mats = mats.reshape(parts, count, VDP * VT * big // count, -1).transpose(1, 0, 2, 3)
        return mats.reshape(count, -1, blocks.shape[2])

    a, b = whole(*pair_a, twist), whole(*pair_b, turn)
    width = a.shape[2]
    tall, high = width // n_dp, width // VDP
    cols = b.reshape(VDP, VT, 2, high, width).transpose(1, 2, 0, 3, 4)
    cols = cols.reshape(VT, 2, n_dp, tall, width).transpose(2, 0, 1, 3, 4)
    cols = cols.reshape(count, 2 * tall, width)
    vec = jnp.broadcast_to(jnp.where(y_own == 0, sums, 0.0)[None], (count,) + sums.shape)
    a = jnp.concatenate([rows_of(a, 4), vec], 1)
    results = []
    for blocks in (a, cols):
        blocks = jnp.take(blocks, jnp.arange(count, dtype=jnp.int32) ^ me, axis=0)
        for axis, bit in reversed(steps_of("dp") + steps_of("tensor")):
            pairs = blocks.reshape((-1, 2) + blocks.shape[1:])
            got = swap(pairs[:, 1].astype(BF16), axis, bit)
            blocks = pairs[:, 0] + got.astype(F32)
        results.append(blocks[0])
    return results


def struct(shape, dtype):
    return jax.ShapeDtypeStruct(shape, dtype)


def call(kernel, name, args, outs, scratch=(), flops=0, limit=8, hbm_outs=True):
    args = [a if isinstance(a, tuple) else (a, pltpu.VMEM) for a in args]
    moved = sum(a.size * a.dtype.itemsize for a, _ in args)
    spaces = [pl.ANY if hbm_outs and isinstance(o, jax.ShapeDtypeStruct) else pltpu.VMEM for o in outs]
    return pl.pallas_call(
        kernel,
        name=name,
        out_shape=outs,
        in_specs=[pl.BlockSpec(memory_space=space) for _, space in args],
        out_specs=[pl.BlockSpec(memory_space=space) for space in spaces],
        scratch_shapes=list(scratch),
        compiler_params=pltpu.CompilerParams(vmem_limit_bytes=limit * MIB),
        cost_estimate=pl.CostEstimate(flops=flops, bytes_accessed=moved, transcendentals=0),
    )(*[a for a, _ in args])


def on_device(tokens, lengths, row_mask, cotangent, w_qkv, w_out, gains, biases, w_up, w_down):
    images, seq_len, width = tokens.shape
    n_dp, n_t = lax.axis_size("dp"), lax.axis_size("tensor")
    index = lax.axis_index("dp") * n_t + lax.axis_index("tensor")
    me = index.astype(jnp.int32).reshape(1)
    usual = (n_dp, n_t) == (VDP, VT)
    virt = me if usual else (index // 2 % 2 * 2).astype(jnp.int32).reshape(1)
    small = width // (n_dp * n_t)
    tall = width // n_dp
    own = images * seq_len // 2
    rows = own // WIN
    per = 12 if rows % 12 == 0 else 1
    some = 6 if rows % 6 == 0 else 1
    less = 4 if rows % 4 == 0 else 1
    smem = pltpu.SMEM
    weights = (w_qkv, w_out, gains, biases, w_up, w_down)
    token_mm = 2 * own * width
    hbm = pltpu.HBM

    def in_hbm(array):
        return (pltpu.with_memory_space_constraint(array, hbm), hbm)

    def first_norm(x):
        return call(
            first_norm_kernel,
            "first_norm",
            [x],
            [
                pltpu.VMEM((own, width), F32),
                pltpu.VMEM((own, 1), F32),
                pltpu.VMEM((width + 16, own), BF16),
            ],
            limit=4,
        )

    def fetch(me):
        flat = [array.reshape(images * seq_len, width) for array in (cotangent, tokens)]
        return call(
            turn_kernel,
            "turn",
            [(me, smem)] + [in_hbm(array) for array in flat],
            [
                pltpu.VMEM((own, width), BF16),
                pltpu.VMEM((width, own), BF16),
                pltpu.VMEM((own, width), BF16),
            ],
            [pltpu.SemaphoreType.DMA((2,))],
            limit=4,
        )

    if usual:
        weights = (w_qkv, w_out, gains, biases, w_up, w_down.T)
        high = 4 * small + 8
        packed = call(
            pack_kernel,
            "pack",
            [(me, smem)] + [in_hbm(w) for w in weights],
            [pltpu.VMEM((1, high + 2 * tall, width), BF16)],
            [pltpu.VMEM(w.shape, BF16) for w in weights] + [pltpu.SemaphoreType.DMA((6,))],
        )[0]
        planes = [packed] + [swap(packed, "dp", bit) for bit in (2, 4, 6)]
        cot, cot_t, x = fetch(after(me, packed))
        planes[3] = after(planes[3], cot)
        held_a = merge([plane[0, :high] for plane in planes])
        b = jnp.concatenate([plane[:, high:] for plane in planes], 0)
        far_b = swap(b, "tensor", 2)
        held_a = merge([held_a, swap(held_a, "dp", 1)])
        b = jnp.concatenate([b, swap(b, "dp", 1)], 0)
        xhat1, inv1, xhat_t = first_norm(after(x, (held_a, far_b)))
        held_a = merge([held_a, after(swap(held_a, "tensor", 2), (b, xhat1))])
        far_x = swap(far_b, "dp", 1)
        got_a = swap(held_a, "tensor", 1)
        got_b = swap(b, "tensor", 1)
    else:
        held_a, got_a, held_b, got_b = other_blocks(*other_pack(*weights, index), index, n_dp, n_t)
        b, far_b = held_b[:VDP], held_b[VDP:]
        got_b, got_far = got_b[:VDP], got_b[VDP:]
        cot, cot_t, x = fetch(me)
        xhat1, inv1, xhat_t = first_norm(x)
    qkv, prob, o, x1, wqkv, wout, vec = call(
        functools.partial(attend_kernel, some),
        "attend",
        [(me, smem), (virt, smem), (lengths, smem), (row_mask, smem), x, xhat1, held_a, got_a],
        [
            pltpu.VMEM((own, 3 * width), BF16),
            pltpu.VMEM((rows, WIN, width), BF16),
            pltpu.VMEM((own, width), BF16),
            pltpu.VMEM((own, width), F32),
            pltpu.VMEM((width, 3 * width), BF16),
            pltpu.VMEM((width, width), BF16),
            pltpu.VMEM((8, width), F32),
        ],
        flops=token_mm * (4 * width + 2 * WIN),
    )
    tall_b = 2 * (width // VDP)
    mats = [pltpu.VMEM((width, 2 * width), BF16)] * 2 + [pltpu.VMEM((2 * width, width), BF16)] * 2
    if usual:
        far_b = jnp.concatenate([far_b, after(far_x, x1)], 0)
        got_far = swap(far_b, "tensor", 1)
        got_b = after(got_b, far_b)
    wide_per = 8 if rows % 8 == 0 else rows
    *first, keep_b, send_b = call(
        functools.partial(hidden_near_kernel, wide_per),
        "hidden_near",
        [(virt, smem), x1, cot, cot_t, vec, b, got_b],
        [
            pltpu.VMEM((own, width), BF16),
            pltpu.VMEM((own, width), F32),
            pltpu.VMEM((own, 1), F32),
            pltpu.VMEM((own, width), F32),
            pltpu.VMEM((own, width), F32),
            pltpu.VMEM((VDP, tall_b, width), F32),
            pltpu.VMEM((VDP, tall_b, width), BF16),
        ],
        [pltpu.VMEM((own, 2 * width), BF16)] * 2 + [pltpu.VMEM((width, own), BF16)] + mats,
        token_mm * 12 * width,
        12,
    )
    y, dx1, g, gout, gvec = call(
        functools.partial(hidden_far_kernel, wide_per),
        "hidden_far",
        [(virt, smem), cot, vec, far_b, got_far, *first, o],
        [
            pltpu.VMEM((own, width), BF16),
            pltpu.VMEM((own, width), F32),
            pltpu.VMEM((own, width), BF16),
            pltpu.VMEM((width, width), F32),
            pltpu.VMEM((8, width), F32),
        ],
        [pltpu.VMEM((width, own), BF16)] + mats,
        token_mm * 9 * width,
    )
    core, xbit, zlo = ("tensor", 1), ("dp", 1), ("dp", 2)
    if usual:
        held_b = fold_step(keep_b, send_b, *core, g)
        y = after(y, held_b)
    y_near = swap(y, "tensor", 1)
    dqkv, keep_a, send_a, sums = call(
        functools.partial(back_kernel, per),
        "back",
        [(virt, smem), qkv, prob, g, xhat_t, wqkv, wout, vec, gout, gvec],
        [
            pltpu.VMEM((own, 3 * width), BF16),
            pltpu.VMEM((VDP, 32, width), F32),
            pltpu.VMEM((VDP * 32 + 8, width), BF16),
            pltpu.VMEM((8, width), F32),
        ],
        [pltpu.VMEM((width, 3 * width), F32)],
        token_mm * (4 * width + 5 * WIN),
    )
    if usual:
        held_b = fold_step(*halves(held_b), *xbit)
        got = after(swap(send_a, *core), held_b).astype(F32)
        held_a = keep_a + got[:-8].reshape(keep_a.shape)
        sums = sums + got[-8:]
        vec = after(vec, held_a)
    gx, gxb, layer_out = call(
        functools.partial(token_grad_kernel, less),
        "token_grad",
        [(me, smem), dqkv, wqkv, vec, xhat1, inv1, dx1, y, y_near],
        [
            pltpu.VMEM((own, width), F32),
            pltpu.VMEM((own, width), BF16),
            struct((images * seq_len, width), BF16),
        ],
        [pltpu.VMEM((3 * width, width), BF16), pltpu.SemaphoreType.DMA((2,))],
        flops=token_mm * 3 * width,
    )
    layer_out = layer_out.reshape(images, seq_len, width)

    def place(gx_near):
        return call(
            functools.partial(place_kernel, less),
            "place",
            [(me, smem), gx, gx_near],
            [struct((images * seq_len, width), F32)],
            [pltpu.VMEM((own, width), F32), pltpu.SemaphoreType.DMA((rows // less + 1,))],
        )[0].reshape(images, seq_len, width)

    if usual:
        held_b = fold_step(*halves(held_b), *zlo, gxb)
        send_a = jnp.concatenate([held_a[4:].reshape(-1, width), sums], 0).astype(BF16)
        got = after(swap(send_a, *xbit), (gxb, held_b)).astype(F32)
        held_a = held_a[:4] + got[:-8].reshape(4, -1, width)
        sums = sums + got[-8:]
        got = [
            swap(jnp.concatenate([held_a[n], sums] + more, 0).astype(BF16), "dp", 2 * n)
            for n, more in ((1, []), (2, [held_b[1]]), (3, []))
        ]
        grad_tokens = place(swap(after(gxb, held_a), "tensor", 1))
        got[2] = after(got[2], grad_tokens)
        shapes = ((small, 3 * width), (small, width), (2, small), (3, small), (tall, width), (tall, width))
        o_qkv, o_out, o_gains, o_bias, o_up, o_down = call(
            finish_kernel,
            "finish",
            [(me, smem), held_a, held_b, sums, *got],
            [struct(shape, F32) for shape in shapes],
            limit=2,
            hbm_outs=False,
        )
    else:
        grad_tokens = place(swap(gxb, "tensor", 1))
        send_a = send_a[:-8].reshape(keep_a.shape)
        grad_a, grad_b = other_reduce((keep_a, send_a), (keep_b, send_b), sums, index, n_dp, n_t)
        o_qkv = jnp.concatenate([grad_a[p * small : (p + 1) * small] for p in range(3)], 1)
        o_out = grad_a[3 * small : 4 * small]
        o_vec = lax.dynamic_slice_in_dim(grad_a[4 * small : 4 * small + 5], index * small, small, 1)
        o_gains, o_bias = o_vec[:2], o_vec[2:]
        o_up, o_down = grad_b[:tall], grad_b[tall:]
    return layer_out, grad_tokens, o_qkv, o_out, o_gains, o_bias, o_up, o_down.T


def solution(mesh):
    in_specs = (
        P("dp", None, None),
        P("dp"),
        P("dp", None),
        P("dp", None, None),
        P(("dp", "tensor"), None),
        P(("dp", "tensor"), None),
        P(None, ("dp", "tensor")),
        P(None, ("dp", "tensor")),
        P("dp", "tensor"),
        P("tensor", "dp"),
    )
    out_specs = (
        P("dp", None, None),
        P("dp", None, None),
        P(("dp", "tensor"), None),
        P(("dp", "tensor"), None),
        P(None, ("dp", "tensor")),
        P(None, ("dp", "tensor")),
        P("dp", "tensor"),
        P("tensor", "dp"),
    )
    return jax.shard_map(
        on_device, mesh=mesh, in_specs=in_specs, out_specs=out_specs, check_vma=False
    )
```

```python
import functools

import jax
import jax.numpy as jnp
from jax import lax
from jax.experimental import pallas as pl
from jax.experimental.pallas import tpu as pltpu
from jax.sharding import PartitionSpec as P

HEADS = 2
WIN = 96
F32 = jnp.float32
BF16 = jnp.bfloat16
VDP, VT = 8, 4
CHIPS = VDP * VT // 2
MIB = 1 << 20

NN = ((1,), (0,))
NT = ((1,), (1,))
TN = ((0,), (0,))


def dot(a, b, dims):
    return lax.dot_general(a, b, (dims, ((), ())), preferred_element_type=F32)


def twist(i):
    return (i & 1) * 4 + (i >> 1)


def turn(i):
    return ((i & 1) << 2) | (i & 2) | ((i & 4) >> 2)


def spot(m):
    return (m % 2) * VDP + twist(m // 2)


def norm_parts(values):
    center = values - jnp.mean(values, -1, keepdims=True)
    inv = lax.rsqrt(jnp.mean(center * center, -1, keepdims=True) + 1e-05)
    return center * inv, inv


def norm_back(grad, xhat, inv, gain):
    scaled = grad * gain
    return inv * (
        scaled
        - jnp.mean(scaled, -1, keepdims=True)
        - xhat * jnp.mean(scaled * xhat, -1, keepdims=True)
    )


def gelu_both(u):
    c = 0.7978845608028654
    u2 = u * u
    t = jnp.tanh(u * (c + (c * 0.044715) * u2))
    half = 0.5 + 0.5 * t
    value = u * half
    slope = half + (value - value * half) * (2 * c + (6 * c * 0.044715) * u2)
    return value, slope


def apart(both, hs):
    blocks = []
    for h in range(HEADS):
        parts = [jnp.zeros((WIN, hs), BF16)] * HEADS
        parts[h] = both[:, h * hs : (h + 1) * hs]
        blocks.append(jnp.concatenate(parts, 1))
        blocks.append(jnp.zeros((hs - WIN, HEADS * hs), BF16))
    return jnp.concatenate(blocks, 0)


def pack_kernel(me, *refs):
    sources, packed, held, sems = refs[:6], refs[6], refs[7:13], refs[13]
    copies = [pltpu.make_async_copy(a, b, sems.at[n]) for n, (a, b) in enumerate(zip(sources, held))]
    for copy in copies:
        copy.start()
    qkv, out, gains, biases, up, down = held
    small, width = out.shape
    tall = up.shape[0]
    lane = lax.broadcasted_iota(jnp.int32, (1, width), 1)
    mine = lane // small == me[0]
    for copy in copies:
        copy.wait()
    for part in range(3):
        packed[0, part * small : (part + 1) * small] = qkv[:, part * width : (part + 1) * width]
    packed[0, 3 * small : 4 * small] = out[...]
    rows = [gains[0:1], gains[1:2], biases[0:1], biases[1:2], biases[2:3]]
    vals = jnp.concatenate(rows + [jnp.zeros((3, small), BF16)], 0).astype(F32)
    wide = jnp.concatenate([vals] * (width // small), 1)
    at = 4 * small + 8
    packed[0, 4 * small : at] = jnp.where(mine, wide, 0.0).astype(BF16)
    packed[0, at : at + tall] = up[...]
    packed[0, at + tall :] = down[...]


def turn_kernel(me, cot, tokens, cot_ref, cot_t, x_ref, sems):
    own = cot_ref.shape[0]
    at = pl.ds(lax.rem(me[0], 2) * own, own)
    copies = [
        pltpu.make_async_copy(cot.at[at], cot_ref, sems.at[0]),
        pltpu.make_async_copy(tokens.at[at], x_ref, sems.at[1]),
    ]
    for copy in copies:
        copy.start()
    size = 256 if own % 256 == 0 else own
    copies[0].wait()
    for n in range(own // size):
        part = slice(n * size, (n + 1) * size)
        cot_t[:, part] = cot_ref[part].T
    copies[1].wait()


def first_norm_kernel(x_ref, xhat_ref, inv_ref, xhat_t):
    own, width = x_ref.shape
    ones = jnp.full((width, width), 1.0 / width, BF16)
    size = 256 if own % 256 == 0 else own
    for n in range(own // size):
        part = slice(n * size, (n + 1) * size)
        x = x_ref[part]
        center = x.astype(F32) - dot(x, ones, NN)
        inv = lax.rsqrt(dot((center * center).astype(BF16), ones, NN) + 1e-05)
        xhat = center * inv
        xhat_ref[part] = xhat
        inv_ref[part] = inv[:, :1]
        xhat_t[:width, part] = xhat.astype(BF16).T
        xhat_t[width:, part] = jnp.ones((16, size), BF16)


def attend_kernel(
    per, me, virt, lens, live, x_ref, xhat_ref, held, got,
    qkv_ref, prob_ref, o_ref, x1_ref, wqkv, wout, vec,
):
    tokens, width = x_ref.shape
    rows = tokens // WIN
    hs = width // HEADS
    here = twist(virt[0] // 4)
    y_own = (virt[0] // 2) % 2
    first = virt[0] % 2 == 0
    for m in range(CHIPS):
        k = spot(m) ^ (here + y_own * VDP)
        at = pl.ds(pl.multiple_of(k * 32, 32), 32)
        a = held[at].astype(F32)
        b = got[at].astype(F32)
        even = jnp.where(first, a, b)
        odd = jnp.where(first, b, a)
        for part in range(3):
            both = jnp.concatenate([even[part * 8 : part * 8 + 8], odd[part * 8 : part * 8 + 8]], 0)
            wqkv[m * 16 : m * 16 + 16, part * width : (part + 1) * width] = both.astype(BF16)
        both = jnp.concatenate([even[24:32], odd[24:32]], 0)
        wout[m * 16 : m * 16 + 16] = both.astype(BF16)
    total = held[CHIPS * 32 :].astype(F32) + got[CHIPS * 32 :].astype(F32)
    vec[...] = total
    scale = hs**-0.5
    ii = lax.broadcasted_iota(jnp.int32, (WIN, hs), 0)
    jj = lax.broadcasted_iota(jnp.int32, (WIN, hs), 1)
    same = ii == jj
    image_rows = live.shape[1]
    base = lax.rem(me[0], 2) * rows

    def enter(c):
        part = slice(c * per * WIN, (c + 1) * per * WIN)
        h1 = (xhat_ref[part] * total[0:1] + total[2:3]).astype(BF16)
        qkv = dot(h1, wqkv[...], NN).astype(BF16)
        qkv_ref[part] = qkv
        scores = []
        for r in range(per):
            at = slice(r * WIN, (r + 1) * WIN)
            scores.append(dot(qkv[at, :width], apart(qkv[at, width : 2 * width], hs), NT))
        return qkv, scores

    ahead = enter(0)
    for c in range(rows // per):
        qkv, scores = ahead
        if c + 1 < rows // per:
            ahead = enter(c + 1)
        part = slice(c * per * WIN, (c + 1) * per * WIN)
        probs = []
        for r in range(per):
            row = base + c * per + r
            image = row // image_rows
            inside = row - image * image_rows
            reach = jnp.where(live[image, inside] == 1, lens[image] - inside * WIN, 0)
            allowed = same | (jj < jnp.minimum(ii, reach))
            heads = []
            for h in range(HEADS):
                s = jnp.where(allowed, scores[r][:, h * hs : (h + 1) * hs], -1e30)
                e = jnp.exp((s - jnp.max(s, -1, keepdims=True)) * scale)
                heads.append((e * (1.0 / jnp.sum(e, -1, keepdims=True))).astype(BF16))
            probs.append(jnp.concatenate(heads, 1))
        mixed = []
        for r in range(per):
            at = slice(r * WIN, (r + 1) * WIN)
            mixed.append(dot(probs[r], apart(qkv[at, 2 * width :], hs), NN).astype(BF16))
        o = jnp.concatenate(mixed, 0)
        for n, p in enumerate(probs):
            prob_ref[c * per + n] = p
        o_ref[part] = o
        x1_ref[part] = x_ref[part].astype(F32) + dot(o, wout[...], NN)


def join(virt, blocks, n, up, down_t):
    tall = blocks.shape[1] // 2
    width = up.shape[0]
    here = twist(virt[0] // 4)
    for i in range(VDP):
        k = twist(i) ^ here
        at = slice(i * tall, (i + 1) * tall)
        cols = slice(n * width, (n + 1) * width)
        up[at, cols] = blocks[k, :tall]
        down_t[at, cols] = blocks[k, tall:]


def hidden_units(h2, dyb, up, down_t):
    u = dot(h2, up[...], NN).astype(BF16)
    da = dot(dyb, down_t[...], NN).astype(BF16)
    a, slope = gelu_both(u)
    return a, da * slope


def hidden_near_kernel(
    per, virt, x1_ref, cot_ref, cot_t, vec, own, got,
    h2_ref, xhat_ref, inv_ref, f_ref, dh2_ref, keep, send,
    a_ref, du_ref, h2_t, up, down_t, up_t, down,
):
    tokens, width = x1_ref.shape
    size = per * WIN
    join(virt, own, 0, up, down_t)
    join(virt, got, 1, up, down_t)
    up_t[...] = up[...].T
    down[...] = down_t[...].T
    for c in range(tokens // size):
        part = slice(c * size, (c + 1) * size)
        x1 = x1_ref[part]
        xhat, inv = norm_parts(x1)
        xhat_ref[part] = xhat
        inv_ref[part] = inv
        h2 = (xhat * vec[1:2] + vec[3:4]).astype(BF16)
        h2_ref[part] = h2
        h2_t[:, part] = h2.T
        a, du = hidden_units(h2, cot_ref[part], up, down_t)
        a_ref[part] = a
        du_ref[part] = du
        f_ref[part] = x1 + vec[4:5] + dot(a, down[...], NN)
        dh2_ref[part] = dot(du, up_t[...], NN)
    gdown = dot(cot_t[...], a_ref[...], NN)
    gup = dot(h2_t[...], du_ref[...], NN)
    tall = width // VDP
    here = turn(virt[0] // 4)
    for i in range(VDP):
        at = slice(i * tall, (i + 1) * tall)
        k = turn(i) ^ here
        keep[k, :tall] = gup[at, :width]
        keep[k, tall:] = gdown[at, :width]
        send[k, :tall] = gup[at, width:].astype(BF16)
        send[k, tall:] = gdown[at, width:].astype(BF16)


def hidden_far_kernel(
    per, virt, cot_ref, vec, own, got, h2_ref, xhat_ref, inv_ref, f_ref, dh2_ref, o_ref,
    y_ref, dx1_ref, g_ref, gout, gvec,
    o_t, up, down_t, up_t, down,
):
    tokens, width = h2_ref.shape
    size = per * WIN
    join(virt, own, 0, up, down_t)
    join(virt, got, 1, up, down_t)
    up_t[...] = up[...].T
    down[...] = down_t[...].T
    sums = [jnp.zeros((1, width), F32)] * 3
    for c in range(tokens // size):
        part = slice(c * size, (c + 1) * size)
        o_t[:, part] = o_ref[part].T
        a, du = hidden_units(h2_ref[part], cot_ref[part], up, down_t)
        y_ref[part] = (f_ref[part] + dot(a, down[...], NN)).astype(BF16)
        dh2 = dh2_ref[part] + dot(du, up_t[...], NN)
        dy = cot_ref[part].astype(F32)
        xhat = xhat_ref[part]
        dx1 = dy + norm_back(dh2, xhat, inv_ref[part], vec[1:2])
        dx1_ref[part] = dx1
        g_ref[part] = dx1.astype(BF16)
        for n, term in enumerate((dh2 * xhat, dh2, dy)):
            sums[n] = sums[n] + jnp.sum(term, 0, keepdims=True)
    gout[...] = dot(o_t[...], g_ref[...], NN)
    zero = jnp.zeros((1, width), F32)
    gvec[...] = jnp.concatenate([zero, sums[0], zero, sums[1], sums[2], zero, zero, zero], 0)


def own_rows(virt, i, other):
    core = virt[0] % 2
    core = 1 - core if other else core
    return pl.ds(pl.multiple_of(i * 32 + ((virt[0] // 2) % 2) * 16 + core * 8, 8), 8)


def back_kernel(
    per, virt, qkv_ref, prob_ref, g_ref, xhat_t, wqkv, wout, vec, gout, gvec,
    dqkv, keep, send, vec_sums,
    gqkv,
):
    tokens, width = g_ref.shape
    hs = width // HEADS
    scale = hs**-0.5
    every = [(r, h) for r in range(tokens // WIN) for h in range(HEADS)]
    groups = [every[n : n + 2 * per] for n in range(0, len(every), 2 * per)]

    def piece(ref, r, h, part=0):
        return ref[r * WIN : (r + 1) * WIN, part * width + h * hs : part * width + (h + 1) * hs]

    def enter(pairs):
        r = pairs[0][0]
        do = dot(g_ref[r * WIN : (r + per) * WIN], wout[...], NT).astype(BF16)
        dos = [do[(n - r) * WIN : (n - r + 1) * WIN, h * hs : (h + 1) * hs] for n, h in pairs]
        probs = [prob_ref[r, :, h * hs : h * hs + WIN] for r, h in pairs]
        dps = [dot(a, piece(qkv_ref, r, h, 2), NT) for a, (r, h) in zip(dos, pairs)]
        dvs = [dot(p, a, TN).astype(BF16) for p, a in zip(probs, dos)]
        return probs, dps, dvs

    ahead = enter(groups[0])
    for place, pairs in enumerate(groups):
        probs, dps, dvs = ahead
        if place + 1 < len(groups):
            ahead = enter(groups[place + 1])
        dss = []
        for p, dp in zip(probs, dps):
            pf = p.astype(F32)
            ds = pf * (dp - jnp.sum(dp * pf, -1, keepdims=True)) * scale
            dss.append(ds.astype(BF16))
        dqs = [dot(ds, piece(qkv_ref, r, h, 1), NN).astype(BF16) for ds, (r, h) in zip(dss, pairs)]
        dks = [dot(ds, piece(qkv_ref, r, h, 0), TN).astype(BF16) for ds, (r, h) in zip(dss, pairs)]
        for n, (r, h) in enumerate(pairs):
            for part, values in enumerate((dqs, dks, dvs)):
                at = slice(part * width + h * hs, part * width + (h + 1) * hs)
                dqkv[r * WIN : (r + 1) * WIN, at] = values[n]
    both = dot(xhat_t[...], dqkv[...], NN)
    grad, total = both[:width], both[width : width + 1]
    w = wqkv[...].astype(F32)
    cols = jnp.concatenate([
        jnp.broadcast_to(jnp.sum(w * grad, -1, keepdims=True), (width, 64)),
        jnp.broadcast_to(jnp.sum(w * total, -1, keepdims=True), (width, 64)),
    ], 1)
    lines = cols.T
    gain, from_total = lines[0:1], lines[64:65]
    vec_t = vec[...].T
    gqkv[...] = grad * vec_t[:, 0:1] + total * vec_t[:, 2:3]
    rest = gvec[...]
    sums = jnp.concatenate([gain, rest[1:2], from_total, rest[3:]], 0)
    here = twist(virt[0] // 4)
    for i in range(VDP):
        k = twist(i) ^ here
        mine, other = own_rows(virt, i, 0), own_rows(virt, i, 1)
        theirs = []
        for part in range(3):
            at = slice(part * width, (part + 1) * width)
            keep[k, part * 8 : part * 8 + 8] = gqkv[mine, at]
            theirs.append(gqkv[other, at])
        keep[k, 24:] = gout[mine]
        at = pl.ds(pl.multiple_of(k * 32, 32), 32)
        send[at] = jnp.concatenate(theirs + [gout[other]], 0).astype(BF16)
    vec_sums[...] = sums
    send[VDP * 32 :] = sums.astype(BF16)


def token_grad_kernel(per, me, dqkv, wqkv, vec, xhat_ref, inv_ref, dx1_ref, y, y_near, gx, gxb, out, turned, sems):
    own = dqkv.shape[0]
    size = per * WIN
    copies = []
    for n, source in enumerate((y, y_near)):
        at = pl.ds((lax.rem(me[0], 2) ^ n) * own, own)
        copies.append(pltpu.make_async_copy(source, out.at[at], sems.at[n]))
        copies[-1].start()
    turned[...] = wqkv[...].T
    for c in range(own // size):
        part = slice(c * size, (c + 1) * size)
        dh1 = dot(dqkv[part], turned[...], NN)
        values = dx1_ref[part] + norm_back(dh1, xhat_ref[part], inv_ref[part], vec[0:1])
        gx[part] = values
        gxb[part] = values.astype(BF16)
    for copy in copies:
        copy.wait()


def place_kernel(per, me, mine, theirs, out, wide, sems):
    own = theirs.shape[0]
    size = per * WIN
    here = lax.rem(me[0], 2) * own
    copies = [pltpu.make_async_copy(mine, out.at[pl.ds(here, own)], sems.at[own // size])]
    copies[0].start()
    for c in range(own // size):
        part = pl.ds(c * size, size)
        wide[part] = theirs[part].astype(F32)
        at = pl.ds(own - here + c * size, size)
        copies.append(pltpu.make_async_copy(wide.at[part], out.at[at], sems.at[c]))
        copies[-1].start()
    for copy in copies:
        copy.wait()


def finish_kernel(me, keep_a, keep_b, sums, *refs):
    qkv, out, gains, biases, up, down = refs[3:]
    small, width = out.shape
    tall = up.shape[0]
    high = 4 * small + 8
    total, vec = keep_a[0], sums[...]
    for got in refs[:3]:
        total = total + got[: 4 * small].astype(F32)
        vec = vec + got[4 * small : high].astype(F32)
    units = keep_b[0] + refs[1][high:].astype(F32)
    for part in range(3):
        qkv[:, part * width : (part + 1) * width] = total[part * small : (part + 1) * small]
    out[...] = total[3 * small :]
    vec = pltpu.roll(vec, width - me[0] * small, 1)[:, :small]
    gains[...] = vec[:2]
    biases[...] = vec[2:5]
    up[...] = units[:tall]
    down[...] = units[tall:]


def swap(block, axis, bit):
    size = lax.axis_size(axis)
    return lax.ppermute(block, axis, [(i, i ^ bit) for i in range(size)])


def swap_diagonal(block):
    n_t = lax.axis_size("tensor")
    count = lax.axis_size("dp") * n_t
    return lax.ppermute(block, ("dp", "tensor"), [(i, i ^ (n_t + 2)) for i in range(count)])


def steps_of(axis):
    return [(axis, 1 << k) for k in reversed(range(lax.axis_size(axis).bit_length() - 1))]


def after(value, other):
    return lax.optimization_barrier((value, other))[0]


def merge(pieces):
    vec = sum(piece[-8:] for piece in pieces)
    return jnp.concatenate([piece[:-8] for piece in pieces] + [vec], 0)


def halves(held):
    half = held.shape[0] // 2
    return held[:half], held[half:].astype(BF16)


def fold_step(keep, send, axis, bit, past=None):
    got = swap(send, axis, bit)
    return keep + (got if past is None else after(got, past)).astype(F32)


def bit_reverse(index, count):
    out = 0 * index
    for k in range(count):
        out = out | (((index >> k) & 1) << (count - 1 - k))
    return out


def by_device(block, me):
    blocks = block[None]
    for axis, bit in steps_of("dp") + steps_of("tensor"):
        blocks = jnp.concatenate([blocks, swap(blocks, axis, bit)], 0)
    count = blocks.shape[0]
    order = jnp.arange(count, dtype=jnp.int32) ^ me
    return jnp.take(blocks, bit_reverse(order, count.bit_length() - 1), axis=0)


def other_pack(w_qkv, w_out, gains, biases, w_up, w_down, me):
    small, width = w_out.shape
    qkv = w_qkv.reshape(small, 3, width).transpose(1, 0, 2).reshape(3 * small, width)
    rows = jnp.concatenate([gains, biases], 0)
    place = jnp.zeros((8, width), BF16)
    place = lax.dynamic_update_slice(place, rows, (jnp.int32(0), me * small))
    return jnp.concatenate([qkv, w_out, place], 0), jnp.concatenate([w_up, w_down.T], 0)


def other_blocks(a, b, me, n_dp, n_t):
    a = by_device(a, me)
    b = by_device(b, me)
    width = a.shape[2]
    count = n_dp * n_t
    small = width // count
    big = width // (VDP * VT)
    mats = a[:, : 4 * small].reshape(count, 4, small, width).transpose(1, 0, 2, 3)
    mats = mats.reshape(4, VDP * VT, big, width).transpose(1, 0, 2, 3).reshape(VDP * VT, 4 * big, width)
    vec = jnp.sum(a[:, 4 * small :].astype(F32), 0).astype(BF16)
    a = mats
    tall = width // n_dp
    b = b.reshape(n_dp, VT, 2, tall, width).transpose(1, 2, 0, 3, 4)
    b = b.reshape(VT, 2, VDP, width // VDP, width).transpose(2, 0, 1, 3, 4)
    b = b.reshape(VDP * VT, 2 * (width // VDP), width)

    y_own = (me // 2) % 2

    def placed(blocks):
        pairs = blocks.reshape((CHIPS, 2) + blocks.shape[1:])
        chips = sorted(range(CHIPS), key=spot)
        pairs = jnp.stack([pairs[m] for m in chips], 0)
        pairs = jnp.where(y_own == 1, jnp.roll(pairs, VDP, 0), pairs)
        return pairs[:, 0], pairs[:, 1]

    held_a, got_a = (part.reshape(-1, width) for part in placed(a))
    held_a = jnp.concatenate([held_a, vec], 0)
    got_a = jnp.concatenate([got_a, jnp.zeros_like(vec)], 0)
    return (held_a, got_a) + placed(b)


def other_reduce(pair_a, pair_b, sums, me, n_dp, n_t):
    count = n_dp * n_t
    y_own = (me // 2) % 2

    def whole(keep, send, order):
        pairs = jnp.stack([keep, send.astype(F32)], 1)
        pairs = jnp.stack([pairs[order(i)] for i in range(VDP)], 0)
        none = jnp.zeros_like(pairs)
        both = jnp.stack([jnp.where(y_own == y, pairs, none) for y in range(2)], 1)
        return both.reshape((VDP * VT,) + keep.shape[1:])

    def rows_of(blocks, parts):
        big = blocks.shape[1] // parts
        mats = blocks.reshape(VDP * VT, parts, big, -1).transpose(1, 0, 2, 3)
        mats = mats.reshape(parts, count, VDP * VT * big // count, -1).transpose(1, 0, 2, 3)
        return mats.reshape(count, -1, blocks.shape[2])

    a, b = whole(*pair_a, twist), whole(*pair_b, turn)
    width = a.shape[2]
    tall, high = width // n_dp, width // VDP
    cols = b.reshape(VDP, VT, 2, high, width).transpose(1, 2, 0, 3, 4)
    cols = cols.reshape(VT, 2, n_dp, tall, width).transpose(2, 0, 1, 3, 4)
    cols = cols.reshape(count, 2 * tall, width)
    vec = jnp.broadcast_to(jnp.where(y_own == 0, sums, 0.0)[None], (count,) + sums.shape)
    a = jnp.concatenate([rows_of(a, 4), vec], 1)
    results = []
    for blocks in (a, cols):
        blocks = jnp.take(blocks, jnp.arange(count, dtype=jnp.int32) ^ me, axis=0)
        for axis, bit in reversed(steps_of("dp") + steps_of("tensor")):
            pairs = blocks.reshape((-1, 2) + blocks.shape[1:])
            got = swap(pairs[:, 1].astype(BF16), axis, bit)
            blocks = pairs[:, 0] + got.astype(F32)
        results.append(blocks[0])
    return results


def struct(shape, dtype):
    return jax.ShapeDtypeStruct(shape, dtype)


def call(kernel, name, args, outs, scratch=(), flops=0, limit=8, hbm_outs=True):
    args = [a if isinstance(a, tuple) else (a, pltpu.VMEM) for a in args]
    moved = sum(a.size * a.dtype.itemsize for a, _ in args)
    spaces = [pl.ANY if hbm_outs and isinstance(o, jax.ShapeDtypeStruct) else pltpu.VMEM for o in outs]
    return pl.pallas_call(
        kernel,
        name=name,
        out_shape=outs,
        in_specs=[pl.BlockSpec(memory_space=space) for _, space in args],
        out_specs=[pl.BlockSpec(memory_space=space) for space in spaces],
        scratch_shapes=list(scratch),
        compiler_params=pltpu.CompilerParams(vmem_limit_bytes=limit * MIB),
        cost_estimate=pl.CostEstimate(flops=flops, bytes_accessed=moved, transcendentals=0),
    )(*[a for a, _ in args])


def on_device(tokens, lengths, row_mask, cotangent, w_qkv, w_out, gains, biases, w_up, w_down):
    images, seq_len, width = tokens.shape
    n_dp, n_t = lax.axis_size("dp"), lax.axis_size("tensor")
    index = lax.axis_index("dp") * n_t + lax.axis_index("tensor")
    me = index.astype(jnp.int32).reshape(1)
    usual = (n_dp, n_t) == (VDP, VT)
    virt = me if usual else (index // 2 % 2 * 2).astype(jnp.int32).reshape(1)
    small = width // (n_dp * n_t)
    tall = width // n_dp
    own = images * seq_len // 2
    rows = own // WIN
    per = 12 if rows % 12 == 0 else 1
    some = 6 if rows % 6 == 0 else 1
    less = 4 if rows % 4 == 0 else 1
    smem = pltpu.SMEM
    weights = (w_qkv, w_out, gains, biases, w_up, w_down)
    token_mm = 2 * own * width
    hbm = pltpu.HBM

    def in_hbm(array):
        return (pltpu.with_memory_space_constraint(array, hbm), hbm)

    def first_norm(x):
        return call(
            first_norm_kernel,
            "first_norm",
            [x],
            [
                pltpu.VMEM((own, width), F32),
                pltpu.VMEM((own, 1), F32),
                pltpu.VMEM((width + 16, own), BF16),
            ],
            limit=4,
        )

    def fetch(me):
        flat = [array.reshape(images * seq_len, width) for array in (cotangent, tokens)]
        return call(
            turn_kernel,
            "turn",
            [(me, smem)] + [in_hbm(array) for array in flat],
            [
                pltpu.VMEM((own, width), BF16),
                pltpu.VMEM((width, own), BF16),
                pltpu.VMEM((own, width), BF16),
            ],
            [pltpu.SemaphoreType.DMA((2,))],
            limit=4,
        )

    if usual:
        weights = (w_qkv, w_out, gains, biases, w_up, w_down.T)
        high = 4 * small + 8
        packed = call(
            pack_kernel,
            "pack",
            [(me, smem)] + [in_hbm(w) for w in weights],
            [pltpu.VMEM((1, high + 2 * tall, width), BF16)],
            [pltpu.VMEM(w.shape, BF16) for w in weights] + [pltpu.SemaphoreType.DMA((6,))],
        )[0]
        planes = [packed] + [swap(packed, "dp", bit) for bit in (2, 4, 6)]
        cot, cot_t, x = fetch(after(me, packed))
        planes[3] = after(planes[3], cot)
        held_a = merge([plane[0, :high] for plane in planes])
        b = jnp.concatenate([plane[:, high:] for plane in planes], 0)
        xhat1, inv1, xhat_t = first_norm(x)
        planes_a = held_a
        near = after(swap(b, "dp", 1), xhat1)
        sides = [swap(planes_a, "dp", 1), swap(planes_a, "tensor", 2), swap_diagonal(planes_a)]
        far_b, far_x = swap(b, "tensor", 2), swap_diagonal(b)
        b = jnp.concatenate([b, near], 0)
        held_a = merge([planes_a] + sides)
        got_a = swap(held_a, "tensor", 1)
        got_b = swap(b, "tensor", 1)
    else:
        held_a, got_a, held_b, got_b = other_blocks(*other_pack(*weights, index), index, n_dp, n_t)
        b, far_b = held_b[:VDP], held_b[VDP:]
        got_b, got_far = got_b[:VDP], got_b[VDP:]
        cot, cot_t, x = fetch(me)
        xhat1, inv1, xhat_t = first_norm(x)
    qkv, prob, o, x1, wqkv, wout, vec = call(
        functools.partial(attend_kernel, some),
        "attend",
        [(me, smem), (virt, smem), (lengths, smem), (row_mask, smem), x, xhat1, held_a, got_a],
        [
            pltpu.VMEM((own, 3 * width), BF16),
            pltpu.VMEM((rows, WIN, width), BF16),
            pltpu.VMEM((own, width), BF16),
            pltpu.VMEM((own, width), F32),
            pltpu.VMEM((width, 3 * width), BF16),
            pltpu.VMEM((width, width), BF16),
            pltpu.VMEM((8, width), F32),
        ],
        flops=token_mm * (4 * width + 2 * WIN),
    )
    tall_b = 2 * (width // VDP)
    mats = [pltpu.VMEM((width, 2 * width), BF16)] * 2 + [pltpu.VMEM((2 * width, width), BF16)] * 2
    if usual:
        far_b = jnp.concatenate([after(far_b, x1), after(far_x, x1)], 0)
        got_far = swap(far_b, "tensor", 1)
        got_b = after(got_b, far_b)
    wide_per = 8 if rows % 8 == 0 else rows
    *first, keep_b, send_b = call(
        functools.partial(hidden_near_kernel, wide_per),
        "hidden_near",
        [(virt, smem), x1, cot, cot_t, vec, b, got_b],
        [
            pltpu.VMEM((own, width), BF16),
            pltpu.VMEM((own, width), F32),
            pltpu.VMEM((own, 1), F32),
            pltpu.VMEM((own, width), F32),
            pltpu.VMEM((own, width), F32),
            pltpu.VMEM((VDP, tall_b, width), F32),
            pltpu.VMEM((VDP, tall_b, width), BF16),
        ],
        [pltpu.VMEM((own, 2 * width), BF16)] * 2 + [pltpu.VMEM((width, own), BF16)] + mats,
        token_mm * 12 * width,
        12,
    )
    y, dx1, g, gout, gvec = call(
        functools.partial(hidden_far_kernel, wide_per),
        "hidden_far",
        [(virt, smem), cot, vec, far_b, got_far, *first, o],
        [
            pltpu.VMEM((own, width), BF16),
            pltpu.VMEM((own, width), F32),
            pltpu.VMEM((own, width), BF16),
            pltpu.VMEM((width, width), F32),
            pltpu.VMEM((8, width), F32),
        ],
        [pltpu.VMEM((width, own), BF16)] + mats,
        token_mm * 9 * width,
    )
    core, xbit, zlo = ("tensor", 1), ("dp", 1), ("dp", 2)
    if usual:
        held_b = fold_step(keep_b, send_b, *core, g)
        y = after(y, held_b)
    y_near = swap(y, "tensor", 1)
    dqkv, keep_a, send_a, sums = call(
        functools.partial(back_kernel, per),
        "back",
        [(virt, smem), qkv, prob, g, xhat_t, wqkv, wout, vec, gout, gvec],
        [
            pltpu.VMEM((own, 3 * width), BF16),
            pltpu.VMEM((VDP, 32, width), F32),
            pltpu.VMEM((VDP * 32 + 8, width), BF16),
            pltpu.VMEM((8, width), F32),
        ],
        [pltpu.VMEM((width, 3 * width), F32)],
        token_mm * (4 * width + 5 * WIN),
    )
    if usual:
        held_b = fold_step(*halves(held_b), *xbit)
        got = after(swap(send_a, *core), held_b).astype(F32)
        held_a = keep_a + got[:-8].reshape(keep_a.shape)
        sums = sums + got[-8:]
        vec = after(vec, held_a)
    gx, gxb, layer_out = call(
        functools.partial(token_grad_kernel, less),
        "token_grad",
        [(me, smem), dqkv, wqkv, vec, xhat1, inv1, dx1, y, y_near],
        [
            pltpu.VMEM((own, width), F32),
            pltpu.VMEM((own, width), BF16),
            struct((images * seq_len, width), BF16),
        ],
        [pltpu.VMEM((3 * width, width), BF16), pltpu.SemaphoreType.DMA((2,))],
        flops=token_mm * 3 * width,
    )
    layer_out = layer_out.reshape(images, seq_len, width)

    def place(gx_near):
        return call(
            functools.partial(place_kernel, less),
            "place",
            [(me, smem), gx, gx_near],
            [struct((images * seq_len, width), F32)],
            [pltpu.VMEM((own, width), F32), pltpu.SemaphoreType.DMA((rows // less + 1,))],
        )[0].reshape(images, seq_len, width)

    if usual:
        held_b = fold_step(*halves(held_b), *zlo, gxb)
        send_a = jnp.concatenate([held_a[4:].reshape(-1, width), sums], 0).astype(BF16)
        got = after(swap(send_a, *xbit), (gxb, held_b)).astype(F32)
        held_a = held_a[:4] + got[:-8].reshape(4, -1, width)
        sums = sums + got[-8:]
        got = [
            swap(jnp.concatenate([held_a[n], sums] + more, 0).astype(BF16), "dp", 2 * n)
            for n, more in ((1, []), (2, [held_b[1]]), (3, []))
        ]
        grad_tokens = place(swap(after(gxb, held_a), "tensor", 1))
        got[2] = after(got[2], grad_tokens)
        shapes = ((small, 3 * width), (small, width), (2, small), (3, small), (tall, width), (tall, width))
        o_qkv, o_out, o_gains, o_bias, o_up, o_down = call(
            finish_kernel,
            "finish",
            [(me, smem), held_a, held_b, sums, *got],
            [struct(shape, F32) for shape in shapes],
            limit=2,
            hbm_outs=False,
        )
    else:
        grad_tokens = place(swap(gxb, "tensor", 1))
        send_a = send_a[:-8].reshape(keep_a.shape)
        grad_a, grad_b = other_reduce((keep_a, send_a), (keep_b, send_b), sums, index, n_dp, n_t)
        o_qkv = jnp.concatenate([grad_a[p * small : (p + 1) * small] for p in range(3)], 1)
        o_out = grad_a[3 * small : 4 * small]
        o_vec = lax.dynamic_slice_in_dim(grad_a[4 * small : 4 * small + 5], index * small, small, 1)
        o_gains, o_bias = o_vec[:2], o_vec[2:]
        o_up, o_down = grad_b[:tall], grad_b[tall:]
    return layer_out, grad_tokens, o_qkv, o_out, o_gains, o_bias, o_up, o_down.T


def solution(mesh):
    in_specs = (
        P("dp", None, None),
        P("dp"),
        P("dp", None),
        P("dp", None, None),
        P(("dp", "tensor"), None),
        P(("dp", "tensor"), None),
        P(None, ("dp", "tensor")),
        P(None, ("dp", "tensor")),
        P("dp", "tensor"),
        P("tensor", "dp"),
    )
    out_specs = (
        P("dp", None, None),
        P("dp", None, None),
        P(("dp", "tensor"), None),
        P(("dp", "tensor"), None),
        P(None, ("dp", "tensor")),
        P(None, ("dp", "tensor")),
        P("dp", "tensor"),
        P("tensor", "dp"),
    )
    return jax.shard_map(
        on_device, mesh=mesh, in_specs=in_specs, out_specs=out_specs, check_vma=False
    )
```

```python
import functools

import jax
import jax.numpy as jnp
from jax import lax
from jax.experimental import pallas as pl
from jax.experimental.pallas import tpu as pltpu
from jax.sharding import PartitionSpec as P

HEADS = 2
WIN = 96
F32 = jnp.float32
BF16 = jnp.bfloat16
VDP, VT = 8, 4
CHIPS = VDP * VT // 2
MIB = 1 << 20

NN = ((1,), (0,))
NT = ((1,), (1,))
TN = ((0,), (0,))


def dot(a, b, dims):
    return lax.dot_general(a, b, (dims, ((), ())), preferred_element_type=F32)


def twist(i):
    return (i & 1) * 4 + (i >> 1)


def turn(i):
    return ((i & 1) << 2) | (i & 2) | ((i & 4) >> 2)


def spot(m):
    return (m % 2) * VDP + twist(m // 2)


def norm_parts(values):
    center = values - jnp.mean(values, -1, keepdims=True)
    inv = lax.rsqrt(jnp.mean(center * center, -1, keepdims=True) + 1e-05)
    return center * inv, inv


def norm_back(grad, xhat, inv, gain):
    scaled = grad * gain
    return inv * (
        scaled
        - jnp.mean(scaled, -1, keepdims=True)
        - xhat * jnp.mean(scaled * xhat, -1, keepdims=True)
    )


def gelu_both(u):
    c = 0.7978845608028654
    u2 = u * u
    t = jnp.tanh(u * (c + (c * 0.044715) * u2))
    half = 0.5 + 0.5 * t
    value = u * half
    slope = half + (value - value * half) * (2 * c + (6 * c * 0.044715) * u2)
    return value, slope


def apart(both, hs):
    blocks = []
    for h in range(HEADS):
        parts = [jnp.zeros((WIN, hs), BF16)] * HEADS
        parts[h] = both[:, h * hs : (h + 1) * hs]
        blocks.append(jnp.concatenate(parts, 1))
        blocks.append(jnp.zeros((hs - WIN, HEADS * hs), BF16))
    return jnp.concatenate(blocks, 0)


def pack_kernel(me, *refs):
    sources, packed, held, sems = refs[:6], refs[6], refs[7:13], refs[13]
    copies = [pltpu.make_async_copy(a, b, sems.at[n]) for n, (a, b) in enumerate(zip(sources, held))]
    for copy in copies:
        copy.start()
    qkv, out, gains, biases, up, down = held
    small, width = out.shape
    tall = up.shape[0]
    lane = lax.broadcasted_iota(jnp.int32, (1, width), 1)
    mine = lane // small == me[0]
    for copy in copies:
        copy.wait()
    for part in range(3):
        packed[0, part * small : (part + 1) * small] = qkv[:, part * width : (part + 1) * width]
    packed[0, 3 * small : 4 * small] = out[...]
    rows = [gains[0:1], gains[1:2], biases[0:1], biases[1:2], biases[2:3]]
    vals = jnp.concatenate(rows + [jnp.zeros((3, small), BF16)], 0).astype(F32)
    wide = jnp.concatenate([vals] * (width // small), 1)
    at = 4 * small + 8
    packed[0, 4 * small : at] = jnp.where(mine, wide, 0.0).astype(BF16)
    packed[0, at : at + tall] = up[...]
    packed[0, at + tall :] = down[...]


def turn_kernel(me, cot, tokens, cot_ref, cot_t, x_ref, sems):
    own = cot_ref.shape[0]
    at = pl.ds(lax.rem(me[0], 2) * own, own)
    copies = [
        pltpu.make_async_copy(cot.at[at], cot_ref, sems.at[0]),
        pltpu.make_async_copy(tokens.at[at], x_ref, sems.at[1]),
    ]
    for copy in copies:
        copy.start()
    size = 256 if own % 256 == 0 else own
    copies[0].wait()
    for n in range(own // size):
        part = slice(n * size, (n + 1) * size)
        cot_t[:, part] = cot_ref[part].T
    copies[1].wait()


def first_norm_kernel(x_ref, xhat_ref, inv_ref, xhat_t):
    own, width = x_ref.shape
    ones = jnp.full((width, width), 1.0 / width, BF16)
    size = 256 if own % 256 == 0 else own
    for n in range(own // size):
        part = slice(n * size, (n + 1) * size)
        x = x_ref[part]
        center = x.astype(F32) - dot(x, ones, NN)
        inv = lax.rsqrt(dot((center * center).astype(BF16), ones, NN) + 1e-05)
        xhat = center * inv
        xhat_ref[part] = xhat
        inv_ref[part] = inv[:, :1]
        xhat_t[:width, part] = xhat.astype(BF16).T
        xhat_t[width:, part] = jnp.ones((16, size), BF16)


def attend_kernel(
    per, me, virt, lens, live, x_ref, xhat_ref, held, got,
    qkv_ref, prob_ref, o_ref, x1_ref, wqkv, wout, vec,
):
    tokens, width = x_ref.shape
    rows = tokens // WIN
    hs = width // HEADS
    here = twist(virt[0] // 4)
    y_own = (virt[0] // 2) % 2
    first = virt[0] % 2 == 0
    for m in range(CHIPS):
        k = spot(m) ^ (here + y_own * VDP)
        at = pl.ds(pl.multiple_of(k * 32, 32), 32)
        a = held[at].astype(F32)
        b = got[at].astype(F32)
        even = jnp.where(first, a, b)
        odd = jnp.where(first, b, a)
        for part in range(3):
            both = jnp.concatenate([even[part * 8 : part * 8 + 8], odd[part * 8 : part * 8 + 8]], 0)
            wqkv[m * 16 : m * 16 + 16, part * width : (part + 1) * width] = both.astype(BF16)
        both = jnp.concatenate([even[24:32], odd[24:32]], 0)
        wout[m * 16 : m * 16 + 16] = both.astype(BF16)
    total = held[CHIPS * 32 :].astype(F32) + got[CHIPS * 32 :].astype(F32)
    vec[...] = total
    scale = hs**-0.5
    ii = lax.broadcasted_iota(jnp.int32, (WIN, hs), 0)
    jj = lax.broadcasted_iota(jnp.int32, (WIN, hs), 1)
    same = ii == jj
    image_rows = live.shape[1]
    base = lax.rem(me[0], 2) * rows

    def enter(c):
        part = slice(c * per * WIN, (c + 1) * per * WIN)
        h1 = (xhat_ref[part] * total[0:1] + total[2:3]).astype(BF16)
        qkv = dot(h1, wqkv[...], NN).astype(BF16)
        qkv_ref[part] = qkv
        scores = []
        for r in range(per):
            at = slice(r * WIN, (r + 1) * WIN)
            scores.append(dot(qkv[at, :width], apart(qkv[at, width : 2 * width], hs), NT))
        return qkv, scores

    ahead = enter(0)
    for c in range(rows // per):
        qkv, scores = ahead
        if c + 1 < rows // per:
            ahead = enter(c + 1)
        part = slice(c * per * WIN, (c + 1) * per * WIN)
        probs = []
        for r in range(per):
            row = base + c * per + r
            image = row // image_rows
            inside = row - image * image_rows
            reach = jnp.where(live[image, inside] == 1, lens[image] - inside * WIN, 0)
            allowed = same | (jj < jnp.minimum(ii, reach))
            heads = []
            for h in range(HEADS):
                s = jnp.where(allowed, scores[r][:, h * hs : (h + 1) * hs], -1e30)
                e = jnp.exp((s - jnp.max(s, -1, keepdims=True)) * scale)
                heads.append((e * (1.0 / jnp.sum(e, -1, keepdims=True))).astype(BF16))
            probs.append(jnp.concatenate(heads, 1))
        mixed = []
        for r in range(per):
            at = slice(r * WIN, (r + 1) * WIN)
            mixed.append(dot(probs[r], apart(qkv[at, 2 * width :], hs), NN).astype(BF16))
        o = jnp.concatenate(mixed, 0)
        for n, p in enumerate(probs):
            prob_ref[c * per + n] = p
        o_ref[part] = o
        x1_ref[part] = x_ref[part].astype(F32) + dot(o, wout[...], NN)


def join(virt, blocks, n, up, down_t):
    tall = blocks.shape[1] // 2
    width = up.shape[0]
    here = twist(virt[0] // 4)
    for i in range(VDP):
        k = twist(i) ^ here
        at = slice(i * tall, (i + 1) * tall)
        cols = slice(n * width, (n + 1) * width)
        up[at, cols] = blocks[k, :tall]
        down_t[at, cols] = blocks[k, tall:]


def hidden_units(h2, dyb, up, down_t, between=None):
    u = dot(h2, up[...], NN).astype(BF16)
    da = dot(dyb, down_t[...], NN).astype(BF16)
    done = between() if between is not None else None
    a, slope = gelu_both(u)
    return a, da * slope, done


def hidden_near_kernel(
    per, virt, x1_ref, cot_ref, cot_t, vec, own, got,
    h2_ref, xhat_ref, inv_ref, f_ref, dh2_ref, keep, send,
    a_ref, du_ref, h2_t, up, down_t, up_t, down,
):
    tokens, width = x1_ref.shape
    size = per * WIN
    join(virt, own, 0, up, down_t)
    join(virt, got, 1, up, down_t)
    up_t[...] = up[...].T
    down[...] = down_t[...].T
    count = tokens // size

    def norm(c):
        part = slice(c * size, (c + 1) * size)
        xhat, inv = norm_parts(x1_ref[part])
        xhat_ref[part] = xhat
        inv_ref[part] = inv
        h2 = (xhat * vec[1:2] + vec[3:4]).astype(BF16)
        h2_ref[part] = h2
        h2_t[:, part] = h2.T
        return h2

    h2 = norm(0)
    for c in range(count):
        part = slice(c * size, (c + 1) * size)
        later = functools.partial(norm, c + 1) if c + 1 < count else None
        a, du, h2 = hidden_units(h2, cot_ref[part], up, down_t, later)
        a_ref[part] = a
        du_ref[part] = du
        f_ref[part] = x1_ref[part] + vec[4:5] + dot(a, down[...], NN)
        dh2_ref[part] = dot(du, up_t[...], NN)
    gdown = dot(cot_t[...], a_ref[...], NN)
    gup = dot(h2_t[...], du_ref[...], NN)
    tall = width // VDP
    here = turn(virt[0] // 4)
    for i in range(VDP):
        at = slice(i * tall, (i + 1) * tall)
        k = turn(i) ^ here
        keep[k, :tall] = gup[at, :width]
        keep[k, tall:] = gdown[at, :width]
        send[k, :tall] = gup[at, width:].astype(BF16)
        send[k, tall:] = gdown[at, width:].astype(BF16)


def hidden_far_kernel(
    per, virt, cot_ref, vec, own, got, h2_ref, xhat_ref, inv_ref, f_ref, dh2_ref, o_ref,
    y_ref, dx1_ref, g_ref, gout, gvec,
    o_t, up, down_t, up_t, down,
):
    tokens, width = h2_ref.shape
    size = per * WIN
    join(virt, own, 0, up, down_t)
    join(virt, got, 1, up, down_t)
    up_t[...] = up[...].T
    down[...] = down_t[...].T
    sums = [jnp.zeros((1, width), F32)] * 3
    count = tokens // size

    def units(c):
        part = slice(c * size, (c + 1) * size)
        o_t[:, part] = o_ref[part].T
        return hidden_units(h2_ref[part], cot_ref[part], up, down_t)[:2]

    ahead = units(0)
    for c in range(count):
        part = slice(c * size, (c + 1) * size)
        a, du = ahead
        y_ref[part] = (f_ref[part] + dot(a, down[...], NN)).astype(BF16)
        dh2 = dh2_ref[part] + dot(du, up_t[...], NN)
        if c + 1 < count:
            ahead = units(c + 1)
        dy = cot_ref[part].astype(F32)
        xhat = xhat_ref[part]
        dx1 = dy + norm_back(dh2, xhat, inv_ref[part], vec[1:2])
        dx1_ref[part] = dx1
        g_ref[part] = dx1.astype(BF16)
        for n, term in enumerate((dh2 * xhat, dh2, dy)):
            sums[n] = sums[n] + jnp.sum(term, 0, keepdims=True)
    gout[...] = dot(o_t[...], g_ref[...], NN)
    zero = jnp.zeros((1, width), F32)
    gvec[...] = jnp.concatenate([zero, sums[0], zero, sums[1], sums[2], zero, zero, zero], 0)


def own_rows(virt, i, other):
    core = virt[0] % 2
    core = 1 - core if other else core
    return pl.ds(pl.multiple_of(i * 32 + ((virt[0] // 2) % 2) * 16 + core * 8, 8), 8)


def back_kernel(
    per, virt, qkv_ref, prob_ref, g_ref, xhat_t, wqkv, wout, vec, gout, gvec,
    dqkv, keep, send, vec_sums,
    gqkv,
):
    tokens, width = g_ref.shape
    hs = width // HEADS
    scale = hs**-0.5
    every = [(r, h) for r in range(tokens // WIN) for h in range(HEADS)]
    groups = [every[n : n + 2 * per] for n in range(0, len(every), 2 * per)]

    def piece(ref, r, h, part=0):
        return ref[r * WIN : (r + 1) * WIN, part * width + h * hs : part * width + (h + 1) * hs]

    def enter(pairs):
        r = pairs[0][0]
        do = dot(g_ref[r * WIN : (r + per) * WIN], wout[...], NT).astype(BF16)
        dos = [do[(n - r) * WIN : (n - r + 1) * WIN, h * hs : (h + 1) * hs] for n, h in pairs]
        probs = [prob_ref[r, :, h * hs : h * hs + WIN] for r, h in pairs]
        dps = [dot(a, piece(qkv_ref, r, h, 2), NT) for a, (r, h) in zip(dos, pairs)]
        dvs = [dot(p, a, TN).astype(BF16) for p, a in zip(probs, dos)]
        return probs, dps, dvs

    ahead = enter(groups[0])
    for place, pairs in enumerate(groups):
        probs, dps, dvs = ahead
        if place + 1 < len(groups):
            ahead = enter(groups[place + 1])
        dss = []
        for p, dp in zip(probs, dps):
            pf = p.astype(F32)
            ds = pf * (dp - jnp.sum(dp * pf, -1, keepdims=True)) * scale
            dss.append(ds.astype(BF16))
        dqs = [dot(ds, piece(qkv_ref, r, h, 1), NN).astype(BF16) for ds, (r, h) in zip(dss, pairs)]
        dks = [dot(ds, piece(qkv_ref, r, h, 0), TN).astype(BF16) for ds, (r, h) in zip(dss, pairs)]
        for n, (r, h) in enumerate(pairs):
            for part, values in enumerate((dqs, dks, dvs)):
                at = slice(part * width + h * hs, part * width + (h + 1) * hs)
                dqkv[r * WIN : (r + 1) * WIN, at] = values[n]
    both = dot(xhat_t[...], dqkv[...], NN)
    grad, total = both[:width], both[width : width + 1]
    w = wqkv[...].astype(F32)
    cols = jnp.concatenate([
        jnp.broadcast_to(jnp.sum(w * grad, -1, keepdims=True), (width, 64)),
        jnp.broadcast_to(jnp.sum(w * total, -1, keepdims=True), (width, 64)),
    ], 1)
    lines = cols.T
    gain, from_total = lines[0:1], lines[64:65]
    vec_t = vec[...].T
    gqkv[...] = grad * vec_t[:, 0:1] + total * vec_t[:, 2:3]
    rest = gvec[...]
    sums = jnp.concatenate([gain, rest[1:2], from_total, rest[3:]], 0)
    here = twist(virt[0] // 4)
    for i in range(VDP):
        k = twist(i) ^ here
        mine, other = own_rows(virt, i, 0), own_rows(virt, i, 1)
        theirs = []
        for part in range(3):
            at = slice(part * width, (part + 1) * width)
            keep[k, part * 8 : part * 8 + 8] = gqkv[mine, at]
            theirs.append(gqkv[other, at])
        keep[k, 24:] = gout[mine]
        at = pl.ds(pl.multiple_of(k * 32, 32), 32)
        send[at] = jnp.concatenate(theirs + [gout[other]], 0).astype(BF16)
    vec_sums[...] = sums
    send[VDP * 32 :] = sums.astype(BF16)


def token_grad_kernel(per, me, dqkv, wqkv, vec, xhat_ref, inv_ref, dx1_ref, y, y_near, gx, gxb, out, turned, sems):
    own = dqkv.shape[0]
    size = per * WIN
    copies = []
    for n, source in enumerate((y, y_near)):
        at = pl.ds((lax.rem(me[0], 2) ^ n) * own, own)
        copies.append(pltpu.make_async_copy(source, out.at[at], sems.at[n]))
        copies[-1].start()
    turned[...] = wqkv[...].T
    for c in range(own // size):
        part = slice(c * size, (c + 1) * size)
        dh1 = dot(dqkv[part], turned[...], NN)
        values = dx1_ref[part] + norm_back(dh1, xhat_ref[part], inv_ref[part], vec[0:1])
        gx[part] = values
        gxb[part] = values.astype(BF16)
    for copy in copies:
        copy.wait()


def place_kernel(per, me, mine, theirs, out, wide, sems):
    own = theirs.shape[0]
    size = per * WIN
    here = lax.rem(me[0], 2) * own
    copies = [pltpu.make_async_copy(mine, out.at[pl.ds(here, own)], sems.at[own // size])]
    copies[0].start()
    for c in range(own // size):
        part = pl.ds(c * size, size)
        wide[part] = theirs[part].astype(F32)
        at = pl.ds(own - here + c * size, size)
        copies.append(pltpu.make_async_copy(wide.at[part], out.at[at], sems.at[c]))
        copies[-1].start()
    for copy in copies:
        copy.wait()


def finish_kernel(me, keep_a, keep_b, sums, *refs):
    qkv, out, gains, biases, up, down = refs[3:]
    small, width = out.shape
    tall = up.shape[0]
    high = 4 * small + 8
    total, vec = keep_a[0], sums[...]
    for got in refs[:3]:
        total = total + got[: 4 * small].astype(F32)
        vec = vec + got[4 * small : high].astype(F32)
    units = keep_b[0] + refs[1][high:].astype(F32)
    for part in range(3):
        qkv[:, part * width : (part + 1) * width] = total[part * small : (part + 1) * small]
    out[...] = total[3 * small :]
    vec = pltpu.roll(vec, width - me[0] * small, 1)[:, :small]
    gains[...] = vec[:2]
    biases[...] = vec[2:5]
    up[...] = units[:tall]
    down[...] = units[tall:]


def swap(block, axis, bit):
    size = lax.axis_size(axis)
    return lax.ppermute(block, axis, [(i, i ^ bit) for i in range(size)])


def steps_of(axis):
    return [(axis, 1 << k) for k in reversed(range(lax.axis_size(axis).bit_length() - 1))]


def after(value, other):
    return lax.optimization_barrier((value, other))[0]


def merge(pieces):
    vec = sum(piece[-8:] for piece in pieces)
    return jnp.concatenate([piece[:-8] for piece in pieces] + [vec], 0)


def halves(held):
    half = held.shape[0] // 2
    return held[:half], held[half:].astype(BF16)


def fold_step(keep, send, axis, bit, past=None):
    got = swap(send, axis, bit)
    return keep + (got if past is None else after(got, past)).astype(F32)


def bit_reverse(index, count):
    out = 0 * index
    for k in range(count):
        out = out | (((index >> k) & 1) << (count - 1 - k))
    return out


def by_device(block, me):
    blocks = block[None]
    for axis, bit in steps_of("dp") + steps_of("tensor"):
        blocks = jnp.concatenate([blocks, swap(blocks, axis, bit)], 0)
    count = blocks.shape[0]
    order = jnp.arange(count, dtype=jnp.int32) ^ me
    return jnp.take(blocks, bit_reverse(order, count.bit_length() - 1), axis=0)


def other_pack(w_qkv, w_out, gains, biases, w_up, w_down, me):
    small, width = w_out.shape
    qkv = w_qkv.reshape(small, 3, width).transpose(1, 0, 2).reshape(3 * small, width)
    rows = jnp.concatenate([gains, biases], 0)
    place = jnp.zeros((8, width), BF16)
    place = lax.dynamic_update_slice(place, rows, (jnp.int32(0), me * small))
    return jnp.concatenate([qkv, w_out, place], 0), jnp.concatenate([w_up, w_down.T], 0)


def other_blocks(a, b, me, n_dp, n_t):
    a = by_device(a, me)
    b = by_device(b, me)
    width = a.shape[2]
    count = n_dp * n_t
    small = width // count
    big = width // (VDP * VT)
    mats = a[:, : 4 * small].reshape(count, 4, small, width).transpose(1, 0, 2, 3)
    mats = mats.reshape(4, VDP * VT, big, width).transpose(1, 0, 2, 3).reshape(VDP * VT, 4 * big, width)
    vec = jnp.sum(a[:, 4 * small :].astype(F32), 0).astype(BF16)
    a = mats
    tall = width // n_dp
    b = b.reshape(n_dp, VT, 2, tall, width).transpose(1, 2, 0, 3, 4)
    b = b.reshape(VT, 2, VDP, width // VDP, width).transpose(2, 0, 1, 3, 4)
    b = b.reshape(VDP * VT, 2 * (width // VDP), width)

    y_own = (me // 2) % 2

    def placed(blocks):
        pairs = blocks.reshape((CHIPS, 2) + blocks.shape[1:])
        chips = sorted(range(CHIPS), key=spot)
        pairs = jnp.stack([pairs[m] for m in chips], 0)
        pairs = jnp.where(y_own == 1, jnp.roll(pairs, VDP, 0), pairs)
        return pairs[:, 0], pairs[:, 1]

    held_a, got_a = (part.reshape(-1, width) for part in placed(a))
    held_a = jnp.concatenate([held_a, vec], 0)
    got_a = jnp.concatenate([got_a, jnp.zeros_like(vec)], 0)
    return (held_a, got_a) + placed(b)


def other_reduce(pair_a, pair_b, sums, me, n_dp, n_t):
    count = n_dp * n_t
    y_own = (me // 2) % 2

    def whole(keep, send, order):
        pairs = jnp.stack([keep, send.astype(F32)], 1)
        pairs = jnp.stack([pairs[order(i)] for i in range(VDP)], 0)
        none = jnp.zeros_like(pairs)
        both = jnp.stack([jnp.where(y_own == y, pairs, none) for y in range(2)], 1)
        return both.reshape((VDP * VT,) + keep.shape[1:])

    def rows_of(blocks, parts):
        big = blocks.shape[1] // parts
        mats = blocks.reshape(VDP * VT, parts, big, -1).transpose(1, 0, 2, 3)
        mats = mats.reshape(parts, count, VDP * VT * big // count, -1).transpose(1, 0, 2, 3)
        return mats.reshape(count, -1, blocks.shape[2])

    a, b = whole(*pair_a, twist), whole(*pair_b, turn)
    width = a.shape[2]
    tall, high = width // n_dp, width // VDP
    cols = b.reshape(VDP, VT, 2, high, width).transpose(1, 2, 0, 3, 4)
    cols = cols.reshape(VT, 2, n_dp, tall, width).transpose(2, 0, 1, 3, 4)
    cols = cols.reshape(count, 2 * tall, width)
    vec = jnp.broadcast_to(jnp.where(y_own == 0, sums, 0.0)[None], (count,) + sums.shape)
    a = jnp.concatenate([rows_of(a, 4), vec], 1)
    results = []
    for blocks in (a, cols):
        blocks = jnp.take(blocks, jnp.arange(count, dtype=jnp.int32) ^ me, axis=0)
        for axis, bit in reversed(steps_of("dp") + steps_of("tensor")):
            pairs = blocks.reshape((-1, 2) + blocks.shape[1:])
            got = swap(pairs[:, 1].astype(BF16), axis, bit)
            blocks = pairs[:, 0] + got.astype(F32)
        results.append(blocks[0])
    return results


def struct(shape, dtype):
    return jax.ShapeDtypeStruct(shape, dtype)


def call(kernel, name, args, outs, scratch=(), flops=0, limit=8, hbm_outs=True):
    args = [a if isinstance(a, tuple) else (a, pltpu.VMEM) for a in args]
    moved = sum(a.size * a.dtype.itemsize for a, _ in args)
    spaces = [pl.ANY if hbm_outs and isinstance(o, jax.ShapeDtypeStruct) else pltpu.VMEM for o in outs]
    return pl.pallas_call(
        kernel,
        name=name,
        out_shape=outs,
        in_specs=[pl.BlockSpec(memory_space=space) for _, space in args],
        out_specs=[pl.BlockSpec(memory_space=space) for space in spaces],
        scratch_shapes=list(scratch),
        compiler_params=pltpu.CompilerParams(vmem_limit_bytes=limit * MIB),
        cost_estimate=pl.CostEstimate(flops=flops, bytes_accessed=moved, transcendentals=0),
    )(*[a for a, _ in args])


def on_device(tokens, lengths, row_mask, cotangent, w_qkv, w_out, gains, biases, w_up, w_down):
    images, seq_len, width = tokens.shape
    n_dp, n_t = lax.axis_size("dp"), lax.axis_size("tensor")
    index = lax.axis_index("dp") * n_t + lax.axis_index("tensor")
    me = index.astype(jnp.int32).reshape(1)
    usual = (n_dp, n_t) == (VDP, VT)
    virt = me if usual else (index // 2 % 2 * 2).astype(jnp.int32).reshape(1)
    small = width // (n_dp * n_t)
    tall = width // n_dp
    own = images * seq_len // 2
    rows = own // WIN
    per = 12 if rows % 12 == 0 else 1
    some = 6 if rows % 6 == 0 else 1
    less = 4 if rows % 4 == 0 else 1
    smem = pltpu.SMEM
    weights = (w_qkv, w_out, gains, biases, w_up, w_down)
    token_mm = 2 * own * width
    hbm = pltpu.HBM

    def in_hbm(array):
        return (pltpu.with_memory_space_constraint(array, hbm), hbm)

    def first_norm(x):
        return call(
            first_norm_kernel,
            "first_norm",
            [x],
            [
                pltpu.VMEM((own, width), F32),
                pltpu.VMEM((own, 1), F32),
                pltpu.VMEM((width + 16, own), BF16),
            ],
            limit=4,
        )

    def fetch(me):
        flat = [array.reshape(images * seq_len, width) for array in (cotangent, tokens)]
        return call(
            turn_kernel,
            "turn",
            [(me, smem)] + [in_hbm(array) for array in flat],
            [
                pltpu.VMEM((own, width), BF16),
                pltpu.VMEM((width, own), BF16),
                pltpu.VMEM((own, width), BF16),
            ],
            [pltpu.SemaphoreType.DMA((2,))],
            limit=4,
        )

    if usual:
        weights = (w_qkv, w_out, gains, biases, w_up, w_down.T)
        high = 4 * small + 8
        packed = call(
            pack_kernel,
            "pack",
            [(me, smem)] + [in_hbm(w) for w in weights],
            [pltpu.VMEM((1, high + 2 * tall, width), BF16)],
            [pltpu.VMEM(w.shape, BF16) for w in weights] + [pltpu.SemaphoreType.DMA((6,))],
        )[0]
        planes = [packed] + [swap(packed, "dp", bit) for bit in (2, 4, 6)]
        cot, cot_t, x = fetch(after(me, packed))
        planes[3] = after(planes[3], cot)
        held_a = merge([plane[0, :high] for plane in planes])
        b = jnp.concatenate([plane[:, high:] for plane in planes], 0)
        far_b = swap(b, "tensor", 2)
        held_a = merge([held_a, swap(held_a, "dp", 1)])
        b = jnp.concatenate([b, swap(b, "dp", 1)], 0)
        xhat1, inv1, xhat_t = first_norm(after(x, (held_a, far_b)))
        held_a = merge([held_a, after(swap(held_a, "tensor", 2), (b, xhat1))])
        far_x = swap(far_b, "dp", 1)
        got_a = swap(held_a, "tensor", 1)
        got_b = swap(b, "tensor", 1)
    else:
        held_a, got_a, held_b, got_b = other_blocks(*other_pack(*weights, index), index, n_dp, n_t)
        b, far_b = held_b[:VDP], held_b[VDP:]
        got_b, got_far = got_b[:VDP], got_b[VDP:]
        cot, cot_t, x = fetch(me)
        xhat1, inv1, xhat_t = first_norm(x)
    qkv, prob, o, x1, wqkv, wout, vec = call(
        functools.partial(attend_kernel, some),
        "attend",
        [(me, smem), (virt, smem), (lengths, smem), (row_mask, smem), x, xhat1, held_a, got_a],
        [
            pltpu.VMEM((own, 3 * width), BF16),
            pltpu.VMEM((rows, WIN, width), BF16),
            pltpu.VMEM((own, width), BF16),
            pltpu.VMEM((own, width), F32),
            pltpu.VMEM((width, 3 * width), BF16),
            pltpu.VMEM((width, width), BF16),
            pltpu.VMEM((8, width), F32),
        ],
        flops=token_mm * (4 * width + 2 * WIN),
    )
    tall_b = 2 * (width // VDP)
    mats = [pltpu.VMEM((width, 2 * width), BF16)] * 2 + [pltpu.VMEM((2 * width, width), BF16)] * 2
    if usual:
        far_b = jnp.concatenate([far_b, after(far_x, x1)], 0)
        got_far = swap(far_b, "tensor", 1)
        got_b = after(got_b, far_b)
    wide_per = 8 if rows % 8 == 0 else rows
    *first, keep_b, send_b = call(
        functools.partial(hidden_near_kernel, wide_per),
        "hidden_near",
        [(virt, smem), x1, cot, cot_t, vec, b, got_b],
        [
            pltpu.VMEM((own, width), BF16),
            pltpu.VMEM((own, width), F32),
            pltpu.VMEM((own, 1), F32),
            pltpu.VMEM((own, width), F32),
            pltpu.VMEM((own, width), F32),
            pltpu.VMEM((VDP, tall_b, width), F32),
            pltpu.VMEM((VDP, tall_b, width), BF16),
        ],
        [pltpu.VMEM((own, 2 * width), BF16)] * 2 + [pltpu.VMEM((width, own), BF16)] + mats,
        token_mm * 12 * width,
        12,
    )
    y, dx1, g, gout, gvec = call(
        functools.partial(hidden_far_kernel, wide_per),
        "hidden_far",
        [(virt, smem), cot, vec, far_b, got_far, *first, o],
        [
            pltpu.VMEM((own, width), BF16),
            pltpu.VMEM((own, width), F32),
            pltpu.VMEM((own, width), BF16),
            pltpu.VMEM((width, width), F32),
            pltpu.VMEM((8, width), F32),
        ],
        [pltpu.VMEM((width, own), BF16)] + mats,
        token_mm * 9 * width,
    )
    core, xbit, zlo = ("tensor", 1), ("dp", 1), ("dp", 2)
    if usual:
        held_b = fold_step(keep_b, send_b, *core, g)
        y = after(y, held_b)
    y_near = swap(y, "tensor", 1)
    dqkv, keep_a, send_a, sums = call(
        functools.partial(back_kernel, per),
        "back",
        [(virt, smem), qkv, prob, g, xhat_t, wqkv, wout, vec, gout, gvec],
        [
            pltpu.VMEM((own, 3 * width), BF16),
            pltpu.VMEM((VDP, 32, width), F32),
            pltpu.VMEM((VDP * 32 + 8, width), BF16),
            pltpu.VMEM((8, width), F32),
        ],
        [pltpu.VMEM((width, 3 * width), F32)],
        token_mm * (4 * width + 5 * WIN),
    )
    if usual:
        held_b = fold_step(*halves(held_b), *xbit)
        got = after(swap(send_a, *core), held_b).astype(F32)
        held_a = keep_a + got[:-8].reshape(keep_a.shape)
        sums = sums + got[-8:]
        vec = after(vec, held_a)
    gx, gxb, layer_out = call(
        functools.partial(token_grad_kernel, less),
        "token_grad",
        [(me, smem), dqkv, wqkv, vec, xhat1, inv1, dx1, y, y_near],
        [
            pltpu.VMEM((own, width), F32),
            pltpu.VMEM((own, width), BF16),
            struct((images * seq_len, width), BF16),
        ],
        [pltpu.VMEM((3 * width, width), BF16), pltpu.SemaphoreType.DMA((2,))],
        flops=token_mm * 3 * width,
    )
    layer_out = layer_out.reshape(images, seq_len, width)

    def place(gx_near):
        return call(
            functools.partial(place_kernel, less),
            "place",
            [(me, smem), gx, gx_near],
            [struct((images * seq_len, width), F32)],
            [pltpu.VMEM((own, width), F32), pltpu.SemaphoreType.DMA((rows // less + 1,))],
        )[0].reshape(images, seq_len, width)

    if usual:
        held_b = fold_step(*halves(held_b), *zlo, gxb)
        send_a = jnp.concatenate([held_a[4:].reshape(-1, width), sums], 0).astype(BF16)
        got = after(swap(send_a, *xbit), (gxb, held_b)).astype(F32)
        held_a = held_a[:4] + got[:-8].reshape(4, -1, width)
        sums = sums + got[-8:]
        got = [
            swap(jnp.concatenate([held_a[n], sums] + more, 0).astype(BF16), "dp", 2 * n)
            for n, more in ((1, []), (2, [held_b[1]]), (3, []))
        ]
        grad_tokens = place(swap(after(gxb, held_a), "tensor", 1))
        got[2] = after(got[2], grad_tokens)
        shapes = ((small, 3 * width), (small, width), (2, small), (3, small), (tall, width), (tall, width))
        o_qkv, o_out, o_gains, o_bias, o_up, o_down = call(
            finish_kernel,
            "finish",
            [(me, smem), held_a, held_b, sums, *got],
            [struct(shape, F32) for shape in shapes],
            limit=2,
            hbm_outs=False,
        )
    else:
        grad_tokens = place(swap(gxb, "tensor", 1))
        send_a = send_a[:-8].reshape(keep_a.shape)
        grad_a, grad_b = other_reduce((keep_a, send_a), (keep_b, send_b), sums, index, n_dp, n_t)
        o_qkv = jnp.concatenate([grad_a[p * small : (p + 1) * small] for p in range(3)], 1)
        o_out = grad_a[3 * small : 4 * small]
        o_vec = lax.dynamic_slice_in_dim(grad_a[4 * small : 4 * small + 5], index * small, small, 1)
        o_gains, o_bias = o_vec[:2], o_vec[2:]
        o_up, o_down = grad_b[:tall], grad_b[tall:]
    return layer_out, grad_tokens, o_qkv, o_out, o_gains, o_bias, o_up, o_down.T


def solution(mesh):
    in_specs = (
        P("dp", None, None),
        P("dp"),
        P("dp", None),
        P("dp", None, None),
        P(("dp", "tensor"), None),
        P(("dp", "tensor"), None),
        P(None, ("dp", "tensor")),
        P(None, ("dp", "tensor")),
        P("dp", "tensor"),
        P("tensor", "dp"),
    )
    out_specs = (
        P("dp", None, None),
        P("dp", None, None),
        P(("dp", "tensor"), None),
        P(("dp", "tensor"), None),
        P(None, ("dp", "tensor")),
        P(None, ("dp", "tensor")),
        P("dp", "tensor"),
        P("tensor", "dp"),
    )
    return jax.shard_map(
        on_device, mesh=mesh, in_specs=in_specs, out_specs=out_specs, check_vma=False
    )
```

```python
import functools

import jax
import jax.numpy as jnp
from jax import lax
from jax.experimental import pallas as pl
from jax.experimental.pallas import tpu as pltpu
from jax.sharding import PartitionSpec as P

HEADS = 2
WIN = 96
F32 = jnp.float32
BF16 = jnp.bfloat16
VDP, VT = 8, 4
CHIPS = VDP * VT // 2
MIB = 1 << 20

NN = ((1,), (0,))
NT = ((1,), (1,))
TN = ((0,), (0,))


def dot(a, b, dims):
    return lax.dot_general(a, b, (dims, ((), ())), preferred_element_type=F32)


def twist(i):
    return (i & 1) * 4 + (i >> 1)


def spot(m):
    return (m % 2) * VDP + twist(m // 2)


def norm_parts(values):
    center = values - jnp.mean(values, -1, keepdims=True)
    inv = lax.rsqrt(jnp.mean(center * center, -1, keepdims=True) + 1e-05)
    return center * inv, inv


def norm_back(grad, xhat, inv, gain):
    scaled = grad * gain
    return inv * (
        scaled
        - jnp.mean(scaled, -1, keepdims=True)
        - xhat * jnp.mean(scaled * xhat, -1, keepdims=True)
    )


def gelu_both(u):
    c = 0.7978845608028654
    u2 = u * u
    t = jnp.tanh(u * (c + (c * 0.044715) * u2))
    half = 0.5 + 0.5 * t
    value = u * half
    slope = half + (value - value * half) * (2 * c + (6 * c * 0.044715) * u2)
    return value, slope


def apart(both, hs):
    blocks = []
    for h in range(HEADS):
        parts = [jnp.zeros((WIN, hs), BF16)] * HEADS
        parts[h] = both[:, h * hs : (h + 1) * hs]
        blocks.append(jnp.concatenate(parts, 1))
        blocks.append(jnp.zeros((hs - WIN, HEADS * hs), BF16))
    return jnp.concatenate(blocks, 0)


def pack_kernel(me, *refs):
    sources, packed, held, sems = refs[:6], refs[6], refs[7:13], refs[13]
    copies = [pltpu.make_async_copy(a, b, sems.at[n]) for n, (a, b) in enumerate(zip(sources, held))]
    for copy in copies:
        copy.start()
    qkv, out, gains, biases, up, down = held
    small, width = out.shape
    tall = up.shape[0]
    lane = lax.broadcasted_iota(jnp.int32, (1, width), 1)
    mine = lane // small == me[0]
    for copy in copies:
        copy.wait()
    for part in range(3):
        packed[0, part * small : (part + 1) * small] = qkv[:, part * width : (part + 1) * width]
    packed[0, 3 * small : 4 * small] = out[...]
    rows = [gains[0:1], gains[1:2], biases[0:1], biases[1:2], biases[2:3]]
    vals = jnp.concatenate(rows + [jnp.zeros((3, small), BF16)], 0).astype(F32)
    wide = jnp.concatenate([vals] * (width // small), 1)
    at = 4 * small + 8
    packed[0, 4 * small : at] = jnp.where(mine, wide, 0.0).astype(BF16)
    packed[0, at : at + tall] = up[...]
    packed[0, at + tall :] = down[...]


def turn_kernel(me, cot, tokens, cot_ref, cot_t, x_ref, sems):
    own = cot_ref.shape[0]
    at = pl.ds(lax.rem(me[0], 2) * own, own)
    copies = [
        pltpu.make_async_copy(cot.at[at], cot_ref, sems.at[0]),
        pltpu.make_async_copy(tokens.at[at], x_ref, sems.at[1]),
    ]
    for copy in copies:
        copy.start()
    size = 256 if own % 256 == 0 else own
    copies[0].wait()
    for n in range(own // size):
        part = slice(n * size, (n + 1) * size)
        cot_t[:, part] = cot_ref[part].T
    copies[1].wait()


def first_norm_kernel(x_ref, xhat_ref, inv_ref, xhat_t):
    own, width = x_ref.shape
    ones = jnp.full((width, width), 1.0 / width, BF16)
    size = 256 if own % 256 == 0 else own
    for n in range(own // size):
        part = slice(n * size, (n + 1) * size)
        x = x_ref[part]
        center = x.astype(F32) - dot(x, ones, NN)
        inv = lax.rsqrt(dot((center * center).astype(BF16), ones, NN) + 1e-05)
        xhat = center * inv
        xhat_ref[part] = xhat
        inv_ref[part] = inv[:, :1]
        xhat_t[:width, part] = xhat.astype(BF16).T
        xhat_t[width:, part] = jnp.ones((16, size), BF16)


def attend_kernel(
    per, me, virt, lens, live, x_ref, xhat_ref, held, got,
    qkv_ref, prob_ref, o_ref, x1_ref, wqkv, wout, vec,
):
    tokens, width = x_ref.shape
    rows = tokens // WIN
    hs = width // HEADS
    here = twist(virt[0] // 4)
    y_own = (virt[0] // 2) % 2
    first = virt[0] % 2 == 0
    for m in range(CHIPS):
        k = spot(m) ^ (here + y_own * VDP)
        at = pl.ds(pl.multiple_of(k * 32, 32), 32)
        a = held[at].astype(F32)
        b = got[at].astype(F32)
        even = jnp.where(first, a, b)
        odd = jnp.where(first, b, a)
        for part in range(3):
            both = jnp.concatenate([even[part * 8 : part * 8 + 8], odd[part * 8 : part * 8 + 8]], 0)
            wqkv[m * 16 : m * 16 + 16, part * width : (part + 1) * width] = both.astype(BF16)
        both = jnp.concatenate([even[24:32], odd[24:32]], 0)
        wout[m * 16 : m * 16 + 16] = both.astype(BF16)
    total = held[CHIPS * 32 :].astype(F32) + got[CHIPS * 32 :].astype(F32)
    vec[...] = total
    scale = hs**-0.5
    ii = lax.broadcasted_iota(jnp.int32, (WIN, hs), 0)
    jj = lax.broadcasted_iota(jnp.int32, (WIN, hs), 1)
    same = ii == jj
    image_rows = live.shape[1]
    base = lax.rem(me[0], 2) * rows

    def enter(c):
        part = slice(c * per * WIN, (c + 1) * per * WIN)
        h1 = (xhat_ref[part] * total[0:1] + total[2:3]).astype(BF16)
        qkv = dot(h1, wqkv[...], NN).astype(BF16)
        qkv_ref[part] = qkv
        scores = []
        for r in range(per):
            at = slice(r * WIN, (r + 1) * WIN)
            scores.append(dot(qkv[at, :width], apart(qkv[at, width : 2 * width], hs), NT))
        return qkv, scores

    ahead = enter(0)
    for c in range(rows // per):
        qkv, scores = ahead
        if c + 1 < rows // per:
            ahead = enter(c + 1)
        part = slice(c * per * WIN, (c + 1) * per * WIN)
        probs = []
        for r in range(per):
            row = base + c * per + r
            image = row // image_rows
            inside = row - image * image_rows
            reach = jnp.where(live[image, inside] == 1, lens[image] - inside * WIN, 0)
            allowed = same | (jj < jnp.minimum(ii, reach))
            heads = []
            for h in range(HEADS):
                s = jnp.where(allowed, scores[r][:, h * hs : (h + 1) * hs], -1e30)
                e = jnp.exp((s - jnp.max(s, -1, keepdims=True)) * scale)
                heads.append((e * (1.0 / jnp.sum(e, -1, keepdims=True))).astype(BF16))
            probs.append(jnp.concatenate(heads, 1))
        mixed = []
        for r in range(per):
            at = slice(r * WIN, (r + 1) * WIN)
            mixed.append(dot(probs[r], apart(qkv[at, 2 * width :], hs), NN).astype(BF16))
        o = jnp.concatenate(mixed, 0)
        for n, p in enumerate(probs):
            prob_ref[c * per + n] = p
        o_ref[part] = o
        x1_ref[part] = x_ref[part].astype(F32) + dot(o, wout[...], NN)


def join(virt, blocks, n, up, down_t):
    tall = blocks.shape[1] // 2
    width = up.shape[0]
    here = twist(virt[0] // 4)
    for i in range(VDP):
        k = twist(i) ^ here
        at = slice(i * tall, (i + 1) * tall)
        cols = slice(n * width, (n + 1) * width)
        up[at, cols] = blocks[k, :tall]
        down_t[at, cols] = blocks[k, tall:]


def hidden_units(h2, dyb, up, down_t, between=None):
    u = dot(h2, up[...], NN).astype(BF16)
    da = dot(dyb, down_t[...], NN).astype(BF16)
    done = between() if between is not None else None
    a, slope = gelu_both(u)
    return a, da * slope, done


def hidden_near_kernel(
    per, virt, x1_ref, cot_ref, cot_t, vec, own, got,
    h2_ref, xhat_ref, inv_ref, f_ref, dh2_ref, keep, send,
    a_ref, du_ref, h2_t, up, down_t, up_t, down,
):
    tokens, width = x1_ref.shape
    size = per * WIN
    join(virt, own, 0, up, down_t)
    join(virt, got, 1, up, down_t)
    up_t[...] = up[...].T
    down[...] = down_t[...].T
    count = tokens // size

    def norm(c):
        part = slice(c * size, (c + 1) * size)
        xhat, inv = norm_parts(x1_ref[part])
        xhat_ref[part] = xhat
        inv_ref[part] = inv
        h2 = (xhat * vec[1:2] + vec[3:4]).astype(BF16)
        h2_ref[part] = h2
        h2_t[:, part] = h2.T
        return h2

    h2 = norm(0)
    for c in range(count):
        part = slice(c * size, (c + 1) * size)
        later = functools.partial(norm, c + 1) if c + 1 < count else None
        a, du, h2 = hidden_units(h2, cot_ref[part], up, down_t, later)
        a_ref[part] = a
        du_ref[part] = du
        f_ref[part] = x1_ref[part] + vec[4:5] + dot(a, down[...], NN)
        dh2_ref[part] = dot(du, up_t[...], NN)
    gdown = dot(cot_t[...], a_ref[...], NN)
    gup = dot(h2_t[...], du_ref[...], NN)
    tall = width // VDP
    here = twist(virt[0] // 4)
    for i in range(VDP):
        at = slice(i * tall, (i + 1) * tall)
        k = twist(i) ^ here
        keep[k, :tall] = gup[at, :width]
        keep[k, tall:] = gdown[at, :width]
        send[k, :tall] = gup[at, width:].astype(BF16)
        send[k, tall:] = gdown[at, width:].astype(BF16)


def hidden_far_kernel(
    per, virt, cot_ref, vec, own, got, h2_ref, xhat_ref, inv_ref, f_ref, dh2_ref, o_ref,
    y_ref, dx1_ref, g_ref, gout, gvec,
    o_t, up, down_t, up_t, down,
):
    tokens, width = h2_ref.shape
    size = per * WIN
    join(virt, own, 0, up, down_t)
    join(virt, got, 1, up, down_t)
    up_t[...] = up[...].T
    down[...] = down_t[...].T
    sums = [jnp.zeros((1, width), F32)] * 3
    count = tokens // size

    def units(c):
        part = slice(c * size, (c + 1) * size)
        o_t[:, part] = o_ref[part].T
        return hidden_units(h2_ref[part], cot_ref[part], up, down_t)[:2]

    ahead = units(0)
    for c in range(count):
        part = slice(c * size, (c + 1) * size)
        a, du = ahead
        y_ref[part] = (f_ref[part] + dot(a, down[...], NN)).astype(BF16)
        dh2 = dh2_ref[part] + dot(du, up_t[...], NN)
        if c + 1 < count:
            ahead = units(c + 1)
        dy = cot_ref[part].astype(F32)
        xhat = xhat_ref[part]
        dx1 = dy + norm_back(dh2, xhat, inv_ref[part], vec[1:2])
        dx1_ref[part] = dx1
        g_ref[part] = dx1.astype(BF16)
        for n, term in enumerate((dh2 * xhat, dh2, dy)):
            sums[n] = sums[n] + jnp.sum(term, 0, keepdims=True)
    gout[...] = dot(o_t[...], g_ref[...], NN)
    zero = jnp.zeros((1, width), F32)
    gvec[...] = jnp.concatenate([zero, sums[0], zero, sums[1], sums[2], zero, zero, zero], 0)


def own_rows(virt, i, other):
    core = virt[0] % 2
    core = 1 - core if other else core
    return pl.ds(pl.multiple_of(i * 32 + ((virt[0] // 2) % 2) * 16 + core * 8, 8), 8)


def back_kernel(
    per, virt, qkv_ref, prob_ref, g_ref, xhat_t, wqkv, wout, vec, gout, gvec,
    dqkv, keep, send, vec_sums,
    gqkv,
):
    tokens, width = g_ref.shape
    hs = width // HEADS
    scale = hs**-0.5
    every = [(r, h) for r in range(tokens // WIN) for h in range(HEADS)]
    groups = [every[n : n + 2 * per] for n in range(0, len(every), 2 * per)]

    def piece(ref, r, h, part=0):
        return ref[r * WIN : (r + 1) * WIN, part * width + h * hs : part * width + (h + 1) * hs]

    def enter(pairs):
        r = pairs[0][0]
        do = dot(g_ref[r * WIN : (r + per) * WIN], wout[...], NT).astype(BF16)
        dos = [do[(n - r) * WIN : (n - r + 1) * WIN, h * hs : (h + 1) * hs] for n, h in pairs]
        probs = [prob_ref[r, :, h * hs : h * hs + WIN] for r, h in pairs]
        dps = [dot(a, piece(qkv_ref, r, h, 2), NT) for a, (r, h) in zip(dos, pairs)]
        dvs = [dot(p, a, TN).astype(BF16) for p, a in zip(probs, dos)]
        return probs, dps, dvs

    ahead = enter(groups[0])
    for place, pairs in enumerate(groups):
        probs, dps, dvs = ahead
        if place + 1 < len(groups):
            ahead = enter(groups[place + 1])
        dss = []
        for p, dp in zip(probs, dps):
            pf = p.astype(F32)
            ds = pf * (dp - jnp.sum(dp * pf, -1, keepdims=True)) * scale
            dss.append(ds.astype(BF16))
        dqs = [dot(ds, piece(qkv_ref, r, h, 1), NN).astype(BF16) for ds, (r, h) in zip(dss, pairs)]
        dks = [dot(ds, piece(qkv_ref, r, h, 0), TN).astype(BF16) for ds, (r, h) in zip(dss, pairs)]
        for n, (r, h) in enumerate(pairs):
            for part, values in enumerate((dqs, dks, dvs)):
                at = slice(part * width + h * hs, part * width + (h + 1) * hs)
                dqkv[r * WIN : (r + 1) * WIN, at] = values[n]
    both = dot(xhat_t[...], dqkv[...], NN)
    grad, total = both[:width], both[width : width + 1]
    w = wqkv[...].astype(F32)
    cols = jnp.concatenate([
        jnp.broadcast_to(jnp.sum(w * grad, -1, keepdims=True), (width, 64)),
        jnp.broadcast_to(jnp.sum(w * total, -1, keepdims=True), (width, 64)),
    ], 1)
    lines = cols.T
    gain, from_total = lines[0:1], lines[64:65]
    vec_t = vec[...].T
    gqkv[...] = grad * vec_t[:, 0:1] + total * vec_t[:, 2:3]
    rest = gvec[...]
    sums = jnp.concatenate([gain, rest[1:2], from_total, rest[3:]], 0)
    here = twist(virt[0] // 4)
    for i in range(VDP):
        k = twist(i) ^ here
        mine, other = own_rows(virt, i, 0), own_rows(virt, i, 1)
        theirs = []
        for part in range(3):
            at = slice(part * width, (part + 1) * width)
            keep[k, part * 8 : part * 8 + 8] = gqkv[mine, at]
            theirs.append(gqkv[other, at])
        keep[k, 24:] = gout[mine]
        at = pl.ds(pl.multiple_of(k * 32, 32), 32)
        send[at] = jnp.concatenate(theirs + [gout[other]], 0).astype(BF16)
    vec_sums[...] = sums
    send[VDP * 32 :] = sums.astype(BF16)


def token_grad_kernel(per, me, dqkv, wqkv, vec, xhat_ref, inv_ref, dx1_ref, y, y_near, gx, gxb, out, turned, sems):
    own = dqkv.shape[0]
    size = per * WIN
    copies = []
    for n, source in enumerate((y, y_near)):
        at = pl.ds((lax.rem(me[0], 2) ^ n) * own, own)
        copies.append(pltpu.make_async_copy(source, out.at[at], sems.at[n]))
        copies[-1].start()
    turned[...] = wqkv[...].T
    for c in range(own // size):
        part = slice(c * size, (c + 1) * size)
        dh1 = dot(dqkv[part], turned[...], NN)
        values = dx1_ref[part] + norm_back(dh1, xhat_ref[part], inv_ref[part], vec[0:1])
        gx[part] = values
        gxb[part] = values.astype(BF16)
    for copy in copies:
        copy.wait()


def place_kernel(per, me, mine, theirs, out, wide, sems):
    own = theirs.shape[0]
    size = per * WIN
    here = lax.rem(me[0], 2) * own
    copies = [pltpu.make_async_copy(mine, out.at[pl.ds(here, own)], sems.at[own // size])]
    copies[0].start()
    for c in range(own // size):
        part = pl.ds(c * size, size)
        wide[part] = theirs[part].astype(F32)
        at = pl.ds(own - here + c * size, size)
        copies.append(pltpu.make_async_copy(wide.at[part], out.at[at], sems.at[c]))
        copies[-1].start()
    for copy in copies:
        copy.wait()


def finish_kernel(me, keep_a, keep_b, sums, *refs):
    qkv, out, gains, biases, up, down = refs[3:]
    small, width = out.shape
    tall = up.shape[0]
    high = 4 * small + 8
    total, vec = keep_a[0], sums[...]
    for got in refs[:3]:
        total = total + got[: 4 * small].astype(F32)
        vec = vec + got[4 * small : high].astype(F32)
    units = keep_b[0] + refs[0][high:].astype(F32)
    for part in range(3):
        qkv[:, part * width : (part + 1) * width] = total[part * small : (part + 1) * small]
    out[...] = total[3 * small :]
    vec = pltpu.roll(vec, width - me[0] * small, 1)[:, :small]
    gains[...] = vec[:2]
    biases[...] = vec[2:5]
    up[...] = units[:tall]
    down[...] = units[tall:]


def swap(block, axis, bit):
    size = lax.axis_size(axis)
    return lax.ppermute(block, axis, [(i, i ^ bit) for i in range(size)])


def steps_of(axis):
    return [(axis, 1 << k) for k in reversed(range(lax.axis_size(axis).bit_length() - 1))]


def after(value, other):
    return lax.optimization_barrier((value, other))[0]


def merge(pieces):
    vec = sum(piece[-8:] for piece in pieces)
    return jnp.concatenate([piece[:-8] for piece in pieces] + [vec], 0)


def halves(held):
    half = held.shape[0] // 2
    return held[:half], held[half:].astype(BF16)


def fold_step(keep, send, axis, bit, past=None):
    got = swap(send, axis, bit)
    return keep + (got if past is None else after(got, past)).astype(F32)


def bit_reverse(index, count):
    out = 0 * index
    for k in range(count):
        out = out | (((index >> k) & 1) << (count - 1 - k))
    return out


def by_device(block, me):
    blocks = block[None]
    for axis, bit in steps_of("dp") + steps_of("tensor"):
        blocks = jnp.concatenate([blocks, swap(blocks, axis, bit)], 0)
    count = blocks.shape[0]
    order = jnp.arange(count, dtype=jnp.int32) ^ me
    return jnp.take(blocks, bit_reverse(order, count.bit_length() - 1), axis=0)


def other_pack(w_qkv, w_out, gains, biases, w_up, w_down, me):
    small, width = w_out.shape
    qkv = w_qkv.reshape(small, 3, width).transpose(1, 0, 2).reshape(3 * small, width)
    rows = jnp.concatenate([gains, biases], 0)
    place = jnp.zeros((8, width), BF16)
    place = lax.dynamic_update_slice(place, rows, (jnp.int32(0), me * small))
    return jnp.concatenate([qkv, w_out, place], 0), jnp.concatenate([w_up, w_down.T], 0)


def other_blocks(a, b, me, n_dp, n_t):
    a = by_device(a, me)
    b = by_device(b, me)
    width = a.shape[2]
    count = n_dp * n_t
    small = width // count
    big = width // (VDP * VT)
    mats = a[:, : 4 * small].reshape(count, 4, small, width).transpose(1, 0, 2, 3)
    mats = mats.reshape(4, VDP * VT, big, width).transpose(1, 0, 2, 3).reshape(VDP * VT, 4 * big, width)
    vec = jnp.sum(a[:, 4 * small :].astype(F32), 0).astype(BF16)
    a = mats
    tall = width // n_dp
    b = b.reshape(n_dp, VT, 2, tall, width).transpose(1, 2, 0, 3, 4)
    b = b.reshape(VT, 2, VDP, width // VDP, width).transpose(2, 0, 1, 3, 4)
    b = b.reshape(VDP * VT, 2 * (width // VDP), width)

    y_own = (me // 2) % 2

    def placed(blocks):
        pairs = blocks.reshape((CHIPS, 2) + blocks.shape[1:])
        chips = sorted(range(CHIPS), key=spot)
        pairs = jnp.stack([pairs[m] for m in chips], 0)
        pairs = jnp.where(y_own == 1, jnp.roll(pairs, VDP, 0), pairs)
        return pairs[:, 0], pairs[:, 1]

    held_a, got_a = (part.reshape(-1, width) for part in placed(a))
    held_a = jnp.concatenate([held_a, vec], 0)
    got_a = jnp.concatenate([got_a, jnp.zeros_like(vec)], 0)
    return (held_a, got_a) + placed(b)


def other_reduce(pair_a, pair_b, sums, me, n_dp, n_t):
    count = n_dp * n_t
    y_own = (me // 2) % 2

    def whole(keep, send):
        pairs = jnp.stack([keep, send.astype(F32)], 1)
        pairs = jnp.stack([pairs[twist(i)] for i in range(VDP)], 0)
        none = jnp.zeros_like(pairs)
        both = jnp.stack([jnp.where(y_own == y, pairs, none) for y in range(2)], 1)
        return both.reshape((VDP * VT,) + keep.shape[1:])

    def rows_of(blocks, parts):
        big = blocks.shape[1] // parts
        mats = blocks.reshape(VDP * VT, parts, big, -1).transpose(1, 0, 2, 3)
        mats = mats.reshape(parts, count, VDP * VT * big // count, -1).transpose(1, 0, 2, 3)
        return mats.reshape(count, -1, blocks.shape[2])

    a, b = whole(*pair_a), whole(*pair_b)
    width = a.shape[2]
    tall, high = width // n_dp, width // VDP
    cols = b.reshape(VDP, VT, 2, high, width).transpose(1, 2, 0, 3, 4)
    cols = cols.reshape(VT, 2, n_dp, tall, width).transpose(2, 0, 1, 3, 4)
    cols = cols.reshape(count, 2 * tall, width)
    vec = jnp.broadcast_to(jnp.where(y_own == 0, sums, 0.0)[None], (count,) + sums.shape)
    a = jnp.concatenate([rows_of(a, 4), vec], 1)
    results = []
    for blocks in (a, cols):
        blocks = jnp.take(blocks, jnp.arange(count, dtype=jnp.int32) ^ me, axis=0)
        for axis, bit in reversed(steps_of("dp") + steps_of("tensor")):
            pairs = blocks.reshape((-1, 2) + blocks.shape[1:])
            got = swap(pairs[:, 1].astype(BF16), axis, bit)
            blocks = pairs[:, 0] + got.astype(F32)
        results.append(blocks[0])
    return results


def struct(shape, dtype):
    return jax.ShapeDtypeStruct(shape, dtype)


def call(kernel, name, args, outs, scratch=(), flops=0, limit=8, hbm_outs=True):
    args = [a if isinstance(a, tuple) else (a, pltpu.VMEM) for a in args]
    moved = sum(a.size * a.dtype.itemsize for a, _ in args)
    spaces = [pl.ANY if hbm_outs and isinstance(o, jax.ShapeDtypeStruct) else pltpu.VMEM for o in outs]
    return pl.pallas_call(
        kernel,
        name=name,
        out_shape=outs,
        in_specs=[pl.BlockSpec(memory_space=space) for _, space in args],
        out_specs=[pl.BlockSpec(memory_space=space) for space in spaces],
        scratch_shapes=list(scratch),
        compiler_params=pltpu.CompilerParams(vmem_limit_bytes=limit * MIB),
        cost_estimate=pl.CostEstimate(flops=flops, bytes_accessed=moved, transcendentals=0),
    )(*[a for a, _ in args])


def on_device(tokens, lengths, row_mask, cotangent, w_qkv, w_out, gains, biases, w_up, w_down):
    images, seq_len, width = tokens.shape
    n_dp, n_t = lax.axis_size("dp"), lax.axis_size("tensor")
    index = lax.axis_index("dp") * n_t + lax.axis_index("tensor")
    me = index.astype(jnp.int32).reshape(1)
    usual = (n_dp, n_t) == (VDP, VT)
    virt = me if usual else (index // 2 % 2 * 2).astype(jnp.int32).reshape(1)
    small = width // (n_dp * n_t)
    tall = width // n_dp
    own = images * seq_len // 2
    rows = own // WIN
    per = 12 if rows % 12 == 0 else 1
    some = 6 if rows % 6 == 0 else 1
    less = 4 if rows % 4 == 0 else 1
    smem = pltpu.SMEM
    weights = (w_qkv, w_out, gains, biases, w_up, w_down)
    token_mm = 2 * own * width
    hbm = pltpu.HBM

    def in_hbm(array):
        return (pltpu.with_memory_space_constraint(array, hbm), hbm)

    def first_norm(x):
        return call(
            first_norm_kernel,
            "first_norm",
            [x],
            [
                pltpu.VMEM((own, width), F32),
                pltpu.VMEM((own, 1), F32),
                pltpu.VMEM((width + 16, own), BF16),
            ],
            limit=4,
        )

    def fetch(me):
        flat = [array.reshape(images * seq_len, width) for array in (cotangent, tokens)]
        return call(
            turn_kernel,
            "turn",
            [(me, smem)] + [in_hbm(array) for array in flat],
            [
                pltpu.VMEM((own, width), BF16),
                pltpu.VMEM((width, own), BF16),
                pltpu.VMEM((own, width), BF16),
            ],
            [pltpu.SemaphoreType.DMA((2,))],
            limit=4,
        )

    if usual:
        weights = (w_qkv, w_out, gains, biases, w_up, w_down.T)
        high = 4 * small + 8
        packed = call(
            pack_kernel,
            "pack",
            [(me, smem)] + [in_hbm(w) for w in weights],
            [pltpu.VMEM((1, high + 2 * tall, width), BF16)],
            [pltpu.VMEM(w.shape, BF16) for w in weights] + [pltpu.SemaphoreType.DMA((6,))],
        )[0]
        planes = [packed] + [swap(packed, "dp", bit) for bit in (2, 4, 6)]
        cot, cot_t, x = fetch(after(me, packed))
        planes[3] = after(planes[3], cot)
        held_a = merge([plane[0, :high] for plane in planes])
        b = jnp.concatenate([plane[:, high:] for plane in planes], 0)
        far_b = swap(b, "tensor", 2)
        held_a = merge([held_a, swap(held_a, "dp", 1)])
        b = jnp.concatenate([b, swap(b, "dp", 1)], 0)
        xhat1, inv1, xhat_t = first_norm(after(x, (held_a, far_b)))
        held_a = merge([held_a, after(swap(held_a, "tensor", 2), (b, xhat1))])
        far_x = swap(far_b, "dp", 1)
        got_a = swap(held_a, "tensor", 1)
        got_b = swap(b, "tensor", 1)
    else:
        held_a, got_a, held_b, got_b = other_blocks(*other_pack(*weights, index), index, n_dp, n_t)
        b, far_b = held_b[:VDP], held_b[VDP:]
        got_b, got_far = got_b[:VDP], got_b[VDP:]
        cot, cot_t, x = fetch(me)
        xhat1, inv1, xhat_t = first_norm(x)
    qkv, prob, o, x1, wqkv, wout, vec = call(
        functools.partial(attend_kernel, some),
        "attend",
        [(me, smem), (virt, smem), (lengths, smem), (row_mask, smem), x, xhat1, held_a, got_a],
        [
            pltpu.VMEM((own, 3 * width), BF16),
            pltpu.VMEM((rows, WIN, width), BF16),
            pltpu.VMEM((own, width), BF16),
            pltpu.VMEM((own, width), F32),
            pltpu.VMEM((width, 3 * width), BF16),
            pltpu.VMEM((width, width), BF16),
            pltpu.VMEM((8, width), F32),
        ],
        flops=token_mm * (4 * width + 2 * WIN),
    )
    tall_b = 2 * (width // VDP)
    mats = [pltpu.VMEM((width, 2 * width), BF16)] * 2 + [pltpu.VMEM((2 * width, width), BF16)] * 2
    if usual:
        far_b = jnp.concatenate([far_b, after(far_x, x1)], 0)
        got_far = swap(far_b, "tensor", 1)
        got_b = after(got_b, far_b)
    wide_per = 8 if rows % 8 == 0 else rows
    *first, keep_b, send_b = call(
        functools.partial(hidden_near_kernel, wide_per),
        "hidden_near",
        [(virt, smem), x1, cot, cot_t, vec, b, got_b],
        [
            pltpu.VMEM((own, width), BF16),
            pltpu.VMEM((own, width), F32),
            pltpu.VMEM((own, 1), F32),
            pltpu.VMEM((own, width), F32),
            pltpu.VMEM((own, width), F32),
            pltpu.VMEM((VDP, tall_b, width), F32),
            pltpu.VMEM((VDP, tall_b, width), BF16),
        ],
        [pltpu.VMEM((own, 2 * width), BF16)] * 2 + [pltpu.VMEM((width, own), BF16)] + mats,
        token_mm * 12 * width,
        12,
    )
    y, dx1, g, gout, gvec = call(
        functools.partial(hidden_far_kernel, wide_per),
        "hidden_far",
        [(virt, smem), cot, vec, far_b, got_far, *first, o],
        [
            pltpu.VMEM((own, width), BF16),
            pltpu.VMEM((own, width), F32),
            pltpu.VMEM((own, width), BF16),
            pltpu.VMEM((width, width), F32),
            pltpu.VMEM((8, width), F32),
        ],
        [pltpu.VMEM((width, own), BF16)] + mats,
        token_mm * 9 * width,
    )
    core, xbit, zhi = ("tensor", 1), ("dp", 1), ("dp", 4)
    if usual:
        held_b = fold_step(keep_b, send_b, *core, g)
        y = after(y, held_b)
    y_near = swap(y, "tensor", 1)
    dqkv, keep_a, send_a, sums = call(
        functools.partial(back_kernel, per),
        "back",
        [(virt, smem), qkv, prob, g, xhat_t, wqkv, wout, vec, gout, gvec],
        [
            pltpu.VMEM((own, 3 * width), BF16),
            pltpu.VMEM((VDP, 32, width), F32),
            pltpu.VMEM((VDP * 32 + 8, width), BF16),
            pltpu.VMEM((8, width), F32),
        ],
        [pltpu.VMEM((width, 3 * width), F32)],
        token_mm * (4 * width + 5 * WIN),
    )
    if usual:
        held_b = fold_step(*halves(held_b), *xbit)
        got = after(swap(send_a, *core), held_b).astype(F32)
        held_a = keep_a + got[:-8].reshape(keep_a.shape)
        sums = sums + got[-8:]
        vec = after(vec, held_a)
    gx, gxb, layer_out = call(
        functools.partial(token_grad_kernel, less),
        "token_grad",
        [(me, smem), dqkv, wqkv, vec, xhat1, inv1, dx1, y, y_near],
        [
            pltpu.VMEM((own, width), F32),
            pltpu.VMEM((own, width), BF16),
            struct((images * seq_len, width), BF16),
        ],
        [pltpu.VMEM((3 * width, width), BF16), pltpu.SemaphoreType.DMA((2,))],
        flops=token_mm * 3 * width,
    )
    layer_out = layer_out.reshape(images, seq_len, width)

    def place(gx_near):
        return call(
            functools.partial(place_kernel, less),
            "place",
            [(me, smem), gx, gx_near],
            [struct((images * seq_len, width), F32)],
            [pltpu.VMEM((own, width), F32), pltpu.SemaphoreType.DMA((rows // less + 1,))],
        )[0].reshape(images, seq_len, width)

    if usual:
        held_b = fold_step(*halves(held_b), *zhi, gxb)
        send_a = jnp.concatenate([held_a[4:].reshape(-1, width), sums], 0).astype(BF16)
        got = after(swap(send_a, *xbit), (gxb, held_b)).astype(F32)
        held_a = held_a[:4] + got[:-8].reshape(4, -1, width)
        sums = sums + got[-8:]
        got = [
            swap(jnp.concatenate([held_a[n], sums] + more, 0).astype(BF16), "dp", 2 * n)
            for n, more in ((1, [held_b[1]]), (2, []), (3, []))
        ]
        grad_tokens = place(swap(after(gxb, held_a), "tensor", 1))
        got[2] = after(got[2], grad_tokens)
        shapes = ((small, 3 * width), (small, width), (2, small), (3, small), (tall, width), (tall, width))
        o_qkv, o_out, o_gains, o_bias, o_up, o_down = call(
            finish_kernel,
            "finish",
            [(me, smem), held_a, held_b, sums, *got],
            [struct(shape, F32) for shape in shapes],
            limit=2,
            hbm_outs=False,
        )
    else:
        grad_tokens = place(swap(gxb, "tensor", 1))
        send_a = send_a[:-8].reshape(keep_a.shape)
        grad_a, grad_b = other_reduce((keep_a, send_a), (keep_b, send_b), sums, index, n_dp, n_t)
        o_qkv = jnp.concatenate([grad_a[p * small : (p + 1) * small] for p in range(3)], 1)
        o_out = grad_a[3 * small : 4 * small]
        o_vec = lax.dynamic_slice_in_dim(grad_a[4 * small : 4 * small + 5], index * small, small, 1)
        o_gains, o_bias = o_vec[:2], o_vec[2:]
        o_up, o_down = grad_b[:tall], grad_b[tall:]
    return layer_out, grad_tokens, o_qkv, o_out, o_gains, o_bias, o_up, o_down.T


def solution(mesh):
    in_specs = (
        P("dp", None, None),
        P("dp"),
        P("dp", None),
        P("dp", None, None),
        P(("dp", "tensor"), None),
        P(("dp", "tensor"), None),
        P(None, ("dp", "tensor")),
        P(None, ("dp", "tensor")),
        P("dp", "tensor"),
        P("tensor", "dp"),
    )
    out_specs = (
        P("dp", None, None),
        P("dp", None, None),
        P(("dp", "tensor"), None),
        P(("dp", "tensor"), None),
        P(None, ("dp", "tensor")),
        P(None, ("dp", "tensor")),
        P("dp", "tensor"),
        P("tensor", "dp"),
    )
    return jax.shard_map(
        on_device, mesh=mesh, in_specs=in_specs, out_specs=out_specs, check_vma=False
    )
```

```python
import functools

import jax
import jax.numpy as jnp
from jax import lax
from jax.experimental import pallas as pl
from jax.experimental.pallas import tpu as pltpu
from jax.sharding import PartitionSpec as P

HEADS = 2
WIN = 96
F32 = jnp.float32
BF16 = jnp.bfloat16
VDP, VT = 8, 4
CHIPS = VDP * VT // 2
MIB = 1 << 20

NN = ((1,), (0,))
NT = ((1,), (1,))
TN = ((0,), (0,))


def dot(a, b, dims):
    return lax.dot_general(a, b, (dims, ((), ())), preferred_element_type=F32)


def twist(i):
    return (i & 1) * 4 + (i >> 1)


def turn(i):
    return ((i & 1) << 2) | (i & 2) | ((i & 4) >> 2)


def spot(m):
    return (m % 2) * VDP + twist(m // 2)


def norm_parts(values):
    center = values - jnp.mean(values, -1, keepdims=True)
    inv = lax.rsqrt(jnp.mean(center * center, -1, keepdims=True) + 1e-05)
    return center * inv, inv


def norm_back(grad, xhat, inv, gain):
    scaled = grad * gain
    return inv * (
        scaled
        - jnp.mean(scaled, -1, keepdims=True)
        - xhat * jnp.mean(scaled * xhat, -1, keepdims=True)
    )


def gelu_both(u):
    c = 0.7978845608028654
    u2 = u * u
    t = jnp.tanh(u * (c + (c * 0.044715) * u2))
    half = 0.5 + 0.5 * t
    value = u * half
    slope = half + (value - value * half) * (2 * c + (6 * c * 0.044715) * u2)
    return value, slope


def apart(both, hs):
    blocks = []
    for h in range(HEADS):
        parts = [jnp.zeros((WIN, hs), BF16)] * HEADS
        parts[h] = both[:, h * hs : (h + 1) * hs]
        blocks.append(jnp.concatenate(parts, 1))
        blocks.append(jnp.zeros((hs - WIN, HEADS * hs), BF16))
    return jnp.concatenate(blocks, 0)


def pack_kernel(me, *refs):
    sources, packed, held, sems = refs[:6], refs[6], refs[7:13], refs[13]
    copies = [pltpu.make_async_copy(a, b, sems.at[n]) for n, (a, b) in enumerate(zip(sources, held))]
    for copy in copies:
        copy.start()
    qkv, out, gains, biases, up, down = held
    small, width = out.shape
    tall = up.shape[0]
    lane = lax.broadcasted_iota(jnp.int32, (1, width), 1)
    mine = lane // small == me[0]
    for copy in copies:
        copy.wait()
    for part in range(3):
        packed[0, part * small : (part + 1) * small] = qkv[:, part * width : (part + 1) * width]
    packed[0, 3 * small : 4 * small] = out[...]
    rows = [gains[0:1], gains[1:2], biases[0:1], biases[1:2], biases[2:3]]
    vals = jnp.concatenate(rows + [jnp.zeros((3, small), BF16)], 0).astype(F32)
    wide = jnp.concatenate([vals] * (width // small), 1)
    at = 4 * small + 8
    packed[0, 4 * small : at] = jnp.where(mine, wide, 0.0).astype(BF16)
    packed[0, at : at + tall] = up[...]
    packed[0, at + tall :] = down[...]


def turn_kernel(me, cot, tokens, cot_ref, cot_t, x_ref, sems):
    own = cot_ref.shape[0]
    at = pl.ds(lax.rem(me[0], 2) * own, own)
    copies = [
        pltpu.make_async_copy(cot.at[at], cot_ref, sems.at[0]),
        pltpu.make_async_copy(tokens.at[at], x_ref, sems.at[1]),
    ]
    for copy in copies:
        copy.start()
    size = 256 if own % 256 == 0 else own
    copies[0].wait()
    for n in range(own // size):
        part = slice(n * size, (n + 1) * size)
        cot_t[:, part] = cot_ref[part].T
    copies[1].wait()


def first_norm_kernel(x_ref, xhat_ref, inv_ref, xhat_t):
    own, width = x_ref.shape
    ones = jnp.full((width, width), 1.0 / width, BF16)
    size = 256 if own % 256 == 0 else own
    for n in range(own // size):
        part = slice(n * size, (n + 1) * size)
        x = x_ref[part]
        center = x.astype(F32) - dot(x, ones, NN)
        inv = lax.rsqrt(dot((center * center).astype(BF16), ones, NN) + 1e-05)
        xhat = center * inv
        xhat_ref[part] = xhat
        inv_ref[part] = inv[:, :1]
        xhat_t[:width, part] = xhat.astype(BF16).T
        xhat_t[width:, part] = jnp.ones((16, size), BF16)


def attend_kernel(
    per, me, virt, lens, live, x_ref, xhat_ref, held, got,
    qkv_ref, prob_ref, o_ref, x1_ref, wqkv, wout, vec,
):
    tokens, width = x_ref.shape
    rows = tokens // WIN
    hs = width // HEADS
    here = twist(virt[0] // 4)
    y_own = (virt[0] // 2) % 2
    first = virt[0] % 2 == 0
    for m in range(CHIPS):
        k = spot(m) ^ (here + y_own * VDP)
        at = pl.ds(pl.multiple_of(k * 32, 32), 32)
        a = held[at].astype(F32)
        b = got[at].astype(F32)
        even = jnp.where(first, a, b)
        odd = jnp.where(first, b, a)
        for part in range(3):
            both = jnp.concatenate([even[part * 8 : part * 8 + 8], odd[part * 8 : part * 8 + 8]], 0)
            wqkv[m * 16 : m * 16 + 16, part * width : (part + 1) * width] = both.astype(BF16)
        both = jnp.concatenate([even[24:32], odd[24:32]], 0)
        wout[m * 16 : m * 16 + 16] = both.astype(BF16)
    total = held[CHIPS * 32 :].astype(F32) + got[CHIPS * 32 :].astype(F32)
    vec[...] = total
    scale = hs**-0.5
    ii = lax.broadcasted_iota(jnp.int32, (WIN, hs), 0)
    jj = lax.broadcasted_iota(jnp.int32, (WIN, hs), 1)
    same = ii == jj
    image_rows = live.shape[1]
    base = lax.rem(me[0], 2) * rows

    def enter(c):
        part = slice(c * per * WIN, (c + 1) * per * WIN)
        h1 = (xhat_ref[part] * total[0:1] + total[2:3]).astype(BF16)
        qkv = dot(h1, wqkv[...], NN).astype(BF16)
        qkv_ref[part] = qkv
        scores = []
        for r in range(per):
            at = slice(r * WIN, (r + 1) * WIN)
            scores.append(dot(qkv[at, :width], apart(qkv[at, width : 2 * width], hs), NT))
        return qkv, scores

    ahead = enter(0)
    for c in range(rows // per):
        qkv, scores = ahead
        if c + 1 < rows // per:
            ahead = enter(c + 1)
        part = slice(c * per * WIN, (c + 1) * per * WIN)
        probs = []
        for r in range(per):
            row = base + c * per + r
            image = row // image_rows
            inside = row - image * image_rows
            reach = jnp.where(live[image, inside] == 1, lens[image] - inside * WIN, 0)
            allowed = same | (jj < jnp.minimum(ii, reach))
            heads = []
            for h in range(HEADS):
                s = jnp.where(allowed, scores[r][:, h * hs : (h + 1) * hs], -1e30)
                e = jnp.exp((s - jnp.max(s, -1, keepdims=True)) * scale)
                heads.append((e * (1.0 / jnp.sum(e, -1, keepdims=True))).astype(BF16))
            probs.append(jnp.concatenate(heads, 1))
        mixed = []
        for r in range(per):
            at = slice(r * WIN, (r + 1) * WIN)
            mixed.append(dot(probs[r], apart(qkv[at, 2 * width :], hs), NN).astype(BF16))
        o = jnp.concatenate(mixed, 0)
        for n, p in enumerate(probs):
            prob_ref[c * per + n] = p
        o_ref[part] = o
        x1_ref[part] = x_ref[part].astype(F32) + dot(o, wout[...], NN)


def join(virt, blocks, n, up, down_t):
    tall = blocks.shape[1] // 2
    width = up.shape[0]
    here = twist(virt[0] // 4)
    for i in range(VDP):
        k = twist(i) ^ here
        at = slice(i * tall, (i + 1) * tall)
        cols = slice(n * width, (n + 1) * width)
        up[at, cols] = blocks[k, :tall]
        down_t[at, cols] = blocks[k, tall:]


def hidden_units(h2, dyb, up, down_t, between=None):
    u = dot(h2, up[...], NN).astype(BF16)
    da = dot(dyb, down_t[...], NN).astype(BF16)
    done = between() if between is not None else None
    a, slope = gelu_both(u)
    return a, da * slope, done


def hidden_near_kernel(
    per, virt, x1_ref, cot_ref, cot_t, vec, own, got,
    h2_ref, xhat_ref, inv_ref, f_ref, dh2_ref, keep, send,
    a_ref, du_ref, h2_t, up, down_t, up_t, down,
):
    tokens, width = x1_ref.shape
    size = per * WIN
    join(virt, own, 0, up, down_t)
    join(virt, got, 1, up, down_t)
    up_t[...] = up[...].T
    down[...] = down_t[...].T
    count = tokens // size

    def norm(c):
        part = slice(c * size, (c + 1) * size)
        xhat, inv = norm_parts(x1_ref[part])
        xhat_ref[part] = xhat
        inv_ref[part] = inv
        h2 = (xhat * vec[1:2] + vec[3:4]).astype(BF16)
        h2_ref[part] = h2
        h2_t[:, part] = h2.T
        return h2

    h2 = norm(0)
    for c in range(count):
        part = slice(c * size, (c + 1) * size)
        later = functools.partial(norm, c + 1) if c + 1 < count else None
        a, du, h2 = hidden_units(h2, cot_ref[part], up, down_t, later)
        a_ref[part] = a
        du_ref[part] = du
        f_ref[part] = x1_ref[part] + vec[4:5] + dot(a, down[...], NN)
        dh2_ref[part] = dot(du, up_t[...], NN)
    gdown = dot(cot_t[...], a_ref[...], NN)
    gup = dot(h2_t[...], du_ref[...], NN)
    tall = width // VDP
    here = turn(virt[0] // 4)
    for i in range(VDP):
        at = slice(i * tall, (i + 1) * tall)
        k = turn(i) ^ here
        keep[k, :tall] = gup[at, :width]
        keep[k, tall:] = gdown[at, :width]
        send[k, :tall] = gup[at, width:].astype(BF16)
        send[k, tall:] = gdown[at, width:].astype(BF16)


def hidden_far_kernel(
    per, virt, cot_ref, vec, own, got, h2_ref, xhat_ref, inv_ref, f_ref, dh2_ref, o_ref,
    y_ref, dx1_ref, g_ref, gout, gvec,
    o_t, up, down_t, up_t, down,
):
    tokens, width = h2_ref.shape
    size = per * WIN
    join(virt, own, 0, up, down_t)
    join(virt, got, 1, up, down_t)
    up_t[...] = up[...].T
    down[...] = down_t[...].T
    sums = [jnp.zeros((1, width), F32)] * 3
    count = tokens // size

    def units(c):
        part = slice(c * size, (c + 1) * size)
        o_t[:, part] = o_ref[part].T
        return hidden_units(h2_ref[part], cot_ref[part], up, down_t)[:2]

    ahead = units(0)
    for c in range(count):
        part = slice(c * size, (c + 1) * size)
        a, du = ahead
        y_ref[part] = (f_ref[part] + dot(a, down[...], NN)).astype(BF16)
        dh2 = dh2_ref[part] + dot(du, up_t[...], NN)
        if c + 1 < count:
            ahead = units(c + 1)
        dy = cot_ref[part].astype(F32)
        xhat = xhat_ref[part]
        dx1 = dy + norm_back(dh2, xhat, inv_ref[part], vec[1:2])
        dx1_ref[part] = dx1
        g_ref[part] = dx1.astype(BF16)
        for n, term in enumerate((dh2 * xhat, dh2, dy)):
            sums[n] = sums[n] + jnp.sum(term, 0, keepdims=True)
    gout[...] = dot(o_t[...], g_ref[...], NN)
    zero = jnp.zeros((1, width), F32)
    gvec[...] = jnp.concatenate([zero, sums[0], zero, sums[1], sums[2], zero, zero, zero], 0)


def own_rows(virt, i, other):
    core = virt[0] % 2
    core = 1 - core if other else core
    return pl.ds(pl.multiple_of(i * 32 + ((virt[0] // 2) % 2) * 16 + core * 8, 8), 8)


def back_kernel(
    per, virt, qkv_ref, prob_ref, g_ref, xhat_t, wqkv, wout, vec, gout, gvec,
    dqkv, keep, send, vec_sums,
    gqkv,
):
    tokens, width = g_ref.shape
    hs = width // HEADS
    scale = hs**-0.5
    every = [(r, h) for r in range(tokens // WIN) for h in range(HEADS)]
    groups = [every[n : n + 2 * per] for n in range(0, len(every), 2 * per)]

    def piece(ref, r, h, part=0):
        return ref[r * WIN : (r + 1) * WIN, part * width + h * hs : part * width + (h + 1) * hs]

    def enter(pairs):
        r = pairs[0][0]
        do = dot(g_ref[r * WIN : (r + per) * WIN], wout[...], NT).astype(BF16)
        dos = [do[(n - r) * WIN : (n - r + 1) * WIN, h * hs : (h + 1) * hs] for n, h in pairs]
        probs = [prob_ref[r, :, h * hs : h * hs + WIN] for r, h in pairs]
        dps = [dot(a, piece(qkv_ref, r, h, 2), NT) for a, (r, h) in zip(dos, pairs)]
        dvs = [dot(p, a, TN).astype(BF16) for p, a in zip(probs, dos)]
        return probs, dps, dvs

    ahead = enter(groups[0])
    for place, pairs in enumerate(groups):
        probs, dps, dvs = ahead
        if place + 1 < len(groups):
            ahead = enter(groups[place + 1])
        dss = []
        for p, dp in zip(probs, dps):
            pf = p.astype(F32)
            ds = pf * (dp - jnp.sum(dp * pf, -1, keepdims=True)) * scale
            dss.append(ds.astype(BF16))
        dqs = [dot(ds, piece(qkv_ref, r, h, 1), NN).astype(BF16) for ds, (r, h) in zip(dss, pairs)]
        dks = [dot(ds, piece(qkv_ref, r, h, 0), TN).astype(BF16) for ds, (r, h) in zip(dss, pairs)]
        for n, (r, h) in enumerate(pairs):
            for part, values in enumerate((dqs, dks, dvs)):
                at = slice(part * width + h * hs, part * width + (h + 1) * hs)
                dqkv[r * WIN : (r + 1) * WIN, at] = values[n]
    both = dot(xhat_t[...], dqkv[...], NN)
    grad, total = both[:width], both[width : width + 1]
    w = wqkv[...].astype(F32)
    cols = jnp.concatenate([
        jnp.broadcast_to(jnp.sum(w * grad, -1, keepdims=True), (width, 64)),
        jnp.broadcast_to(jnp.sum(w * total, -1, keepdims=True), (width, 64)),
    ], 1)
    lines = cols.T
    gain, from_total = lines[0:1], lines[64:65]
    vec_t = vec[...].T
    gqkv[...] = grad * vec_t[:, 0:1] + total * vec_t[:, 2:3]
    rest = gvec[...]
    sums = jnp.concatenate([gain, rest[1:2], from_total, rest[3:]], 0)
    here = twist(virt[0] // 4)
    for i in range(VDP):
        k = twist(i) ^ here
        mine, other = own_rows(virt, i, 0), own_rows(virt, i, 1)
        theirs = []
        for part in range(3):
            at = slice(part * width, (part + 1) * width)
            keep[k, part * 8 : part * 8 + 8] = gqkv[mine, at]
            theirs.append(gqkv[other, at])
        keep[k, 24:] = gout[mine]
        at = pl.ds(pl.multiple_of(k * 32, 32), 32)
        send[at] = jnp.concatenate(theirs + [gout[other]], 0).astype(BF16)
    vec_sums[...] = sums
    send[VDP * 32 :] = sums.astype(BF16)


def token_grad_kernel(per, me, dqkv, wqkv, vec, xhat_ref, inv_ref, dx1_ref, y, y_near, gx, gxb, out, turned, sems):
    own = dqkv.shape[0]
    size = per * WIN
    copies = []
    for n, source in enumerate((y, y_near)):
        at = pl.ds((lax.rem(me[0], 2) ^ n) * own, own)
        copies.append(pltpu.make_async_copy(source, out.at[at], sems.at[n]))
        copies[-1].start()
    turned[...] = wqkv[...].T
    for c in range(own // size):
        part = slice(c * size, (c + 1) * size)
        dh1 = dot(dqkv[part], turned[...], NN)
        values = dx1_ref[part] + norm_back(dh1, xhat_ref[part], inv_ref[part], vec[0:1])
        gx[part] = values
        gxb[part] = values.astype(BF16)
    for copy in copies:
        copy.wait()


def place_kernel(per, me, mine, theirs, out, wide, sems):
    own = theirs.shape[0]
    size = per * WIN
    here = lax.rem(me[0], 2) * own
    copies = [pltpu.make_async_copy(mine, out.at[pl.ds(here, own)], sems.at[own // size])]
    copies[0].start()
    for c in range(own // size):
        part = pl.ds(c * size, size)
        wide[part] = theirs[part].astype(F32)
        at = pl.ds(own - here + c * size, size)
        copies.append(pltpu.make_async_copy(wide.at[part], out.at[at], sems.at[c]))
        copies[-1].start()
    for copy in copies:
        copy.wait()


def finish_kernel(me, keep_a, keep_b, sums, *refs):
    qkv, out, gains, biases, up, down = refs[3:]
    small, width = out.shape
    tall = up.shape[0]
    high = 4 * small + 8
    total, vec = keep_a[0], sums[...]
    for got in refs[:3]:
        total = total + got[: 4 * small].astype(F32)
        vec = vec + got[4 * small : high].astype(F32)
    units = keep_b[0] + refs[1][high:].astype(F32)
    for part in range(3):
        qkv[:, part * width : (part + 1) * width] = total[part * small : (part + 1) * small]
    out[...] = total[3 * small :]
    vec = pltpu.roll(vec, width - me[0] * small, 1)[:, :small]
    gains[...] = vec[:2]
    biases[...] = vec[2:5]
    up[...] = units[:tall]
    down[...] = units[tall:]


def swap(block, axis, bit):
    size = lax.axis_size(axis)
    return lax.ppermute(block, axis, [(i, i ^ bit) for i in range(size)])


def steps_of(axis):
    return [(axis, 1 << k) for k in reversed(range(lax.axis_size(axis).bit_length() - 1))]


def after(value, other):
    return lax.optimization_barrier((value, other))[0]


def merge(pieces):
    vec = sum(piece[-8:] for piece in pieces)
    return jnp.concatenate([piece[:-8] for piece in pieces] + [vec], 0)


def halves(held):
    half = held.shape[0] // 2
    return held[:half], held[half:].astype(BF16)


def fold_step(keep, send, axis, bit, past=None):
    got = swap(send, axis, bit)
    return keep + (got if past is None else after(got, past)).astype(F32)


def bit_reverse(index, count):
    out = 0 * index
    for k in range(count):
        out = out | (((index >> k) & 1) << (count - 1 - k))
    return out


def by_device(block, me):
    blocks = block[None]
    for axis, bit in steps_of("dp") + steps_of("tensor"):
        blocks = jnp.concatenate([blocks, swap(blocks, axis, bit)], 0)
    count = blocks.shape[0]
    order = jnp.arange(count, dtype=jnp.int32) ^ me
    return jnp.take(blocks, bit_reverse(order, count.bit_length() - 1), axis=0)


def other_pack(w_qkv, w_out, gains, biases, w_up, w_down, me):
    small, width = w_out.shape
    qkv = w_qkv.reshape(small, 3, width).transpose(1, 0, 2).reshape(3 * small, width)
    rows = jnp.concatenate([gains, biases], 0)
    place = jnp.zeros((8, width), BF16)
    place = lax.dynamic_update_slice(place, rows, (jnp.int32(0), me * small))
    return jnp.concatenate([qkv, w_out, place], 0), jnp.concatenate([w_up, w_down.T], 0)


def other_blocks(a, b, me, n_dp, n_t):
    a = by_device(a, me)
    b = by_device(b, me)
    width = a.shape[2]
    count = n_dp * n_t
    small = width // count
    big = width // (VDP * VT)
    mats = a[:, : 4 * small].reshape(count, 4, small, width).transpose(1, 0, 2, 3)
    mats = mats.reshape(4, VDP * VT, big, width).transpose(1, 0, 2, 3).reshape(VDP * VT, 4 * big, width)
    vec = jnp.sum(a[:, 4 * small :].astype(F32), 0).astype(BF16)
    a = mats
    tall = width // n_dp
    b = b.reshape(n_dp, VT, 2, tall, width).transpose(1, 2, 0, 3, 4)
    b = b.reshape(VT, 2, VDP, width // VDP, width).transpose(2, 0, 1, 3, 4)
    b = b.reshape(VDP * VT, 2 * (width // VDP), width)

    y_own = (me // 2) % 2

    def placed(blocks):
        pairs = blocks.reshape((CHIPS, 2) + blocks.shape[1:])
        chips = sorted(range(CHIPS), key=spot)
        pairs = jnp.stack([pairs[m] for m in chips], 0)
        pairs = jnp.where(y_own == 1, jnp.roll(pairs, VDP, 0), pairs)
        return pairs[:, 0], pairs[:, 1]

    held_a, got_a = (part.reshape(-1, width) for part in placed(a))
    held_a = jnp.concatenate([held_a, vec], 0)
    got_a = jnp.concatenate([got_a, jnp.zeros_like(vec)], 0)
    return (held_a, got_a) + placed(b)


def other_reduce(pair_a, pair_b, sums, me, n_dp, n_t):
    count = n_dp * n_t
    y_own = (me // 2) % 2

    def whole(keep, send, order):
        pairs = jnp.stack([keep, send.astype(F32)], 1)
        pairs = jnp.stack([pairs[order(i)] for i in range(VDP)], 0)
        none = jnp.zeros_like(pairs)
        both = jnp.stack([jnp.where(y_own == y, pairs, none) for y in range(2)], 1)
        return both.reshape((VDP * VT,) + keep.shape[1:])

    def rows_of(blocks, parts):
        big = blocks.shape[1] // parts
        mats = blocks.reshape(VDP * VT, parts, big, -1).transpose(1, 0, 2, 3)
        mats = mats.reshape(parts, count, VDP * VT * big // count, -1).transpose(1, 0, 2, 3)
        return mats.reshape(count, -1, blocks.shape[2])

    a, b = whole(*pair_a, twist), whole(*pair_b, turn)
    width = a.shape[2]
    tall, high = width // n_dp, width // VDP
    cols = b.reshape(VDP, VT, 2, high, width).transpose(1, 2, 0, 3, 4)
    cols = cols.reshape(VT, 2, n_dp, tall, width).transpose(2, 0, 1, 3, 4)
    cols = cols.reshape(count, 2 * tall, width)
    vec = jnp.broadcast_to(jnp.where(y_own == 0, sums, 0.0)[None], (count,) + sums.shape)
    a = jnp.concatenate([rows_of(a, 4), vec], 1)
    results = []
    for blocks in (a, cols):
        blocks = jnp.take(blocks, jnp.arange(count, dtype=jnp.int32) ^ me, axis=0)
        for axis, bit in reversed(steps_of("dp") + steps_of("tensor")):
            pairs = blocks.reshape((-1, 2) + blocks.shape[1:])
            got = swap(pairs[:, 1].astype(BF16), axis, bit)
            blocks = pairs[:, 0] + got.astype(F32)
        results.append(blocks[0])
    return results


def struct(shape, dtype):
    return jax.ShapeDtypeStruct(shape, dtype)


def call(kernel, name, args, outs, scratch=(), flops=0, limit=8, hbm_outs=True):
    args = [a if isinstance(a, tuple) else (a, pltpu.VMEM) for a in args]
    moved = sum(a.size * a.dtype.itemsize for a, _ in args)
    spaces = [pl.ANY if hbm_outs and isinstance(o, jax.ShapeDtypeStruct) else pltpu.VMEM for o in outs]
    return pl.pallas_call(
        kernel,
        name=name,
        out_shape=outs,
        in_specs=[pl.BlockSpec(memory_space=space) for _, space in args],
        out_specs=[pl.BlockSpec(memory_space=space) for space in spaces],
        scratch_shapes=list(scratch),
        compiler_params=pltpu.CompilerParams(vmem_limit_bytes=limit * MIB),
        cost_estimate=pl.CostEstimate(flops=flops, bytes_accessed=moved, transcendentals=0),
    )(*[a for a, _ in args])


def on_device(tokens, lengths, row_mask, cotangent, w_qkv, w_out, gains, biases, w_up, w_down):
    images, seq_len, width = tokens.shape
    n_dp, n_t = lax.axis_size("dp"), lax.axis_size("tensor")
    index = lax.axis_index("dp") * n_t + lax.axis_index("tensor")
    me = index.astype(jnp.int32).reshape(1)
    usual = (n_dp, n_t) == (VDP, VT)
    virt = me if usual else (index // 2 % 2 * 2).astype(jnp.int32).reshape(1)
    small = width // (n_dp * n_t)
    tall = width // n_dp
    own = images * seq_len // 2
    rows = own // WIN
    per = 12 if rows % 12 == 0 else 1
    some = 6 if rows % 6 == 0 else 1
    less = 4 if rows % 4 == 0 else 1
    smem = pltpu.SMEM
    weights = (w_qkv, w_out, gains, biases, w_up, w_down)
    token_mm = 2 * own * width
    hbm = pltpu.HBM

    def in_hbm(array):
        return (pltpu.with_memory_space_constraint(array, hbm), hbm)

    def first_norm(x):
        return call(
            first_norm_kernel,
            "first_norm",
            [x],
            [
                pltpu.VMEM((own, width), F32),
                pltpu.VMEM((own, 1), F32),
                pltpu.VMEM((width + 16, own), BF16),
            ],
            limit=4,
        )

    def fetch(me):
        flat = [array.reshape(images * seq_len, width) for array in (cotangent, tokens)]
        return call(
            turn_kernel,
            "turn",
            [(me, smem)] + [in_hbm(array) for array in flat],
            [
                pltpu.VMEM((own, width), BF16),
                pltpu.VMEM((width, own), BF16),
                pltpu.VMEM((own, width), BF16),
            ],
            [pltpu.SemaphoreType.DMA((2,))],
            limit=4,
        )

    if usual:
        weights = (w_qkv, w_out, gains, biases, w_up, w_down.T)
        high = 4 * small + 8
        packed = call(
            pack_kernel,
            "pack",
            [(me, smem)] + [in_hbm(w) for w in weights],
            [pltpu.VMEM((1, high + 2 * tall, width), BF16)],
            [pltpu.VMEM(w.shape, BF16) for w in weights] + [pltpu.SemaphoreType.DMA((6,))],
        )[0]
        planes = [packed] + [swap(packed, "dp", bit) for bit in (2, 4, 6)]
        cot, cot_t, x = fetch(after(me, packed))
        planes[3] = after(planes[3], cot)
        held_a = merge([plane[0, :high] for plane in planes])
        b = jnp.concatenate([plane[:, high:] for plane in planes], 0)
        far_b = swap(b, "tensor", 2)
        held_a = merge([held_a, swap(held_a, "dp", 1)])
        b = jnp.concatenate([b, swap(b, "dp", 1)], 0)
        xhat1, inv1, xhat_t = first_norm(after(x, (held_a, far_b)))
        held_a = merge([held_a, after(swap(held_a, "tensor", 2), (b, xhat1))])
        far_x = swap(far_b, "dp", 1)
        got_a = swap(held_a, "tensor", 1)
        got_b = swap(b, "tensor", 1)
    else:
        held_a, got_a, held_b, got_b = other_blocks(*other_pack(*weights, index), index, n_dp, n_t)
        b, far_b = held_b[:VDP], held_b[VDP:]
        got_b, got_far = got_b[:VDP], got_b[VDP:]
        cot, cot_t, x = fetch(me)
        xhat1, inv1, xhat_t = first_norm(x)
    qkv, prob, o, x1, wqkv, wout, vec = call(
        functools.partial(attend_kernel, some),
        "attend",
        [(me, smem), (virt, smem), (lengths, smem), (row_mask, smem), x, xhat1, held_a, got_a],
        [
            pltpu.VMEM((own, 3 * width), BF16),
            pltpu.VMEM((rows, WIN, width), BF16),
            pltpu.VMEM((own, width), BF16),
            pltpu.VMEM((own, width), F32),
            pltpu.VMEM((width, 3 * width), BF16),
            pltpu.VMEM((width, width), BF16),
            pltpu.VMEM((8, width), F32),
        ],
        flops=token_mm * (4 * width + 2 * WIN),
    )
    tall_b = 2 * (width // VDP)
    mats = [pltpu.VMEM((width, 2 * width), BF16)] * 2 + [pltpu.VMEM((2 * width, width), BF16)] * 2
    if usual:
        far_b = jnp.concatenate([far_b, after(far_x, x1)], 0)
        got_far = swap(far_b, "tensor", 1)
        got_b = after(got_b, far_b)
    wide_per = 4 if rows % 4 == 0 else rows
    *first, keep_b, send_b = call(
        functools.partial(hidden_near_kernel, wide_per),
        "hidden_near",
        [(virt, smem), x1, cot, cot_t, vec, b, got_b],
        [
            pltpu.VMEM((own, width), BF16),
            pltpu.VMEM((own, width), F32),
            pltpu.VMEM((own, 1), F32),
            pltpu.VMEM((own, width), F32),
            pltpu.VMEM((own, width), F32),
            pltpu.VMEM((VDP, tall_b, width), F32),
            pltpu.VMEM((VDP, tall_b, width), BF16),
        ],
        [pltpu.VMEM((own, 2 * width), BF16)] * 2 + [pltpu.VMEM((width, own), BF16)] + mats,
        token_mm * 12 * width,
        12,
    )
    y, dx1, g, gout, gvec = call(
        functools.partial(hidden_far_kernel, wide_per),
        "hidden_far",
        [(virt, smem), cot, vec, far_b, got_far, *first, o],
        [
            pltpu.VMEM((own, width), BF16),
            pltpu.VMEM((own, width), F32),
            pltpu.VMEM((own, width), BF16),
            pltpu.VMEM((width, width), F32),
            pltpu.VMEM((8, width), F32),
        ],
        [pltpu.VMEM((width, own), BF16)] + mats,
        token_mm * 9 * width,
    )
    core, xbit, zlo = ("tensor", 1), ("dp", 1), ("dp", 2)
    if usual:
        held_b = fold_step(keep_b, send_b, *core, g)
        y = after(y, held_b)
    y_near = swap(y, "tensor", 1)
    dqkv, keep_a, send_a, sums = call(
        functools.partial(back_kernel, per),
        "back",
        [(virt, smem), qkv, prob, g, xhat_t, wqkv, wout, vec, gout, gvec],
        [
            pltpu.VMEM((own, 3 * width), BF16),
            pltpu.VMEM((VDP, 32, width), F32),
            pltpu.VMEM((VDP * 32 + 8, width), BF16),
            pltpu.VMEM((8, width), F32),
        ],
        [pltpu.VMEM((width, 3 * width), F32)],
        token_mm * (4 * width + 5 * WIN),
    )
    if usual:
        held_b = fold_step(*halves(held_b), *xbit)
        got = after(swap(send_a, *core), held_b).astype(F32)
        held_a = keep_a + got[:-8].reshape(keep_a.shape)
        sums = sums + got[-8:]
        vec = after(vec, held_a)
    gx, gxb, layer_out = call(
        functools.partial(token_grad_kernel, less),
        "token_grad",
        [(me, smem), dqkv, wqkv, vec, xhat1, inv1, dx1, y, y_near],
        [
            pltpu.VMEM((own, width), F32),
            pltpu.VMEM((own, width), BF16),
            struct((images * seq_len, width), BF16),
        ],
        [pltpu.VMEM((3 * width, width), BF16), pltpu.SemaphoreType.DMA((2,))],
        flops=token_mm * 3 * width,
    )
    layer_out = layer_out.reshape(images, seq_len, width)

    def place(gx_near):
        return call(
            functools.partial(place_kernel, less),
            "place",
            [(me, smem), gx, gx_near],
            [struct((images * seq_len, width), F32)],
            [pltpu.VMEM((own, width), F32), pltpu.SemaphoreType.DMA((rows // less + 1,))],
        )[0].reshape(images, seq_len, width)

    if usual:
        held_b = fold_step(*halves(held_b), *zlo, gxb)
        send_a = jnp.concatenate([held_a[4:].reshape(-1, width), sums], 0).astype(BF16)
        got = after(swap(send_a, *xbit), (gxb, held_b)).astype(F32)
        held_a = held_a[:4] + got[:-8].reshape(4, -1, width)
        sums = sums + got[-8:]
        got = [
            swap(jnp.concatenate([held_a[n], sums] + more, 0).astype(BF16), "dp", 2 * n)
            for n, more in ((1, []), (2, [held_b[1]]), (3, []))
        ]
        grad_tokens = place(swap(after(gxb, held_a), "tensor", 1))
        got[2] = after(got[2], grad_tokens)
        shapes = ((small, 3 * width), (small, width), (2, small), (3, small), (tall, width), (tall, width))
        o_qkv, o_out, o_gains, o_bias, o_up, o_down = call(
            finish_kernel,
            "finish",
            [(me, smem), held_a, held_b, sums, *got],
            [struct(shape, F32) for shape in shapes],
            limit=2,
            hbm_outs=False,
        )
    else:
        grad_tokens = place(swap(gxb, "tensor", 1))
        send_a = send_a[:-8].reshape(keep_a.shape)
        grad_a, grad_b = other_reduce((keep_a, send_a), (keep_b, send_b), sums, index, n_dp, n_t)
        o_qkv = jnp.concatenate([grad_a[p * small : (p + 1) * small] for p in range(3)], 1)
        o_out = grad_a[3 * small : 4 * small]
        o_vec = lax.dynamic_slice_in_dim(grad_a[4 * small : 4 * small + 5], index * small, small, 1)
        o_gains, o_bias = o_vec[:2], o_vec[2:]
        o_up, o_down = grad_b[:tall], grad_b[tall:]
    return layer_out, grad_tokens, o_qkv, o_out, o_gains, o_bias, o_up, o_down.T


def solution(mesh):
    in_specs = (
        P("dp", None, None),
        P("dp"),
        P("dp", None),
        P("dp", None, None),
        P(("dp", "tensor"), None),
        P(("dp", "tensor"), None),
        P(None, ("dp", "tensor")),
        P(None, ("dp", "tensor")),
        P("dp", "tensor"),
        P("tensor", "dp"),
    )
    out_specs = (
        P("dp", None, None),
        P("dp", None, None),
        P(("dp", "tensor"), None),
        P(("dp", "tensor"), None),
        P(None, ("dp", "tensor")),
        P(None, ("dp", "tensor")),
        P("dp", "tensor"),
        P("tensor", "dp"),
    )
    return jax.shard_map(
        on_device, mesh=mesh, in_specs=in_specs, out_specs=out_specs, check_vma=False
    )
```
